32 devices in a mesh: ctx: 8 (over y, x, core), wt: 4 (over z).
Axes of the slice: x: 2, y: 2, z: 4, core: 2. Of those that a mesh axis runs over, the one named last changes fastest.
Arguments:
- tokens: bfloat16 [16, 1024, 768], P('wt', 'ctx'), may hold values from -6 to 6
- doc_starts: int32 [16, 4], P('wt'), may hold values from 0 to 1023, as said below
- attn_master: float32 [768, 1664], P('wt')
- attn_mom: float32 [768, 1664], P('wt')
- attn_sq: float32 [768, 1664], P('wt'), may hold values from 77 to 309
- ffn_master: float32 [768, 2, 3072], P('wt')
- ffn_mom: float32 [768, 2, 3072], P('wt')
- ffn_sq: float32 [768, 2, 3072], P('wt'), may hold values from 77 to 309
- small_master: float32 [8512], replicated
- small_mom: float32 [8512], replicated
- small_sq: float32 [8512], replicated, may hold values from 77 to 309
- cotangent: bfloat16 [16, 1024, 768], P('wt', 'ctx'), may hold values from -6 to 6
Outputs:
- layer_out: bfloat16 [16, 1024, 768], P('wt', 'ctx')
- input_grad: float32 [16, 1024, 768], P('wt', 'ctx')
- attn_mom_new: float32 [768, 1664], P('wt')
- attn_sq_new: float32 [768, 1664], P('wt')
- attn_new: float32 [768, 1664], P('wt')
- ffn_mom_new: float32 [768, 2, 3072], P('wt')
- ffn_sq_new: float32 [768, 2, 3072], P('wt')
- ffn_new: float32 [768, 2, 3072], P('wt')
- small_mom_new: float32 [8512], replicated
- small_sq_new: float32 [8512], replicated
- small_new: float32 [8512], replicated
The draws below stay inside these ranges and needn't reach their ends.
Inputs may be any that keep to these rules, and one draw needn't show every extreme that they name: `doc_starts`: in each stream the starts rise strictly from 0; the second document begins at one of positions 1 to 64 and the third begins within the last half of the final 128 positions; some stream's last document is its final position alone.
All inputs are finite; a program needn't handle non-finite values.
Results may differ from the reference program's by a relative error of at most 0.015.
Values may be sent and summed in bfloat16 or wider, within the bound.
No kernel may reach another device: no remote copies, remote signals or barrier semaphores. Data moves between devices by JAX's collectives and lax.ppermute only.
A program may use at most 256 MiB of HBM per device.

```python
import math
import jax
import jax.numpy as jnp
from jax import lax

D = 768
H = 12
HS = 64
FF = 3072
TOK_DEV = 128
STEP = 10
LEN = 1024
STREAMS = 16
TOKENS = 16384
ATT_COLS = 1664
NSMALL = 8512


def moment_draw(key, shape):
    return jax.random.normal(key, shape, jnp.float32) * (0.033 * math.sqrt(TOKENS))


def draw_attn_master(key, part):
    key = jax.random.fold_in(key, 11)
    values = jax.random.normal(key, (D, 2 * D + 2 * HS), jnp.float32)
    column = jnp.arange(2 * D + 2 * HS)
    factor = jnp.where(column < D + 2 * HS, 1.0, min(8.0, math.sqrt(LEN / 64.0))) / math.sqrt(D)
    return values * factor[None, :]


def draw_ffn_master(key, part):
    key = jax.random.fold_in(key, 12)
    values = jax.random.normal(key, (D, 2, FF), jnp.float32)
    factor = jnp.array([1.0 / math.sqrt(D), 1.0 / math.sqrt(FF)], jnp.float32)
    return values * factor[None, :, None]


def draw_small_master(key, part):
    key = jax.random.fold_in(key, 13)
    values = jax.random.normal(key, (7 * D + HS + FF,), jnp.float32)
    index = jnp.arange(7 * D + HS + FF)
    is_gain = (index < D) | (index >= 2 * D) & (index < 3 * D)
    return jnp.where(is_gain, 1.0 + 0.1 * values, 0.2 * values)


def draw_attn_mom(key, part):
    key = jax.random.fold_in(key, 21)
    return moment_draw(key, (D, 2 * D + 2 * HS))


def draw_ffn_mom(key, part):
    key = jax.random.fold_in(key, 22)
    return moment_draw(key, (D, 2, FF))


def draw_small_mom(key, part):
    key = jax.random.fold_in(key, 23)
    return moment_draw(key, (7 * D + HS + FF,))


def draw_doc_starts(key, part):
    key = jax.random.fold_in(key, 31)
    first_key, second_key, third_key, pick_key = jax.random.split(key, 4)
    zeros_col = jnp.zeros((STREAMS, 1), jnp.int32)
    second = jax.random.randint(first_key, (STREAMS, 1), 1, TOK_DEV // 2 + 1)
    third = jax.random.randint(second_key, (STREAMS, 1), LEN - TOK_DEV // 2, LEN - TOK_DEV // 4)
    fourth = jax.random.randint(third_key, (STREAMS, 1), LEN - TOK_DEV // 4, LEN)
    chosen = jax.random.randint(pick_key, (), 0, STREAMS)
    rows = jnp.arange(STREAMS, dtype=jnp.int32)[:, None]
    fourth = jnp.where(rows == chosen, LEN - 1, fourth)
    return jnp.concatenate([zeros_col, second, third, fourth], axis=1).astype(jnp.int32)


def block_scale(own_key, extent, cuts, low, top_value):
    level, own = 1.0, jax.random.fold_in(own_key, 6)
    for position, shards_of in cuts:
        heights = jnp.exp(jax.random.uniform(jax.random.fold_in(own, position), (shards_of,), jnp.float32, low / len(cuts), top_value / len(cuts)))
        level = level * jnp.repeat(heights, extent[position] // shards_of).reshape([-1 if axis == position else 1 for axis in range(len(extent))])
    return level


def bell_draw(key, dims, scale, limit, cuts=(), kind=jnp.bfloat16):
    loudness = block_scale(key, dims, cuts, -0.22, 0.18) if cuts else 1.0
    values = jax.random.normal(key, dims, jnp.float32) * scale * loudness
    return jnp.minimum(jnp.maximum(values, -limit), limit).astype(kind)


def setup_inputs(seed: int = 0) -> dict:
    seeds = jax.random.split(jax.random.key(seed), 13)
    return {
        "tokens": bell_draw(seeds[0], (STREAMS, LEN, D), 1.0, 6.0, ((0, 4), (1, 8))),
        "doc_starts": draw_doc_starts(jax.random.fold_in(seeds[12], 71), 0),
        "attn_master": draw_attn_master(jax.random.fold_in(seeds[12], 71), 0),
        "attn_mom": draw_attn_mom(jax.random.fold_in(seeds[12], 71), 0),
        "attn_sq": jnp.clip(jnp.exp(math.log(309.0) - 1.3895359 * jax.random.uniform(seeds[4], (D, ATT_COLS), jnp.float32) ** block_scale(seeds[4], (D, ATT_COLS), ((0, 4),), -0.2, 0.2)), 77.0, 309.0),
        "ffn_master": draw_ffn_master(jax.random.fold_in(seeds[12], 71), 0),
        "ffn_mom": draw_ffn_mom(jax.random.fold_in(seeds[12], 71), 0),
        "ffn_sq": jnp.clip(jnp.exp(math.log(309.0) - 1.3895359 * jax.random.uniform(seeds[7], (D, 2, FF), jnp.float32) ** block_scale(seeds[7], (D, 2, FF), ((0, 4),), -0.2, 0.2)), 77.0, 309.0),
        "small_master": draw_small_master(jax.random.fold_in(seeds[12], 71), 0),
        "small_mom": draw_small_mom(jax.random.fold_in(seeds[12], 71), 0),
        "small_sq": jnp.clip(jnp.exp(jax.random.uniform(seeds[10], (NSMALL,), jnp.float32, math.log(77.0), math.log(309.0))), 77.0, 309.0),
        "cotangent": bell_draw(seeds[11], (STREAMS, LEN, D), 1.0, 6.0, ((0, 4), (1, 8))),
    }


@jax.custom_vjp
def low(v):
    return lax.optimization_barrier(v.astype(jnp.bfloat16)).astype(jnp.float32)

@jax.custom_vjp
def low_back(v):
    return v

def low_keep(v):
    return (low(v), None)

def low_pass(kept, grad):
    return (grad,)

def back_keep(v):
    return (v, None)

def back_low(kept, grad):
    return (low(grad),)
low.defvjp(low_keep, low_pass)
low_back.defvjp(back_keep, back_low)
NORM_EPS = 1e-05
GELU_COEF = 0.7978845608028654
BETA_ONE = 0.9
BETA_TWO = 0.95
ADAM_EPS = 1e-08

def layer_norm(values, gain, shift):
    centre = values - lax.optimization_barrier(jnp.mean(values, axis=-1, keepdims=True))
    spread = lax.optimization_barrier(jnp.mean(centre * centre, axis=-1, keepdims=True))
    return centre * lax.rsqrt(spread + NORM_EPS) * gain + shift

def gelu(values):
    return 0.5 * values * (1.0 + jnp.tanh(GELU_COEF * (values + 0.044715 * values * values * values)))

def matmul(left, right):
    return jnp.dot(left, right, precision=lax.Precision.HIGHEST)

def split_small(small):
    return (small[0:D], small[D:2 * D], small[2 * D:3 * D], small[3 * D:4 * D], small[4 * D:5 * D], small[5 * D:6 * D], small[6 * D:7 * D], small[7 * D:7 * D + HS], small[7 * D + HS:])

def attend_block(queries, query_pos, query_doc, keys, values_all, key_doc):
    scores = jnp.einsum('thd,kd->thk', queries, keys, precision=lax.Precision.HIGHEST) * HS ** (-0.5)
    scores = low_back(scores)
    key_pos = jnp.arange(keys.shape[0], dtype=jnp.int32)
    allowed = (query_doc[:, None] == key_doc[None, :]) & (key_pos[None, :] <= query_pos[:, None])
    scores = jnp.where(allowed[:, None, :], scores, -1e+30)
    peak = lax.optimization_barrier(jnp.max(scores, axis=-1, keepdims=True))
    expo = jnp.exp(scores - peak)
    weights = low(expo / lax.optimization_barrier(jnp.sum(expo, axis=-1, keepdims=True)))
    return jnp.einsum('thk,kd->thd', weights, values_all, precision=lax.Precision.HIGHEST)

def forward(attn_vals, ffn_vals, small_vals, stream, starts):
    gain_one, shift_one, gain_two, shift_two, bias_query, bias_out, bias_proj, bias_value, bias_hidden = split_small(small_vals)
    normed = low(layer_norm(stream, gain_one, shift_one))
    mixed = matmul(normed, attn_vals[:, :D + 2 * HS])
    queries = low(low_back(mixed[:, :D] + bias_query))
    keys = low(low_back(mixed[:, D:D + HS]))
    values_all = low(low_back(mixed[:, D + HS:] + bias_value))
    positions = jnp.arange(LEN, dtype=jnp.int32)
    docs = lax.optimization_barrier(jnp.sum((starts[None, :] <= positions[:, None]).astype(jnp.int32), axis=1)) - 1
    block_rows = min(512, LEN)
    block_count = LEN // block_rows
    checked = jax.checkpoint(attend_block)
    pieces = (queries.reshape(block_count, block_rows, H, HS), positions.reshape(block_count, block_rows), docs.reshape(block_count, block_rows))
    heads_out = lax.map(lambda piece: checked(piece[0], piece[1], piece[2], keys, values_all, docs), pieces)
    attended = low(low_back(heads_out.reshape(LEN, D)))
    hidden = stream + low_back(matmul(attended, attn_vals[:, D + 2 * HS:])) + bias_out
    normed_two = low(layer_norm(hidden, gain_two, shift_two))
    up_vals = low_back(matmul(normed_two, ffn_vals[:, 0, :]) + bias_hidden)
    activated = low(gelu(up_vals))
    return hidden + matmul(activated, ffn_vals[:, 1, :].T) + bias_proj

def adam_update(master, gradient, first, second, step_rate, decay_rate):
    first_new = BETA_ONE * first + (1.0 - BETA_ONE) * gradient
    second_new = BETA_TWO * second + (1.0 - BETA_TWO) * gradient * gradient
    first_hat = first_new / (1.0 - BETA_ONE ** STEP)
    second_hat = second_new / (1.0 - BETA_TWO ** STEP)
    master_new = master - step_rate * (first_hat / (jnp.sqrt(second_hat) + ADAM_EPS) + decay_rate * master)
    return (first_new, second_new, master_new)

def reference(tokens, doc_starts, attn_master, attn_mom, attn_sq, ffn_master, ffn_mom, ffn_sq, small_master, small_mom, small_sq, cotangent):
    attn_low = attn_master.astype(jnp.bfloat16).astype(jnp.float32)
    ffn_low = ffn_master.astype(jnp.bfloat16).astype(jnp.float32)

    def one_stream(totals, inputs):
        stream, starts, back_rows = inputs

        def layer_fn(attn_vals, ffn_vals, small_vals, stream_vals):
            return forward(attn_vals, ffn_vals, small_vals, stream_vals, starts)
        result, pullback = jax.vjp(layer_fn, attn_low, ffn_low, small_master, stream.astype(jnp.float32))
        grads = pullback(back_rows.astype(jnp.float32))
        totals = (totals[0] + grads[0], totals[1] + grads[1], totals[2] + grads[2])
        return (totals, (result.astype(jnp.bfloat16), grads[3]))
    start_totals = (jnp.zeros(attn_master.shape, jnp.float32), jnp.zeros(ffn_master.shape, jnp.float32), jnp.zeros(small_master.shape, jnp.float32))
    totals, (layer_out, input_grad) = lax.scan(one_stream, start_totals, (tokens, doc_starts, cotangent))
    attn_first, attn_second, attn_next = adam_update(attn_master, totals[0], attn_mom, attn_sq, 0.1, 0.1)
    ffn_first, ffn_second, ffn_next = adam_update(ffn_master, totals[1], ffn_mom, ffn_sq, 0.1, 0.1)
    small_first, small_second, small_next = adam_update(small_master, totals[2], small_mom, small_sq, 1.0, 0.0)
    return (layer_out, input_grad, attn_first, attn_second, attn_next, ffn_first, ffn_second, ffn_next, small_first, small_second, small_next)
```

```python
import jax
import jax.numpy as jnp
from jax import lax
from jax.sharding import PartitionSpec as P

D = 768
HS = 64
FF = 3072
STEP = 10


NORM_EPS = 1e-05
GELU_COEF = 0.7978845608028654
GELU_CUBE = 0.044715
BETA_ONE = 0.9
BETA_TWO = 0.95
ADAM_EPS = 1e-08


def layer_norm(values, gain, shift):
    centre = values - jnp.mean(values, axis=-1, keepdims=True)
    spread = jnp.mean(centre * centre, axis=-1, keepdims=True)
    return centre * lax.rsqrt(spread + NORM_EPS) * gain + shift


def gelu_both(u):
    inner = jnp.tanh(GELU_COEF * (u + GELU_CUBE * u * u * u))
    value = 0.5 * u * (1.0 + inner)
    slope = 0.5 * (1.0 + inner) + 0.5 * u * (1.0 - inner * inner) * (
        GELU_COEF * (1.0 + 3.0 * GELU_CUBE * u * u)
    )
    return value, slope


def split_small(small):
    return (
        small[0:D],
        small[D : 2 * D],
        small[2 * D : 3 * D],
        small[3 * D : 4 * D],
        small[4 * D : 5 * D],
        small[5 * D : 6 * D],
        small[6 * D : 7 * D],
        small[7 * D : 7 * D + HS],
        small[7 * D + HS :],
    )


def rows_dot(left, right):
    return lax.dot_general(
        left, right, (((0,), (0,)), ((), ())), preferred_element_type=jnp.float32
    )


def cols_dot(left, right):
    return lax.dot_general(
        left, right, (((1,), (1,)), ((), ())), preferred_element_type=jnp.float32
    )


def dot(left, right):
    return jnp.dot(left, right, preferred_element_type=jnp.float32)


def low(values):
    return values.astype(jnp.bfloat16)


def wide(values):
    return values.astype(jnp.float32)


def adam_update(master, gradient, first, second, step_rate, decay_rate):
    first_new = BETA_ONE * first + (1.0 - BETA_ONE) * gradient
    second_new = BETA_TWO * second + (1.0 - BETA_TWO) * gradient * gradient
    first_hat = first_new / (1.0 - BETA_ONE**STEP)
    second_hat = second_new / (1.0 - BETA_TWO**STEP)
    master_new = master - step_rate * (
        first_hat / (jnp.sqrt(second_hat) + ADAM_EPS) + decay_rate * master
    )
    return (first_new, second_new, master_new)


def xor_send(array, mask):
    count = lax.axis_size("ctx")
    return lax.ppermute(array, "ctx", [(i, i ^ mask) for i in range(count)])


def shift_send(array, shift):
    count = lax.axis_size("wt")
    return lax.ppermute(array, "wt", [(i, (i + shift) % count) for i in range(count)])


def put(buffer, piece, place, axis):
    starts = [0] * buffer.ndim
    starts[axis] = place * piece.shape[axis]
    return lax.dynamic_update_slice(buffer, piece, starts)


def take(buffer, place, axis, size):
    return lax.dynamic_slice_in_dim(buffer, place * size, size, axis)


def gather_wt(piece, axis):
    count, place = lax.axis_size("wt"), lax.axis_index("wt")
    shape = list(piece.shape)
    shape[axis] *= count
    buffer = put(jnp.zeros(shape, piece.dtype), piece, place, axis)
    for shift in range(1, count):
        buffer = put(buffer, shift_send(piece, shift), (place - shift) % count, axis)
    return buffer


def gather_ctx(piece):
    count = lax.axis_size("ctx")
    got = {0: piece}
    for mask in range(2, count, 2):
        got[mask] = xor_send(piece, mask)
    for mask in range(0, count, 2):
        got[mask + 1] = xor_send(got[mask], 1)
    return [got[mask] for mask in range(count)]


def scatter_ctx(pieces):
    count = lax.axis_size("ctx")
    half = {}
    for mask in range(count - 2, -1, -2):
        other = xor_send(pieces[mask + 1], 1)
        half[mask] = low(wide(pieces[mask]) + wide(other))
    total = wide(half[0])
    for mask in range(2, count, 2):
        total = total + wide(xor_send(half[mask], mask))
    return total


def scatter_wt(array, axis):
    count, place = lax.axis_size("wt"), lax.axis_index("wt")
    size = array.shape[axis] // count
    total = wide(take(array, place, axis, size))
    for shift in range(1, count):
        sent = take(array, (place + shift) % count, axis, size)
        total = total + wide(shift_send(sent, shift))
    return total


def shards(
    tokens,
    doc_starts,
    attn_master,
    attn_mom,
    attn_sq,
    ffn_master,
    ffn_mom,
    ffn_sq,
    small_master,
    small_mom,
    small_sq,
    cotangent,
):
    ctx_count = lax.axis_size("ctx")
    ctx_place = lax.axis_index("ctx")
    wt_count = lax.axis_size("wt")
    batches, rows_here, width = tokens.shape
    heads = width // HS
    qkv_cols = width + 2 * HS
    all_rows = batches * rows_here
    shard_rows = attn_master.shape[0]
    piece_rows = shard_rows // ctx_count
    chunk = FF // ctx_count
    order = ctx_place ^ jnp.arange(ctx_count, dtype=jnp.int32)
    (
        gain_one,
        shift_one,
        gain_two,
        shift_two,
        bias_query,
        bias_out,
        bias_proj,
        bias_value,
        bias_hidden,
    ) = split_small(small_master)

    attn_piece = low(take(attn_master, ctx_place, 0, piece_rows))

    def whole_rows(piece):
        parts = gather_ctx(gather_wt(piece[None], 0))
        buffer = jnp.zeros((wt_count, ctx_count) + piece.shape, piece.dtype)
        for k, part in enumerate(parts):
            buffer = put(buffer, part[:, None], ctx_place ^ k, 1)
        return buffer.reshape((width,) + piece.shape[1:])

    weight_qkv = whole_rows(attn_piece[:, :qkv_cols])
    weight_out = whole_rows(attn_piece[:, qkv_cols:])
    ffn_piece = low(jnp.swapaxes(take(ffn_master, ctx_place, 2, chunk), 0, 1))
    ffn_parts = gather_ctx(gather_wt(ffn_piece, 1))
    bias_parts = bias_hidden.reshape(ctx_count, chunk)[order]

    stream = wide(tokens.reshape(all_rows, width))
    normed, norm_back_one = jax.vjp(layer_norm, stream, gain_one, shift_one)
    normed_low = low(normed)
    mixed = dot(normed_low, weight_qkv)
    queries = low(mixed[:, :width] + bias_query)
    kv_local = low(
        mixed[:, width:] + jnp.concatenate([jnp.zeros((HS,), jnp.float32), bias_value])
    ).reshape(batches, rows_here, 2 * HS)
    kv_parts = jnp.stack(gather_ctx(kv_local), axis=1).reshape(
        batches, ctx_count * rows_here, 2 * HS
    )
    keys_all, values_all = kv_parts[..., :HS], kv_parts[..., HS:]
    local_pos = jnp.arange(rows_here, dtype=jnp.int32)
    query_pos = ctx_place * rows_here + local_pos
    key_pos = (order[:, None] * rows_here + local_pos[None, :]).reshape(-1)
    queries = queries.reshape(batches, rows_here * heads, HS)
    scale = HS ** (-0.5)
    attended_list, log_list, allowed_list = [], [], []
    for b in range(batches):
        starts = doc_starts[b]
        query_doc = jnp.sum((starts[None, :] <= query_pos[:, None]).astype(jnp.int32), axis=1)
        key_doc = jnp.sum((starts[None, :] <= key_pos[:, None]).astype(jnp.int32), axis=1)
        allowed = (query_doc[:, None] == key_doc[None, :]) & (key_pos[None, :] <= query_pos[:, None])
        allowed = jnp.repeat(allowed, heads, axis=0)
        allowed_list.append(allowed)
        scores = jnp.where(allowed, cols_dot(queries[b], keys_all[b]) * scale, -1e30)
        peak = jnp.max(scores, axis=-1, keepdims=True)
        expo = jnp.exp(scores - peak)
        total = jnp.sum(expo, axis=-1, keepdims=True)
        attended_list.append(dot(low(expo / total), values_all[b]))
        log_list.append(peak + jnp.log(total))
    attended = jnp.stack(attended_list)
    attended_low = low(attended).reshape(all_rows, width)
    hidden = stream + dot(attended_low, weight_out) + bias_out
    normed_two, norm_back_two = jax.vjp(layer_norm, hidden, gain_two, shift_two)
    normed_two_low = low(normed_two)

    back_low = cotangent.reshape(all_rows, width)
    back_rows = wide(back_low)
    down_vals = jnp.zeros((all_rows, width), jnp.float32)
    grad_normed_two = jnp.zeros((all_rows, width), jnp.float32)
    ffn_grads, hidden_grads = [], []
    for k in range(ctx_count):
        weight_up, weight_down = ffn_parts[k][0], ffn_parts[k][1]
        value, slope = gelu_both(dot(normed_two_low, weight_up) + bias_parts[k])
        act = low(value)
        down_vals = down_vals + cols_dot(act, weight_down)
        grad_up = low(dot(back_low, weight_down) * slope)
        hidden_grads.append(jnp.sum(wide(grad_up), axis=0))
        grad_normed_two = grad_normed_two + cols_dot(grad_up, weight_up)
        ffn_grads.append(
            jnp.stack([low(rows_dot(normed_two_low, grad_up)), low(rows_dot(back_low, act))])
        )
    layer_out = low(hidden + down_vals + bias_proj).reshape(batches, rows_here, width)
    grad_bias_proj = jnp.sum(back_rows, axis=0)
    grad_bias_hidden = jnp.stack(hidden_grads)[order].reshape(FF)
    ffn_part = low(scatter_wt(low(scatter_ctx(ffn_grads)), 1))

    grad_hidden_part, grad_gain_two, grad_shift_two = norm_back_two(grad_normed_two)
    grad_hidden = back_rows + grad_hidden_part
    grad_bias_out = jnp.sum(grad_hidden, axis=0)
    grad_hidden_low = low(grad_hidden)
    grad_out = rows_dot(attended_low, grad_hidden_low)

    def summed_rows(grad):
        blocks = low(grad).reshape(wt_count, ctx_count, piece_rows, grad.shape[1])
        pieces = [take(blocks, ctx_place ^ k, 1, 1)[:, 0] for k in range(ctx_count)]
        part = low(scatter_wt(low(scatter_ctx(pieces)), 0)[0])
        buffer = jnp.zeros((ctx_count,) + part.shape, part.dtype)
        for k, got in enumerate(gather_ctx(part)):
            buffer = put(buffer, got[None], ctx_place ^ k, 0)
        return wide(buffer.reshape(shard_rows, grad.shape[1]))

    out_total = summed_rows(grad_out)

    grad_attended = low(cols_dot(grad_hidden_low, weight_out)).reshape(
        batches, rows_here * heads, HS
    )
    grad_query_list, grad_kv_list = [], []
    for b in range(batches):
        grads = grad_attended[b]
        delta = jnp.sum(wide(grads) * attended[b], axis=-1, keepdims=True)
        scores = jnp.where(allowed_list[b], cols_dot(queries[b], keys_all[b]) * scale, -1e30)
        weights = jnp.exp(scores - log_list[b])
        grad_scores = low(weights * (cols_dot(grads, values_all[b]) - delta))
        grad_query_list.append(low(dot(grad_scores, keys_all[b]) * scale))
        grad_kv_list.append(
            jnp.concatenate(
                [
                    low(rows_dot(grad_scores, queries[b]) * scale),
                    low(rows_dot(low(weights), grads)),
                ],
                axis=1,
            )
        )
    grad_query = jnp.stack(grad_query_list).reshape(all_rows, width)
    grad_kv = jnp.stack(grad_kv_list).reshape(batches, ctx_count, rows_here, 2 * HS)
    grad_kv_low = low(scatter_ctx([grad_kv[:, k] for k in range(ctx_count)])).reshape(
        all_rows, 2 * HS
    )
    grad_bias_query = jnp.sum(wide(grad_query), axis=0)
    grad_bias_value = jnp.sum(wide(grad_kv_low[:, HS:]), axis=0)
    grad_mixed = jnp.concatenate([grad_query, grad_kv_low], axis=1)
    qkv_total = summed_rows(rows_dot(normed_low, grad_mixed))
    grad_normed = cols_dot(grad_mixed, weight_qkv)
    grad_stream_part, grad_gain_one, grad_shift_one = norm_back_one(grad_normed)
    input_grad = (grad_hidden + grad_stream_part).reshape(batches, rows_here, width)

    ffn_buffer = jnp.zeros((ctx_count,) + ffn_part.shape, ffn_part.dtype)
    for k, got in enumerate(gather_ctx(ffn_part)):
        ffn_buffer = put(ffn_buffer, got[None], ctx_place ^ k, 0)
    ffn_total = wide(jnp.transpose(ffn_buffer, (2, 1, 0, 3)).reshape(shard_rows, 2, FF))
    attn_total = jnp.concatenate([qkv_total, out_total], axis=1)
    grad_small = jnp.concatenate(
        [
            grad_gain_one,
            grad_shift_one,
            grad_gain_two,
            grad_shift_two,
            grad_bias_query,
            grad_bias_out,
            grad_bias_proj,
            grad_bias_value,
            grad_bias_hidden,
        ]
    )
    small_total = lax.psum(grad_small, ("ctx", "wt"))
    attn_new = adam_update(attn_master, attn_total, attn_mom, attn_sq, 0.1, 0.1)
    ffn_new = adam_update(ffn_master, ffn_total, ffn_mom, ffn_sq, 0.1, 0.1)
    small_new = adam_update(small_master, small_total, small_mom, small_sq, 1.0, 0.0)
    return (layer_out, input_grad) + attn_new + ffn_new + small_new


def solution(mesh):
    rows, cube = P("wt", None), P("wt", None, None)
    flow = P("wt", "ctx", None)
    in_specs = (flow, rows, rows, rows, rows, cube, cube, cube, P(), P(), P(), flow)
    out_specs = (flow, flow, rows, rows, rows, cube, cube, cube, P(), P(), P())
    return jax.shard_map(shards, mesh=mesh, in_specs=in_specs, out_specs=out_specs, check_vma=False)
```

```python
import jax
import jax.numpy as jnp
from jax import lax
from jax.experimental import pallas as pl
from jax.experimental.pallas import tpu as pltpu
from jax.sharding import PartitionSpec as P

D = 768
HS = 64
FF = 3072
STEP = 10


NORM_EPS = 1e-05
GELU_COEF = 0.7978845608028654
GELU_CUBE = 0.044715
BETA_ONE = 0.9
BETA_TWO = 0.95
ADAM_EPS = 1e-08
VMEM_LIMIT = 56 << 20


def layer_norm(values, gain, shift):
    centre = values - jnp.mean(values, axis=-1, keepdims=True)
    spread = jnp.mean(centre * centre, axis=-1, keepdims=True)
    return centre * lax.rsqrt(spread + NORM_EPS) * gain + shift


def gelu_both(u):
    inner = jnp.tanh(GELU_COEF * (u + GELU_CUBE * u * u * u))
    value = 0.5 * u * (1.0 + inner)
    slope = 0.5 * (1.0 + inner) + 0.5 * u * (1.0 - inner * inner) * (
        GELU_COEF * (1.0 + 3.0 * GELU_CUBE * u * u)
    )
    return value, slope


def split_small(small):
    return (
        small[0:D],
        small[D : 2 * D],
        small[2 * D : 3 * D],
        small[3 * D : 4 * D],
        small[4 * D : 5 * D],
        small[5 * D : 6 * D],
        small[6 * D : 7 * D],
        small[7 * D : 7 * D + HS],
        small[7 * D + HS :],
    )


def rows_dot(left, right):
    return lax.dot_general(
        left, right, (((0,), (0,)), ((), ())), preferred_element_type=jnp.float32
    )


def cols_dot(left, right):
    return lax.dot_general(
        left, right, (((1,), (1,)), ((), ())), preferred_element_type=jnp.float32
    )


def dot(left, right):
    return jnp.dot(left, right, preferred_element_type=jnp.float32)


def low(values):
    return values.astype(jnp.bfloat16)


def wide(values):
    return values.astype(jnp.float32)


def adam_update(master, gradient, first, second, step_rate, decay_rate):
    first_new = BETA_ONE * first + (1.0 - BETA_ONE) * gradient
    second_new = BETA_TWO * second + (1.0 - BETA_TWO) * gradient * gradient
    first_hat = first_new / (1.0 - BETA_ONE**STEP)
    second_hat = second_new / (1.0 - BETA_TWO**STEP)
    master_new = master - step_rate * (
        first_hat / (jnp.sqrt(second_hat) + ADAM_EPS) + decay_rate * master
    )
    return (first_new, second_new, master_new)


def xor_send(array, mask):
    count = lax.axis_size("ctx")
    return lax.ppermute(array, "ctx", [(i, i ^ mask) for i in range(count)])


def shift_send(array, shift):
    count = lax.axis_size("wt")
    return lax.ppermute(array, "wt", [(i, (i + shift) % count) for i in range(count)])


def put(buffer, piece, place, axis):
    starts = [0] * buffer.ndim
    starts[axis] = place * piece.shape[axis]
    return lax.dynamic_update_slice(buffer, piece, starts)


def take(buffer, place, axis, size):
    return lax.dynamic_slice_in_dim(buffer, place * size, size, axis)


def gather_wt(piece, axis):
    count, place = lax.axis_size("wt"), lax.axis_index("wt")
    shape = list(piece.shape)
    shape[axis] *= count
    buffer = put(jnp.zeros(shape, piece.dtype), piece, place, axis)
    for shift in range(1, count):
        buffer = put(buffer, shift_send(piece, shift), (place - shift) % count, axis)
    return buffer


def gather_chips(piece):
    count = lax.axis_size("ctx")
    return [piece] + [xor_send(piece, mask) for mask in range(2, count, 2)]


def scatter_chips(pieces):
    total = wide(pieces[0])
    for m in range(1, len(pieces)):
        total = total + wide(xor_send(pieces[m], 2 * m))
    return total


def gather_ctx(piece):
    even = jnp.stack(gather_chips(piece))
    return even, xor_send(even, 1)


def scatter_ctx(even, odd):
    half = low(wide(even) + wide(xor_send(odd, 1)))
    return scatter_chips([half[m] for m in range(half.shape[0])])


def scatter_wt(array, axis):
    count, place = lax.axis_size("wt"), lax.axis_index("wt")
    size = array.shape[axis] // count
    total = wide(take(array, place, axis, size))
    for shift in range(1, count):
        sent = take(array, (place + shift) % count, axis, size)
        total = total + wide(shift_send(sent, shift))
    return total


def attention_kernels(batches, rows, width, parts):
    half_parts = parts // 2
    keys = parts * rows
    pair = 2 * HS
    groups = width // (2 * pair)
    factor = HS ** (-0.5) * 1.4426950408889634
    masks = list(range(0, parts, 2)) + list(range(1, parts, 2))

    def lanes(shape):
        return lax.broadcasted_iota(jnp.int32, shape, 1)

    def spread(even_ref, odd_ref, key_ref, value_ref):
        for j in range(parts):
            ref = even_ref if j < half_parts else odd_ref
            block = wide(ref[j % half_parts, 0])
            turned = pltpu.roll(block, HS, 1)
            first = lanes(block.shape) < HS
            here = pl.ds(j * rows, rows)
            key_ref[0, here, :] = low(jnp.where(first, block, 0.0))
            key_ref[1, here, :] = low(jnp.where(first, 0.0, turned))
            value_ref[0, here, :] = low(jnp.where(first, turned, 0.0))
            value_ref[1, here, :] = low(jnp.where(first, 0.0, block))

    def doc_begin(starts_ref, stream, positions):
        begin = jnp.zeros_like(positions)
        for j in range(starts_ref.shape[1]):
            start = starts_ref[stream, j]
            begin = jnp.where(start <= positions, jnp.maximum(begin, start), begin)
        return begin

    def forward(starts_ref, place_ref, query_ref, even_ref, odd_ref, low_ref, full_ref, log_ref, cap, key, value):
        stream, place = pl.program_id(0), place_ref[0]
        spread(even_ref, odd_ref, key, value)
        query_pos = place * rows + lax.broadcasted_iota(jnp.int32, (rows, 1), 0)
        begin = doc_begin(starts_ref, stream, query_pos)
        for j, mask in enumerate(masks):
            key_pos = (place ^ mask) * rows + lax.broadcasted_iota(jnp.int32, (rows, rows), 1)
            allowed = (key_pos >= begin) & (key_pos <= query_pos)
            cap[:, j * rows : (j + 1) * rows] = jnp.where(allowed, 3.0e38, -1e30)
        log_ref[...] = jnp.zeros_like(log_ref)

        def group(g, carry):
            at = pl.multiple_of(g * 2 * pair, 2 * pair)
            both = query_ref[0, :, pl.ds(at, 2 * pair)]
            two = jnp.concatenate([both[:, :pair], both[:, pair:]], axis=0)
            limit = cap[...]
            limit = jnp.concatenate([limit, limit], axis=0)
            total = jnp.zeros((2 * rows, pair), jnp.float32)
            logs = log_ref[0]
            for half in range(2):
                scores = jnp.minimum(cols_dot(two, key[half]) * factor, limit)
                peak = jnp.max(scores, axis=1, keepdims=True)
                expo = jnp.exp2(scores - peak)
                norm = jnp.sum(expo, axis=1, keepdims=True)
                total = total + dot(low(expo), value[half]) / norm
                log = peak + jnp.log2(norm)
                column = lanes((rows, pair))
                logs = jnp.where(column == 4 * g + half, log[:rows], logs)
                logs = jnp.where(column == 4 * g + 2 + half, log[rows:], logs)
            log_ref[0] = logs
            total = jnp.concatenate([total[:rows], total[rows:]], axis=1)
            full_ref[0, :, pl.ds(at, 2 * pair)] = total
            low_ref[0, :, pl.ds(at, 2 * pair)] = low(total)
            return carry

        lax.fori_loop(0, groups, group, 0)

    def backward(
        starts_ref, place_ref, query_ref, even_ref, odd_ref, full_ref, log_ref, grad_ref,
        query_grad_ref, even_grad_ref, odd_grad_ref,
        cap, key, value, key_turned, log_rows, delta_rows, weight_buf, score_buf, query_buf, grad_buf,
    ):
        stream, place = pl.program_id(0), place_ref[0]
        spread(even_ref, odd_ref, key, value)
        query_pos = place * rows + lax.broadcasted_iota(jnp.int32, (1, rows), 1)
        begin = doc_begin(starts_ref, stream, query_pos)
        for j, mask in enumerate(masks):
            key_pos = (place ^ mask) * rows + lax.broadcasted_iota(jnp.int32, (rows, rows), 0)
            allowed = (key_pos >= begin) & (key_pos <= query_pos)
            cap[j * rows : (j + 1) * rows, :] = jnp.where(allowed, 3.0e38, -1e30)
            here = pl.ds(j * rows, rows)
            key_turned[:, j * rows : (j + 1) * rows] = low(wide(key[0, here, :]).T[:HS])
        log_rows[...] = log_ref[0].T[: log_rows.shape[0]]
        head_of = lax.broadcasted_iota(jnp.int32, (delta_rows.shape[0], width), 1) // HS
        chosen = (head_of == lax.broadcasted_iota(jnp.int32, (delta_rows.shape[0], width), 0)).astype(jnp.float32)
        delta_rows[...] = lax.dot_general(
            chosen, wide(grad_ref[0]) * full_ref[0], (((1,), (1,)), ((), ())),
            precision=lax.Precision.HIGHEST, preferred_element_type=jnp.float32,
        )
        first = lanes((2 * rows, pair)) < HS
        for g in range(groups):
            at = g * 2 * pair
            both, both_grad = query_ref[0, :, at : at + 2 * pair], grad_ref[0, :, at : at + 2 * pair]
            two = jnp.concatenate([both[:, :pair], both[:, pair:]], axis=0)
            two_grad = jnp.concatenate([both_grad[:, :pair], both_grad[:, pair:]], axis=0)
            limit = cap[...]
            limit = jnp.concatenate([limit, limit], axis=1)
            turned = []
            for half in range(2):
                h = 4 * g + half
                span = slice((2 * g + half) * 2 * rows, (2 * g + half + 1) * 2 * rows)
                keep = first if half == 0 else jnp.logical_not(first)
                query_buf[span, :] = low(jnp.where(keep, wide(two), 0.0))
                grad_buf[span, :] = low(jnp.where(keep, wide(two_grad), 0.0))
                log = jnp.concatenate([log_rows[h : h + 1, :], log_rows[h + 2 : h + 3, :]], axis=1)
                delta = jnp.concatenate([delta_rows[h : h + 1, :], delta_rows[h + 2 : h + 3, :]], axis=1)
                scores = jnp.minimum(cols_dot(key[half], two) * factor, limit)
                weights = jnp.exp2(scores - log)
                grad_scores = low(weights * (cols_dot(value[half], two_grad) - delta))
                weight_buf[:, span] = low(weights)
                score_buf[:, span] = grad_scores
                turned.append(dot(key_turned[...], grad_scores))
            turned = jnp.concatenate(turned, axis=0) * HS ** (-0.5)
            query_grad_ref[0, :, at : at + pair] = low(turned[:, :rows].T)
            query_grad_ref[0, :, at + pair : at + 2 * pair] = low(turned[:, rows:].T)
        for j in range(parts):
            here = pl.ds(j * rows, rows)
            value_sum = dot(weight_buf[here, :], grad_buf[...])
            key_sum = dot(score_buf[here, :], query_buf[...]) * HS ** (-0.5)
            value_sum = value_sum + pltpu.roll(value_sum, HS, 1)
            key_sum = key_sum + pltpu.roll(key_sum, HS, 1)
            ref = even_grad_ref if j < half_parts else odd_grad_ref
            ref[j % half_parts, 0] = low(jnp.where(lanes((rows, pair)) < HS, key_sum, value_sum))

    flow = pl.BlockSpec((1, rows, width), lambda b, *_: (b, 0, 0))
    logs = pl.BlockSpec((1, rows, pair), lambda b, *_: (b, 0, 0))
    blocks = pl.BlockSpec((half_parts, 1, rows, pair), lambda b, *_: (0, b, 0, 0))
    work = batches * rows * keys * (width // HS)

    def cost(products):
        return pl.CostEstimate(flops=work * 256 * products, bytes_accessed=8 << 20, transcendentals=work)

    shared = [
        pltpu.VMEM((2, keys, pair), jnp.bfloat16),
        pltpu.VMEM((2, keys, pair), jnp.bfloat16),
    ]
    run_forward = pl.pallas_call(
        forward,
        grid_spec=pltpu.PrefetchScalarGridSpec(
            num_scalar_prefetch=2,
            grid=(batches,),
            in_specs=[flow, blocks, blocks],
            out_specs=[flow, flow, logs],
            scratch_shapes=[pltpu.VMEM((rows, keys), jnp.float32)] + shared,
        ),
        out_shape=[
            jax.ShapeDtypeStruct((batches, rows, width), jnp.bfloat16),
            jax.ShapeDtypeStruct((batches, rows, width), jnp.float32),
            jax.ShapeDtypeStruct((batches, rows, pair), jnp.float32),
        ],
        compiler_params=pltpu.CompilerParams(vmem_limit_bytes=VMEM_LIMIT),
        cost_estimate=cost(2),
        name="attention_forward",
    )
    head_rows = -(-(width // HS) // 8) * 8
    all_columns = rows * (width // HS)
    run_backward = pl.pallas_call(
        backward,
        grid_spec=pltpu.PrefetchScalarGridSpec(
            num_scalar_prefetch=2,
            grid=(batches,),
            in_specs=[flow, blocks, blocks, flow, logs, flow],
            out_specs=[flow, blocks, blocks],
            scratch_shapes=[pltpu.VMEM((keys, rows), jnp.float32)]
            + shared
            + [
                pltpu.VMEM((HS, keys), jnp.bfloat16),
                pltpu.VMEM((head_rows, rows), jnp.float32),
                pltpu.VMEM((head_rows, rows), jnp.float32),
                pltpu.VMEM((keys, all_columns), jnp.bfloat16),
                pltpu.VMEM((keys, all_columns), jnp.bfloat16),
                pltpu.VMEM((all_columns, pair), jnp.bfloat16),
                pltpu.VMEM((all_columns, pair), jnp.bfloat16),
            ],
        ),
        out_shape=[
            jax.ShapeDtypeStruct((batches, rows, width), jnp.bfloat16),
            jax.ShapeDtypeStruct((half_parts, batches, rows, pair), jnp.bfloat16),
            jax.ShapeDtypeStruct((half_parts, batches, rows, pair), jnp.bfloat16),
        ],
        compiler_params=pltpu.CompilerParams(vmem_limit_bytes=VMEM_LIMIT),
        cost_estimate=cost(5),
        name="attention_backward",
    )
    return run_forward, run_backward


def ffn_kernels(rows, width, chunks, chunk):
    tile = 256
    tiles = rows // tile
    all_rows = 2 * rows
    any_spec = pl.BlockSpec(memory_space=pl.ANY)
    vmem = pl.BlockSpec(memory_space=pltpu.VMEM)
    params = pltpu.CompilerParams(vmem_limit_bytes=VMEM_LIMIT)

    def cost(products):
        return pl.CostEstimate(
            flops=2 * products * all_rows * width * chunks * chunk, bytes_accessed=12 << 20, transcendentals=0
        )

    def turn(refs, turned):
        for s, ref in enumerate(refs):
            for i in range(rows // 128):
                block = wide(ref[i * 128 : (i + 1) * 128, :])
                turned[:, s * rows + i * 128 : s * rows + (i + 1) * 128] = low(block.T)

    def first(*args):
        inputs, grads, bias_ref, weights = args[0:2], args[2:4], args[4], args[5 : 5 + chunks]
        act_ref, grad_ref = args[5 + chunks], args[6 + chunks]
        outs, bias_grad_ref = args[7 + chunks : 7 + 2 * chunks], args[7 + 2 * chunks]
        held, turned, sems = args[8 + 2 * chunks :]
        copies = [pltpu.make_async_copy(weights[m], held.at[m], sems.at[m]) for m in range(chunks)]
        for copy in copies:
            copy.start()
        turn(grads, turned)
        bias_grad_ref[...] = jnp.zeros_like(bias_grad_ref)
        for m in range(chunks):
            copies[m].wait()
            for s in range(2):

                def block(i, carry):
                    at = pl.multiple_of(i * tile, tile)
                    to = pl.ds(pl.multiple_of(s * rows + i * tile, tile), tile)
                    here = pl.ds(at, tile)
                    up = dot(inputs[s][here, :], held[m, 0]) + bias_ref[m : m + 1, :]
                    value, slope = gelu_both(up)
                    grad = low(dot(grads[s][here, :], held[m, 1]) * slope)
                    act_ref[m, to, :] = low(value)
                    grad_ref[m, to, :] = grad
                    bias_grad_ref[m : m + 1, :] += jnp.sum(wide(grad), axis=0, keepdims=True)
                    return carry

                lax.fori_loop(0, tiles, block, 0)

            def column(i, carry):
                here = pl.ds(pl.multiple_of(i * tile, tile), tile)
                outs[m][here, :] = low(dot(turned[here, :], act_ref[m]))
                return carry

            lax.fori_loop(0, width // tile, column, 0)

    def second(*args):
        inputs, grad_ref, weights = args[0:2], args[2], args[3 : 3 + chunks]
        own_ref, other_ref = args[3 + chunks : 5 + chunks]
        outs = args[5 + chunks : 5 + 2 * chunks]
        held, turned, sems = args[5 + 2 * chunks :]
        copies = [pltpu.make_async_copy(weights[m].at[0], held.at[m], sems.at[m]) for m in range(chunks)]
        for copy in copies:
            copy.start()
        turn(inputs, turned)
        for m in range(chunks):

            def column(i, carry):
                here = pl.ds(pl.multiple_of(i * tile, tile), tile)
                outs[m][here, :] = low(dot(turned[here, :], grad_ref[m]))
                return carry

            lax.fori_loop(0, width // tile, column, 0)
        for copy in copies:
            copy.wait()
        back(grad_ref, held, own_ref, other_ref)

    def back(source, held, own_ref, other_ref):
        for s, ref in enumerate((own_ref, other_ref)):

            def block(i, carry):
                here = pl.ds(pl.multiple_of(i * tile, tile), tile)
                there = pl.ds(pl.multiple_of(s * rows + i * tile, tile), tile)
                total = cols_dot(source[0, there, :], held[0])
                for m in range(1, chunks):
                    total = total + cols_dot(source[m, there, :], held[m])
                ref[here, :] = total.astype(ref.dtype)
                return carry

            lax.fori_loop(0, tiles, block, 0)

    def third(*args):
        act_ref, weights = args[0], args[1 : 1 + chunks]
        own_ref, other_ref, held, sems = args[1 + chunks :]
        copies = [pltpu.make_async_copy(weights[m].at[1], held.at[m], sems.at[m]) for m in range(chunks)]
        for copy in copies:
            copy.start()
        for copy in copies:
            copy.wait()
        back(act_ref, held, own_ref, other_ref)

    units = jax.ShapeDtypeStruct((chunks, all_rows, chunk), jnp.bfloat16)
    gradient = jax.ShapeDtypeStruct((width, chunk), jnp.bfloat16)
    own = jax.ShapeDtypeStruct((rows, width), jnp.float32)
    other = jax.ShapeDtypeStruct((rows, width), jnp.bfloat16)
    run_first = pl.pallas_call(
        first,
        in_specs=[vmem] * 5 + [any_spec] * chunks,
        out_specs=[vmem] * (3 + chunks),
        out_shape=[units, units] + [gradient] * chunks + [jax.ShapeDtypeStruct((chunks, chunk), jnp.float32)],
        scratch_shapes=[
            pltpu.VMEM((chunks, 2, width, chunk), jnp.bfloat16),
            pltpu.VMEM((width, all_rows), jnp.bfloat16),
            pltpu.SemaphoreType.DMA((chunks,)),
        ],
        compiler_params=params,
        cost_estimate=cost(3),
        name="ffn_first",
    )
    run_second = pl.pallas_call(
        second,
        in_specs=[vmem] * 3 + [any_spec] * chunks,
        out_specs=[vmem] * (2 + chunks),
        out_shape=[own, other] + [gradient] * chunks,
        scratch_shapes=[
            pltpu.VMEM((chunks, width, chunk), jnp.bfloat16),
            pltpu.VMEM((width, all_rows), jnp.bfloat16),
            pltpu.SemaphoreType.DMA((chunks,)),
        ],
        compiler_params=params,
        cost_estimate=cost(2),
        name="ffn_second",
    )
    run_third = pl.pallas_call(
        third,
        in_specs=[vmem] + [any_spec] * chunks,
        out_specs=[vmem] * 2,
        out_shape=[own, other],
        scratch_shapes=[
            pltpu.VMEM((chunks, width, chunk), jnp.bfloat16),
            pltpu.SemaphoreType.DMA((chunks,)),
        ],
        compiler_params=params,
        cost_estimate=cost(1),
        name="ffn_third",
    )
    return run_first, run_second, run_third


def ffn_update(rows, units, parts, chunk):
    per_row = 2 * units // 128
    step = 32
    lines = step * per_row

    def kernel(place_ref, *refs):
        pieces, (master, first, second) = refs[:parts], refs[parts : parts + 3]
        first_out, second_out, master_out = refs[parts + 3 :]
        place = place_ref[0]
        for k in range(parts):
            base = (place ^ k) * (2 * chunk // 128)
            for j in range(chunk // 128):
                for which in range(2):
                    here = pl.ds(base + 2 * j + which, step, per_row)
                    grad = wide(pieces[k][which, :, j * 128 : (j + 1) * 128])
                    got = adam_update(master[here, :], grad, first[here, :], second[here, :], 0.1, 0.1)
                    first_out[here, :] = got[0]
                    second_out[here, :] = got[1]
                    master_out[here, :] = got[2]

    block = pl.BlockSpec((lines, 128), lambda i, *_: (i, 0))
    piece = pl.BlockSpec((2, step, chunk), lambda i, *_: (0, i, 0))
    shape = jax.ShapeDtypeStruct((rows * per_row, 128), jnp.float32)
    call = pl.pallas_call(
        kernel,
        grid_spec=pltpu.PrefetchScalarGridSpec(
            num_scalar_prefetch=1,
            grid=(rows // step,),
            in_specs=[piece] * parts + [block] * 3,
            out_specs=[block] * 3,
        ),
        out_shape=[shape] * 3,
        compiler_params=pltpu.CompilerParams(vmem_limit_bytes=VMEM_LIMIT),
        cost_estimate=pl.CostEstimate(flops=0, bytes_accessed=rows * 2 * units * 26, transcendentals=0),
        name="ffn_update",
    )

    def fold(array):
        return jnp.swapaxes(array.reshape(rows, 2, units // 128, 128), 1, 2).reshape(-1, 128)

    def unfold(array):
        return jnp.swapaxes(array.reshape(rows, units // 128, 2, 128), 1, 2).reshape(rows, 2, units)

    def run(place, pieces, master, first, second):
        got = call(place, *pieces, fold(master), fold(first), fold(second))
        return tuple(unfold(array) for array in got)

    return run


def shards(
    tokens,
    doc_starts,
    attn_master,
    attn_mom,
    attn_sq,
    ffn_master,
    ffn_mom,
    ffn_sq,
    small_master,
    small_mom,
    small_sq,
    cotangent,
):
    ctx_count = lax.axis_size("ctx")
    ctx_place = lax.axis_index("ctx")
    wt_count = lax.axis_size("wt")
    batches, rows_here, width = tokens.shape
    heads = width // HS
    qkv_cols = width + 2 * HS
    all_rows = batches * rows_here
    shard_rows = attn_master.shape[0]
    piece_rows = shard_rows // ctx_count
    chunk = FF // ctx_count
    order = ctx_place ^ jnp.arange(ctx_count, dtype=jnp.int32)
    (
        gain_one,
        shift_one,
        gain_two,
        shift_two,
        bias_query,
        bias_out,
        bias_proj,
        bias_value,
        bias_hidden,
    ) = split_small(small_master)

    place = ctx_place[None].astype(jnp.int32)
    chips = ctx_count // 2

    def in_order(even, odd):
        buffer = jnp.zeros((ctx_count,) + even.shape[1:], even.dtype)
        for m in range(chips):
            buffer = put(buffer, even[m][None], ctx_place ^ (2 * m), 0)
            buffer = put(buffer, odd[m][None], ctx_place ^ (2 * m + 1), 0)
        return buffer

    attn_piece = low(take(attn_master, ctx_place, 0, piece_rows))

    def whole_rows(piece):
        blocks = in_order(*gather_ctx(gather_wt(piece[None], 0)))
        return jnp.swapaxes(blocks, 0, 1).reshape((width,) + piece.shape[1:])

    weight_qkv = whole_rows(attn_piece[:, :qkv_cols])
    ffn_piece = low(jnp.swapaxes(take(ffn_master, ctx_place, 2, chunk), 0, 1))
    ffn_parts = gather_chips(gather_wt(ffn_piece, 1))
    weight_out = whole_rows(attn_piece[:, qkv_cols:])
    bias_parts = bias_hidden.reshape(ctx_count, chunk)[order[::2]]
    back_low = cotangent.reshape(all_rows, width)
    back_rows = wide(back_low)
    back_other = xor_send(back_low, 1)

    run_forward, run_backward = attention_kernels(batches, rows_here, width, ctx_count)
    stream = wide(tokens.reshape(all_rows, width))
    normed, norm_back_one = jax.vjp(layer_norm, stream, gain_one, shift_one)
    normed_low = low(normed)
    mixed = dot(normed_low, weight_qkv)
    queries = low(mixed[:, :width] + bias_query).reshape(batches, rows_here, width)
    kv_bias = jnp.concatenate([jnp.zeros((HS,), jnp.float32), bias_value])
    kv_local = low(mixed[:, width:] + kv_bias).reshape(batches, rows_here, 2 * HS)
    kv_even, kv_odd = gather_ctx(kv_local)
    attended_low, attended, logs = run_forward(doc_starts, place, queries, kv_even, kv_odd)
    attended_low = attended_low.reshape(all_rows, width)
    hidden = stream + dot(attended_low, weight_out) + bias_out
    normed_two, norm_back_two = jax.vjp(layer_norm, hidden, gain_two, shift_two)
    normed_two_low = low(normed_two)
    normed_two_other = xor_send(normed_two_low, 1)

    ffn_first, ffn_second, ffn_third = ffn_kernels(all_rows, width, chips, chunk)
    act, grad_up, *rest = ffn_first(
        normed_two_low, normed_two_other, back_low, back_other, bias_parts, *ffn_parts
    )
    down_grads, hidden_grads = rest[:chips], rest[chips]
    own_part, other_part, *up_grads = ffn_second(normed_two_low, normed_two_other, grad_up, *ffn_parts)
    grad_normed_two = own_part + wide(xor_send(other_part, 1))
    own_part, other_part = ffn_third(act, *ffn_parts)
    down_vals = own_part + wide(xor_send(other_part, 1))
    layer_out = low(hidden + down_vals + bias_proj).reshape(batches, rows_here, width)
    down_part = scatter_wt(low(scatter_chips(down_grads)), 0)
    up_part = scatter_wt(low(scatter_chips(up_grads)), 0)
    ffn_part = jnp.stack([low(up_part), low(down_part)])
    ffn_even, ffn_odd = gather_ctx(ffn_part)

    grad_hidden_part, grad_gain_two, grad_shift_two = norm_back_two(grad_normed_two)
    grad_hidden = back_rows + grad_hidden_part
    grad_hidden_low = low(grad_hidden)
    grad_out = rows_dot(attended_low, grad_hidden_low)

    grad_attended = low(cols_dot(grad_hidden_low, weight_out)).reshape(batches, rows_here, width)
    grad_query, dkv_even, dkv_odd = run_backward(
        doc_starts, place, queries, kv_even, kv_odd, attended, logs, grad_attended
    )
    grad_query = grad_query.reshape(all_rows, width)
    grad_kv = low(scatter_ctx(dkv_even, dkv_odd)).reshape(all_rows, 2 * HS)

    def row_pieces(grad):
        blocks = grad.reshape(wt_count, ctx_count, piece_rows, grad.shape[1])
        pieces = [take(blocks, ctx_place ^ k, 1, 1)[:, 0] for k in range(ctx_count)]
        return jnp.stack(pieces[::2]), jnp.stack(pieces[1::2])

    grad_wide = jnp.concatenate([low(rows_dot(normed_low, grad_query)), low(grad_out)], axis=1)
    wide_part = low(scatter_wt(low(scatter_ctx(*row_pieces(grad_wide))), 0)[0])
    wide_total = wide(in_order(*gather_ctx(wide_part)).reshape(shard_rows, 2 * width))

    grad_normed = cols_dot(grad_query, weight_qkv[:, :width]) + cols_dot(grad_kv, weight_qkv[:, width:])
    grad_stream_part, grad_gain_one, grad_shift_one = norm_back_one(grad_normed)
    input_grad = (grad_hidden + grad_stream_part).reshape(batches, rows_here, width)

    own_units = jnp.zeros((ctx_count, chunk), jnp.float32)
    for m in range(chips):
        own_units = put(own_units, hidden_grads[m][None], ctx_place ^ (2 * m), 0)
    grad_small = jnp.concatenate(
        [
            grad_gain_one,
            grad_shift_one,
            grad_gain_two,
            grad_shift_two,
            jnp.sum(wide(grad_query), axis=0),
            jnp.sum(grad_hidden, axis=0),
            jnp.sum(back_rows, axis=0),
            jnp.sum(wide(grad_kv[:, HS:]), axis=0),
            own_units.reshape(FF),
        ]
    )
    small_size = grad_small.shape[0]
    lines = -(-small_size // (128 * ctx_count))
    small_blocks = jnp.pad(grad_small, (0, lines * 128 * ctx_count - small_size))
    small_blocks = small_blocks.reshape(ctx_count, lines, 128)
    kv_blocks = rows_dot(normed_low, grad_kv).reshape(wt_count, ctx_count, piece_rows, 2 * HS)
    kv_blocks = jnp.swapaxes(kv_blocks, 0, 1)
    small_blocks = jnp.broadcast_to(small_blocks[:, None], (ctx_count, wt_count, lines, 128))
    tail = jnp.concatenate([kv_blocks, small_blocks], axis=2)
    tail_pieces = [take(tail, ctx_place ^ k, 0, 1)[0] for k in range(ctx_count)]
    tail_even, tail_odd = jnp.stack(tail_pieces[::2]), jnp.stack(tail_pieces[1::2])
    tail_half = tail_even + xor_send(tail_odd, 1)
    tail_part = scatter_wt(scatter_chips([tail_half[m] for m in range(chips)]), 0)[0]
    tail_total = in_order(*gather_ctx(tail_part))
    kv_total = tail_total[:, :piece_rows].reshape(shard_rows, 2 * HS)
    small_total = tail_total[:, piece_rows:].reshape(-1)[:small_size]

    attn_total = jnp.concatenate([wide_total[:, :width], kv_total, wide_total[:, width:]], axis=1)
    attn_new = adam_update(attn_master, attn_total, attn_mom, attn_sq, 0.1, 0.1)
    if chunk % 128 == 0 and shard_rows % 32 == 0:
        pieces = [(ffn_even, ffn_odd)[k % 2][k // 2] for k in range(ctx_count)]
        ffn_new = ffn_update(shard_rows, FF, ctx_count, chunk)(place, pieces, ffn_master, ffn_mom, ffn_sq)
    else:
        ffn_total = jnp.transpose(in_order(ffn_even, ffn_odd), (2, 1, 0, 3)).reshape(shard_rows, 2, FF)
        ffn_new = adam_update(ffn_master, wide(ffn_total), ffn_mom, ffn_sq, 0.1, 0.1)
    small_new = adam_update(small_master, small_total, small_mom, small_sq, 1.0, 0.0)
    return (layer_out, input_grad) + attn_new + ffn_new + small_new


def solution(mesh):
    rows, cube = P("wt", None), P("wt", None, None)
    flow = P("wt", "ctx", None)
    in_specs = (flow, rows, rows, rows, rows, cube, cube, cube, P(), P(), P(), flow)
    out_specs = (flow, flow, rows, rows, rows, cube, cube, cube, P(), P(), P())
    return jax.shard_map(shards, mesh=mesh, in_specs=in_specs, out_specs=out_specs, check_vma=False)
```

```python
import jax
import jax.numpy as jnp
from jax import lax
from jax.experimental import pallas as pl
from jax.experimental.pallas import tpu as pltpu
from jax.sharding import PartitionSpec as P

D = 768
HS = 64
FF = 3072
STEP = 10


NORM_EPS = 1e-05
GELU_COEF = 0.7978845608028654
GELU_CUBE = 0.044715
BETA_ONE = 0.9
BETA_TWO = 0.95
ADAM_EPS = 1e-08
VMEM_LIMIT = 56 << 20


def layer_norm(values, gain, shift):
    centre = values - jnp.mean(values, axis=-1, keepdims=True)
    spread = jnp.mean(centre * centre, axis=-1, keepdims=True)
    return centre * lax.rsqrt(spread + NORM_EPS) * gain + shift


def gelu_both(u):
    inner = jnp.tanh(GELU_COEF * (u + GELU_CUBE * u * u * u))
    value = 0.5 * u * (1.0 + inner)
    slope = 0.5 * (1.0 + inner) + 0.5 * u * (1.0 - inner * inner) * (
        GELU_COEF * (1.0 + 3.0 * GELU_CUBE * u * u)
    )
    return value, slope


def split_small(small):
    return (
        small[0:D],
        small[D : 2 * D],
        small[2 * D : 3 * D],
        small[3 * D : 4 * D],
        small[4 * D : 5 * D],
        small[5 * D : 6 * D],
        small[6 * D : 7 * D],
        small[7 * D : 7 * D + HS],
        small[7 * D + HS :],
    )


def rows_dot(left, right):
    return lax.dot_general(
        left, right, (((0,), (0,)), ((), ())), preferred_element_type=jnp.float32
    )


def cols_dot(left, right):
    return lax.dot_general(
        left, right, (((1,), (1,)), ((), ())), preferred_element_type=jnp.float32
    )


def dot(left, right):
    return jnp.dot(left, right, preferred_element_type=jnp.float32)


def low(values):
    return values.astype(jnp.bfloat16)


def wide(values):
    return values.astype(jnp.float32)


def adam_update(master, gradient, first, second, step_rate, decay_rate):
    first_new = BETA_ONE * first + (1.0 - BETA_ONE) * gradient
    second_new = BETA_TWO * second + (1.0 - BETA_TWO) * gradient * gradient
    first_hat = first_new / (1.0 - BETA_ONE**STEP)
    second_hat = second_new / (1.0 - BETA_TWO**STEP)
    master_new = master - step_rate * (
        first_hat / (jnp.sqrt(second_hat) + ADAM_EPS) + decay_rate * master
    )
    return (first_new, second_new, master_new)


def xor_send(array, mask):
    count = lax.axis_size("ctx")
    return lax.ppermute(array, "ctx", [(i, i ^ mask) for i in range(count)])


def xor_wt(array, mask):
    count = lax.axis_size("wt")
    return lax.ppermute(array, "wt", [(i, i ^ mask) for i in range(count)])


def after(array, *others):
    return lax.optimization_barrier((array,) + others)[0]


def put(buffer, piece, place, axis):
    starts = [0] * buffer.ndim
    starts[axis] = place * piece.shape[axis]
    return lax.dynamic_update_slice(buffer, piece, starts)


def take(buffer, place, axis, size):
    return lax.dynamic_slice_in_dim(buffer, place * size, size, axis)


def gather_wt(piece):
    count, place = lax.axis_size("wt"), lax.axis_index("wt")
    buffer = put(jnp.zeros((count,) + piece.shape, piece.dtype), piece[None], place, 0)
    for mask in range(1, count):
        buffer = put(buffer, xor_wt(piece, mask)[None], place ^ mask, 0)
    return buffer


def gather_chips(piece):
    count = lax.axis_size("ctx")
    return [piece] + [xor_send(piece, mask) for mask in range(2, count, 2)]


def scatter_chips(pieces):
    total = wide(pieces[0])
    for m in range(1, len(pieces)):
        total = total + wide(xor_send(pieces[m], 2 * m))
    return total


def gather_ctx(piece):
    even = jnp.stack(gather_chips(piece))
    return even, xor_send(even, 1)


def scatter_ctx(even, odd):
    half = low(wide(even) + wide(xor_send(odd, 1)))
    return scatter_chips([half[m] for m in range(half.shape[0])])


def scatter_wt(array, axis):
    count, place = lax.axis_size("wt"), lax.axis_index("wt")
    size = array.shape[axis] // count
    total = wide(take(array, place, axis, size))
    for mask in range(1, count):
        total = total + wide(xor_wt(take(array, place ^ mask, axis, size), mask))
    return total


def attention_kernels(batches, rows, width, parts):
    half_parts = parts // 2
    keys = parts * rows
    pair = 2 * HS
    groups = width // (2 * pair)
    factor = HS ** (-0.5) * 1.4426950408889634
    masks = list(range(0, parts, 2)) + list(range(1, parts, 2))

    def lanes(shape):
        return lax.broadcasted_iota(jnp.int32, shape, 1)

    def spread(even_ref, odd_ref, key_ref, value_ref):
        for j in range(parts):
            ref = even_ref if j < half_parts else odd_ref
            block = wide(ref[j % half_parts, 0])
            turned = pltpu.roll(block, HS, 1)
            first = lanes(block.shape) < HS
            here = pl.ds(j * rows, rows)
            key_ref[0, here, :] = low(jnp.where(first, block, 0.0))
            key_ref[1, here, :] = low(jnp.where(first, 0.0, turned))
            value_ref[0, here, :] = low(jnp.where(first, turned, 0.0))
            value_ref[1, here, :] = low(jnp.where(first, 0.0, block))

    def doc_begin(starts_ref, stream, positions):
        begin = jnp.zeros_like(positions)
        for j in range(starts_ref.shape[1]):
            start = starts_ref[stream, j]
            begin = jnp.where(start <= positions, jnp.maximum(begin, start), begin)
        return begin

    def forward(starts_ref, place_ref, query_ref, even_ref, odd_ref, low_ref, full_ref, log_ref, cap, key, value):
        stream, place = pl.program_id(0), place_ref[0]
        spread(even_ref, odd_ref, key, value)
        query_pos = place * rows + lax.broadcasted_iota(jnp.int32, (rows, 1), 0)
        begin = doc_begin(starts_ref, stream, query_pos)
        for j, mask in enumerate(masks):
            key_pos = (place ^ mask) * rows + lax.broadcasted_iota(jnp.int32, (rows, rows), 1)
            allowed = (key_pos >= begin) & (key_pos <= query_pos)
            cap[:, j * rows : (j + 1) * rows] = jnp.where(allowed, 3.0e38, -1e30)
        log_ref[...] = jnp.zeros_like(log_ref)

        def group(g, carry):
            at = pl.multiple_of(g * 2 * pair, 2 * pair)
            both = query_ref[0, :, pl.ds(at, 2 * pair)]
            two = jnp.concatenate([both[:, :pair], both[:, pair:]], axis=0)
            limit = cap[...]
            limit = jnp.concatenate([limit, limit], axis=0)
            total = jnp.zeros((2 * rows, pair), jnp.float32)
            logs = log_ref[0]
            for half in range(2):
                scores = jnp.minimum(cols_dot(two, key[half]) * factor, limit)
                peak = jnp.max(scores, axis=1, keepdims=True)
                expo = jnp.exp2(scores - peak)
                norm = jnp.sum(expo, axis=1, keepdims=True)
                total = total + dot(low(expo), value[half]) / norm
                log = peak + jnp.log2(norm)
                column = lanes((rows, pair))
                logs = jnp.where(column == 4 * g + half, log[:rows], logs)
                logs = jnp.where(column == 4 * g + 2 + half, log[rows:], logs)
            log_ref[0] = logs
            total = jnp.concatenate([total[:rows], total[rows:]], axis=1)
            full_ref[0, :, pl.ds(at, 2 * pair)] = total
            low_ref[0, :, pl.ds(at, 2 * pair)] = low(total)
            return carry

        lax.fori_loop(0, groups, group, 0)

    def backward(
        starts_ref, place_ref, query_ref, even_ref, odd_ref, full_ref, log_ref, grad_ref,
        query_grad_ref, even_grad_ref, odd_grad_ref,
        cap, key, value, key_turned, log_rows, delta_rows, weight_buf, score_buf, query_buf, grad_buf,
    ):
        stream, place = pl.program_id(0), place_ref[0]
        spread(even_ref, odd_ref, key, value)
        query_pos = place * rows + lax.broadcasted_iota(jnp.int32, (1, rows), 1)
        begin = doc_begin(starts_ref, stream, query_pos)
        for j, mask in enumerate(masks):
            key_pos = (place ^ mask) * rows + lax.broadcasted_iota(jnp.int32, (rows, rows), 0)
            allowed = (key_pos >= begin) & (key_pos <= query_pos)
            cap[j * rows : (j + 1) * rows, :] = jnp.where(allowed, 3.0e38, -1e30)
            here = pl.ds(j * rows, rows)
            key_turned[:, j * rows : (j + 1) * rows] = low(wide(key[0, here, :]).T[:HS])
        log_rows[...] = log_ref[0].T[: log_rows.shape[0]]
        head_of = lax.broadcasted_iota(jnp.int32, (delta_rows.shape[0], width), 1) // HS
        chosen = (head_of == lax.broadcasted_iota(jnp.int32, (delta_rows.shape[0], width), 0)).astype(jnp.float32)
        delta_rows[...] = lax.dot_general(
            chosen, wide(grad_ref[0]) * full_ref[0], (((1,), (1,)), ((), ())),
            precision=lax.Precision.HIGHEST, preferred_element_type=jnp.float32,
        )
        first = lanes((2 * rows, pair)) < HS
        for g in range(groups):
            at = g * 2 * pair
            both, both_grad = query_ref[0, :, at : at + 2 * pair], grad_ref[0, :, at : at + 2 * pair]
            two = jnp.concatenate([both[:, :pair], both[:, pair:]], axis=0)
            two_grad = jnp.concatenate([both_grad[:, :pair], both_grad[:, pair:]], axis=0)
            limit = cap[...]
            limit = jnp.concatenate([limit, limit], axis=1)
            turned = []
            for half in range(2):
                h = 4 * g + half
                span = slice((2 * g + half) * 2 * rows, (2 * g + half + 1) * 2 * rows)
                keep = first if half == 0 else jnp.logical_not(first)
                query_buf[span, :] = low(jnp.where(keep, wide(two), 0.0))
                grad_buf[span, :] = low(jnp.where(keep, wide(two_grad), 0.0))
                log = jnp.concatenate([log_rows[h : h + 1, :], log_rows[h + 2 : h + 3, :]], axis=1)
                delta = jnp.concatenate([delta_rows[h : h + 1, :], delta_rows[h + 2 : h + 3, :]], axis=1)
                scores = jnp.minimum(cols_dot(key[half], two) * factor, limit)
                weights = jnp.exp2(scores - log)
                grad_scores = low(weights * (cols_dot(value[half], two_grad) - delta))
                weight_buf[:, span] = low(weights)
                score_buf[:, span] = grad_scores
                turned.append(dot(key_turned[...], grad_scores))
            turned = jnp.concatenate(turned, axis=0) * HS ** (-0.5)
            query_grad_ref[0, :, at : at + pair] = low(turned[:, :rows].T)
            query_grad_ref[0, :, at + pair : at + 2 * pair] = low(turned[:, rows:].T)
        for j in range(parts):
            here = pl.ds(j * rows, rows)
            value_sum = dot(weight_buf[here, :], grad_buf[...])
            key_sum = dot(score_buf[here, :], query_buf[...]) * HS ** (-0.5)
            value_sum = value_sum + pltpu.roll(value_sum, HS, 1)
            key_sum = key_sum + pltpu.roll(key_sum, HS, 1)
            ref = even_grad_ref if j < half_parts else odd_grad_ref
            ref[j % half_parts, 0] = low(jnp.where(lanes((rows, pair)) < HS, key_sum, value_sum))

    flow = pl.BlockSpec((1, rows, width), lambda b, *_: (b, 0, 0))
    logs = pl.BlockSpec((1, rows, pair), lambda b, *_: (b, 0, 0))
    blocks = pl.BlockSpec((half_parts, 1, rows, pair), lambda b, *_: (0, b, 0, 0))
    work = batches * rows * keys * (width // HS)

    def cost(products):
        return pl.CostEstimate(flops=work * 256 * products, bytes_accessed=8 << 20, transcendentals=work)

    shared = [
        pltpu.VMEM((2, keys, pair), jnp.bfloat16),
        pltpu.VMEM((2, keys, pair), jnp.bfloat16),
    ]
    run_forward = pl.pallas_call(
        forward,
        grid_spec=pltpu.PrefetchScalarGridSpec(
            num_scalar_prefetch=2,
            grid=(batches,),
            in_specs=[flow, blocks, blocks],
            out_specs=[flow, flow, logs],
            scratch_shapes=[pltpu.VMEM((rows, keys), jnp.float32)] + shared,
        ),
        out_shape=[
            jax.ShapeDtypeStruct((batches, rows, width), jnp.bfloat16),
            jax.ShapeDtypeStruct((batches, rows, width), jnp.float32),
            jax.ShapeDtypeStruct((batches, rows, pair), jnp.float32),
        ],
        compiler_params=pltpu.CompilerParams(vmem_limit_bytes=VMEM_LIMIT),
        cost_estimate=cost(2),
        name="attention_forward",
    )
    head_rows = -(-(width // HS) // 8) * 8
    all_columns = rows * (width // HS)
    run_backward = pl.pallas_call(
        backward,
        grid_spec=pltpu.PrefetchScalarGridSpec(
            num_scalar_prefetch=2,
            grid=(batches,),
            in_specs=[flow, blocks, blocks, flow, logs, flow],
            out_specs=[flow, blocks, blocks],
            scratch_shapes=[pltpu.VMEM((keys, rows), jnp.float32)]
            + shared
            + [
                pltpu.VMEM((HS, keys), jnp.bfloat16),
                pltpu.VMEM((head_rows, rows), jnp.float32),
                pltpu.VMEM((head_rows, rows), jnp.float32),
                pltpu.VMEM((keys, all_columns), jnp.bfloat16),
                pltpu.VMEM((keys, all_columns), jnp.bfloat16),
                pltpu.VMEM((all_columns, pair), jnp.bfloat16),
                pltpu.VMEM((all_columns, pair), jnp.bfloat16),
            ],
        ),
        out_shape=[
            jax.ShapeDtypeStruct((batches, rows, width), jnp.bfloat16),
            jax.ShapeDtypeStruct((half_parts, batches, rows, pair), jnp.bfloat16),
            jax.ShapeDtypeStruct((half_parts, batches, rows, pair), jnp.bfloat16),
        ],
        compiler_params=pltpu.CompilerParams(vmem_limit_bytes=VMEM_LIMIT),
        cost_estimate=cost(5),
        name="attention_backward",
    )
    return run_forward, run_backward


def ffn_kernels(rows, width, chunks, chunk, sources):
    units = chunks * chunk
    all_rows = 2 * rows
    arrays = 1 + max(source[0] for source in sources)
    block_rows = width * chunks // len(sources)
    any_spec = pl.BlockSpec(memory_space=pl.ANY)
    vmem = pl.BlockSpec(memory_space=pltpu.VMEM)
    params = pltpu.CompilerParams(vmem_limit_bytes=VMEM_LIMIT)
    span = chunk
    while span < 512 and units % (2 * span) == 0:
        span *= 2

    def cost(products):
        return pl.CostEstimate(
            flops=2 * products * all_rows * width * units, bytes_accessed=12 << 20, transcendentals=0
        )

    def fetch(weights, which, held, sem):
        copies = []
        for array, block, row, unit in sources:
            copies.append(
                pltpu.make_async_copy(
                    weights[array].at[block, pl.ds(which * block_rows, block_rows), :],
                    held.at[pl.ds(row * block_rows, block_rows), pl.ds(unit * chunk, chunk)],
                    sem.at[len(copies)],
                )
            )
        for copy in copies:
            copy.start()
        return copies

    def first(*args):
        inputs, grads, turned_ref, bias_ref, weights = args[0:2], args[2:4], args[4], args[5], args[6 : 6 + arrays]
        act_ref, grad_ref = args[6 + arrays : 8 + arrays]
        outs, bias_grad_ref = args[8 + arrays : 8 + arrays + chunks], args[8 + arrays + chunks]
        held_up, held_down, sems = args[9 + arrays + chunks :]
        copies = fetch(weights, 0, held_up, sems.at[0]) + fetch(weights, 1, held_down, sems.at[1])
        for copy in copies:
            copy.wait()
        for i in range(units // span):
            cols = slice(i * span, (i + 1) * span)
            sums = jnp.zeros((1, span), jnp.float32)
            for s in range(2):
                here = slice(s * rows, (s + 1) * rows)
                up = dot(inputs[s][...], held_up[:, cols]) + bias_ref[:, cols]
                value, slope = gelu_both(up)
                grad = dot(grads[s][...], held_down[:, cols]) * slope
                act_ref[here, cols] = low(value)
                grad_ref[here, cols] = low(grad)
                sums = sums + jnp.sum(grad, axis=0, keepdims=True)
            bias_grad_ref[:, cols] = sums
            total = low(dot(turned_ref[...], act_ref[:, cols]))
            for j in range(span // chunk):
                outs[i * (span // chunk) + j][...] = total[:, j * chunk : (j + 1) * chunk]

    def back(which):
        def kernel(*args):
            source, weights = args[0], args[1 : 1 + arrays]
            own_ref, other_ref, held, sems = args[1 + arrays :]
            for copy in fetch(weights, which, held, sems):
                copy.wait()
            own_ref[...] = cols_dot(source[:rows, :], held[...])
            other_ref[...] = low(cols_dot(source[rows:, :], held[...]))

        return pl.pallas_call(
            kernel,
            in_specs=[vmem] + [any_spec] * arrays,
            out_specs=[vmem] * 2,
            out_shape=[own, other],
            scratch_shapes=[
                pltpu.VMEM((width, units), jnp.bfloat16),
                pltpu.SemaphoreType.DMA((len(sources),)),
            ],
            compiler_params=params,
            cost_estimate=cost(1),
            name="ffn_back" if which == 0 else "ffn_down",
        )

    def third(*args):
        inputs, grad_ref, outs, turned = args[0:2], args[2], args[3 : 3 + chunks], args[3 + chunks]
        for s in range(2):
            for i in range(rows // 128):
                block = wide(inputs[s][i * 128 : (i + 1) * 128, :])
                turned[:, s * rows + i * 128 : s * rows + (i + 1) * 128] = low(block.T)
        for i in range(units // span):
            total = low(dot(turned[...], grad_ref[:, i * span : (i + 1) * span]))
            for j in range(span // chunk):
                outs[i * (span // chunk) + j][...] = total[:, j * chunk : (j + 1) * chunk]

    flow = jax.ShapeDtypeStruct((all_rows, units), jnp.bfloat16)
    gradient = jax.ShapeDtypeStruct((width, chunk), jnp.bfloat16)
    own = jax.ShapeDtypeStruct((rows, width), jnp.float32)
    other = jax.ShapeDtypeStruct((rows, width), jnp.bfloat16)
    run_first = pl.pallas_call(
        first,
        in_specs=[vmem] * 6 + [any_spec] * arrays,
        out_specs=[vmem] * (3 + chunks),
        out_shape=[flow, flow] + [gradient] * chunks + [jax.ShapeDtypeStruct((1, units), jnp.float32)],
        scratch_shapes=[
            pltpu.VMEM((width, units), jnp.bfloat16),
            pltpu.VMEM((width, units), jnp.bfloat16),
            pltpu.SemaphoreType.DMA((2, len(sources))),
        ],
        compiler_params=params,
        cost_estimate=cost(3),
        name="ffn_first",
    )
    run_third = pl.pallas_call(
        third,
        in_specs=[vmem] * 3,
        out_specs=[vmem] * chunks,
        out_shape=[gradient] * chunks,
        scratch_shapes=[pltpu.VMEM((width, all_rows), jnp.bfloat16)],
        compiler_params=params,
        cost_estimate=cost(1),
        name="ffn_grads",
    )
    return run_first, back(0), run_third, back(1)


def ffn_plain(chunks, chunk):
    def first(own, other, grad_own, grad_other, turned, bias, up, down):
        value, slope = gelu_both(dot(jnp.concatenate([own, other]), up) + bias)
        grad = low(dot(jnp.concatenate([grad_own, grad_other]), down) * slope)
        act = low(value)
        sums = jnp.sum(wide(grad), axis=0, keepdims=True)
        return [act, grad] + jnp.split(low(dot(turned, act)), chunks, axis=1) + [sums]

    def back(source, weights):
        own, other = jnp.split(cols_dot(source, weights), 2)
        return own, low(other)

    def third(own, other, grad):
        return jnp.split(low(rows_dot(jnp.concatenate([own, other]), grad)), chunks, axis=1)

    return first, back, third, back


def attn_grads(rows, width, row_groups, parts, piece):
    def kernel(place_ref, left_a, right_a, left_b, right_b, even_ref, odd_ref, turned, total):
        place = place_ref[0]
        for n, (left, right) in enumerate(((left_a, right_a), (left_b, right_b))):
            for i in range(rows // 128):
                turned[:, i * 128 : (i + 1) * 128] = low(wide(left[i * 128 : (i + 1) * 128, :]).T)
            total[:, n * width : (n + 1) * width] = dot(turned[...], right[...])
        for k in range(parts):
            ref = odd_ref if k % 2 else even_ref
            for w in range(row_groups):
                at = pl.multiple_of(w * piece * parts + (place ^ k) * piece, 8)
                ref[k // 2, w] = low(total[pl.ds(at, piece), :])

    vmem = pl.BlockSpec(memory_space=pltpu.VMEM)
    shape = jax.ShapeDtypeStruct((parts // 2, row_groups, piece, 2 * width), jnp.bfloat16)
    return pl.pallas_call(
        kernel,
        grid_spec=pltpu.PrefetchScalarGridSpec(
            num_scalar_prefetch=1,
            grid=(),
            in_specs=[vmem] * 4,
            out_specs=[vmem] * 2,
            scratch_shapes=[pltpu.VMEM((width, rows), jnp.bfloat16), pltpu.VMEM((width, 2 * width), jnp.float32)],
        ),
        out_shape=[shape] * 2,
        compiler_params=pltpu.CompilerParams(vmem_limit_bytes=VMEM_LIMIT),
        cost_estimate=pl.CostEstimate(flops=4 * rows * width * width, bytes_accessed=6 << 20, transcendentals=0),
        name="attn_grads",
    )


def attn_update(rows, columns, width, parts, piece, lines):
    qkv = columns - width

    def kernel(place_ref, even_ref, odd_ref, tail_even_ref, tail_odd_ref, master, first, second, *outs):
        place = place_ref[0]
        for k in range(parts):
            ref, tail_ref = (odd_ref, tail_odd_ref) if k % 2 else (even_ref, tail_even_ref)
            here = pl.ds(pl.multiple_of((place ^ k) * piece, 8), piece)
            for cols, grad in (
                (slice(0, width), wide(ref[k // 2, :, :width])),
                (slice(width, qkv), tail_ref[k // 2, :piece, :]),
                (slice(qkv, columns), wide(ref[k // 2, :, width:])),
            ):
                got = adam_update(master[here, cols], grad, first[here, cols], second[here, cols], 0.1, 0.1)
                outs[0][here, cols] = got[0]
                outs[1][here, cols] = got[1]
                outs[2][here, cols] = got[2]

    vmem = pl.BlockSpec(memory_space=pltpu.VMEM)
    return pl.pallas_call(
        kernel,
        grid_spec=pltpu.PrefetchScalarGridSpec(
            num_scalar_prefetch=1, grid=(), in_specs=[vmem] * 7, out_specs=[vmem] * 3, scratch_shapes=[]
        ),
        out_shape=[jax.ShapeDtypeStruct((rows, columns), jnp.float32)] * 3,
        compiler_params=pltpu.CompilerParams(vmem_limit_bytes=VMEM_LIMIT),
        cost_estimate=pl.CostEstimate(flops=0, bytes_accessed=rows * columns * 26, transcendentals=0),
        name="attn_update",
    )


def ffn_update(rows, units, parts, chunk):
    per_row = 2 * units // 128
    step = 32
    lines = step * per_row

    def kernel(place_ref, *refs):
        pieces, (master, first, second) = refs[:parts], refs[parts : parts + 3]
        first_out, second_out, master_out = refs[parts + 3 :]
        place = place_ref[0]
        for k in range(parts):
            base = (place ^ k) * (2 * chunk // 128)
            for j in range(chunk // 128):
                for which in range(2):
                    here = pl.ds(base + 2 * j + which, step, per_row)
                    grad = wide(pieces[k][which, :, j * 128 : (j + 1) * 128])
                    got = adam_update(master[here, :], grad, first[here, :], second[here, :], 0.1, 0.1)
                    first_out[here, :] = got[0]
                    second_out[here, :] = got[1]
                    master_out[here, :] = got[2]

    block = pl.BlockSpec((lines, 128), lambda i, *_: (i, 0))
    piece = pl.BlockSpec((2, step, chunk), lambda i, *_: (0, i, 0))
    shape = jax.ShapeDtypeStruct((rows * per_row, 128), jnp.float32)
    call = pl.pallas_call(
        kernel,
        grid_spec=pltpu.PrefetchScalarGridSpec(
            num_scalar_prefetch=1,
            grid=(rows // step,),
            in_specs=[piece] * parts + [block] * 3,
            out_specs=[block] * 3,
        ),
        out_shape=[shape] * 3,
        compiler_params=pltpu.CompilerParams(vmem_limit_bytes=VMEM_LIMIT),
        cost_estimate=pl.CostEstimate(flops=0, bytes_accessed=rows * 2 * units * 26, transcendentals=0),
        name="ffn_update",
    )

    def fold(array):
        return jnp.swapaxes(array.reshape(rows, 2, units // 128, 128), 1, 2).reshape(-1, 128)

    def unfold(array):
        return jnp.swapaxes(array.reshape(rows, units // 128, 2, 128), 1, 2).reshape(rows, 2, units)

    def run(place, pieces, master, first, second):
        got = call(place, *pieces, fold(master), fold(first), fold(second))
        return tuple(unfold(array) for array in got)

    return run


def shards(
    tokens,
    doc_starts,
    attn_master,
    attn_mom,
    attn_sq,
    ffn_master,
    ffn_mom,
    ffn_sq,
    small_master,
    small_mom,
    small_sq,
    cotangent,
):
    ctx_count = lax.axis_size("ctx")
    ctx_place = lax.axis_index("ctx")
    wt_count = lax.axis_size("wt")
    batches, rows_here, width = tokens.shape
    heads = width // HS
    qkv_cols = width + 2 * HS
    all_rows = batches * rows_here
    shard_rows = attn_master.shape[0]
    piece_rows = shard_rows // ctx_count
    chunk = FF // ctx_count
    order = ctx_place ^ jnp.arange(ctx_count, dtype=jnp.int32)
    (
        gain_one,
        shift_one,
        gain_two,
        shift_two,
        bias_query,
        bias_out,
        bias_proj,
        bias_value,
        bias_hidden,
    ) = split_small(small_master)

    place = ctx_place[None].astype(jnp.int32)
    chips = ctx_count // 2

    def in_order(even, odd):
        buffer = jnp.zeros((ctx_count,) + even.shape[1:], even.dtype)
        for m in range(chips):
            buffer = put(buffer, even[m][None], ctx_place ^ (2 * m), 0)
            buffer = put(buffer, odd[m][None], ctx_place ^ (2 * m + 1), 0)
        return buffer

    fitted = chunk % 128 == 0 and shard_rows % 32 == 0 and piece_rows % 8 == 0

    attn_piece = low(take(attn_master, ctx_place, 0, piece_rows))
    qkv_blocks = in_order(*gather_ctx(gather_wt(attn_piece[:, :qkv_cols])))
    weight_qkv = jnp.swapaxes(qkv_blocks, 0, 1).reshape(width, qkv_cols)
    ffn_piece = low(jnp.swapaxes(take(ffn_master, ctx_place, 2, chunk), 0, 1)).reshape(2 * shard_rows, chunk)
    rest_piece = jnp.concatenate([ffn_piece, attn_piece[:, qkv_cols:].reshape(-1, chunk)])
    rest = gather_wt(rest_piece)
    back_low = cotangent.reshape(all_rows, width)
    back_rows = wide(back_low)
    back_other = xor_send(back_low, 1)
    back_turned = jnp.concatenate([back_low, back_other]).T
    bias_parts = bias_hidden.reshape(ctx_count, chunk)[order[::2]].reshape(1, chips * chunk)

    run_forward, run_backward = attention_kernels(batches, rows_here, width, ctx_count)
    stream = wide(tokens.reshape(all_rows, width))
    normed, norm_back_one = jax.vjp(layer_norm, stream, gain_one, shift_one)
    normed_low = low(normed)
    mixed = dot(normed_low, weight_qkv)
    queries = low(mixed[:, :width] + bias_query).reshape(batches, rows_here, width)
    kv_bias = jnp.concatenate([jnp.zeros((HS,), jnp.float32), bias_value])
    kv_local = low(mixed[:, width:] + kv_bias).reshape(batches, rows_here, 2 * HS)
    if chips == 4:
        along_x, along_y = xor_send(rest, 2), xor_send(rest, 4)
    kv_even, kv_odd = gather_ctx(kv_local)
    if chips == 4:
        count = wt_count // 2
        from_y = xor_send(after(along_x[:count], kv_even), 4)
        from_x = xor_send(after(along_y[count:], kv_even), 2)
        out_rows = [along[:, 2 * shard_rows :] for along in (rest, along_x, along_y, from_y, from_x)]
        out_rows = out_rows[:3] + [jnp.concatenate(out_rows[3:])]
        rest_parts = (rest, along_x, along_y, from_y, from_x)
        sources = [(m, w, w, m) for m in range(3) for w in range(wt_count)]
        sources += [(3 + w // count, w % count, w, 3) for w in range(wt_count)]
    else:
        rest_parts = gather_chips(rest)
        out_rows = [part[:, 2 * shard_rows :] for part in rest_parts]
        sources = [(m, w, w, m) for m in range(chips) for w in range(wt_count)]
    out_even = jnp.stack(out_rows)
    out_blocks = in_order(out_even, xor_send(out_even, 1))
    out_blocks = out_blocks.reshape(ctx_count, wt_count, piece_rows, width)
    weight_out = jnp.swapaxes(out_blocks, 0, 1).reshape(width, width)
    attended_low, attended, logs = run_forward(doc_starts, place, queries, kv_even, kv_odd)
    attended_low = attended_low.reshape(all_rows, width)
    hidden = stream + dot(attended_low, weight_out) + bias_out
    normed_two, norm_back_two = jax.vjp(layer_norm, hidden, gain_two, shift_two)
    normed_two_low = low(normed_two)
    normed_two_other = xor_send(normed_two_low, 1)

    if fitted:
        ffn_first, ffn_back, ffn_third, ffn_down = ffn_kernels(all_rows, width, chips, chunk, sources)
        up_weights = down_weights = rest_parts
    else:
        ffn_first, ffn_back, ffn_third, ffn_down = ffn_plain(chips, chunk)
        up_weights = (jnp.concatenate([p[:, :shard_rows].reshape(width, chunk) for p in rest_parts], axis=1),)
        down_weights = (
            jnp.concatenate([p[:, shard_rows : 2 * shard_rows].reshape(width, chunk) for p in rest_parts], axis=1),
        )
    both_weights = rest_parts if fitted else up_weights + down_weights
    act, grad_up, *got = ffn_first(
        normed_two_low, normed_two_other, back_low, back_other, back_turned, bias_parts, *both_weights
    )
    down_grads, hidden_grads = got[:chips], got[chips].reshape(chips, chunk)
    own_part, other_part = ffn_back(grad_up, *up_weights)
    other_part = xor_send(other_part, 1)
    up_grads = ffn_third(normed_two_low, normed_two_other, grad_up)
    grad_normed_two = own_part + wide(other_part)
    own_part, other_part = ffn_down(act, *down_weights)
    down_vals = own_part + wide(xor_send(other_part, 1))
    layer_out = low(hidden + down_vals + bias_proj).reshape(batches, rows_here, width)

    grad_hidden_part, grad_gain_two, grad_shift_two = norm_back_two(grad_normed_two)
    grad_hidden = back_rows + grad_hidden_part
    grad_hidden_low = low(grad_hidden)
    grad_attended = low(cols_dot(grad_hidden_low, weight_out)).reshape(batches, rows_here, width)

    if chips == 4:
        met = after(xor_send(down_grads[3], 4), up_grads[0])
        down_along_x = xor_send(low(wide(down_grads[1]) + wide(met)), 2)
        down_along_y = xor_send(down_grads[2], 4)
        met = after(xor_send(up_grads[3], 2), grad_attended)
        up_along_x = xor_send(up_grads[1], 2)
        up_along_y = xor_send(low(wide(up_grads[2]) + wide(met)), 4)

    grad_query, dkv_even, dkv_odd = run_backward(
        doc_starts, place, queries, kv_even, kv_odd, attended, logs, grad_attended
    )
    grad_query = grad_query.reshape(all_rows, width)
    grad_kv = low(scatter_ctx(dkv_even, dkv_odd)).reshape(all_rows, 2 * HS)

    if chips == 4:
        down_along_x, down_along_y = after(down_along_x, dkv_odd), after(down_along_y, dkv_odd)
        up_along_x, up_along_y = after(up_along_x, dkv_odd), after(up_along_y, dkv_odd)
        down_sum = wide(down_grads[0]) + wide(down_along_x) + wide(down_along_y)
        up_sum = wide(up_grads[0]) + wide(up_along_x) + wide(up_along_y)
    else:
        down_sum, up_sum = scatter_chips(down_grads), scatter_chips(up_grads)
    both_sums = jnp.stack([low(up_sum), low(down_sum)]).reshape(2, wt_count, shard_rows, chunk)
    ffn_part = low(scatter_wt(both_sums, 1)[:, 0])
    ffn_even, ffn_odd = gather_ctx(ffn_part)

    if fitted:
        wide_even, wide_odd = attn_grads(all_rows, width, wt_count, ctx_count, piece_rows)(
            place, normed_low, grad_query, attended_low, grad_hidden_low
        )
    else:
        grad_wide = jnp.concatenate(
            [low(rows_dot(normed_low, grad_query)), low(rows_dot(attended_low, grad_hidden_low))], axis=1
        )
        grad_wide = grad_wide.reshape(wt_count, ctx_count, piece_rows, 2 * width)
        pieces = [take(grad_wide, ctx_place ^ k, 1, 1)[:, 0] for k in range(ctx_count)]
        wide_even, wide_odd = jnp.stack(pieces[::2]), jnp.stack(pieces[1::2])
    wide_part = low(scatter_wt(low(scatter_ctx(wide_even, wide_odd)), 0)[0])
    wide_even, wide_odd = gather_ctx(wide_part)

    grad_normed = cols_dot(grad_query, weight_qkv[:, :width]) + cols_dot(grad_kv, weight_qkv[:, width:])
    grad_stream_part, grad_gain_one, grad_shift_one = norm_back_one(grad_normed)
    input_grad = (grad_hidden + grad_stream_part).reshape(batches, rows_here, width)

    own_units = jnp.zeros((ctx_count, chunk), jnp.float32)
    for m in range(chips):
        own_units = put(own_units, hidden_grads[m][None], ctx_place ^ (2 * m), 0)
    grad_small = jnp.concatenate(
        [
            grad_gain_one,
            grad_shift_one,
            grad_gain_two,
            grad_shift_two,
            jnp.sum(wide(grad_query), axis=0),
            jnp.sum(grad_hidden, axis=0),
            jnp.sum(back_rows, axis=0),
            jnp.sum(wide(grad_kv[:, HS:]), axis=0),
            own_units.reshape(FF),
        ]
    )
    small_size = grad_small.shape[0]
    lines = -(-small_size // (128 * ctx_count))
    small_blocks = jnp.pad(grad_small, (0, lines * 128 * ctx_count - small_size))
    small_blocks = small_blocks.reshape(ctx_count, lines, 128)
    kv_blocks = rows_dot(normed_low, grad_kv).reshape(wt_count, ctx_count, piece_rows, 2 * HS)
    kv_blocks = jnp.swapaxes(kv_blocks, 0, 1)
    small_blocks = jnp.broadcast_to(small_blocks[:, None], (ctx_count, wt_count, lines, 128))
    tail = jnp.concatenate([kv_blocks, small_blocks], axis=2)
    tail_pieces = [take(tail, ctx_place ^ k, 0, 1)[0] for k in range(ctx_count)]
    tail_even, tail_odd = jnp.stack(tail_pieces[::2]), jnp.stack(tail_pieces[1::2])
    tail_half = tail_even + xor_send(tail_odd, 1)
    tail_part = scatter_wt(scatter_chips([tail_half[m] for m in range(chips)]), 0)[0]
    tail_even, tail_odd = gather_ctx(tail_part)
    tail_total = in_order(tail_even, tail_odd)
    small_total = tail_total[:, piece_rows:].reshape(-1)[:small_size]

    if fitted:
        attn_new = attn_update(shard_rows, attn_master.shape[1], width, ctx_count, piece_rows, lines)(
            place, wide_even, wide_odd, tail_even, tail_odd, attn_master, attn_mom, attn_sq
        )
        pieces = [(ffn_even, ffn_odd)[k % 2][k // 2] for k in range(ctx_count)]
        ffn_new = ffn_update(shard_rows, FF, ctx_count, chunk)(place, pieces, ffn_master, ffn_mom, ffn_sq)
    else:
        kv_total = tail_total[:, :piece_rows].reshape(shard_rows, 2 * HS)
        wide_total = wide(in_order(wide_even, wide_odd).reshape(shard_rows, 2 * width))
        attn_total = jnp.concatenate([wide_total[:, :width], kv_total, wide_total[:, width:]], axis=1)
        attn_new = adam_update(attn_master, attn_total, attn_mom, attn_sq, 0.1, 0.1)
        ffn_total = jnp.transpose(in_order(ffn_even, ffn_odd), (2, 1, 0, 3)).reshape(shard_rows, 2, FF)
        ffn_new = adam_update(ffn_master, wide(ffn_total), ffn_mom, ffn_sq, 0.1, 0.1)
    small_new = adam_update(small_master, small_total, small_mom, small_sq, 1.0, 0.0)
    return (layer_out, input_grad) + tuple(attn_new) + tuple(ffn_new) + small_new


def solution(mesh):
    rows, cube = P("wt", None), P("wt", None, None)
    flow = P("wt", "ctx", None)
    in_specs = (flow, rows, rows, rows, rows, cube, cube, cube, P(), P(), P(), flow)
    out_specs = (flow, flow, rows, rows, rows, cube, cube, cube, P(), P(), P())
    return jax.shard_map(shards, mesh=mesh, in_specs=in_specs, out_specs=out_specs, check_vma=False)
```

```python
import jax
import jax.numpy as jnp
from jax import lax
from jax.experimental import pallas as pl
from jax.experimental.pallas import tpu as pltpu
from jax.sharding import PartitionSpec as P

D = 768
HS = 64
FF = 3072
STEP = 10


NORM_EPS = 1e-05
GELU_COEF = 0.7978845608028654
GELU_CUBE = 0.044715
BETA_ONE = 0.9
BETA_TWO = 0.95
ADAM_EPS = 1e-08
MIB = 1 << 20
NO_COST = pl.CostEstimate(flops=0, bytes_accessed=0, transcendentals=0)


def layer_norm(values, gain, shift):
    centre = values - jnp.mean(values, axis=-1, keepdims=True)
    spread = jnp.mean(centre * centre, axis=-1, keepdims=True)
    return centre * lax.rsqrt(spread + NORM_EPS) * gain + shift


def gelu_both(u):
    square = u * u
    share = 0.5 * jnp.tanh(u * (GELU_COEF * GELU_CUBE * square + GELU_COEF)) + 0.5
    bend = u * (6.0 * GELU_COEF * GELU_CUBE * square + 2.0 * GELU_COEF)
    return u * share, share * ((1.0 - share) * bend) + share


def split_small(small):
    return (
        small[0:D],
        small[D : 2 * D],
        small[2 * D : 3 * D],
        small[3 * D : 4 * D],
        small[4 * D : 5 * D],
        small[5 * D : 6 * D],
        small[6 * D : 7 * D],
        small[7 * D : 7 * D + HS],
        small[7 * D + HS :],
    )


def rows_dot(left, right):
    return lax.dot_general(
        left, right, (((0,), (0,)), ((), ())), preferred_element_type=jnp.float32
    )


def cols_dot(left, right):
    return lax.dot_general(
        left, right, (((1,), (1,)), ((), ())), preferred_element_type=jnp.float32
    )


def dot(left, right):
    return jnp.dot(left, right, preferred_element_type=jnp.float32)


def low(values):
    return values.astype(jnp.bfloat16)


def wide(values):
    return values.astype(jnp.float32)


def adam_update(master, gradient, first, second, step_rate, decay_rate):
    first_new = BETA_ONE * first + (1.0 - BETA_ONE) * gradient
    second_new = BETA_TWO * second + (1.0 - BETA_TWO) * gradient * gradient
    first_hat = first_new / (1.0 - BETA_ONE**STEP)
    second_hat = second_new / (1.0 - BETA_TWO**STEP)
    master_new = master - step_rate * (
        first_hat / (jnp.sqrt(second_hat) + ADAM_EPS) + decay_rate * master
    )
    return (first_new, second_new, master_new)


def xor_send(array, mask):
    count = lax.axis_size("ctx")
    return lax.ppermute(array, "ctx", [(i, i ^ mask) for i in range(count)])


def xor_wt(array, mask):
    count = lax.axis_size("wt")
    return lax.ppermute(array, "wt", [(i, i ^ mask) for i in range(count)])


def after(array, *others):
    return lax.optimization_barrier((array,) + others)[0]


def put(buffer, piece, place, axis):
    starts = [0] * buffer.ndim
    starts[axis] = place * piece.shape[axis]
    return lax.dynamic_update_slice(buffer, piece, starts)


def take(buffer, place, axis, size):
    return lax.dynamic_slice_in_dim(buffer, place * size, size, axis)


def gather_wt(piece):
    count, place = lax.axis_size("wt"), lax.axis_index("wt")
    buffer = put(jnp.zeros((count,) + piece.shape, piece.dtype), piece[None], place, 0)
    for mask in range(1, count):
        buffer = put(buffer, xor_wt(piece, mask)[None], place ^ mask, 0)
    return buffer


def gather_wt_halves(piece):
    count, place = lax.axis_size("wt"), lax.axis_index("wt")
    half = count // 2
    near = jnp.zeros((half,) + piece.shape, piece.dtype)
    far = near
    near = put(near, piece[None], place % half, 0)
    for mask in range(1, half):
        near = put(near, xor_wt(piece, mask)[None], (place ^ mask) % half, 0)
    for mask in range(half, count):
        far = put(far, xor_wt(piece, mask)[None], (place ^ mask) % half, 0)
    return near, far


def gather_chips(piece):
    count = lax.axis_size("ctx")
    return [piece] + [xor_send(piece, mask) for mask in range(2, count, 2)]


def scatter_chips(pieces):
    total = wide(pieces[0])
    for m in range(1, len(pieces)):
        total = total + wide(xor_send(pieces[m], 2 * m))
    return total


def gather_ctx(piece):
    even = jnp.stack(gather_chips(piece))
    return even, xor_send(even, 1)


def scatter_ctx(even, odd):
    half = low(wide(even) + wide(xor_send(odd, 1)))
    return scatter_chips([half[m] for m in range(half.shape[0])])


def scatter_wt(array, axis):
    count, place = lax.axis_size("wt"), lax.axis_index("wt")
    size = array.shape[axis] // count
    total = wide(take(array, place, axis, size))
    for mask in range(1, count):
        total = total + wide(xor_wt(take(array, place ^ mask, axis, size), mask))
    return total


def attention_kernels(batches, rows, width, parts, runs):
    half_parts = parts // 2
    keys = parts * rows
    pair = 2 * HS
    groups = width // (2 * pair)
    factor = HS ** (-0.5) * 1.4426950408889634
    masks = list(range(0, parts, 2)) + list(range(1, parts, 2))

    def lanes(shape):
        return lax.broadcasted_iota(jnp.int32, shape, 1)

    def spread(even_ref, odd_ref, key_ref, value_ref):
        for j in range(parts):
            ref = even_ref if j < half_parts else odd_ref
            block = wide(ref[j % half_parts, 0])
            turned = pltpu.roll(block, HS, 1)
            first = lanes(block.shape) < HS
            here = pl.ds(j * rows, rows)
            key_ref[0, here, :] = low(jnp.where(first, block, 0.0))
            key_ref[1, here, :] = low(jnp.where(first, 0.0, turned))
            value_ref[0, here, :] = low(jnp.where(first, turned, 0.0))
            value_ref[1, here, :] = low(jnp.where(first, 0.0, block))

    def doc_begin(starts_ref, stream, positions):
        begin = jnp.zeros_like(positions)
        for j in range(starts_ref.shape[1]):
            start = starts_ref[stream, j]
            begin = jnp.where(start <= positions, jnp.maximum(begin, start), begin)
        return begin

    def forward(starts_ref, place_ref, query_ref, even_ref, odd_ref, low_ref, full_ref, log_ref, cap, key, value):
        stream, place = pl.program_id(0), place_ref[0]
        spread(even_ref, odd_ref, key, value)
        query_pos = place * rows + lax.broadcasted_iota(jnp.int32, (rows, 1), 0)
        begin = doc_begin(starts_ref, stream, query_pos)
        for j, mask in enumerate(masks):
            key_pos = (place ^ mask) * rows + lax.broadcasted_iota(jnp.int32, (rows, rows), 1)
            allowed = (key_pos >= begin) & (key_pos <= query_pos)
            cap[:, j * rows : (j + 1) * rows] = jnp.where(allowed, 3.0e38, -1e30)
        log_ref[...] = jnp.zeros_like(log_ref)

        def group(g, carry):
            at = pl.multiple_of(g * 2 * pair, 2 * pair)
            both = query_ref[0, :, pl.ds(at, 2 * pair)]
            two = jnp.concatenate([both[:, :pair], both[:, pair:]], axis=0)
            limit = cap[...]
            limit = jnp.concatenate([limit, limit], axis=0)
            total = jnp.zeros((2 * rows, pair), jnp.float32)
            logs = log_ref[0]
            for half in range(2):
                scores = jnp.minimum(cols_dot(two, key[half]) * factor, limit)
                peak = jnp.max(scores, axis=1, keepdims=True)
                expo = jnp.exp2(scores - peak)
                norm = jnp.sum(expo, axis=1, keepdims=True)
                total = total + dot(low(expo), value[half]) / norm
                log = peak + jnp.log2(norm)
                column = lanes((rows, pair))
                logs = jnp.where(column == 4 * g + half, log[:rows], logs)
                logs = jnp.where(column == 4 * g + 2 + half, log[rows:], logs)
            log_ref[0] = logs
            total = jnp.concatenate([total[:rows], total[rows:]], axis=1)
            full_ref[0, :, pl.ds(at, 2 * pair)] = total
            low_ref[0, :, pl.ds(at, 2 * pair)] = low(total)
            return carry

        lax.fori_loop(0, groups, group, 0, unroll=True)

    def backward(
        starts_ref, place_ref, query_ref, even_ref, odd_ref, full_ref, log_ref, grad_ref,
        query_grad_ref, even_grad_ref, odd_grad_ref,
        cap, key, value, key_turned, log_rows, delta_rows, weight_buf, score_buf, query_buf, grad_buf,
    ):
        stream, place = pl.program_id(0) + place_ref[1], place_ref[0]
        spread(even_ref, odd_ref, key, value)
        query_pos = place * rows + lax.broadcasted_iota(jnp.int32, (1, rows), 1)
        begin = doc_begin(starts_ref, stream, query_pos)
        for j, mask in enumerate(masks):
            key_pos = (place ^ mask) * rows + lax.broadcasted_iota(jnp.int32, (rows, rows), 0)
            allowed = (key_pos >= begin) & (key_pos <= query_pos)
            cap[j * rows : (j + 1) * rows, :] = jnp.where(allowed, 3.0e38, -1e30)
            here = pl.ds(j * rows, rows)
            key_turned[:, j * rows : (j + 1) * rows] = low(wide(key[0, here, :]).T[:HS])
        log_rows[...] = log_ref[0].T[: log_rows.shape[0]]
        head_of = lax.broadcasted_iota(jnp.int32, (delta_rows.shape[0], width), 1) // HS
        chosen = (head_of == lax.broadcasted_iota(jnp.int32, (delta_rows.shape[0], width), 0)).astype(jnp.float32)
        delta_rows[...] = lax.dot_general(
            chosen, wide(grad_ref[0]) * full_ref[0], (((1,), (1,)), ((), ())),
            precision=lax.Precision.HIGHEST, preferred_element_type=jnp.float32,
        )
        first = lanes((2 * rows, pair)) < HS
        for g in range(groups):
            at = g * 2 * pair
            both, both_grad = query_ref[0, :, at : at + 2 * pair], grad_ref[0, :, at : at + 2 * pair]
            two = jnp.concatenate([both[:, :pair], both[:, pair:]], axis=0)
            two_grad = jnp.concatenate([both_grad[:, :pair], both_grad[:, pair:]], axis=0)
            limit = cap[...]
            limit = jnp.concatenate([limit, limit], axis=1)
            turned = []
            for half in range(2):
                h = 4 * g + half
                span = slice((2 * g + half) * 2 * rows, (2 * g + half + 1) * 2 * rows)
                keep = first if half == 0 else jnp.logical_not(first)
                query_buf[span, :] = low(jnp.where(keep, wide(two), 0.0))
                grad_buf[span, :] = low(jnp.where(keep, wide(two_grad), 0.0))
                log = jnp.concatenate([log_rows[h : h + 1, :], log_rows[h + 2 : h + 3, :]], axis=1)
                delta = jnp.concatenate([delta_rows[h : h + 1, :], delta_rows[h + 2 : h + 3, :]], axis=1)
                scores = jnp.minimum(cols_dot(key[half], two) * factor, limit)
                weights = jnp.exp2(scores - log)
                grad_scores = low(weights * (cols_dot(value[half], two_grad) - delta))
                weight_buf[:, span] = low(weights)
                score_buf[:, span] = grad_scores
                turned.append(dot(key_turned[...], grad_scores))
            turned = jnp.concatenate(turned, axis=0) * HS ** (-0.5)
            query_grad_ref[0, :, at : at + pair] = low(turned[:, :rows].T)
            query_grad_ref[0, :, at + pair : at + 2 * pair] = low(turned[:, rows:].T)
        for j in range(parts):
            here = pl.ds(j * rows, rows)
            value_sum = dot(weight_buf[here, :], grad_buf[...])
            key_sum = dot(score_buf[here, :], query_buf[...]) * HS ** (-0.5)
            value_sum = value_sum + pltpu.roll(value_sum, HS, 1)
            key_sum = key_sum + pltpu.roll(key_sum, HS, 1)
            ref = even_grad_ref if j < half_parts else odd_grad_ref
            ref[j % half_parts, 0] = low(jnp.where(lanes((rows, pair)) < HS, key_sum, value_sum))

    def specs(first):
        return (
            pl.BlockSpec((1, rows, width), lambda b, *_: (b + first, 0, 0)),
            pl.BlockSpec((1, rows, pair), lambda b, *_: (b + first, 0, 0)),
            pl.BlockSpec((half_parts, 1, rows, pair), lambda b, *_: (0, b + first, 0, 0)),
        )

    flow, logs, blocks = specs(0)

    shared = [
        pltpu.VMEM((2, keys, pair), jnp.bfloat16),
        pltpu.VMEM((2, keys, pair), jnp.bfloat16),
    ]
    run_forward = pl.pallas_call(
        forward,
        grid_spec=pltpu.PrefetchScalarGridSpec(
            num_scalar_prefetch=2,
            grid=(batches,),
            in_specs=[flow, blocks, blocks],
            out_specs=[flow, flow, logs],
            scratch_shapes=[pltpu.VMEM((rows, keys), jnp.float32)] + shared,
        ),
        out_shape=[
            jax.ShapeDtypeStruct((batches, rows, width), jnp.bfloat16),
            jax.ShapeDtypeStruct((batches, rows, width), jnp.float32),
            jax.ShapeDtypeStruct((batches, rows, pair), jnp.float32),
        ],
        compiler_params=pltpu.CompilerParams(vmem_limit_bytes=20 * MIB),
        cost_estimate=NO_COST,
        name="attention_forward",
    )
    head_rows = -(-(width // HS) // 8) * 8
    all_columns = rows * (width // HS)
    count = batches // runs

    def call_backward(run):
        here_flow, here_logs, here_blocks = specs(run * count)
        return pl.pallas_call(
        backward,
        grid_spec=pltpu.PrefetchScalarGridSpec(
            num_scalar_prefetch=2,
            grid=(count,),
            in_specs=[here_flow, here_blocks, here_blocks, here_flow, here_logs, here_flow],
            out_specs=[flow, blocks, blocks],
            scratch_shapes=[pltpu.VMEM((keys, rows), jnp.float32)]
            + shared
            + [
                pltpu.VMEM((HS, keys), jnp.bfloat16),
                pltpu.VMEM((head_rows, rows), jnp.float32),
                pltpu.VMEM((head_rows, rows), jnp.float32),
                pltpu.VMEM((keys, all_columns), jnp.bfloat16),
                pltpu.VMEM((keys, all_columns), jnp.bfloat16),
                pltpu.VMEM((all_columns, pair), jnp.bfloat16),
                pltpu.VMEM((all_columns, pair), jnp.bfloat16),
            ],
        ),
        out_shape=[
            jax.ShapeDtypeStruct((count, rows, width), jnp.bfloat16),
            jax.ShapeDtypeStruct((half_parts, count, rows, pair), jnp.bfloat16),
            jax.ShapeDtypeStruct((half_parts, count, rows, pair), jnp.bfloat16),
        ],
        compiler_params=pltpu.CompilerParams(vmem_limit_bytes=32 * MIB),
        cost_estimate=NO_COST,
        name="attention_backward",
    )

    return run_forward, [call_backward(run) for run in range(runs)]


def ffn_kernels(rows, width, chunks, chunk, sources):
    units = chunks * chunk
    all_rows = 2 * rows
    arrays = 1 + max(source[0] for source in sources)
    block_rows = width * chunks // len(sources)
    any_spec = pl.BlockSpec(memory_space=pl.ANY)
    vmem = pl.BlockSpec(memory_space=pltpu.VMEM)
    smem = pl.BlockSpec(memory_space=pltpu.SMEM)
    span = chunk
    while span < 512 and units % (2 * span) == 0:
        span *= 2

    def fetch(place_ref, weights, which, held, sem):
        copies = []
        for array, block, far, unit in sources:
            row = place_ref[far] + block
            copies.append(
                pltpu.make_async_copy(
                    weights[array].at[block, pl.ds(which * block_rows, block_rows), :],
                    held.at[
                        pl.ds(pl.multiple_of(row * block_rows, 16), block_rows), pl.ds(unit * chunk, chunk)
                    ],
                    sem.at[len(copies)],
                )
            )
        for copy in copies:
            copy.start()
        return copies

    per_span = len(sources) // (units // span)

    def first(place_ref, *args):
        inputs, grads, turned_ref, bias_ref, weights = args[0:2], args[2:4], args[4], args[5], args[6 : 6 + arrays]
        act_ref, grad_ref = args[6 + arrays : 8 + arrays]
        outs, bias_grad_ref = args[8 + arrays : 8 + arrays + chunks], args[8 + arrays + chunks]
        held_up, held_down, act, grad_buf, product, sems, out_sems = args[9 + arrays + chunks :]
        ups = fetch(place_ref, weights, 0, held_up, sems.at[0])
        downs = fetch(place_ref, weights, 1, held_down, sems.at[1])
        sent = []

        def send(source, target):
            sent.append(pltpu.make_async_copy(source, target, out_sems.at[len(sent)]))
            sent[-1].start()

        for i in range(units // span):
            cols = slice(i * span, (i + 1) * span)
            for copy in ups[i * per_span : (i + 1) * per_span] + downs[i * per_span : (i + 1) * per_span]:
                copy.wait()
            sums = jnp.zeros((1, span), jnp.float32)
            for s in range(2):
                here = slice(s * rows, (s + 1) * rows)
                up = dot(inputs[s][...], held_up[:, cols]) + bias_ref[:, cols]
                value, slope = gelu_both(up)
                grad = dot(grads[s][...], held_down[:, cols]) * slope
                act[here, cols] = low(value)
                grad_buf[here, cols] = low(grad)
                sums = sums + jnp.sum(grad, axis=0, keepdims=True)
            bias_grad_ref[:, cols] = sums
            send(act.at[:, pl.ds(i * span, span)], act_ref.at[:, pl.ds(i * span, span)])
            send(grad_buf.at[:, pl.ds(i * span, span)], grad_ref.at[:, pl.ds(i * span, span)])
            product[:, cols] = low(dot(turned_ref[...], act[:, cols]))
            for j in range(span // chunk):
                m = i * (span // chunk) + j
                send(product.at[:, pl.ds(m * chunk, chunk)], outs[m])
        for copy in sent:
            copy.wait()

    def back(which):
        def kernel(place_ref, *args):
            source, weights = args[0], args[1 : 1 + arrays]
            own_ref, other_ref, held, sems = args[1 + arrays :]
            for copy in fetch(place_ref, weights, which, held, sems):
                copy.wait()
            own_ref[...] = cols_dot(source[:rows, :], held[...])
            other_ref[...] = low(cols_dot(source[rows:, :], held[...]))

        return pl.pallas_call(
            kernel,
            in_specs=[smem, vmem] + [any_spec] * arrays,
            out_specs=[vmem] * 2,
            out_shape=[own, other],
            scratch_shapes=[
                pltpu.VMEM((width, units), jnp.bfloat16),
                pltpu.SemaphoreType.DMA((len(sources),)),
            ],
            compiler_params=pltpu.CompilerParams(vmem_limit_bytes=18 * MIB),
            cost_estimate=NO_COST,
            name="ffn_back" if which == 0 else "ffn_down",
        )

    def third(*args):
        inputs, grad_ref, outs, turned = args[0:2], args[2], args[3 : 3 + chunks], args[3 + chunks]
        for s in range(2):
            for i in range(rows // 128):
                block = wide(inputs[s][i * 128 : (i + 1) * 128, :])
                turned[:, s * rows + i * 128 : s * rows + (i + 1) * 128] = low(block.T)
        for i in range(units // span):
            total = low(dot(turned[...], grad_ref[:, i * span : (i + 1) * span]))
            for j in range(span // chunk):
                outs[i * (span // chunk) + j][...] = total[:, j * chunk : (j + 1) * chunk]

    flow = jax.ShapeDtypeStruct((all_rows, units), jnp.bfloat16)
    gradient = jax.ShapeDtypeStruct((width, chunk), jnp.bfloat16)
    own = jax.ShapeDtypeStruct((rows, width), jnp.float32)
    other = jax.ShapeDtypeStruct((rows, width), jnp.bfloat16)
    run_first = pl.pallas_call(
        first,
        in_specs=[smem] + [vmem] * 6 + [any_spec] * arrays,
        out_specs=[any_spec] * (2 + chunks) + [vmem],
        out_shape=[flow, flow] + [gradient] * chunks + [jax.ShapeDtypeStruct((1, units), jnp.float32)],
        scratch_shapes=[
            pltpu.VMEM((width, units), jnp.bfloat16),
            pltpu.VMEM((width, units), jnp.bfloat16),
            pltpu.VMEM((all_rows, units), jnp.bfloat16),
            pltpu.VMEM((all_rows, units), jnp.bfloat16),
            pltpu.VMEM((width, units), jnp.bfloat16),
            pltpu.SemaphoreType.DMA((2, len(sources))),
            pltpu.SemaphoreType.DMA((2 * (units // span) + chunks,)),
        ],
        compiler_params=pltpu.CompilerParams(vmem_limit_bytes=40 * MIB),
        cost_estimate=NO_COST,
        name="ffn_first",
    )
    run_third = pl.pallas_call(
        third,
        in_specs=[vmem] * 3,
        out_specs=[vmem] * chunks,
        out_shape=[gradient] * chunks,
        scratch_shapes=[pltpu.VMEM((width, all_rows), jnp.bfloat16)],
        compiler_params=pltpu.CompilerParams(vmem_limit_bytes=20 * MIB),
        cost_estimate=NO_COST,
        name="ffn_grads",
    )
    return run_first, back(0), run_third, back(1)


def ffn_plain(chunks, chunk):
    def first(_, own, other, grad_own, grad_other, turned, bias, up, down):
        value, slope = gelu_both(dot(jnp.concatenate([own, other]), up) + bias)
        grad = low(dot(jnp.concatenate([grad_own, grad_other]), down) * slope)
        act = low(value)
        sums = jnp.sum(wide(grad), axis=0, keepdims=True)
        return [act, grad] + jnp.split(low(dot(turned, act)), chunks, axis=1) + [sums]

    def back(_, source, weights):
        own, other = jnp.split(cols_dot(source, weights), 2)
        return own, low(other)

    def third(own, other, grad):
        return jnp.split(low(rows_dot(jnp.concatenate([own, other]), grad)), chunks, axis=1)

    return first, back, third, back


def attn_grads(rows, width, row_groups, parts, piece):
    def kernel(place_ref, left_a, right_a, left_b, right_b, even_ref, odd_ref, turned, total):
        place = place_ref[0]
        for n, (left, right) in enumerate(((left_a, right_a), (left_b, right_b))):
            for i in range(rows // 128):
                turned[:, i * 128 : (i + 1) * 128] = low(wide(left[i * 128 : (i + 1) * 128, :]).T)
            total[:, n * width : (n + 1) * width] = dot(turned[...], right[...])
        for k in range(parts):
            ref = odd_ref if k % 2 else even_ref
            for w in range(row_groups):
                at = pl.multiple_of(w * piece * parts + (place ^ k) * piece, 8)
                ref[k // 2, w] = low(total[pl.ds(at, piece), :])

    vmem = pl.BlockSpec(memory_space=pltpu.VMEM)
    shape = jax.ShapeDtypeStruct((parts // 2, row_groups, piece, 2 * width), jnp.bfloat16)
    return pl.pallas_call(
        kernel,
        grid_spec=pltpu.PrefetchScalarGridSpec(
            num_scalar_prefetch=1,
            grid=(),
            in_specs=[vmem] * 4,
            out_specs=[vmem] * 2,
            scratch_shapes=[pltpu.VMEM((width, rows), jnp.bfloat16), pltpu.VMEM((width, 2 * width), jnp.float32)],
        ),
        out_shape=[shape] * 2,
        compiler_params=pltpu.CompilerParams(vmem_limit_bytes=24 * MIB),
        cost_estimate=NO_COST,
        name="attn_grads",
    )


def attn_update(rows, columns, width, parts, piece):
    qkv = columns - width

    def kernel(place_ref, even_ref, odd_ref, master, first, second, *outs):
        place = place_ref[0]
        for k in range(parts):
            ref = odd_ref if k % 2 else even_ref
            here = pl.ds(pl.multiple_of((place ^ k) * piece, 8), piece)
            for cols, source in (
                (slice(0, width), slice(0, width)),
                (slice(width, qkv), slice(2 * width, columns)),
                (slice(qkv, columns), slice(width, 2 * width)),
            ):
                grad = wide(ref[k // 2, :, source])
                got = adam_update(master[here, cols], grad, first[here, cols], second[here, cols], 0.1, 0.1)
                outs[0][here, cols] = got[0]
                outs[1][here, cols] = got[1]
                outs[2][here, cols] = got[2]

    vmem = pl.BlockSpec(memory_space=pltpu.VMEM)
    return pl.pallas_call(
        kernel,
        grid_spec=pltpu.PrefetchScalarGridSpec(
            num_scalar_prefetch=1, grid=(), in_specs=[vmem] * 5, out_specs=[vmem] * 3, scratch_shapes=[]
        ),
        out_shape=[jax.ShapeDtypeStruct((rows, columns), jnp.float32)] * 3,
        compiler_params=pltpu.CompilerParams(vmem_limit_bytes=20 * MIB),
        cost_estimate=NO_COST,
        name="attn_update",
    )


def ffn_update(rows, units, parts, chunk):
    per_row = 2 * units // 128
    step = 32
    lines = step * per_row

    def kernel(place_ref, *refs):
        pieces, (master, first, second) = refs[:parts], refs[parts : parts + 3]
        first_out, second_out, master_out, total = refs[parts + 3 :]
        place = place_ref[0]
        for k in range(parts):
            base = (place ^ k) * (2 * chunk // 128)
            for j in range(chunk // 128):
                for which in range(2):
                    here = pl.ds(base + 2 * j + which, step, per_row)
                    total[here, :] = wide(pieces[k][which, :, j * 128 : (j + 1) * 128])
        got = adam_update(master[...], total[...], first[...], second[...], 0.1, 0.1)
        first_out[...] = got[0]
        second_out[...] = got[1]
        master_out[...] = got[2]

    block = pl.BlockSpec((lines, 128), lambda i, *_: (i, 0))
    piece = pl.BlockSpec((2, step, chunk), lambda i, *_: (0, i, 0))
    shape = jax.ShapeDtypeStruct((rows * per_row, 128), jnp.float32)
    call = pl.pallas_call(
        kernel,
        grid_spec=pltpu.PrefetchScalarGridSpec(
            num_scalar_prefetch=1,
            grid=(rows // step,),
            in_specs=[piece] * parts + [block] * 3,
            out_specs=[block] * 3,
            scratch_shapes=[pltpu.VMEM((lines, 128), jnp.float32)],
        ),
        out_shape=[shape] * 3,
        compiler_params=pltpu.CompilerParams(vmem_limit_bytes=20 * MIB),
        cost_estimate=NO_COST,
        name="ffn_update",
    )

    def fold(array):
        return jnp.swapaxes(array.reshape(rows, 2, units // 128, 128), 1, 2).reshape(-1, 128)

    def unfold(array):
        return jnp.swapaxes(array.reshape(rows, units // 128, 2, 128), 1, 2).reshape(rows, 2, units)

    def run(place, pieces, master, first, second):
        got = call(place, *pieces, fold(master), fold(first), fold(second))
        return tuple(unfold(array) for array in got)

    return run


def shards(
    tokens,
    doc_starts,
    attn_master,
    attn_mom,
    attn_sq,
    ffn_master,
    ffn_mom,
    ffn_sq,
    small_master,
    small_mom,
    small_sq,
    cotangent,
):
    ctx_count = lax.axis_size("ctx")
    ctx_place = lax.axis_index("ctx")
    wt_count = lax.axis_size("wt")
    batches, rows_here, width = tokens.shape
    heads = width // HS
    qkv_cols = width + 2 * HS
    all_rows = batches * rows_here
    shard_rows = attn_master.shape[0]
    piece_rows = shard_rows // ctx_count
    chunk = FF // ctx_count
    order = ctx_place ^ jnp.arange(ctx_count, dtype=jnp.int32)
    (
        gain_one,
        shift_one,
        gain_two,
        shift_two,
        bias_query,
        bias_out,
        bias_proj,
        bias_value,
        bias_hidden,
    ) = split_small(small_master)

    runs = 2 if batches % 2 == 0 else 1
    places = [jnp.stack([ctx_place, jnp.int32(run * (batches // runs))]) for run in range(runs)]
    place = places[0]
    wt_half = wt_count // 2
    near_row = lax.axis_index("wt") // wt_half * wt_half
    row_starts = jnp.stack([near_row, wt_half - near_row])
    chips = ctx_count // 2

    def in_order(even, odd):
        buffer = jnp.zeros((ctx_count,) + even.shape[1:], even.dtype)
        for m in range(chips):
            buffer = put(buffer, even[m][None], ctx_place ^ (2 * m), 0)
            buffer = put(buffer, odd[m][None], ctx_place ^ (2 * m + 1), 0)
        return buffer

    fitted = chunk % 128 == 0 and shard_rows % 32 == 0 and piece_rows % 8 == 0

    attn_piece = low(take(attn_master, ctx_place, 0, piece_rows))
    qkv_blocks = in_order(*gather_ctx(gather_wt(attn_piece[:, :qkv_cols])))
    weight_qkv = jnp.swapaxes(qkv_blocks, 0, 1).reshape(width, qkv_cols)
    ffn_piece = low(jnp.swapaxes(take(ffn_master, ctx_place, 2, chunk), 0, 1)).reshape(2 * shard_rows, chunk)
    rest_piece = jnp.concatenate([ffn_piece, attn_piece[:, qkv_cols:].reshape(-1, chunk)])
    near, far = gather_wt_halves(rest_piece)
    back_low = cotangent.reshape(all_rows, width)
    back_rows = wide(back_low)
    back_other = xor_send(back_low, 1)
    back_turned = jnp.concatenate([back_low, back_other]).T
    bias_parts = bias_hidden.reshape(ctx_count, chunk)[order[::2]].reshape(1, chips * chunk)

    run_forward, run_backward = attention_kernels(batches, rows_here, width, ctx_count, runs)
    stream = wide(tokens.reshape(all_rows, width))
    normed, norm_back_one = jax.vjp(layer_norm, stream, gain_one, shift_one)
    normed_low = low(normed)
    mixed = dot(normed_low, weight_qkv)
    queries = low(mixed[:, :width] + bias_query).reshape(batches, rows_here, width)
    kv_bias = jnp.concatenate([jnp.zeros((HS,), jnp.float32), bias_value])
    kv_local = low(mixed[:, width:] + kv_bias).reshape(batches, rows_here, 2 * HS)
    near_parts = [near] + ([xor_send(near, 2), xor_send(near, 4)] if chips == 4 else [])
    kv_even = jnp.stack(gather_chips(kv_local))
    far = after(far, kv_even)
    kv_odd = xor_send(kv_even, 1)
    queries = after(queries, back_turned, bias_parts)
    attended_low, attended, logs = run_forward(doc_starts, place, queries, kv_even, kv_odd)
    attended_low = attended_low.reshape(all_rows, width)
    if chips == 4:
        far_parts = [far, xor_send(far, 2), xor_send(far, 4)]
        near_parts.append(after(xor_send(near_parts[1], 4), attended_low))
        far_parts.append(after(xor_send(far_parts[2], 2), attended_low))
    else:
        near_parts, far_parts = gather_chips(near), gather_chips(far)
    rest_parts = near_parts + far_parts
    sources = [(half * chips + m, z, half, m) for m in range(chips) for half in range(2) for z in range(wt_half)]
    out_even = jnp.stack(
        [jnp.stack([a[:, 2 * shard_rows :], b[:, 2 * shard_rows :]]) for a, b in zip(near_parts, far_parts)]
    )
    out_both = jnp.stack([out_even, xor_send(out_even, 1)])
    out_both = out_both.reshape(2, chips, 2, wt_half, piece_rows, width)
    out_buffer = jnp.zeros((2, wt_half, ctx_count, piece_rows, width), out_both.dtype)
    for k in range(ctx_count):
        for half in range(2):
            block = out_both[k % 2, k // 2, half][None, :, None]
            side = near_row // wt_half ^ half
            out_buffer = lax.dynamic_update_slice(out_buffer, block, (side, 0, ctx_place ^ k, 0, 0))
    weight_out = out_buffer.reshape(width, width)
    hidden = stream + dot(attended_low, weight_out) + bias_out
    normed_two, norm_back_two = jax.vjp(layer_norm, hidden, gain_two, shift_two)
    normed_two_low = low(normed_two)
    normed_two_other = xor_send(normed_two_low, 1)

    if fitted:
        ffn_first, ffn_back, ffn_third, ffn_down = ffn_kernels(all_rows, width, chips, chunk, sources)
        up_weights = down_weights = rest_parts
    else:
        ffn_first, ffn_back, ffn_third, ffn_down = ffn_plain(chips, chunk)
        ordered = []
        for a, b in zip(near_parts, far_parts):
            both = jnp.stack([a, b])
            ordered.append(jnp.where(near_row == 0, both, both[::-1]).reshape((wt_count,) + a.shape[1:]))
        up_weights = (jnp.concatenate([p[:, :shard_rows].reshape(width, chunk) for p in ordered], axis=1),)
        down_weights = (
            jnp.concatenate([p[:, shard_rows : 2 * shard_rows].reshape(width, chunk) for p in ordered], axis=1),
        )
    both_weights = rest_parts if fitted else up_weights + down_weights
    act, grad_up, *got = ffn_first(
        row_starts, normed_two_low, normed_two_other, back_low, back_other, back_turned, bias_parts, *both_weights
    )
    down_grads, hidden_grads = got[:chips], got[chips].reshape(chips, chunk)
    own_part, other_part = ffn_back(row_starts, grad_up, *up_weights)
    other_part = xor_send(other_part, 1)
    up_grads = ffn_third(normed_two_low, normed_two_other, grad_up)
    grad_normed_two = own_part + wide(other_part)
    grad_hidden_part, grad_gain_two, grad_shift_two = norm_back_two(grad_normed_two)
    grad_hidden = back_rows + grad_hidden_part
    grad_hidden_low = low(grad_hidden)
    grad_attended = low(cols_dot(grad_hidden_low, weight_out)).reshape(batches, rows_here, width)

    if chips == 4:
        met = after(xor_send(down_grads[3], 4), up_grads[0])
        down_along_x = xor_send(low(wide(down_grads[1]) + wide(met)), 2)
        down_along_y = xor_send(down_grads[2], 4)

    backs = [
        run(doc_starts, places[i], queries, kv_even, kv_odd, attended, logs, grad_attended)
        for i, run in enumerate(run_backward[:1])
    ]
    if chips == 4:
        met = after(xor_send(up_grads[3], 2), backs[0][0])
        up_along_x = xor_send(up_grads[1], 2)
        up_along_y = xor_send(low(wide(up_grads[2]) + wide(met)), 4)
    grad_attended = after(grad_attended, backs[0][0])
    backs += [
        run(doc_starts, places[i + 1], queries, kv_even, kv_odd, attended, logs, grad_attended)
        for i, run in enumerate(run_backward[1:])
    ]
    last = backs[-1][0]
    grad_query = jnp.concatenate([back[0] for back in backs]).reshape(all_rows, width)
    kv_halves = [low(wide(back[1]) + wide(xor_send(back[2], 1))) for back in backs]
    kv_half = jnp.concatenate(kv_halves, axis=1)
    grad_kv = low(scatter_chips([kv_half[m] for m in range(chips)])).reshape(all_rows, 2 * HS)

    if chips == 4:
        down_along_x, down_along_y = after(down_along_x, last), after(down_along_y, last)
        up_along_x, up_along_y = after(up_along_x, last), after(up_along_y, last)
        down_sum = wide(down_grads[0]) + wide(down_along_x) + wide(down_along_y)
        up_sum = wide(up_grads[0]) + wide(up_along_x) + wide(up_along_y)
    else:
        down_sum, up_sum = scatter_chips(down_grads), scatter_chips(up_grads)
    down_part = low(scatter_wt(low(down_sum), 0))
    up_part = low(scatter_wt(low(up_sum), 0))
    ffn_part = jnp.stack([up_part, down_part])
    ffn_even, ffn_odd = gather_ctx(ffn_part)

    own_part, other_part = ffn_down(row_starts, after(act, last), *down_weights)
    down_vals = own_part + wide(xor_send(other_part, 1))
    layer_out = low(hidden + down_vals + bias_proj).reshape(batches, rows_here, width)

    if fitted:
        wide_even, wide_odd = attn_grads(all_rows, width, wt_count, ctx_count, piece_rows)(
            place, normed_low, grad_query, attended_low, grad_hidden_low
        )
    else:
        grad_wide = jnp.concatenate(
            [low(rows_dot(normed_low, grad_query)), low(rows_dot(attended_low, grad_hidden_low))], axis=1
        )
        grad_wide = grad_wide.reshape(wt_count, ctx_count, piece_rows, 2 * width)
        pieces = [take(grad_wide, ctx_place ^ k, 1, 1)[:, 0] for k in range(ctx_count)]
        wide_even, wide_odd = jnp.stack(pieces[::2]), jnp.stack(pieces[1::2])
    wide_half = low(wide(wide_even) + wide(xor_send(wide_odd, 1)))

    grad_normed = cols_dot(grad_query, weight_qkv[:, :width]) + cols_dot(grad_kv, weight_qkv[:, width:])
    grad_stream_part, grad_gain_one, grad_shift_one = norm_back_one(grad_normed)
    input_grad = (grad_hidden + grad_stream_part).reshape(batches, rows_here, width)

    own_units = jnp.zeros((ctx_count, chunk), jnp.float32)
    for m in range(chips):
        own_units = put(own_units, hidden_grads[m][None], ctx_place ^ (2 * m), 0)
    grad_small = jnp.concatenate(
        [
            grad_gain_one,
            grad_shift_one,
            grad_gain_two,
            grad_shift_two,
            jnp.sum(wide(grad_query), axis=0),
            jnp.sum(grad_hidden, axis=0),
            jnp.sum(back_rows, axis=0),
            jnp.sum(wide(grad_kv[:, HS:]), axis=0),
            own_units.reshape(FF),
        ]
    )
    small_size = grad_small.shape[0]
    small_columns = 128 * -(-small_size // (128 * piece_rows * ctx_count))
    small_blocks = jnp.pad(low(grad_small), (0, ctx_count * piece_rows * small_columns - small_size))
    small_blocks = small_blocks.reshape(ctx_count, 1, piece_rows, small_columns)
    kv_blocks = low(rows_dot(normed_low, grad_kv)).reshape(wt_count, ctx_count, piece_rows, 2 * HS)
    kv_blocks = jnp.swapaxes(kv_blocks, 0, 1)
    small_blocks = jnp.broadcast_to(small_blocks, kv_blocks.shape[:3] + (small_columns,))
    tail = jnp.concatenate([kv_blocks, small_blocks], axis=3)
    tail_pieces = [take(tail, ctx_place ^ k, 0, 1)[0] for k in range(ctx_count)]
    tail_even, tail_odd = jnp.stack(tail_pieces[::2]), jnp.stack(tail_pieces[1::2])
    tail_half = low(wide(tail_even) + wide(xor_send(tail_odd, 1)))
    attn_half = jnp.concatenate([wide_half, tail_half], axis=3)
    attn_part = scatter_chips([attn_half[m] for m in range(chips)])
    attn_even, attn_odd = gather_ctx(low(scatter_wt(low(attn_part), 0)[0]))
    attn_columns = attn_master.shape[1]
    small_total = in_order(attn_even[..., attn_columns:], attn_odd[..., attn_columns:])
    small_total = wide(small_total.reshape(-1)[:small_size])

    if fitted:
        attn_new = attn_update(shard_rows, attn_columns, width, ctx_count, piece_rows)(
            place, attn_even, attn_odd, attn_master, attn_mom, attn_sq
        )
        pieces = [(ffn_even, ffn_odd)[k % 2][k // 2] for k in range(ctx_count)]
        ffn_new = ffn_update(shard_rows, FF, ctx_count, chunk)(place, pieces, ffn_master, ffn_mom, ffn_sq)
    else:
        attn_total = wide(in_order(attn_even, attn_odd).reshape(shard_rows, attn_columns + small_columns))
        attn_total = jnp.concatenate(
            [attn_total[:, :width], attn_total[:, 2 * width : attn_columns], attn_total[:, width : 2 * width]], axis=1
        )
        attn_new = adam_update(attn_master, attn_total, attn_mom, attn_sq, 0.1, 0.1)
        ffn_total = jnp.transpose(in_order(ffn_even, ffn_odd), (2, 1, 0, 3)).reshape(shard_rows, 2, FF)
        ffn_new = adam_update(ffn_master, wide(ffn_total), ffn_mom, ffn_sq, 0.1, 0.1)
    small_new = adam_update(small_master, small_total, small_mom, small_sq, 1.0, 0.0)
    return (layer_out, input_grad) + tuple(attn_new) + tuple(ffn_new) + small_new


def solution(mesh):
    rows, cube = P("wt", None), P("wt", None, None)
    flow = P("wt", "ctx", None)
    in_specs = (flow, rows, rows, rows, rows, cube, cube, cube, P(), P(), P(), flow)
    out_specs = (flow, flow, rows, rows, rows, cube, cube, cube, P(), P(), P())
    return jax.shard_map(shards, mesh=mesh, in_specs=in_specs, out_specs=out_specs, check_vma=False)
```

```python
import jax
import jax.numpy as jnp
from jax import lax
from jax.experimental import pallas as pl
from jax.experimental.pallas import tpu as pltpu
from jax.sharding import PartitionSpec as P

D = 768
HS = 64
FF = 3072
STEP = 10


NORM_EPS = 1e-05
GELU_COEF = 0.7978845608028654
GELU_CUBE = 0.044715
BETA_ONE = 0.9
BETA_TWO = 0.95
ADAM_EPS = 1e-08
MIB = 1 << 20
NO_COST = pl.CostEstimate(flops=0, bytes_accessed=0, transcendentals=0)


def layer_norm(values, gain, shift):
    centre = values - jnp.mean(values, axis=-1, keepdims=True)
    spread = jnp.mean(centre * centre, axis=-1, keepdims=True)
    return centre * lax.rsqrt(spread + NORM_EPS) * gain + shift


def gelu_both(u):
    square = u * u
    share = 0.5 * jnp.tanh(u * (GELU_COEF * GELU_CUBE * square + GELU_COEF)) + 0.5
    bend = u * (6.0 * GELU_COEF * GELU_CUBE * square + 2.0 * GELU_COEF)
    return u * share, share * ((1.0 - share) * bend) + share


def split_small(small):
    return (
        small[0:D],
        small[D : 2 * D],
        small[2 * D : 3 * D],
        small[3 * D : 4 * D],
        small[4 * D : 5 * D],
        small[5 * D : 6 * D],
        small[6 * D : 7 * D],
        small[7 * D : 7 * D + HS],
        small[7 * D + HS :],
    )


def rows_dot(left, right):
    return lax.dot_general(
        left, right, (((0,), (0,)), ((), ())), preferred_element_type=jnp.float32
    )


def cols_dot(left, right):
    return lax.dot_general(
        left, right, (((1,), (1,)), ((), ())), preferred_element_type=jnp.float32
    )


def dot(left, right):
    return jnp.dot(left, right, preferred_element_type=jnp.float32)


def low(values):
    return values.astype(jnp.bfloat16)


def wide(values):
    return values.astype(jnp.float32)


def adam_update(master, gradient, first, second, step_rate, decay_rate):
    first_new = BETA_ONE * first + (1.0 - BETA_ONE) * gradient
    second_new = BETA_TWO * second + (1.0 - BETA_TWO) * gradient * gradient
    first_hat = first_new / (1.0 - BETA_ONE**STEP)
    second_hat = second_new / (1.0 - BETA_TWO**STEP)
    master_new = master - step_rate * (
        first_hat / (jnp.sqrt(second_hat) + ADAM_EPS) + decay_rate * master
    )
    return (first_new, second_new, master_new)


def xor_send(array, mask):
    count = lax.axis_size("ctx")
    return lax.ppermute(array, "ctx", [(i, i ^ mask) for i in range(count)])


def xor_wt(array, mask):
    count = lax.axis_size("wt")
    return lax.ppermute(array, "wt", [(i, i ^ mask) for i in range(count)])


def after(array, *others):
    return lax.optimization_barrier((array,) + others)[0]


def put(buffer, piece, place, axis):
    starts = [0] * buffer.ndim
    starts[axis] = place * piece.shape[axis]
    return lax.dynamic_update_slice(buffer, piece, starts)


def take(buffer, place, axis, size):
    return lax.dynamic_slice_in_dim(buffer, place * size, size, axis)


def gather_wt(piece):
    count, place = lax.axis_size("wt"), lax.axis_index("wt")
    buffer = put(jnp.zeros((count,) + piece.shape, piece.dtype), piece[None], place, 0)
    for mask in range(1, count):
        buffer = put(buffer, xor_wt(piece, mask)[None], place ^ mask, 0)
    return buffer


def gather_wt_halves(piece):
    count, place = lax.axis_size("wt"), lax.axis_index("wt")
    half = count // 2
    near = jnp.zeros((half,) + piece.shape, piece.dtype)
    far = near
    near = put(near, piece[None], place % half, 0)
    for mask in range(1, half):
        near = put(near, xor_wt(piece, mask)[None], (place ^ mask) % half, 0)
    for mask in range(half, count):
        far = put(far, xor_wt(piece, mask)[None], (place ^ mask) % half, 0)
    return near, far


def gather_chips(piece):
    count = lax.axis_size("ctx")
    return [piece] + [xor_send(piece, mask) for mask in range(2, count, 2)]


def scatter_chips(pieces):
    total = wide(pieces[0])
    for m in range(1, len(pieces)):
        total = total + wide(xor_send(pieces[m], 2 * m))
    return total


def gather_ctx(piece):
    even = jnp.stack(gather_chips(piece))
    return even, xor_send(even, 1)


def scatter_ctx(even, odd):
    half = low(wide(even) + wide(xor_send(odd, 1)))
    return scatter_chips([half[m] for m in range(half.shape[0])])


def scatter_wt(array, axis):
    count, place = lax.axis_size("wt"), lax.axis_index("wt")
    size = array.shape[axis] // count
    total = wide(take(array, place, axis, size))
    for mask in range(1, count):
        total = total + wide(xor_wt(take(array, place ^ mask, axis, size), mask))
    return total


def attention_kernels(batches, rows, width, parts, runs):
    half_parts = parts // 2
    keys = parts * rows
    pair = 2 * HS
    groups = width // (2 * pair)
    factor = HS ** (-0.5) * 1.4426950408889634
    masks = list(range(0, parts, 2)) + list(range(1, parts, 2))

    def lanes(shape):
        return lax.broadcasted_iota(jnp.int32, shape, 1)

    def spread(even_ref, odd_ref, key_ref, value_ref):
        for j in range(parts):
            ref = even_ref if j < half_parts else odd_ref
            block = wide(ref[j % half_parts, 0])
            turned = pltpu.roll(block, HS, 1)
            first = lanes(block.shape) < HS
            here = pl.ds(j * rows, rows)
            key_ref[0, here, :] = low(jnp.where(first, block, 0.0))
            key_ref[1, here, :] = low(jnp.where(first, 0.0, turned))
            value_ref[0, here, :] = low(jnp.where(first, turned, 0.0))
            value_ref[1, here, :] = low(jnp.where(first, 0.0, block))

    def doc_begin(starts_ref, stream, positions):
        begin = jnp.zeros_like(positions)
        for j in range(starts_ref.shape[1]):
            start = starts_ref[stream, j]
            begin = jnp.where(start <= positions, jnp.maximum(begin, start), begin)
        return begin

    def forward(starts_ref, place_ref, query_ref, even_ref, odd_ref, low_ref, full_ref, log_ref, cap, key, value):
        stream, place = pl.program_id(0), place_ref[0]
        spread(even_ref, odd_ref, key, value)
        query_pos = place * rows + lax.broadcasted_iota(jnp.int32, (rows, 1), 0)
        begin = doc_begin(starts_ref, stream, query_pos)
        for j, mask in enumerate(masks):
            key_pos = (place ^ mask) * rows + lax.broadcasted_iota(jnp.int32, (rows, rows), 1)
            allowed = (key_pos >= begin) & (key_pos <= query_pos)
            cap[:, j * rows : (j + 1) * rows] = jnp.where(allowed, 3.0e38, -1e30)
        log_ref[...] = jnp.zeros_like(log_ref)

        def group(g, carry):
            at = pl.multiple_of(g * 2 * pair, 2 * pair)
            both = query_ref[0, :, pl.ds(at, 2 * pair)]
            two = jnp.concatenate([both[:, :pair], both[:, pair:]], axis=0)
            limit = cap[...]
            limit = jnp.concatenate([limit, limit], axis=0)
            total = jnp.zeros((2 * rows, pair), jnp.float32)
            logs = log_ref[0]
            for half in range(2):
                scores = jnp.minimum(cols_dot(two, key[half]) * factor, limit)
                peak = jnp.max(scores, axis=1, keepdims=True)
                expo = jnp.exp2(scores - peak)
                norm = jnp.sum(expo, axis=1, keepdims=True)
                total = total + dot(low(expo), value[half]) / norm
                log = peak + jnp.log2(norm)
                column = lanes((rows, pair))
                logs = jnp.where(column == 4 * g + half, log[:rows], logs)
                logs = jnp.where(column == 4 * g + 2 + half, log[rows:], logs)
            log_ref[0] = logs
            total = jnp.concatenate([total[:rows], total[rows:]], axis=1)
            full_ref[0, :, pl.ds(at, 2 * pair)] = total
            low_ref[0, :, pl.ds(at, 2 * pair)] = low(total)
            return carry

        lax.fori_loop(0, groups, group, 0, unroll=True)

    def backward(
        starts_ref, place_ref, query_ref, even_ref, odd_ref, full_ref, log_ref, grad_ref,
        query_grad_ref, even_grad_ref, odd_grad_ref,
        cap, key, value, key_turned, log_rows, delta_rows, weight_buf, score_buf, query_buf, grad_buf,
    ):
        stream, place = pl.program_id(0) + place_ref[1], place_ref[0]
        spread(even_ref, odd_ref, key, value)
        query_pos = place * rows + lax.broadcasted_iota(jnp.int32, (1, rows), 1)
        begin = doc_begin(starts_ref, stream, query_pos)
        for j, mask in enumerate(masks):
            key_pos = (place ^ mask) * rows + lax.broadcasted_iota(jnp.int32, (rows, rows), 0)
            allowed = (key_pos >= begin) & (key_pos <= query_pos)
            cap[j * rows : (j + 1) * rows, :] = jnp.where(allowed, 3.0e38, -1e30)
            here = pl.ds(j * rows, rows)
            key_turned[:, j * rows : (j + 1) * rows] = low(wide(key[0, here, :]).T[:HS])
        log_rows[...] = log_ref[0].T[: log_rows.shape[0]]
        head_of = lax.broadcasted_iota(jnp.int32, (delta_rows.shape[0], width), 1) // HS
        chosen = (head_of == lax.broadcasted_iota(jnp.int32, (delta_rows.shape[0], width), 0)).astype(jnp.float32)
        delta_rows[...] = lax.dot_general(
            chosen, wide(grad_ref[0]) * full_ref[0], (((1,), (1,)), ((), ())),
            precision=lax.Precision.HIGHEST, preferred_element_type=jnp.float32,
        )
        first = lanes((2 * rows, pair)) < HS
        for g in range(groups):
            at = g * 2 * pair
            both, both_grad = query_ref[0, :, at : at + 2 * pair], grad_ref[0, :, at : at + 2 * pair]
            two = jnp.concatenate([both[:, :pair], both[:, pair:]], axis=0)
            two_grad = jnp.concatenate([both_grad[:, :pair], both_grad[:, pair:]], axis=0)
            limit = cap[...]
            limit = jnp.concatenate([limit, limit], axis=1)
            turned = []
            for half in range(2):
                h = 4 * g + half
                span = slice((2 * g + half) * 2 * rows, (2 * g + half + 1) * 2 * rows)
                keep = first if half == 0 else jnp.logical_not(first)
                query_buf[span, :] = low(jnp.where(keep, wide(two), 0.0))
                grad_buf[span, :] = low(jnp.where(keep, wide(two_grad), 0.0))
                log = jnp.concatenate([log_rows[h : h + 1, :], log_rows[h + 2 : h + 3, :]], axis=1)
                delta = jnp.concatenate([delta_rows[h : h + 1, :], delta_rows[h + 2 : h + 3, :]], axis=1)
                scores = jnp.minimum(cols_dot(key[half], two) * factor, limit)
                weights = jnp.exp2(scores - log)
                grad_scores = low(weights * (cols_dot(value[half], two_grad) - delta))
                weight_buf[:, span] = low(weights)
                score_buf[:, span] = grad_scores
                turned.append(dot(key_turned[...], grad_scores))
            turned = jnp.concatenate(turned, axis=0) * HS ** (-0.5)
            query_grad_ref[0, :, at : at + pair] = low(turned[:, :rows].T)
            query_grad_ref[0, :, at + pair : at + 2 * pair] = low(turned[:, rows:].T)
        for j in range(parts):
            here = pl.ds(j * rows, rows)
            value_sum = dot(weight_buf[here, :], grad_buf[...])
            key_sum = dot(score_buf[here, :], query_buf[...]) * HS ** (-0.5)
            value_sum = value_sum + pltpu.roll(value_sum, HS, 1)
            key_sum = key_sum + pltpu.roll(key_sum, HS, 1)
            ref = even_grad_ref if j < half_parts else odd_grad_ref
            ref[j % half_parts, 0] = low(jnp.where(lanes((rows, pair)) < HS, key_sum, value_sum))

    def specs(first):
        return (
            pl.BlockSpec((1, rows, width), lambda b, *_: (b + first, 0, 0)),
            pl.BlockSpec((1, rows, pair), lambda b, *_: (b + first, 0, 0)),
            pl.BlockSpec((half_parts, 1, rows, pair), lambda b, *_: (0, b + first, 0, 0)),
        )

    flow, logs, blocks = specs(0)

    shared = [
        pltpu.VMEM((2, keys, pair), jnp.bfloat16),
        pltpu.VMEM((2, keys, pair), jnp.bfloat16),
    ]
    run_forward = pl.pallas_call(
        forward,
        grid_spec=pltpu.PrefetchScalarGridSpec(
            num_scalar_prefetch=2,
            grid=(batches,),
            in_specs=[flow, blocks, blocks],
            out_specs=[flow, flow, logs],
            scratch_shapes=[pltpu.VMEM((rows, keys), jnp.float32)] + shared,
        ),
        out_shape=[
            jax.ShapeDtypeStruct((batches, rows, width), jnp.bfloat16),
            jax.ShapeDtypeStruct((batches, rows, width), jnp.float32),
            jax.ShapeDtypeStruct((batches, rows, pair), jnp.float32),
        ],
        compiler_params=pltpu.CompilerParams(vmem_limit_bytes=20 * MIB),
        cost_estimate=NO_COST,
        name="attention_forward",
    )
    head_rows = -(-(width // HS) // 8) * 8
    all_columns = rows * (width // HS)
    count = batches // runs

    def call_backward(run):
        here_flow, here_logs, here_blocks = specs(run * count)
        return pl.pallas_call(
        backward,
        grid_spec=pltpu.PrefetchScalarGridSpec(
            num_scalar_prefetch=2,
            grid=(count,),
            in_specs=[here_flow, here_blocks, here_blocks, here_flow, here_logs, here_flow],
            out_specs=[flow, blocks, blocks],
            scratch_shapes=[pltpu.VMEM((keys, rows), jnp.float32)]
            + shared
            + [
                pltpu.VMEM((HS, keys), jnp.bfloat16),
                pltpu.VMEM((head_rows, rows), jnp.float32),
                pltpu.VMEM((head_rows, rows), jnp.float32),
                pltpu.VMEM((keys, all_columns), jnp.bfloat16),
                pltpu.VMEM((keys, all_columns), jnp.bfloat16),
                pltpu.VMEM((all_columns, pair), jnp.bfloat16),
                pltpu.VMEM((all_columns, pair), jnp.bfloat16),
            ],
        ),
        out_shape=[
            jax.ShapeDtypeStruct((count, rows, width), jnp.bfloat16),
            jax.ShapeDtypeStruct((half_parts, count, rows, pair), jnp.bfloat16),
            jax.ShapeDtypeStruct((half_parts, count, rows, pair), jnp.bfloat16),
        ],
        compiler_params=pltpu.CompilerParams(vmem_limit_bytes=32 * MIB),
        cost_estimate=NO_COST,
        name="attention_backward",
    )

    return run_forward, [call_backward(run) for run in range(runs)]


def in_hbm(arrays):
    return [pltpu.with_memory_space_constraint(array, pltpu.HBM) for array in arrays]


def ffn_kernels(rows, width, chunks, chunk, wt_half, groups):
    count = chunks // groups
    units = count * chunk
    all_rows = 2 * rows
    block_rows = width // (2 * wt_half)
    hbm = pl.BlockSpec(memory_space=pltpu.HBM)
    vmem = pl.BlockSpec(memory_space=pltpu.VMEM)
    smem = pl.BlockSpec(memory_space=pltpu.SMEM)

    def fetch(place_ref, weights, which, held, sem):
        copies = []
        for n, array in enumerate(weights):
            for block in range(wt_half):
                row = pl.multiple_of((place_ref[n % 2] + block) * block_rows, 16)
                copies.append(
                    pltpu.make_async_copy(
                        array.at[block, pl.ds(which * block_rows, block_rows), :],
                        held.at[pl.ds(row, block_rows), pl.ds(n // 2 * chunk, chunk)],
                        sem.at[len(copies)],
                    )
                )
        for copy in copies:
            copy.start()
        return copies

    def first(place_ref, *args):
        inputs, grads, turned_ref, bias_ref, weights = args[0:2], args[2:4], args[4], args[5], args[6 : 6 + 2 * count]
        act_ref, grad_ref, *outs = args[6 + 2 * count : 8 + 3 * count]
        bias_grad_ref, held_up, held_down, product, sems, out_sems = args[8 + 3 * count :]
        ups = fetch(place_ref, weights, 0, held_up, sems.at[0])
        downs = fetch(place_ref, weights, 1, held_down, sems.at[1])
        for copy in ups + downs:
            copy.wait()
        sums = jnp.zeros((1, units), jnp.float32)
        for s in range(2):
            here = slice(s * rows, (s + 1) * rows)
            up = dot(inputs[s][...], held_up[...]) + bias_ref[...]
            value, slope = gelu_both(up)
            grad = dot(grads[s][...], held_down[...]) * slope
            act_ref[here, :] = low(value)
            grad_ref[here, :] = low(grad)
            sums = sums + jnp.sum(grad, axis=0, keepdims=True)
        bias_grad_ref[...] = sums
        store_product(turned_ref, act_ref, outs, product, out_sems)

    def store_product(turned, right, outs, product, out_sems):
        sent = []
        for m, out in enumerate(outs):
            cols = slice(m * chunk, (m + 1) * chunk)
            product[:, cols] = low(dot(turned[...], right[:, cols]))
            sent.append(pltpu.make_async_copy(product.at[:, pl.ds(m * chunk, chunk)], out, out_sems.at[m]))
            sent[-1].start()
        for copy in sent:
            copy.wait()

    def back(which):
        def kernel(place_ref, *args):
            sources, weights = args[:groups], args[groups : groups + 2 * chunks]
            own_ref, other_ref, held, sems = args[groups + 2 * chunks :]
            for copy in fetch(place_ref, weights, which, held, sems):
                copy.wait()
            for s, ref in enumerate((own_ref, other_ref)):
                here = slice(s * rows, (s + 1) * rows)
                total = cols_dot(sources[0][here, :], held[:, :units])
                for g in range(1, groups):
                    total = total + cols_dot(sources[g][here, :], held[:, g * units : (g + 1) * units])
                ref[...] = total.astype(ref.dtype)

        return pl.pallas_call(
            kernel,
            in_specs=[smem] + [vmem] * groups + [hbm] * (2 * chunks),
            out_specs=[vmem] * 2,
            out_shape=[
                jax.ShapeDtypeStruct((rows, width), jnp.float32),
                jax.ShapeDtypeStruct((rows, width), jnp.bfloat16),
            ],
            scratch_shapes=[
                pltpu.VMEM((width, chunks * chunk), jnp.bfloat16),
                pltpu.SemaphoreType.DMA((2 * chunks * wt_half,)),
            ],
            compiler_params=pltpu.CompilerParams(vmem_limit_bytes=20 * MIB),
            cost_estimate=NO_COST,
            name="ffn_back" if which == 0 else "ffn_down",
        )

    def third(*args):
        inputs, sources, outs = args[0:2], args[2 : 2 + groups], args[2 + groups : 2 + groups + chunks]
        turned, products, out_sems = args[2 + groups + chunks :]
        turn(inputs, turned)
        sent = []
        for m, out in enumerate(outs):
            cols = slice(m % count * chunk, (m % count + 1) * chunk)
            products[m] = low(dot(turned[...], sources[m // count][:, cols]))
            sent.append(pltpu.make_async_copy(products.at[m], out, out_sems.at[m]))
            sent[-1].start()
        for copy in sent:
            copy.wait()

    run_first = pl.pallas_call(
        first,
        in_specs=[smem] + [vmem] * 6 + [hbm] * (2 * count),
        out_specs=[vmem] * 2 + [hbm] * count + [vmem],
        out_shape=[pltpu.VMEM((all_rows, units), jnp.bfloat16)] * 2
        + [pltpu.HBM((width, chunk), jnp.bfloat16)] * count
        + [jax.ShapeDtypeStruct((1, units), jnp.float32)],
        scratch_shapes=[
            pltpu.VMEM((width, units), jnp.bfloat16),
            pltpu.VMEM((width, units), jnp.bfloat16),
            pltpu.VMEM((width, units), jnp.bfloat16),
            pltpu.SemaphoreType.DMA((2, 2 * count * wt_half)),
            pltpu.SemaphoreType.DMA((count,)),
        ],
        compiler_params=pltpu.CompilerParams(vmem_limit_bytes=36 * MIB),
        cost_estimate=NO_COST,
        name="ffn_first",
    )
    run_third = pl.pallas_call(
        third,
        in_specs=[vmem] * (2 + groups),
        out_specs=[hbm] * chunks,
        out_shape=[pltpu.HBM((width, chunk), jnp.bfloat16)] * chunks,
        scratch_shapes=[
            pltpu.VMEM((width, all_rows), jnp.bfloat16),
            pltpu.VMEM((chunks, width, chunk), jnp.bfloat16),
            pltpu.SemaphoreType.DMA((chunks,)),
        ],
        compiler_params=pltpu.CompilerParams(vmem_limit_bytes=24 * MIB),
        cost_estimate=NO_COST,
        name="ffn_grads",
    )
    return run_first, back(0), run_third, back(1)


def turn(refs, turned):
    rows = refs[0].shape[0]
    for s, ref in enumerate(refs):
        for i in range(rows // 128):
            block = wide(ref[i * 128 : (i + 1) * 128, :])
            turned[:, s * rows + i * 128 : s * rows + (i + 1) * 128] = low(block.T)


def turn_both(own, other):
    vmem = pl.BlockSpec(memory_space=pltpu.VMEM)
    rows, width = own.shape
    return pl.pallas_call(
        lambda a, b, out: turn((a, b), out),
        in_specs=[vmem] * 2,
        out_specs=vmem,
        out_shape=jax.ShapeDtypeStruct((width, 2 * rows), own.dtype),
        compiler_params=pltpu.CompilerParams(vmem_limit_bytes=16 * MIB),
        cost_estimate=NO_COST,
        name="turn",
    )(own, other)


def out_projection(rows, width, wt_count, chips, piece):
    def kernel(place_ref, attended, stream, bias, gain, shift, even_ref, odd_ref, hidden_ref, normed_ref, weight_ref, held, sems):
        chip, core = place_ref[0] // 2, place_ref[0] % 2
        copies = []
        for p, ref in enumerate((even_ref, odd_ref)):
            for m in range(chips):
                for z in range(wt_count):
                    row = pl.multiple_of((z * chips + (chip ^ m)) * piece, 16)
                    column = pl.multiple_of((core ^ p) * (width // 2), 128)
                    copies.append(
                        pltpu.make_async_copy(
                            ref.at[m, z],
                            held.at[pl.ds(row, piece), pl.ds(column, width // 2)],
                            sems.at[len(copies)],
                        )
                    )
                    copies[-1].start()
        for copy in copies:
            copy.wait()
        hidden = wide(stream[...]) + dot(attended[...], held[...]) + bias[...]
        hidden_ref[...] = hidden
        normed_ref[...] = low(layer_norm(hidden, gain[...], shift[...]))
        weight_ref[...] = held[...]

    vmem = pl.BlockSpec(memory_space=pltpu.VMEM)
    hbm = pl.BlockSpec(memory_space=pltpu.HBM)
    return pl.pallas_call(
        kernel,
        in_specs=[pl.BlockSpec(memory_space=pltpu.SMEM)] + [vmem] * 5 + [hbm] * 2,
        out_specs=[vmem] * 3,
        out_shape=[
            jax.ShapeDtypeStruct((rows, width), jnp.float32),
            jax.ShapeDtypeStruct((rows, width), jnp.bfloat16),
            jax.ShapeDtypeStruct((width, width), jnp.bfloat16),
        ],
        scratch_shapes=[pltpu.VMEM((width, width), jnp.bfloat16), pltpu.SemaphoreType.DMA((2 * chips * wt_count,))],
        compiler_params=pltpu.CompilerParams(vmem_limit_bytes=20 * MIB),
        cost_estimate=NO_COST,
        name="out_projection",
    )


def ffn_plain(chunks, chunk):
    def first(_, own, other, grad_own, grad_other, turned, bias, up, down):
        value, slope = gelu_both(dot(jnp.concatenate([own, other]), up) + bias)
        grad = low(dot(jnp.concatenate([grad_own, grad_other]), down) * slope)
        act = low(value)
        sums = jnp.sum(wide(grad), axis=0, keepdims=True)
        return [act, grad] + jnp.split(low(dot(turned, act)), chunks, axis=1) + [sums]

    def back(_, source, weights):
        own, other = jnp.split(cols_dot(source, weights), 2)
        return own, low(other)

    def third(own, other, grad):
        return jnp.split(low(rows_dot(jnp.concatenate([own, other]), grad)), chunks, axis=1)

    return first, back, third, back


def attn_grads(rows, width, row_groups, parts, piece):
    def kernel(place_ref, left_a, right_a, left_b, right_b, even_ref, odd_ref, turned, total):
        place = place_ref[0]
        for n, (left, right) in enumerate(((left_a, right_a), (left_b, right_b))):
            for i in range(rows // 128):
                turned[:, i * 128 : (i + 1) * 128] = low(wide(left[i * 128 : (i + 1) * 128, :]).T)
            total[:, n * width : (n + 1) * width] = dot(turned[...], right[...])
        for k in range(parts):
            ref = odd_ref if k % 2 else even_ref
            for w in range(row_groups):
                at = pl.multiple_of(w * piece * parts + (place ^ k) * piece, 8)
                ref[k // 2, w] = low(total[pl.ds(at, piece), :])

    vmem = pl.BlockSpec(memory_space=pltpu.VMEM)
    shape = jax.ShapeDtypeStruct((parts // 2, row_groups, piece, 2 * width), jnp.bfloat16)
    return pl.pallas_call(
        kernel,
        grid_spec=pltpu.PrefetchScalarGridSpec(
            num_scalar_prefetch=1,
            grid=(),
            in_specs=[vmem] * 4,
            out_specs=[vmem] * 2,
            scratch_shapes=[pltpu.VMEM((width, rows), jnp.bfloat16), pltpu.VMEM((width, 2 * width), jnp.float32)],
        ),
        out_shape=[shape] * 2,
        compiler_params=pltpu.CompilerParams(vmem_limit_bytes=24 * MIB),
        cost_estimate=NO_COST,
        name="attn_grads",
    )


def attn_update(rows, columns, width, parts, piece):
    qkv = columns - width

    def kernel(place_ref, even_ref, odd_ref, master, first, second, *outs):
        place = place_ref[0]
        for k in range(parts):
            ref = odd_ref if k % 2 else even_ref
            here = pl.ds(pl.multiple_of((place ^ k) * piece, 8), piece)
            for cols, source in (
                (slice(0, width), slice(0, width)),
                (slice(width, qkv), slice(2 * width, columns)),
                (slice(qkv, columns), slice(width, 2 * width)),
            ):
                grad = wide(ref[k // 2, :, source])
                got = adam_update(master[here, cols], grad, first[here, cols], second[here, cols], 0.1, 0.1)
                outs[0][here, cols] = got[0]
                outs[1][here, cols] = got[1]
                outs[2][here, cols] = got[2]

    vmem = pl.BlockSpec(memory_space=pltpu.VMEM)
    return pl.pallas_call(
        kernel,
        grid_spec=pltpu.PrefetchScalarGridSpec(
            num_scalar_prefetch=1, grid=(), in_specs=[vmem] * 5, out_specs=[vmem] * 3, scratch_shapes=[]
        ),
        out_shape=[jax.ShapeDtypeStruct((rows, columns), jnp.float32)] * 3,
        compiler_params=pltpu.CompilerParams(vmem_limit_bytes=20 * MIB),
        cost_estimate=NO_COST,
        name="attn_update",
    )


def ffn_update(rows, units, parts, chunk):
    per_row = 2 * units // 128
    step = 32
    lines = step * per_row

    def kernel(place_ref, *refs):
        pieces, (master, first, second) = refs[:parts], refs[parts : parts + 3]
        first_out, second_out, master_out, total = refs[parts + 3 :]
        place = place_ref[0]
        for k in range(parts):
            base = (place ^ k) * (2 * chunk // 128)
            for j in range(chunk // 128):
                for which in range(2):
                    here = pl.ds(base + 2 * j + which, step, per_row)
                    total[here, :] = wide(pieces[k][which, :, j * 128 : (j + 1) * 128])
        got = adam_update(master[...], total[...], first[...], second[...], 0.1, 0.1)
        first_out[...] = got[0]
        second_out[...] = got[1]
        master_out[...] = got[2]

    block = pl.BlockSpec((lines, 128), lambda i, *_: (i, 0))
    piece = pl.BlockSpec((2, step, chunk), lambda i, *_: (0, i, 0))
    shape = jax.ShapeDtypeStruct((rows * per_row, 128), jnp.float32)
    call = pl.pallas_call(
        kernel,
        grid_spec=pltpu.PrefetchScalarGridSpec(
            num_scalar_prefetch=1,
            grid=(rows // step,),
            in_specs=[piece] * parts + [block] * 3,
            out_specs=[block] * 3,
            scratch_shapes=[pltpu.VMEM((lines, 128), jnp.float32)],
        ),
        out_shape=[shape] * 3,
        compiler_params=pltpu.CompilerParams(vmem_limit_bytes=20 * MIB),
        cost_estimate=NO_COST,
        name="ffn_update",
    )

    def fold(array):
        return jnp.swapaxes(array.reshape(rows, 2, units // 128, 128), 1, 2).reshape(-1, 128)

    def unfold(array):
        return jnp.swapaxes(array.reshape(rows, units // 128, 2, 128), 1, 2).reshape(rows, 2, units)

    def run(place, pieces, master, first, second):
        got = call(place, *pieces, fold(master), fold(first), fold(second))
        return tuple(unfold(array) for array in got)

    return run


def shards(
    tokens,
    doc_starts,
    attn_master,
    attn_mom,
    attn_sq,
    ffn_master,
    ffn_mom,
    ffn_sq,
    small_master,
    small_mom,
    small_sq,
    cotangent,
):
    ctx_count = lax.axis_size("ctx")
    ctx_place = lax.axis_index("ctx")
    wt_count = lax.axis_size("wt")
    batches, rows_here, width = tokens.shape
    heads = width // HS
    qkv_cols = width + 2 * HS
    all_rows = batches * rows_here
    shard_rows = attn_master.shape[0]
    piece_rows = shard_rows // ctx_count
    chunk = FF // ctx_count
    order = ctx_place ^ jnp.arange(ctx_count, dtype=jnp.int32)
    (
        gain_one,
        shift_one,
        gain_two,
        shift_two,
        bias_query,
        bias_out,
        bias_proj,
        bias_value,
        bias_hidden,
    ) = split_small(small_master)

    runs = 2 if batches % 2 == 0 else 1
    places = [jnp.stack([ctx_place, jnp.int32(run * (batches // runs))]) for run in range(runs)]
    place = places[0]
    wt_half = wt_count // 2
    near_row = lax.axis_index("wt") // wt_half * wt_half
    row_starts = jnp.stack([near_row, wt_half - near_row])
    chips = ctx_count // 2

    def in_order(even, odd):
        buffer = jnp.zeros((ctx_count,) + even.shape[1:], even.dtype)
        for m in range(chips):
            buffer = put(buffer, even[m][None], ctx_place ^ (2 * m), 0)
            buffer = put(buffer, odd[m][None], ctx_place ^ (2 * m + 1), 0)
        return buffer

    fitted = chunk % 128 == 0 and shard_rows % 32 == 0 and piece_rows % 8 == 0

    attn_piece = low(take(attn_master, ctx_place, 0, piece_rows))
    qkv_blocks = in_order(*gather_ctx(gather_wt(attn_piece[:, :qkv_cols])))
    weight_qkv = jnp.swapaxes(qkv_blocks, 0, 1).reshape(width, qkv_cols)
    ffn_piece = low(jnp.swapaxes(take(ffn_master, ctx_place, 2, chunk), 0, 1)).reshape(2 * shard_rows, chunk)
    out_groups = width // chunk
    out_rows = shard_rows * out_groups // ctx_count
    out_piece = lax.dynamic_slice(
        attn_master,
        (ctx_place // out_groups * out_rows, qkv_cols + ctx_place % out_groups * chunk),
        (out_rows, chunk),
    )
    near, far = gather_wt_halves(jnp.concatenate([ffn_piece, low(out_piece)]))
    out_near, out_far = near[:, 2 * shard_rows :], far[:, 2 * shard_rows :]
    near, far = near[:, : 2 * shard_rows], far[:, : 2 * shard_rows]
    out_own = jnp.where(near_row == 0, jnp.concatenate([out_near, out_far]), jnp.concatenate([out_far, out_near]))
    back_low = cotangent.reshape(all_rows, width)
    back_rows = wide(back_low)
    back_other = xor_send(back_low, 1)
    back_turned = turn_both(back_low, back_other) if fitted else jnp.concatenate([back_low, back_other]).T
    bias_parts = bias_hidden.reshape(ctx_count, chunk)[order[::2]].reshape(1, chips * chunk)

    run_forward, run_backward = attention_kernels(batches, rows_here, width, ctx_count, runs)
    stream = wide(tokens.reshape(all_rows, width))
    normed, norm_back_one = jax.vjp(layer_norm, stream, gain_one, shift_one)
    normed_low = low(normed)
    mixed = dot(normed_low, weight_qkv)
    queries = low(mixed[:, :width] + bias_query).reshape(batches, rows_here, width)
    kv_bias = jnp.concatenate([jnp.zeros((HS,), jnp.float32), bias_value])
    kv_local = low(mixed[:, width:] + kv_bias).reshape(batches, rows_here, 2 * HS)
    near_parts = [near] + ([xor_send(near, 2), xor_send(near, 4)] if chips == 4 else [])
    kv_even = jnp.stack(gather_chips(kv_local))
    out_own = after(out_own, kv_even)
    out_even, out_odd = gather_ctx(out_own)
    far = after(far, kv_even)
    kv_odd = xor_send(kv_even, 1)
    queries = after(queries, back_turned, bias_parts)
    attended_low, attended, logs = run_forward(doc_starts, place, queries, kv_even, kv_odd)
    attended_low = attended_low.reshape(all_rows, width)
    if chips == 4:
        far_parts = [far, xor_send(far, 2), xor_send(far, 4)]
        near_parts.append(xor_send(after(near_parts[1], kv_odd), 4))
        far_parts.append(xor_send(after(far_parts[2], attended_low), 2))
    else:
        near_parts, far_parts = gather_chips(near), gather_chips(far)
    if fitted:
        hidden, normed_two_low, weight_out = out_projection(all_rows, width, wt_count, chips, out_rows)(
            place, attended_low, tokens.reshape(all_rows, width), bias_out[None], gain_two[None], shift_two[None],
            *in_hbm([out_even, out_odd])
        )
    else:
        weight_out = in_order(out_even, out_odd).reshape(-1, out_groups, wt_count, out_rows, chunk)
        weight_out = jnp.transpose(weight_out, (2, 0, 3, 1, 4)).reshape(width, width)
        hidden = stream + dot(attended_low, weight_out) + bias_out
        normed_two_low = low(layer_norm(hidden, gain_two, shift_two))
    norm_back_two = jax.vjp(layer_norm, hidden, gain_two, shift_two)[1]
    normed_two_other = xor_send(normed_two_low, 1)

    if fitted:
        groups = 2
        ffn_first, ffn_back, ffn_third, ffn_down = ffn_kernels(all_rows, width, chips, chunk, wt_half, groups)
        up_weights = down_weights = in_hbm([part for pair in zip(near_parts, far_parts) for part in pair])
        first_weights = [up_weights[: len(up_weights) // 2], up_weights[len(up_weights) // 2 :]]
    else:
        groups = 1
        ffn_first, ffn_back, ffn_third, ffn_down = ffn_plain(chips, chunk)
        ordered = []
        for pair in zip(near_parts, far_parts):
            both = jnp.stack(pair)
            both = jnp.where(near_row == 0, both, both[::-1])
            ordered.append(both.reshape((wt_count,) + pair[0].shape[1:]))
        up_weights = [jnp.concatenate([p[:, :shard_rows].reshape(width, chunk) for p in ordered], axis=1)]
        down_weights = [jnp.concatenate([p[:, shard_rows:].reshape(width, chunk) for p in ordered], axis=1)]
        first_weights = [up_weights + down_weights]
    acts, unit_grads, down_grads, hidden_grads = [], [], [], []
    for weights, bias in zip(first_weights, jnp.split(bias_parts, groups, axis=1)):
        act, unit_grad, *got = ffn_first(
            row_starts, normed_two_low, normed_two_other, back_low, back_other, back_turned, bias, *weights
        )
        acts.append(act)
        unit_grads.append(unit_grad)
        down_grads += got[:-1]
        hidden_grads.append(got[-1].reshape(-1, chunk))
    hidden_grads = jnp.concatenate(hidden_grads)
    own_part, other_part = ffn_back(row_starts, *unit_grads, *up_weights)
    other_part = xor_send(other_part, 1)
    up_grads = ffn_third(normed_two_low, normed_two_other, *unit_grads)
    grad_normed_two = own_part + wide(other_part)

    grad_hidden_part, grad_gain_two, grad_shift_two = norm_back_two(grad_normed_two)
    grad_hidden = back_rows + grad_hidden_part
    grad_hidden_low = low(grad_hidden)
    grad_attended = low(cols_dot(grad_hidden_low, weight_out)).reshape(batches, rows_here, width)

    if chips == 4:
        met = after(xor_send(down_grads[3], 4), up_grads[0])
        down_along_x = xor_send(low(wide(down_grads[1]) + wide(met)), 2)
        down_along_y = xor_send(down_grads[2], 4)

    backs = [
        run(doc_starts, places[i], queries, kv_even, kv_odd, attended, logs, grad_attended)
        for i, run in enumerate(run_backward[:1])
    ]
    if chips == 4:
        met = after(xor_send(up_grads[3], 2), backs[0][0])
        up_along_x = xor_send(after(up_grads[1], grad_attended), 2)
        up_along_y = xor_send(low(wide(up_grads[2]) + wide(met)), 4)
    grad_attended = after(grad_attended, backs[0][0])
    backs += [
        run(doc_starts, places[i + 1], queries, kv_even, kv_odd, attended, logs, grad_attended)
        for i, run in enumerate(run_backward[1:])
    ]
    last = backs[-1][0]
    grad_query = jnp.concatenate([back[0] for back in backs]).reshape(all_rows, width)
    kv_halves = [low(wide(back[1]) + wide(xor_send(back[2], 1))) for back in backs]
    kv_half = jnp.concatenate(kv_halves, axis=1)
    grad_kv = low(scatter_chips([kv_half[m] for m in range(chips)])).reshape(all_rows, 2 * HS)

    if chips == 4:
        down_along_x, down_along_y = after(down_along_x, last), after(down_along_y, last)
        up_along_x, up_along_y = after(up_along_x, last), after(up_along_y, last)
        down_sum = wide(down_grads[0]) + wide(down_along_x) + wide(down_along_y)
        up_sum = wide(up_grads[0]) + wide(up_along_x) + wide(up_along_y)
    else:
        down_sum, up_sum = scatter_chips(down_grads), scatter_chips(up_grads)
    both_sums = jnp.stack([low(up_sum), low(down_sum)]).reshape(2, wt_count, shard_rows, chunk)
    ffn_part = low(scatter_wt(both_sums, 1)[:, 0])
    ffn_even, ffn_odd = gather_ctx(ffn_part)

    if fitted:
        wide_even, wide_odd = attn_grads(all_rows, width, wt_count, ctx_count, piece_rows)(
            place, normed_low, grad_query, attended_low, grad_hidden_low
        )
    else:
        grad_wide = jnp.concatenate(
            [low(rows_dot(normed_low, grad_query)), low(rows_dot(attended_low, grad_hidden_low))], axis=1
        )
        grad_wide = grad_wide.reshape(wt_count, ctx_count, piece_rows, 2 * width)
        pieces = [take(grad_wide, ctx_place ^ k, 1, 1)[:, 0] for k in range(ctx_count)]
        wide_even, wide_odd = jnp.stack(pieces[::2]), jnp.stack(pieces[1::2])
    wide_half = low(wide(wide_even) + wide(xor_send(wide_odd, 1)))

    grad_normed = cols_dot(grad_query, weight_qkv[:, :width]) + cols_dot(grad_kv, weight_qkv[:, width:])
    grad_stream_part, grad_gain_one, grad_shift_one = norm_back_one(grad_normed)
    input_grad = (grad_hidden + grad_stream_part).reshape(batches, rows_here, width)

    own_units = jnp.zeros((ctx_count, chunk), jnp.float32)
    for m in range(chips):
        own_units = put(own_units, hidden_grads[m][None], ctx_place ^ (2 * m), 0)
    grad_small = jnp.concatenate(
        [
            grad_gain_one,
            grad_shift_one,
            grad_gain_two,
            grad_shift_two,
            jnp.sum(wide(grad_query), axis=0),
            jnp.sum(grad_hidden, axis=0),
            jnp.sum(back_rows, axis=0),
            jnp.sum(wide(grad_kv[:, HS:]), axis=0),
            own_units.reshape(FF),
        ]
    )
    small_size = grad_small.shape[0]
    small_columns = 128 * -(-small_size // (128 * piece_rows * ctx_count))
    small_blocks = jnp.pad(low(grad_small), (0, ctx_count * piece_rows * small_columns - small_size))
    small_blocks = small_blocks.reshape(ctx_count, 1, piece_rows, small_columns)
    kv_blocks = low(rows_dot(normed_low, grad_kv)).reshape(wt_count, ctx_count, piece_rows, 2 * HS)
    kv_blocks = jnp.swapaxes(kv_blocks, 0, 1)
    small_blocks = jnp.broadcast_to(small_blocks, kv_blocks.shape[:3] + (small_columns,))
    tail = jnp.concatenate([kv_blocks, small_blocks], axis=3)
    tail_pieces = [take(tail, ctx_place ^ k, 0, 1)[0] for k in range(ctx_count)]
    tail_even, tail_odd = jnp.stack(tail_pieces[::2]), jnp.stack(tail_pieces[1::2])
    tail_half = low(wide(tail_even) + wide(xor_send(tail_odd, 1)))
    attn_half = jnp.concatenate([wide_half, tail_half], axis=3)
    own_part, other_part = ffn_down(row_starts, *[after(act, attn_half) for act in acts], *down_weights)
    down_vals = own_part + wide(xor_send(other_part, 1))
    layer_out = low(hidden + down_vals + bias_proj).reshape(batches, rows_here, width)
    attn_part = scatter_chips([attn_half[m] for m in range(chips)])
    attn_even, attn_odd = gather_ctx(low(scatter_wt(low(attn_part), 0)[0]))
    attn_columns = attn_master.shape[1]
    small_total = in_order(attn_even[..., attn_columns:], attn_odd[..., attn_columns:])
    small_total = wide(small_total.reshape(-1)[:small_size])

    if fitted:
        attn_new = attn_update(shard_rows, attn_columns, width, ctx_count, piece_rows)(
            place, attn_even, attn_odd, attn_master, attn_mom, attn_sq
        )
        pieces = [(ffn_even, ffn_odd)[k % 2][k // 2] for k in range(ctx_count)]
        ffn_new = ffn_update(shard_rows, FF, ctx_count, chunk)(place, pieces, ffn_master, ffn_mom, ffn_sq)
    else:
        attn_total = wide(in_order(attn_even, attn_odd).reshape(shard_rows, attn_columns + small_columns))
        attn_total = jnp.concatenate(
            [attn_total[:, :width], attn_total[:, 2 * width : attn_columns], attn_total[:, width : 2 * width]], axis=1
        )
        attn_new = adam_update(attn_master, attn_total, attn_mom, attn_sq, 0.1, 0.1)
        ffn_total = jnp.transpose(in_order(ffn_even, ffn_odd), (2, 1, 0, 3)).reshape(shard_rows, 2, FF)
        ffn_new = adam_update(ffn_master, wide(ffn_total), ffn_mom, ffn_sq, 0.1, 0.1)
    small_new = adam_update(small_master, small_total, small_mom, small_sq, 1.0, 0.0)
    return (layer_out, input_grad) + tuple(attn_new) + tuple(ffn_new) + small_new


def solution(mesh):
    rows, cube = P("wt", None), P("wt", None, None)
    flow = P("wt", "ctx", None)
    in_specs = (flow, rows, rows, rows, rows, cube, cube, cube, P(), P(), P(), flow)
    out_specs = (flow, flow, rows, rows, rows, cube, cube, cube, P(), P(), P())
    return jax.shard_map(shards, mesh=mesh, in_specs=in_specs, out_specs=out_specs, check_vma=False)
```

```python
import jax
import jax.numpy as jnp
from jax import lax
from jax.experimental import pallas as pl
from jax.experimental.pallas import tpu as pltpu
from jax.sharding import PartitionSpec as P

D = 768
HS = 64
FF = 3072
STEP = 10


NORM_EPS = 1e-05
GELU_COEF = 0.7978845608028654
GELU_CUBE = 0.044715
BETA_ONE = 0.9
BETA_TWO = 0.95
ADAM_EPS = 1e-08
VMEM_LIMIT = 56 << 20
NO_COST = pl.CostEstimate(flops=0, bytes_accessed=0, transcendentals=0)


def layer_norm(values, gain, shift):
    centre = values - jnp.mean(values, axis=-1, keepdims=True)
    spread = jnp.mean(centre * centre, axis=-1, keepdims=True)
    return centre * lax.rsqrt(spread + NORM_EPS) * gain + shift


def gelu_both(u):
    square = u * u
    share = 0.5 * jnp.tanh(u * (GELU_COEF * GELU_CUBE * square + GELU_COEF)) + 0.5
    bend = u * (6.0 * GELU_COEF * GELU_CUBE * square + 2.0 * GELU_COEF)
    return u * share, share * ((1.0 - share) * bend) + share


def split_small(small):
    return (
        small[0:D],
        small[D : 2 * D],
        small[2 * D : 3 * D],
        small[3 * D : 4 * D],
        small[4 * D : 5 * D],
        small[5 * D : 6 * D],
        small[6 * D : 7 * D],
        small[7 * D : 7 * D + HS],
        small[7 * D + HS :],
    )


def rows_dot(left, right):
    return lax.dot_general(
        left, right, (((0,), (0,)), ((), ())), preferred_element_type=jnp.float32
    )


def cols_dot(left, right):
    return lax.dot_general(
        left, right, (((1,), (1,)), ((), ())), preferred_element_type=jnp.float32
    )


def dot(left, right):
    return jnp.dot(left, right, preferred_element_type=jnp.float32)


def low(values):
    return values.astype(jnp.bfloat16)


def wide(values):
    return values.astype(jnp.float32)


def adam_update(master, gradient, first, second, step_rate, decay_rate):
    first_new = BETA_ONE * first + (1.0 - BETA_ONE) * gradient
    second_new = BETA_TWO * second + (1.0 - BETA_TWO) * gradient * gradient
    first_hat = first_new / (1.0 - BETA_ONE**STEP)
    second_hat = second_new / (1.0 - BETA_TWO**STEP)
    master_new = master - step_rate * (
        first_hat / (jnp.sqrt(second_hat) + ADAM_EPS) + decay_rate * master
    )
    return (first_new, second_new, master_new)


def xor_send(array, mask):
    count = lax.axis_size("ctx")
    return lax.ppermute(array, "ctx", [(i, i ^ mask) for i in range(count)])


def xor_wt(array, mask):
    count = lax.axis_size("wt")
    return lax.ppermute(array, "wt", [(i, i ^ mask) for i in range(count)])


class Steps:
    def __init__(self):
        self.last = ()

    def __call__(self, function, *args):
        flat, tree = jax.tree.flatten(args)
        held = lax.optimization_barrier(tuple(flat) + self.last)[: len(flat)]
        result = function(*jax.tree.unflatten(tree, held))
        self.last = tuple(jax.tree.leaves(result))
        return result


def put(buffer, piece, place, axis):
    starts = [0] * buffer.ndim
    starts[axis] = place * piece.shape[axis]
    return lax.dynamic_update_slice(buffer, piece, starts)


def take(buffer, place, axis, size):
    return lax.dynamic_slice_in_dim(buffer, place * size, size, axis)


def attention_kernels(batches, rows, width, parts, runs):
    half_parts = parts // 2
    keys = parts * rows
    pair = 2 * HS
    groups = width // (2 * pair)
    factor = HS ** (-0.5) * 1.4426950408889634
    masks = list(range(0, parts, 2)) + list(range(1, parts, 2))

    def lanes(shape):
        return lax.broadcasted_iota(jnp.int32, shape, 1)

    def spread(even_ref, odd_ref, key_ref, value_ref):
        for j in range(parts):
            ref = even_ref if j < half_parts else odd_ref
            block = wide(ref[j % half_parts, 0])
            turned = pltpu.roll(block, HS, 1)
            first = lanes(block.shape) < HS
            here = pl.ds(j * rows, rows)
            key_ref[0, here, :] = low(jnp.where(first, block, 0.0))
            key_ref[1, here, :] = low(jnp.where(first, 0.0, turned))
            value_ref[0, here, :] = low(jnp.where(first, turned, 0.0))
            value_ref[1, here, :] = low(jnp.where(first, 0.0, block))

    def doc_begin(starts_ref, stream, positions):
        begin = jnp.zeros_like(positions)
        for j in range(starts_ref.shape[1]):
            start = starts_ref[stream, j]
            begin = jnp.where(start <= positions, jnp.maximum(begin, start), begin)
        return begin

    def forward(starts_ref, place_ref, query_ref, even_ref, odd_ref, low_ref, full_ref, log_ref, cap, key, value):
        stream, place = pl.program_id(0), place_ref[0]
        spread(even_ref, odd_ref, key, value)
        query_pos = place * rows + lax.broadcasted_iota(jnp.int32, (rows, 1), 0)
        begin = doc_begin(starts_ref, stream, query_pos)
        for j, mask in enumerate(masks):
            key_pos = (place ^ mask) * rows + lax.broadcasted_iota(jnp.int32, (rows, rows), 1)
            allowed = (key_pos >= begin) & (key_pos <= query_pos)
            cap[:, j * rows : (j + 1) * rows] = jnp.where(allowed, 3.0e38, -1e30)
        log_ref[...] = jnp.zeros_like(log_ref)

        def group(g, carry):
            at = pl.multiple_of(g * 2 * pair, 2 * pair)
            both = query_ref[0, :, pl.ds(at, 2 * pair)]
            two = jnp.concatenate([both[:, :pair], both[:, pair:]], axis=0)
            limit = cap[...]
            limit = jnp.concatenate([limit, limit], axis=0)
            total = jnp.zeros((2 * rows, pair), jnp.float32)
            logs = log_ref[0]
            for half in range(2):
                scores = jnp.minimum(cols_dot(two, key[half]) * factor, limit)
                peak = jnp.max(scores, axis=1, keepdims=True)
                expo = jnp.exp2(scores - peak)
                norm = jnp.sum(expo, axis=1, keepdims=True)
                total = total + dot(low(expo), value[half]) / norm
                log = peak + jnp.log2(norm)
                column = lanes((rows, pair))
                logs = jnp.where(column == 4 * g + half, log[:rows], logs)
                logs = jnp.where(column == 4 * g + 2 + half, log[rows:], logs)
            log_ref[0] = logs
            total = jnp.concatenate([total[:rows], total[rows:]], axis=1)
            full_ref[0, :, pl.ds(at, 2 * pair)] = total
            low_ref[0, :, pl.ds(at, 2 * pair)] = low(total)
            return carry

        lax.fori_loop(0, groups, group, 0, unroll=True)

    def backward(
        starts_ref, place_ref, query_ref, even_ref, odd_ref, full_ref, log_ref, grad_ref,
        query_grad_ref, even_grad_ref, odd_grad_ref,
        cap, key, value, key_turned, log_rows, delta_rows, weight_buf, score_buf, query_buf, grad_buf,
    ):
        stream, place = pl.program_id(0) + place_ref[1], place_ref[0]
        spread(even_ref, odd_ref, key, value)
        query_pos = place * rows + lax.broadcasted_iota(jnp.int32, (1, rows), 1)
        begin = doc_begin(starts_ref, stream, query_pos)
        for j, mask in enumerate(masks):
            key_pos = (place ^ mask) * rows + lax.broadcasted_iota(jnp.int32, (rows, rows), 0)
            allowed = (key_pos >= begin) & (key_pos <= query_pos)
            cap[j * rows : (j + 1) * rows, :] = jnp.where(allowed, 3.0e38, -1e30)
            here = pl.ds(j * rows, rows)
            key_turned[:, j * rows : (j + 1) * rows] = low(wide(key[0, here, :]).T[:HS])
        log_rows[...] = log_ref[0].T[: log_rows.shape[0]]
        head_of = lax.broadcasted_iota(jnp.int32, (delta_rows.shape[0], width), 1) // HS
        chosen = (head_of == lax.broadcasted_iota(jnp.int32, (delta_rows.shape[0], width), 0)).astype(jnp.float32)
        delta_rows[...] = lax.dot_general(
            chosen, wide(grad_ref[0]) * full_ref[0], (((1,), (1,)), ((), ())),
            precision=lax.Precision.HIGHEST, preferred_element_type=jnp.float32,
        )
        first = lanes((2 * rows, pair)) < HS
        for g in range(groups):
            at = g * 2 * pair
            both, both_grad = query_ref[0, :, at : at + 2 * pair], grad_ref[0, :, at : at + 2 * pair]
            two = jnp.concatenate([both[:, :pair], both[:, pair:]], axis=0)
            two_grad = jnp.concatenate([both_grad[:, :pair], both_grad[:, pair:]], axis=0)
            limit = cap[...]
            limit = jnp.concatenate([limit, limit], axis=1)
            turned = []
            for half in range(2):
                h = 4 * g + half
                span = slice((2 * g + half) * 2 * rows, (2 * g + half + 1) * 2 * rows)
                keep = first if half == 0 else jnp.logical_not(first)
                query_buf[span, :] = low(jnp.where(keep, wide(two), 0.0))
                grad_buf[span, :] = low(jnp.where(keep, wide(two_grad), 0.0))
                log = jnp.concatenate([log_rows[h : h + 1, :], log_rows[h + 2 : h + 3, :]], axis=1)
                delta = jnp.concatenate([delta_rows[h : h + 1, :], delta_rows[h + 2 : h + 3, :]], axis=1)
                scores = jnp.minimum(cols_dot(key[half], two) * factor, limit)
                weights = jnp.exp2(scores - log)
                grad_scores = low(weights * (cols_dot(value[half], two_grad) - delta))
                weight_buf[:, span] = low(weights)
                score_buf[:, span] = grad_scores
                turned.append(dot(key_turned[...], grad_scores))
            turned = jnp.concatenate(turned, axis=0) * HS ** (-0.5)
            query_grad_ref[0, :, at : at + pair] = low(turned[:, :rows].T)
            query_grad_ref[0, :, at + pair : at + 2 * pair] = low(turned[:, rows:].T)
        for j in range(parts):
            here = pl.ds(j * rows, rows)
            value_sum = dot(weight_buf[here, :], grad_buf[...])
            key_sum = dot(score_buf[here, :], query_buf[...]) * HS ** (-0.5)
            value_sum = value_sum + pltpu.roll(value_sum, HS, 1)
            key_sum = key_sum + pltpu.roll(key_sum, HS, 1)
            ref = even_grad_ref if j < half_parts else odd_grad_ref
            ref[j % half_parts, 0] = low(jnp.where(lanes((rows, pair)) < HS, key_sum, value_sum))

    def specs(first):
        return (
            pl.BlockSpec((1, rows, width), lambda b, *_: (b + first, 0, 0)),
            pl.BlockSpec((1, rows, pair), lambda b, *_: (b + first, 0, 0)),
            pl.BlockSpec((half_parts, 1, rows, pair), lambda b, *_: (0, b + first, 0, 0)),
        )

    flow, logs, blocks = specs(0)

    shared = [
        pltpu.VMEM((2, keys, pair), jnp.bfloat16),
        pltpu.VMEM((2, keys, pair), jnp.bfloat16),
    ]
    run_forward = pl.pallas_call(
        forward,
        grid_spec=pltpu.PrefetchScalarGridSpec(
            num_scalar_prefetch=2,
            grid=(batches,),
            in_specs=[flow, blocks, blocks],
            out_specs=[flow, flow, logs],
            scratch_shapes=[pltpu.VMEM((rows, keys), jnp.float32)] + shared,
        ),
        out_shape=[
            jax.ShapeDtypeStruct((batches, rows, width), jnp.bfloat16),
            jax.ShapeDtypeStruct((batches, rows, width), jnp.float32),
            jax.ShapeDtypeStruct((batches, rows, pair), jnp.float32),
        ],
        compiler_params=pltpu.CompilerParams(vmem_limit_bytes=VMEM_LIMIT),
        cost_estimate=NO_COST,
        name="attention_forward",
    )
    head_rows = -(-(width // HS) // 8) * 8
    all_columns = rows * (width // HS)
    count = batches // runs

    def call_backward(run):
        here_flow, here_logs, here_blocks = specs(run * count)
        return pl.pallas_call(
        backward,
        grid_spec=pltpu.PrefetchScalarGridSpec(
            num_scalar_prefetch=2,
            grid=(count,),
            in_specs=[here_flow, here_blocks, here_blocks, here_flow, here_logs, here_flow],
            out_specs=[flow, blocks, blocks],
            scratch_shapes=[pltpu.VMEM((keys, rows), jnp.float32)]
            + shared
            + [
                pltpu.VMEM((HS, keys), jnp.bfloat16),
                pltpu.VMEM((head_rows, rows), jnp.float32),
                pltpu.VMEM((head_rows, rows), jnp.float32),
                pltpu.VMEM((keys, all_columns), jnp.bfloat16),
                pltpu.VMEM((keys, all_columns), jnp.bfloat16),
                pltpu.VMEM((all_columns, pair), jnp.bfloat16),
                pltpu.VMEM((all_columns, pair), jnp.bfloat16),
            ],
        ),
        out_shape=[
            jax.ShapeDtypeStruct((count, rows, width), jnp.bfloat16),
            jax.ShapeDtypeStruct((half_parts, count, rows, pair), jnp.bfloat16),
            jax.ShapeDtypeStruct((half_parts, count, rows, pair), jnp.bfloat16),
        ],
        compiler_params=pltpu.CompilerParams(vmem_limit_bytes=VMEM_LIMIT),
        cost_estimate=NO_COST,
        name="attention_backward",
    )

    return run_forward, [call_backward(run) for run in range(runs)]


def in_hbm(arrays):
    return [pltpu.with_memory_space_constraint(array, pltpu.HBM) for array in arrays]


def ffn_kernels(rows, width, chunk, wt_half):
    units = 2 * chunk
    all_rows = 2 * rows
    block_rows = width // (2 * wt_half)
    hbm = pl.BlockSpec(memory_space=pltpu.HBM)
    vmem = pl.BlockSpec(memory_space=pltpu.VMEM)
    smem = pl.BlockSpec(memory_space=pltpu.SMEM)
    params = pltpu.CompilerParams(vmem_limit_bytes=VMEM_LIMIT)

    def fetch(place_ref, weights, which, held, sem):
        copies = []
        for n, array in enumerate(weights):
            for block in range(wt_half):
                row = pl.multiple_of((place_ref[n % 2] + block) * block_rows, 16)
                copies.append(
                    pltpu.make_async_copy(
                        array.at[block, pl.ds(which * block_rows, block_rows), :],
                        held.at[pl.ds(row, block_rows), pl.ds(n // 2 * chunk, chunk)],
                        sem.at[len(copies)],
                    )
                )
        for copy in copies:
            copy.start()
        return copies

    def send(pairs, sems):
        copies = [pltpu.make_async_copy(source, out, sems.at[n]) for n, (source, out) in enumerate(pairs)]
        for copy in copies:
            copy.start()
        return copies

    def units_of(inputs, grads, bias, held_up, held_down, act, grad_units):
        sums = jnp.zeros((1, units), jnp.float32)
        for s in range(2):
            here = slice(s * rows, (s + 1) * rows)
            up = dot(inputs[s][...], held_up[...]) + bias
            value, slope = gelu_both(up)
            grad = dot(grads[s][...], held_down[...]) * slope
            act[here, :] = low(value)
            grad_units[here, :] = low(grad)
            sums = sums + jnp.sum(grad, axis=0, keepdims=True)
        return sums

    def halves(product, m):
        cols = pl.ds(m * chunk, chunk)
        return [product.at[pl.ds(h * width // 2, width // 2), cols] for h in range(2)]

    def first(
        place_ref, own, other, grad_own, grad_other, turned, bias, w0, w1, w2, w3,
        act_out, units_out, out_a, out_b, out_c, sums_out,
        held_up, held_down, act, grad_units, product, sems, out_sems,
    ):
        weights = (w0, w1, w2, w3)
        copies = fetch(place_ref, weights, 0, held_up, sems.at[0]) + fetch(place_ref, weights, 1, held_down, sems.at[1])
        for copy in copies:
            copy.wait()
        sums_out[...] = units_of((own, other), (grad_own, grad_other), bias[...], held_up, held_down, act, grad_units)
        sent = send(((act, act_out), (grad_units, units_out)), out_sems.at[0])
        product[...] = low(dot(turned[...], act[...]))
        top, bottom = halves(product, 1)
        sent += send(((product.at[:, pl.ds(0, chunk)], out_a), (top, out_b), (bottom, out_c)), out_sems.at[1])
        for copy in sent:
            copy.wait()

    def second(
        place_ref, own, other, grad_own, grad_other, turned, bias, units_first, w0, w1, w2, w3, w4, w5, w6, w7,
        act_out, units_out, out_a, out_b, sums_out, back_own, back_other,
        held_up, held_more, held_down, act, grad_units, more_units, product, sems, out_sems, more_sem,
    ):
        weights, later = (w0, w1, w2, w3), (w4, w5, w6, w7)
        copies = fetch(place_ref, weights, 0, held_up, sems.at[0]) + fetch(place_ref, weights, 1, held_down, sems.at[1])
        more = fetch(place_ref, later, 0, held_more, sems.at[2])
        more.append(pltpu.make_async_copy(units_first, more_units, more_sem))
        more[-1].start()
        for copy in copies:
            copy.wait()
        sums_out[...] = units_of((own, other), (grad_own, grad_other), bias[...], held_up, held_down, act, grad_units)
        sent = send(((act, act_out), (grad_units, units_out)), out_sems.at[0])
        product[...] = low(dot(turned[...], act[...]))
        sent += send(
            ((product.at[:, pl.ds(0, chunk)], out_a), (product.at[:, pl.ds(chunk, chunk)], out_b)), out_sems.at[1]
        )
        for copy in more:
            copy.wait()
        for s, ref in enumerate((back_own, back_other)):
            here = slice(s * rows, (s + 1) * rows)
            total = cols_dot(grad_units[here, :], held_up[...]) + cols_dot(more_units[here, :], held_more[...])
            ref[...] = total.astype(ref.dtype)
        for copy in sent:
            copy.wait()

    def third(own, other, units_a, units_b, out_0, out_1, out_2, out_3, out_4, turned, held, products, sems, out_sems):
        copies = send(((units_a, held.at[0]), (units_b, held.at[1])), sems)
        turn((own, other), turned)
        for copy in copies:
            copy.wait()
        products[1] = low(dot(turned[...], held[1]))
        top, bottom = halves(products.at[1], 1)
        sent = send(((products.at[1, :, pl.ds(0, chunk)], out_2), (top, out_3), (bottom, out_4)), out_sems.at[0])
        products[0] = low(dot(turned[...], held[0]))
        sent += send(
            ((products.at[0, :, pl.ds(0, chunk)], out_0), (products.at[0, :, pl.ds(chunk, chunk)], out_1)),
            out_sems.at[1],
        )
        for copy in sent:
            copy.wait()

    def down(place_ref, act_a, act_b, w0, w1, w2, w3, w4, w5, w6, w7, own_ref, other_ref, held_a, held_b, sems):
        copies = fetch(place_ref, (w0, w1, w2, w3), 1, held_a, sems.at[0])
        copies += fetch(place_ref, (w4, w5, w6, w7), 1, held_b, sems.at[1])
        for copy in copies:
            copy.wait()
        for s, ref in enumerate((own_ref, other_ref)):
            here = slice(s * rows, (s + 1) * rows)
            total = cols_dot(act_a[here, :], held_a[...]) + cols_dot(act_b[here, :], held_b[...])
            ref[...] = total.astype(ref.dtype)

    dma = pltpu.SemaphoreType.DMA
    held = pltpu.VMEM((width, units), jnp.bfloat16)
    flow = pltpu.VMEM((all_rows, units), jnp.bfloat16)
    flow_out = pltpu.HBM((all_rows, units), jnp.bfloat16)
    whole = pltpu.HBM((width, chunk), jnp.bfloat16)
    part = pltpu.HBM((width // 2, chunk), jnp.bfloat16)
    sums = jax.ShapeDtypeStruct((1, units), jnp.float32)
    own = jax.ShapeDtypeStruct((rows, width), jnp.float32)
    other = jax.ShapeDtypeStruct((rows, width), jnp.bfloat16)
    run_first = pl.pallas_call(
        first,
        in_specs=[smem] + [vmem] * 6 + [hbm] * 4,
        out_specs=[hbm] * 5 + [vmem],
        out_shape=[flow_out, flow_out, whole, part, part, sums],
        scratch_shapes=[held, held, flow, flow, held, dma((2, 4 * wt_half)), dma((2, 3))],
        compiler_params=params,
        cost_estimate=NO_COST,
        name="ffn_first",
    )
    run_second = pl.pallas_call(
        second,
        in_specs=[smem] + [vmem] * 6 + [hbm] * 9,
        out_specs=[hbm] * 4 + [vmem] * 3,
        out_shape=[flow_out, flow_out, whole, whole, sums, own, other],
        scratch_shapes=[held, held, held, flow, flow, flow, held, dma((3, 4 * wt_half)), dma((2, 2)), dma(())],
        compiler_params=params,
        cost_estimate=NO_COST,
        name="ffn_second",
    )
    run_third = pl.pallas_call(
        third,
        in_specs=[vmem] * 2 + [hbm] * 2,
        out_specs=[hbm] * 5,
        out_shape=[whole, whole, whole, part, part],
        scratch_shapes=[
            pltpu.VMEM((width, all_rows), jnp.bfloat16),
            pltpu.VMEM((2, all_rows, units), jnp.bfloat16),
            pltpu.VMEM((2, width, units), jnp.bfloat16),
            dma((2,)),
            dma((2, 3)),
        ],
        compiler_params=params,
        cost_estimate=NO_COST,
        name="ffn_grads",
    )
    run_down = pl.pallas_call(
        down,
        in_specs=[smem] + [vmem] * 2 + [hbm] * 8,
        out_specs=[vmem] * 2,
        out_shape=[own, other],
        scratch_shapes=[held, held, dma((2, 4 * wt_half))],
        compiler_params=params,
        cost_estimate=NO_COST,
        name="ffn_down",
    )
    return run_first, run_second, run_third, run_down


def turn(refs, turned):
    rows = refs[0].shape[0]
    for s, ref in enumerate(refs):
        for i in range(rows // 128):
            block = wide(ref[i * 128 : (i + 1) * 128, :])
            turned[:, s * rows + i * 128 : s * rows + (i + 1) * 128] = low(block.T)


def turn_both(own, other):
    vmem = pl.BlockSpec(memory_space=pltpu.VMEM)
    rows, width = own.shape
    return pl.pallas_call(
        lambda a, b, out: turn((a, b), out),
        in_specs=[vmem] * 2,
        out_specs=vmem,
        out_shape=jax.ShapeDtypeStruct((width, 2 * rows), own.dtype),
        compiler_params=pltpu.CompilerParams(vmem_limit_bytes=VMEM_LIMIT),
        cost_estimate=NO_COST,
        name="turn",
    )(own, other)


def out_projection(rows, width, wt_count, chips, piece):
    def kernel(place_ref, attended, stream, bias, gain, shift, even_ref, odd_ref, hidden_ref, normed_ref, weight_ref, held, sems):
        chip, core = place_ref[0] // 2, place_ref[0] % 2
        copies = []
        for p, ref in enumerate((even_ref, odd_ref)):
            for m in range(chips):
                for z in range(wt_count):
                    row = pl.multiple_of((z * chips + (chip ^ m)) * piece, 16)
                    column = pl.multiple_of((core ^ p) * (width // 2), 128)
                    copies.append(
                        pltpu.make_async_copy(
                            ref.at[m, z],
                            held.at[pl.ds(row, piece), pl.ds(column, width // 2)],
                            sems.at[len(copies)],
                        )
                    )
                    copies[-1].start()
        for copy in copies:
            copy.wait()
        hidden = wide(stream[...]) + dot(attended[...], held[...]) + bias[...]
        hidden_ref[...] = hidden
        normed_ref[...] = low(layer_norm(hidden, gain[...], shift[...]))
        weight_ref[...] = held[...]

    vmem = pl.BlockSpec(memory_space=pltpu.VMEM)
    hbm = pl.BlockSpec(memory_space=pltpu.HBM)
    return pl.pallas_call(
        kernel,
        in_specs=[pl.BlockSpec(memory_space=pltpu.SMEM)] + [vmem] * 5 + [hbm] * 2,
        out_specs=[vmem] * 3,
        out_shape=[
            jax.ShapeDtypeStruct((rows, width), jnp.float32),
            jax.ShapeDtypeStruct((rows, width), jnp.bfloat16),
            jax.ShapeDtypeStruct((width, width), jnp.bfloat16),
        ],
        scratch_shapes=[pltpu.VMEM((width, width), jnp.bfloat16), pltpu.SemaphoreType.DMA((2 * chips * wt_count,))],
        compiler_params=pltpu.CompilerParams(vmem_limit_bytes=VMEM_LIMIT),
        cost_estimate=NO_COST,
        name="out_projection",
    )


def attn_grads(rows, width, row_groups, parts, piece):
    def kernel(place_ref, left_a, right_a, left_b, right_b, even_ref, odd_ref, turned, total):
        place = place_ref[0]
        for n, (left, right) in enumerate(((left_a, right_a), (left_b, right_b))):
            for i in range(rows // 128):
                turned[:, i * 128 : (i + 1) * 128] = low(wide(left[i * 128 : (i + 1) * 128, :]).T)
            total[:, n * width : (n + 1) * width] = dot(turned[...], right[...])
        for k in range(parts):
            ref = odd_ref if k % 2 else even_ref
            for w in range(row_groups):
                at = pl.multiple_of(w * piece * parts + (place ^ k) * piece, 8)
                ref[k // 2, w] = low(total[pl.ds(at, piece), :])

    vmem = pl.BlockSpec(memory_space=pltpu.VMEM)
    shape = jax.ShapeDtypeStruct((parts // 2, row_groups, piece, 2 * width), jnp.bfloat16)
    return pl.pallas_call(
        kernel,
        grid_spec=pltpu.PrefetchScalarGridSpec(
            num_scalar_prefetch=1,
            grid=(),
            in_specs=[vmem] * 4,
            out_specs=[vmem] * 2,
            scratch_shapes=[pltpu.VMEM((width, rows), jnp.bfloat16), pltpu.VMEM((width, 2 * width), jnp.float32)],
        ),
        out_shape=[shape] * 2,
        compiler_params=pltpu.CompilerParams(vmem_limit_bytes=VMEM_LIMIT),
        cost_estimate=NO_COST,
        name="attn_grads",
    )


def attn_update(rows, columns, width, parts, piece):
    qkv = columns - width

    def kernel(place_ref, even_ref, odd_ref, master, first, second, *outs):
        place = place_ref[0]
        for k in range(parts):
            ref = odd_ref if k % 2 else even_ref
            here = pl.ds(pl.multiple_of((place ^ k) * piece, 8), piece)
            for cols, source in (
                (slice(0, width), slice(0, width)),
                (slice(width, qkv), slice(2 * width, columns)),
                (slice(qkv, columns), slice(width, 2 * width)),
            ):
                grad = wide(ref[k // 2, :, source])
                got = adam_update(master[here, cols], grad, first[here, cols], second[here, cols], 0.1, 0.1)
                outs[0][here, cols] = got[0]
                outs[1][here, cols] = got[1]
                outs[2][here, cols] = got[2]

    vmem = pl.BlockSpec(memory_space=pltpu.VMEM)
    return pl.pallas_call(
        kernel,
        grid_spec=pltpu.PrefetchScalarGridSpec(
            num_scalar_prefetch=1, grid=(), in_specs=[vmem] * 5, out_specs=[vmem] * 3, scratch_shapes=[]
        ),
        out_shape=[jax.ShapeDtypeStruct((rows, columns), jnp.float32)] * 3,
        compiler_params=pltpu.CompilerParams(vmem_limit_bytes=VMEM_LIMIT),
        cost_estimate=NO_COST,
        name="attn_update",
    )


def ffn_update(rows, units, parts, chunk):
    per_row = 2 * units // 128
    step = 32
    lines = step * per_row

    def kernel(place_ref, *refs):
        pieces, (master, first, second) = refs[:parts], refs[parts : parts + 3]
        first_out, second_out, master_out, total = refs[parts + 3 :]
        place = place_ref[0]
        for k in range(parts):
            base = (place ^ k) * (2 * chunk // 128)
            for j in range(chunk // 128):
                for which in range(2):
                    here = pl.ds(base + 2 * j + which, step, per_row)
                    total[here, :] = wide(pieces[k][which, :, j * 128 : (j + 1) * 128])
        got = adam_update(master[...], total[...], first[...], second[...], 0.1, 0.1)
        first_out[...] = got[0]
        second_out[...] = got[1]
        master_out[...] = got[2]

    block = pl.BlockSpec((lines, 128), lambda i, *_: (i, 0))
    piece = pl.BlockSpec((2, step, chunk), lambda i, *_: (0, i, 0))
    shape = jax.ShapeDtypeStruct((rows * per_row, 128), jnp.float32)
    call = pl.pallas_call(
        kernel,
        grid_spec=pltpu.PrefetchScalarGridSpec(
            num_scalar_prefetch=1,
            grid=(rows // step,),
            in_specs=[piece] * parts + [block] * 3,
            out_specs=[block] * 3,
            scratch_shapes=[pltpu.VMEM((lines, 128), jnp.float32)],
        ),
        out_shape=[shape] * 3,
        compiler_params=pltpu.CompilerParams(vmem_limit_bytes=VMEM_LIMIT),
        cost_estimate=NO_COST,
        name="ffn_update",
    )

    def fold(array):
        return jnp.swapaxes(array.reshape(rows, 2, units // 128, 128), 1, 2).reshape(-1, 128)

    def unfold(array):
        return jnp.swapaxes(array.reshape(rows, units // 128, 2, 128), 1, 2).reshape(rows, 2, units)

    def run(place, pieces, master, first, second):
        got = call(place, *pieces, fold(master), fold(first), fold(second))
        return tuple(unfold(array) for array in got)

    return run


def shards(
    tokens,
    doc_starts,
    attn_master,
    attn_mom,
    attn_sq,
    ffn_master,
    ffn_mom,
    ffn_sq,
    small_master,
    small_mom,
    small_sq,
    cotangent,
):
    ctx_count, wt_count = lax.axis_size("ctx"), lax.axis_size("wt")
    ctx_place, wt_place = lax.axis_index("ctx"), lax.axis_index("wt")
    batches, rows_here, width = tokens.shape
    qkv_cols = width + 2 * HS
    attn_columns = attn_master.shape[1]
    all_rows = batches * rows_here
    shard_rows = attn_master.shape[0]
    piece_rows = shard_rows // ctx_count
    chunk = FF // ctx_count
    chips = ctx_count // 2
    order = ctx_place ^ jnp.arange(ctx_count, dtype=jnp.int32)
    (
        gain_one,
        shift_one,
        gain_two,
        shift_two,
        bias_query,
        bias_out,
        bias_proj,
        bias_value,
        bias_hidden,
    ) = split_small(small_master)
    runs = 2 if batches % 2 == 0 else 1
    places = [jnp.stack([ctx_place, jnp.int32(run * (batches // runs))]) for run in range(runs)]
    place = places[0]
    wt_half = wt_count // 2
    near_row = wt_place // wt_half * wt_half
    row_starts = jnp.stack([near_row, wt_half - near_row])
    out_rows = shard_rows // chips
    run_forward, run_backward = attention_kernels(batches, rows_here, width, ctx_count, runs)
    ffn_first, ffn_second, ffn_third, ffn_down = ffn_kernels(all_rows, width, chunk, wt_half)
    step = Steps()

    def in_order(even, odd):
        buffer = jnp.zeros((ctx_count,) + even.shape[1:], even.dtype)
        for m in range(chips):
            buffer = put(buffer, even[m][None], ctx_place ^ (2 * m), 0)
            buffer = put(buffer, odd[m][None], ctx_place ^ (2 * m + 1), 0)
        return buffer

    def send_chips(piece):
        return [xor_send(piece, mask) for mask in range(2, ctx_count, 2)]

    def send_wt(piece):
        return [xor_wt(piece, mask) for mask in range(1, wt_count)]

    def send_rows(array, axis):
        size = array.shape[axis] // wt_count
        return [xor_wt(take(array, wt_place ^ mask, axis, size), mask) for mask in range(1, wt_count)]

    def add_low(*arrays):
        return low(sum(wide(array) for array in arrays))

    qkv_piece = step(
        lambda master: low(lax.dynamic_slice(master, (ctx_place * piece_rows, 0), (piece_rows, qkv_cols))), attn_master
    )
    qkv_got = send_wt(qkv_piece)

    def cut_rest(ffn, attn):
        ffn = jnp.swapaxes(take(ffn, ctx_place, 2, chunk), 0, 1).reshape(2 * shard_rows, chunk)
        out = lax.dynamic_slice(
            attn, (ctx_place // 2 * out_rows, qkv_cols + ctx_place % 2 * chunk), (out_rows, chunk)
        )
        return low(jnp.concatenate([ffn, out]))

    rest_piece = step(cut_rest, ffn_master, attn_master)
    rest_got = send_wt(rest_piece)
    back_low = cotangent.reshape(all_rows, width)
    back_other = xor_send(back_low, 1)
    stream = wide(tokens.reshape(all_rows, width))
    normed_low = step(
        lambda tokens, gain, shift: low(layer_norm(wide(tokens), gain, shift)),
        tokens.reshape(all_rows, width), gain_one, shift_one,
    )

    def by_wt(piece, got):
        buffer = put(jnp.zeros((wt_count,) + piece.shape, piece.dtype), piece[None], wt_place, 0)
        for mask, array in enumerate(got, 1):
            buffer = put(buffer, array[None], wt_place ^ mask, 0)
        return buffer

    qkv_own = step(by_wt, qkv_piece, qkv_got)
    qkv_got = send_chips(qkv_own)

    def half_of(pieces, masks, rows):
        buffer = jnp.zeros((wt_half, rows.stop - rows.start, chunk), jnp.bfloat16)
        for mask, piece in zip(masks, pieces):
            buffer = put(buffer, piece[None, rows], (wt_place ^ mask) % wt_half, 0)
        return buffer

    ffn_rows, out_slice = slice(0, 2 * shard_rows), slice(2 * shard_rows, 2 * shard_rows + out_rows)
    near_masks, far_masks = list(range(wt_half)), list(range(wt_half, wt_count))
    near = step(lambda *pieces: half_of(pieces, near_masks, ffn_rows), rest_piece, *rest_got[: wt_half - 1])
    near_x, near_y = xor_send(near, 2), xor_send(near, 4)
    qkv_even = step(lambda *parts: jnp.stack(parts), qkv_own, *qkv_got)
    qkv_odd = xor_send(qkv_even, 1)
    back_turned = step(turn_both, back_low, back_other)

    def project(even, odd, normed):
        weight = jnp.swapaxes(in_order(even, odd), 0, 1).reshape(width, qkv_cols)
        mixed = dot(normed, weight)
        queries = low(mixed[:, :width] + bias_query).reshape(batches, rows_here, width)
        kv_bias = jnp.concatenate([jnp.zeros((HS,), jnp.float32), bias_value])
        kv_local = low(mixed[:, width:] + kv_bias).reshape(batches, rows_here, 2 * HS)
        return weight, queries, kv_local

    weight_qkv, queries, kv_local = step(project, qkv_even, qkv_odd, normed_low)
    kv_got = send_chips(kv_local)

    def rest_far(piece, *got):
        far = half_of(got[wt_half - 1 :], far_masks, ffn_rows)
        out = jnp.zeros((wt_count, out_rows, chunk), jnp.bfloat16)
        for mask, array in enumerate((piece,) + got):
            out = put(out, array[None, out_slice], wt_place ^ mask, 0)
        return far, out

    far, out_own = step(rest_far, rest_piece, *rest_got)
    kv_even = step(lambda *parts: jnp.stack(parts), kv_local, *kv_got)
    kv_odd = xor_send(kv_even, 1)
    out_own, far, near_x = step(lambda *arrays: arrays, out_own, far, near_x)
    out_got = send_chips(out_own)
    far_x, far_y = xor_send(far, 2), xor_send(far, 4)
    near_diagonal = xor_send(near_x, 4)
    out_even = step(lambda *parts: jnp.stack(parts), out_own, *out_got)
    out_odd = xor_send(out_even, 1)

    attended_low, attended, logs = step(run_forward, doc_starts, place, queries, kv_even, kv_odd)
    attended_low = attended_low.reshape(all_rows, width)
    far_y = step(lambda array: array, far_y)
    far_diagonal = xor_send(far_y, 2)
    hidden, normed_two, weight_out = step(
        lambda *args: out_projection(all_rows, width, wt_count, chips, out_rows)(*args[:6], *in_hbm(args[6:])),
        place, attended_low, tokens.reshape(all_rows, width), bias_out[None], gain_two[None], shift_two[None],
        out_even, out_odd,
    )
    normed_other = xor_send(normed_two, 1)

    bias_parts = bias_hidden.reshape(ctx_count, chunk)[order[::2]].reshape(1, chips * chunk)
    bias_near, bias_far = jnp.split(bias_parts, 2, axis=1)
    weights_first = in_hbm([near_y, far_y, near_diagonal, far_diagonal])
    weights_second = in_hbm([near, far, near_x, far_x])
    flows = (normed_two, normed_other, back_low, back_other, back_turned)
    act_first, units_first, down_y, down_top, down_bottom, sums_first = step(
        lambda *args: ffn_first(*args[:7], *in_hbm(args[7:])), row_starts, *flows, bias_far, *weights_first
    )
    top_got, bottom_got = xor_send(down_top, 4), xor_send(down_bottom, 2)
    act_second, units_second, down_own, down_x, sums_second, back_own, back_part = step(
        lambda *args: ffn_second(*args[:7], *in_hbm(args[7:])),
        row_starts, *flows, bias_near, units_first, *weights_second, *weights_first,
    )
    back_got = xor_send(back_part, 1)

    def meet(along_x, along_y, top, bottom):
        half = width // 2
        return (
            jnp.concatenate([add_low(along_x[:half], top), along_x[half:]]),
            jnp.concatenate([along_y[:half], add_low(along_y[half:], bottom)]),
        )

    down_x, down_y = step(meet, down_x, down_y, top_got, bottom_got)
    down_got = [xor_send(down_x, 2), xor_send(down_y, 4)]
    up_own, up_x, up_y, up_top, up_bottom = step(
        lambda *args: ffn_third(*args[:2], *in_hbm(args[2:])), normed_two, normed_other, units_second, units_first
    )
    top_got, bottom_got = xor_send(up_top, 4), xor_send(up_bottom, 2)

    def hidden_back(own, got, hidden, back, gain, shift, weight):
        pulled = jax.vjp(layer_norm, hidden, gain, shift)[1](own + wide(got))
        grad = wide(back) + pulled[0]
        grad_low = low(grad)
        return grad, grad_low, low(cols_dot(grad_low, weight)).reshape(batches, rows_here, width), pulled[1:]

    grad_hidden, grad_hidden_low, grad_attended, (grad_gain_two, grad_shift_two) = step(
        hidden_back, back_own, back_got, hidden, back_low, gain_two, shift_two, weight_out
    )
    up_x, up_y = step(meet, up_x, up_y, top_got, bottom_got)
    up_got = [xor_send(up_x, 2), xor_send(up_y, 4)]
    down_sum = step(add_low, down_own, *down_got)
    down_got = send_rows(down_sum, 0)

    backs = []
    for run in range(runs):
        grad_queries, dkv_even, dkv_odd = step(
            run_backward[run], doc_starts, places[run], queries, kv_even, kv_odd, attended, logs, grad_attended
        )
        backs.append((grad_queries, dkv_even, xor_send(dkv_odd, 1)))
        if run == 0:
            up_sum = step(add_low, up_own, *up_got)
            up_got = send_rows(up_sum, 0)

    kv_half = step(
        lambda pairs: jnp.concatenate([add_low(*pair) for pair in pairs], axis=1), [back[1:] for back in backs]
    )
    kv_got = [xor_send(kv_half[m], 2 * m) for m in range(1, chips)]
    grad_query = jnp.concatenate([back[0] for back in backs]).reshape(all_rows, width)

    def own_rows(up_sum, down_sum, up_got, down_got):
        return jnp.stack(
            [
                add_low(take(up_sum, wt_place, 0, shard_rows), *up_got),
                add_low(take(down_sum, wt_place, 0, shard_rows), *down_got),
            ]
        )

    wide_even, wide_odd = step(
        attn_grads(all_rows, width, wt_count, ctx_count, piece_rows),
        place, normed_low, grad_query, attended_low, grad_hidden_low,
    )
    wide_odd = xor_send(wide_odd, 1)
    ffn_part = step(own_rows, up_sum, down_sum, up_got, down_got)
    ffn_got = send_chips(ffn_part)
    wide_half = step(add_low, wide_even, wide_odd)
    wide_got = [xor_send(wide_half[m], 2 * m) for m in range(1, chips)]

    small_size = small_master.shape[0]
    small_columns = 128 * -(-small_size // (128 * piece_rows * ctx_count))

    def stream_back(kv_own, kv_got, grad_query, weight, tokens, gain, shift, grad_hidden, normed, back, sums_a, sums_b):
        grad_kv = add_low(kv_own, *kv_got).reshape(all_rows, 2 * HS)
        grad_normed = cols_dot(grad_query, weight[:, :width]) + cols_dot(grad_kv, weight[:, width:])
        pulled = jax.vjp(layer_norm, wide(tokens), gain, shift)[1](grad_normed)
        own_units = jnp.zeros((ctx_count, chunk), jnp.float32)
        hidden_sums = jnp.concatenate([sums_a.reshape(2, chunk), sums_b.reshape(2, chunk)])
        for m in range(chips):
            own_units = put(own_units, hidden_sums[m][None], ctx_place ^ (2 * m), 0)
        grad_small = jnp.concatenate(
            [
                pulled[1],
                pulled[2],
                grad_gain_two,
                grad_shift_two,
                jnp.sum(wide(grad_query), axis=0),
                jnp.sum(grad_hidden, axis=0),
                jnp.sum(wide(back), axis=0),
                jnp.sum(wide(grad_kv[:, HS:]), axis=0),
                own_units.reshape(FF),
            ]
        )
        small = jnp.pad(low(grad_small), (0, ctx_count * piece_rows * small_columns - small_size))
        small = small.reshape(ctx_count, 1, piece_rows, small_columns)
        blocks = low(rows_dot(normed, grad_kv)).reshape(wt_count, ctx_count, piece_rows, 2 * HS)
        blocks = jnp.swapaxes(blocks, 0, 1)
        tail = jnp.concatenate([blocks, jnp.broadcast_to(small, blocks.shape[:3] + (small_columns,))], axis=3)
        pieces = [take(tail, ctx_place ^ k, 0, 1)[0] for k in range(ctx_count)]
        return (grad_hidden + pulled[0]).reshape(tokens.shape), jnp.stack(pieces[::2]), jnp.stack(pieces[1::2])

    input_grad, tail_even, tail_odd = step(
        stream_back, kv_half[0], kv_got, grad_query, weight_qkv, tokens.reshape(all_rows, width), gain_one, shift_one,
        grad_hidden, normed_low, back_low, sums_second, sums_first,
    )
    input_grad = input_grad.reshape(batches, rows_here, width)
    tail_odd = xor_send(tail_odd, 1)
    ffn_even = step(lambda *parts: jnp.stack(parts), ffn_part, *ffn_got)
    ffn_odd = xor_send(ffn_even, 1)
    tail_half = step(add_low, tail_even, tail_odd)
    tail_got = [xor_send(tail_half[m], 2 * m) for m in range(1, chips)]
    down_out, down_part = step(
        lambda *args: ffn_down(*args[:3], *in_hbm(args[3:])),
        row_starts, act_second, act_first, *weights_second, *weights_first,
    )
    down_part = xor_send(down_part, 1)
    attn_sum = step(
        lambda *args: jnp.concatenate([add_low(*args[:chips]), add_low(*args[chips:])], axis=2),
        wide_half[0], *wide_got, tail_half[0], *tail_got,
    )
    attn_got = send_rows(attn_sum, 0)
    layer_out = step(
        lambda hidden, own, got: low(hidden + own + wide(got) + bias_proj).reshape(batches, rows_here, width),
        hidden, down_out, down_part,
    )
    attn_part = step(lambda total, *got: add_low(take(total, wt_place, 0, 1), *got)[0], attn_sum, *attn_got)
    attn_got = send_chips(attn_part)

    ffn_pieces = [(ffn_even, ffn_odd)[k % 2][k // 2] for k in range(ctx_count)]
    ffn_new = step(
        lambda place, pieces, *arrays: ffn_update(shard_rows, FF, ctx_count, chunk)(place, pieces, *arrays),
        place, ffn_pieces, ffn_master, ffn_mom, ffn_sq,
    )
    attn_even = step(lambda *parts: jnp.stack(parts), attn_part, *attn_got)
    attn_odd = xor_send(attn_even, 1)
    small_total = in_order(attn_even[..., attn_columns:], attn_odd[..., attn_columns:])
    small_total = wide(small_total.reshape(-1)[:small_size])
    small_new = adam_update(small_master, small_total, small_mom, small_sq, 1.0, 0.0)
    attn_new = attn_update(shard_rows, attn_columns, width, ctx_count, piece_rows)(
        place, attn_even, attn_odd, attn_master, attn_mom, attn_sq
    )
    return (layer_out, input_grad) + tuple(attn_new) + tuple(ffn_new) + tuple(small_new)


def shift_wt(array, shift):
    count = lax.axis_size("wt")
    return lax.ppermute(array, "wt", [(i, (i + shift) % count) for i in range(count)])


def whole_wt(piece, axis):
    count, place = lax.axis_size("wt"), lax.axis_index("wt")
    shape = list(piece.shape)
    shape[axis] *= count
    buffer = put(jnp.zeros(shape, piece.dtype), piece, place, axis)
    for shift in range(1, count):
        buffer = put(buffer, shift_wt(piece, shift), (place - shift) % count, axis)
    return buffer


def whole_ctx(piece):
    count = lax.axis_size("ctx")
    got = {0: piece}
    for mask in range(2, count, 2):
        got[mask] = xor_send(piece, mask)
    for mask in range(0, count, 2):
        got[mask + 1] = xor_send(got[mask], 1)
    return [got[mask] for mask in range(count)]


def sum_ctx(pieces):
    count = lax.axis_size("ctx")
    half = {}
    for mask in range(count - 2, -1, -2):
        other = xor_send(pieces[mask + 1], 1)
        half[mask] = low(wide(pieces[mask]) + wide(other))
    total = wide(half[0])
    for mask in range(2, count, 2):
        total = total + wide(xor_send(half[mask], mask))
    return total


def sum_wt(array, axis):
    count, place = lax.axis_size("wt"), lax.axis_index("wt")
    size = array.shape[axis] // count
    total = wide(take(array, place, axis, size))
    for shift in range(1, count):
        sent = take(array, (place + shift) % count, axis, size)
        total = total + wide(shift_wt(sent, shift))
    return total


def any_shards(
    tokens,
    doc_starts,
    attn_master,
    attn_mom,
    attn_sq,
    ffn_master,
    ffn_mom,
    ffn_sq,
    small_master,
    small_mom,
    small_sq,
    cotangent,
):
    ctx_count = lax.axis_size("ctx")
    ctx_place = lax.axis_index("ctx")
    wt_count = lax.axis_size("wt")
    batches, rows_here, width = tokens.shape
    heads = width // HS
    qkv_cols = width + 2 * HS
    all_rows = batches * rows_here
    shard_rows = attn_master.shape[0]
    piece_rows = shard_rows // ctx_count
    chunk = FF // ctx_count
    order = ctx_place ^ jnp.arange(ctx_count, dtype=jnp.int32)
    (
        gain_one,
        shift_one,
        gain_two,
        shift_two,
        bias_query,
        bias_out,
        bias_proj,
        bias_value,
        bias_hidden,
    ) = split_small(small_master)

    attn_piece = low(take(attn_master, ctx_place, 0, piece_rows))

    def whole_rows(piece):
        parts = whole_ctx(whole_wt(piece[None], 0))
        buffer = jnp.zeros((wt_count, ctx_count) + piece.shape, piece.dtype)
        for k, part in enumerate(parts):
            buffer = put(buffer, part[:, None], ctx_place ^ k, 1)
        return buffer.reshape((width,) + piece.shape[1:])

    weight_qkv = whole_rows(attn_piece[:, :qkv_cols])
    weight_out = whole_rows(attn_piece[:, qkv_cols:])
    ffn_piece = low(jnp.swapaxes(take(ffn_master, ctx_place, 2, chunk), 0, 1))
    ffn_parts = whole_ctx(whole_wt(ffn_piece, 1))
    bias_parts = bias_hidden.reshape(ctx_count, chunk)[order]

    stream = wide(tokens.reshape(all_rows, width))
    normed, norm_back_one = jax.vjp(layer_norm, stream, gain_one, shift_one)
    normed_low = low(normed)
    mixed = dot(normed_low, weight_qkv)
    queries = low(mixed[:, :width] + bias_query)
    kv_local = low(
        mixed[:, width:] + jnp.concatenate([jnp.zeros((HS,), jnp.float32), bias_value])
    ).reshape(batches, rows_here, 2 * HS)
    kv_parts = jnp.stack(whole_ctx(kv_local), axis=1).reshape(
        batches, ctx_count * rows_here, 2 * HS
    )
    keys_all, values_all = kv_parts[..., :HS], kv_parts[..., HS:]
    local_pos = jnp.arange(rows_here, dtype=jnp.int32)
    query_pos = ctx_place * rows_here + local_pos
    key_pos = (order[:, None] * rows_here + local_pos[None, :]).reshape(-1)
    queries = queries.reshape(batches, rows_here * heads, HS)
    scale = HS ** (-0.5)
    attended_list, log_list, allowed_list = [], [], []
    for b in range(batches):
        starts = doc_starts[b]
        query_doc = jnp.sum((starts[None, :] <= query_pos[:, None]).astype(jnp.int32), axis=1)
        key_doc = jnp.sum((starts[None, :] <= key_pos[:, None]).astype(jnp.int32), axis=1)
        allowed = (query_doc[:, None] == key_doc[None, :]) & (key_pos[None, :] <= query_pos[:, None])
        allowed = jnp.repeat(allowed, heads, axis=0)
        allowed_list.append(allowed)
        scores = jnp.where(allowed, cols_dot(queries[b], keys_all[b]) * scale, -1e30)
        peak = jnp.max(scores, axis=-1, keepdims=True)
        expo = jnp.exp(scores - peak)
        total = jnp.sum(expo, axis=-1, keepdims=True)
        attended_list.append(dot(low(expo / total), values_all[b]))
        log_list.append(peak + jnp.log(total))
    attended = jnp.stack(attended_list)
    attended_low = low(attended).reshape(all_rows, width)
    hidden = stream + dot(attended_low, weight_out) + bias_out
    normed_two, norm_back_two = jax.vjp(layer_norm, hidden, gain_two, shift_two)
    normed_two_low = low(normed_two)

    back_low = cotangent.reshape(all_rows, width)
    back_rows = wide(back_low)
    down_vals = jnp.zeros((all_rows, width), jnp.float32)
    grad_normed_two = jnp.zeros((all_rows, width), jnp.float32)
    ffn_grads, hidden_grads = [], []
    for k in range(ctx_count):
        weight_up, weight_down = ffn_parts[k][0], ffn_parts[k][1]
        value, slope = gelu_both(dot(normed_two_low, weight_up) + bias_parts[k])
        act = low(value)
        down_vals = down_vals + cols_dot(act, weight_down)
        grad_up = low(dot(back_low, weight_down) * slope)
        hidden_grads.append(jnp.sum(wide(grad_up), axis=0))
        grad_normed_two = grad_normed_two + cols_dot(grad_up, weight_up)
        ffn_grads.append(
            jnp.stack([low(rows_dot(normed_two_low, grad_up)), low(rows_dot(back_low, act))])
        )
    layer_out = low(hidden + down_vals + bias_proj).reshape(batches, rows_here, width)
    grad_bias_proj = jnp.sum(back_rows, axis=0)
    grad_bias_hidden = jnp.stack(hidden_grads)[order].reshape(FF)
    ffn_part = low(sum_wt(low(sum_ctx(ffn_grads)), 1))

    grad_hidden_part, grad_gain_two, grad_shift_two = norm_back_two(grad_normed_two)
    grad_hidden = back_rows + grad_hidden_part
    grad_bias_out = jnp.sum(grad_hidden, axis=0)
    grad_hidden_low = low(grad_hidden)
    grad_out = rows_dot(attended_low, grad_hidden_low)

    def summed_rows(grad):
        blocks = low(grad).reshape(wt_count, ctx_count, piece_rows, grad.shape[1])
        pieces = [take(blocks, ctx_place ^ k, 1, 1)[:, 0] for k in range(ctx_count)]
        part = low(sum_wt(low(sum_ctx(pieces)), 0)[0])
        buffer = jnp.zeros((ctx_count,) + part.shape, part.dtype)
        for k, got in enumerate(whole_ctx(part)):
            buffer = put(buffer, got[None], ctx_place ^ k, 0)
        return wide(buffer.reshape(shard_rows, grad.shape[1]))

    out_total = summed_rows(grad_out)

    grad_attended = low(cols_dot(grad_hidden_low, weight_out)).reshape(
        batches, rows_here * heads, HS
    )
    grad_query_list, grad_kv_list = [], []
    for b in range(batches):
        grads = grad_attended[b]
        delta = jnp.sum(wide(grads) * attended[b], axis=-1, keepdims=True)
        scores = jnp.where(allowed_list[b], cols_dot(queries[b], keys_all[b]) * scale, -1e30)
        weights = jnp.exp(scores - log_list[b])
        grad_scores = low(weights * (cols_dot(grads, values_all[b]) - delta))
        grad_query_list.append(low(dot(grad_scores, keys_all[b]) * scale))
        grad_kv_list.append(
            jnp.concatenate(
                [
                    low(rows_dot(grad_scores, queries[b]) * scale),
                    low(rows_dot(low(weights), grads)),
                ],
                axis=1,
            )
        )
    grad_query = jnp.stack(grad_query_list).reshape(all_rows, width)
    grad_kv = jnp.stack(grad_kv_list).reshape(batches, ctx_count, rows_here, 2 * HS)
    grad_kv_low = low(sum_ctx([grad_kv[:, k] for k in range(ctx_count)])).reshape(
        all_rows, 2 * HS
    )
    grad_bias_query = jnp.sum(wide(grad_query), axis=0)
    grad_bias_value = jnp.sum(wide(grad_kv_low[:, HS:]), axis=0)
    grad_mixed = jnp.concatenate([grad_query, grad_kv_low], axis=1)
    qkv_total = summed_rows(rows_dot(normed_low, grad_mixed))
    grad_normed = cols_dot(grad_mixed, weight_qkv)
    grad_stream_part, grad_gain_one, grad_shift_one = norm_back_one(grad_normed)
    input_grad = (grad_hidden + grad_stream_part).reshape(batches, rows_here, width)

    ffn_buffer = jnp.zeros((ctx_count,) + ffn_part.shape, ffn_part.dtype)
    for k, got in enumerate(whole_ctx(ffn_part)):
        ffn_buffer = put(ffn_buffer, got[None], ctx_place ^ k, 0)
    ffn_total = wide(jnp.transpose(ffn_buffer, (2, 1, 0, 3)).reshape(shard_rows, 2, FF))
    attn_total = jnp.concatenate([qkv_total, out_total], axis=1)
    grad_small = jnp.concatenate(
        [
            grad_gain_one,
            grad_shift_one,
            grad_gain_two,
            grad_shift_two,
            grad_bias_query,
            grad_bias_out,
            grad_bias_proj,
            grad_bias_value,
            grad_bias_hidden,
        ]
    )
    small_total = lax.psum(grad_small, ("ctx", "wt"))
    attn_new = adam_update(attn_master, attn_total, attn_mom, attn_sq, 0.1, 0.1)
    ffn_new = adam_update(ffn_master, ffn_total, ffn_mom, ffn_sq, 0.1, 0.1)
    small_new = adam_update(small_master, small_total, small_mom, small_sq, 1.0, 0.0)
    return (layer_out, input_grad) + attn_new + ffn_new + small_new


def solution(mesh):
    rows, cube = P("wt", None), P("wt", None, None)
    flow = P("wt", "ctx", None)
    in_specs = (flow, rows, rows, rows, rows, cube, cube, cube, P(), P(), P(), flow)
    out_specs = (flow, flow, rows, rows, rows, cube, cube, cube, P(), P(), P())
    ctx_count, wt_count = mesh.shape["ctx"], mesh.shape["wt"]
    fitted = ctx_count == 8 and wt_count % 2 == 0 and D // wt_count % (4 * ctx_count) == 0
    body = shards if fitted else any_shards
    return jax.shard_map(body, mesh=mesh, in_specs=in_specs, out_specs=out_specs, check_vma=False)
```

```python
import jax
import jax.numpy as jnp
from jax import lax
from jax.experimental import pallas as pl
from jax.experimental.pallas import tpu as pltpu
from jax.sharding import PartitionSpec as P

D = 768
HS = 64
FF = 3072
STEP = 10


NORM_EPS = 1e-05
GELU_COEF = 0.7978845608028654
GELU_CUBE = 0.044715
BETA_ONE = 0.9
BETA_TWO = 0.95
ADAM_EPS = 1e-08
VMEM_LIMIT = 56 << 20
NO_COST = pl.CostEstimate(flops=0, bytes_accessed=0, transcendentals=0)


def layer_norm(values, gain, shift):
    centre = values - jnp.mean(values, axis=-1, keepdims=True)
    spread = jnp.mean(centre * centre, axis=-1, keepdims=True)
    return centre * lax.rsqrt(spread + NORM_EPS) * gain + shift


def gelu_both(u):
    square = u * u
    share = 0.5 * jnp.tanh(u * (GELU_COEF * GELU_CUBE * square + GELU_COEF)) + 0.5
    bend = u * (6.0 * GELU_COEF * GELU_CUBE * square + 2.0 * GELU_COEF)
    return u * share, share * ((1.0 - share) * bend) + share


def split_small(small):
    return (
        small[0:D],
        small[D : 2 * D],
        small[2 * D : 3 * D],
        small[3 * D : 4 * D],
        small[4 * D : 5 * D],
        small[5 * D : 6 * D],
        small[6 * D : 7 * D],
        small[7 * D : 7 * D + HS],
        small[7 * D + HS :],
    )


def rows_dot(left, right):
    return lax.dot_general(
        left, right, (((0,), (0,)), ((), ())), preferred_element_type=jnp.float32
    )


def cols_dot(left, right):
    return lax.dot_general(
        left, right, (((1,), (1,)), ((), ())), preferred_element_type=jnp.float32
    )


def dot(left, right):
    return jnp.dot(left, right, preferred_element_type=jnp.float32)


def low(values):
    return values.astype(jnp.bfloat16)


def wide(values):
    return values.astype(jnp.float32)


def adam_update(master, gradient, first, second, step_rate, decay_rate):
    first_new = BETA_ONE * first + (1.0 - BETA_ONE) * gradient
    second_new = BETA_TWO * second + (1.0 - BETA_TWO) * gradient * gradient
    first_hat = first_new / (1.0 - BETA_ONE**STEP)
    second_hat = second_new / (1.0 - BETA_TWO**STEP)
    master_new = master - step_rate * (
        first_hat / (jnp.sqrt(second_hat) + ADAM_EPS) + decay_rate * master
    )
    return (first_new, second_new, master_new)


def xor_send(array, mask):
    count = lax.axis_size("ctx")
    return lax.ppermute(array, "ctx", [(i, i ^ mask) for i in range(count)])


def xor_wt(array, mask):
    count = lax.axis_size("wt")
    return lax.ppermute(array, "wt", [(i, i ^ mask) for i in range(count)])


class Steps:
    def __init__(self):
        self.last = ()

    def __call__(self, function, *args):
        flat, tree = jax.tree.flatten(args)
        held = lax.optimization_barrier(tuple(flat) + self.last)[: len(flat)]
        result = function(*jax.tree.unflatten(tree, held))
        self.last = tuple(jax.tree.leaves(result))
        return result


def put(buffer, piece, place, axis):
    starts = [0] * buffer.ndim
    starts[axis] = place * piece.shape[axis]
    return lax.dynamic_update_slice(buffer, piece, starts)


def take(buffer, place, axis, size):
    return lax.dynamic_slice_in_dim(buffer, place * size, size, axis)


def attention_kernels(batches, rows, width, parts, runs):
    half_parts = parts // 2
    keys = parts * rows
    pair = 2 * HS
    groups = width // (2 * pair)
    factor = HS ** (-0.5) * 1.4426950408889634
    masks = list(range(0, parts, 2)) + list(range(1, parts, 2))

    def lanes(shape):
        return lax.broadcasted_iota(jnp.int32, shape, 1)

    def spread(even_ref, odd_ref, key_ref, value_ref):
        for j in range(parts):
            ref = even_ref if j < half_parts else odd_ref
            block = wide(ref[j % half_parts, 0])
            turned = pltpu.roll(block, HS, 1)
            first = lanes(block.shape) < HS
            here = pl.ds(j * rows, rows)
            key_ref[0, here, :] = low(jnp.where(first, block, 0.0))
            key_ref[1, here, :] = low(jnp.where(first, 0.0, turned))
            value_ref[0, here, :] = low(jnp.where(first, turned, 0.0))
            value_ref[1, here, :] = low(jnp.where(first, 0.0, block))

    def doc_begin(starts_ref, stream, positions):
        begin = jnp.zeros_like(positions)
        for j in range(starts_ref.shape[1]):
            start = starts_ref[stream, j]
            begin = jnp.where(start <= positions, jnp.maximum(begin, start), begin)
        return begin

    def forward(starts_ref, place_ref, query_ref, even_ref, odd_ref, low_ref, full_ref, log_ref, cap, key, value):
        stream, place = pl.program_id(0), place_ref[0]
        spread(even_ref, odd_ref, key, value)
        query_pos = place * rows + lax.broadcasted_iota(jnp.int32, (rows, 1), 0)
        begin = doc_begin(starts_ref, stream, query_pos)
        for j, mask in enumerate(masks):
            key_pos = (place ^ mask) * rows + lax.broadcasted_iota(jnp.int32, (rows, rows), 1)
            allowed = (key_pos >= begin) & (key_pos <= query_pos)
            cap[:, j * rows : (j + 1) * rows] = jnp.where(allowed, 3.0e38, -1e30)
        log_ref[...] = jnp.zeros_like(log_ref)

        def group(g, carry):
            at = pl.multiple_of(g * 2 * pair, 2 * pair)
            both = query_ref[0, :, pl.ds(at, 2 * pair)]
            two = jnp.concatenate([both[:, :pair], both[:, pair:]], axis=0)
            limit = cap[...]
            limit = jnp.concatenate([limit, limit], axis=0)
            total = jnp.zeros((2 * rows, pair), jnp.float32)
            logs = log_ref[0]
            for half in range(2):
                scores = jnp.minimum(cols_dot(two, key[half]) * factor, limit)
                peak = jnp.max(scores, axis=1, keepdims=True)
                expo = jnp.exp2(scores - peak)
                norm = jnp.sum(expo, axis=1, keepdims=True)
                total = total + dot(low(expo), value[half]) / norm
                log = peak + jnp.log2(norm)
                column = lanes((rows, pair))
                logs = jnp.where(column == 4 * g + half, log[:rows], logs)
                logs = jnp.where(column == 4 * g + 2 + half, log[rows:], logs)
            log_ref[0] = logs
            total = jnp.concatenate([total[:rows], total[rows:]], axis=1)
            full_ref[0, :, pl.ds(at, 2 * pair)] = total
            low_ref[0, :, pl.ds(at, 2 * pair)] = low(total)
            return carry

        lax.fori_loop(0, groups, group, 0, unroll=True)

    def backward(
        starts_ref, place_ref, query_ref, even_ref, odd_ref, full_ref, log_ref, grad_ref,
        query_grad_ref, even_grad_ref, odd_grad_ref,
        cap, key, value, key_turned, log_rows, delta_rows, weight_buf, score_buf, query_buf, grad_buf,
    ):
        stream, place = pl.program_id(0) + place_ref[1], place_ref[0]
        spread(even_ref, odd_ref, key, value)
        query_pos = place * rows + lax.broadcasted_iota(jnp.int32, (1, rows), 1)
        begin = doc_begin(starts_ref, stream, query_pos)
        for j, mask in enumerate(masks):
            key_pos = (place ^ mask) * rows + lax.broadcasted_iota(jnp.int32, (rows, rows), 0)
            allowed = (key_pos >= begin) & (key_pos <= query_pos)
            cap[j * rows : (j + 1) * rows, :] = jnp.where(allowed, 3.0e38, -1e30)
            here = pl.ds(j * rows, rows)
            key_turned[:, j * rows : (j + 1) * rows] = low(wide(key[0, here, :]).T[:HS])
        log_rows[...] = log_ref[0].T[: log_rows.shape[0]]
        head_of = lax.broadcasted_iota(jnp.int32, (delta_rows.shape[0], width), 1) // HS
        chosen = (head_of == lax.broadcasted_iota(jnp.int32, (delta_rows.shape[0], width), 0)).astype(jnp.float32)
        delta_rows[...] = lax.dot_general(
            chosen, wide(grad_ref[0]) * full_ref[0], (((1,), (1,)), ((), ())),
            precision=lax.Precision.HIGHEST, preferred_element_type=jnp.float32,
        )
        first = lanes((2 * rows, pair)) < HS
        for g in range(groups):
            at = g * 2 * pair
            both, both_grad = query_ref[0, :, at : at + 2 * pair], grad_ref[0, :, at : at + 2 * pair]
            two = jnp.concatenate([both[:, :pair], both[:, pair:]], axis=0)
            two_grad = jnp.concatenate([both_grad[:, :pair], both_grad[:, pair:]], axis=0)
            limit = cap[...]
            limit = jnp.concatenate([limit, limit], axis=1)
            turned = []
            for half in range(2):
                h = 4 * g + half
                span = slice((2 * g + half) * 2 * rows, (2 * g + half + 1) * 2 * rows)
                keep = first if half == 0 else jnp.logical_not(first)
                query_buf[span, :] = low(jnp.where(keep, wide(two), 0.0))
                grad_buf[span, :] = low(jnp.where(keep, wide(two_grad), 0.0))
                log = jnp.concatenate([log_rows[h : h + 1, :], log_rows[h + 2 : h + 3, :]], axis=1)
                delta = jnp.concatenate([delta_rows[h : h + 1, :], delta_rows[h + 2 : h + 3, :]], axis=1)
                scores = jnp.minimum(cols_dot(key[half], two) * factor, limit)
                weights = jnp.exp2(scores - log)
                grad_scores = low(weights * (cols_dot(value[half], two_grad) - delta))
                weight_buf[:, span] = low(weights)
                score_buf[:, span] = grad_scores
                turned.append(dot(key_turned[...], grad_scores))
            turned = jnp.concatenate(turned, axis=0) * HS ** (-0.5)
            query_grad_ref[0, :, at : at + pair] = low(turned[:, :rows].T)
            query_grad_ref[0, :, at + pair : at + 2 * pair] = low(turned[:, rows:].T)
        for j in range(parts):
            here = pl.ds(j * rows, rows)
            value_sum = dot(weight_buf[here, :], grad_buf[...])
            key_sum = dot(score_buf[here, :], query_buf[...]) * HS ** (-0.5)
            value_sum = value_sum + pltpu.roll(value_sum, HS, 1)
            key_sum = key_sum + pltpu.roll(key_sum, HS, 1)
            ref = even_grad_ref if j < half_parts else odd_grad_ref
            ref[j % half_parts, 0] = low(jnp.where(lanes((rows, pair)) < HS, key_sum, value_sum))

    def specs(first):
        return (
            pl.BlockSpec((1, rows, width), lambda b, *_: (b + first, 0, 0)),
            pl.BlockSpec((1, rows, pair), lambda b, *_: (b + first, 0, 0)),
            pl.BlockSpec((half_parts, 1, rows, pair), lambda b, *_: (0, b + first, 0, 0)),
        )

    flow, logs, blocks = specs(0)

    shared = [
        pltpu.VMEM((2, keys, pair), jnp.bfloat16),
        pltpu.VMEM((2, keys, pair), jnp.bfloat16),
    ]
    run_forward = pl.pallas_call(
        forward,
        grid_spec=pltpu.PrefetchScalarGridSpec(
            num_scalar_prefetch=2,
            grid=(batches,),
            in_specs=[flow, blocks, blocks],
            out_specs=[flow, flow, logs],
            scratch_shapes=[pltpu.VMEM((rows, keys), jnp.float32)] + shared,
        ),
        out_shape=[
            jax.ShapeDtypeStruct((batches, rows, width), jnp.bfloat16),
            jax.ShapeDtypeStruct((batches, rows, width), jnp.float32),
            jax.ShapeDtypeStruct((batches, rows, pair), jnp.float32),
        ],
        compiler_params=pltpu.CompilerParams(vmem_limit_bytes=VMEM_LIMIT),
        cost_estimate=NO_COST,
        name="attention_forward",
    )
    head_rows = -(-(width // HS) // 8) * 8
    all_columns = rows * (width // HS)
    count = batches // runs

    def call_backward(run):
        here_flow, here_logs, here_blocks = specs(run * count)
        return pl.pallas_call(
        backward,
        grid_spec=pltpu.PrefetchScalarGridSpec(
            num_scalar_prefetch=2,
            grid=(count,),
            in_specs=[here_flow, here_blocks, here_blocks, here_flow, here_logs, here_flow],
            out_specs=[flow, blocks, blocks],
            scratch_shapes=[pltpu.VMEM((keys, rows), jnp.float32)]
            + shared
            + [
                pltpu.VMEM((HS, keys), jnp.bfloat16),
                pltpu.VMEM((head_rows, rows), jnp.float32),
                pltpu.VMEM((head_rows, rows), jnp.float32),
                pltpu.VMEM((keys, all_columns), jnp.bfloat16),
                pltpu.VMEM((keys, all_columns), jnp.bfloat16),
                pltpu.VMEM((all_columns, pair), jnp.bfloat16),
                pltpu.VMEM((all_columns, pair), jnp.bfloat16),
            ],
        ),
        out_shape=[
            jax.ShapeDtypeStruct((count, rows, width), jnp.bfloat16),
            jax.ShapeDtypeStruct((half_parts, count, rows, pair), jnp.bfloat16),
            jax.ShapeDtypeStruct((half_parts, count, rows, pair), jnp.bfloat16),
        ],
        compiler_params=pltpu.CompilerParams(vmem_limit_bytes=VMEM_LIMIT),
        cost_estimate=NO_COST,
        name="attention_backward",
    )

    return run_forward, [call_backward(run) for run in range(runs)]


def in_hbm(arrays):
    return [pltpu.with_memory_space_constraint(array, pltpu.HBM) for array in arrays]


def ffn_kernels(rows, width, chunk, wt_count):
    units = 2 * chunk
    all_rows = 2 * rows
    block_rows = width // wt_count
    hbm = pl.BlockSpec(memory_space=pltpu.HBM)
    vmem = pl.BlockSpec(memory_space=pltpu.VMEM)
    params = pltpu.CompilerParams(vmem_limit_bytes=VMEM_LIMIT)

    def fetch(weights, which, held, sem):
        copies = []
        for n, arrays in enumerate(weights):
            blocks = [array.at[block] for array in arrays for block in range(array.shape[0])]
            for row, block in enumerate(blocks):
                copies.append(
                    pltpu.make_async_copy(
                        block.at[pl.ds(which * block_rows, block_rows), :],
                        held.at[pl.ds(row * block_rows, block_rows), pl.ds(n * chunk, chunk)],
                        sem.at[len(copies)],
                    )
                )
        for copy in copies:
            copy.start()
        return copies

    def send(pairs, sems):
        copies = [pltpu.make_async_copy(source, out, sems.at[n]) for n, (source, out) in enumerate(pairs)]
        for copy in copies:
            copy.start()
        return copies

    def units_of(inputs, grads, bias, held_up, held_down, act, grad_units):
        sums = jnp.zeros((1, units), jnp.float32)
        for s in range(2):
            here = slice(s * rows, (s + 1) * rows)
            up = dot(inputs[s][...], held_up[...]) + bias
            value, slope = gelu_both(up)
            grad = dot(grads[s][...], held_down[...]) * slope
            act[here, :] = low(value)
            grad_units[here, :] = low(grad)
            sums = sums + jnp.sum(grad, axis=0, keepdims=True)
        return sums

    def halves(product, m):
        cols = pl.ds(m * chunk, chunk)
        return [product.at[pl.ds(h * width // 2, width // 2), cols] for h in range(2)]

    def first(
        own, other, grad_own, grad_other, turned, bias, w0, w1,
        act_out, units_out, out_a, out_b, sums_out,
        held_up, held_down, act, grad_units, product, sems, out_sems,
    ):
        weights = ((w0,), (w1,))
        copies = fetch(weights, 0, held_up, sems.at[0]) + fetch(weights, 1, held_down, sems.at[1])
        for copy in copies:
            copy.wait()
        sums_out[...] = units_of((own, other), (grad_own, grad_other), bias[...], held_up, held_down, act, grad_units)
        sent = send(((act, act_out), (grad_units, units_out)), out_sems.at[0])
        product[...] = low(dot(turned[...], act[...]))
        sent += send(
            ((product.at[:, pl.ds(0, chunk)], out_a), (product.at[:, pl.ds(chunk, chunk)], out_b)), out_sems.at[1]
        )
        for copy in sent:
            copy.wait()

    def second(
        own, other, grad_own, grad_other, turned, bias, units_first, w0, w1, w2, w3, w4,
        act_out, units_out, out_a, out_b, out_c, sums_out, back_own, back_other,
        held_up, held_more, held_down, act, grad_units, more_units, product, sems, out_sems, more_sem,
    ):
        weights, before = ((w2,), (w3, w4)), ((w0,), (w1,))
        copies = fetch(weights, 0, held_up, sems.at[0]) + fetch(weights, 1, held_down, sems.at[1])
        more = fetch(before, 0, held_more, sems.at[2])
        more.append(pltpu.make_async_copy(units_first, more_units, more_sem))
        more[-1].start()
        for copy in copies:
            copy.wait()
        sums_out[...] = units_of((own, other), (grad_own, grad_other), bias[...], held_up, held_down, act, grad_units)
        sent = send(((act, act_out), (grad_units, units_out)), out_sems.at[0])
        product[...] = low(dot(turned[...], act[...]))
        top, bottom = halves(product, 1)
        sent += send(((product.at[:, pl.ds(0, chunk)], out_a), (top, out_b), (bottom, out_c)), out_sems.at[1])
        for copy in more:
            copy.wait()
        for s, ref in enumerate((back_own, back_other)):
            here = slice(s * rows, (s + 1) * rows)
            total = cols_dot(grad_units[here, :], held_up[...]) + cols_dot(more_units[here, :], held_more[...])
            ref[...] = total.astype(ref.dtype)
        for copy in sent:
            copy.wait()

    def third(own, other, units_a, units_b, out_0, out_1, out_2, out_3, out_4, turned, held, products, sems, out_sems):
        copies = send(((units_a, held.at[0]), (units_b, held.at[1])), sems)
        turn((own, other), turned)
        for copy in copies:
            copy.wait()
        products[1] = low(dot(turned[...], held[1]))
        top, bottom = halves(products.at[1], 1)
        sent = send(((products.at[1, :, pl.ds(0, chunk)], out_2), (top, out_3), (bottom, out_4)), out_sems.at[0])
        products[0] = low(dot(turned[...], held[0]))
        sent += send(
            ((products.at[0, :, pl.ds(0, chunk)], out_0), (products.at[0, :, pl.ds(chunk, chunk)], out_1)),
            out_sems.at[1],
        )
        for copy in sent:
            copy.wait()

    def down(act_a, act_b, w0, w1, w2, w3, w4, own_ref, other_ref, held_a, held_b, sems):
        copies = fetch(((w0,), (w1,)), 1, held_a, sems.at[0]) + fetch(((w2,), (w3, w4)), 1, held_b, sems.at[1])
        for copy in copies:
            copy.wait()
        for s, ref in enumerate((own_ref, other_ref)):
            here = slice(s * rows, (s + 1) * rows)
            total = cols_dot(act_a[here, :], held_a[...]) + cols_dot(act_b[here, :], held_b[...])
            ref[...] = total.astype(ref.dtype)

    dma = pltpu.SemaphoreType.DMA
    held = pltpu.VMEM((width, units), jnp.bfloat16)
    flow = pltpu.VMEM((all_rows, units), jnp.bfloat16)
    flow_out = pltpu.HBM((all_rows, units), jnp.bfloat16)
    whole = pltpu.HBM((width, chunk), jnp.bfloat16)
    part = pltpu.HBM((width // 2, chunk), jnp.bfloat16)
    sums = jax.ShapeDtypeStruct((1, units), jnp.float32)
    own = jax.ShapeDtypeStruct((rows, width), jnp.float32)
    other = jax.ShapeDtypeStruct((rows, width), jnp.bfloat16)
    run_first = pl.pallas_call(
        first,
        in_specs=[vmem] * 6 + [hbm] * 2,
        out_specs=[hbm] * 4 + [vmem],
        out_shape=[flow_out, flow_out, whole, whole, sums],
        scratch_shapes=[held, held, flow, flow, held, dma((2, 2 * wt_count)), dma((2, 2))],
        compiler_params=params,
        cost_estimate=NO_COST,
        name="ffn_first",
    )
    run_second = pl.pallas_call(
        second,
        in_specs=[vmem] * 6 + [hbm] * 6,
        out_specs=[hbm] * 5 + [vmem] * 3,
        out_shape=[flow_out, flow_out, whole, part, part, sums, own, other],
        scratch_shapes=[held, held, held, flow, flow, flow, held, dma((3, 2 * wt_count)), dma((2, 3)), dma(())],
        compiler_params=params,
        cost_estimate=NO_COST,
        name="ffn_second",
    )
    run_third = pl.pallas_call(
        third,
        in_specs=[vmem] * 2 + [hbm] * 2,
        out_specs=[hbm] * 5,
        out_shape=[whole, whole, whole, part, part],
        scratch_shapes=[
            pltpu.VMEM((width, all_rows), jnp.bfloat16),
            pltpu.VMEM((2, all_rows, units), jnp.bfloat16),
            pltpu.VMEM((2, width, units), jnp.bfloat16),
            dma((2,)),
            dma((2, 3)),
        ],
        compiler_params=params,
        cost_estimate=NO_COST,
        name="ffn_grads",
    )
    run_down = pl.pallas_call(
        down,
        in_specs=[vmem] * 2 + [hbm] * 5,
        out_specs=[vmem] * 2,
        out_shape=[own, other],
        scratch_shapes=[held, held, dma((2, 2 * wt_count))],
        compiler_params=params,
        cost_estimate=NO_COST,
        name="ffn_down",
    )
    return run_first, run_second, run_third, run_down


def turn(refs, turned):
    rows = refs[0].shape[0]
    for s, ref in enumerate(refs):
        for i in range(rows // 128):
            block = wide(ref[i * 128 : (i + 1) * 128, :])
            turned[:, s * rows + i * 128 : s * rows + (i + 1) * 128] = low(block.T)


def turn_both(own, other):
    vmem = pl.BlockSpec(memory_space=pltpu.VMEM)
    rows, width = own.shape
    return pl.pallas_call(
        lambda a, b, out: turn((a, b), out),
        in_specs=[vmem] * 2,
        out_specs=vmem,
        out_shape=jax.ShapeDtypeStruct((width, 2 * rows), own.dtype),
        compiler_params=pltpu.CompilerParams(vmem_limit_bytes=VMEM_LIMIT),
        cost_estimate=NO_COST,
        name="turn",
    )(own, other)


def out_projection(rows, width, wt_count, chips, piece):
    def kernel(place_ref, attended, stream, bias, gain, shift, even_ref, odd_ref, hidden_ref, normed_ref, weight_ref, held, sems):
        chip, core = place_ref[0] // 2, place_ref[0] % 2
        copies = []
        for p, ref in enumerate((even_ref, odd_ref)):
            for m in range(chips):
                for z in range(wt_count):
                    row = pl.multiple_of((z * chips + (chip ^ m)) * piece, 16)
                    column = pl.multiple_of((core ^ p) * (width // 2), 128)
                    copies.append(
                        pltpu.make_async_copy(
                            ref.at[m, z],
                            held.at[pl.ds(row, piece), pl.ds(column, width // 2)],
                            sems.at[len(copies)],
                        )
                    )
                    copies[-1].start()
        for copy in copies:
            copy.wait()
        hidden = wide(stream[...]) + dot(attended[...], held[...]) + bias[...]
        hidden_ref[...] = hidden
        normed_ref[...] = low(layer_norm(hidden, gain[...], shift[...]))
        weight_ref[...] = held[...]

    vmem = pl.BlockSpec(memory_space=pltpu.VMEM)
    hbm = pl.BlockSpec(memory_space=pltpu.HBM)
    return pl.pallas_call(
        kernel,
        in_specs=[pl.BlockSpec(memory_space=pltpu.SMEM)] + [vmem] * 5 + [hbm] * 2,
        out_specs=[vmem] * 3,
        out_shape=[
            jax.ShapeDtypeStruct((rows, width), jnp.float32),
            jax.ShapeDtypeStruct((rows, width), jnp.bfloat16),
            jax.ShapeDtypeStruct((width, width), jnp.bfloat16),
        ],
        scratch_shapes=[pltpu.VMEM((width, width), jnp.bfloat16), pltpu.SemaphoreType.DMA((2 * chips * wt_count,))],
        compiler_params=pltpu.CompilerParams(vmem_limit_bytes=VMEM_LIMIT),
        cost_estimate=NO_COST,
        name="out_projection",
    )


def attn_grads(rows, width, row_groups, parts, piece):
    def kernel(place_ref, left_a, right_a, left_b, right_b, even_ref, odd_ref, turned, total):
        place = place_ref[0]
        for n, (left, right) in enumerate(((left_a, right_a), (left_b, right_b))):
            for i in range(rows // 128):
                turned[:, i * 128 : (i + 1) * 128] = low(wide(left[i * 128 : (i + 1) * 128, :]).T)
            total[:, n * width : (n + 1) * width] = dot(turned[...], right[...])
        for k in range(parts):
            ref = odd_ref if k % 2 else even_ref
            for w in range(row_groups):
                at = pl.multiple_of(w * piece * parts + (place ^ k) * piece, 8)
                ref[k // 2, w] = low(total[pl.ds(at, piece), :])

    vmem = pl.BlockSpec(memory_space=pltpu.VMEM)
    shape = jax.ShapeDtypeStruct((parts // 2, row_groups, piece, 2 * width), jnp.bfloat16)
    return pl.pallas_call(
        kernel,
        grid_spec=pltpu.PrefetchScalarGridSpec(
            num_scalar_prefetch=1,
            grid=(),
            in_specs=[vmem] * 4,
            out_specs=[vmem] * 2,
            scratch_shapes=[pltpu.VMEM((width, rows), jnp.bfloat16), pltpu.VMEM((width, 2 * width), jnp.float32)],
        ),
        out_shape=[shape] * 2,
        compiler_params=pltpu.CompilerParams(vmem_limit_bytes=VMEM_LIMIT),
        cost_estimate=NO_COST,
        name="attn_grads",
    )


def attn_update(rows, columns, width, parts, piece):
    qkv = columns - width

    def kernel(place_ref, even_ref, odd_ref, master, first, second, *outs):
        place = place_ref[0]
        for k in range(parts):
            ref = odd_ref if k % 2 else even_ref
            here = pl.ds(pl.multiple_of((place ^ k) * piece, 8), piece)
            for cols, source in (
                (slice(0, width), slice(0, width)),
                (slice(width, qkv), slice(2 * width, columns)),
                (slice(qkv, columns), slice(width, 2 * width)),
            ):
                grad = wide(ref[k // 2, :, source])
                got = adam_update(master[here, cols], grad, first[here, cols], second[here, cols], 0.1, 0.1)
                outs[0][here, cols] = got[0]
                outs[1][here, cols] = got[1]
                outs[2][here, cols] = got[2]

    vmem = pl.BlockSpec(memory_space=pltpu.VMEM)
    return pl.pallas_call(
        kernel,
        grid_spec=pltpu.PrefetchScalarGridSpec(
            num_scalar_prefetch=1, grid=(), in_specs=[vmem] * 5, out_specs=[vmem] * 3, scratch_shapes=[]
        ),
        out_shape=[jax.ShapeDtypeStruct((rows, columns), jnp.float32)] * 3,
        compiler_params=pltpu.CompilerParams(vmem_limit_bytes=VMEM_LIMIT),
        cost_estimate=NO_COST,
        name="attn_update",
    )


def ffn_update(rows, units, parts, chunk):
    per_row = 2 * units // 128
    rows_once = 32
    lines = rows_once * per_row

    def kernel(grad, master, first, second, first_out, second_out, master_out, total):
        for k in range(parts):
            for j in range(chunk // 128):
                for which in range(2):
                    line = k * (2 * chunk // 128) + 2 * j + which
                    total[pl.ds(line, rows_once, per_row), :] = wide(grad[k, which, :, j * 128 : (j + 1) * 128])
        got = adam_update(master[...], total[...], first[...], second[...], 0.1, 0.1)
        first_out[...] = got[0]
        second_out[...] = got[1]
        master_out[...] = got[2]

    block = pl.BlockSpec((lines, 128), lambda i: (i, 0))
    call = pl.pallas_call(
        kernel,
        grid=(rows // rows_once,),
        in_specs=[pl.BlockSpec((parts, 2, rows_once, chunk), lambda i: (0, 0, i, 0))] + [block] * 3,
        out_specs=[block] * 3,
        out_shape=[jax.ShapeDtypeStruct((rows * per_row, 128), jnp.float32)] * 3,
        scratch_shapes=[pltpu.VMEM((lines, 128), jnp.float32)],
        compiler_params=pltpu.CompilerParams(vmem_limit_bytes=VMEM_LIMIT),
        cost_estimate=NO_COST,
        name="ffn_update",
    )

    def fold(array):
        return jnp.swapaxes(array.reshape(rows, 2, units // 128, 128), 1, 2).reshape(-1, 128)

    def unfold(array):
        return jnp.swapaxes(array.reshape(rows, units // 128, 2, 128), 1, 2).reshape(rows, 2, units)

    def run(grad, master, first, second):
        return tuple(unfold(array) for array in call(grad, fold(master), fold(first), fold(second)))

    return run


def shards(
    tokens,
    doc_starts,
    attn_master,
    attn_mom,
    attn_sq,
    ffn_master,
    ffn_mom,
    ffn_sq,
    small_master,
    small_mom,
    small_sq,
    cotangent,
):
    ctx_count, wt_count = lax.axis_size("ctx"), lax.axis_size("wt")
    ctx_place, wt_place = lax.axis_index("ctx"), lax.axis_index("wt")
    batches, rows_here, width = tokens.shape
    qkv_cols = width + 2 * HS
    attn_columns = attn_master.shape[1]
    all_rows = batches * rows_here
    shard_rows = attn_master.shape[0]
    piece_rows = shard_rows // ctx_count
    chunk = FF // ctx_count
    chips = ctx_count // 2
    order = ctx_place ^ jnp.arange(ctx_count, dtype=jnp.int32)
    (
        gain_one,
        shift_one,
        gain_two,
        shift_two,
        bias_query,
        bias_out,
        bias_proj,
        bias_value,
        bias_hidden,
    ) = split_small(small_master)
    runs = 2 if batches % 2 == 0 else 1
    places = [jnp.stack([ctx_place, jnp.int32(run * (batches // runs))]) for run in range(runs)]
    place = places[0]
    wt_half = wt_count // 2
    out_rows = shard_rows // chips
    run_forward, run_backward = attention_kernels(batches, rows_here, width, ctx_count, runs)
    ffn_first, ffn_second, ffn_third, ffn_down = ffn_kernels(all_rows, width, chunk, wt_count)
    step = Steps()

    def both(own, got, place, bit, axis=0):
        ahead, behind = jnp.stack([own, got], axis), jnp.stack([got, own], axis)
        return jnp.where((place & bit) == 0, ahead, behind)

    def in_order(even, odd):
        buffer = jnp.zeros((ctx_count,) + even.shape[1:], even.dtype)
        for m in range(chips):
            buffer = put(buffer, even[m][None], ctx_place ^ (2 * m), 0)
            buffer = put(buffer, odd[m][None], ctx_place ^ (2 * m + 1), 0)
        return buffer

    def send_chips(piece):
        return [xor_send(piece, mask) for mask in range(2, ctx_count, 2)]

    def send_wt(pieces):
        return [xor_wt(piece, mask) for mask, piece in enumerate(pieces, 1)]

    def rows_out(array, axis):
        size = array.shape[axis] // wt_count
        return [take(array, wt_place ^ mask, axis, size) for mask in range(1, wt_count)]

    def add_low(*arrays):
        return low(sum(wide(array) for array in arrays))

    qkv = step(
        lambda master: low(lax.dynamic_slice(master, (ctx_place * piece_rows, 0), (piece_rows, qkv_cols))), attn_master
    )
    qkv_got = xor_wt(qkv, 1)

    def cut_rest(ffn, attn):
        ffn = jnp.swapaxes(take(ffn, ctx_place, 2, chunk), 0, 1).reshape(2 * shard_rows, chunk)
        out = lax.dynamic_slice(
            attn, (ctx_place // 2 * out_rows, qkv_cols + ctx_place % 2 * chunk), (out_rows, chunk)
        )
        return low(jnp.concatenate([ffn, out]))

    rest = step(cut_rest, ffn_master, attn_master)
    rest = lax.all_gather(rest, "wt", axis=0)
    back_low = cotangent.reshape(all_rows, width)
    back_other = xor_send(back_low, 1)
    flat_tokens = tokens.reshape(all_rows, width)
    qkv = step(lambda own, got: both(own, got, wt_place, 1), qkv, qkv_got)
    for bit in [1 << n for n in range(1, wt_count.bit_length() - 1)]:
        qkv_got = xor_wt(qkv, bit)
        qkv = step(
            lambda own, got: both(own, got, wt_place, bit).reshape((-1,) + own.shape[1:]), qkv, qkv_got
        )
    qkv_got = xor_send(qkv, 2)
    normed_low = step(
        lambda tokens, gain, shift: low(layer_norm(wide(tokens), gain, shift)), flat_tokens, gain_one, shift_one
    )
    qkv = step(lambda own, got: both(own, got, ctx_place, 2), qkv, qkv_got)
    qkv_got = xor_send(qkv, 4)
    back_turned = step(turn_both, back_low, back_other)
    qkv = step(lambda own, got: both(own, got, ctx_place, 4), qkv, qkv_got)
    qkv_got = xor_send(qkv, 1)

    def project(own, got, normed):
        blocks = both(own, got, ctx_place, 1, 2)
        weight = jnp.transpose(blocks, (3, 0, 1, 2, 4, 5)).reshape(width, qkv_cols)
        mixed = dot(normed, weight)
        queries = low(mixed[:, :width] + bias_query).reshape(batches, rows_here, width)
        kv_bias = jnp.concatenate([jnp.zeros((HS,), jnp.float32), bias_value])
        kv_local = low(mixed[:, width:] + kv_bias).reshape(batches, rows_here, 2 * HS)
        return weight, queries, kv_local

    weight_qkv, queries, kv_local = step(project, qkv, qkv_got, normed_low)
    kv_got = send_chips(kv_local)
    rest_low, rest_high, out_own = step(
        lambda rest: (
            rest[:wt_half, : 2 * shard_rows], rest[wt_half:, : 2 * shard_rows], rest[:, 2 * shard_rows :]
        ),
        rest,
    )
    kv_even = step(lambda *parts: jnp.stack(parts), kv_local, *kv_got)
    kv_odd = xor_send(kv_even, 1)
    rest = step(lambda low_half, high: jnp.concatenate([low_half, high]), rest_low, rest_high)
    rest_x, rest_y = xor_send(rest, 2), xor_send(rest, 4)
    out_got = send_chips(out_own)

    attended_low, attended, logs = step(run_forward, doc_starts, place, queries, kv_even, kv_odd)
    attended_low = attended_low.reshape(all_rows, width)
    out_even = step(lambda *parts: jnp.stack(parts), out_own, *out_got)
    out_odd = xor_send(out_even, 1)
    low_half, high_half = step(lambda x, y: (x[:wt_half], y[wt_half:]), rest_x, rest_y)
    diagonal_low, diagonal_high = xor_send(low_half, 4), xor_send(high_half, 2)
    hidden, normed_two, weight_out = step(
        lambda *args: out_projection(all_rows, width, wt_count, chips, out_rows)(*args[:6], *in_hbm(args[6:])),
        place, attended_low, flat_tokens, bias_out[None], gain_two[None], shift_two[None],
        out_even, out_odd,
    )
    normed_other = xor_send(normed_two, 1)

    bias_parts = bias_hidden.reshape(ctx_count, chunk)[order[::2]].reshape(1, chips * chunk)
    bias_near, bias_far = jnp.split(bias_parts, 2, axis=1)
    weights = [rest, rest_x, rest_y, diagonal_low, diagonal_high]
    flows = (normed_two, normed_other, back_low, back_other, back_turned)
    act_first, units_first, down_own, down_x, sums_first = step(
        lambda *args: ffn_first(*args[:6], *in_hbm(args[6:])), *flows, bias_near, *weights[:2]
    )
    act_second, units_second, down_y, down_top, down_bottom, sums_second, back_own, back_part = step(
        lambda *args: ffn_second(*args[:6], *in_hbm(args[6:])), *flows, bias_far, units_first, *weights
    )
    back_got = xor_send(back_part, 1)
    top_got, bottom_got = xor_send(down_top, 4), xor_send(down_bottom, 2)

    def meet(along_x, along_y, top, bottom):
        half = width // 2
        return (
            jnp.concatenate([add_low(along_x[:half], top), along_x[half:]]),
            jnp.concatenate([along_y[:half], add_low(along_y[half:], bottom)]),
        )

    up_own, up_x, up_y, up_top, up_bottom = step(
        lambda *args: ffn_third(*args[:2], *in_hbm(args[2:])), normed_two, normed_other, units_first, units_second
    )
    down_x, down_y = step(meet, down_x, down_y, top_got, bottom_got)
    down_got = [xor_send(down_x, 2), xor_send(down_y, 4)]
    top_got, bottom_got = xor_send(up_top, 4), xor_send(up_bottom, 2)

    def hidden_back(own, got, hidden, back, gain, shift, weight):
        pulled = jax.vjp(layer_norm, hidden, gain, shift)[1](own + wide(got))
        grad = wide(back) + pulled[0]
        grad_low = low(grad)
        return grad, grad_low, low(cols_dot(grad_low, weight)).reshape(batches, rows_here, width), pulled[1:]

    grad_hidden, grad_hidden_low, grad_attended, (grad_gain_two, grad_shift_two) = step(
        hidden_back, back_own, back_got, hidden, back_low, gain_two, shift_two, weight_out
    )
    up_x, up_y = step(meet, up_x, up_y, top_got, bottom_got)
    up_got = [xor_send(up_x, 2), xor_send(up_y, 4)]

    def rows_by_wt(own, *got):
        total = add_low(own, *got)
        return [take(total, wt_place, 0, shard_rows)] + rows_out(total, 0)

    backs = []
    for run in range(runs):
        backs.append(
            step(run_backward[run], doc_starts, places[run], queries, kv_even, kv_odd, attended, logs, grad_attended)
        )
        if run == 0:
            down_rows = step(rows_by_wt, down_own, *down_got)
            down_got = send_wt(down_rows[1:])
    kv_got = [xor_send(back[2], 1) for back in backs]
    up_rows = step(rows_by_wt, up_own, *up_got)
    up_got = send_wt(up_rows[1:])
    kv_half = step(
        lambda evens, odds: [
            jnp.concatenate([add_low(a[m], b[m]) for a, b in zip(evens, odds)]) for m in range(chips)
        ],
        [back[1] for back in backs], kv_got,
    )
    kv_got = [xor_send(kv_half[m], 2 * m) for m in range(1, chips)]
    grad_query = jnp.concatenate([back[0] for back in backs]).reshape(all_rows, width)
    wide_even, wide_odd = step(
        attn_grads(all_rows, width, wt_count, ctx_count, piece_rows),
        place, normed_low, grad_query, attended_low, grad_hidden_low,
    )
    wide_odd = xor_send(wide_odd, 1)
    ffn_part = step(
        lambda up_own, down_own, up_got, down_got: jnp.stack([add_low(up_own, *up_got), add_low(down_own, *down_got)]),
        up_rows[0], down_rows[0], up_got, down_got,
    )
    ffn_whole = lax.all_gather(ffn_part, "ctx", axis=0)
    wide_half = step(lambda a, b: [add_low(a[m], b[m]) for m in range(chips)], wide_even, wide_odd)
    wide_got = [xor_send(wide_half[m], 2 * m) for m in range(1, chips)]

    small_size = small_master.shape[0]
    small_columns = 128 * -(-small_size // (128 * piece_rows * ctx_count))

    def stream_back(kv_own, kv_got, grad_query, weight, tokens, gain, shift, grad_hidden, normed, back, sums_a, sums_b):
        grad_kv = add_low(kv_own, *kv_got).reshape(all_rows, 2 * HS)
        grad_normed = cols_dot(grad_query, weight[:, :width]) + cols_dot(grad_kv, weight[:, width:])
        pulled = jax.vjp(layer_norm, wide(tokens), gain, shift)[1](grad_normed)
        own_units = jnp.zeros((ctx_count, chunk), jnp.float32)
        hidden_sums = jnp.concatenate([sums_a.reshape(2, chunk), sums_b.reshape(2, chunk)])
        for m in range(chips):
            own_units = put(own_units, hidden_sums[m][None], ctx_place ^ (2 * m), 0)
        grad_small = jnp.concatenate(
            [
                pulled[1],
                pulled[2],
                grad_gain_two,
                grad_shift_two,
                jnp.sum(wide(grad_query), axis=0),
                jnp.sum(grad_hidden, axis=0),
                jnp.sum(wide(back), axis=0),
                jnp.sum(wide(grad_kv[:, HS:]), axis=0),
                own_units.reshape(FF),
            ]
        )
        small = jnp.pad(low(grad_small), (0, ctx_count * piece_rows * small_columns - small_size))
        small = small.reshape(ctx_count, 1, piece_rows, small_columns)
        blocks = low(rows_dot(normed, grad_kv)).reshape(wt_count, ctx_count, piece_rows, 2 * HS)
        blocks = jnp.swapaxes(blocks, 0, 1)
        tail = jnp.concatenate([blocks, jnp.broadcast_to(small, blocks.shape[:3] + (small_columns,))], axis=3)
        pieces = [take(tail, ctx_place ^ k, 0, 1)[0] for k in range(ctx_count)]
        return (grad_hidden + pulled[0]).reshape(tokens.shape), jnp.stack(pieces[::2]), jnp.stack(pieces[1::2])

    input_grad, tail_even, tail_odd = step(
        stream_back, kv_half[0], kv_got, grad_query, weight_qkv, flat_tokens, gain_one, shift_one,
        grad_hidden, normed_low, back_low, sums_first, sums_second,
    )
    input_grad = input_grad.reshape(batches, rows_here, width)
    tail_odd = xor_send(tail_odd, 1)
    tail_half = step(lambda a, b: [add_low(a[m], b[m]) for m in range(chips)], tail_even, tail_odd)
    tail_got = [xor_send(tail_half[m], 2 * m) for m in range(1, chips)]
    down_out, down_part = step(
        lambda *args: ffn_down(*args[:2], *in_hbm(args[2:])), act_first, act_second, *weights
    )
    down_part = xor_send(down_part, 1)

    def attn_by_wt(*args):
        total = jnp.concatenate([add_low(*args[:chips]), add_low(*args[chips:])], axis=2)
        return [take(total, wt_place, 0, 1)] + rows_out(total, 0)

    attn_rows = step(attn_by_wt, wide_half[0], *wide_got, tail_half[0], *tail_got)
    attn_got = send_wt(attn_rows[1:])
    layer_out = step(
        lambda hidden, own, got: low(hidden + own + wide(got) + bias_proj).reshape(batches, rows_here, width),
        hidden, down_out, down_part,
    )
    attn_part = step(lambda *parts: add_low(*parts)[0], attn_rows[0], *attn_got)
    attn_got = send_chips(attn_part)

    ffn_new = step(
        ffn_update(shard_rows, FF, ctx_count, chunk),
        ffn_whole, ffn_master, ffn_mom, ffn_sq,
    )
    attn_even = step(lambda *parts: jnp.stack(parts), attn_part, *attn_got)
    attn_odd = xor_send(attn_even, 1)
    small_total = in_order(attn_even[..., attn_columns:], attn_odd[..., attn_columns:])
    small_total = wide(small_total.reshape(-1)[:small_size])
    small_new = adam_update(small_master, small_total, small_mom, small_sq, 1.0, 0.0)
    attn_new = attn_update(shard_rows, attn_columns, width, ctx_count, piece_rows)(
        place, attn_even, attn_odd, attn_master, attn_mom, attn_sq
    )
    return (layer_out, input_grad) + tuple(attn_new) + tuple(ffn_new) + tuple(small_new)


def shift_wt(array, shift):
    count = lax.axis_size("wt")
    return lax.ppermute(array, "wt", [(i, (i + shift) % count) for i in range(count)])


def whole_wt(piece, axis):
    count, place = lax.axis_size("wt"), lax.axis_index("wt")
    shape = list(piece.shape)
    shape[axis] *= count
    buffer = put(jnp.zeros(shape, piece.dtype), piece, place, axis)
    for shift in range(1, count):
        buffer = put(buffer, shift_wt(piece, shift), (place - shift) % count, axis)
    return buffer


def whole_ctx(piece):
    count = lax.axis_size("ctx")
    got = {0: piece}
    for mask in range(2, count, 2):
        got[mask] = xor_send(piece, mask)
    for mask in range(0, count, 2):
        got[mask + 1] = xor_send(got[mask], 1)
    return [got[mask] for mask in range(count)]


def sum_ctx(pieces):
    count = lax.axis_size("ctx")
    half = {}
    for mask in range(count - 2, -1, -2):
        other = xor_send(pieces[mask + 1], 1)
        half[mask] = low(wide(pieces[mask]) + wide(other))
    total = wide(half[0])
    for mask in range(2, count, 2):
        total = total + wide(xor_send(half[mask], mask))
    return total


def sum_wt(array, axis):
    count, place = lax.axis_size("wt"), lax.axis_index("wt")
    size = array.shape[axis] // count
    total = wide(take(array, place, axis, size))
    for shift in range(1, count):
        sent = take(array, (place + shift) % count, axis, size)
        total = total + wide(shift_wt(sent, shift))
    return total


def any_shards(
    tokens,
    doc_starts,
    attn_master,
    attn_mom,
    attn_sq,
    ffn_master,
    ffn_mom,
    ffn_sq,
    small_master,
    small_mom,
    small_sq,
    cotangent,
):
    ctx_count = lax.axis_size("ctx")
    ctx_place = lax.axis_index("ctx")
    wt_count = lax.axis_size("wt")
    batches, rows_here, width = tokens.shape
    heads = width // HS
    qkv_cols = width + 2 * HS
    all_rows = batches * rows_here
    shard_rows = attn_master.shape[0]
    piece_rows = shard_rows // ctx_count
    chunk = FF // ctx_count
    order = ctx_place ^ jnp.arange(ctx_count, dtype=jnp.int32)
    (
        gain_one,
        shift_one,
        gain_two,
        shift_two,
        bias_query,
        bias_out,
        bias_proj,
        bias_value,
        bias_hidden,
    ) = split_small(small_master)

    attn_piece = low(take(attn_master, ctx_place, 0, piece_rows))

    def whole_rows(piece):
        parts = whole_ctx(whole_wt(piece[None], 0))
        buffer = jnp.zeros((wt_count, ctx_count) + piece.shape, piece.dtype)
        for k, part in enumerate(parts):
            buffer = put(buffer, part[:, None], ctx_place ^ k, 1)
        return buffer.reshape((width,) + piece.shape[1:])

    weight_qkv = whole_rows(attn_piece[:, :qkv_cols])
    weight_out = whole_rows(attn_piece[:, qkv_cols:])
    ffn_piece = low(jnp.swapaxes(take(ffn_master, ctx_place, 2, chunk), 0, 1))
    ffn_parts = whole_ctx(whole_wt(ffn_piece, 1))
    bias_parts = bias_hidden.reshape(ctx_count, chunk)[order]

    stream = wide(tokens.reshape(all_rows, width))
    normed, norm_back_one = jax.vjp(layer_norm, stream, gain_one, shift_one)
    normed_low = low(normed)
    mixed = dot(normed_low, weight_qkv)
    queries = low(mixed[:, :width] + bias_query)
    kv_local = low(
        mixed[:, width:] + jnp.concatenate([jnp.zeros((HS,), jnp.float32), bias_value])
    ).reshape(batches, rows_here, 2 * HS)
    kv_parts = jnp.stack(whole_ctx(kv_local), axis=1).reshape(
        batches, ctx_count * rows_here, 2 * HS
    )
    keys_all, values_all = kv_parts[..., :HS], kv_parts[..., HS:]
    local_pos = jnp.arange(rows_here, dtype=jnp.int32)
    query_pos = ctx_place * rows_here + local_pos
    key_pos = (order[:, None] * rows_here + local_pos[None, :]).reshape(-1)
    queries = queries.reshape(batches, rows_here * heads, HS)
    scale = HS ** (-0.5)
    attended_list, log_list, allowed_list = [], [], []
    for b in range(batches):
        starts = doc_starts[b]
        query_doc = jnp.sum((starts[None, :] <= query_pos[:, None]).astype(jnp.int32), axis=1)
        key_doc = jnp.sum((starts[None, :] <= key_pos[:, None]).astype(jnp.int32), axis=1)
        allowed = (query_doc[:, None] == key_doc[None, :]) & (key_pos[None, :] <= query_pos[:, None])
        allowed = jnp.repeat(allowed, heads, axis=0)
        allowed_list.append(allowed)
        scores = jnp.where(allowed, cols_dot(queries[b], keys_all[b]) * scale, -1e30)
        peak = jnp.max(scores, axis=-1, keepdims=True)
        expo = jnp.exp(scores - peak)
        total = jnp.sum(expo, axis=-1, keepdims=True)
        attended_list.append(dot(low(expo / total), values_all[b]))
        log_list.append(peak + jnp.log(total))
    attended = jnp.stack(attended_list)
    attended_low = low(attended).reshape(all_rows, width)
    hidden = stream + dot(attended_low, weight_out) + bias_out
    normed_two, norm_back_two = jax.vjp(layer_norm, hidden, gain_two, shift_two)
    normed_two_low = low(normed_two)

    back_low = cotangent.reshape(all_rows, width)
    back_rows = wide(back_low)
    down_vals = jnp.zeros((all_rows, width), jnp.float32)
    grad_normed_two = jnp.zeros((all_rows, width), jnp.float32)
    ffn_grads, hidden_grads = [], []
    for k in range(ctx_count):
        weight_up, weight_down = ffn_parts[k][0], ffn_parts[k][1]
        value, slope = gelu_both(dot(normed_two_low, weight_up) + bias_parts[k])
        act = low(value)
        down_vals = down_vals + cols_dot(act, weight_down)
        grad_up = low(dot(back_low, weight_down) * slope)
        hidden_grads.append(jnp.sum(wide(grad_up), axis=0))
        grad_normed_two = grad_normed_two + cols_dot(grad_up, weight_up)
        ffn_grads.append(
            jnp.stack([low(rows_dot(normed_two_low, grad_up)), low(rows_dot(back_low, act))])
        )
    layer_out = low(hidden + down_vals + bias_proj).reshape(batches, rows_here, width)
    grad_bias_proj = jnp.sum(back_rows, axis=0)
    grad_bias_hidden = jnp.stack(hidden_grads)[order].reshape(FF)
    ffn_part = low(sum_wt(low(sum_ctx(ffn_grads)), 1))

    grad_hidden_part, grad_gain_two, grad_shift_two = norm_back_two(grad_normed_two)
    grad_hidden = back_rows + grad_hidden_part
    grad_bias_out = jnp.sum(grad_hidden, axis=0)
    grad_hidden_low = low(grad_hidden)
    grad_out = rows_dot(attended_low, grad_hidden_low)

    def summed_rows(grad):
        blocks = low(grad).reshape(wt_count, ctx_count, piece_rows, grad.shape[1])
        pieces = [take(blocks, ctx_place ^ k, 1, 1)[:, 0] for k in range(ctx_count)]
        part = low(sum_wt(low(sum_ctx(pieces)), 0)[0])
        buffer = jnp.zeros((ctx_count,) + part.shape, part.dtype)
        for k, got in enumerate(whole_ctx(part)):
            buffer = put(buffer, got[None], ctx_place ^ k, 0)
        return wide(buffer.reshape(shard_rows, grad.shape[1]))

    out_total = summed_rows(grad_out)

    grad_attended = low(cols_dot(grad_hidden_low, weight_out)).reshape(
        batches, rows_here * heads, HS
    )
    grad_query_list, grad_kv_list = [], []
    for b in range(batches):
        grads = grad_attended[b]
        delta = jnp.sum(wide(grads) * attended[b], axis=-1, keepdims=True)
        scores = jnp.where(allowed_list[b], cols_dot(queries[b], keys_all[b]) * scale, -1e30)
        weights = jnp.exp(scores - log_list[b])
        grad_scores = low(weights * (cols_dot(grads, values_all[b]) - delta))
        grad_query_list.append(low(dot(grad_scores, keys_all[b]) * scale))
        grad_kv_list.append(
            jnp.concatenate(
                [
                    low(rows_dot(grad_scores, queries[b]) * scale),
                    low(rows_dot(low(weights), grads)),
                ],
                axis=1,
            )
        )
    grad_query = jnp.stack(grad_query_list).reshape(all_rows, width)
    grad_kv = jnp.stack(grad_kv_list).reshape(batches, ctx_count, rows_here, 2 * HS)
    grad_kv_low = low(sum_ctx([grad_kv[:, k] for k in range(ctx_count)])).reshape(
        all_rows, 2 * HS
    )
    grad_bias_query = jnp.sum(wide(grad_query), axis=0)
    grad_bias_value = jnp.sum(wide(grad_kv_low[:, HS:]), axis=0)
    grad_mixed = jnp.concatenate([grad_query, grad_kv_low], axis=1)
    qkv_total = summed_rows(rows_dot(normed_low, grad_mixed))
    grad_normed = cols_dot(grad_mixed, weight_qkv)
    grad_stream_part, grad_gain_one, grad_shift_one = norm_back_one(grad_normed)
    input_grad = (grad_hidden + grad_stream_part).reshape(batches, rows_here, width)

    ffn_buffer = jnp.zeros((ctx_count,) + ffn_part.shape, ffn_part.dtype)
    for k, got in enumerate(whole_ctx(ffn_part)):
        ffn_buffer = put(ffn_buffer, got[None], ctx_place ^ k, 0)
    ffn_total = wide(jnp.transpose(ffn_buffer, (2, 1, 0, 3)).reshape(shard_rows, 2, FF))
    attn_total = jnp.concatenate([qkv_total, out_total], axis=1)
    grad_small = jnp.concatenate(
        [
            grad_gain_one,
            grad_shift_one,
            grad_gain_two,
            grad_shift_two,
            grad_bias_query,
            grad_bias_out,
            grad_bias_proj,
            grad_bias_value,
            grad_bias_hidden,
        ]
    )
    small_total = lax.psum(grad_small, ("ctx", "wt"))
    attn_new = adam_update(attn_master, attn_total, attn_mom, attn_sq, 0.1, 0.1)
    ffn_new = adam_update(ffn_master, ffn_total, ffn_mom, ffn_sq, 0.1, 0.1)
    small_new = adam_update(small_master, small_total, small_mom, small_sq, 1.0, 0.0)
    return (layer_out, input_grad) + attn_new + ffn_new + small_new


def solution(mesh):
    rows, cube = P("wt", None), P("wt", None, None)
    flow = P("wt", "ctx", None)
    in_specs = (flow, rows, rows, rows, rows, cube, cube, cube, P(), P(), P(), flow)
    out_specs = (flow, flow, rows, rows, rows, cube, cube, cube, P(), P(), P())
    ctx_count, wt_count = mesh.shape["ctx"], mesh.shape["wt"]
    fitted = ctx_count == 8 and wt_count % 2 == 0 and D // wt_count % (4 * ctx_count) == 0
    body = shards if fitted else any_shards
    return jax.shard_map(body, mesh=mesh, in_specs=in_specs, out_specs=out_specs, check_vma=False)
```

```python
import jax
import jax.numpy as jnp
from jax import lax
from jax.experimental import pallas as pl
from jax.experimental.pallas import tpu as pltpu
from jax.sharding import PartitionSpec as P

D = 768
HS = 64
FF = 3072
STEP = 10


NORM_EPS = 1e-05
GELU_COEF = 0.7978845608028654
GELU_CUBE = 0.044715
BETA_ONE = 0.9
BETA_TWO = 0.95
ADAM_EPS = 1e-08
VMEM_LIMIT = 56 << 20
NO_COST = pl.CostEstimate(flops=0, bytes_accessed=0, transcendentals=0)


def layer_norm(values, gain, shift):
    centre = values - jnp.mean(values, axis=-1, keepdims=True)
    spread = jnp.mean(centre * centre, axis=-1, keepdims=True)
    return centre * lax.rsqrt(spread + NORM_EPS) * gain + shift


def gelu_both(u):
    square = u * u
    share = 0.5 * jnp.tanh(u * (GELU_COEF * GELU_CUBE * square + GELU_COEF)) + 0.5
    bend = u * (6.0 * GELU_COEF * GELU_CUBE * square + 2.0 * GELU_COEF)
    return u * share, share * ((1.0 - share) * bend) + share


def split_small(small):
    return (
        small[0:D],
        small[D : 2 * D],
        small[2 * D : 3 * D],
        small[3 * D : 4 * D],
        small[4 * D : 5 * D],
        small[5 * D : 6 * D],
        small[6 * D : 7 * D],
        small[7 * D : 7 * D + HS],
        small[7 * D + HS :],
    )


def rows_dot(left, right):
    return lax.dot_general(
        left, right, (((0,), (0,)), ((), ())), preferred_element_type=jnp.float32
    )


def cols_dot(left, right):
    return lax.dot_general(
        left, right, (((1,), (1,)), ((), ())), preferred_element_type=jnp.float32
    )


def dot(left, right):
    return jnp.dot(left, right, preferred_element_type=jnp.float32)


def low(values):
    return values.astype(jnp.bfloat16)


def wide(values):
    return values.astype(jnp.float32)


def adam_update(master, gradient, first, second, step_rate, decay_rate):
    first_new = BETA_ONE * first + (1.0 - BETA_ONE) * gradient
    second_new = BETA_TWO * second + (1.0 - BETA_TWO) * gradient * gradient
    first_hat = first_new / (1.0 - BETA_ONE**STEP)
    second_hat = second_new / (1.0 - BETA_TWO**STEP)
    master_new = master - step_rate * (
        first_hat / (jnp.sqrt(second_hat) + ADAM_EPS) + decay_rate * master
    )
    return (first_new, second_new, master_new)


def xor_send(array, mask):
    count = lax.axis_size("ctx")
    return lax.ppermute(array, "ctx", [(i, i ^ mask) for i in range(count)])


def xor_wt(array, mask):
    count = lax.axis_size("wt")
    return lax.ppermute(array, "wt", [(i, i ^ mask) for i in range(count)])


class Steps:
    def __init__(self):
        self.last = ()

    def __call__(self, function, *args):
        flat, tree = jax.tree.flatten(args)
        held = lax.optimization_barrier(tuple(flat) + self.last)[: len(flat)]
        result = function(*jax.tree.unflatten(tree, held))
        self.last = tuple(jax.tree.leaves(result))
        return result


def put(buffer, piece, place, axis):
    starts = [0] * buffer.ndim
    starts[axis] = place * piece.shape[axis]
    return lax.dynamic_update_slice(buffer, piece, starts)


def take(buffer, place, axis, size):
    return lax.dynamic_slice_in_dim(buffer, place * size, size, axis)


def attention_kernels(batches, rows, width, parts, runs):
    half_parts = parts // 2
    keys = parts * rows
    pair = 2 * HS
    groups = width // (2 * pair)
    factor = HS ** (-0.5) * 1.4426950408889634
    tile = 32
    masks = list(range(0, parts, 2)) + list(range(1, parts, 2))

    def lanes(shape):
        return lax.broadcasted_iota(jnp.int32, shape, 1)

    def spread(even_ref, odd_ref, key_ref, value_ref):
        for j in range(parts):
            ref = even_ref if j < half_parts else odd_ref
            block = wide(ref[j % half_parts, 0])
            turned = pltpu.roll(block, HS, 1)
            first = lanes(block.shape) < HS
            here = pl.ds(j * rows, rows)
            key_ref[0, here, :] = low(jnp.where(first, block, 0.0))
            key_ref[1, here, :] = low(jnp.where(first, 0.0, turned))
            value_ref[0, here, :] = low(jnp.where(first, turned, 0.0))
            value_ref[1, here, :] = low(jnp.where(first, 0.0, block))

    def doc_begin(starts_ref, stream, positions):
        begin = jnp.zeros_like(positions)
        for j in range(starts_ref.shape[1]):
            start = starts_ref[stream, j]
            begin = jnp.where(start <= positions, jnp.maximum(begin, start), begin)
        return begin

    def forward(starts_ref, place_ref, query_ref, even_ref, odd_ref, low_ref, full_ref, log_ref, cap, key, value, weight):
        stream, place = pl.program_id(0), place_ref[0]
        spread(even_ref, odd_ref, key, value)
        query_pos = place * rows + lax.broadcasted_iota(jnp.int32, (rows, 1), 0)
        begin = doc_begin(starts_ref, stream, query_pos)
        for j, mask in enumerate(masks):
            key_pos = (place ^ mask) * rows + lax.broadcasted_iota(jnp.int32, (rows, rows), 1)
            allowed = (key_pos >= begin) & (key_pos <= query_pos)
            cap[:, j * rows : (j + 1) * rows] = jnp.where(allowed, 3.0e38, -1e30)
        column = lanes((tile, pair))
        logs = [jnp.zeros((tile, pair), jnp.float32) for _ in range(rows // tile)]
        for g in range(groups):
            at = g * 2 * pair
            two = jnp.concatenate([query_ref[0, :, at : at + pair], query_ref[0, :, at + pair : at + 2 * pair]], axis=0)
            totals = []
            for half in range(2):
                scores = cols_dot(two, key[half])
                norms = []
                for t in range(2 * rows // tile):
                    own = slice(t * tile, (t + 1) * tile)
                    n = t % (rows // tile)
                    part = jnp.minimum(scores[own] * factor, cap[n * tile : (n + 1) * tile, :])
                    peak = jnp.max(part, axis=1, keepdims=True)
                    expo = jnp.exp2(part - peak)
                    norm = jnp.sum(expo, axis=1, keepdims=True)
                    weight[half, own, :] = low(expo)
                    norms.append(norm)
                    head = 4 * g + 2 * (t * tile // rows) + half
                    logs[n] = jnp.where(column == head, peak + jnp.log2(norm), logs[n])
                totals.append(dot(weight[half], value[half]) / jnp.concatenate(norms, axis=0))
            total = totals[0] + totals[1]
            for j in range(2):
                part = total[j * rows : (j + 1) * rows]
                full_ref[0, :, at + j * pair : at + (j + 1) * pair] = part
                low_ref[0, :, at + j * pair : at + (j + 1) * pair] = low(part)
        for n, log in enumerate(logs):
            log_ref[0, n * tile : (n + 1) * tile, :] = log

    def backward(
        starts_ref, place_ref, query_ref, even_ref, odd_ref, full_ref, log_ref, grad_ref,
        query_grad_ref, even_grad_ref, odd_grad_ref,
        cap, key, value, key_turned, log_rows, delta_rows, weight_buf, score_buf, query_buf, grad_buf,
    ):
        stream, place = pl.program_id(0) + place_ref[1], place_ref[0]
        spread(even_ref, odd_ref, key, value)
        query_pos = place * rows + lax.broadcasted_iota(jnp.int32, (1, rows), 1)
        begin = doc_begin(starts_ref, stream, query_pos)
        for j, mask in enumerate(masks):
            key_pos = (place ^ mask) * rows + lax.broadcasted_iota(jnp.int32, (rows, rows), 0)
            allowed = (key_pos >= begin) & (key_pos <= query_pos)
            cap[j * rows : (j + 1) * rows, :] = jnp.where(allowed, 3.0e38, -1e30)
            here = pl.ds(j * rows, rows)
            key_turned[:, j * rows : (j + 1) * rows] = low(wide(key[0, here, :]).T[:HS])
        log_rows[...] = log_ref[0].T[: log_rows.shape[0]]
        head_of = lax.broadcasted_iota(jnp.int32, (delta_rows.shape[0], width), 1) // HS
        chosen = (head_of == lax.broadcasted_iota(jnp.int32, (delta_rows.shape[0], width), 0)).astype(jnp.float32)
        delta_rows[...] = lax.dot_general(
            chosen, wide(grad_ref[0]) * full_ref[0], (((1,), (1,)), ((), ())),
            precision=lax.Precision.HIGHEST, preferred_element_type=jnp.float32,
        )
        first = lanes((2 * rows, pair)) < HS
        for g in range(groups):
            at = g * 2 * pair
            both, both_grad = query_ref[0, :, at : at + 2 * pair], grad_ref[0, :, at : at + 2 * pair]
            two = jnp.concatenate([both[:, :pair], both[:, pair:]], axis=0)
            two_grad = jnp.concatenate([both_grad[:, :pair], both_grad[:, pair:]], axis=0)
            turned = []
            for half in range(2):
                h = 4 * g + half
                span = slice((2 * g + half) * 2 * rows, (2 * g + half + 1) * 2 * rows)
                keep = first if half == 0 else jnp.logical_not(first)
                query_buf[span, :] = low(jnp.where(keep, wide(two), 0.0))
                grad_buf[span, :] = low(jnp.where(keep, wide(two_grad), 0.0))
                log = jnp.concatenate([log_rows[h : h + 1, :], log_rows[h + 2 : h + 3, :]], axis=1)
                delta = jnp.concatenate([delta_rows[h : h + 1, :], delta_rows[h + 2 : h + 3, :]], axis=1)
                scores, weight_grads = cols_dot(key[half], two), cols_dot(value[half], two_grad)
                for t in range(keys // (2 * tile)):
                    own = slice(t * 2 * tile, (t + 1) * 2 * tile)
                    limit = cap[own, :]
                    limit = jnp.concatenate([limit, limit], axis=1)
                    weights = jnp.exp2(jnp.minimum(scores[own] * factor, limit) - log)
                    weight_buf[own, span] = low(weights)
                    score_buf[own, span] = low(weights * (weight_grads[own] - delta))
                turned.append(dot(key_turned[...], score_buf[:, span]))
            turned = jnp.concatenate(turned, axis=0) * HS ** (-0.5)
            query_grad_ref[0, :, at : at + pair] = low(turned[:, :rows].T)
            query_grad_ref[0, :, at + pair : at + 2 * pair] = low(turned[:, rows:].T)
        for j in range(parts):
            here = pl.ds(j * rows, rows)
            value_sum = dot(weight_buf[here, :], grad_buf[...])
            key_sum = dot(score_buf[here, :], query_buf[...]) * HS ** (-0.5)
            value_sum = value_sum + pltpu.roll(value_sum, HS, 1)
            key_sum = key_sum + pltpu.roll(key_sum, HS, 1)
            ref = even_grad_ref if j < half_parts else odd_grad_ref
            ref[j % half_parts, 0] = low(jnp.where(lanes((rows, pair)) < HS, key_sum, value_sum))

    def specs(first):
        return (
            pl.BlockSpec((1, rows, width), lambda b, *_: (b + first, 0, 0)),
            pl.BlockSpec((1, rows, pair), lambda b, *_: (b + first, 0, 0)),
            pl.BlockSpec((half_parts, 1, rows, pair), lambda b, *_: (0, b + first, 0, 0)),
        )

    flow, logs, blocks = specs(0)

    shared = [
        pltpu.VMEM((2, keys, pair), jnp.bfloat16),
        pltpu.VMEM((2, keys, pair), jnp.bfloat16),
    ]
    run_forward = pl.pallas_call(
        forward,
        grid_spec=pltpu.PrefetchScalarGridSpec(
            num_scalar_prefetch=2,
            grid=(batches,),
            in_specs=[flow, blocks, blocks],
            out_specs=[flow, flow, logs],
            scratch_shapes=[pltpu.VMEM((rows, keys), jnp.float32)]
            + shared
            + [pltpu.VMEM((2, 2 * rows, keys), jnp.bfloat16)],
        ),
        out_shape=[
            jax.ShapeDtypeStruct((batches, rows, width), jnp.bfloat16),
            jax.ShapeDtypeStruct((batches, rows, width), jnp.float32),
            jax.ShapeDtypeStruct((batches, rows, pair), jnp.float32),
        ],
        compiler_params=pltpu.CompilerParams(vmem_limit_bytes=VMEM_LIMIT),
        cost_estimate=NO_COST,
        name="attention_forward",
    )
    head_rows = -(-(width // HS) // 8) * 8
    all_columns = rows * (width // HS)
    count = batches // runs

    def call_backward(run):
        here_flow, here_logs, here_blocks = specs(run * count)
        return pl.pallas_call(
        backward,
        grid_spec=pltpu.PrefetchScalarGridSpec(
            num_scalar_prefetch=2,
            grid=(count,),
            in_specs=[here_flow, here_blocks, here_blocks, here_flow, here_logs, here_flow],
            out_specs=[flow, blocks, blocks],
            scratch_shapes=[pltpu.VMEM((keys, rows), jnp.float32)]
            + shared
            + [
                pltpu.VMEM((HS, keys), jnp.bfloat16),
                pltpu.VMEM((head_rows, rows), jnp.float32),
                pltpu.VMEM((head_rows, rows), jnp.float32),
                pltpu.VMEM((keys, all_columns), jnp.bfloat16),
                pltpu.VMEM((keys, all_columns), jnp.bfloat16),
                pltpu.VMEM((all_columns, pair), jnp.bfloat16),
                pltpu.VMEM((all_columns, pair), jnp.bfloat16),
            ],
        ),
        out_shape=[
            jax.ShapeDtypeStruct((count, rows, width), jnp.bfloat16),
            jax.ShapeDtypeStruct((half_parts, count, rows, pair), jnp.bfloat16),
            jax.ShapeDtypeStruct((half_parts, count, rows, pair), jnp.bfloat16),
        ],
        compiler_params=pltpu.CompilerParams(vmem_limit_bytes=VMEM_LIMIT),
        cost_estimate=NO_COST,
        name="attention_backward",
    )

    return run_forward, [call_backward(run) for run in range(runs)]


def in_hbm(arrays):
    return [pltpu.with_memory_space_constraint(array, pltpu.HBM) for array in arrays]


def ffn_kernels(rows, width, chunk, wt_count):
    units = 2 * chunk
    all_rows = 2 * rows
    block_rows = width // wt_count
    hbm = pl.BlockSpec(memory_space=pltpu.HBM)
    vmem = pl.BlockSpec(memory_space=pltpu.VMEM)
    params = pltpu.CompilerParams(vmem_limit_bytes=VMEM_LIMIT)

    def fetch(weights, which, held, sem):
        copies = []
        for n, arrays in enumerate(weights):
            blocks = [array.at[block] for array in arrays for block in range(array.shape[0])]
            for row, block in enumerate(blocks):
                copies.append(
                    pltpu.make_async_copy(
                        block.at[pl.ds(which * block_rows, block_rows), :],
                        held.at[pl.ds(row * block_rows, block_rows), pl.ds(n * chunk, chunk)],
                        sem.at[len(copies)],
                    )
                )
        for copy in copies:
            copy.start()
        return copies

    def send(pairs, sems):
        copies = [pltpu.make_async_copy(source, out, sems.at[n]) for n, (source, out) in enumerate(pairs)]
        for copy in copies:
            copy.start()
        return copies

    def units_of(inputs, grads, bias, held_up, held_down, act, grad_units):
        tile = 16
        sums = jnp.zeros((8, units), jnp.float32)
        for s in range(2):
            up = dot(inputs[s][...], held_up[...])
            act_grad = dot(grads[s][...], held_down[...])
            for t in range(rows // tile):
                own = slice(t * tile, (t + 1) * tile)
                here = slice(s * rows + t * tile, s * rows + (t + 1) * tile)
                value, slope = gelu_both(up[own] + bias)
                grad = act_grad[own] * slope
                act[here, :] = low(value)
                grad_units[here, :] = low(grad)
                sums = sums + (grad[:8] + grad[8:])
        return jnp.sum(sums, axis=0, keepdims=True)

    def halves(product, m):
        cols = pl.ds(m * chunk, chunk)
        return [product.at[pl.ds(h * width // 2, width // 2), cols] for h in range(2)]

    def first(
        own, other, grad_own, grad_other, turned, bias, w0, w1,
        act_out, units_out, out_a, out_b, sums_out,
        held_up, held_down, act, grad_units, product, sems, out_sems,
    ):
        weights = ((w0,), (w1,))
        copies = fetch(weights, 0, held_up, sems.at[0]) + fetch(weights, 1, held_down, sems.at[1])
        for copy in copies:
            copy.wait()
        sums_out[...] = units_of((own, other), (grad_own, grad_other), bias[...], held_up, held_down, act, grad_units)
        sent = send(((act, act_out), (grad_units, units_out)), out_sems.at[0])
        product[...] = low(dot(turned[...], act[...]))
        sent += send(
            ((product.at[:, pl.ds(0, chunk)], out_a), (product.at[:, pl.ds(chunk, chunk)], out_b)), out_sems.at[1]
        )
        for copy in sent:
            copy.wait()

    def second(
        own, other, grad_own, grad_other, turned, bias, units_first, w0, w1, w2, w3, w4,
        act_out, units_out, out_a, out_b, out_c, sums_out, back_own, back_other,
        held_up, held_more, held_down, act, grad_units, more_units, product, sems, out_sems, more_sem,
    ):
        weights, before = ((w2,), (w3, w4)), ((w0,), (w1,))
        copies = fetch(weights, 0, held_up, sems.at[0]) + fetch(weights, 1, held_down, sems.at[1])
        more = fetch(before, 0, held_more, sems.at[2])
        more.append(pltpu.make_async_copy(units_first, more_units, more_sem))
        more[-1].start()
        for copy in copies:
            copy.wait()
        sums_out[...] = units_of((own, other), (grad_own, grad_other), bias[...], held_up, held_down, act, grad_units)
        sent = send(((act, act_out), (grad_units, units_out)), out_sems.at[0])
        product[...] = low(dot(turned[...], act[...]))
        top, bottom = halves(product, 1)
        sent += send(((product.at[:, pl.ds(0, chunk)], out_a), (top, out_b), (bottom, out_c)), out_sems.at[1])
        for copy in more:
            copy.wait()
        for s, ref in enumerate((back_own, back_other)):
            here = slice(s * rows, (s + 1) * rows)
            total = cols_dot(grad_units[here, :], held_up[...]) + cols_dot(more_units[here, :], held_more[...])
            ref[...] = total.astype(ref.dtype)
        for copy in sent:
            copy.wait()

    def third(own, other, units_a, units_b, out_0, out_1, out_2, out_3, out_4, turned, held, products, sems, out_sems):
        copies = send(((units_a, held.at[0]), (units_b, held.at[1])), sems)
        turn((own, other), turned)
        for copy in copies:
            copy.wait()
        products[1] = low(dot(turned[...], held[1]))
        top, bottom = halves(products.at[1], 1)
        sent = send(((products.at[1, :, pl.ds(0, chunk)], out_2), (top, out_3), (bottom, out_4)), out_sems.at[0])
        products[0] = low(dot(turned[...], held[0]))
        sent += send(
            ((products.at[0, :, pl.ds(0, chunk)], out_0), (products.at[0, :, pl.ds(chunk, chunk)], out_1)),
            out_sems.at[1],
        )
        for copy in sent:
            copy.wait()

    def down(act_a, act_b, w0, w1, w2, w3, w4, own_ref, other_ref, held_a, held_b, sems):
        copies = fetch(((w0,), (w1,)), 1, held_a, sems.at[0]) + fetch(((w2,), (w3, w4)), 1, held_b, sems.at[1])
        for copy in copies:
            copy.wait()
        for s, ref in enumerate((own_ref, other_ref)):
            here = slice(s * rows, (s + 1) * rows)
            total = cols_dot(act_a[here, :], held_a[...]) + cols_dot(act_b[here, :], held_b[...])
            ref[...] = total.astype(ref.dtype)

    dma = pltpu.SemaphoreType.DMA
    held = pltpu.VMEM((width, units), jnp.bfloat16)
    flow = pltpu.VMEM((all_rows, units), jnp.bfloat16)
    flow_out = pltpu.HBM((all_rows, units), jnp.bfloat16)
    whole = pltpu.HBM((width, chunk), jnp.bfloat16)
    part = pltpu.HBM((width // 2, chunk), jnp.bfloat16)
    sums = jax.ShapeDtypeStruct((1, units), jnp.float32)
    own = jax.ShapeDtypeStruct((rows, width), jnp.float32)
    other = jax.ShapeDtypeStruct((rows, width), jnp.bfloat16)
    run_first = pl.pallas_call(
        first,
        in_specs=[vmem] * 6 + [hbm] * 2,
        out_specs=[hbm] * 4 + [vmem],
        out_shape=[flow_out, flow_out, whole, whole, sums],
        scratch_shapes=[held, held, flow, flow, held, dma((2, 2 * wt_count)), dma((2, 2))],
        compiler_params=params,
        cost_estimate=NO_COST,
        name="ffn_first",
    )
    run_second = pl.pallas_call(
        second,
        in_specs=[vmem] * 6 + [hbm] * 6,
        out_specs=[hbm] * 5 + [vmem] * 3,
        out_shape=[flow_out, flow_out, whole, part, part, sums, own, other],
        scratch_shapes=[held, held, held, flow, flow, flow, held, dma((3, 2 * wt_count)), dma((2, 3)), dma(())],
        compiler_params=params,
        cost_estimate=NO_COST,
        name="ffn_second",
    )
    run_third = pl.pallas_call(
        third,
        in_specs=[vmem] * 2 + [hbm] * 2,
        out_specs=[hbm] * 5,
        out_shape=[whole, whole, whole, part, part],
        scratch_shapes=[
            pltpu.VMEM((width, all_rows), jnp.bfloat16),
            pltpu.VMEM((2, all_rows, units), jnp.bfloat16),
            pltpu.VMEM((2, width, units), jnp.bfloat16),
            dma((2,)),
            dma((2, 3)),
        ],
        compiler_params=params,
        cost_estimate=NO_COST,
        name="ffn_grads",
    )
    run_down = pl.pallas_call(
        down,
        in_specs=[vmem] * 2 + [hbm] * 5,
        out_specs=[vmem] * 2,
        out_shape=[own, other],
        scratch_shapes=[held, held, dma((2, 2 * wt_count))],
        compiler_params=params,
        cost_estimate=NO_COST,
        name="ffn_down",
    )
    return run_first, run_second, run_third, run_down


def turn(refs, turned):
    rows = refs[0].shape[0]
    for s, ref in enumerate(refs):
        for i in range(rows // 128):
            block = wide(ref[i * 128 : (i + 1) * 128, :])
            turned[:, s * rows + i * 128 : s * rows + (i + 1) * 128] = low(block.T)


def turn_both(own, other):
    vmem = pl.BlockSpec(memory_space=pltpu.VMEM)
    rows, width = own.shape
    return pl.pallas_call(
        lambda a, b, out: turn((a, b), out),
        in_specs=[vmem] * 2,
        out_specs=vmem,
        out_shape=jax.ShapeDtypeStruct((width, 2 * rows), own.dtype),
        compiler_params=pltpu.CompilerParams(vmem_limit_bytes=VMEM_LIMIT),
        cost_estimate=NO_COST,
        name="turn",
    )(own, other)


def out_projection(rows, width, wt_count, chips, piece):
    def kernel(place_ref, attended, stream, bias, gain, shift, even_ref, odd_ref, hidden_ref, normed_ref, weight_ref, held, sems):
        chip, core = place_ref[0] // 2, place_ref[0] % 2
        copies = []
        for p, ref in enumerate((even_ref, odd_ref)):
            for m in range(chips):
                for z in range(wt_count):
                    row = pl.multiple_of((z * chips + (chip ^ m)) * piece, 16)
                    column = pl.multiple_of((core ^ p) * (width // 2), 128)
                    copies.append(
                        pltpu.make_async_copy(
                            ref.at[m, z],
                            held.at[pl.ds(row, piece), pl.ds(column, width // 2)],
                            sems.at[len(copies)],
                        )
                    )
                    copies[-1].start()
        for copy in copies:
            copy.wait()
        hidden = wide(stream[...]) + dot(attended[...], held[...]) + bias[...]
        hidden_ref[...] = hidden
        normed_ref[...] = low(layer_norm(hidden, gain[...], shift[...]))
        weight_ref[...] = held[...]

    vmem = pl.BlockSpec(memory_space=pltpu.VMEM)
    hbm = pl.BlockSpec(memory_space=pltpu.HBM)
    return pl.pallas_call(
        kernel,
        in_specs=[pl.BlockSpec(memory_space=pltpu.SMEM)] + [vmem] * 5 + [hbm] * 2,
        out_specs=[vmem] * 3,
        out_shape=[
            jax.ShapeDtypeStruct((rows, width), jnp.float32),
            jax.ShapeDtypeStruct((rows, width), jnp.bfloat16),
            jax.ShapeDtypeStruct((width, width), jnp.bfloat16),
        ],
        scratch_shapes=[pltpu.VMEM((width, width), jnp.bfloat16), pltpu.SemaphoreType.DMA((2 * chips * wt_count,))],
        compiler_params=pltpu.CompilerParams(vmem_limit_bytes=VMEM_LIMIT),
        cost_estimate=NO_COST,
        name="out_projection",
    )


def norm_back(values, gain, grad):
    centre = values - jnp.mean(values, axis=-1, keepdims=True)
    scale = lax.rsqrt(jnp.mean(centre * centre, axis=-1, keepdims=True) + NORM_EPS)
    unit = centre * scale
    inner = grad * gain
    mean = jnp.mean(inner, axis=-1, keepdims=True)
    along = jnp.mean(inner * unit, axis=-1, keepdims=True)
    return scale * (inner - mean - unit * along), grad * unit


def fold_rows(values):
    total = values[:8]
    for i in range(1, values.shape[0] // 8):
        total = total + values[i * 8 : (i + 1) * 8]
    return total


def hidden_back(rows, width):
    tile = 32

    def kernel(own, got, hidden, back, gain, weight, grad_ref, low_ref, attended_ref, sums_ref):
        sums = [jnp.zeros((8, width), jnp.float32) for _ in range(3)]
        for t in range(rows // tile):
            here = slice(t * tile, (t + 1) * tile)
            pulled, terms = norm_back(hidden[here, :], gain[...], own[here, :] + wide(got[here, :]))
            grad = wide(back[here, :]) + pulled
            grad_ref[here, :] = grad
            low_ref[here, :] = low(grad)
            for n, part in enumerate((terms, own[here, :] + wide(got[here, :]), grad)):
                sums[n] = sums[n] + fold_rows(part)
        for n in range(3):
            sums_ref[n : n + 1, :] = jnp.sum(sums[n], axis=0, keepdims=True)
        attended_ref[...] = low(cols_dot(low_ref[...], weight[...]))

    vmem = pl.BlockSpec(memory_space=pltpu.VMEM)
    return pl.pallas_call(
        kernel,
        in_specs=[vmem] * 6,
        out_specs=[vmem] * 4,
        out_shape=[
            jax.ShapeDtypeStruct((rows, width), jnp.float32),
            jax.ShapeDtypeStruct((rows, width), jnp.bfloat16),
            jax.ShapeDtypeStruct((rows, width), jnp.bfloat16),
            jax.ShapeDtypeStruct((3, width), jnp.float32),
        ],
        compiler_params=pltpu.CompilerParams(vmem_limit_bytes=VMEM_LIMIT),
        cost_estimate=NO_COST,
        name="hidden_back",
    )


def stream_back(rows, width, parts, row_groups, piece):
    tile = 32
    chips = parts // 2

    def kernel(
        place_ref, kv_0, kv_1, kv_2, kv_3, queries, weight, tokens, gain, grad_hidden, normed, back, hidden_sums,
        units_a, units_b, input_ref, even_ref, odd_ref, grad_kv, grads, turned, product, small,
    ):
        place = place_ref[0]
        sums = [jnp.zeros((8, width), jnp.float32) for _ in range(4)]
        value_sums = jnp.zeros((8, 2 * HS), jnp.float32)
        for t in range(rows // tile):
            here = slice(t * tile, (t + 1) * tile)
            total = wide(kv_0[here, :]) + wide(kv_1[here, :]) + wide(kv_2[here, :]) + wide(kv_3[here, :])
            grad_kv[here, :] = low(total)
            value_sums = value_sums + fold_rows(total)
        turn((normed,), turned)
        product[...] = dot(turned[...], grad_kv[...])
        grads[...] = cols_dot(queries[...], weight[:, :width]) + cols_dot(grad_kv[...], weight[:, width:])
        for t in range(rows // tile):
            here = slice(t * tile, (t + 1) * tile)
            grad = grads[here, :]
            pulled, terms = norm_back(wide(tokens[here, :]), gain[...], grad)
            input_ref[here, :] = grad_hidden[here, :] + pulled
            for n, part in enumerate((terms, grad, wide(queries[here, :]), wide(back[here, :]))):
                sums[n] = sums[n] + fold_rows(part)
        sums = [jnp.sum(part, axis=0, keepdims=True) for part in sums]
        small[...] = jnp.zeros_like(small)
        rows_in = (sums[0], sums[1], hidden_sums[0:1, :], hidden_sums[1:2, :], sums[2], hidden_sums[2:3, :], sums[3])
        for n, row in enumerate(rows_in):
            for j in range(width // 128):
                line = n * (width // 128) + j
                small[line : line + 1, :] = row[:, j * 128 : (j + 1) * 128]
        start = 7 * (width // 128)
        small[start : start + 1, :] = jnp.sum(value_sums, axis=0, keepdims=True)
        lines = FF // parts // 128
        for m in range(chips):
            units = (units_a, units_b)[m // 2]
            for j in range(lines):
                line = start + 1 + (place ^ (2 * m)) * lines + j
                at = (m % 2 * lines + j) * 128
                small[pl.ds(line, 1), :] = units[:, at : at + 128]
        for k in range(parts):
            ref = odd_ref if k % 2 else even_ref
            mine = low(small[pl.ds(pl.multiple_of((place ^ k) * piece, 8), piece), :])
            for w in range(row_groups):
                at = pl.multiple_of(w * piece * parts + (place ^ k) * piece, 8)
                ref[k // 2, w, :, :128] = low(product[pl.ds(at, piece), :])
                ref[k // 2, w, :, 128:] = mine

    vmem = pl.BlockSpec(memory_space=pltpu.VMEM)
    stack = jax.ShapeDtypeStruct((chips, row_groups, piece, 256), jnp.bfloat16)
    return pl.pallas_call(
        kernel,
        in_specs=[pl.BlockSpec(memory_space=pltpu.SMEM)] + [vmem] * 14,
        out_specs=[vmem] * 3,
        out_shape=[jax.ShapeDtypeStruct((rows, width), jnp.float32), stack, stack],
        scratch_shapes=[
            pltpu.VMEM((rows, 2 * HS), jnp.bfloat16),
            pltpu.VMEM((rows, width), jnp.float32),
            pltpu.VMEM((width, rows), jnp.bfloat16),
            pltpu.VMEM((width, 2 * HS), jnp.float32),
            pltpu.VMEM((parts * piece, 128), jnp.float32),
        ],
        compiler_params=pltpu.CompilerParams(vmem_limit_bytes=VMEM_LIMIT),
        cost_estimate=NO_COST,
        name="stream_back",
    )


def attn_grads(rows, width, row_groups, parts, piece):
    def kernel(place_ref, left_a, right_a, left_b, right_b, even_ref, odd_ref, turned, total):
        place = place_ref[0]
        for n, (left, right) in enumerate(((left_a, right_a), (left_b, right_b))):
            for i in range(rows // 128):
                turned[:, i * 128 : (i + 1) * 128] = low(wide(left[i * 128 : (i + 1) * 128, :]).T)
            total[:, n * width : (n + 1) * width] = dot(turned[...], right[...])
        for k in range(parts):
            ref = odd_ref if k % 2 else even_ref
            for w in range(row_groups):
                at = pl.multiple_of(w * piece * parts + (place ^ k) * piece, 8)
                ref[k // 2, w] = low(total[pl.ds(at, piece), :])

    vmem = pl.BlockSpec(memory_space=pltpu.VMEM)
    shape = jax.ShapeDtypeStruct((parts // 2, row_groups, piece, 2 * width), jnp.bfloat16)
    return pl.pallas_call(
        kernel,
        grid_spec=pltpu.PrefetchScalarGridSpec(
            num_scalar_prefetch=1,
            grid=(),
            in_specs=[vmem] * 4,
            out_specs=[vmem] * 2,
            scratch_shapes=[pltpu.VMEM((width, rows), jnp.bfloat16), pltpu.VMEM((width, 2 * width), jnp.float32)],
        ),
        out_shape=[shape] * 2,
        compiler_params=pltpu.CompilerParams(vmem_limit_bytes=VMEM_LIMIT),
        cost_estimate=NO_COST,
        name="attn_grads",
    )


def attn_update(rows, columns, width, parts, piece):
    qkv = columns - width

    def kernel(place_ref, even_ref, odd_ref, master, first, second, *outs):
        place = place_ref[0]
        for k in range(parts):
            ref = odd_ref if k % 2 else even_ref
            here = pl.ds(pl.multiple_of((place ^ k) * piece, 8), piece)
            for cols, source in (
                (slice(0, width), slice(0, width)),
                (slice(width, qkv), slice(2 * width, columns)),
                (slice(qkv, columns), slice(width, 2 * width)),
            ):
                grad = wide(ref[k // 2, :, source])
                got = adam_update(master[here, cols], grad, first[here, cols], second[here, cols], 0.1, 0.1)
                outs[0][here, cols] = got[0]
                outs[1][here, cols] = got[1]
                outs[2][here, cols] = got[2]

    vmem = pl.BlockSpec(memory_space=pltpu.VMEM)
    return pl.pallas_call(
        kernel,
        grid_spec=pltpu.PrefetchScalarGridSpec(
            num_scalar_prefetch=1, grid=(), in_specs=[vmem] * 5, out_specs=[vmem] * 3, scratch_shapes=[]
        ),
        out_shape=[jax.ShapeDtypeStruct((rows, columns), jnp.float32)] * 3,
        compiler_params=pltpu.CompilerParams(vmem_limit_bytes=VMEM_LIMIT),
        cost_estimate=NO_COST,
        name="attn_update",
    )


def ffn_update(rows, units, parts, chunk):
    per_row = 2 * units // 128
    rows_once = 32
    lines = rows_once * per_row

    def kernel(grad, master, first, second, first_out, second_out, master_out, total):
        for k in range(parts):
            for j in range(chunk // 128):
                for which in range(2):
                    line = k * (2 * chunk // 128) + 2 * j + which
                    total[pl.ds(line, rows_once, per_row), :] = wide(grad[k, which, :, j * 128 : (j + 1) * 128])
        for t in range(lines // 64):
            own = slice(t * 64, (t + 1) * 64)
            got = adam_update(master[own, :], total[own, :], first[own, :], second[own, :], 0.1, 0.1)
            first_out[own, :] = got[0]
            second_out[own, :] = got[1]
            master_out[own, :] = got[2]

    block = pl.BlockSpec((lines, 128), lambda i: (i, 0))
    call = pl.pallas_call(
        kernel,
        grid=(rows // rows_once,),
        in_specs=[pl.BlockSpec((parts, 2, rows_once, chunk), lambda i: (0, 0, i, 0))] + [block] * 3,
        out_specs=[block] * 3,
        out_shape=[jax.ShapeDtypeStruct((rows * per_row, 128), jnp.float32)] * 3,
        scratch_shapes=[pltpu.VMEM((lines, 128), jnp.float32)],
        compiler_params=pltpu.CompilerParams(vmem_limit_bytes=VMEM_LIMIT),
        cost_estimate=NO_COST,
        name="ffn_update",
    )

    def fold(array):
        return jnp.swapaxes(array.reshape(rows, 2, units // 128, 128), 1, 2).reshape(-1, 128)

    def unfold(array):
        return jnp.swapaxes(array.reshape(rows, units // 128, 2, 128), 1, 2).reshape(rows, 2, units)

    def run(grad, master, first, second):
        return tuple(unfold(array) for array in call(grad, fold(master), fold(first), fold(second)))

    return run


def shards(
    tokens,
    doc_starts,
    attn_master,
    attn_mom,
    attn_sq,
    ffn_master,
    ffn_mom,
    ffn_sq,
    small_master,
    small_mom,
    small_sq,
    cotangent,
):
    ctx_count, wt_count = lax.axis_size("ctx"), lax.axis_size("wt")
    ctx_place, wt_place = lax.axis_index("ctx"), lax.axis_index("wt")
    batches, rows_here, width = tokens.shape
    qkv_cols = width + 2 * HS
    attn_columns = attn_master.shape[1]
    all_rows = batches * rows_here
    shard_rows = attn_master.shape[0]
    piece_rows = shard_rows // ctx_count
    chunk = FF // ctx_count
    chips = ctx_count // 2
    order = ctx_place ^ jnp.arange(ctx_count, dtype=jnp.int32)
    (
        gain_one,
        shift_one,
        gain_two,
        shift_two,
        bias_query,
        bias_out,
        bias_proj,
        bias_value,
        bias_hidden,
    ) = split_small(small_master)
    runs = 2 if batches % 2 == 0 else 1
    places = [jnp.stack([ctx_place, jnp.int32(run * (batches // runs))]) for run in range(runs)]
    place = places[0]
    wt_half = wt_count // 2
    out_rows = shard_rows // chips
    run_forward, run_backward = attention_kernels(batches, rows_here, width, ctx_count, runs)
    ffn_first, ffn_second, ffn_third, ffn_down = ffn_kernels(all_rows, width, chunk, wt_count)
    step = Steps()

    def both(own, got, place, bit, axis=0):
        ahead, behind = jnp.stack([own, got], axis), jnp.stack([got, own], axis)
        return jnp.where((place & bit) == 0, ahead, behind)

    def in_order(even, odd):
        buffer = jnp.zeros((ctx_count,) + even.shape[1:], even.dtype)
        for m in range(chips):
            buffer = put(buffer, even[m][None], ctx_place ^ (2 * m), 0)
            buffer = put(buffer, odd[m][None], ctx_place ^ (2 * m + 1), 0)
        return buffer

    def send_chips(piece):
        return [xor_send(piece, mask) for mask in range(2, ctx_count, 2)]

    def split_wt(total, bit):
        ahead, behind = jnp.split(total, 2)
        kept, sent = jnp.where((wt_place & bit) == 0, ahead, behind), jnp.where((wt_place & bit) == 0, behind, ahead)
        return kept, sent

    wt_bits = [1 << n for n in reversed(range(wt_count.bit_length() - 1))]

    def add_low(*arrays):
        return low(sum(wide(array) for array in arrays))

    qkv = step(
        lambda master: low(lax.dynamic_slice(master, (ctx_place * piece_rows, 0), (piece_rows, qkv_cols))), attn_master
    )
    qkv_got = xor_wt(qkv, 1)

    def cut_rest(ffn, attn):
        ffn = jnp.swapaxes(take(ffn, ctx_place, 2, chunk), 0, 1).reshape(2 * shard_rows, chunk)
        out = lax.dynamic_slice(
            attn, (ctx_place // 2 * out_rows, qkv_cols + ctx_place % 2 * chunk), (out_rows, chunk)
        )
        return low(jnp.concatenate([ffn, out]))

    rest = step(cut_rest, ffn_master, attn_master)
    rest = lax.all_gather(rest, "wt", axis=0)
    back_low = cotangent.reshape(all_rows, width)
    back_other = xor_send(back_low, 1)
    flat_tokens = tokens.reshape(all_rows, width)
    qkv = step(lambda own, got: both(own, got, wt_place, 1), qkv, qkv_got)
    for bit in [1 << n for n in range(1, wt_count.bit_length() - 1)]:
        qkv_got = xor_wt(qkv, bit)
        qkv = step(
            lambda own, got: both(own, got, wt_place, bit).reshape((-1,) + own.shape[1:]), qkv, qkv_got
        )
    qkv_got = xor_send(qkv, 2)
    normed_low = step(
        lambda tokens, gain, shift: low(layer_norm(wide(tokens), gain, shift)), flat_tokens, gain_one, shift_one
    )
    qkv = step(lambda own, got: both(own, got, ctx_place, 2), qkv, qkv_got)
    qkv_got = xor_send(qkv, 4)
    back_turned = step(turn_both, back_low, back_other)
    qkv = step(lambda own, got: both(own, got, ctx_place, 4), qkv, qkv_got)
    qkv_got = xor_send(qkv, 1)

    def project(own, got, normed):
        blocks = both(own, got, ctx_place, 1, 2)
        weight = jnp.transpose(blocks, (3, 0, 1, 2, 4, 5)).reshape(width, qkv_cols)
        mixed = dot(normed, weight)
        queries = low(mixed[:, :width] + bias_query).reshape(batches, rows_here, width)
        kv_bias = jnp.concatenate([jnp.zeros((HS,), jnp.float32), bias_value])
        kv_local = low(mixed[:, width:] + kv_bias).reshape(batches, rows_here, 2 * HS)
        return weight, queries, kv_local

    weight_qkv, queries, kv_local = step(project, qkv, qkv_got, normed_low)
    kv_got = send_chips(kv_local)
    kv_even = step(lambda *parts: jnp.stack(parts), kv_local, *kv_got)
    kv_odd = xor_send(kv_even, 1)
    out_own = step(lambda rest: rest[:, 2 * shard_rows :], rest)
    out_got = send_chips(out_own)
    kv_odd = step(lambda odd: odd, kv_odd)
    rest = step(lambda rest: rest[:, : 2 * shard_rows], rest)
    rest_x, rest_y = xor_send(rest, 2), xor_send(rest, 4)

    attended_low, attended, logs = step(run_forward, doc_starts, place, queries, kv_even, kv_odd)
    attended_low = attended_low.reshape(all_rows, width)
    out_even = step(lambda *parts: jnp.stack(parts), out_own, *out_got)
    out_odd = xor_send(out_even, 1)
    low_half, high_half = step(lambda x, y: (x[:wt_half], y[wt_half:]), rest_x, rest_y)
    diagonal_low, diagonal_high = xor_send(low_half, 4), xor_send(high_half, 2)
    hidden, normed_two, weight_out = step(
        lambda *args: out_projection(all_rows, width, wt_count, chips, out_rows)(*args[:6], *in_hbm(args[6:])),
        place, attended_low, flat_tokens, bias_out[None], gain_two[None], shift_two[None],
        out_even, out_odd,
    )
    normed_other = xor_send(normed_two, 1)

    bias_parts = bias_hidden.reshape(ctx_count, chunk)[order[::2]].reshape(1, chips * chunk)
    bias_near, bias_far = jnp.split(bias_parts, 2, axis=1)
    weights = [rest, rest_x, rest_y, diagonal_low, diagonal_high]
    flows = (normed_two, normed_other, back_low, back_other, back_turned)
    act_first, units_first, down_own, down_x, sums_first = step(
        lambda *args: ffn_first(*args[:6], *in_hbm(args[6:])), *flows, bias_near, *weights[:2]
    )
    act_second, units_second, down_y, down_top, down_bottom, sums_second, back_own, back_part = step(
        lambda *args: ffn_second(*args[:6], *in_hbm(args[6:])), *flows, bias_far, units_first, *weights
    )
    back_got = xor_send(back_part, 1)
    top_got, bottom_got = xor_send(down_top, 4), xor_send(down_bottom, 2)

    def meet(along_x, along_y, top, bottom):
        half = width // 2
        return (
            jnp.concatenate([add_low(along_x[:half], top), along_x[half:]]),
            jnp.concatenate([along_y[:half], add_low(along_y[half:], bottom)]),
        )

    up_own, up_x, up_y, up_top, up_bottom = step(
        lambda *args: ffn_third(*args[:2], *in_hbm(args[2:])), normed_two, normed_other, units_first, units_second
    )
    down_x, down_y = step(meet, down_x, down_y, top_got, bottom_got)
    down_got = [xor_send(down_x, 2), xor_send(down_y, 4)]
    top_got, bottom_got = xor_send(up_top, 4), xor_send(up_bottom, 2)

    grad_hidden, grad_hidden_low, grad_attended, hidden_sums = step(
        hidden_back(all_rows, width), back_own, back_got, hidden, back_low, gain_two[None], weight_out
    )
    grad_attended = grad_attended.reshape(batches, rows_here, width)
    up_x, up_y = step(meet, up_x, up_y, top_got, bottom_got)
    up_got = [xor_send(up_x, 2), xor_send(up_y, 4)]

    def by_wt(own, *got):
        total = add_low(own, *got)
        return split_wt(total.reshape(wt_count, shard_rows, chunk), wt_bits[0])

    def next_wt(bit):
        return lambda kept, got: split_wt(add_low(kept, got), bit)

    backs = [step(run_backward[0], doc_starts, places[0], queries, kv_even, kv_odd, attended, logs, grad_attended)]
    kv_got = [xor_send(backs[0][2], 1)]
    down_kept, down_sent = step(by_wt, down_own, *down_got)
    down_got = xor_wt(down_sent, wt_bits[0])
    backs += [
        step(run_backward[run], doc_starts, places[run], queries, kv_even, kv_odd, attended, logs, grad_attended)
        for run in range(1, runs)
    ]
    kv_got += [xor_send(back[2], 1) for back in backs[1:]]
    grad_query = jnp.concatenate([back[0] for back in backs]).reshape(all_rows, width)

    def kv_pieces(evens, odds):
        total = jnp.concatenate([add_low(a, b) for a, b in zip(evens, odds)], axis=1)
        return [total[m] for m in range(chips)]

    for bit in wt_bits[1:]:
        down_kept, down_sent = step(next_wt(bit), down_kept, down_got)
        down_got = xor_wt(down_sent, bit)
    up_kept, up_sent = step(by_wt, up_own, *up_got)
    up_got = xor_wt(up_sent, wt_bits[0])
    kv_half = step(kv_pieces, [back[1] for back in backs], kv_got)
    kv_got = [xor_send(kv_half[m], 2 * m) for m in range(1, chips)]
    wide_even, wide_odd = step(
        attn_grads(all_rows, width, wt_count, ctx_count, piece_rows),
        place, normed_low, grad_query, attended_low, grad_hidden_low,
    )
    down_part = step(add_low, down_kept, down_got)
    wide_odd = xor_send(wide_odd, 1)

    small_size = small_master.shape[0]
    input_grad, tail_even, tail_odd = step(
        stream_back(all_rows, width, ctx_count, wt_count, piece_rows),
        place, *[array.reshape(all_rows, 2 * HS) for array in (kv_half[0], *kv_got)], grad_query, weight_qkv,
        flat_tokens, gain_one[None], grad_hidden, normed_low, back_low, hidden_sums, sums_first, sums_second,
    )
    input_grad = input_grad.reshape(batches, rows_here, width)
    tail_odd = xor_send(tail_odd, 1)
    for bit in wt_bits[1:]:
        up_kept, up_sent = step(next_wt(bit), up_kept, up_got)
        up_got = xor_wt(up_sent, bit)

    def attn_pieces(wide_even, wide_odd, tail_even, tail_odd):
        total = jnp.concatenate([add_low(wide_even, wide_odd), add_low(tail_even, tail_odd)], axis=3)
        return [total[m] for m in range(chips)]

    attn_half = step(attn_pieces, wide_even, wide_odd, tail_even, tail_odd)
    attn_got = [xor_send(attn_half[m], 2 * m) for m in range(1, chips)]
    ffn_part = step(
        lambda up_kept, up_got, down_part: jnp.concatenate([add_low(up_kept, up_got), down_part]),
        up_kept, up_got, down_part,
    )
    ffn_got = xor_send(ffn_part, 2)
    down_out, down_other = step(
        lambda *args: ffn_down(*args[:2], *in_hbm(args[2:])), act_first, act_second, *weights
    )
    down_other = xor_send(down_other, 1)
    ffn_part = step(lambda own, got: both(own, got, ctx_place, 2), ffn_part, ffn_got)
    ffn_got = xor_send(ffn_part, 4)

    def attn_by_wt(*parts):
        return split_wt(add_low(*parts), wt_bits[0])

    attn_kept, attn_sent = step(attn_by_wt, attn_half[0], *attn_got)
    attn_got = xor_wt(attn_sent, wt_bits[0])
    layer_out = step(
        lambda hidden, own, got: low(hidden + own + wide(got) + bias_proj).reshape(batches, rows_here, width),
        hidden, down_out, down_other,
    )
    for bit in wt_bits[1:]:
        attn_kept, attn_sent = step(next_wt(bit), attn_kept, attn_got)
        attn_got = xor_wt(attn_sent, bit)
    ffn_part = step(lambda own, got: both(own, got, ctx_place, 4), ffn_part, ffn_got)
    ffn_got = xor_send(ffn_part, 1)
    attn_part = step(lambda *parts: add_low(*parts)[0], attn_kept, attn_got)
    attn_got = send_chips(attn_part)

    ffn_new = step(
        lambda own, got, *arrays: ffn_update(shard_rows, FF, ctx_count, chunk)(
            both(own, got, ctx_place, 1, 2).reshape(ctx_count, 2, shard_rows, chunk), *arrays
        ),
        ffn_part, ffn_got, ffn_master, ffn_mom, ffn_sq,
    )
    attn_even = step(lambda *parts: jnp.stack(parts), attn_part, *attn_got)
    attn_odd = xor_send(attn_even, 1)
    small_total = in_order(attn_even[..., attn_columns:], attn_odd[..., attn_columns:])
    small_total = wide(small_total.reshape(-1))
    most = small_size - FF - HS
    small_total = jnp.concatenate(
        [small_total[:most], small_total[most + HS : most + 2 * HS], small_total[most + 2 * HS : most + 2 * HS + FF]]
    )
    small_new = adam_update(small_master, small_total, small_mom, small_sq, 1.0, 0.0)
    attn_new = attn_update(shard_rows, attn_columns, width, ctx_count, piece_rows)(
        place, attn_even, attn_odd, attn_master, attn_mom, attn_sq
    )
    return (layer_out, input_grad) + tuple(attn_new) + tuple(ffn_new) + tuple(small_new)


def shift_wt(array, shift):
    count = lax.axis_size("wt")
    return lax.ppermute(array, "wt", [(i, (i + shift) % count) for i in range(count)])


def whole_wt(piece, axis):
    count, place = lax.axis_size("wt"), lax.axis_index("wt")
    shape = list(piece.shape)
    shape[axis] *= count
    buffer = put(jnp.zeros(shape, piece.dtype), piece, place, axis)
    for shift in range(1, count):
        buffer = put(buffer, shift_wt(piece, shift), (place - shift) % count, axis)
    return buffer


def whole_ctx(piece):
    count = lax.axis_size("ctx")
    got = {0: piece}
    for mask in range(2, count, 2):
        got[mask] = xor_send(piece, mask)
    for mask in range(0, count, 2):
        got[mask + 1] = xor_send(got[mask], 1)
    return [got[mask] for mask in range(count)]


def sum_ctx(pieces):
    count = lax.axis_size("ctx")
    half = {}
    for mask in range(count - 2, -1, -2):
        other = xor_send(pieces[mask + 1], 1)
        half[mask] = low(wide(pieces[mask]) + wide(other))
    total = wide(half[0])
    for mask in range(2, count, 2):
        total = total + wide(xor_send(half[mask], mask))
    return total


def sum_wt(array, axis):
    count, place = lax.axis_size("wt"), lax.axis_index("wt")
    size = array.shape[axis] // count
    total = wide(take(array, place, axis, size))
    for shift in range(1, count):
        sent = take(array, (place + shift) % count, axis, size)
        total = total + wide(shift_wt(sent, shift))
    return total


def any_shards(
    tokens,
    doc_starts,
    attn_master,
    attn_mom,
    attn_sq,
    ffn_master,
    ffn_mom,
    ffn_sq,
    small_master,
    small_mom,
    small_sq,
    cotangent,
):
    ctx_count = lax.axis_size("ctx")
    ctx_place = lax.axis_index("ctx")
    wt_count = lax.axis_size("wt")
    batches, rows_here, width = tokens.shape
    heads = width // HS
    qkv_cols = width + 2 * HS
    all_rows = batches * rows_here
    shard_rows = attn_master.shape[0]
    piece_rows = shard_rows // ctx_count
    chunk = FF // ctx_count
    order = ctx_place ^ jnp.arange(ctx_count, dtype=jnp.int32)
    (
        gain_one,
        shift_one,
        gain_two,
        shift_two,
        bias_query,
        bias_out,
        bias_proj,
        bias_value,
        bias_hidden,
    ) = split_small(small_master)

    attn_piece = low(take(attn_master, ctx_place, 0, piece_rows))

    def whole_rows(piece):
        parts = whole_ctx(whole_wt(piece[None], 0))
        buffer = jnp.zeros((wt_count, ctx_count) + piece.shape, piece.dtype)
        for k, part in enumerate(parts):
            buffer = put(buffer, part[:, None], ctx_place ^ k, 1)
        return buffer.reshape((width,) + piece.shape[1:])

    weight_qkv = whole_rows(attn_piece[:, :qkv_cols])
    weight_out = whole_rows(attn_piece[:, qkv_cols:])
    ffn_piece = low(jnp.swapaxes(take(ffn_master, ctx_place, 2, chunk), 0, 1))
    ffn_parts = whole_ctx(whole_wt(ffn_piece, 1))
    bias_parts = bias_hidden.reshape(ctx_count, chunk)[order]

    stream = wide(tokens.reshape(all_rows, width))
    normed, norm_back_one = jax.vjp(layer_norm, stream, gain_one, shift_one)
    normed_low = low(normed)
    mixed = dot(normed_low, weight_qkv)
    queries = low(mixed[:, :width] + bias_query)
    kv_local = low(
        mixed[:, width:] + jnp.concatenate([jnp.zeros((HS,), jnp.float32), bias_value])
    ).reshape(batches, rows_here, 2 * HS)
    kv_parts = jnp.stack(whole_ctx(kv_local), axis=1).reshape(
        batches, ctx_count * rows_here, 2 * HS
    )
    keys_all, values_all = kv_parts[..., :HS], kv_parts[..., HS:]
    local_pos = jnp.arange(rows_here, dtype=jnp.int32)
    query_pos = ctx_place * rows_here + local_pos
    key_pos = (order[:, None] * rows_here + local_pos[None, :]).reshape(-1)
    queries = queries.reshape(batches, rows_here * heads, HS)
    scale = HS ** (-0.5)
    attended_list, log_list, allowed_list = [], [], []
    for b in range(batches):
        starts = doc_starts[b]
        query_doc = jnp.sum((starts[None, :] <= query_pos[:, None]).astype(jnp.int32), axis=1)
        key_doc = jnp.sum((starts[None, :] <= key_pos[:, None]).astype(jnp.int32), axis=1)
        allowed = (query_doc[:, None] == key_doc[None, :]) & (key_pos[None, :] <= query_pos[:, None])
        allowed = jnp.repeat(allowed, heads, axis=0)
        allowed_list.append(allowed)
        scores = jnp.where(allowed, cols_dot(queries[b], keys_all[b]) * scale, -1e30)
        peak = jnp.max(scores, axis=-1, keepdims=True)
        expo = jnp.exp(scores - peak)
        total = jnp.sum(expo, axis=-1, keepdims=True)
        attended_list.append(dot(low(expo / total), values_all[b]))
        log_list.append(peak + jnp.log(total))
    attended = jnp.stack(attended_list)
    attended_low = low(attended).reshape(all_rows, width)
    hidden = stream + dot(attended_low, weight_out) + bias_out
    normed_two, norm_back_two = jax.vjp(layer_norm, hidden, gain_two, shift_two)
    normed_two_low = low(normed_two)

    back_low = cotangent.reshape(all_rows, width)
    back_rows = wide(back_low)
    down_vals = jnp.zeros((all_rows, width), jnp.float32)
    grad_normed_two = jnp.zeros((all_rows, width), jnp.float32)
    ffn_grads, hidden_grads = [], []
    for k in range(ctx_count):
        weight_up, weight_down = ffn_parts[k][0], ffn_parts[k][1]
        value, slope = gelu_both(dot(normed_two_low, weight_up) + bias_parts[k])
        act = low(value)
        down_vals = down_vals + cols_dot(act, weight_down)
        grad_up = low(dot(back_low, weight_down) * slope)
        hidden_grads.append(jnp.sum(wide(grad_up), axis=0))
        grad_normed_two = grad_normed_two + cols_dot(grad_up, weight_up)
        ffn_grads.append(
            jnp.stack([low(rows_dot(normed_two_low, grad_up)), low(rows_dot(back_low, act))])
        )
    layer_out = low(hidden + down_vals + bias_proj).reshape(batches, rows_here, width)
    grad_bias_proj = jnp.sum(back_rows, axis=0)
    grad_bias_hidden = jnp.stack(hidden_grads)[order].reshape(FF)
    ffn_part = low(sum_wt(low(sum_ctx(ffn_grads)), 1))

    grad_hidden_part, grad_gain_two, grad_shift_two = norm_back_two(grad_normed_two)
    grad_hidden = back_rows + grad_hidden_part
    grad_bias_out = jnp.sum(grad_hidden, axis=0)
    grad_hidden_low = low(grad_hidden)
    grad_out = rows_dot(attended_low, grad_hidden_low)

    def summed_rows(grad):
        blocks = low(grad).reshape(wt_count, ctx_count, piece_rows, grad.shape[1])
        pieces = [take(blocks, ctx_place ^ k, 1, 1)[:, 0] for k in range(ctx_count)]
        part = low(sum_wt(low(sum_ctx(pieces)), 0)[0])
        buffer = jnp.zeros((ctx_count,) + part.shape, part.dtype)
        for k, got in enumerate(whole_ctx(part)):
            buffer = put(buffer, got[None], ctx_place ^ k, 0)
        return wide(buffer.reshape(shard_rows, grad.shape[1]))

    out_total = summed_rows(grad_out)

    grad_attended = low(cols_dot(grad_hidden_low, weight_out)).reshape(
        batches, rows_here * heads, HS
    )
    grad_query_list, grad_kv_list = [], []
    for b in range(batches):
        grads = grad_attended[b]
        delta = jnp.sum(wide(grads) * attended[b], axis=-1, keepdims=True)
        scores = jnp.where(allowed_list[b], cols_dot(queries[b], keys_all[b]) * scale, -1e30)
        weights = jnp.exp(scores - log_list[b])
        grad_scores = low(weights * (cols_dot(grads, values_all[b]) - delta))
        grad_query_list.append(low(dot(grad_scores, keys_all[b]) * scale))
        grad_kv_list.append(
            jnp.concatenate(
                [
                    low(rows_dot(grad_scores, queries[b]) * scale),
                    low(rows_dot(low(weights), grads)),
                ],
                axis=1,
            )
        )
    grad_query = jnp.stack(grad_query_list).reshape(all_rows, width)
    grad_kv = jnp.stack(grad_kv_list).reshape(batches, ctx_count, rows_here, 2 * HS)
    grad_kv_low = low(sum_ctx([grad_kv[:, k] for k in range(ctx_count)])).reshape(
        all_rows, 2 * HS
    )
    grad_bias_query = jnp.sum(wide(grad_query), axis=0)
    grad_bias_value = jnp.sum(wide(grad_kv_low[:, HS:]), axis=0)
    grad_mixed = jnp.concatenate([grad_query, grad_kv_low], axis=1)
    qkv_total = summed_rows(rows_dot(normed_low, grad_mixed))
    grad_normed = cols_dot(grad_mixed, weight_qkv)
    grad_stream_part, grad_gain_one, grad_shift_one = norm_back_one(grad_normed)
    input_grad = (grad_hidden + grad_stream_part).reshape(batches, rows_here, width)

    ffn_buffer = jnp.zeros((ctx_count,) + ffn_part.shape, ffn_part.dtype)
    for k, got in enumerate(whole_ctx(ffn_part)):
        ffn_buffer = put(ffn_buffer, got[None], ctx_place ^ k, 0)
    ffn_total = wide(jnp.transpose(ffn_buffer, (2, 1, 0, 3)).reshape(shard_rows, 2, FF))
    attn_total = jnp.concatenate([qkv_total, out_total], axis=1)
    grad_small = jnp.concatenate(
        [
            grad_gain_one,
            grad_shift_one,
            grad_gain_two,
            grad_shift_two,
            grad_bias_query,
            grad_bias_out,
            grad_bias_proj,
            grad_bias_value,
            grad_bias_hidden,
        ]
    )
    small_total = lax.psum(grad_small, ("ctx", "wt"))
    attn_new = adam_update(attn_master, attn_total, attn_mom, attn_sq, 0.1, 0.1)
    ffn_new = adam_update(ffn_master, ffn_total, ffn_mom, ffn_sq, 0.1, 0.1)
    small_new = adam_update(small_master, small_total, small_mom, small_sq, 1.0, 0.0)
    return (layer_out, input_grad) + attn_new + ffn_new + small_new


def solution(mesh):
    rows, cube = P("wt", None), P("wt", None, None)
    flow = P("wt", "ctx", None)
    in_specs = (flow, rows, rows, rows, rows, cube, cube, cube, P(), P(), P(), flow)
    out_specs = (flow, flow, rows, rows, rows, cube, cube, cube, P(), P(), P())
    ctx_count, wt_count = mesh.shape["ctx"], mesh.shape["wt"]
    fitted = ctx_count == 8 and wt_count % 2 == 0 and D // wt_count % (4 * ctx_count) == 0
    body = shards if fitted else any_shards
    return jax.shard_map(body, mesh=mesh, in_specs=in_specs, out_specs=out_specs, check_vma=False)
```

```python
import jax
import jax.numpy as jnp
from jax import lax
from jax.experimental import pallas as pl
from jax.experimental.pallas import tpu as pltpu
from jax.sharding import PartitionSpec as P

D = 768
HS = 64
FF = 3072
STEP = 10


NORM_EPS = 1e-05
GELU_COEF = 0.7978845608028654
GELU_CUBE = 0.044715
BETA_ONE = 0.9
BETA_TWO = 0.95
ADAM_EPS = 1e-08
VMEM_LIMIT = 56 << 20
NO_COST = pl.CostEstimate(flops=0, bytes_accessed=0, transcendentals=0)


def layer_norm(values, gain, shift):
    centre = values - jnp.mean(values, axis=-1, keepdims=True)
    spread = jnp.mean(centre * centre, axis=-1, keepdims=True)
    return centre * lax.rsqrt(spread + NORM_EPS) * gain + shift


def gelu_both(u):
    square = u * u
    share = 0.5 * jnp.tanh(u * (GELU_COEF * GELU_CUBE * square + GELU_COEF)) + 0.5
    bend = u * (6.0 * GELU_COEF * GELU_CUBE * square + 2.0 * GELU_COEF)
    return u * share, share * ((1.0 - share) * bend) + share


def split_small(small):
    return (
        small[0:D],
        small[D : 2 * D],
        small[2 * D : 3 * D],
        small[3 * D : 4 * D],
        small[4 * D : 5 * D],
        small[5 * D : 6 * D],
        small[6 * D : 7 * D],
        small[7 * D : 7 * D + HS],
        small[7 * D + HS :],
    )


def rows_dot(left, right):
    return lax.dot_general(
        left, right, (((0,), (0,)), ((), ())), preferred_element_type=jnp.float32
    )


def cols_dot(left, right):
    return lax.dot_general(
        left, right, (((1,), (1,)), ((), ())), preferred_element_type=jnp.float32
    )


def dot(left, right):
    return jnp.dot(left, right, preferred_element_type=jnp.float32)


def low(values):
    return values.astype(jnp.bfloat16)


def wide(values):
    return values.astype(jnp.float32)


def adam_update(master, gradient, first, second, step_rate, decay_rate):
    first_new = BETA_ONE * first + (1.0 - BETA_ONE) * gradient
    second_new = BETA_TWO * second + (1.0 - BETA_TWO) * gradient * gradient
    first_hat = first_new / (1.0 - BETA_ONE**STEP)
    second_hat = second_new / (1.0 - BETA_TWO**STEP)
    master_new = master - step_rate * (
        first_hat / (jnp.sqrt(second_hat) + ADAM_EPS) + decay_rate * master
    )
    return (first_new, second_new, master_new)


def xor_send(array, mask):
    count = lax.axis_size("ctx")
    return lax.ppermute(array, "ctx", [(i, i ^ mask) for i in range(count)])


def xor_wt(array, mask):
    count = lax.axis_size("wt")
    return lax.ppermute(array, "wt", [(i, i ^ mask) for i in range(count)])


class Steps:
    def __init__(self):
        self.last = ()

    def __call__(self, function, *args):
        flat, tree = jax.tree.flatten(args)
        held = lax.optimization_barrier(tuple(flat) + self.last)[: len(flat)]
        result = function(*jax.tree.unflatten(tree, held))
        self.last = tuple(jax.tree.leaves(result))
        return result


def loop(count, body, carry=0):
    return lax.fori_loop(0, count, body, carry)


def rows_at(i, size):
    return pl.ds(pl.multiple_of(i * size, size), size)


def put(buffer, piece, place, axis):
    starts = [0] * buffer.ndim
    starts[axis] = place * piece.shape[axis]
    return lax.dynamic_update_slice(buffer, piece, starts)


def take(buffer, place, axis, size):
    return lax.dynamic_slice_in_dim(buffer, place * size, size, axis)


def attention_kernels(batches, rows, width, parts, runs):
    half_parts = parts // 2
    keys = parts * rows
    pair = 2 * HS
    groups = width // (2 * pair)
    factor = HS ** (-0.5) * 1.4426950408889634
    tile = 32

    def lanes(shape):
        return lax.broadcasted_iota(jnp.int32, shape, 1)

    def spread(even_ref, odd_ref, key_ref, value_ref):
        for odd, ref in enumerate((even_ref, odd_ref)):

            def block(j, carry):
                block = wide(ref[j, 0])
                turned = pltpu.roll(block, HS, 1)
                first = lanes(block.shape) < HS
                here = rows_at(odd * half_parts + j, rows)
                key_ref[0, here, :] = low(jnp.where(first, block, 0.0))
                key_ref[1, here, :] = low(jnp.where(first, 0.0, turned))
                value_ref[0, here, :] = low(jnp.where(first, turned, 0.0))
                value_ref[1, here, :] = low(jnp.where(first, 0.0, block))
                return carry

            loop(half_parts, block)

    def mask_of(j):
        return jnp.where(j < half_parts, 2 * j, 2 * (j - half_parts) + 1)

    def doc_begin(starts_ref, stream, positions):
        begin = jnp.zeros_like(positions)
        for j in range(starts_ref.shape[1]):
            start = starts_ref[stream, j]
            begin = jnp.where(start <= positions, jnp.maximum(begin, start), begin)
        return begin

    def forward(starts_ref, place_ref, query_ref, even_ref, odd_ref, low_ref, full_ref, log_ref, cap, key, value, weight):
        stream, place = pl.program_id(0), place_ref[0]
        spread(even_ref, odd_ref, key, value)
        query_pos = place * rows + lax.broadcasted_iota(jnp.int32, (rows, 1), 0)
        begin = doc_begin(starts_ref, stream, query_pos)

        def limit(j, carry):
            key_pos = (place ^ mask_of(j)) * rows + lax.broadcasted_iota(jnp.int32, (rows, rows), 1)
            allowed = (key_pos >= begin) & (key_pos <= query_pos)
            cap[:, rows_at(j, rows)] = jnp.where(allowed, 3.0e38, -1e30)
            return carry

        loop(parts, limit)
        log_ref[...] = jnp.zeros_like(log_ref)
        column = lanes((tile, pair))

        def group(g, carry):
            at, more = rows_at(2 * g, pair), rows_at(2 * g + 1, pair)
            two = jnp.concatenate([query_ref[0, :, at], query_ref[0, :, more]], axis=0)
            totals = []
            for half in range(2):
                scores = cols_dot(two, key[half])
                norms = []
                for t in range(2 * rows // tile):
                    own = slice(t * tile, (t + 1) * tile)
                    here = slice(t % (rows // tile) * tile, (t % (rows // tile) + 1) * tile)
                    part = jnp.minimum(scores[own] * factor, cap[here, :])
                    peak = jnp.max(part, axis=1, keepdims=True)
                    expo = jnp.exp2(part - peak)
                    norm = jnp.sum(expo, axis=1, keepdims=True)
                    weight[half, own, :] = low(expo)
                    norms.append(norm)
                    head = 4 * g + 2 * (t * tile // rows) + half
                    log_ref[0, here, :] = jnp.where(column == head, peak + jnp.log2(norm), log_ref[0, here, :])
                totals.append(dot(weight[half], value[half]) / jnp.concatenate(norms, axis=0))
            total = totals[0] + totals[1]
            for j, lane in enumerate((at, more)):
                part = total[j * rows : (j + 1) * rows]
                full_ref[0, :, lane] = part
                low_ref[0, :, lane] = low(part)
            return carry

        loop(groups, group)

    def backward(
        starts_ref, place_ref, query_ref, even_ref, odd_ref, full_ref, log_ref, grad_ref,
        query_grad_ref, even_grad_ref, odd_grad_ref,
        cap, key, value, key_turned, log_rows, delta_rows, weight_buf, score_buf, query_buf, grad_buf, turned_buf,
    ):
        stream, place = pl.program_id(0) + place_ref[1], place_ref[0]
        spread(even_ref, odd_ref, key, value)
        query_pos = place * rows + lax.broadcasted_iota(jnp.int32, (1, rows), 1)
        begin = doc_begin(starts_ref, stream, query_pos)

        def limit(j, carry):
            key_pos = (place ^ mask_of(j)) * rows + lax.broadcasted_iota(jnp.int32, (rows, rows), 0)
            allowed = (key_pos >= begin) & (key_pos <= query_pos)
            here = rows_at(j, rows)
            cap[here, :] = jnp.where(allowed, 3.0e38, -1e30)
            key_turned[:, here] = low(wide(key[0, here, :]).T[:HS])
            return carry

        loop(parts, limit)
        log_rows[...] = log_ref[0].T[: log_rows.shape[0]]
        head_of = lax.broadcasted_iota(jnp.int32, (delta_rows.shape[0], width), 1) // HS
        chosen = (head_of == lax.broadcasted_iota(jnp.int32, (delta_rows.shape[0], width), 0)).astype(jnp.float32)
        delta_rows[...] = lax.dot_general(
            chosen, wide(grad_ref[0]) * full_ref[0], (((1,), (1,)), ((), ())),
            precision=lax.Precision.HIGHEST, preferred_element_type=jnp.float32,
        )
        first = lanes((2 * rows, pair)) < HS
        part_rows = 256

        def group(i, carry):
            g, half = i // 2, i % 2
            at, more = rows_at(2 * g, pair), rows_at(2 * g + 1, pair)
            two = jnp.concatenate([query_ref[0, :, at], query_ref[0, :, more]], axis=0)
            two_grad = jnp.concatenate([grad_ref[0, :, at], grad_ref[0, :, more]], axis=0)
            span = rows_at(i, 2 * rows)
            keep = first == (half == 0)
            query_buf[span, :] = low(jnp.where(keep, wide(two), 0.0))
            grad_buf[span, :] = low(jnp.where(keep, wide(two_grad), 0.0))
            h = 4 * g + half
            log = jnp.concatenate([log_rows[pl.ds(h, 1), :], log_rows[pl.ds(h + 2, 1), :]], axis=1)
            delta = jnp.concatenate([delta_rows[pl.ds(h, 1), :], delta_rows[pl.ds(h + 2, 1), :]], axis=1)

            def part(t, carry):
                here = rows_at(t, part_rows)
                scores, weight_grads = cols_dot(key[half, here, :], two), cols_dot(value[half, here, :], two_grad)
                limit = cap[here, :]
                limit = jnp.concatenate([limit, limit], axis=1)
                weights = jnp.exp2(jnp.minimum(scores * factor, limit) - log)
                weight_buf[here, span] = low(weights)
                score_buf[here, span] = low(weights * (weight_grads - delta))
                return carry

            loop(keys // part_rows, part)
            turned_buf[g, pl.ds(pl.multiple_of(half * HS, HS), HS), :] = dot(key_turned[...], score_buf[:, span])
            return carry

        loop(2 * groups, group)

        def turn_back(g, carry):
            turned = turned_buf[g] * HS ** (-0.5)
            query_grad_ref[0, :, rows_at(2 * g, pair)] = low(turned[:, :rows].T)
            query_grad_ref[0, :, rows_at(2 * g + 1, pair)] = low(turned[:, rows:].T)
            return carry

        loop(groups, turn_back)
        for odd, ref in enumerate((even_grad_ref, odd_grad_ref)):

            def key_side(j, carry):
                here = rows_at(odd * half_parts // 2 + j, 2 * rows)
                value_sum = dot(weight_buf[here, :], grad_buf[...])
                key_sum = dot(score_buf[here, :], query_buf[...]) * HS ** (-0.5)
                value_sum = value_sum + pltpu.roll(value_sum, HS, 1)
                key_sum = key_sum + pltpu.roll(key_sum, HS, 1)
                both = low(jnp.where(lanes((2 * rows, pair)) < HS, key_sum, value_sum))
                ref[2 * j, 0] = both[:rows]
                ref[2 * j + 1, 0] = both[rows:]
                return carry

            loop(half_parts // 2, key_side)

    def specs(first):
        return (
            pl.BlockSpec((1, rows, width), lambda b, *_: (b + first, 0, 0)),
            pl.BlockSpec((1, rows, pair), lambda b, *_: (b + first, 0, 0)),
            pl.BlockSpec((half_parts, 1, rows, pair), lambda b, *_: (0, b + first, 0, 0)),
        )

    flow, logs, blocks = specs(0)

    shared = [
        pltpu.VMEM((2, keys, pair), jnp.bfloat16),
        pltpu.VMEM((2, keys, pair), jnp.bfloat16),
    ]
    run_forward = pl.pallas_call(
        forward,
        grid_spec=pltpu.PrefetchScalarGridSpec(
            num_scalar_prefetch=2,
            grid=(batches,),
            in_specs=[flow, blocks, blocks],
            out_specs=[flow, flow, logs],
            scratch_shapes=[pltpu.VMEM((rows, keys), jnp.float32)]
            + shared
            + [pltpu.VMEM((2, 2 * rows, keys), jnp.bfloat16)],
        ),
        out_shape=[
            jax.ShapeDtypeStruct((batches, rows, width), jnp.bfloat16),
            jax.ShapeDtypeStruct((batches, rows, width), jnp.float32),
            jax.ShapeDtypeStruct((batches, rows, pair), jnp.float32),
        ],
        compiler_params=pltpu.CompilerParams(vmem_limit_bytes=VMEM_LIMIT),
        cost_estimate=NO_COST,
        name="attention_forward",
    )
    head_rows = -(-(width // HS) // 8) * 8
    all_columns = rows * (width // HS)
    count = batches // runs

    def call_backward(run):
        here_flow, here_logs, here_blocks = specs(run * count)
        return pl.pallas_call(
        backward,
        grid_spec=pltpu.PrefetchScalarGridSpec(
            num_scalar_prefetch=2,
            grid=(count,),
            in_specs=[here_flow, here_blocks, here_blocks, here_flow, here_logs, here_flow],
            out_specs=[flow, blocks, blocks],
            scratch_shapes=[pltpu.VMEM((keys, rows), jnp.float32)]
            + shared
            + [
                pltpu.VMEM((HS, keys), jnp.bfloat16),
                pltpu.VMEM((head_rows, rows), jnp.float32),
                pltpu.VMEM((head_rows, rows), jnp.float32),
                pltpu.VMEM((keys, all_columns), jnp.bfloat16),
                pltpu.VMEM((keys, all_columns), jnp.bfloat16),
                pltpu.VMEM((all_columns, pair), jnp.bfloat16),
                pltpu.VMEM((all_columns, pair), jnp.bfloat16),
                pltpu.VMEM((groups, pair, 2 * rows), jnp.float32),
            ],
        ),
        out_shape=[
            jax.ShapeDtypeStruct((count, rows, width), jnp.bfloat16),
            jax.ShapeDtypeStruct((half_parts, count, rows, pair), jnp.bfloat16),
            jax.ShapeDtypeStruct((half_parts, count, rows, pair), jnp.bfloat16),
        ],
        compiler_params=pltpu.CompilerParams(vmem_limit_bytes=VMEM_LIMIT),
        cost_estimate=NO_COST,
        name="attention_backward",
    )

    return run_forward, [call_backward(run) for run in range(runs)]


def in_hbm(arrays):
    return [pltpu.with_memory_space_constraint(array, pltpu.HBM) for array in arrays]


def ffn_kernels(rows, width, chunk, wt_count):
    units = 2 * chunk
    all_rows = 2 * rows
    block_rows = width // wt_count
    hbm = pl.BlockSpec(memory_space=pltpu.HBM)
    vmem = pl.BlockSpec(memory_space=pltpu.VMEM)
    params = pltpu.CompilerParams(vmem_limit_bytes=VMEM_LIMIT)

    def fetch(weights, which, held, sem):
        copies = []
        for n, arrays in enumerate(weights):
            blocks = [array.at[block] for array in arrays for block in range(array.shape[0])]
            for row, block in enumerate(blocks):
                copies.append(
                    pltpu.make_async_copy(
                        block.at[pl.ds(which * block_rows, block_rows), :],
                        held.at[pl.ds(row * block_rows, block_rows), pl.ds(n * chunk, chunk)],
                        sem.at[len(copies)],
                    )
                )
        for copy in copies:
            copy.start()
        return copies

    def send(pairs, sems):
        copies = [pltpu.make_async_copy(source, out, sems.at[n]) for n, (source, out) in enumerate(pairs)]
        for copy in copies:
            copy.start()
        return copies

    part_rows = 256
    tile = 16

    def units_of(inputs, grads, bias, held_up, held_down, act, grad_units):
        sums = jnp.zeros((8, units), jnp.float32)
        for s in range(2):

            def part(i, sums):
                here = rows_at(i, part_rows)
                up = dot(inputs[s][here, :], held_up[...])
                act_grad = dot(grads[s][here, :], held_down[...])
                for t in range(part_rows // tile):
                    own = slice(t * tile, (t + 1) * tile)
                    there = pl.ds(pl.multiple_of(s * rows + i * part_rows + t * tile, tile), tile)
                    value, slope = gelu_both(up[own] + bias)
                    grad = act_grad[own] * slope
                    act[there, :] = low(value)
                    grad_units[there, :] = low(grad)
                    sums = sums + (grad[:8] + grad[8:])
                return sums

            sums = loop(rows // part_rows, part, sums)
        return jnp.sum(sums, axis=0, keepdims=True)

    def product_of(turned, right, product):
        def part(i, carry):
            here = rows_at(i, part_rows)
            product[here, :] = low(dot(turned[here, :], right[...]))
            return carry

        loop(width // part_rows, part)

    def back_to(refs, sources, weights):
        for s, ref in enumerate(refs):

            def part(i, carry):
                here = pl.ds(pl.multiple_of(s * rows + i * part_rows, part_rows), part_rows)
                total = cols_dot(sources[0][here, :], weights[0][...]) + cols_dot(sources[1][here, :], weights[1][...])
                ref[rows_at(i, part_rows), :] = total.astype(ref.dtype)
                return carry

            loop(rows // part_rows, part)

    def halves(product, m):
        cols = pl.ds(m * chunk, chunk)
        return [product.at[pl.ds(h * width // 2, width // 2), cols] for h in range(2)]

    def first(
        own, other, grad_own, grad_other, turned, bias, w0, w1,
        act_out, units_out, out_a, out_b, sums_out,
        held_up, held_down, act, grad_units, product, sems, out_sems,
    ):
        weights = ((w0,), (w1,))
        copies = fetch(weights, 0, held_up, sems.at[0]) + fetch(weights, 1, held_down, sems.at[1])
        for copy in copies:
            copy.wait()
        sums_out[...] = units_of((own, other), (grad_own, grad_other), bias[...], held_up, held_down, act, grad_units)
        sent = send(((act, act_out), (grad_units, units_out)), out_sems.at[0])
        product_of(turned, act, product)
        sent += send(
            ((product.at[:, pl.ds(0, chunk)], out_a), (product.at[:, pl.ds(chunk, chunk)], out_b)), out_sems.at[1]
        )
        for copy in sent:
            copy.wait()

    def second(
        own, other, grad_own, grad_other, turned, bias, units_first, w0, w1, w2, w3, w4,
        act_out, units_out, out_a, out_b, out_c, sums_out, back_own, back_other,
        held_up, held_more, held_down, act, grad_units, more_units, product, sems, out_sems, more_sem,
    ):
        weights, before = ((w2,), (w3, w4)), ((w0,), (w1,))
        copies = fetch(weights, 0, held_up, sems.at[0]) + fetch(weights, 1, held_down, sems.at[1])
        more = fetch(before, 0, held_more, sems.at[2])
        more.append(pltpu.make_async_copy(units_first, more_units, more_sem))
        more[-1].start()
        for copy in copies:
            copy.wait()
        sums_out[...] = units_of((own, other), (grad_own, grad_other), bias[...], held_up, held_down, act, grad_units)
        sent = send(((act, act_out), (grad_units, units_out)), out_sems.at[0])
        product_of(turned, act, product)
        top, bottom = halves(product, 1)
        sent += send(((product.at[:, pl.ds(0, chunk)], out_a), (top, out_b), (bottom, out_c)), out_sems.at[1])
        for copy in more:
            copy.wait()
        back_to((back_own, back_other), (grad_units, more_units), (held_up, held_more))
        for copy in sent:
            copy.wait()

    def third(own, other, units_a, units_b, out_0, out_1, out_2, out_3, out_4, turned, held, products, sems, out_sems):
        copies = send(((units_a, held.at[0]), (units_b, held.at[1])), sems)
        turn((own, other), turned)
        for copy in copies:
            copy.wait()
        product_of(turned, held.at[1], products.at[1])
        top, bottom = halves(products.at[1], 1)
        sent = send(((products.at[1, :, pl.ds(0, chunk)], out_2), (top, out_3), (bottom, out_4)), out_sems.at[0])
        product_of(turned, held.at[0], products.at[0])
        sent += send(
            ((products.at[0, :, pl.ds(0, chunk)], out_0), (products.at[0, :, pl.ds(chunk, chunk)], out_1)),
            out_sems.at[1],
        )
        for copy in sent:
            copy.wait()

    def down(act_a, act_b, w0, w1, w2, w3, w4, own_ref, other_ref, held_a, held_b, sems):
        copies = fetch(((w0,), (w1,)), 1, held_a, sems.at[0]) + fetch(((w2,), (w3, w4)), 1, held_b, sems.at[1])
        for copy in copies:
            copy.wait()
        back_to((own_ref, other_ref), (act_a, act_b), (held_a, held_b))

    dma = pltpu.SemaphoreType.DMA
    held = pltpu.VMEM((width, units), jnp.bfloat16)
    flow = pltpu.VMEM((all_rows, units), jnp.bfloat16)
    flow_out = pltpu.HBM((all_rows, units), jnp.bfloat16)
    whole = pltpu.HBM((width, chunk), jnp.bfloat16)
    part = pltpu.HBM((width // 2, chunk), jnp.bfloat16)
    sums = jax.ShapeDtypeStruct((1, units), jnp.float32)
    own = jax.ShapeDtypeStruct((rows, width), jnp.float32)
    other = jax.ShapeDtypeStruct((rows, width), jnp.bfloat16)
    run_first = pl.pallas_call(
        first,
        in_specs=[vmem] * 6 + [hbm] * 2,
        out_specs=[hbm] * 4 + [vmem],
        out_shape=[flow_out, flow_out, whole, whole, sums],
        scratch_shapes=[held, held, flow, flow, held, dma((2, 2 * wt_count)), dma((2, 2))],
        compiler_params=params,
        cost_estimate=NO_COST,
        name="ffn_first",
    )
    run_second = pl.pallas_call(
        second,
        in_specs=[vmem] * 6 + [hbm] * 6,
        out_specs=[hbm] * 5 + [vmem] * 3,
        out_shape=[flow_out, flow_out, whole, part, part, sums, own, other],
        scratch_shapes=[held, held, held, flow, flow, flow, held, dma((3, 2 * wt_count)), dma((2, 3)), dma(())],
        compiler_params=params,
        cost_estimate=NO_COST,
        name="ffn_second",
    )
    run_third = pl.pallas_call(
        third,
        in_specs=[vmem] * 2 + [hbm] * 2,
        out_specs=[hbm] * 5,
        out_shape=[whole, whole, whole, part, part],
        scratch_shapes=[
            pltpu.VMEM((width, all_rows), jnp.bfloat16),
            pltpu.VMEM((2, all_rows, units), jnp.bfloat16),
            pltpu.VMEM((2, width, units), jnp.bfloat16),
            dma((2,)),
            dma((2, 3)),
        ],
        compiler_params=params,
        cost_estimate=NO_COST,
        name="ffn_grads",
    )
    run_down = pl.pallas_call(
        down,
        in_specs=[vmem] * 2 + [hbm] * 5,
        out_specs=[vmem] * 2,
        out_shape=[own, other],
        scratch_shapes=[held, held, dma((2, 2 * wt_count))],
        compiler_params=params,
        cost_estimate=NO_COST,
        name="ffn_down",
    )
    return run_first, run_second, run_third, run_down


def turn(refs, turned):
    rows = refs[0].shape[0]
    for s, ref in enumerate(refs):

        def block(i, carry):
            turned[:, rows_at(s * (rows // 128) + i, 128)] = low(wide(ref[rows_at(i, 128), :]).T)
            return carry

        loop(rows // 128, block)


def turn_both(own, other):
    vmem = pl.BlockSpec(memory_space=pltpu.VMEM)
    rows, width = own.shape
    return pl.pallas_call(
        lambda a, b, out: turn((a, b), out),
        in_specs=[vmem] * 2,
        out_specs=vmem,
        out_shape=jax.ShapeDtypeStruct((width, 2 * rows), own.dtype),
        compiler_params=pltpu.CompilerParams(vmem_limit_bytes=VMEM_LIMIT),
        cost_estimate=NO_COST,
        name="turn",
    )(own, other)


def out_projection(rows, width):
    tile = 128

    def kernel(attended, weight, stream, bias, gain, shift, hidden_ref, normed_ref):
        def part(i, carry):
            here = rows_at(i, tile)
            hidden = wide(stream[here, :]) + dot(attended[here, :], weight[...]) + bias[...]
            hidden_ref[here, :] = hidden
            normed_ref[here, :] = low(layer_norm(hidden, gain[...], shift[...]))
            return carry

        loop(rows // tile, part)

    vmem = pl.BlockSpec(memory_space=pltpu.VMEM)
    return pl.pallas_call(
        kernel,
        in_specs=[vmem] * 6,
        out_specs=[vmem] * 2,
        out_shape=[
            jax.ShapeDtypeStruct((rows, width), jnp.float32),
            jax.ShapeDtypeStruct((rows, width), jnp.bfloat16),
        ],
        compiler_params=pltpu.CompilerParams(vmem_limit_bytes=VMEM_LIMIT),
        cost_estimate=NO_COST,
        name="out_projection",
    )


def norm_back(values, gain, grad):
    centre = values - jnp.mean(values, axis=-1, keepdims=True)
    scale = lax.rsqrt(jnp.mean(centre * centre, axis=-1, keepdims=True) + NORM_EPS)
    unit = centre * scale
    inner = grad * gain
    mean = jnp.mean(inner, axis=-1, keepdims=True)
    along = jnp.mean(inner * unit, axis=-1, keepdims=True)
    return scale * (inner - mean - unit * along), grad * unit


def fold_rows(values):
    total = values[:8]
    for i in range(1, values.shape[0] // 8):
        total = total + values[i * 8 : (i + 1) * 8]
    return total


def hidden_back(rows, width):
    tile = 32

    def kernel(own, got, hidden, back, gain, weight, grad_ref, low_ref, attended_ref, sums_ref):
        def part(t, sums):
            here = rows_at(t, tile)
            total = own[here, :] + wide(got[here, :])
            pulled, terms = norm_back(hidden[here, :], gain[...], total)
            grad = wide(back[here, :]) + pulled
            grad_ref[here, :] = grad
            low_ref[here, :] = low(grad)
            return tuple(a + fold_rows(b) for a, b in zip(sums, (terms, total, grad)))

        sums = loop(rows // tile, part, tuple(jnp.zeros((8, width), jnp.float32) for _ in range(3)))
        for n in range(3):
            sums_ref[n : n + 1, :] = jnp.sum(sums[n], axis=0, keepdims=True)

        def product(i, carry):
            here = rows_at(i, 256)
            attended_ref[here, :] = low(cols_dot(low_ref[here, :], weight[...]))
            return carry

        loop(rows // 256, product)

    vmem = pl.BlockSpec(memory_space=pltpu.VMEM)
    return pl.pallas_call(
        kernel,
        in_specs=[vmem] * 6,
        out_specs=[vmem] * 4,
        out_shape=[
            jax.ShapeDtypeStruct((rows, width), jnp.float32),
            jax.ShapeDtypeStruct((rows, width), jnp.bfloat16),
            jax.ShapeDtypeStruct((rows, width), jnp.bfloat16),
            jax.ShapeDtypeStruct((3, width), jnp.float32),
        ],
        compiler_params=pltpu.CompilerParams(vmem_limit_bytes=VMEM_LIMIT),
        cost_estimate=NO_COST,
        name="hidden_back",
    )


def stream_back(rows, width, parts, row_groups, piece):
    tile = 32
    chips = parts // 2

    def kernel(
        place_ref, kv_0, kv_1, kv_2, kv_3, queries, weight, tokens, gain, grad_hidden, normed, back, hidden_sums,
        units_a, units_b, input_ref, even_ref, odd_ref, grad_kv, grads, turned, product, small,
    ):
        place = place_ref[0]

        def values(t, value_sums):
            here = rows_at(t, tile)
            total = wide(kv_0[here, :]) + wide(kv_1[here, :]) + wide(kv_2[here, :]) + wide(kv_3[here, :])
            grad_kv[here, :] = low(total)
            return value_sums + fold_rows(total)

        value_sums = loop(rows // tile, values, jnp.zeros((8, 2 * HS), jnp.float32))
        turn((normed,), turned)
        product[...] = dot(turned[...], grad_kv[...])

        def back_part(i, carry):
            here = rows_at(i, 256)
            grads[here, :] = cols_dot(queries[here, :], weight[:, :width]) + cols_dot(grad_kv[here, :], weight[:, width:])
            return carry

        loop(rows // 256, back_part)

        def part(t, sums):
            here = rows_at(t, tile)
            grad = grads[here, :]
            pulled, terms = norm_back(wide(tokens[here, :]), gain[...], grad)
            input_ref[here, :] = grad_hidden[here, :] + pulled
            parts_now = (terms, grad, wide(queries[here, :]), wide(back[here, :]))
            return tuple(a + fold_rows(b) for a, b in zip(sums, parts_now))

        sums = loop(rows // tile, part, tuple(jnp.zeros((8, width), jnp.float32) for _ in range(4)))
        sums = [jnp.sum(part, axis=0, keepdims=True) for part in sums]
        small[...] = jnp.zeros_like(small)
        rows_in = (sums[0], sums[1], hidden_sums[0:1, :], hidden_sums[1:2, :], sums[2], hidden_sums[2:3, :], sums[3])
        for n, row in enumerate(rows_in):
            for j in range(width // 128):
                line = n * (width // 128) + j
                small[line : line + 1, :] = row[:, j * 128 : (j + 1) * 128]
        start = 7 * (width // 128)
        small[start : start + 1, :] = jnp.sum(value_sums, axis=0, keepdims=True)
        lines = FF // parts // 128
        for m in range(chips):
            units = (units_a, units_b)[m // 2]
            for j in range(lines):
                line = start + 1 + (place ^ (2 * m)) * lines + j
                at = (m % 2 * lines + j) * 128
                small[pl.ds(line, 1), :] = units[:, at : at + 128]
        for odd, ref in enumerate((even_ref, odd_ref)):

            def piece_of(m, carry):
                owner = place ^ (2 * m + odd)
                mine = low(small[pl.ds(pl.multiple_of(owner * piece, 8), piece), :])
                for w in range(row_groups):
                    at = pl.multiple_of(w * piece * parts + owner * piece, 8)
                    ref[m, w, :, :128] = low(product[pl.ds(at, piece), :])
                    ref[m, w, :, 128:] = mine
                return carry

            loop(chips, piece_of)

    vmem = pl.BlockSpec(memory_space=pltpu.VMEM)
    stack = jax.ShapeDtypeStruct((chips, row_groups, piece, 256), jnp.bfloat16)
    return pl.pallas_call(
        kernel,
        in_specs=[pl.BlockSpec(memory_space=pltpu.SMEM)] + [vmem] * 14,
        out_specs=[vmem] * 3,
        out_shape=[jax.ShapeDtypeStruct((rows, width), jnp.float32), stack, stack],
        scratch_shapes=[
            pltpu.VMEM((rows, 2 * HS), jnp.bfloat16),
            pltpu.VMEM((rows, width), jnp.float32),
            pltpu.VMEM((width, rows), jnp.bfloat16),
            pltpu.VMEM((width, 2 * HS), jnp.float32),
            pltpu.VMEM((parts * piece, 128), jnp.float32),
        ],
        compiler_params=pltpu.CompilerParams(vmem_limit_bytes=VMEM_LIMIT),
        cost_estimate=NO_COST,
        name="stream_back",
    )


def attn_grads(rows, width, row_groups, parts, piece):
    def kernel(place_ref, left_a, right_a, left_b, right_b, even_ref, odd_ref, turned, total):
        place = place_ref[0]
        for n, (left, right) in enumerate(((left_a, right_a), (left_b, right_b))):
            turn((left,), turned)

            def part(i, carry):
                here = rows_at(i, 256)
                total[here, n * width : (n + 1) * width] = dot(turned[here, :], right[...])
                return carry

            loop(width // 256, part)
        for odd, ref in enumerate((even_ref, odd_ref)):

            def piece_of(m, carry):
                for w in range(row_groups):
                    at = pl.multiple_of(w * piece * parts + (place ^ (2 * m + odd)) * piece, 8)
                    ref[m, w] = low(total[pl.ds(at, piece), :])
                return carry

            loop(parts // 2, piece_of)

    vmem = pl.BlockSpec(memory_space=pltpu.VMEM)
    shape = jax.ShapeDtypeStruct((parts // 2, row_groups, piece, 2 * width), jnp.bfloat16)
    return pl.pallas_call(
        kernel,
        grid_spec=pltpu.PrefetchScalarGridSpec(
            num_scalar_prefetch=1,
            grid=(),
            in_specs=[vmem] * 4,
            out_specs=[vmem] * 2,
            scratch_shapes=[pltpu.VMEM((width, rows), jnp.bfloat16), pltpu.VMEM((width, 2 * width), jnp.float32)],
        ),
        out_shape=[shape] * 2,
        compiler_params=pltpu.CompilerParams(vmem_limit_bytes=VMEM_LIMIT),
        cost_estimate=NO_COST,
        name="attn_grads",
    )


def attn_update(rows, columns, width, parts, piece):
    qkv = columns - width

    def kernel(place_ref, even_ref, odd_ref, master, first, second, *outs):
        place = place_ref[0]
        for odd, ref in enumerate((even_ref, odd_ref)):

            def piece_of(m, carry):
                here = pl.ds(pl.multiple_of((place ^ (2 * m + odd)) * piece, 8), piece)
                for cols, source in (
                    (slice(0, width), slice(0, width)),
                    (slice(width, qkv), slice(2 * width, columns)),
                    (slice(qkv, columns), slice(width, 2 * width)),
                ):
                    grad = wide(ref[m, :, source])
                    got = adam_update(master[here, cols], grad, first[here, cols], second[here, cols], 0.1, 0.1)
                    outs[0][here, cols] = got[0]
                    outs[1][here, cols] = got[1]
                    outs[2][here, cols] = got[2]
                return carry

            loop(parts // 2, piece_of)

    vmem = pl.BlockSpec(memory_space=pltpu.VMEM)
    return pl.pallas_call(
        kernel,
        grid_spec=pltpu.PrefetchScalarGridSpec(
            num_scalar_prefetch=1, grid=(), in_specs=[vmem] * 5, out_specs=[vmem] * 3, scratch_shapes=[]
        ),
        out_shape=[jax.ShapeDtypeStruct((rows, columns), jnp.float32)] * 3,
        compiler_params=pltpu.CompilerParams(vmem_limit_bytes=VMEM_LIMIT),
        cost_estimate=NO_COST,
        name="attn_update",
    )


def ffn_update(rows, units, parts, chunk):
    per_row = 2 * units // 128
    rows_once = 32
    lines = rows_once * per_row

    def kernel(grad, master, first, second, first_out, second_out, master_out, total):
        def spread(k, carry):
            for j in range(chunk // 128):
                for which in range(2):
                    line = k * (2 * chunk // 128) + 2 * j + which
                    total[pl.ds(line, rows_once, per_row), :] = wide(grad[k, which, :, j * 128 : (j + 1) * 128])
            return carry

        loop(parts, spread)

        def part(t, carry):
            own = rows_at(t, 128)
            got = adam_update(master[own, :], total[own, :], first[own, :], second[own, :], 0.1, 0.1)
            first_out[own, :] = got[0]
            second_out[own, :] = got[1]
            master_out[own, :] = got[2]
            return carry

        loop(lines // 128, part)

    block = pl.BlockSpec((lines, 128), lambda i: (i, 0))
    call = pl.pallas_call(
        kernel,
        grid=(rows // rows_once,),
        in_specs=[pl.BlockSpec((parts, 2, rows_once, chunk), lambda i: (0, 0, i, 0))] + [block] * 3,
        out_specs=[block] * 3,
        out_shape=[jax.ShapeDtypeStruct((rows * per_row, 128), jnp.float32)] * 3,
        scratch_shapes=[pltpu.VMEM((lines, 128), jnp.float32)],
        compiler_params=pltpu.CompilerParams(vmem_limit_bytes=VMEM_LIMIT),
        cost_estimate=NO_COST,
        name="ffn_update",
    )

    def fold(array):
        return jnp.swapaxes(array.reshape(rows, 2, units // 128, 128), 1, 2).reshape(-1, 128)

    def unfold(array):
        return jnp.swapaxes(array.reshape(rows, units // 128, 2, 128), 1, 2).reshape(rows, 2, units)

    def run(grad, master, first, second):
        return tuple(unfold(array) for array in call(grad, fold(master), fold(first), fold(second)))

    return run


def shards(
    tokens,
    doc_starts,
    attn_master,
    attn_mom,
    attn_sq,
    ffn_master,
    ffn_mom,
    ffn_sq,
    small_master,
    small_mom,
    small_sq,
    cotangent,
):
    ctx_count, wt_count = lax.axis_size("ctx"), lax.axis_size("wt")
    ctx_place, wt_place = lax.axis_index("ctx"), lax.axis_index("wt")
    batches, rows_here, width = tokens.shape
    qkv_cols = width + 2 * HS
    attn_columns = attn_master.shape[1]
    all_rows = batches * rows_here
    shard_rows = attn_master.shape[0]
    piece_rows = shard_rows // ctx_count
    chunk = FF // ctx_count
    chips = ctx_count // 2
    order = ctx_place ^ jnp.arange(ctx_count, dtype=jnp.int32)
    (
        gain_one,
        shift_one,
        gain_two,
        shift_two,
        bias_query,
        bias_out,
        bias_proj,
        bias_value,
        bias_hidden,
    ) = split_small(small_master)
    runs = 2 if batches % 2 == 0 else 1
    places = [jnp.stack([ctx_place, jnp.int32(run * (batches // runs))]) for run in range(runs)]
    place = places[0]
    wt_half = wt_count // 2
    out_rows = shard_rows // chips
    run_forward, run_backward = attention_kernels(batches, rows_here, width, ctx_count, runs)
    ffn_first, ffn_second, ffn_third, ffn_down = ffn_kernels(all_rows, width, chunk, wt_count)
    step = Steps()

    def both(own, got, place, bit, axis=0):
        ahead, behind = jnp.stack([own, got], axis), jnp.stack([got, own], axis)
        return jnp.where((place & bit) == 0, ahead, behind)

    def in_order(even, odd):
        buffer = jnp.zeros((ctx_count,) + even.shape[1:], even.dtype)
        for m in range(chips):
            buffer = put(buffer, even[m][None], ctx_place ^ (2 * m), 0)
            buffer = put(buffer, odd[m][None], ctx_place ^ (2 * m + 1), 0)
        return buffer

    def send_chips(piece):
        return [xor_send(piece, mask) for mask in range(2, ctx_count, 2)]

    def split_wt(total, bit):
        ahead, behind = jnp.split(total, 2)
        kept, sent = jnp.where((wt_place & bit) == 0, ahead, behind), jnp.where((wt_place & bit) == 0, behind, ahead)
        return kept, sent

    def add_low(*arrays):
        return low(sum(wide(array) for array in arrays))

    qkv = low(lax.dynamic_slice(attn_master, (ctx_place * piece_rows, 0), (piece_rows, qkv_cols)))
    qkv_got = xor_wt(qkv, 1)
    out = low(
        lax.dynamic_slice(
            attn_master, (ctx_place // 2 * out_rows, qkv_cols + ctx_place % 2 * chunk), (out_rows, chunk)
        )
    )
    rest = low(jnp.swapaxes(take(ffn_master, ctx_place, 2, chunk), 0, 1).reshape(2 * shard_rows, chunk))
    qkv_got, rest = lax.optimization_barrier((qkv_got, rest))
    rest = lax.all_gather(rest, "wt", axis=0)
    out_got = xor_wt(out, 1)
    back_low = cotangent.reshape(all_rows, width)
    back_other = xor_send(back_low, 1)
    flat_tokens = tokens.reshape(all_rows, width)
    wt_bits = [1 << n for n in reversed(range(wt_count.bit_length() - 1))]
    qkv = step(lambda own, got: both(own, got, wt_place, 1), qkv, qkv_got)
    for bit in wt_bits[::-1][1:]:
        qkv_got = xor_wt(qkv, bit)
        out = step(lambda own, got: both(own, got, wt_place, 1), out, out_got) if out.ndim == 2 else out
        out_got = xor_wt(out, bit)
        join = lambda own, got: both(own, got, wt_place, bit).reshape((-1,) + own.shape[1:])
        qkv = step(join, qkv, qkv_got)
        qkv_next = xor_send(qkv, 2)
        out = step(join, out, out_got)
    qkv_got, out_got = qkv_next, xor_send(out, 2)
    normed_low = step(
        lambda tokens, gain, shift: low(layer_norm(wide(tokens), gain, shift)), flat_tokens, gain_one, shift_one
    )
    qkv = step(lambda own, got: both(own, got, ctx_place, 2), qkv, qkv_got)
    qkv_got = xor_send(qkv, 4)
    out = step(lambda own, got: both(own, got, ctx_place, 2), out, out_got)
    out_got = xor_send(out, 4)
    back_turned = step(turn_both, back_low, back_other)
    qkv = step(lambda own, got: both(own, got, ctx_place, 4), qkv, qkv_got)
    qkv_got = xor_send(qkv, 1)

    def project(own, got, normed):
        blocks = both(own, got, ctx_place, 1, 2)
        weight = jnp.transpose(blocks, (3, 0, 1, 2, 4, 5)).reshape(width, qkv_cols)
        mixed = dot(normed, weight)
        queries = low(mixed[:, :width] + bias_query).reshape(batches, rows_here, width)
        kv_bias = jnp.concatenate([jnp.zeros((HS,), jnp.float32), bias_value])
        kv_local = low(mixed[:, width:] + kv_bias).reshape(batches, rows_here, 2 * HS)
        return weight, queries, kv_local

    weight_qkv, queries, kv_local = step(project, qkv, qkv_got, normed_low)
    kv_got = send_chips(kv_local)
    out = step(lambda own, got: both(own, got, ctx_place, 4), out, out_got)
    out_got = xor_send(out, 1)
    kv_even = step(lambda *parts: jnp.stack(parts), kv_local, *kv_got)
    kv_odd = xor_send(kv_even, 1)

    def join_out(own, got):
        blocks = both(own, got, ctx_place, 1, 2)
        return jnp.transpose(blocks, (3, 0, 1, 4, 2, 5)).reshape(width, width)

    weight_out = step(join_out, out, out_got)
    queries, rest, weight_out = lax.optimization_barrier((queries, rest, weight_out))
    rest_x, rest_y = xor_send(rest, 2), xor_send(rest, 4)

    attended_low, attended, logs = step(run_forward, doc_starts, place, queries, kv_even, kv_odd)
    attended_low = attended_low.reshape(all_rows, width)
    low_half, high_half = step(lambda x, y: (x[:wt_half], y[wt_half:]), rest_x, rest_y)
    diagonal_low, diagonal_high = xor_send(low_half, 4), xor_send(high_half, 2)
    hidden, normed_two = step(
        out_projection(all_rows, width), attended_low, weight_out, flat_tokens, bias_out[None], gain_two[None],
        shift_two[None],
    )
    normed_other = xor_send(normed_two, 1)

    bias_parts = bias_hidden.reshape(ctx_count, chunk)[order[::2]].reshape(1, chips * chunk)
    bias_near, bias_far = jnp.split(bias_parts, 2, axis=1)
    weights = [rest, rest_x, rest_y, diagonal_low, diagonal_high]
    flows = (normed_two, normed_other, back_low, back_other, back_turned)
    act_first, units_first, down_own, down_x, sums_first = step(
        lambda *args: ffn_first(*args[:6], *in_hbm(args[6:])), *flows, bias_near, *weights[:2]
    )
    act_second, units_second, down_y, down_top, down_bottom, sums_second, back_own, back_part = step(
        lambda *args: ffn_second(*args[:6], *in_hbm(args[6:])), *flows, bias_far, units_first, *weights
    )
    back_got = xor_send(back_part, 1)
    top_got, bottom_got = xor_send(down_top, 4), xor_send(down_bottom, 2)

    def meet(along_x, along_y, top, bottom):
        half = width // 2
        return (
            jnp.concatenate([add_low(along_x[:half], top), along_x[half:]]),
            jnp.concatenate([along_y[:half], add_low(along_y[half:], bottom)]),
        )

    up_own, up_x, up_y, up_top, up_bottom = step(
        lambda *args: ffn_third(*args[:2], *in_hbm(args[2:])), normed_two, normed_other, units_first, units_second
    )
    down_x, down_y = step(meet, down_x, down_y, top_got, bottom_got)
    down_got = [xor_send(down_x, 2), xor_send(down_y, 4)]
    top_got, bottom_got = xor_send(up_top, 4), xor_send(up_bottom, 2)

    grad_hidden, grad_hidden_low, grad_attended, hidden_sums = step(
        hidden_back(all_rows, width), back_own, back_got, hidden, back_low, gain_two[None], weight_out
    )
    grad_attended = grad_attended.reshape(batches, rows_here, width)
    up_x, up_y = step(meet, up_x, up_y, top_got, bottom_got)
    up_got = [xor_send(up_x, 2), xor_send(up_y, 4)]

    def by_wt(own, *got):
        total = add_low(own, *got)
        return split_wt(total.reshape(wt_count, shard_rows, chunk), wt_bits[0])

    def next_wt(bit):
        return lambda kept, got: split_wt(add_low(kept, got), bit)

    backs = [step(run_backward[0], doc_starts, places[0], queries, kv_even, kv_odd, attended, logs, grad_attended)]
    kv_got = [xor_send(backs[0][2], 1)]
    down_kept, down_sent = step(by_wt, down_own, *down_got)
    down_got = xor_wt(down_sent, wt_bits[0])
    backs += [
        step(run_backward[run], doc_starts, places[run], queries, kv_even, kv_odd, attended, logs, grad_attended)
        for run in range(1, runs)
    ]
    kv_got += [xor_send(back[2], 1) for back in backs[1:]]
    grad_query = jnp.concatenate([back[0] for back in backs]).reshape(all_rows, width)

    def kv_pieces(evens, odds):
        total = jnp.concatenate([add_low(a, b) for a, b in zip(evens, odds)], axis=1)
        return [total[m] for m in range(chips)]

    for bit in wt_bits[1:]:
        down_kept, down_sent = step(next_wt(bit), down_kept, down_got)
        down_got = xor_wt(down_sent, bit)
    up_kept, up_sent = step(by_wt, up_own, *up_got)
    up_got = xor_wt(up_sent, wt_bits[0])
    kv_half = step(kv_pieces, [back[1] for back in backs], kv_got)
    kv_got = [xor_send(kv_half[m], 2 * m) for m in range(1, chips)]
    wide_even, wide_odd = step(
        attn_grads(all_rows, width, wt_count, ctx_count, piece_rows),
        place, normed_low, grad_query, attended_low, grad_hidden_low,
    )
    down_part = step(add_low, down_kept, down_got)
    wide_odd = xor_send(wide_odd, 1)

    small_size = small_master.shape[0]
    input_grad, tail_even, tail_odd = step(
        stream_back(all_rows, width, ctx_count, wt_count, piece_rows),
        place, *[array.reshape(all_rows, 2 * HS) for array in (kv_half[0], *kv_got)], grad_query, weight_qkv,
        flat_tokens, gain_one[None], grad_hidden, normed_low, back_low, hidden_sums, sums_first, sums_second,
    )
    input_grad = input_grad.reshape(batches, rows_here, width)
    tail_odd = xor_send(tail_odd, 1)
    for bit in wt_bits[1:]:
        up_kept, up_sent = step(next_wt(bit), up_kept, up_got)
        up_got = xor_wt(up_sent, bit)

    def attn_pieces(wide_even, wide_odd, tail_even, tail_odd):
        total = jnp.concatenate([add_low(wide_even, wide_odd), add_low(tail_even, tail_odd)], axis=3)
        return [total[m] for m in range(chips)]

    attn_half = step(attn_pieces, wide_even, wide_odd, tail_even, tail_odd)
    attn_got = [xor_send(attn_half[m], 2 * m) for m in range(1, chips)]
    ffn_part = step(
        lambda up_kept, up_got, down_part: jnp.concatenate([add_low(up_kept, up_got), down_part]),
        up_kept, up_got, down_part,
    )
    ffn_got = xor_send(ffn_part, 2)
    down_out, down_other = step(
        lambda *args: ffn_down(*args[:2], *in_hbm(args[2:])), act_first, act_second, *weights
    )
    down_other = xor_send(down_other, 1)
    ffn_part = step(lambda own, got: both(own, got, ctx_place, 2), ffn_part, ffn_got)
    ffn_got = xor_send(ffn_part, 4)

    def attn_by_wt(*parts):
        return split_wt(add_low(*parts), wt_bits[0])

    attn_kept, attn_sent = step(attn_by_wt, attn_half[0], *attn_got)
    attn_got = xor_wt(attn_sent, wt_bits[0])
    layer_out = step(
        lambda hidden, own, got: low(hidden + own + wide(got) + bias_proj).reshape(batches, rows_here, width),
        hidden, down_out, down_other,
    )
    for bit in wt_bits[1:]:
        attn_kept, attn_sent = step(next_wt(bit), attn_kept, attn_got)
        attn_got = xor_wt(attn_sent, bit)
    ffn_part = step(lambda own, got: both(own, got, ctx_place, 4), ffn_part, ffn_got)
    ffn_got = xor_send(ffn_part, 1)
    attn_part = step(lambda *parts: add_low(*parts)[0], attn_kept, attn_got)
    attn_got = send_chips(attn_part)

    ffn_new = step(
        lambda own, got, *arrays: ffn_update(shard_rows, FF, ctx_count, chunk)(
            both(own, got, ctx_place, 1, 2).reshape(ctx_count, 2, shard_rows, chunk), *arrays
        ),
        ffn_part, ffn_got, ffn_master, ffn_mom, ffn_sq,
    )
    attn_even = step(lambda *parts: jnp.stack(parts), attn_part, *attn_got)
    attn_odd = xor_send(attn_even, 1)
    small_total = in_order(attn_even[..., attn_columns:], attn_odd[..., attn_columns:])
    small_total = wide(small_total.reshape(-1))
    most = small_size - FF - HS
    small_total = jnp.concatenate(
        [small_total[:most], small_total[most + HS : most + 2 * HS], small_total[most + 2 * HS : most + 2 * HS + FF]]
    )
    small_new = adam_update(small_master, small_total, small_mom, small_sq, 1.0, 0.0)
    attn_new = attn_update(shard_rows, attn_columns, width, ctx_count, piece_rows)(
        place, attn_even, attn_odd, attn_master, attn_mom, attn_sq
    )
    return (layer_out, input_grad) + tuple(attn_new) + tuple(ffn_new) + tuple(small_new)


def shift_wt(array, shift):
    count = lax.axis_size("wt")
    return lax.ppermute(array, "wt", [(i, (i + shift) % count) for i in range(count)])


def whole_wt(piece, axis):
    count, place = lax.axis_size("wt"), lax.axis_index("wt")
    shape = list(piece.shape)
    shape[axis] *= count
    buffer = put(jnp.zeros(shape, piece.dtype), piece, place, axis)
    for shift in range(1, count):
        buffer = put(buffer, shift_wt(piece, shift), (place - shift) % count, axis)
    return buffer


def whole_ctx(piece):
    count = lax.axis_size("ctx")
    got = {0: piece}
    for mask in range(2, count, 2):
        got[mask] = xor_send(piece, mask)
    for mask in range(0, count, 2):
        got[mask + 1] = xor_send(got[mask], 1)
    return [got[mask] for mask in range(count)]


def sum_ctx(pieces):
    count = lax.axis_size("ctx")
    half = {}
    for mask in range(count - 2, -1, -2):
        other = xor_send(pieces[mask + 1], 1)
        half[mask] = low(wide(pieces[mask]) + wide(other))
    total = wide(half[0])
    for mask in range(2, count, 2):
        total = total + wide(xor_send(half[mask], mask))
    return total


def sum_wt(array, axis):
    count, place = lax.axis_size("wt"), lax.axis_index("wt")
    size = array.shape[axis] // count
    total = wide(take(array, place, axis, size))
    for shift in range(1, count):
        sent = take(array, (place + shift) % count, axis, size)
        total = total + wide(shift_wt(sent, shift))
    return total


def any_shards(
    tokens,
    doc_starts,
    attn_master,
    attn_mom,
    attn_sq,
    ffn_master,
    ffn_mom,
    ffn_sq,
    small_master,
    small_mom,
    small_sq,
    cotangent,
):
    ctx_count = lax.axis_size("ctx")
    ctx_place = lax.axis_index("ctx")
    wt_count = lax.axis_size("wt")
    batches, rows_here, width = tokens.shape
    heads = width // HS
    qkv_cols = width + 2 * HS
    all_rows = batches * rows_here
    shard_rows = attn_master.shape[0]
    piece_rows = shard_rows // ctx_count
    chunk = FF // ctx_count
    order = ctx_place ^ jnp.arange(ctx_count, dtype=jnp.int32)
    (
        gain_one,
        shift_one,
        gain_two,
        shift_two,
        bias_query,
        bias_out,
        bias_proj,
        bias_value,
        bias_hidden,
    ) = split_small(small_master)

    attn_piece = low(take(attn_master, ctx_place, 0, piece_rows))

    def whole_rows(piece):
        parts = whole_ctx(whole_wt(piece[None], 0))
        buffer = jnp.zeros((wt_count, ctx_count) + piece.shape, piece.dtype)
        for k, part in enumerate(parts):
            buffer = put(buffer, part[:, None], ctx_place ^ k, 1)
        return buffer.reshape((width,) + piece.shape[1:])

    weight_qkv = whole_rows(attn_piece[:, :qkv_cols])
    weight_out = whole_rows(attn_piece[:, qkv_cols:])
    ffn_piece = low(jnp.swapaxes(take(ffn_master, ctx_place, 2, chunk), 0, 1))
    ffn_parts = whole_ctx(whole_wt(ffn_piece, 1))
    bias_parts = bias_hidden.reshape(ctx_count, chunk)[order]

    stream = wide(tokens.reshape(all_rows, width))
    normed, norm_back_one = jax.vjp(layer_norm, stream, gain_one, shift_one)
    normed_low = low(normed)
    mixed = dot(normed_low, weight_qkv)
    queries = low(mixed[:, :width] + bias_query)
    kv_local = low(
        mixed[:, width:] + jnp.concatenate([jnp.zeros((HS,), jnp.float32), bias_value])
    ).reshape(batches, rows_here, 2 * HS)
    kv_parts = jnp.stack(whole_ctx(kv_local), axis=1).reshape(
        batches, ctx_count * rows_here, 2 * HS
    )
    keys_all, values_all = kv_parts[..., :HS], kv_parts[..., HS:]
    local_pos = jnp.arange(rows_here, dtype=jnp.int32)
    query_pos = ctx_place * rows_here + local_pos
    key_pos = (order[:, None] * rows_here + local_pos[None, :]).reshape(-1)
    queries = queries.reshape(batches, rows_here * heads, HS)
    scale = HS ** (-0.5)
    attended_list, log_list, allowed_list = [], [], []
    for b in range(batches):
        starts = doc_starts[b]
        query_doc = jnp.sum((starts[None, :] <= query_pos[:, None]).astype(jnp.int32), axis=1)
        key_doc = jnp.sum((starts[None, :] <= key_pos[:, None]).astype(jnp.int32), axis=1)
        allowed = (query_doc[:, None] == key_doc[None, :]) & (key_pos[None, :] <= query_pos[:, None])
        allowed = jnp.repeat(allowed, heads, axis=0)
        allowed_list.append(allowed)
        scores = jnp.where(allowed, cols_dot(queries[b], keys_all[b]) * scale, -1e30)
        peak = jnp.max(scores, axis=-1, keepdims=True)
        expo = jnp.exp(scores - peak)
        total = jnp.sum(expo, axis=-1, keepdims=True)
        attended_list.append(dot(low(expo / total), values_all[b]))
        log_list.append(peak + jnp.log(total))
    attended = jnp.stack(attended_list)
    attended_low = low(attended).reshape(all_rows, width)
    hidden = stream + dot(attended_low, weight_out) + bias_out
    normed_two, norm_back_two = jax.vjp(layer_norm, hidden, gain_two, shift_two)
    normed_two_low = low(normed_two)

    back_low = cotangent.reshape(all_rows, width)
    back_rows = wide(back_low)
    down_vals = jnp.zeros((all_rows, width), jnp.float32)
    grad_normed_two = jnp.zeros((all_rows, width), jnp.float32)
    ffn_grads, hidden_grads = [], []
    for k in range(ctx_count):
        weight_up, weight_down = ffn_parts[k][0], ffn_parts[k][1]
        value, slope = gelu_both(dot(normed_two_low, weight_up) + bias_parts[k])
        act = low(value)
        down_vals = down_vals + cols_dot(act, weight_down)
        grad_up = low(dot(back_low, weight_down) * slope)
        hidden_grads.append(jnp.sum(wide(grad_up), axis=0))
        grad_normed_two = grad_normed_two + cols_dot(grad_up, weight_up)
        ffn_grads.append(
            jnp.stack([low(rows_dot(normed_two_low, grad_up)), low(rows_dot(back_low, act))])
        )
    layer_out = low(hidden + down_vals + bias_proj).reshape(batches, rows_here, width)
    grad_bias_proj = jnp.sum(back_rows, axis=0)
    grad_bias_hidden = jnp.stack(hidden_grads)[order].reshape(FF)
    ffn_part = low(sum_wt(low(sum_ctx(ffn_grads)), 1))

    grad_hidden_part, grad_gain_two, grad_shift_two = norm_back_two(grad_normed_two)
    grad_hidden = back_rows + grad_hidden_part
    grad_bias_out = jnp.sum(grad_hidden, axis=0)
    grad_hidden_low = low(grad_hidden)
    grad_out = rows_dot(attended_low, grad_hidden_low)

    def summed_rows(grad):
        blocks = low(grad).reshape(wt_count, ctx_count, piece_rows, grad.shape[1])
        pieces = [take(blocks, ctx_place ^ k, 1, 1)[:, 0] for k in range(ctx_count)]
        part = low(sum_wt(low(sum_ctx(pieces)), 0)[0])
        buffer = jnp.zeros((ctx_count,) + part.shape, part.dtype)
        for k, got in enumerate(whole_ctx(part)):
            buffer = put(buffer, got[None], ctx_place ^ k, 0)
        return wide(buffer.reshape(shard_rows, grad.shape[1]))

    out_total = summed_rows(grad_out)

    grad_attended = low(cols_dot(grad_hidden_low, weight_out)).reshape(
        batches, rows_here * heads, HS
    )
    grad_query_list, grad_kv_list = [], []
    for b in range(batches):
        grads = grad_attended[b]
        delta = jnp.sum(wide(grads) * attended[b], axis=-1, keepdims=True)
        scores = jnp.where(allowed_list[b], cols_dot(queries[b], keys_all[b]) * scale, -1e30)
        weights = jnp.exp(scores - log_list[b])
        grad_scores = low(weights * (cols_dot(grads, values_all[b]) - delta))
        grad_query_list.append(low(dot(grad_scores, keys_all[b]) * scale))
        grad_kv_list.append(
            jnp.concatenate(
                [
                    low(rows_dot(grad_scores, queries[b]) * scale),
                    low(rows_dot(low(weights), grads)),
                ],
                axis=1,
            )
        )
    grad_query = jnp.stack(grad_query_list).reshape(all_rows, width)
    grad_kv = jnp.stack(grad_kv_list).reshape(batches, ctx_count, rows_here, 2 * HS)
    grad_kv_low = low(sum_ctx([grad_kv[:, k] for k in range(ctx_count)])).reshape(
        all_rows, 2 * HS
    )
    grad_bias_query = jnp.sum(wide(grad_query), axis=0)
    grad_bias_value = jnp.sum(wide(grad_kv_low[:, HS:]), axis=0)
    grad_mixed = jnp.concatenate([grad_query, grad_kv_low], axis=1)
    qkv_total = summed_rows(rows_dot(normed_low, grad_mixed))
    grad_normed = cols_dot(grad_mixed, weight_qkv)
    grad_stream_part, grad_gain_one, grad_shift_one = norm_back_one(grad_normed)
    input_grad = (grad_hidden + grad_stream_part).reshape(batches, rows_here, width)

    ffn_buffer = jnp.zeros((ctx_count,) + ffn_part.shape, ffn_part.dtype)
    for k, got in enumerate(whole_ctx(ffn_part)):
        ffn_buffer = put(ffn_buffer, got[None], ctx_place ^ k, 0)
    ffn_total = wide(jnp.transpose(ffn_buffer, (2, 1, 0, 3)).reshape(shard_rows, 2, FF))
    attn_total = jnp.concatenate([qkv_total, out_total], axis=1)
    grad_small = jnp.concatenate(
        [
            grad_gain_one,
            grad_shift_one,
            grad_gain_two,
            grad_shift_two,
            grad_bias_query,
            grad_bias_out,
            grad_bias_proj,
            grad_bias_value,
            grad_bias_hidden,
        ]
    )
    small_total = lax.psum(grad_small, ("ctx", "wt"))
    attn_new = adam_update(attn_master, attn_total, attn_mom, attn_sq, 0.1, 0.1)
    ffn_new = adam_update(ffn_master, ffn_total, ffn_mom, ffn_sq, 0.1, 0.1)
    small_new = adam_update(small_master, small_total, small_mom, small_sq, 1.0, 0.0)
    return (layer_out, input_grad) + attn_new + ffn_new + small_new


def solution(mesh):
    rows, cube = P("wt", None), P("wt", None, None)
    flow = P("wt", "ctx", None)
    in_specs = (flow, rows, rows, rows, rows, cube, cube, cube, P(), P(), P(), flow)
    out_specs = (flow, flow, rows, rows, rows, cube, cube, cube, P(), P(), P())
    ctx_count, wt_count = mesh.shape["ctx"], mesh.shape["wt"]
    fitted = ctx_count == 8 and wt_count % 2 == 0 and D // wt_count % (4 * ctx_count) == 0
    body = shards if fitted else any_shards
    return jax.shard_map(body, mesh=mesh, in_specs=in_specs, out_specs=out_specs, check_vma=False)
```

```python
import jax
import jax.numpy as jnp
from jax import lax
from jax.experimental import pallas as pl
from jax.experimental.pallas import tpu as pltpu
from jax.sharding import PartitionSpec as P

D = 768
HS = 64
FF = 3072
STEP = 10


NORM_EPS = 1e-05
GELU_COEF = 0.7978845608028654
GELU_CUBE = 0.044715
BETA_ONE = 0.9
BETA_TWO = 0.95
ADAM_EPS = 1e-08
VMEM_LIMIT = 22 << 20
NO_COST = pl.CostEstimate(flops=0, bytes_accessed=0, transcendentals=0)


def layer_norm(values, gain, shift):
    centre = values - jnp.mean(values, axis=-1, keepdims=True)
    spread = jnp.mean(centre * centre, axis=-1, keepdims=True)
    return centre * lax.rsqrt(spread + NORM_EPS) * gain + shift


def gelu_both(u):
    square = u * u
    share = 0.5 * jnp.tanh(u * (GELU_COEF * GELU_CUBE * square + GELU_COEF)) + 0.5
    bend = u * (6.0 * GELU_COEF * GELU_CUBE * square + 2.0 * GELU_COEF)
    return u * share, share * ((1.0 - share) * bend) + share


def split_small(small):
    return (
        small[0:D],
        small[D : 2 * D],
        small[2 * D : 3 * D],
        small[3 * D : 4 * D],
        small[4 * D : 5 * D],
        small[5 * D : 6 * D],
        small[6 * D : 7 * D],
        small[7 * D : 7 * D + HS],
        small[7 * D + HS :],
    )


def rows_dot(left, right):
    return lax.dot_general(
        left, right, (((0,), (0,)), ((), ())), preferred_element_type=jnp.float32
    )


def cols_dot(left, right):
    return lax.dot_general(
        left, right, (((1,), (1,)), ((), ())), preferred_element_type=jnp.float32
    )


def dot(left, right):
    return jnp.dot(left, right, preferred_element_type=jnp.float32)


def low(values):
    return values.astype(jnp.bfloat16)


def wide(values):
    return values.astype(jnp.float32)


def adam_update(master, gradient, first, second, step_rate, decay_rate):
    first_new = BETA_ONE * first + (1.0 - BETA_ONE) * gradient
    second_new = BETA_TWO * second + (1.0 - BETA_TWO) * gradient * gradient
    first_hat = first_new / (1.0 - BETA_ONE**STEP)
    second_hat = second_new / (1.0 - BETA_TWO**STEP)
    master_new = master - step_rate * (
        first_hat / (jnp.sqrt(second_hat) + ADAM_EPS) + decay_rate * master
    )
    return (first_new, second_new, master_new)


def xor_send(array, mask):
    count = lax.axis_size("ctx")
    return lax.ppermute(array, "ctx", [(i, i ^ mask) for i in range(count)])


def xor_wt(array, mask):
    count = lax.axis_size("wt")
    return lax.ppermute(array, "wt", [(i, i ^ mask) for i in range(count)])


class Steps:
    def __init__(self):
        self.last = ()

    def __call__(self, function, *args):
        flat, tree = jax.tree.flatten(args)
        held = lax.optimization_barrier(tuple(flat) + self.last)[: len(flat)]
        result = function(*jax.tree.unflatten(tree, held))
        self.last = tuple(jax.tree.leaves(result))
        return result


def put(buffer, piece, place, axis):
    starts = [0] * buffer.ndim
    starts[axis] = place * piece.shape[axis]
    return lax.dynamic_update_slice(buffer, piece, starts)


def take(buffer, place, axis, size):
    return lax.dynamic_slice_in_dim(buffer, place * size, size, axis)


def attention_kernels(batches, rows, width, parts, runs):
    half_parts = parts // 2
    keys = parts * rows
    pair = 2 * HS
    groups = width // (2 * pair)
    factor = HS ** (-0.5) * 1.4426950408889634
    tile = 32

    def lanes(shape):
        return lax.broadcasted_iota(jnp.int32, shape, 1)

    def spread(even_ref, odd_ref, key_ref, value_ref):
        for j in range(parts):
            ref = even_ref if j < half_parts else odd_ref
            block = wide(ref[j % half_parts, 0])
            turned = pltpu.roll(block, HS, 1)
            first = lanes(block.shape) < HS
            here = pl.ds(j * rows, rows)
            key_ref[0, here, :] = low(jnp.where(first, block, 0.0))
            key_ref[1, here, :] = low(jnp.where(first, 0.0, turned))
            value_ref[0, here, :] = low(jnp.where(first, turned, 0.0))
            value_ref[1, here, :] = low(jnp.where(first, 0.0, block))

    def doc_begin(starts_ref, stream, positions):
        begin = jnp.zeros_like(positions)
        for j in range(starts_ref.shape[1]):
            start = starts_ref[stream, j]
            begin = jnp.where(start <= positions, jnp.maximum(begin, start), begin)
        return begin

    def forward(starts_ref, place_ref, query_ref, even_ref, odd_ref, low_ref, full_ref, log_ref, cap, key, value, weight):
        stream, place = pl.program_id(0), place_ref[0]
        spread(even_ref, odd_ref, key, value)
        query_pos = place * rows + lax.broadcasted_iota(jnp.int32, (rows, 1), 0)
        begin = doc_begin(starts_ref, stream, query_pos)
        for j in range(parts):
            key_pos = (2 * (j % half_parts) + (place + j // half_parts) % 2) * rows + lax.broadcasted_iota(jnp.int32, (rows, rows), 1)
            allowed = (key_pos >= begin) & (key_pos <= query_pos)
            cap[:, j * rows : (j + 1) * rows] = jnp.where(allowed, 3.0e38, -1e30)
        column = lanes((tile, pair))
        logs = [jnp.zeros((tile, pair), jnp.float32) for _ in range(rows // tile)]
        for g in range(groups):
            at = g * 2 * pair
            two = jnp.concatenate([query_ref[0, :, at : at + pair], query_ref[0, :, at + pair : at + 2 * pair]], axis=0)
            totals = []
            for half in range(2):
                scores = cols_dot(two, key[half])
                norms = []
                for t in range(2 * rows // tile):
                    own = slice(t * tile, (t + 1) * tile)
                    n = t % (rows // tile)
                    part = jnp.minimum(scores[own] * factor, cap[n * tile : (n + 1) * tile, :])
                    peak = jnp.max(part, axis=1, keepdims=True)
                    expo = jnp.exp2(part - peak)
                    norm = jnp.sum(expo, axis=1, keepdims=True)
                    weight[half, own, :] = low(expo)
                    norms.append(norm)
                    head = 4 * g + 2 * (t * tile // rows) + half
                    logs[n] = jnp.where(column == head, peak + jnp.log2(norm), logs[n])
                totals.append(dot(weight[half], value[half]) / jnp.concatenate(norms, axis=0))
            total = totals[0] + totals[1]
            for j in range(2):
                part = total[j * rows : (j + 1) * rows]
                full_ref[0, :, at + j * pair : at + (j + 1) * pair] = part
                low_ref[0, :, at + j * pair : at + (j + 1) * pair] = low(part)
        for n, log in enumerate(logs):
            log_ref[0, n * tile : (n + 1) * tile, :] = log

    def backward(
        starts_ref, place_ref, query_ref, even_ref, odd_ref, full_ref, log_ref, grad_ref,
        query_grad_ref, even_grad_ref, odd_grad_ref,
        cap, key, value, key_turned, log_rows, delta_rows, weight_buf, score_buf, query_buf, grad_buf,
    ):
        stream, place = pl.program_id(0) + place_ref[1], place_ref[0]
        spread(even_ref, odd_ref, key, value)
        query_pos = place * rows + lax.broadcasted_iota(jnp.int32, (1, rows), 1)
        begin = doc_begin(starts_ref, stream, query_pos)
        for j in range(parts):
            key_pos = (2 * (j % half_parts) + (place + j // half_parts) % 2) * rows + lax.broadcasted_iota(jnp.int32, (rows, rows), 0)
            allowed = (key_pos >= begin) & (key_pos <= query_pos)
            cap[j * rows : (j + 1) * rows, :] = jnp.where(allowed, 3.0e38, -1e30)
            here = pl.ds(j * rows, rows)
            key_turned[:, j * rows : (j + 1) * rows] = low(wide(key[0, here, :]).T[:HS])
        log_rows[...] = log_ref[0].T[: log_rows.shape[0]]
        head_of = lax.broadcasted_iota(jnp.int32, (delta_rows.shape[0], width), 1) // HS
        chosen = (head_of == lax.broadcasted_iota(jnp.int32, (delta_rows.shape[0], width), 0)).astype(jnp.float32)
        delta_rows[...] = lax.dot_general(
            chosen, wide(grad_ref[0]) * full_ref[0], (((1,), (1,)), ((), ())),
            precision=lax.Precision.HIGHEST, preferred_element_type=jnp.float32,
        )
        first = lanes((2 * rows, pair)) < HS
        for g in range(groups):
            at = g * 2 * pair
            both, both_grad = query_ref[0, :, at : at + 2 * pair], grad_ref[0, :, at : at + 2 * pair]
            two = jnp.concatenate([both[:, :pair], both[:, pair:]], axis=0)
            two_grad = jnp.concatenate([both_grad[:, :pair], both_grad[:, pair:]], axis=0)
            turned = []
            for half in range(2):
                h = 4 * g + half
                span = slice((2 * g + half) * 2 * rows, (2 * g + half + 1) * 2 * rows)
                keep = first if half == 0 else jnp.logical_not(first)
                query_buf[span, :] = low(jnp.where(keep, wide(two), 0.0))
                grad_buf[span, :] = low(jnp.where(keep, wide(two_grad), 0.0))
                log = jnp.concatenate([log_rows[h : h + 1, :], log_rows[h + 2 : h + 3, :]], axis=1)
                delta = jnp.concatenate([delta_rows[h : h + 1, :], delta_rows[h + 2 : h + 3, :]], axis=1)
                scores, weight_grads = cols_dot(key[half], two), cols_dot(value[half], two_grad)
                for t in range(keys // (2 * tile)):
                    own = slice(t * 2 * tile, (t + 1) * 2 * tile)
                    limit = cap[own, :]
                    limit = jnp.concatenate([limit, limit], axis=1)
                    weights = jnp.exp2(jnp.minimum(scores[own] * factor, limit) - log)
                    weight_buf[own, span] = low(weights)
                    score_buf[own, span] = low(weights * (weight_grads[own] - delta))
                turned.append(dot(key_turned[...], score_buf[:, span]))
            turned = jnp.concatenate(turned, axis=0) * HS ** (-0.5)
            query_grad_ref[0, :, at : at + pair] = low(turned[:, :rows].T)
            query_grad_ref[0, :, at + pair : at + 2 * pair] = low(turned[:, rows:].T)
        for j in range(parts):
            here = pl.ds(j * rows, rows)
            value_sum = dot(weight_buf[here, :], grad_buf[...])
            key_sum = dot(score_buf[here, :], query_buf[...]) * HS ** (-0.5)
            value_sum = value_sum + pltpu.roll(value_sum, HS, 1)
            key_sum = key_sum + pltpu.roll(key_sum, HS, 1)
            ref = even_grad_ref if j < half_parts else odd_grad_ref
            ref[j % half_parts, 0] = low(jnp.where(lanes((rows, pair)) < HS, key_sum, value_sum))

    def specs(first):
        return (
            pl.BlockSpec((1, rows, width), lambda b, *_: (b + first, 0, 0)),
            pl.BlockSpec((1, rows, pair), lambda b, *_: (b + first, 0, 0)),
            pl.BlockSpec((half_parts, 1, rows, pair), lambda b, *_: (0, b + first, 0, 0)),
        )

    flow, logs, blocks = specs(0)

    shared = [
        pltpu.VMEM((2, keys, pair), jnp.bfloat16),
        pltpu.VMEM((2, keys, pair), jnp.bfloat16),
    ]
    run_forward = pl.pallas_call(
        forward,
        grid_spec=pltpu.PrefetchScalarGridSpec(
            num_scalar_prefetch=2,
            grid=(batches,),
            in_specs=[flow, blocks, blocks],
            out_specs=[flow, flow, logs],
            scratch_shapes=[pltpu.VMEM((rows, keys), jnp.float32)]
            + shared
            + [pltpu.VMEM((2, 2 * rows, keys), jnp.bfloat16)],
        ),
        out_shape=[
            jax.ShapeDtypeStruct((batches, rows, width), jnp.bfloat16),
            jax.ShapeDtypeStruct((batches, rows, width), jnp.float32),
            jax.ShapeDtypeStruct((batches, rows, pair), jnp.float32),
        ],
        compiler_params=pltpu.CompilerParams(vmem_limit_bytes=VMEM_LIMIT),
        cost_estimate=NO_COST,
        name="attention_forward",
    )
    head_rows = -(-(width // HS) // 8) * 8
    all_columns = rows * (width // HS)
    count = batches // runs

    def call_backward(run):
        here_flow, here_logs, here_blocks = specs(run * count)
        return pl.pallas_call(
        backward,
        grid_spec=pltpu.PrefetchScalarGridSpec(
            num_scalar_prefetch=2,
            grid=(count,),
            in_specs=[here_flow, here_blocks, here_blocks, here_flow, here_logs, here_flow],
            out_specs=[flow, blocks, blocks],
            scratch_shapes=[pltpu.VMEM((keys, rows), jnp.float32)]
            + shared
            + [
                pltpu.VMEM((HS, keys), jnp.bfloat16),
                pltpu.VMEM((head_rows, rows), jnp.float32),
                pltpu.VMEM((head_rows, rows), jnp.float32),
                pltpu.VMEM((keys, all_columns), jnp.bfloat16),
                pltpu.VMEM((keys, all_columns), jnp.bfloat16),
                pltpu.VMEM((all_columns, pair), jnp.bfloat16),
                pltpu.VMEM((all_columns, pair), jnp.bfloat16),
            ],
        ),
        out_shape=[
            jax.ShapeDtypeStruct((count, rows, width), jnp.bfloat16),
            jax.ShapeDtypeStruct((half_parts, count, rows, pair), jnp.bfloat16),
            jax.ShapeDtypeStruct((half_parts, count, rows, pair), jnp.bfloat16),
        ],
        compiler_params=pltpu.CompilerParams(vmem_limit_bytes=VMEM_LIMIT),
        cost_estimate=NO_COST,
        name="attention_backward",
    )

    return run_forward, [call_backward(run) for run in range(runs)]


def in_hbm(arrays):
    return [pltpu.with_memory_space_constraint(array, pltpu.HBM) for array in arrays]


def ffn_kernels(rows, width, chunk, wt_count):
    units = 2 * chunk
    all_rows = 2 * rows
    block_rows = width // wt_count
    hbm = pl.BlockSpec(memory_space=pltpu.HBM)
    vmem = pl.BlockSpec(memory_space=pltpu.VMEM)
    params = pltpu.CompilerParams(vmem_limit_bytes=VMEM_LIMIT)

    def fetch(weights, which, held, sem):
        copies = []
        for n, arrays in enumerate(weights):
            blocks = [array.at[block] for array in arrays for block in range(array.shape[0])]
            for row, block in enumerate(blocks):
                copies.append(
                    pltpu.make_async_copy(
                        block.at[pl.ds(which * block_rows, block_rows), :],
                        held.at[pl.ds(row * block_rows, block_rows), pl.ds(n * chunk, chunk)],
                        sem.at[len(copies)],
                    )
                )
        for copy in copies:
            copy.start()
        return copies

    def send(pairs, sems):
        copies = [pltpu.make_async_copy(source, out, sems.at[n]) for n, (source, out) in enumerate(pairs)]
        for copy in copies:
            copy.start()
        return copies

    def units_of(inputs, grads, bias, held_up, held_down, act, grad_units):
        tile = 16
        sums = jnp.zeros((8, units), jnp.float32)
        for s in range(2):
            up = dot(inputs[s][...], held_up[...])
            act_grad = dot(grads[s][...], held_down[...])
            for t in range(rows // tile):
                own = slice(t * tile, (t + 1) * tile)
                here = slice(s * rows + t * tile, s * rows + (t + 1) * tile)
                value, slope = gelu_both(up[own] + bias)
                grad = act_grad[own] * slope
                act[here, :] = low(value)
                grad_units[here, :] = low(grad)
                sums = sums + (grad[:8] + grad[8:])
        return jnp.sum(sums, axis=0, keepdims=True)

    def halves(product, m):
        cols = pl.ds(m * chunk, chunk)
        return [product.at[pl.ds(h * width // 2, width // 2), cols] for h in range(2)]

    def first(
        own, other, grad_own, grad_other, turned, bias, w0, w1,
        act_out, units_out, out_a, out_b, sums_out,
        held_up, held_down, act, grad_units, product, sems, out_sems,
    ):
        weights = ((w0,), (w1,))
        copies = fetch(weights, 0, held_up, sems.at[0]) + fetch(weights, 1, held_down, sems.at[1])
        for copy in copies:
            copy.wait()
        sums_out[...] = units_of((own, other), (grad_own, grad_other), bias[...], held_up, held_down, act, grad_units)
        sent = send(((act, act_out), (grad_units, units_out)), out_sems.at[0])
        product[...] = low(dot(turned[...], act[...]))
        sent += send(
            ((product.at[:, pl.ds(0, chunk)], out_a), (product.at[:, pl.ds(chunk, chunk)], out_b)), out_sems.at[1]
        )
        for copy in sent:
            copy.wait()

    def second(
        own, other, grad_own, grad_other, turned, bias, units_first, w0, w1, w2, w3, w4,
        act_out, units_out, out_a, out_b, out_c, sums_out, back_own, back_other,
        held_up, held_more, held_down, act, grad_units, more_units, product, sems, out_sems, more_sem,
    ):
        weights, before = ((w2,), (w3, w4)), ((w0,), (w1,))
        copies = fetch(weights, 0, held_up, sems.at[0]) + fetch(weights, 1, held_down, sems.at[1])
        more = fetch(before, 0, held_more, sems.at[2])
        more.append(pltpu.make_async_copy(units_first, more_units, more_sem))
        more[-1].start()
        for copy in copies:
            copy.wait()
        sums_out[...] = units_of((own, other), (grad_own, grad_other), bias[...], held_up, held_down, act, grad_units)
        sent = send(((act, act_out), (grad_units, units_out)), out_sems.at[0])
        product[...] = low(dot(turned[...], act[...]))
        top, bottom = halves(product, 1)
        sent += send(((product.at[:, pl.ds(0, chunk)], out_a), (top, out_b), (bottom, out_c)), out_sems.at[1])
        for copy in more:
            copy.wait()
        for s, ref in enumerate((back_own, back_other)):
            here = slice(s * rows, (s + 1) * rows)
            total = cols_dot(grad_units[here, :], held_up[...]) + cols_dot(more_units[here, :], held_more[...])
            ref[...] = total.astype(ref.dtype)
        for copy in sent:
            copy.wait()

    def third(own, other, units_a, units_b, out_0, out_1, out_2, out_3, out_4, turned, held, products, sems, out_sems):
        copies = send(((units_a, held.at[0]), (units_b, held.at[1])), sems)
        turn((own, other), turned)
        for copy in copies:
            copy.wait()
        products[1] = low(dot(turned[...], held[1]))
        top, bottom = halves(products.at[1], 1)
        sent = send(((products.at[1, :, pl.ds(0, chunk)], out_2), (top, out_3), (bottom, out_4)), out_sems.at[0])
        products[0] = low(dot(turned[...], held[0]))
        sent += send(
            ((products.at[0, :, pl.ds(0, chunk)], out_0), (products.at[0, :, pl.ds(chunk, chunk)], out_1)),
            out_sems.at[1],
        )
        for copy in sent:
            copy.wait()

    def down(act_a, act_b, w0, w1, w2, w3, w4, own_ref, other_ref, held_a, held_b, sems):
        copies = fetch(((w0,), (w1,)), 1, held_a, sems.at[0]) + fetch(((w2,), (w3, w4)), 1, held_b, sems.at[1])
        for copy in copies:
            copy.wait()
        for s, ref in enumerate((own_ref, other_ref)):
            here = slice(s * rows, (s + 1) * rows)
            total = cols_dot(act_a[here, :], held_a[...]) + cols_dot(act_b[here, :], held_b[...])
            ref[...] = total.astype(ref.dtype)

    dma = pltpu.SemaphoreType.DMA
    held = pltpu.VMEM((width, units), jnp.bfloat16)
    flow = pltpu.VMEM((all_rows, units), jnp.bfloat16)
    flow_out = pltpu.HBM((all_rows, units), jnp.bfloat16)
    whole = pltpu.HBM((width, chunk), jnp.bfloat16)
    part = pltpu.HBM((width // 2, chunk), jnp.bfloat16)
    sums = jax.ShapeDtypeStruct((1, units), jnp.float32)
    own = jax.ShapeDtypeStruct((rows, width), jnp.float32)
    other = jax.ShapeDtypeStruct((rows, width), jnp.bfloat16)
    run_first = pl.pallas_call(
        first,
        in_specs=[vmem] * 6 + [hbm] * 2,
        out_specs=[hbm] * 4 + [vmem],
        out_shape=[flow_out, flow_out, whole, whole, sums],
        scratch_shapes=[held, held, flow, flow, held, dma((2, 2 * wt_count)), dma((2, 2))],
        compiler_params=params,
        cost_estimate=NO_COST,
        name="ffn_first",
    )
    run_second = pl.pallas_call(
        second,
        in_specs=[vmem] * 6 + [hbm] * 6,
        out_specs=[hbm] * 5 + [vmem] * 3,
        out_shape=[flow_out, flow_out, whole, part, part, sums, own, other],
        scratch_shapes=[held, held, held, flow, flow, flow, held, dma((3, 2 * wt_count)), dma((2, 3)), dma(())],
        compiler_params=params,
        cost_estimate=NO_COST,
        name="ffn_second",
    )
    run_third = pl.pallas_call(
        third,
        in_specs=[vmem] * 2 + [hbm] * 2,
        out_specs=[hbm] * 5,
        out_shape=[whole, whole, whole, part, part],
        scratch_shapes=[
            pltpu.VMEM((width, all_rows), jnp.bfloat16),
            pltpu.VMEM((2, all_rows, units), jnp.bfloat16),
            pltpu.VMEM((2, width, units), jnp.bfloat16),
            dma((2,)),
            dma((2, 3)),
        ],
        compiler_params=params,
        cost_estimate=NO_COST,
        name="ffn_grads",
    )
    run_down = pl.pallas_call(
        down,
        in_specs=[vmem] * 2 + [hbm] * 5,
        out_specs=[vmem] * 2,
        out_shape=[own, other],
        scratch_shapes=[held, held, dma((2, 2 * wt_count))],
        compiler_params=params,
        cost_estimate=NO_COST,
        name="ffn_down",
    )
    return run_first, run_second, run_third, run_down


def turn(refs, turned):
    rows = refs[0].shape[0]
    for s, ref in enumerate(refs):
        for i in range(rows // 128):
            block = wide(ref[i * 128 : (i + 1) * 128, :])
            turned[:, s * rows + i * 128 : s * rows + (i + 1) * 128] = low(block.T)


def turn_both(own, other):
    vmem = pl.BlockSpec(memory_space=pltpu.VMEM)
    rows, width = own.shape
    return pl.pallas_call(
        lambda a, b, out: turn((a, b), out),
        in_specs=[vmem] * 2,
        out_specs=vmem,
        out_shape=jax.ShapeDtypeStruct((width, 2 * rows), own.dtype),
        compiler_params=pltpu.CompilerParams(vmem_limit_bytes=VMEM_LIMIT),
        cost_estimate=NO_COST,
        name="turn",
    )(own, other)


def out_projection(rows, width):
    tile = 32

    def kernel(attended, weight, stream, bias, gain, shift, hidden_ref, normed_ref):
        product = dot(attended[...], weight[...])
        for t in range(rows // tile):
            here = slice(t * tile, (t + 1) * tile)
            hidden = wide(stream[here, :]) + product[here] + bias[...]
            hidden_ref[here, :] = hidden
            normed_ref[here, :] = low(layer_norm(hidden, gain[...], shift[...]))

    vmem = pl.BlockSpec(memory_space=pltpu.VMEM)
    return pl.pallas_call(
        kernel,
        in_specs=[vmem] * 6,
        out_specs=[vmem] * 2,
        out_shape=[
            jax.ShapeDtypeStruct((rows, width), jnp.float32),
            jax.ShapeDtypeStruct((rows, width), jnp.bfloat16),
        ],
        compiler_params=pltpu.CompilerParams(vmem_limit_bytes=VMEM_LIMIT),
        cost_estimate=NO_COST,
        name="out_projection",
    )


def norm_back(values, gain, grad):
    centre = values - jnp.mean(values, axis=-1, keepdims=True)
    scale = lax.rsqrt(jnp.mean(centre * centre, axis=-1, keepdims=True) + NORM_EPS)
    unit = centre * scale
    inner = grad * gain
    mean = jnp.mean(inner, axis=-1, keepdims=True)
    along = jnp.mean(inner * unit, axis=-1, keepdims=True)
    return scale * (inner - mean - unit * along), grad * unit


def fold_rows(values):
    total = values[:8]
    for i in range(1, values.shape[0] // 8):
        total = total + values[i * 8 : (i + 1) * 8]
    return total


def hidden_back(rows, width):
    tile = 32

    def kernel(own, got, hidden, back, gain, weight, grad_ref, low_ref, attended_ref, sums_ref):
        sums = [jnp.zeros((8, width), jnp.float32) for _ in range(3)]
        for t in range(rows // tile):
            here = slice(t * tile, (t + 1) * tile)
            pulled, terms = norm_back(hidden[here, :], gain[...], own[here, :] + wide(got[here, :]))
            grad = wide(back[here, :]) + pulled
            grad_ref[here, :] = grad
            low_ref[here, :] = low(grad)
            for n, part in enumerate((terms, own[here, :] + wide(got[here, :]), grad)):
                sums[n] = sums[n] + fold_rows(part)
        for n in range(3):
            sums_ref[n : n + 1, :] = jnp.sum(sums[n], axis=0, keepdims=True)
        attended_ref[...] = low(cols_dot(low_ref[...], weight[...]))

    vmem = pl.BlockSpec(memory_space=pltpu.VMEM)
    return pl.pallas_call(
        kernel,
        in_specs=[vmem] * 6,
        out_specs=[vmem] * 4,
        out_shape=[
            jax.ShapeDtypeStruct((rows, width), jnp.float32),
            jax.ShapeDtypeStruct((rows, width), jnp.bfloat16),
            jax.ShapeDtypeStruct((rows, width), jnp.bfloat16),
            jax.ShapeDtypeStruct((3, width), jnp.float32),
        ],
        compiler_params=pltpu.CompilerParams(vmem_limit_bytes=VMEM_LIMIT),
        cost_estimate=NO_COST,
        name="hidden_back",
    )


def stream_back(rows, width, parts, row_groups, piece):
    tile = 32
    chips = parts // 2

    def kernel(
        place_ref, kv_0, kv_1, kv_2, kv_3, queries, weight, tokens, gain, grad_hidden, normed, back, hidden_sums,
        units_a, units_b, input_ref, even_ref, odd_ref, grad_kv, grads, turned, product, small,
    ):
        place = place_ref[0]
        sums = [jnp.zeros((8, width), jnp.float32) for _ in range(4)]
        value_sums = jnp.zeros((8, 2 * HS), jnp.float32)
        for t in range(rows // tile):
            here = slice(t * tile, (t + 1) * tile)
            total = wide(kv_0[here, :]) + wide(kv_1[here, :]) + wide(kv_2[here, :]) + wide(kv_3[here, :])
            grad_kv[here, :] = low(total)
            value_sums = value_sums + fold_rows(total)
        turn((normed,), turned)
        product[...] = dot(turned[...], grad_kv[...])
        grads[...] = cols_dot(queries[...], weight[:, :width]) + cols_dot(grad_kv[...], weight[:, width:])
        for t in range(rows // tile):
            here = slice(t * tile, (t + 1) * tile)
            grad = grads[here, :]
            pulled, terms = norm_back(wide(tokens[here, :]), gain[...], grad)
            input_ref[here, :] = grad_hidden[here, :] + pulled
            for n, part in enumerate((terms, grad, wide(queries[here, :]), wide(back[here, :]))):
                sums[n] = sums[n] + fold_rows(part)
        sums = [jnp.sum(part, axis=0, keepdims=True) for part in sums]
        small[...] = jnp.zeros_like(small)
        rows_in = (sums[0], sums[1], hidden_sums[0:1, :], hidden_sums[1:2, :], sums[2], hidden_sums[2:3, :], sums[3])
        for n, row in enumerate(rows_in):
            for j in range(width // 128):
                line = n * (width // 128) + j
                small[line : line + 1, :] = row[:, j * 128 : (j + 1) * 128]
        start = 7 * (width // 128)
        small[start : start + 1, :] = jnp.sum(value_sums, axis=0, keepdims=True)
        lines = FF // parts // 128
        for m in range(chips):
            units = (units_a, units_b)[m // 2]
            for j in range(lines):
                line = start + 1 + (place ^ (2 * m)) * lines + j
                at = (m % 2 * lines + j) * 128
                small[pl.ds(line, 1), :] = units[:, at : at + 128]
        for k in range(parts):
            ref = odd_ref if k % 2 else even_ref
            mine = low(small[pl.ds(pl.multiple_of((place ^ k) * piece, 8), piece), :])
            for w in range(row_groups):
                at = pl.multiple_of(w * piece * parts + (place ^ k) * piece, 8)
                ref[k // 2, w, :, :128] = low(product[pl.ds(at, piece), :])
                ref[k // 2, w, :, 128:] = mine

    vmem = pl.BlockSpec(memory_space=pltpu.VMEM)
    stack = jax.ShapeDtypeStruct((chips, row_groups, piece, 256), jnp.bfloat16)
    return pl.pallas_call(
        kernel,
        in_specs=[pl.BlockSpec(memory_space=pltpu.SMEM)] + [vmem] * 14,
        out_specs=[vmem] * 3,
        out_shape=[jax.ShapeDtypeStruct((rows, width), jnp.float32), stack, stack],
        scratch_shapes=[
            pltpu.VMEM((rows, 2 * HS), jnp.bfloat16),
            pltpu.VMEM((rows, width), jnp.float32),
            pltpu.VMEM((width, rows), jnp.bfloat16),
            pltpu.VMEM((width, 2 * HS), jnp.float32),
            pltpu.VMEM((parts * piece, 128), jnp.float32),
        ],
        compiler_params=pltpu.CompilerParams(vmem_limit_bytes=VMEM_LIMIT),
        cost_estimate=NO_COST,
        name="stream_back",
    )


def attn_grads(rows, width, row_groups, parts, piece):
    def kernel(place_ref, left_a, right_a, left_b, right_b, even_ref, odd_ref, turned, total):
        place = place_ref[0]
        for n, (left, right) in enumerate(((left_a, right_a), (left_b, right_b))):
            for i in range(rows // 128):
                turned[:, i * 128 : (i + 1) * 128] = low(wide(left[i * 128 : (i + 1) * 128, :]).T)
            total[:, n * width : (n + 1) * width] = dot(turned[...], right[...])
        for k in range(parts):
            ref = odd_ref if k % 2 else even_ref
            for w in range(row_groups):
                at = pl.multiple_of(w * piece * parts + (place ^ k) * piece, 8)
                ref[k // 2, w] = low(total[pl.ds(at, piece), :])

    vmem = pl.BlockSpec(memory_space=pltpu.VMEM)
    shape = jax.ShapeDtypeStruct((parts // 2, row_groups, piece, 2 * width), jnp.bfloat16)
    return pl.pallas_call(
        kernel,
        grid_spec=pltpu.PrefetchScalarGridSpec(
            num_scalar_prefetch=1,
            grid=(),
            in_specs=[vmem] * 4,
            out_specs=[vmem] * 2,
            scratch_shapes=[pltpu.VMEM((width, rows), jnp.bfloat16), pltpu.VMEM((width, 2 * width), jnp.float32)],
        ),
        out_shape=[shape] * 2,
        compiler_params=pltpu.CompilerParams(vmem_limit_bytes=VMEM_LIMIT),
        cost_estimate=NO_COST,
        name="attn_grads",
    )


def attn_update(rows, columns, width, parts, piece):
    qkv = columns - width

    def kernel(place_ref, even_ref, odd_ref, master, first, second, *outs):
        place = place_ref[0]
        for k in range(parts):
            ref = odd_ref if k % 2 else even_ref
            here = pl.ds(pl.multiple_of((place ^ k) * piece, 8), piece)
            for cols, source in (
                (slice(0, width), slice(0, width)),
                (slice(width, qkv), slice(2 * width, columns)),
                (slice(qkv, columns), slice(width, 2 * width)),
            ):
                grad = wide(ref[k // 2, :, source])
                got = adam_update(master[here, cols], grad, first[here, cols], second[here, cols], 0.1, 0.1)
                outs[0][here, cols] = got[0]
                outs[1][here, cols] = got[1]
                outs[2][here, cols] = got[2]

    vmem = pl.BlockSpec(memory_space=pltpu.VMEM)
    return pl.pallas_call(
        kernel,
        grid_spec=pltpu.PrefetchScalarGridSpec(
            num_scalar_prefetch=1, grid=(), in_specs=[vmem] * 5, out_specs=[vmem] * 3, scratch_shapes=[]
        ),
        out_shape=[jax.ShapeDtypeStruct((rows, columns), jnp.float32)] * 3,
        compiler_params=pltpu.CompilerParams(vmem_limit_bytes=VMEM_LIMIT),
        cost_estimate=NO_COST,
        name="attn_update",
    )


def ffn_update(rows, units, parts, chunk):
    per_row = 2 * units // 128
    rows_once = 32
    lines = rows_once * per_row

    def kernel(place_ref, even, odd, master, first, second, first_out, second_out, master_out, total):
        place = place_ref[0]
        for k in range(parts):
            grad = odd if k % 2 else even
            for j in range(chunk // 128):
                for which in range(2):
                    line = (place ^ k) * (2 * chunk // 128) + 2 * j + which
                    total[pl.ds(line, rows_once, per_row), :] = wide(
                        grad[k // 2, which, :, j * 128 : (j + 1) * 128]
                    )
        for t in range(lines // 64):
            own = slice(t * 64, (t + 1) * 64)
            got = adam_update(master[own, :], total[own, :], first[own, :], second[own, :], 0.1, 0.1)
            first_out[own, :] = got[0]
            second_out[own, :] = got[1]
            master_out[own, :] = got[2]

    block = pl.BlockSpec((lines, 128), lambda i, *_: (i, 0))
    stack = pl.BlockSpec((parts // 2, 2, rows_once, chunk), lambda i, *_: (0, 0, i, 0))
    call = pl.pallas_call(
        kernel,
        grid_spec=pltpu.PrefetchScalarGridSpec(
            num_scalar_prefetch=1,
            grid=(rows // rows_once,),
            in_specs=[stack] * 2 + [block] * 3,
            out_specs=[block] * 3,
            scratch_shapes=[pltpu.VMEM((lines, 128), jnp.float32)],
        ),
        out_shape=[jax.ShapeDtypeStruct((rows * per_row, 128), jnp.float32)] * 3,
        compiler_params=pltpu.CompilerParams(vmem_limit_bytes=VMEM_LIMIT),
        cost_estimate=NO_COST,
        name="ffn_update",
    )

    def fold(array):
        return jnp.swapaxes(array.reshape(rows, 2, units // 128, 128), 1, 2).reshape(-1, 128)

    def unfold(array):
        return jnp.swapaxes(array.reshape(rows, units // 128, 2, 128), 1, 2).reshape(rows, 2, units)

    def run(place, even, odd, master, first, second):
        return tuple(unfold(array) for array in call(place, even, odd, fold(master), fold(first), fold(second)))

    return run


def shards(
    tokens,
    doc_starts,
    attn_master,
    attn_mom,
    attn_sq,
    ffn_master,
    ffn_mom,
    ffn_sq,
    small_master,
    small_mom,
    small_sq,
    cotangent,
):
    ctx_count, wt_count = lax.axis_size("ctx"), lax.axis_size("wt")
    ctx_place, wt_place = lax.axis_index("ctx"), lax.axis_index("wt")
    batches, rows_here, width = tokens.shape
    qkv_cols = width + 2 * HS
    attn_columns = attn_master.shape[1]
    all_rows = batches * rows_here
    shard_rows = attn_master.shape[0]
    piece_rows = shard_rows // ctx_count
    chunk = FF // ctx_count
    chips = ctx_count // 2
    order = ctx_place ^ jnp.arange(ctx_count, dtype=jnp.int32)
    (
        gain_one,
        shift_one,
        gain_two,
        shift_two,
        bias_query,
        bias_out,
        bias_proj,
        bias_value,
        bias_hidden,
    ) = split_small(small_master)
    runs = 2 if batches % 2 == 0 else 1
    places = [jnp.stack([ctx_place, jnp.int32(run * (batches // runs))]) for run in range(runs)]
    place = places[0]
    wt_half = wt_count // 2
    out_rows = shard_rows // chips
    run_forward, run_backward = attention_kernels(batches, rows_here, width, ctx_count, runs)
    ffn_first, ffn_second, ffn_third, ffn_down = ffn_kernels(all_rows, width, chunk, wt_count)
    step = Steps()

    def both(own, got, place, bit, axis=0):
        ahead, behind = jnp.stack([own, got], axis), jnp.stack([got, own], axis)
        return jnp.where((place & bit) == 0, ahead, behind)

    def in_order(even, odd):
        buffer = jnp.zeros((ctx_count,) + even.shape[1:], even.dtype)
        for m in range(chips):
            buffer = put(buffer, even[m][None], ctx_place ^ (2 * m), 0)
            buffer = put(buffer, odd[m][None], ctx_place ^ (2 * m + 1), 0)
        return buffer

    def send_chips(piece):
        return [xor_send(piece, mask) for mask in range(2, ctx_count, 2)]

    def split_wt(total, bit):
        ahead, behind = jnp.split(total, 2)
        kept, sent = jnp.where((wt_place & bit) == 0, ahead, behind), jnp.where((wt_place & bit) == 0, behind, ahead)
        return kept, sent

    def add_low(*arrays):
        return low(sum(wide(array) for array in arrays))

    qkv = low(lax.dynamic_slice(attn_master, (ctx_place * piece_rows, 0), (piece_rows, qkv_cols)))
    qkv_got = xor_wt(qkv, 1)

    def cut_rest(ffn, attn):
        ffn = jnp.swapaxes(take(ffn, ctx_place, 2, chunk), 0, 1).reshape(2 * shard_rows, chunk)
        out = lax.dynamic_slice(
            attn, (ctx_place // 2 * out_rows, qkv_cols + ctx_place % 2 * chunk), (out_rows, chunk)
        )
        return low(jnp.concatenate([ffn, out]))

    rest = cut_rest(ffn_master, attn_master)
    rest_got = xor_wt(rest, 1)
    back_low = cotangent.reshape(all_rows, width)
    back_other = xor_send(back_low, 1)
    flat_tokens = tokens.reshape(all_rows, width)
    wt_bits = [1 << n for n in reversed(range(wt_count.bit_length() - 1))]
    qkv = both(qkv, qkv_got, wt_place, 1)
    for bit in wt_bits[::-1][1:]:
        qkv_got = xor_wt(qkv, bit)
        rest = both(rest, rest_got, wt_place, 1) if rest.ndim == 2 else rest
        rest_got = xor_wt(rest, bit)
        qkv = both(qkv, qkv_got, wt_place, bit).reshape((-1,) + qkv.shape[1:])
    qkv_got = xor_send(qkv, 2)
    normed_low = step(
        lambda tokens, gain, shift: low(layer_norm(wide(tokens), gain, shift)), flat_tokens, gain_one, shift_one
    )
    qkv = both(qkv, qkv_got, ctx_place, 2)
    qkv_got = xor_send(qkv, 4)
    back_turned = step(turn_both, back_low, back_other)
    qkv = step(lambda own, got: both(own, got, ctx_place, 4), qkv, qkv_got)
    qkv_got = xor_send(qkv, 1)

    def project(own, got, normed):
        blocks = both(own, got, ctx_place, 1, 2)
        weight = jnp.transpose(blocks, (3, 0, 1, 2, 4, 5)).reshape(width, qkv_cols)
        mixed = dot(normed, weight)
        queries = low(mixed[:, :width] + bias_query).reshape(batches, rows_here, width)
        kv_bias = jnp.concatenate([jnp.zeros((HS,), jnp.float32), bias_value])
        kv_local = low(mixed[:, width:] + kv_bias).reshape(batches, rows_here, 2 * HS)
        return weight, queries, kv_local

    weight_qkv, queries, kv_local = step(project, qkv, qkv_got, normed_low)
    kv_got = xor_send(kv_local, 2)
    kv_even = both(kv_local, kv_got, ctx_place, 2)
    kv_got = xor_send(kv_even, 4)

    def last_rest(rest, got, rows):
        ahead, behind = jnp.concatenate([rest[:, rows], got[:, rows]]), jnp.concatenate([got[:, rows], rest[:, rows]])
        return jnp.where((wt_place & wt_bits[0]) == 0, ahead, behind)

    ffn_slice, out_slice = slice(0, 2 * shard_rows), slice(2 * shard_rows, 2 * shard_rows + out_rows)
    out_own = last_rest(rest, rest_got, out_slice)
    out_got = send_chips(out_own)
    kv_even = both(kv_even, kv_got, ctx_place, 4).reshape((chips,) + kv_local.shape)
    kv_odd = xor_send(kv_even, 1)
    kv_even, rest, rest_got = lax.optimization_barrier((kv_even, rest, rest_got))
    rest = last_rest(rest, rest_got, ffn_slice)
    rest_x, rest_y = xor_send(rest, 2), xor_send(rest, 4)
    out_even = step(lambda *parts: jnp.stack(parts), out_own, *out_got)
    out_odd = xor_send(out_even, 1)
    queries, out_even, back_turned, rest = lax.optimization_barrier((queries, out_even, back_turned, rest))

    attended_low, attended, logs = step(run_forward, doc_starts, place, queries, kv_even, kv_odd)
    attended_low = attended_low.reshape(all_rows, width)
    low_half, high_half = step(lambda x, y: (x[:wt_half], y[wt_half:]), rest_x, rest_y)
    diagonal_low, diagonal_high = xor_send(low_half, 4), xor_send(high_half, 2)

    def join_out(even, odd):
        columns = jnp.where((ctx_place & 1) == 0, jnp.concatenate([even, odd], axis=3), jnp.concatenate([odd, even], axis=3))
        for n in range(chips.bit_length() - 1):
            pairs = columns.reshape((-1, 2, 1 << n) + columns.shape[1:])
            columns = jnp.where((ctx_place & (2 << n)) == 0, pairs, pairs[:, ::-1]).reshape(columns.shape)
        return jnp.swapaxes(columns, 0, 1).reshape(width, width)

    weight_out = step(join_out, out_even, out_odd)
    hidden, normed_two = step(
        out_projection(all_rows, width), attended_low, weight_out, flat_tokens, bias_out[None], gain_two[None],
        shift_two[None],
    )
    normed_other = xor_send(normed_two, 1)

    bias_parts = bias_hidden.reshape(ctx_count, chunk)[order[::2]].reshape(1, chips * chunk)
    bias_near, bias_far = jnp.split(bias_parts, 2, axis=1)
    weights = [rest, rest_x, rest_y, diagonal_low, diagonal_high]
    flows = (normed_two, normed_other, back_low, back_other, back_turned)
    act_first, units_first, down_own, down_x, sums_first = step(
        lambda *args: ffn_first(*args[:6], *in_hbm(args[6:])), *flows, bias_near, *weights[:2]
    )
    act_second, units_second, down_y, down_top, down_bottom, sums_second, back_own, back_part = step(
        lambda *args: ffn_second(*args[:6], *in_hbm(args[6:])), *flows, bias_far, units_first, *weights
    )
    back_got = xor_send(back_part, 1)
    top_got, bottom_got = xor_send(down_top, 4), xor_send(down_bottom, 2)

    def meet(along_x, along_y, top, bottom):
        half = width // 2
        return (
            jnp.concatenate([add_low(along_x[:half], top), along_x[half:]]),
            jnp.concatenate([along_y[:half], add_low(along_y[half:], bottom)]),
        )

    up_own, up_x, up_y, up_top, up_bottom = step(
        lambda *args: ffn_third(*args[:2], *in_hbm(args[2:])), normed_two, normed_other, units_first, units_second
    )
    down_x, down_y = step(meet, down_x, down_y, top_got, bottom_got)
    down_got = [xor_send(down_x, 2), xor_send(down_y, 4)]
    top_got, bottom_got = xor_send(up_top, 4), xor_send(up_bottom, 2)

    grad_hidden, grad_hidden_low, grad_attended, hidden_sums = step(
        hidden_back(all_rows, width), back_own, back_got, hidden, back_low, gain_two[None], weight_out
    )
    grad_attended = grad_attended.reshape(batches, rows_here, width)
    up_x, up_y = step(meet, up_x, up_y, top_got, bottom_got)
    up_got = [xor_send(up_x, 2), xor_send(up_y, 4)]

    def by_wt(own, *got):
        total = add_low(own, *got)
        return split_wt(total.reshape(wt_count, shard_rows, chunk), wt_bits[0])

    def next_wt(bit):
        return lambda kept, got: split_wt(add_low(kept, got), bit)

    backs = [step(run_backward[0], doc_starts, places[0], queries, kv_even, kv_odd, attended, logs, grad_attended)]
    kv_got = [xor_send(backs[0][2], 1)]
    down_kept, down_sent = step(by_wt, down_own, *down_got)
    down_got = xor_wt(down_sent, wt_bits[0])
    backs += [
        step(run_backward[run], doc_starts, places[run], queries, kv_even, kv_odd, attended, logs, grad_attended)
        for run in range(1, runs)
    ]
    kv_got += [xor_send(back[2], 1) for back in backs[1:]]
    grad_query = jnp.concatenate([back[0] for back in backs]).reshape(all_rows, width)

    def kv_pieces(evens, odds):
        total = jnp.concatenate([add_low(a, b) for a, b in zip(evens, odds)], axis=1)
        return [lax.dynamic_index_in_dim(total, (ctx_place // 2) ^ m, 0, False) for m in range(chips)]

    for bit in wt_bits[1:]:
        down_kept, down_sent = step(next_wt(bit), down_kept, down_got)
        down_got = xor_wt(down_sent, bit)
    up_kept, up_sent = step(by_wt, up_own, *up_got)
    up_got = xor_wt(up_sent, wt_bits[0])
    kv_half = step(kv_pieces, [back[1] for back in backs], kv_got)
    kv_got = [xor_send(kv_half[m], 2 * m) for m in range(1, chips)]
    wide_even, wide_odd = step(
        attn_grads(all_rows, width, wt_count, ctx_count, piece_rows),
        place, normed_low, grad_query, attended_low, grad_hidden_low,
    )
    down_part = step(add_low, down_kept, down_got)

    small_size = small_master.shape[0]
    input_grad, tail_even, tail_odd = step(
        stream_back(all_rows, width, ctx_count, wt_count, piece_rows),
        place, *[array.reshape(all_rows, 2 * HS) for array in (kv_half[0], *kv_got)], grad_query, weight_qkv,
        flat_tokens, gain_one[None], grad_hidden, normed_low, back_low, hidden_sums, sums_first, sums_second,
    )
    input_grad = input_grad.reshape(batches, rows_here, width)
    wide_odd, tail_odd = lax.optimization_barrier((wide_odd, tail_odd))
    wide_odd, tail_odd = xor_send(wide_odd, 1), xor_send(tail_odd, 1)
    for bit in wt_bits[1:]:
        up_kept, up_sent = step(next_wt(bit), up_kept, up_got)
        up_got = xor_wt(up_sent, bit)

    def attn_pieces(wide_even, wide_odd, tail_even, tail_odd):
        total = jnp.concatenate([add_low(wide_even, wide_odd), add_low(tail_even, tail_odd)], axis=3)
        return [total[m] for m in range(chips)]

    attn_half = step(attn_pieces, wide_even, wide_odd, tail_even, tail_odd)
    attn_got = [xor_send(attn_half[m], 2 * m) for m in range(1, chips)]
    ffn_part = step(
        lambda up_kept, up_got, down_part: jnp.concatenate([add_low(up_kept, up_got), down_part]),
        up_kept, up_got, down_part,
    )
    ffn_got = send_chips(ffn_part)
    down_out, down_other = step(
        lambda *args: ffn_down(*args[:2], *in_hbm(args[2:])), act_first, act_second, *weights
    )
    down_other = xor_send(down_other, 1)

    def attn_by_wt(*parts):
        return split_wt(add_low(*parts), wt_bits[0])

    attn_kept, attn_sent = step(attn_by_wt, attn_half[0], *attn_got)
    attn_got = xor_wt(attn_sent, wt_bits[0])
    ffn_even = step(lambda *parts: jnp.stack(parts), ffn_part, *ffn_got)
    ffn_odd = xor_send(ffn_even, 1)
    layer_out = step(
        lambda hidden, own, got: low(hidden + own + wide(got) + bias_proj).reshape(batches, rows_here, width),
        hidden, down_out, down_other,
    )
    for bit in wt_bits[1:]:
        attn_kept, attn_sent = step(next_wt(bit), attn_kept, attn_got)
        attn_got = xor_wt(attn_sent, bit)
    attn_part = step(lambda *parts: add_low(*parts)[0], attn_kept, attn_got)
    attn_got = send_chips(attn_part)
    attn_even = step(lambda *parts: jnp.stack(parts), attn_part, *attn_got)
    attn_odd = xor_send(attn_even, 1)

    ffn_new = step(
        ffn_update(shard_rows, FF, ctx_count, chunk), place, ffn_even, ffn_odd, ffn_master, ffn_mom, ffn_sq
    )
    small_total = in_order(attn_even[..., attn_columns:], attn_odd[..., attn_columns:])
    small_total = wide(small_total.reshape(-1))
    most = small_size - FF - HS
    small_total = jnp.concatenate(
        [small_total[:most], small_total[most + HS : most + 2 * HS], small_total[most + 2 * HS : most + 2 * HS + FF]]
    )
    small_new = adam_update(small_master, small_total, small_mom, small_sq, 1.0, 0.0)
    attn_new = attn_update(shard_rows, attn_columns, width, ctx_count, piece_rows)(
        place, attn_even, attn_odd, attn_master, attn_mom, attn_sq
    )
    return (layer_out, input_grad) + tuple(attn_new) + tuple(ffn_new) + tuple(small_new)


def shift_wt(array, shift):
    count = lax.axis_size("wt")
    return lax.ppermute(array, "wt", [(i, (i + shift) % count) for i in range(count)])


def whole_wt(piece, axis):
    count, place = lax.axis_size("wt"), lax.axis_index("wt")
    shape = list(piece.shape)
    shape[axis] *= count
    buffer = put(jnp.zeros(shape, piece.dtype), piece, place, axis)
    for shift in range(1, count):
        buffer = put(buffer, shift_wt(piece, shift), (place - shift) % count, axis)
    return buffer


def whole_ctx(piece):
    count = lax.axis_size("ctx")
    got = {0: piece}
    for mask in range(2, count, 2):
        got[mask] = xor_send(piece, mask)
    for mask in range(0, count, 2):
        got[mask + 1] = xor_send(got[mask], 1)
    return [got[mask] for mask in range(count)]


def sum_ctx(pieces):
    count = lax.axis_size("ctx")
    half = {}
    for mask in range(count - 2, -1, -2):
        other = xor_send(pieces[mask + 1], 1)
        half[mask] = low(wide(pieces[mask]) + wide(other))
    total = wide(half[0])
    for mask in range(2, count, 2):
        total = total + wide(xor_send(half[mask], mask))
    return total


def sum_wt(array, axis):
    count, place = lax.axis_size("wt"), lax.axis_index("wt")
    size = array.shape[axis] // count
    total = wide(take(array, place, axis, size))
    for shift in range(1, count):
        sent = take(array, (place + shift) % count, axis, size)
        total = total + wide(shift_wt(sent, shift))
    return total


def any_shards(
    tokens,
    doc_starts,
    attn_master,
    attn_mom,
    attn_sq,
    ffn_master,
    ffn_mom,
    ffn_sq,
    small_master,
    small_mom,
    small_sq,
    cotangent,
):
    ctx_count = lax.axis_size("ctx")
    ctx_place = lax.axis_index("ctx")
    wt_count = lax.axis_size("wt")
    batches, rows_here, width = tokens.shape
    heads = width // HS
    qkv_cols = width + 2 * HS
    all_rows = batches * rows_here
    shard_rows = attn_master.shape[0]
    piece_rows = shard_rows // ctx_count
    chunk = FF // ctx_count
    order = ctx_place ^ jnp.arange(ctx_count, dtype=jnp.int32)
    (
        gain_one,
        shift_one,
        gain_two,
        shift_two,
        bias_query,
        bias_out,
        bias_proj,
        bias_value,
        bias_hidden,
    ) = split_small(small_master)

    attn_piece = low(take(attn_master, ctx_place, 0, piece_rows))

    def whole_rows(piece):
        parts = whole_ctx(whole_wt(piece[None], 0))
        buffer = jnp.zeros((wt_count, ctx_count) + piece.shape, piece.dtype)
        for k, part in enumerate(parts):
            buffer = put(buffer, part[:, None], ctx_place ^ k, 1)
        return buffer.reshape((width,) + piece.shape[1:])

    weight_qkv = whole_rows(attn_piece[:, :qkv_cols])
    weight_out = whole_rows(attn_piece[:, qkv_cols:])
    ffn_piece = low(jnp.swapaxes(take(ffn_master, ctx_place, 2, chunk), 0, 1))
    ffn_parts = whole_ctx(whole_wt(ffn_piece, 1))
    bias_parts = bias_hidden.reshape(ctx_count, chunk)[order]

    stream = wide(tokens.reshape(all_rows, width))
    normed, norm_back_one = jax.vjp(layer_norm, stream, gain_one, shift_one)
    normed_low = low(normed)
    mixed = dot(normed_low, weight_qkv)
    queries = low(mixed[:, :width] + bias_query)
    kv_local = low(
        mixed[:, width:] + jnp.concatenate([jnp.zeros((HS,), jnp.float32), bias_value])
    ).reshape(batches, rows_here, 2 * HS)
    kv_parts = jnp.stack(whole_ctx(kv_local), axis=1).reshape(
        batches, ctx_count * rows_here, 2 * HS
    )
    keys_all, values_all = kv_parts[..., :HS], kv_parts[..., HS:]
    local_pos = jnp.arange(rows_here, dtype=jnp.int32)
    query_pos = ctx_place * rows_here + local_pos
    key_pos = (order[:, None] * rows_here + local_pos[None, :]).reshape(-1)
    queries = queries.reshape(batches, rows_here * heads, HS)
    scale = HS ** (-0.5)
    attended_list, log_list, allowed_list = [], [], []
    for b in range(batches):
        starts = doc_starts[b]
        query_doc = jnp.sum((starts[None, :] <= query_pos[:, None]).astype(jnp.int32), axis=1)
        key_doc = jnp.sum((starts[None, :] <= key_pos[:, None]).astype(jnp.int32), axis=1)
        allowed = (query_doc[:, None] == key_doc[None, :]) & (key_pos[None, :] <= query_pos[:, None])
        allowed = jnp.repeat(allowed, heads, axis=0)
        allowed_list.append(allowed)
        scores = jnp.where(allowed, cols_dot(queries[b], keys_all[b]) * scale, -1e30)
        peak = jnp.max(scores, axis=-1, keepdims=True)
        expo = jnp.exp(scores - peak)
        total = jnp.sum(expo, axis=-1, keepdims=True)
        attended_list.append(dot(low(expo / total), values_all[b]))
        log_list.append(peak + jnp.log(total))
    attended = jnp.stack(attended_list)
    attended_low = low(attended).reshape(all_rows, width)
    hidden = stream + dot(attended_low, weight_out) + bias_out
    normed_two, norm_back_two = jax.vjp(layer_norm, hidden, gain_two, shift_two)
    normed_two_low = low(normed_two)

    back_low = cotangent.reshape(all_rows, width)
    back_rows = wide(back_low)
    down_vals = jnp.zeros((all_rows, width), jnp.float32)
    grad_normed_two = jnp.zeros((all_rows, width), jnp.float32)
    ffn_grads, hidden_grads = [], []
    for k in range(ctx_count):
        weight_up, weight_down = ffn_parts[k][0], ffn_parts[k][1]
        value, slope = gelu_both(dot(normed_two_low, weight_up) + bias_parts[k])
        act = low(value)
        down_vals = down_vals + cols_dot(act, weight_down)
        grad_up = low(dot(back_low, weight_down) * slope)
        hidden_grads.append(jnp.sum(wide(grad_up), axis=0))
        grad_normed_two = grad_normed_two + cols_dot(grad_up, weight_up)
        ffn_grads.append(
            jnp.stack([low(rows_dot(normed_two_low, grad_up)), low(rows_dot(back_low, act))])
        )
    layer_out = low(hidden + down_vals + bias_proj).reshape(batches, rows_here, width)
    grad_bias_proj = jnp.sum(back_rows, axis=0)
    grad_bias_hidden = jnp.stack(hidden_grads)[order].reshape(FF)
    ffn_part = low(sum_wt(low(sum_ctx(ffn_grads)), 1))

    grad_hidden_part, grad_gain_two, grad_shift_two = norm_back_two(grad_normed_two)
    grad_hidden = back_rows + grad_hidden_part
    grad_bias_out = jnp.sum(grad_hidden, axis=0)
    grad_hidden_low = low(grad_hidden)
    grad_out = rows_dot(attended_low, grad_hidden_low)

    def summed_rows(grad):
        blocks = low(grad).reshape(wt_count, ctx_count, piece_rows, grad.shape[1])
        pieces = [take(blocks, ctx_place ^ k, 1, 1)[:, 0] for k in range(ctx_count)]
        part = low(sum_wt(low(sum_ctx(pieces)), 0)[0])
        buffer = jnp.zeros((ctx_count,) + part.shape, part.dtype)
        for k, got in enumerate(whole_ctx(part)):
            buffer = put(buffer, got[None], ctx_place ^ k, 0)
        return wide(buffer.reshape(shard_rows, grad.shape[1]))

    out_total = summed_rows(grad_out)

    grad_attended = low(cols_dot(grad_hidden_low, weight_out)).reshape(
        batches, rows_here * heads, HS
    )
    grad_query_list, grad_kv_list = [], []
    for b in range(batches):
        grads = grad_attended[b]
        delta = jnp.sum(wide(grads) * attended[b], axis=-1, keepdims=True)
        scores = jnp.where(allowed_list[b], cols_dot(queries[b], keys_all[b]) * scale, -1e30)
        weights = jnp.exp(scores - log_list[b])
        grad_scores = low(weights * (cols_dot(grads, values_all[b]) - delta))
        grad_query_list.append(low(dot(grad_scores, keys_all[b]) * scale))
        grad_kv_list.append(
            jnp.concatenate(
                [
                    low(rows_dot(grad_scores, queries[b]) * scale),
                    low(rows_dot(low(weights), grads)),
                ],
                axis=1,
            )
        )
    grad_query = jnp.stack(grad_query_list).reshape(all_rows, width)
    grad_kv = jnp.stack(grad_kv_list).reshape(batches, ctx_count, rows_here, 2 * HS)
    grad_kv_low = low(sum_ctx([grad_kv[:, k] for k in range(ctx_count)])).reshape(
        all_rows, 2 * HS
    )
    grad_bias_query = jnp.sum(wide(grad_query), axis=0)
    grad_bias_value = jnp.sum(wide(grad_kv_low[:, HS:]), axis=0)
    grad_mixed = jnp.concatenate([grad_query, grad_kv_low], axis=1)
    qkv_total = summed_rows(rows_dot(normed_low, grad_mixed))
    grad_normed = cols_dot(grad_mixed, weight_qkv)
    grad_stream_part, grad_gain_one, grad_shift_one = norm_back_one(grad_normed)
    input_grad = (grad_hidden + grad_stream_part).reshape(batches, rows_here, width)

    ffn_buffer = jnp.zeros((ctx_count,) + ffn_part.shape, ffn_part.dtype)
    for k, got in enumerate(whole_ctx(ffn_part)):
        ffn_buffer = put(ffn_buffer, got[None], ctx_place ^ k, 0)
    ffn_total = wide(jnp.transpose(ffn_buffer, (2, 1, 0, 3)).reshape(shard_rows, 2, FF))
    attn_total = jnp.concatenate([qkv_total, out_total], axis=1)
    grad_small = jnp.concatenate(
        [
            grad_gain_one,
            grad_shift_one,
            grad_gain_two,
            grad_shift_two,
            grad_bias_query,
            grad_bias_out,
            grad_bias_proj,
            grad_bias_value,
            grad_bias_hidden,
        ]
    )
    small_total = lax.psum(grad_small, ("ctx", "wt"))
    attn_new = adam_update(attn_master, attn_total, attn_mom, attn_sq, 0.1, 0.1)
    ffn_new = adam_update(ffn_master, ffn_total, ffn_mom, ffn_sq, 0.1, 0.1)
    small_new = adam_update(small_master, small_total, small_mom, small_sq, 1.0, 0.0)
    return (layer_out, input_grad) + attn_new + ffn_new + small_new


def solution(mesh):
    rows, cube = P("wt", None), P("wt", None, None)
    flow = P("wt", "ctx", None)
    in_specs = (flow, rows, rows, rows, rows, cube, cube, cube, P(), P(), P(), flow)
    out_specs = (flow, flow, rows, rows, rows, cube, cube, cube, P(), P(), P())
    ctx_count, wt_count = mesh.shape["ctx"], mesh.shape["wt"]
    fitted = (ctx_count, wt_count) == (8, 4)
    body = shards if fitted else any_shards
    return jax.shard_map(body, mesh=mesh, in_specs=in_specs, out_specs=out_specs, check_vma=False)
```

```python
import jax
import jax.numpy as jnp
from jax import lax
from jax.experimental import pallas as pl
from jax.experimental.pallas import tpu as pltpu
from jax.sharding import PartitionSpec as P

D = 768
HS = 64
FF = 3072
STEP = 10


NORM_EPS = 1e-05
GELU_COEF = 0.7978845608028654
GELU_CUBE = 0.044715
BETA_ONE = 0.9
BETA_TWO = 0.95
ADAM_EPS = 1e-08
VMEM_LIMIT = 22 << 20
NO_COST = pl.CostEstimate(flops=0, bytes_accessed=0, transcendentals=0)


def layer_norm(values, gain, shift):
    centre = values - jnp.mean(values, axis=-1, keepdims=True)
    spread = jnp.mean(centre * centre, axis=-1, keepdims=True)
    return centre * lax.rsqrt(spread + NORM_EPS) * gain + shift


def gelu_both(u):
    square = u * u
    share = 0.5 * jnp.tanh(u * (GELU_COEF * GELU_CUBE * square + GELU_COEF)) + 0.5
    bend = u * (6.0 * GELU_COEF * GELU_CUBE * square + 2.0 * GELU_COEF)
    return u * share, share * ((1.0 - share) * bend) + share


def split_small(small):
    return (
        small[0:D],
        small[D : 2 * D],
        small[2 * D : 3 * D],
        small[3 * D : 4 * D],
        small[4 * D : 5 * D],
        small[5 * D : 6 * D],
        small[6 * D : 7 * D],
        small[7 * D : 7 * D + HS],
        small[7 * D + HS :],
    )


def rows_dot(left, right):
    return lax.dot_general(
        left, right, (((0,), (0,)), ((), ())), preferred_element_type=jnp.float32
    )


def cols_dot(left, right):
    return lax.dot_general(
        left, right, (((1,), (1,)), ((), ())), preferred_element_type=jnp.float32
    )


def dot(left, right):
    return jnp.dot(left, right, preferred_element_type=jnp.float32)


def low(values):
    return values.astype(jnp.bfloat16)


def wide(values):
    return values.astype(jnp.float32)


def adam_update(master, gradient, first, second, step_rate, decay_rate):
    first_new = BETA_ONE * first + (1.0 - BETA_ONE) * gradient
    second_new = BETA_TWO * second + (1.0 - BETA_TWO) * gradient * gradient
    first_hat = first_new / (1.0 - BETA_ONE**STEP)
    second_hat = second_new / (1.0 - BETA_TWO**STEP)
    master_new = master - step_rate * (
        first_hat / (jnp.sqrt(second_hat) + ADAM_EPS) + decay_rate * master
    )
    return (first_new, second_new, master_new)


def xor_send(array, mask):
    count = lax.axis_size("ctx")
    return lax.ppermute(array, "ctx", [(i, i ^ mask) for i in range(count)])


def xor_wt(array, mask):
    count = lax.axis_size("wt")
    return lax.ppermute(array, "wt", [(i, i ^ mask) for i in range(count)])


class Steps:
    def __init__(self):
        self.last = ()

    def __call__(self, function, *args):
        flat, tree = jax.tree.flatten(args)
        held = lax.optimization_barrier(tuple(flat) + self.last)[: len(flat)]
        result = function(*jax.tree.unflatten(tree, held))
        self.last = tuple(jax.tree.leaves(result))
        return result


def loop(count, body, carry=0):
    return lax.fori_loop(0, count, body, carry)


def rows_at(i, size):
    return pl.ds(pl.multiple_of(i * size, size), size)


def together(*arrays):
    return lax.optimization_barrier(arrays)


def put(buffer, piece, place, axis):
    starts = [0] * buffer.ndim
    starts[axis] = place * piece.shape[axis]
    return lax.dynamic_update_slice(buffer, piece, starts)


def take(buffer, place, axis, size):
    return lax.dynamic_slice_in_dim(buffer, place * size, size, axis)


def attention_kernels(batches, rows, width, parts, runs):
    half_parts = parts // 2
    keys = parts * rows
    pair = 2 * HS
    groups = width // (2 * pair)
    factor = HS ** (-0.5) * 1.4426950408889634
    tile = 32

    def lanes(shape):
        return lax.broadcasted_iota(jnp.int32, shape, 1)

    def spread(even_ref, odd_ref, key_ref, value_ref):
        for j in range(parts):
            ref = even_ref if j < half_parts else odd_ref
            block = wide(ref[j % half_parts, 0])
            turned = pltpu.roll(block, HS, 1)
            first = lanes(block.shape) < HS
            here = pl.ds(j * rows, rows)
            key_ref[0, here, :] = low(jnp.where(first, block, 0.0))
            key_ref[1, here, :] = low(jnp.where(first, 0.0, turned))
            value_ref[0, here, :] = low(jnp.where(first, turned, 0.0))
            value_ref[1, here, :] = low(jnp.where(first, 0.0, block))

    def doc_begin(starts_ref, stream, positions):
        begin = jnp.zeros_like(positions)
        for j in range(starts_ref.shape[1]):
            start = starts_ref[stream, j]
            begin = jnp.where(start <= positions, jnp.maximum(begin, start), begin)
        return begin

    def forward(starts_ref, place_ref, query_ref, even_ref, odd_ref, low_ref, full_ref, log_ref, cap, key, value, weight):
        stream, place = pl.program_id(0), place_ref[0]
        spread(even_ref, odd_ref, key, value)
        query_pos = place * rows + lax.broadcasted_iota(jnp.int32, (rows, 1), 0)
        begin = doc_begin(starts_ref, stream, query_pos)
        for j in range(parts):
            key_pos = (2 * (j % half_parts) + (place + j // half_parts) % 2) * rows + lax.broadcasted_iota(jnp.int32, (rows, rows), 1)
            allowed = (key_pos >= begin) & (key_pos <= query_pos)
            cap[:, j * rows : (j + 1) * rows] = jnp.where(allowed, 3.0e38, -1e30)
        column = lanes((tile, pair))
        logs = [jnp.zeros((tile, pair), jnp.float32) for _ in range(rows // tile)]
        for g in range(groups):
            at = g * 2 * pair
            two = jnp.concatenate([query_ref[0, :, at : at + pair], query_ref[0, :, at + pair : at + 2 * pair]], axis=0)
            totals = []
            for half in range(2):
                scores = cols_dot(two, key[half])
                norms = []
                for t in range(2 * rows // tile):
                    own = slice(t * tile, (t + 1) * tile)
                    n = t % (rows // tile)
                    part = jnp.minimum(scores[own] * factor, cap[n * tile : (n + 1) * tile, :])
                    peak = jnp.max(part, axis=1, keepdims=True)
                    expo = jnp.exp2(part - peak)
                    norm = jnp.sum(expo, axis=1, keepdims=True)
                    weight[half, own, :] = low(expo)
                    norms.append(norm)
                    head = 4 * g + 2 * (t * tile // rows) + half
                    logs[n] = jnp.where(column == head, peak + jnp.log2(norm), logs[n])
                totals.append(dot(weight[half], value[half]) / jnp.concatenate(norms, axis=0))
            total = totals[0] + totals[1]
            for j in range(2):
                part = total[j * rows : (j + 1) * rows]
                full_ref[0, :, at + j * pair : at + (j + 1) * pair] = part
                low_ref[0, :, at + j * pair : at + (j + 1) * pair] = low(part)
        for n, log in enumerate(logs):
            log_ref[0, n * tile : (n + 1) * tile, :] = log

    def backward(
        starts_ref, place_ref, query_ref, even_ref, odd_ref, full_ref, log_ref, grad_ref,
        query_grad_ref, even_grad_ref, odd_grad_ref,
        cap, key, value, key_turned, log_rows, delta_rows, weight_buf, score_buf, query_buf, grad_buf,
    ):
        stream, place = pl.program_id(0) + place_ref[1], place_ref[0]
        spread(even_ref, odd_ref, key, value)
        query_pos = place * rows + lax.broadcasted_iota(jnp.int32, (1, rows), 1)
        begin = doc_begin(starts_ref, stream, query_pos)
        for j in range(parts):
            key_pos = (2 * (j % half_parts) + (place + j // half_parts) % 2) * rows + lax.broadcasted_iota(jnp.int32, (rows, rows), 0)
            allowed = (key_pos >= begin) & (key_pos <= query_pos)
            cap[j * rows : (j + 1) * rows, :] = jnp.where(allowed, 3.0e38, -1e30)
            here = pl.ds(j * rows, rows)
            key_turned[:, j * rows : (j + 1) * rows] = low(wide(key[0, here, :]).T[:HS])
        log_rows[...] = log_ref[0].T[: log_rows.shape[0]]
        head_of = lax.broadcasted_iota(jnp.int32, (delta_rows.shape[0], width), 1) // HS
        chosen = (head_of == lax.broadcasted_iota(jnp.int32, (delta_rows.shape[0], width), 0)).astype(jnp.float32)
        delta_rows[...] = lax.dot_general(
            chosen, wide(grad_ref[0]) * full_ref[0], (((1,), (1,)), ((), ())),
            precision=lax.Precision.HIGHEST, preferred_element_type=jnp.float32,
        )
        first = lanes((2 * rows, pair)) < HS
        for g in range(groups):
            at = g * 2 * pair
            both, both_grad = query_ref[0, :, at : at + 2 * pair], grad_ref[0, :, at : at + 2 * pair]
            two = jnp.concatenate([both[:, :pair], both[:, pair:]], axis=0)
            two_grad = jnp.concatenate([both_grad[:, :pair], both_grad[:, pair:]], axis=0)
            turned = []
            for half in range(2):
                h = 4 * g + half
                span = slice((2 * g + half) * 2 * rows, (2 * g + half + 1) * 2 * rows)
                keep = first if half == 0 else jnp.logical_not(first)
                query_buf[span, :] = low(jnp.where(keep, wide(two), 0.0))
                grad_buf[span, :] = low(jnp.where(keep, wide(two_grad), 0.0))
                log = jnp.concatenate([log_rows[h : h + 1, :], log_rows[h + 2 : h + 3, :]], axis=1)
                delta = jnp.concatenate([delta_rows[h : h + 1, :], delta_rows[h + 2 : h + 3, :]], axis=1)
                scores, weight_grads = cols_dot(key[half], two), cols_dot(value[half], two_grad)
                for t in range(keys // (2 * tile)):
                    own = slice(t * 2 * tile, (t + 1) * 2 * tile)
                    limit = cap[own, :]
                    limit = jnp.concatenate([limit, limit], axis=1)
                    weights = jnp.exp2(jnp.minimum(scores[own] * factor, limit) - log)
                    weight_buf[own, span] = low(weights)
                    score_buf[own, span] = low(weights * (weight_grads[own] - delta))
                turned.append(dot(key_turned[...], score_buf[:, span]))
            turned = jnp.concatenate(turned, axis=0) * HS ** (-0.5)
            query_grad_ref[0, :, at : at + pair] = low(turned[:, :rows].T)
            query_grad_ref[0, :, at + pair : at + 2 * pair] = low(turned[:, rows:].T)
        for j in range(parts):
            here = pl.ds(j * rows, rows)
            value_sum = dot(weight_buf[here, :], grad_buf[...])
            key_sum = dot(score_buf[here, :], query_buf[...]) * HS ** (-0.5)
            value_sum = value_sum + pltpu.roll(value_sum, HS, 1)
            key_sum = key_sum + pltpu.roll(key_sum, HS, 1)
            ref = even_grad_ref if j < half_parts else odd_grad_ref
            ref[j % half_parts, 0] = low(jnp.where(lanes((rows, pair)) < HS, key_sum, value_sum))

    def specs(first):
        return (
            pl.BlockSpec((1, rows, width), lambda b, *_: (b + first, 0, 0)),
            pl.BlockSpec((1, rows, pair), lambda b, *_: (b + first, 0, 0)),
            pl.BlockSpec((half_parts, 1, rows, pair), lambda b, *_: (0, b + first, 0, 0)),
        )

    flow, logs, blocks = specs(0)

    shared = [
        pltpu.VMEM((2, keys, pair), jnp.bfloat16),
        pltpu.VMEM((2, keys, pair), jnp.bfloat16),
    ]
    run_forward = pl.pallas_call(
        forward,
        grid_spec=pltpu.PrefetchScalarGridSpec(
            num_scalar_prefetch=2,
            grid=(batches,),
            in_specs=[flow, blocks, blocks],
            out_specs=[flow, flow, logs],
            scratch_shapes=[pltpu.VMEM((rows, keys), jnp.float32)]
            + shared
            + [pltpu.VMEM((2, 2 * rows, keys), jnp.bfloat16)],
        ),
        out_shape=[
            jax.ShapeDtypeStruct((batches, rows, width), jnp.bfloat16),
            jax.ShapeDtypeStruct((batches, rows, width), jnp.float32),
            jax.ShapeDtypeStruct((batches, rows, pair), jnp.float32),
        ],
        compiler_params=pltpu.CompilerParams(vmem_limit_bytes=VMEM_LIMIT),
        cost_estimate=NO_COST,
        name="attention_forward",
    )
    head_rows = -(-(width // HS) // 8) * 8
    all_columns = rows * (width // HS)
    count = batches // runs

    def call_backward(run):
        here_flow, here_logs, here_blocks = specs(run * count)
        return pl.pallas_call(
        backward,
        grid_spec=pltpu.PrefetchScalarGridSpec(
            num_scalar_prefetch=2,
            grid=(count,),
            in_specs=[here_flow, here_blocks, here_blocks, here_flow, here_logs, here_flow],
            out_specs=[flow, blocks, blocks],
            scratch_shapes=[pltpu.VMEM((keys, rows), jnp.float32)]
            + shared
            + [
                pltpu.VMEM((HS, keys), jnp.bfloat16),
                pltpu.VMEM((head_rows, rows), jnp.float32),
                pltpu.VMEM((head_rows, rows), jnp.float32),
                pltpu.VMEM((keys, all_columns), jnp.bfloat16),
                pltpu.VMEM((keys, all_columns), jnp.bfloat16),
                pltpu.VMEM((all_columns, pair), jnp.bfloat16),
                pltpu.VMEM((all_columns, pair), jnp.bfloat16),
            ],
        ),
        out_shape=[
            jax.ShapeDtypeStruct((count, rows, width), jnp.bfloat16),
            jax.ShapeDtypeStruct((half_parts, count, rows, pair), jnp.bfloat16),
            jax.ShapeDtypeStruct((half_parts, count, rows, pair), jnp.bfloat16),
        ],
        compiler_params=pltpu.CompilerParams(vmem_limit_bytes=VMEM_LIMIT),
        cost_estimate=NO_COST,
        name="attention_backward",
    )

    return run_forward, [call_backward(run) for run in range(runs)]


def in_hbm(arrays):
    return [pltpu.with_memory_space_constraint(array, pltpu.HBM) for array in arrays]


def ffn_kernels(rows, width, chunk, wt_count):
    units = 2 * chunk
    all_rows = 2 * rows
    block_rows = width // wt_count
    hbm = pl.BlockSpec(memory_space=pltpu.HBM)
    vmem = pl.BlockSpec(memory_space=pltpu.VMEM)
    params = pltpu.CompilerParams(vmem_limit_bytes=VMEM_LIMIT)

    def fetch(weights, which, held, sem):
        copies = []
        for n, arrays in enumerate(weights):
            blocks = [array.at[block] for array in arrays for block in range(array.shape[0])]
            for row, block in enumerate(blocks):
                copies.append(
                    pltpu.make_async_copy(
                        block.at[pl.ds(which * block_rows, block_rows), :],
                        held.at[pl.ds(row * block_rows, block_rows), pl.ds(n * chunk, chunk)],
                        sem.at[len(copies)],
                    )
                )
        for copy in copies:
            copy.start()
        return copies

    def send(pairs, sems):
        copies = [pltpu.make_async_copy(source, out, sems.at[n]) for n, (source, out) in enumerate(pairs)]
        for copy in copies:
            copy.start()
        return copies

    part_rows = 256
    tile = 16

    def units_of(inputs, grads, bias, held_up, held_down, act, grad_units):
        sums = jnp.zeros((8, units), jnp.float32)
        for s in range(2):

            def part(i, sums):
                here = rows_at(i, part_rows)
                up = dot(inputs[s][here, :], held_up[...])
                act_grad = dot(grads[s][here, :], held_down[...])
                for t in range(part_rows // tile):
                    own = slice(t * tile, (t + 1) * tile)
                    there = pl.ds(pl.multiple_of(s * rows + i * part_rows + t * tile, tile), tile)
                    value, slope = gelu_both(up[own] + bias)
                    grad = act_grad[own] * slope
                    act[there, :] = low(value)
                    grad_units[there, :] = low(grad)
                    sums = sums + (grad[:8] + grad[8:])
                return sums

            sums = loop(rows // part_rows, part, sums)
        return jnp.sum(sums, axis=0, keepdims=True)

    def product_of(turned, right, product):
        def part(i, carry):
            here = rows_at(i, part_rows)
            product[here, :] = low(dot(turned[here, :], right[...]))
            return carry

        loop(width // part_rows, part)

    def back_to(refs, sources, weights):
        for s, ref in enumerate(refs):

            def part(i, carry):
                here = pl.ds(pl.multiple_of(s * rows + i * part_rows, part_rows), part_rows)
                total = cols_dot(sources[0][here, :], weights[0][...]) + cols_dot(sources[1][here, :], weights[1][...])
                ref[rows_at(i, part_rows), :] = total.astype(ref.dtype)
                return carry

            loop(rows // part_rows, part)

    def halves(product, m):
        cols = pl.ds(m * chunk, chunk)
        return [product.at[pl.ds(h * width // 2, width // 2), cols] for h in range(2)]

    def first(
        own, other, grad_own, grad_other, turned, bias, w0, w1,
        act_out, units_out, out_a, out_b, sums_out,
        held_up, held_down, act, grad_units, product, sems, out_sems,
    ):
        weights = ((w0,), (w1,))
        copies = fetch(weights, 0, held_up, sems.at[0]) + fetch(weights, 1, held_down, sems.at[1])
        for copy in copies:
            copy.wait()
        sums_out[...] = units_of((own, other), (grad_own, grad_other), bias[...], held_up, held_down, act, grad_units)
        sent = send(((act, act_out), (grad_units, units_out)), out_sems.at[0])
        product_of(turned, act, product)
        sent += send(
            ((product.at[:, pl.ds(0, chunk)], out_a), (product.at[:, pl.ds(chunk, chunk)], out_b)), out_sems.at[1]
        )
        for copy in sent:
            copy.wait()

    def second(
        own, other, grad_own, grad_other, turned, bias, units_first, w0, w1, w2, w3, w4,
        act_out, units_out, out_a, out_b, out_c, sums_out, back_own, back_other,
        held_up, held_more, held_down, act, grad_units, more_units, product, sems, out_sems, more_sem,
    ):
        weights, before = ((w2,), (w3, w4)), ((w0,), (w1,))
        copies = fetch(weights, 0, held_up, sems.at[0]) + fetch(weights, 1, held_down, sems.at[1])
        more = fetch(before, 0, held_more, sems.at[2])
        more.append(pltpu.make_async_copy(units_first, more_units, more_sem))
        more[-1].start()
        for copy in copies:
            copy.wait()
        sums_out[...] = units_of((own, other), (grad_own, grad_other), bias[...], held_up, held_down, act, grad_units)
        sent = send(((act, act_out), (grad_units, units_out)), out_sems.at[0])
        product_of(turned, act, product)
        top, bottom = halves(product, 1)
        sent += send(((product.at[:, pl.ds(0, chunk)], out_a), (top, out_b), (bottom, out_c)), out_sems.at[1])
        for copy in more:
            copy.wait()
        back_to((back_own, back_other), (grad_units, more_units), (held_up, held_more))
        for copy in sent:
            copy.wait()

    def third(own, other, units_a, units_b, out_0, out_1, out_2, out_3, out_4, turned, held, products, sems, out_sems):
        copies = send(((units_a, held.at[0]), (units_b, held.at[1])), sems)
        turn((own, other), turned)
        for copy in copies:
            copy.wait()
        product_of(turned, held.at[1], products.at[1])
        top, bottom = halves(products.at[1], 1)
        sent = send(((products.at[1, :, pl.ds(0, chunk)], out_2), (top, out_3), (bottom, out_4)), out_sems.at[0])
        product_of(turned, held.at[0], products.at[0])
        sent += send(
            ((products.at[0, :, pl.ds(0, chunk)], out_0), (products.at[0, :, pl.ds(chunk, chunk)], out_1)),
            out_sems.at[1],
        )
        for copy in sent:
            copy.wait()

    def down(act_a, act_b, w0, w1, w2, w3, w4, own_ref, other_ref, held_a, held_b, sems):
        copies = fetch(((w0,), (w1,)), 1, held_a, sems.at[0]) + fetch(((w2,), (w3, w4)), 1, held_b, sems.at[1])
        for copy in copies:
            copy.wait()
        back_to((own_ref, other_ref), (act_a, act_b), (held_a, held_b))

    dma = pltpu.SemaphoreType.DMA
    held = pltpu.VMEM((width, units), jnp.bfloat16)
    flow = pltpu.VMEM((all_rows, units), jnp.bfloat16)
    flow_out = pltpu.HBM((all_rows, units), jnp.bfloat16)
    whole = pltpu.HBM((width, chunk), jnp.bfloat16)
    part = pltpu.HBM((width // 2, chunk), jnp.bfloat16)
    sums = jax.ShapeDtypeStruct((1, units), jnp.float32)
    own = jax.ShapeDtypeStruct((rows, width), jnp.float32)
    other = jax.ShapeDtypeStruct((rows, width), jnp.bfloat16)
    run_first = pl.pallas_call(
        first,
        in_specs=[vmem] * 6 + [hbm] * 2,
        out_specs=[hbm] * 4 + [vmem],
        out_shape=[flow_out, flow_out, whole, whole, sums],
        scratch_shapes=[held, held, flow, flow, held, dma((2, 2 * wt_count)), dma((2, 2))],
        compiler_params=params,
        cost_estimate=NO_COST,
        name="ffn_first",
    )
    run_second = pl.pallas_call(
        second,
        in_specs=[vmem] * 6 + [hbm] * 6,
        out_specs=[hbm] * 5 + [vmem] * 3,
        out_shape=[flow_out, flow_out, whole, part, part, sums, own, other],
        scratch_shapes=[held, held, held, flow, flow, flow, held, dma((3, 2 * wt_count)), dma((2, 3)), dma(())],
        compiler_params=params,
        cost_estimate=NO_COST,
        name="ffn_second",
    )
    run_third = pl.pallas_call(
        third,
        in_specs=[vmem] * 2 + [hbm] * 2,
        out_specs=[hbm] * 5,
        out_shape=[whole, whole, whole, part, part],
        scratch_shapes=[
            pltpu.VMEM((width, all_rows), jnp.bfloat16),
            pltpu.VMEM((2, all_rows, units), jnp.bfloat16),
            pltpu.VMEM((2, width, units), jnp.bfloat16),
            dma((2,)),
            dma((2, 3)),
        ],
        compiler_params=params,
        cost_estimate=NO_COST,
        name="ffn_grads",
    )
    run_down = pl.pallas_call(
        down,
        in_specs=[vmem] * 2 + [hbm] * 5,
        out_specs=[vmem] * 2,
        out_shape=[own, other],
        scratch_shapes=[held, held, dma((2, 2 * wt_count))],
        compiler_params=params,
        cost_estimate=NO_COST,
        name="ffn_down",
    )
    return run_first, run_second, run_third, run_down


def turn(refs, turned):
    rows = refs[0].shape[0]
    for s, ref in enumerate(refs):
        for i in range(rows // 128):
            block = wide(ref[i * 128 : (i + 1) * 128, :])
            turned[:, s * rows + i * 128 : s * rows + (i + 1) * 128] = low(block.T)


def turn_both(own, other):
    vmem = pl.BlockSpec(memory_space=pltpu.VMEM)
    rows, width = own.shape
    return pl.pallas_call(
        lambda a, b, out: turn((a, b), out),
        in_specs=[vmem] * 2,
        out_specs=vmem,
        out_shape=jax.ShapeDtypeStruct((width, 2 * rows), own.dtype),
        compiler_params=pltpu.CompilerParams(vmem_limit_bytes=VMEM_LIMIT),
        cost_estimate=NO_COST,
        name="turn",
    )(own, other)


def out_projection(rows, width):
    tile = 32

    def kernel(attended, weight, stream, bias, gain, shift, hidden_ref, normed_ref):
        product = dot(attended[...], weight[...])
        for t in range(rows // tile):
            here = slice(t * tile, (t + 1) * tile)
            hidden = wide(stream[here, :]) + product[here] + bias[...]
            hidden_ref[here, :] = hidden
            normed_ref[here, :] = low(layer_norm(hidden, gain[...], shift[...]))

    vmem = pl.BlockSpec(memory_space=pltpu.VMEM)
    return pl.pallas_call(
        kernel,
        in_specs=[vmem] * 6,
        out_specs=[vmem] * 2,
        out_shape=[
            jax.ShapeDtypeStruct((rows, width), jnp.float32),
            jax.ShapeDtypeStruct((rows, width), jnp.bfloat16),
        ],
        compiler_params=pltpu.CompilerParams(vmem_limit_bytes=VMEM_LIMIT),
        cost_estimate=NO_COST,
        name="out_projection",
    )


def norm_back(values, gain, grad):
    centre = values - jnp.mean(values, axis=-1, keepdims=True)
    scale = lax.rsqrt(jnp.mean(centre * centre, axis=-1, keepdims=True) + NORM_EPS)
    unit = centre * scale
    inner = grad * gain
    mean = jnp.mean(inner, axis=-1, keepdims=True)
    along = jnp.mean(inner * unit, axis=-1, keepdims=True)
    return scale * (inner - mean - unit * along), grad * unit


def fold_rows(values):
    total = values[:8]
    for i in range(1, values.shape[0] // 8):
        total = total + values[i * 8 : (i + 1) * 8]
    return total


def hidden_back(rows, width):
    tile = 32

    def kernel(own, got, hidden, back, gain, weight, grad_ref, low_ref, attended_ref, sums_ref):
        sums = [jnp.zeros((8, width), jnp.float32) for _ in range(3)]
        for t in range(rows // tile):
            here = slice(t * tile, (t + 1) * tile)
            pulled, terms = norm_back(hidden[here, :], gain[...], own[here, :] + wide(got[here, :]))
            grad = wide(back[here, :]) + pulled
            grad_ref[here, :] = grad
            low_ref[here, :] = low(grad)
            for n, part in enumerate((terms, own[here, :] + wide(got[here, :]), grad)):
                sums[n] = sums[n] + fold_rows(part)
        for n in range(3):
            sums_ref[n : n + 1, :] = jnp.sum(sums[n], axis=0, keepdims=True)
        attended_ref[...] = low(cols_dot(low_ref[...], weight[...]))

    vmem = pl.BlockSpec(memory_space=pltpu.VMEM)
    return pl.pallas_call(
        kernel,
        in_specs=[vmem] * 6,
        out_specs=[vmem] * 4,
        out_shape=[
            jax.ShapeDtypeStruct((rows, width), jnp.float32),
            jax.ShapeDtypeStruct((rows, width), jnp.bfloat16),
            jax.ShapeDtypeStruct((rows, width), jnp.bfloat16),
            jax.ShapeDtypeStruct((3, width), jnp.float32),
        ],
        compiler_params=pltpu.CompilerParams(vmem_limit_bytes=VMEM_LIMIT),
        cost_estimate=NO_COST,
        name="hidden_back",
    )


def stream_back(rows, width, parts, row_groups, piece):
    tile = 32
    chips = parts // 2

    def kernel(
        place_ref, kv_0, kv_1, kv_2, kv_3, queries, weight, tokens, gain, grad_hidden, normed, back, hidden_sums,
        units_a, units_b, input_ref, even_ref, odd_ref, grad_kv, grads, turned, product, small,
    ):
        place = place_ref[0]
        sums = [jnp.zeros((8, width), jnp.float32) for _ in range(4)]
        value_sums = jnp.zeros((8, 2 * HS), jnp.float32)
        for t in range(rows // tile):
            here = slice(t * tile, (t + 1) * tile)
            total = wide(kv_0[here, :]) + wide(kv_1[here, :]) + wide(kv_2[here, :]) + wide(kv_3[here, :])
            grad_kv[here, :] = low(total)
            value_sums = value_sums + fold_rows(total)
        turn((normed,), turned)
        product[...] = dot(turned[...], grad_kv[...])
        grads[...] = cols_dot(queries[...], weight[:, :width]) + cols_dot(grad_kv[...], weight[:, width:])
        for t in range(rows // tile):
            here = slice(t * tile, (t + 1) * tile)
            grad = grads[here, :]
            pulled, terms = norm_back(wide(tokens[here, :]), gain[...], grad)
            input_ref[here, :] = grad_hidden[here, :] + pulled
            for n, part in enumerate((terms, grad, wide(queries[here, :]), wide(back[here, :]))):
                sums[n] = sums[n] + fold_rows(part)
        sums = [jnp.sum(part, axis=0, keepdims=True) for part in sums]
        small[...] = jnp.zeros_like(small)
        rows_in = (sums[0], sums[1], hidden_sums[0:1, :], hidden_sums[1:2, :], sums[2], hidden_sums[2:3, :], sums[3])
        for n, row in enumerate(rows_in):
            for j in range(width // 128):
                line = n * (width // 128) + j
                small[line : line + 1, :] = row[:, j * 128 : (j + 1) * 128]
        start = 7 * (width // 128)
        small[start : start + 1, :] = jnp.sum(value_sums, axis=0, keepdims=True)
        lines = FF // parts // 128
        for m in range(chips):
            units = (units_a, units_b)[m // 2]
            for j in range(lines):
                line = start + 1 + (place ^ (2 * m)) * lines + j
                at = (m % 2 * lines + j) * 128
                small[pl.ds(line, 1), :] = units[:, at : at + 128]
        for k in range(parts):
            ref = odd_ref if k % 2 else even_ref
            mine = low(small[pl.ds(pl.multiple_of((place ^ k) * piece, 8), piece), :])
            for w in range(row_groups):
                at = pl.multiple_of(w * piece * parts + (place ^ k) * piece, 8)
                ref[k // 2, w, :, :128] = low(product[pl.ds(at, piece), :])
                ref[k // 2, w, :, 128:] = mine

    vmem = pl.BlockSpec(memory_space=pltpu.VMEM)
    stack = jax.ShapeDtypeStruct((chips, row_groups, piece, 256), jnp.bfloat16)
    return pl.pallas_call(
        kernel,
        in_specs=[pl.BlockSpec(memory_space=pltpu.SMEM)] + [vmem] * 14,
        out_specs=[vmem] * 3,
        out_shape=[jax.ShapeDtypeStruct((rows, width), jnp.float32), stack, stack],
        scratch_shapes=[
            pltpu.VMEM((rows, 2 * HS), jnp.bfloat16),
            pltpu.VMEM((rows, width), jnp.float32),
            pltpu.VMEM((width, rows), jnp.bfloat16),
            pltpu.VMEM((width, 2 * HS), jnp.float32),
            pltpu.VMEM((parts * piece, 128), jnp.float32),
        ],
        compiler_params=pltpu.CompilerParams(vmem_limit_bytes=VMEM_LIMIT),
        cost_estimate=NO_COST,
        name="stream_back",
    )


def attn_grads(rows, width, row_groups, parts, piece):
    def kernel(place_ref, left_a, right_a, left_b, right_b, even_ref, odd_ref, turned, total):
        place = place_ref[0]
        for n, (left, right) in enumerate(((left_a, right_a), (left_b, right_b))):
            for i in range(rows // 128):
                turned[:, i * 128 : (i + 1) * 128] = low(wide(left[i * 128 : (i + 1) * 128, :]).T)
            total[:, n * width : (n + 1) * width] = dot(turned[...], right[...])
        for k in range(parts):
            ref = odd_ref if k % 2 else even_ref
            for w in range(row_groups):
                at = pl.multiple_of(w * piece * parts + (place ^ k) * piece, 8)
                ref[k // 2, w] = low(total[pl.ds(at, piece), :])

    vmem = pl.BlockSpec(memory_space=pltpu.VMEM)
    shape = jax.ShapeDtypeStruct((parts // 2, row_groups, piece, 2 * width), jnp.bfloat16)
    return pl.pallas_call(
        kernel,
        grid_spec=pltpu.PrefetchScalarGridSpec(
            num_scalar_prefetch=1,
            grid=(),
            in_specs=[vmem] * 4,
            out_specs=[vmem] * 2,
            scratch_shapes=[pltpu.VMEM((width, rows), jnp.bfloat16), pltpu.VMEM((width, 2 * width), jnp.float32)],
        ),
        out_shape=[shape] * 2,
        compiler_params=pltpu.CompilerParams(vmem_limit_bytes=VMEM_LIMIT),
        cost_estimate=NO_COST,
        name="attn_grads",
    )


def attn_update(rows, columns, width, parts, piece):
    qkv = columns - width

    def kernel(place_ref, even_ref, odd_ref, master, first, second, *outs):
        place = place_ref[0]
        for k in range(parts):
            ref = odd_ref if k % 2 else even_ref
            here = pl.ds(pl.multiple_of((place ^ k) * piece, 8), piece)
            for cols, source in (
                (slice(0, width), slice(0, width)),
                (slice(width, qkv), slice(2 * width, columns)),
                (slice(qkv, columns), slice(width, 2 * width)),
            ):
                grad = wide(ref[k // 2, :, source])
                got = adam_update(master[here, cols], grad, first[here, cols], second[here, cols], 0.1, 0.1)
                outs[0][here, cols] = got[0]
                outs[1][here, cols] = got[1]
                outs[2][here, cols] = got[2]

    vmem = pl.BlockSpec(memory_space=pltpu.VMEM)
    return pl.pallas_call(
        kernel,
        grid_spec=pltpu.PrefetchScalarGridSpec(
            num_scalar_prefetch=1, grid=(), in_specs=[vmem] * 5, out_specs=[vmem] * 3, scratch_shapes=[]
        ),
        out_shape=[jax.ShapeDtypeStruct((rows, columns), jnp.float32)] * 3,
        compiler_params=pltpu.CompilerParams(vmem_limit_bytes=VMEM_LIMIT),
        cost_estimate=NO_COST,
        name="attn_update",
    )


def ffn_update(rows, units, parts, chunk):
    per_row = 2 * units // 128
    rows_once = 32
    lines = rows_once * per_row

    def kernel(place_ref, even, odd, master, first, second, first_out, second_out, master_out, total):
        place = place_ref[0]
        for k in range(parts):
            grad = odd if k % 2 else even
            for j in range(chunk // 128):
                for which in range(2):
                    line = (place ^ k) * (2 * chunk // 128) + 2 * j + which
                    total[pl.ds(line, rows_once, per_row), :] = wide(
                        grad[k // 2, which, :, j * 128 : (j + 1) * 128]
                    )
        for t in range(lines // 64):
            own = slice(t * 64, (t + 1) * 64)
            got = adam_update(master[own, :], total[own, :], first[own, :], second[own, :], 0.1, 0.1)
            first_out[own, :] = got[0]
            second_out[own, :] = got[1]
            master_out[own, :] = got[2]

    block = pl.BlockSpec((lines, 128), lambda i, *_: (i, 0))
    stack = pl.BlockSpec((parts // 2, 2, rows_once, chunk), lambda i, *_: (0, 0, i, 0))
    call = pl.pallas_call(
        kernel,
        grid_spec=pltpu.PrefetchScalarGridSpec(
            num_scalar_prefetch=1,
            grid=(rows // rows_once,),
            in_specs=[stack] * 2 + [block] * 3,
            out_specs=[block] * 3,
            scratch_shapes=[pltpu.VMEM((lines, 128), jnp.float32)],
        ),
        out_shape=[jax.ShapeDtypeStruct((rows * per_row, 128), jnp.float32)] * 3,
        compiler_params=pltpu.CompilerParams(vmem_limit_bytes=VMEM_LIMIT),
        cost_estimate=NO_COST,
        name="ffn_update",
    )

    def fold(array):
        return jnp.swapaxes(array.reshape(rows, 2, units // 128, 128), 1, 2).reshape(-1, 128)

    def unfold(array):
        return jnp.swapaxes(array.reshape(rows, units // 128, 2, 128), 1, 2).reshape(rows, 2, units)

    def run(place, even, odd, master, first, second):
        return tuple(unfold(array) for array in call(place, even, odd, fold(master), fold(first), fold(second)))

    return run


def shards(
    tokens,
    doc_starts,
    attn_master,
    attn_mom,
    attn_sq,
    ffn_master,
    ffn_mom,
    ffn_sq,
    small_master,
    small_mom,
    small_sq,
    cotangent,
):
    ctx_count, wt_count = lax.axis_size("ctx"), lax.axis_size("wt")
    ctx_place, wt_place = lax.axis_index("ctx"), lax.axis_index("wt")
    batches, rows_here, width = tokens.shape
    qkv_cols = width + 2 * HS
    attn_columns = attn_master.shape[1]
    all_rows = batches * rows_here
    shard_rows = attn_master.shape[0]
    piece_rows = shard_rows // ctx_count
    chunk = FF // ctx_count
    chips = ctx_count // 2
    order = ctx_place ^ jnp.arange(ctx_count, dtype=jnp.int32)
    (
        gain_one,
        shift_one,
        gain_two,
        shift_two,
        bias_query,
        bias_out,
        bias_proj,
        bias_value,
        bias_hidden,
    ) = split_small(small_master)
    runs = 2 if batches % 2 == 0 else 1
    places = [jnp.stack([ctx_place, jnp.int32(run * (batches // runs))]) for run in range(runs)]
    place = places[0]
    wt_half = wt_count // 2
    out_rows = shard_rows // chips
    run_forward, run_backward = attention_kernels(batches, rows_here, width, ctx_count, runs)
    ffn_first, ffn_second, ffn_third, ffn_down = ffn_kernels(all_rows, width, chunk, wt_count)
    step = Steps()

    def both(own, got, place, bit, axis=0):
        ahead, behind = jnp.stack([own, got], axis), jnp.stack([got, own], axis)
        return jnp.where((place & bit) == 0, ahead, behind)

    def in_order(even, odd):
        buffer = jnp.zeros((ctx_count,) + even.shape[1:], even.dtype)
        for m in range(chips):
            buffer = put(buffer, even[m][None], ctx_place ^ (2 * m), 0)
            buffer = put(buffer, odd[m][None], ctx_place ^ (2 * m + 1), 0)
        return buffer

    def send_chips(piece):
        return [xor_send(piece, mask) for mask in range(2, ctx_count, 2)]

    def split_wt(total, bit):
        ahead, behind = jnp.split(total, 2)
        kept, sent = jnp.where((wt_place & bit) == 0, ahead, behind), jnp.where((wt_place & bit) == 0, behind, ahead)
        return kept, sent

    def add_low(*arrays):
        return low(sum(wide(array) for array in arrays))

    qkv = low(lax.dynamic_slice(attn_master, (ctx_place * piece_rows, 0), (piece_rows, qkv_cols)))
    qkv_got = xor_wt(qkv, 1)
    rest = low(jnp.swapaxes(take(ffn_master, ctx_place, 2, chunk), 0, 1).reshape(2 * shard_rows, chunk))
    out = low(
        lax.dynamic_slice(
            attn_master, (ctx_place // 2 * out_rows, qkv_cols + ctx_place % 2 * chunk), (out_rows, chunk)
        )
    )
    qkv_got, rest, out = together(qkv_got, rest, out)
    rest_got, out_got = xor_wt(rest, 1), xor_wt(out, 1)
    flat_tokens = tokens.reshape(all_rows, width)
    qkv = both(qkv, qkv_got, wt_place, 1)
    qkv_got = xor_wt(qkv, 2)
    normed_low = step(
        lambda tokens, gain, shift: low(layer_norm(wide(tokens), gain, shift)), flat_tokens, gain_one, shift_one
    )
    qkv_got, rest_got, out_got = together(qkv_got, rest_got, out_got)
    qkv = both(qkv, qkv_got, wt_place, 2).reshape((wt_count,) + qkv.shape[1:])
    rest, out = both(rest, rest_got, wt_place, 1), both(out, out_got, wt_place, 1)
    qkv, rest, out = together(qkv, rest, out)
    qkv_got = xor_send(qkv, 2)
    rest_got, out_got = xor_wt(rest, 2), xor_wt(out, 2)
    back_low = cotangent.reshape(all_rows, width)
    qkv_got, back_low = together(qkv_got, back_low)
    qkv = both(qkv, qkv_got, ctx_place, 2)
    qkv_got = xor_send(qkv, 4)
    back_other = xor_send(back_low, 1)
    qkv_got, out_got = together(qkv_got, out_got)
    out = both(out, out_got, wt_place, 2).reshape((wt_count,) + out.shape[1:])
    qkv = both(qkv, qkv_got, ctx_place, 4)
    qkv_got = xor_send(qkv, 1)
    back_turned = turn_both(back_low, back_other)
    qkv_got, back_turned = together(qkv_got, back_turned)

    def project(own, got, normed):
        blocks = both(own, got, ctx_place, 1, 2)
        weight = jnp.transpose(blocks, (3, 0, 1, 2, 4, 5)).reshape(width, qkv_cols)
        mixed = dot(normed, weight)
        queries = low(mixed[:, :width] + bias_query).reshape(batches, rows_here, width)
        kv_bias = jnp.concatenate([jnp.zeros((HS,), jnp.float32), bias_value])
        kv_local = low(mixed[:, width:] + kv_bias).reshape(batches, rows_here, 2 * HS)
        return weight, queries, kv_local

    weight_qkv, queries, kv_local = project(qkv, qkv_got, normed_low)
    kv_got = xor_send(kv_local, 2)
    kv_even = both(kv_local, kv_got, ctx_place, 2)
    kv_even, out = together(kv_even, out)
    kv_got = xor_send(kv_even, 4)
    out_got = send_chips(out)
    kv_even = both(kv_even, kv_got, ctx_place, 4).reshape((chips,) + kv_local.shape)
    kv_odd = xor_send(kv_even, 1)
    kv_even, rest_got = together(kv_even, rest_got)
    rest = both(rest, rest_got, wt_place, 2).reshape((wt_count,) + rest.shape[1:])
    out_even = jnp.stack([out] + out_got)
    out_odd = xor_send(out_even, 1)
    rest_x, rest_y = xor_send(rest, 2), xor_send(rest, 4)
    queries, out_even, rest = together(queries, out_even, rest)

    attended_low, attended, logs = step(run_forward, doc_starts, place, queries, kv_even, kv_odd)
    attended_low = attended_low.reshape(all_rows, width)
    low_half, high_half = step(lambda x, y: (x[:wt_half], y[wt_half:]), rest_x, rest_y)
    diagonal_low, diagonal_high = xor_send(low_half, 4), xor_send(high_half, 2)

    def join_out(even, odd):
        columns = jnp.where((ctx_place & 1) == 0, jnp.concatenate([even, odd], axis=3), jnp.concatenate([odd, even], axis=3))
        for n in range(chips.bit_length() - 1):
            pairs = columns.reshape((-1, 2, 1 << n) + columns.shape[1:])
            columns = jnp.where((ctx_place & (2 << n)) == 0, pairs, pairs[:, ::-1]).reshape(columns.shape)
        return jnp.swapaxes(columns, 0, 1).reshape(width, width)

    weight_out = step(join_out, out_even, out_odd)
    hidden, normed_two = step(
        out_projection(all_rows, width), attended_low, weight_out, flat_tokens, bias_out[None], gain_two[None],
        shift_two[None],
    )
    normed_other = xor_send(normed_two, 1)

    bias_parts = bias_hidden.reshape(ctx_count, chunk)[order[::2]].reshape(1, chips * chunk)
    bias_near, bias_far = jnp.split(bias_parts, 2, axis=1)
    weights = [rest, rest_x, rest_y, diagonal_low, diagonal_high]
    flows = (normed_two, normed_other, back_low, back_other, back_turned)
    act_first, units_first, down_own, down_x, sums_first = step(
        lambda *args: ffn_first(*args[:6], *in_hbm(args[6:])), *flows, bias_near, *weights[:2]
    )
    act_second, units_second, down_y, down_top, down_bottom, sums_second, back_own, back_part = step(
        lambda *args: ffn_second(*args[:6], *in_hbm(args[6:])), *flows, bias_far, units_first, *weights
    )
    back_got = xor_send(back_part, 1)
    top_got, bottom_got = xor_send(down_top, 4), xor_send(down_bottom, 2)

    def meet(along_x, along_y, top, bottom):
        half = width // 2
        return (
            jnp.concatenate([add_low(along_x[:half], top), along_x[half:]]),
            jnp.concatenate([along_y[:half], add_low(along_y[half:], bottom)]),
        )

    up_own, up_x, up_y, up_top, up_bottom = step(
        lambda *args: ffn_third(*args[:2], *in_hbm(args[2:])), normed_two, normed_other, units_first, units_second
    )
    down_x, down_y = step(meet, down_x, down_y, top_got, bottom_got)
    down_got = [xor_send(down_x, 2), xor_send(down_y, 4)]
    top_got, bottom_got = xor_send(up_top, 4), xor_send(up_bottom, 2)

    grad_hidden, grad_hidden_low, grad_attended, hidden_sums = step(
        hidden_back(all_rows, width), back_own, back_got, hidden, back_low, gain_two[None], weight_out
    )
    grad_attended = grad_attended.reshape(batches, rows_here, width)
    up_x, up_y = step(meet, up_x, up_y, top_got, bottom_got)
    up_got = [xor_send(up_x, 2), xor_send(up_y, 4)]

    def split_both(total, bit):
        ahead, behind = jnp.split(total, 2, axis=1)
        kept, sent = jnp.where((wt_place & bit) == 0, ahead, behind), jnp.where((wt_place & bit) == 0, behind, ahead)
        return kept, sent

    def by_wt(*arrays):
        half = len(arrays) // 2
        total = jnp.stack([add_low(*arrays[:half]), add_low(*arrays[half:])])
        return split_both(total.reshape(2, wt_count, shard_rows, chunk), 2)

    def kv_pieces(evens, odds):
        total = jnp.concatenate([add_low(a, b) for a, b in zip(evens, odds)], axis=1)
        return [lax.dynamic_index_in_dim(total, (ctx_place // 2) ^ m, 0, False) for m in range(chips)]

    backs = [step(run_backward[0], doc_starts, places[0], queries, kv_even, kv_odd, attended, logs, grad_attended)]
    kv_got = [xor_send(backs[0][2], 1)]
    ffn_kept, ffn_sent = step(by_wt, up_own, *up_got, down_own, *down_got)
    grad_attended, ffn_kept, ffn_sent = together(grad_attended, ffn_kept, ffn_sent)
    ffn_got = xor_wt(ffn_sent, 2)
    backs += [
        step(run_backward[run], doc_starts, places[run], queries, kv_even, kv_odd, attended, logs, grad_attended)
        for run in range(1, runs)
    ]
    kv_got += [xor_send(back[2], 1) for back in backs[1:]]
    grad_query = jnp.concatenate([back[0] for back in backs]).reshape(all_rows, width)
    kv_half = step(kv_pieces, [back[1] for back in backs], kv_got)
    kv_got = [xor_send(kv_half[m], 2 * m) for m in range(1, chips)]
    wide_even, wide_odd = step(
        attn_grads(all_rows, width, wt_count, ctx_count, piece_rows),
        place, normed_low, grad_query, attended_low, grad_hidden_low,
    )
    small_size = small_master.shape[0]
    ffn_kept, ffn_sent = step(lambda kept, got: split_both(add_low(kept, got), 1), ffn_kept, ffn_got)
    kv_got[0], ffn_kept, ffn_sent = together(kv_got[0], ffn_kept, ffn_sent)
    ffn_got = xor_wt(ffn_sent, 1)
    input_grad, tail_even, tail_odd = step(
        stream_back(all_rows, width, ctx_count, wt_count, piece_rows),
        place, *[array.reshape(all_rows, 2 * HS) for array in (kv_half[0], *kv_got)], grad_query, weight_qkv,
        flat_tokens, gain_one[None], grad_hidden, normed_low, back_low, hidden_sums, sums_first, sums_second,
    )
    input_grad = input_grad.reshape(batches, rows_here, width)
    wide_odd, tail_odd = lax.optimization_barrier((wide_odd, tail_odd))
    wide_odd, tail_odd = xor_send(wide_odd, 1), xor_send(tail_odd, 1)
    def attn_pieces(wide_even, wide_odd, tail_even, tail_odd):
        total = jnp.concatenate([add_low(wide_even, wide_odd), add_low(tail_even, tail_odd)], axis=3)
        return [total[m] for m in range(chips)]

    attn_half = step(attn_pieces, wide_even, wide_odd, tail_even, tail_odd)
    attn_got = [xor_send(attn_half[m], 2 * m) for m in range(1, chips)]
    ffn_part = step(lambda kept, got: add_low(kept, got)[:, 0], ffn_kept, ffn_got)
    ffn_got = send_chips(ffn_part)
    down_out, down_other = step(
        lambda *args: ffn_down(*args[:2], *in_hbm(args[2:])), act_first, act_second, *weights
    )
    down_other = xor_send(down_other, 1)
    attn_kept, attn_sent = step(lambda *parts: split_wt(add_low(*parts), 2), attn_half[0], *attn_got)
    attn_got = xor_wt(attn_sent, 2)
    ffn_even = step(lambda *parts: jnp.stack(parts), ffn_part, *ffn_got)
    ffn_odd = xor_send(ffn_even, 1)
    layer_out = step(
        lambda hidden, own, got: low(hidden + own + wide(got) + bias_proj).reshape(batches, rows_here, width),
        hidden, down_out, down_other,
    )
    attn_kept, attn_sent = step(lambda kept, got: split_wt(add_low(kept, got), 1), attn_kept, attn_got)
    attn_got = xor_wt(attn_sent, 1)
    attn_part = step(lambda *parts: add_low(*parts)[0], attn_kept, attn_got)
    attn_got = send_chips(attn_part)

    ffn_new = step(
        ffn_update(shard_rows, FF, ctx_count, chunk), place, ffn_even, ffn_odd, ffn_master, ffn_mom, ffn_sq
    )
    attn_even = step(lambda *parts: jnp.stack(parts), attn_part, *attn_got)
    attn_odd = xor_send(attn_even, 1)
    small_total = in_order(attn_even[..., attn_columns:], attn_odd[..., attn_columns:])
    small_total = wide(small_total.reshape(-1))
    most = small_size - FF - HS
    small_total = jnp.concatenate(
        [small_total[:most], small_total[most + HS : most + 2 * HS], small_total[most + 2 * HS : most + 2 * HS + FF]]
    )
    small_new = adam_update(small_master, small_total, small_mom, small_sq, 1.0, 0.0)
    attn_new = attn_update(shard_rows, attn_columns, width, ctx_count, piece_rows)(
        place, attn_even, attn_odd, attn_master, attn_mom, attn_sq
    )
    return (layer_out, input_grad) + tuple(attn_new) + tuple(ffn_new) + tuple(small_new)


def shift_wt(array, shift):
    count = lax.axis_size("wt")
    return lax.ppermute(array, "wt", [(i, (i + shift) % count) for i in range(count)])


def whole_wt(piece, axis):
    count, place = lax.axis_size("wt"), lax.axis_index("wt")
    shape = list(piece.shape)
    shape[axis] *= count
    buffer = put(jnp.zeros(shape, piece.dtype), piece, place, axis)
    for shift in range(1, count):
        buffer = put(buffer, shift_wt(piece, shift), (place - shift) % count, axis)
    return buffer


def whole_ctx(piece):
    count = lax.axis_size("ctx")
    got = {0: piece}
    for mask in range(2, count, 2):
        got[mask] = xor_send(piece, mask)
    for mask in range(0, count, 2):
        got[mask + 1] = xor_send(got[mask], 1)
    return [got[mask] for mask in range(count)]


def sum_ctx(pieces):
    count = lax.axis_size("ctx")
    half = {}
    for mask in range(count - 2, -1, -2):
        other = xor_send(pieces[mask + 1], 1)
        half[mask] = low(wide(pieces[mask]) + wide(other))
    total = wide(half[0])
    for mask in range(2, count, 2):
        total = total + wide(xor_send(half[mask], mask))
    return total


def sum_wt(array, axis):
    count, place = lax.axis_size("wt"), lax.axis_index("wt")
    size = array.shape[axis] // count
    total = wide(take(array, place, axis, size))
    for shift in range(1, count):
        sent = take(array, (place + shift) % count, axis, size)
        total = total + wide(shift_wt(sent, shift))
    return total


def any_shards(
    tokens,
    doc_starts,
    attn_master,
    attn_mom,
    attn_sq,
    ffn_master,
    ffn_mom,
    ffn_sq,
    small_master,
    small_mom,
    small_sq,
    cotangent,
):
    ctx_count = lax.axis_size("ctx")
    ctx_place = lax.axis_index("ctx")
    wt_count = lax.axis_size("wt")
    batches, rows_here, width = tokens.shape
    heads = width // HS
    qkv_cols = width + 2 * HS
    all_rows = batches * rows_here
    shard_rows = attn_master.shape[0]
    piece_rows = shard_rows // ctx_count
    chunk = FF // ctx_count
    order = ctx_place ^ jnp.arange(ctx_count, dtype=jnp.int32)
    (
        gain_one,
        shift_one,
        gain_two,
        shift_two,
        bias_query,
        bias_out,
        bias_proj,
        bias_value,
        bias_hidden,
    ) = split_small(small_master)

    attn_piece = low(take(attn_master, ctx_place, 0, piece_rows))

    def whole_rows(piece):
        parts = whole_ctx(whole_wt(piece[None], 0))
        buffer = jnp.zeros((wt_count, ctx_count) + piece.shape, piece.dtype)
        for k, part in enumerate(parts):
            buffer = put(buffer, part[:, None], ctx_place ^ k, 1)
        return buffer.reshape((width,) + piece.shape[1:])

    weight_qkv = whole_rows(attn_piece[:, :qkv_cols])
    weight_out = whole_rows(attn_piece[:, qkv_cols:])
    ffn_piece = low(jnp.swapaxes(take(ffn_master, ctx_place, 2, chunk), 0, 1))
    ffn_parts = whole_ctx(whole_wt(ffn_piece, 1))
    bias_parts = bias_hidden.reshape(ctx_count, chunk)[order]

    stream = wide(tokens.reshape(all_rows, width))
    normed, norm_back_one = jax.vjp(layer_norm, stream, gain_one, shift_one)
    normed_low = low(normed)
    mixed = dot(normed_low, weight_qkv)
    queries = low(mixed[:, :width] + bias_query)
    kv_local = low(
        mixed[:, width:] + jnp.concatenate([jnp.zeros((HS,), jnp.float32), bias_value])
    ).reshape(batches, rows_here, 2 * HS)
    kv_parts = jnp.stack(whole_ctx(kv_local), axis=1).reshape(
        batches, ctx_count * rows_here, 2 * HS
    )
    keys_all, values_all = kv_parts[..., :HS], kv_parts[..., HS:]
    local_pos = jnp.arange(rows_here, dtype=jnp.int32)
    query_pos = ctx_place * rows_here + local_pos
    key_pos = (order[:, None] * rows_here + local_pos[None, :]).reshape(-1)
    queries = queries.reshape(batches, rows_here * heads, HS)
    scale = HS ** (-0.5)
    attended_list, log_list, allowed_list = [], [], []
    for b in range(batches):
        starts = doc_starts[b]
        query_doc = jnp.sum((starts[None, :] <= query_pos[:, None]).astype(jnp.int32), axis=1)
        key_doc = jnp.sum((starts[None, :] <= key_pos[:, None]).astype(jnp.int32), axis=1)
        allowed = (query_doc[:, None] == key_doc[None, :]) & (key_pos[None, :] <= query_pos[:, None])
        allowed = jnp.repeat(allowed, heads, axis=0)
        allowed_list.append(allowed)
        scores = jnp.where(allowed, cols_dot(queries[b], keys_all[b]) * scale, -1e30)
        peak = jnp.max(scores, axis=-1, keepdims=True)
        expo = jnp.exp(scores - peak)
        total = jnp.sum(expo, axis=-1, keepdims=True)
        attended_list.append(dot(low(expo / total), values_all[b]))
        log_list.append(peak + jnp.log(total))
    attended = jnp.stack(attended_list)
    attended_low = low(attended).reshape(all_rows, width)
    hidden = stream + dot(attended_low, weight_out) + bias_out
    normed_two, norm_back_two = jax.vjp(layer_norm, hidden, gain_two, shift_two)
    normed_two_low = low(normed_two)

    back_low = cotangent.reshape(all_rows, width)
    back_rows = wide(back_low)
    down_vals = jnp.zeros((all_rows, width), jnp.float32)
    grad_normed_two = jnp.zeros((all_rows, width), jnp.float32)
    ffn_grads, hidden_grads = [], []
    for k in range(ctx_count):
        weight_up, weight_down = ffn_parts[k][0], ffn_parts[k][1]
        value, slope = gelu_both(dot(normed_two_low, weight_up) + bias_parts[k])
        act = low(value)
        down_vals = down_vals + cols_dot(act, weight_down)
        grad_up = low(dot(back_low, weight_down) * slope)
        hidden_grads.append(jnp.sum(wide(grad_up), axis=0))
        grad_normed_two = grad_normed_two + cols_dot(grad_up, weight_up)
        ffn_grads.append(
            jnp.stack([low(rows_dot(normed_two_low, grad_up)), low(rows_dot(back_low, act))])
        )
    layer_out = low(hidden + down_vals + bias_proj).reshape(batches, rows_here, width)
    grad_bias_proj = jnp.sum(back_rows, axis=0)
    grad_bias_hidden = jnp.stack(hidden_grads)[order].reshape(FF)
    ffn_part = low(sum_wt(low(sum_ctx(ffn_grads)), 1))

    grad_hidden_part, grad_gain_two, grad_shift_two = norm_back_two(grad_normed_two)
    grad_hidden = back_rows + grad_hidden_part
    grad_bias_out = jnp.sum(grad_hidden, axis=0)
    grad_hidden_low = low(grad_hidden)
    grad_out = rows_dot(attended_low, grad_hidden_low)

    def summed_rows(grad):
        blocks = low(grad).reshape(wt_count, ctx_count, piece_rows, grad.shape[1])
        pieces = [take(blocks, ctx_place ^ k, 1, 1)[:, 0] for k in range(ctx_count)]
        part = low(sum_wt(low(sum_ctx(pieces)), 0)[0])
        buffer = jnp.zeros((ctx_count,) + part.shape, part.dtype)
        for k, got in enumerate(whole_ctx(part)):
            buffer = put(buffer, got[None], ctx_place ^ k, 0)
        return wide(buffer.reshape(shard_rows, grad.shape[1]))

    out_total = summed_rows(grad_out)

    grad_attended = low(cols_dot(grad_hidden_low, weight_out)).reshape(
        batches, rows_here * heads, HS
    )
    grad_query_list, grad_kv_list = [], []
    for b in range(batches):
        grads = grad_attended[b]
        delta = jnp.sum(wide(grads) * attended[b], axis=-1, keepdims=True)
        scores = jnp.where(allowed_list[b], cols_dot(queries[b], keys_all[b]) * scale, -1e30)
        weights = jnp.exp(scores - log_list[b])
        grad_scores = low(weights * (cols_dot(grads, values_all[b]) - delta))
        grad_query_list.append(low(dot(grad_scores, keys_all[b]) * scale))
        grad_kv_list.append(
            jnp.concatenate(
                [
                    low(rows_dot(grad_scores, queries[b]) * scale),
                    low(rows_dot(low(weights), grads)),
                ],
                axis=1,
            )
        )
    grad_query = jnp.stack(grad_query_list).reshape(all_rows, width)
    grad_kv = jnp.stack(grad_kv_list).reshape(batches, ctx_count, rows_here, 2 * HS)
    grad_kv_low = low(sum_ctx([grad_kv[:, k] for k in range(ctx_count)])).reshape(
        all_rows, 2 * HS
    )
    grad_bias_query = jnp.sum(wide(grad_query), axis=0)
    grad_bias_value = jnp.sum(wide(grad_kv_low[:, HS:]), axis=0)
    grad_mixed = jnp.concatenate([grad_query, grad_kv_low], axis=1)
    qkv_total = summed_rows(rows_dot(normed_low, grad_mixed))
    grad_normed = cols_dot(grad_mixed, weight_qkv)
    grad_stream_part, grad_gain_one, grad_shift_one = norm_back_one(grad_normed)
    input_grad = (grad_hidden + grad_stream_part).reshape(batches, rows_here, width)

    ffn_buffer = jnp.zeros((ctx_count,) + ffn_part.shape, ffn_part.dtype)
    for k, got in enumerate(whole_ctx(ffn_part)):
        ffn_buffer = put(ffn_buffer, got[None], ctx_place ^ k, 0)
    ffn_total = wide(jnp.transpose(ffn_buffer, (2, 1, 0, 3)).reshape(shard_rows, 2, FF))
    attn_total = jnp.concatenate([qkv_total, out_total], axis=1)
    grad_small = jnp.concatenate(
        [
            grad_gain_one,
            grad_shift_one,
            grad_gain_two,
            grad_shift_two,
            grad_bias_query,
            grad_bias_out,
            grad_bias_proj,
            grad_bias_value,
            grad_bias_hidden,
        ]
    )
    small_total = lax.psum(grad_small, ("ctx", "wt"))
    attn_new = adam_update(attn_master, attn_total, attn_mom, attn_sq, 0.1, 0.1)
    ffn_new = adam_update(ffn_master, ffn_total, ffn_mom, ffn_sq, 0.1, 0.1)
    small_new = adam_update(small_master, small_total, small_mom, small_sq, 1.0, 0.0)
    return (layer_out, input_grad) + attn_new + ffn_new + small_new


def solution(mesh):
    rows, cube = P("wt", None), P("wt", None, None)
    flow = P("wt", "ctx", None)
    in_specs = (flow, rows, rows, rows, rows, cube, cube, cube, P(), P(), P(), flow)
    out_specs = (flow, flow, rows, rows, rows, cube, cube, cube, P(), P(), P())
    ctx_count, wt_count = mesh.shape["ctx"], mesh.shape["wt"]
    fitted = (ctx_count, wt_count) == (8, 4)
    body = shards if fitted else any_shards
    return jax.shard_map(body, mesh=mesh, in_specs=in_specs, out_specs=out_specs, check_vma=False)
```

```python
import jax
import jax.numpy as jnp
from jax import lax
from jax.experimental import pallas as pl
from jax.experimental.pallas import tpu as pltpu
from jax.sharding import PartitionSpec as P

D = 768
HS = 64
FF = 3072
STEP = 10


NORM_EPS = 1e-05
GELU_COEF = 0.7978845608028654
GELU_CUBE = 0.044715
BETA_ONE = 0.9
BETA_TWO = 0.95
ADAM_EPS = 1e-08
VMEM_LIMIT = 22 << 20
NO_COST = pl.CostEstimate(flops=0, bytes_accessed=0, transcendentals=0)


def layer_norm(values, gain, shift):
    centre = values - jnp.mean(values, axis=-1, keepdims=True)
    spread = jnp.mean(centre * centre, axis=-1, keepdims=True)
    return centre * lax.rsqrt(spread + NORM_EPS) * gain + shift


def gelu_both(u):
    square = u * u
    share = 0.5 * jnp.tanh(u * (GELU_COEF * GELU_CUBE * square + GELU_COEF)) + 0.5
    bend = u * (6.0 * GELU_COEF * GELU_CUBE * square + 2.0 * GELU_COEF)
    return u * share, share * ((1.0 - share) * bend) + share


def split_small(small):
    return (
        small[0:D],
        small[D : 2 * D],
        small[2 * D : 3 * D],
        small[3 * D : 4 * D],
        small[4 * D : 5 * D],
        small[5 * D : 6 * D],
        small[6 * D : 7 * D],
        small[7 * D : 7 * D + HS],
        small[7 * D + HS :],
    )


def rows_dot(left, right):
    return lax.dot_general(
        left, right, (((0,), (0,)), ((), ())), preferred_element_type=jnp.float32
    )


def cols_dot(left, right):
    return lax.dot_general(
        left, right, (((1,), (1,)), ((), ())), preferred_element_type=jnp.float32
    )


def dot(left, right):
    return jnp.dot(left, right, preferred_element_type=jnp.float32)


def low(values):
    return values.astype(jnp.bfloat16)


def wide(values):
    return values.astype(jnp.float32)


def adam_update(master, gradient, first, second, step_rate, decay_rate):
    first_new = BETA_ONE * first + (1.0 - BETA_ONE) * gradient
    second_new = BETA_TWO * second + (1.0 - BETA_TWO) * gradient * gradient
    first_hat = first_new / (1.0 - BETA_ONE**STEP)
    second_hat = second_new / (1.0 - BETA_TWO**STEP)
    master_new = master - step_rate * (
        first_hat / (jnp.sqrt(second_hat) + ADAM_EPS) + decay_rate * master
    )
    return (first_new, second_new, master_new)


def xor_send(array, mask):
    count = lax.axis_size("ctx")
    return lax.ppermute(array, "ctx", [(i, i ^ mask) for i in range(count)])


def xor_wt(array, mask):
    count = lax.axis_size("wt")
    return lax.ppermute(array, "wt", [(i, i ^ mask) for i in range(count)])


class Steps:
    def __init__(self):
        self.last = ()

    def __call__(self, function, *args):
        flat, tree = jax.tree.flatten(args)
        held = lax.optimization_barrier(tuple(flat) + self.last)[: len(flat)]
        result = function(*jax.tree.unflatten(tree, held))
        self.last = tuple(jax.tree.leaves(result))
        return result


def loop(count, body, carry=0):
    return lax.fori_loop(0, count, body, carry)


def rows_at(i, size):
    return pl.ds(pl.multiple_of(i * size, size), size)


def together(*arrays):
    return lax.optimization_barrier(arrays)


def put(buffer, piece, place, axis):
    starts = [0] * buffer.ndim
    starts[axis] = place * piece.shape[axis]
    return lax.dynamic_update_slice(buffer, piece, starts)


def take(buffer, place, axis, size):
    return lax.dynamic_slice_in_dim(buffer, place * size, size, axis)


def attention_kernels(batches, rows, width, parts, runs):
    half_parts = parts // 2
    keys = parts * rows
    pair = 2 * HS
    groups = width // (2 * pair)
    factor = HS ** (-0.5) * 1.4426950408889634
    tile = 32

    def lanes(shape):
        return lax.broadcasted_iota(jnp.int32, shape, 1)

    def spread(even_ref, odd_ref, key_ref, value_ref):
        for j in range(parts):
            ref = even_ref if j < half_parts else odd_ref
            block = wide(ref[j % half_parts, 0])
            turned = pltpu.roll(block, HS, 1)
            first = lanes(block.shape) < HS
            here = pl.ds(j * rows, rows)
            key_ref[0, here, :] = low(jnp.where(first, block, 0.0))
            key_ref[1, here, :] = low(jnp.where(first, 0.0, turned))
            value_ref[0, here, :] = low(jnp.where(first, turned, 0.0))
            value_ref[1, here, :] = low(jnp.where(first, 0.0, block))

    def doc_begin(starts_ref, stream, positions):
        begin = jnp.zeros_like(positions)
        for j in range(starts_ref.shape[1]):
            start = starts_ref[stream, j]
            begin = jnp.where(start <= positions, jnp.maximum(begin, start), begin)
        return begin

    def forward(starts_ref, place_ref, query_ref, even_ref, odd_ref, low_ref, full_ref, log_ref, cap, key, value, weight):
        stream, place = pl.program_id(0), place_ref[0]
        spread(even_ref, odd_ref, key, value)
        query_pos = place * rows + lax.broadcasted_iota(jnp.int32, (rows, 1), 0)
        begin = doc_begin(starts_ref, stream, query_pos)
        for j in range(parts):
            key_pos = (2 * (j % half_parts) + (place + j // half_parts) % 2) * rows + lax.broadcasted_iota(jnp.int32, (rows, rows), 1)
            allowed = (key_pos >= begin) & (key_pos <= query_pos)
            cap[:, j * rows : (j + 1) * rows] = jnp.where(allowed, 3.0e38, -1e30)
        column = lanes((tile, pair))
        logs = [jnp.zeros((tile, pair), jnp.float32) for _ in range(rows // tile)]
        for g in range(groups):
            at = g * 2 * pair
            two = jnp.concatenate([query_ref[0, :, at : at + pair], query_ref[0, :, at + pair : at + 2 * pair]], axis=0)
            totals = []
            for half in range(2):
                scores = cols_dot(two, key[half])
                norms = []
                for t in range(2 * rows // tile):
                    own = slice(t * tile, (t + 1) * tile)
                    n = t % (rows // tile)
                    part = jnp.minimum(scores[own] * factor, cap[n * tile : (n + 1) * tile, :])
                    peak = jnp.max(part, axis=1, keepdims=True)
                    expo = jnp.exp2(part - peak)
                    norm = jnp.sum(expo, axis=1, keepdims=True)
                    weight[half, own, :] = low(expo)
                    norms.append(norm)
                    head = 4 * g + 2 * (t * tile // rows) + half
                    logs[n] = jnp.where(column == head, peak + jnp.log2(norm), logs[n])
                totals.append(dot(weight[half], value[half]) / jnp.concatenate(norms, axis=0))
            total = totals[0] + totals[1]
            for j in range(2):
                part = total[j * rows : (j + 1) * rows]
                full_ref[0, :, at + j * pair : at + (j + 1) * pair] = part
                low_ref[0, :, at + j * pair : at + (j + 1) * pair] = low(part)
        for n, log in enumerate(logs):
            log_ref[0, n * tile : (n + 1) * tile, :] = log

    def backward(
        starts_ref, place_ref, query_ref, even_ref, odd_ref, full_ref, log_ref, grad_ref,
        query_grad_ref, even_grad_ref, odd_grad_ref,
        cap, key, value, key_turned, log_rows, delta_rows, weight_buf, score_buf, query_buf, grad_buf,
    ):
        stream, place = pl.program_id(0) + place_ref[1], place_ref[0]
        spread(even_ref, odd_ref, key, value)
        query_pos = place * rows + lax.broadcasted_iota(jnp.int32, (1, rows), 1)
        begin = doc_begin(starts_ref, stream, query_pos)
        for j in range(parts):
            key_pos = (2 * (j % half_parts) + (place + j // half_parts) % 2) * rows + lax.broadcasted_iota(jnp.int32, (rows, rows), 0)
            allowed = (key_pos >= begin) & (key_pos <= query_pos)
            cap[j * rows : (j + 1) * rows, :] = jnp.where(allowed, 3.0e38, -1e30)
            here = pl.ds(j * rows, rows)
            key_turned[:, j * rows : (j + 1) * rows] = low(wide(key[0, here, :]).T[:HS])
        log_rows[...] = log_ref[0].T[: log_rows.shape[0]]
        head_of = lax.broadcasted_iota(jnp.int32, (delta_rows.shape[0], width), 1) // HS
        chosen = (head_of == lax.broadcasted_iota(jnp.int32, (delta_rows.shape[0], width), 0)).astype(jnp.float32)
        delta_rows[...] = lax.dot_general(
            chosen, wide(grad_ref[0]) * full_ref[0], (((1,), (1,)), ((), ())),
            precision=lax.Precision.HIGHEST, preferred_element_type=jnp.float32,
        )
        first = lanes((2 * rows, pair)) < HS
        for g in range(groups):
            at = g * 2 * pair
            both, both_grad = query_ref[0, :, at : at + 2 * pair], grad_ref[0, :, at : at + 2 * pair]
            two = jnp.concatenate([both[:, :pair], both[:, pair:]], axis=0)
            two_grad = jnp.concatenate([both_grad[:, :pair], both_grad[:, pair:]], axis=0)
            turned = []
            for half in range(2):
                h = 4 * g + half
                span = slice((2 * g + half) * 2 * rows, (2 * g + half + 1) * 2 * rows)
                keep = first if half == 0 else jnp.logical_not(first)
                query_buf[span, :] = low(jnp.where(keep, wide(two), 0.0))
                grad_buf[span, :] = low(jnp.where(keep, wide(two_grad), 0.0))
                log = jnp.concatenate([log_rows[h : h + 1, :], log_rows[h + 2 : h + 3, :]], axis=1)
                delta = jnp.concatenate([delta_rows[h : h + 1, :], delta_rows[h + 2 : h + 3, :]], axis=1)
                scores, weight_grads = cols_dot(key[half], two), cols_dot(value[half], two_grad)
                for t in range(keys // (2 * tile)):
                    own = slice(t * 2 * tile, (t + 1) * 2 * tile)
                    limit = cap[own, :]
                    limit = jnp.concatenate([limit, limit], axis=1)
                    weights = jnp.exp2(jnp.minimum(scores[own] * factor, limit) - log)
                    weight_buf[own, span] = low(weights)
                    score_buf[own, span] = low(weights * (weight_grads[own] - delta))
                turned.append(dot(key_turned[...], score_buf[:, span]))
            turned = jnp.concatenate(turned, axis=0) * HS ** (-0.5)
            query_grad_ref[0, :, at : at + pair] = low(turned[:, :rows].T)
            query_grad_ref[0, :, at + pair : at + 2 * pair] = low(turned[:, rows:].T)
        for j in range(parts):
            here = pl.ds(j * rows, rows)
            value_sum = dot(weight_buf[here, :], grad_buf[...])
            key_sum = dot(score_buf[here, :], query_buf[...]) * HS ** (-0.5)
            value_sum = value_sum + pltpu.roll(value_sum, HS, 1)
            key_sum = key_sum + pltpu.roll(key_sum, HS, 1)
            ref = even_grad_ref if j < half_parts else odd_grad_ref
            ref[j % half_parts, 0] = low(jnp.where(lanes((rows, pair)) < HS, key_sum, value_sum))

    def specs(first):
        return (
            pl.BlockSpec((1, rows, width), lambda b, *_: (b + first, 0, 0)),
            pl.BlockSpec((1, rows, pair), lambda b, *_: (b + first, 0, 0)),
            pl.BlockSpec((half_parts, 1, rows, pair), lambda b, *_: (0, b + first, 0, 0)),
        )

    flow, logs, blocks = specs(0)

    shared = [
        pltpu.VMEM((2, keys, pair), jnp.bfloat16),
        pltpu.VMEM((2, keys, pair), jnp.bfloat16),
    ]
    run_forward = pl.pallas_call(
        forward,
        grid_spec=pltpu.PrefetchScalarGridSpec(
            num_scalar_prefetch=2,
            grid=(batches,),
            in_specs=[flow, blocks, blocks],
            out_specs=[flow, flow, logs],
            scratch_shapes=[pltpu.VMEM((rows, keys), jnp.float32)]
            + shared
            + [pltpu.VMEM((2, 2 * rows, keys), jnp.bfloat16)],
        ),
        out_shape=[
            jax.ShapeDtypeStruct((batches, rows, width), jnp.bfloat16),
            jax.ShapeDtypeStruct((batches, rows, width), jnp.float32),
            jax.ShapeDtypeStruct((batches, rows, pair), jnp.float32),
        ],
        compiler_params=pltpu.CompilerParams(vmem_limit_bytes=VMEM_LIMIT),
        cost_estimate=NO_COST,
        name="attention_forward",
    )
    head_rows = -(-(width // HS) // 8) * 8
    all_columns = rows * (width // HS)
    count = batches // runs

    def call_backward(run):
        here_flow, here_logs, here_blocks = specs(run * count)
        return pl.pallas_call(
        backward,
        grid_spec=pltpu.PrefetchScalarGridSpec(
            num_scalar_prefetch=2,
            grid=(count,),
            in_specs=[here_flow, here_blocks, here_blocks, here_flow, here_logs, here_flow],
            out_specs=[flow, blocks, blocks],
            scratch_shapes=[pltpu.VMEM((keys, rows), jnp.float32)]
            + shared
            + [
                pltpu.VMEM((HS, keys), jnp.bfloat16),
                pltpu.VMEM((head_rows, rows), jnp.float32),
                pltpu.VMEM((head_rows, rows), jnp.float32),
                pltpu.VMEM((keys, all_columns), jnp.bfloat16),
                pltpu.VMEM((keys, all_columns), jnp.bfloat16),
                pltpu.VMEM((all_columns, pair), jnp.bfloat16),
                pltpu.VMEM((all_columns, pair), jnp.bfloat16),
            ],
        ),
        out_shape=[
            jax.ShapeDtypeStruct((count, rows, width), jnp.bfloat16),
            jax.ShapeDtypeStruct((half_parts, count, rows, pair), jnp.bfloat16),
            jax.ShapeDtypeStruct((half_parts, count, rows, pair), jnp.bfloat16),
        ],
        compiler_params=pltpu.CompilerParams(vmem_limit_bytes=VMEM_LIMIT),
        cost_estimate=NO_COST,
        name="attention_backward",
    )

    return run_forward, [call_backward(run) for run in range(runs)]


def in_hbm(arrays):
    return [pltpu.with_memory_space_constraint(array, pltpu.HBM) for array in arrays]


def ffn_kernels(rows, width, chunk, wt_count):
    units = 2 * chunk
    all_rows = 2 * rows
    block_rows = width // wt_count
    hbm = pl.BlockSpec(memory_space=pltpu.HBM)
    vmem = pl.BlockSpec(memory_space=pltpu.VMEM)
    params = pltpu.CompilerParams(vmem_limit_bytes=VMEM_LIMIT)

    def fetch(weights, which, held, sem):
        copies = []
        for n, arrays in enumerate(weights):
            blocks = [array.at[block] for array in arrays for block in range(array.shape[0])]
            for row, block in enumerate(blocks):
                copies.append(
                    pltpu.make_async_copy(
                        block.at[pl.ds(which * block_rows, block_rows), :],
                        held.at[pl.ds(row * block_rows, block_rows), pl.ds(n * chunk, chunk)],
                        sem.at[len(copies)],
                    )
                )
        for copy in copies:
            copy.start()
        return copies

    def send(pairs, sems):
        copies = [pltpu.make_async_copy(source, out, sems.at[n]) for n, (source, out) in enumerate(pairs)]
        for copy in copies:
            copy.start()
        return copies

    part_rows = 256
    tile = 16

    def units_of(inputs, grads, bias, held_up, held_down, act, grad_units):
        sums = jnp.zeros((8, units), jnp.float32)
        for s in range(2):

            def part(i, sums):
                here = rows_at(i, part_rows)
                up = dot(inputs[s][here, :], held_up[...])
                act_grad = dot(grads[s][here, :], held_down[...])
                for t in range(part_rows // tile):
                    own = slice(t * tile, (t + 1) * tile)
                    there = pl.ds(pl.multiple_of(s * rows + i * part_rows + t * tile, tile), tile)
                    value, slope = gelu_both(up[own] + bias)
                    grad = act_grad[own] * slope
                    act[there, :] = low(value)
                    grad_units[there, :] = low(grad)
                    sums = sums + (grad[:8] + grad[8:])
                return sums

            sums = loop(rows // part_rows, part, sums)
        return jnp.sum(sums, axis=0, keepdims=True)

    def product_of(turned, right, product):
        def part(i, carry):
            here = rows_at(i, part_rows)
            product[here, :] = low(dot(turned[here, :], right[...]))
            return carry

        loop(width // part_rows, part)

    def back_to(refs, sources, weights):
        for s, ref in enumerate(refs):

            def part(i, carry):
                here = pl.ds(pl.multiple_of(s * rows + i * part_rows, part_rows), part_rows)
                total = cols_dot(sources[0][here, :], weights[0][...]) + cols_dot(sources[1][here, :], weights[1][...])
                ref[rows_at(i, part_rows), :] = total.astype(ref.dtype)
                return carry

            loop(rows // part_rows, part)

    def halves(product, m):
        cols = pl.ds(m * chunk, chunk)
        return [product.at[pl.ds(h * width // 2, width // 2), cols] for h in range(2)]

    def first(
        own, other, grad_own, grad_other, turned, bias, w0, w1,
        act_out, units_out, out_a, out_b, sums_out,
        held_up, held_down, act, grad_units, product, sems, out_sems,
    ):
        weights = ((w0,), (w1,))
        copies = fetch(weights, 0, held_up, sems.at[0]) + fetch(weights, 1, held_down, sems.at[1])
        for copy in copies:
            copy.wait()
        sums_out[...] = units_of((own, other), (grad_own, grad_other), bias[...], held_up, held_down, act, grad_units)
        sent = send(((act, act_out), (grad_units, units_out)), out_sems.at[0])
        product_of(turned, act, product)
        sent += send(
            ((product.at[:, pl.ds(0, chunk)], out_a), (product.at[:, pl.ds(chunk, chunk)], out_b)), out_sems.at[1]
        )
        for copy in sent:
            copy.wait()

    def second(
        own, other, grad_own, grad_other, turned, bias, units_first, w0, w1, w2, w3, w4,
        act_out, units_out, out_a, out_b, out_c, sums_out, back_own, back_other,
        held_up, held_more, held_down, act, grad_units, more_units, product, sems, out_sems, more_sem,
    ):
        weights, before = ((w2,), (w3, w4)), ((w0,), (w1,))
        copies = fetch(weights, 0, held_up, sems.at[0]) + fetch(weights, 1, held_down, sems.at[1])
        more = fetch(before, 0, held_more, sems.at[2])
        more.append(pltpu.make_async_copy(units_first, more_units, more_sem))
        more[-1].start()
        for copy in copies:
            copy.wait()
        sums_out[...] = units_of((own, other), (grad_own, grad_other), bias[...], held_up, held_down, act, grad_units)
        sent = send(((act, act_out), (grad_units, units_out)), out_sems.at[0])
        product_of(turned, act, product)
        top, bottom = halves(product, 1)
        sent += send(((product.at[:, pl.ds(0, chunk)], out_a), (top, out_b), (bottom, out_c)), out_sems.at[1])
        for copy in more:
            copy.wait()
        back_to((back_own, back_other), (grad_units, more_units), (held_up, held_more))
        for copy in sent:
            copy.wait()

    def third(own, other, units_a, units_b, out_0, out_1, out_2, out_3, out_4, turned, held, products, sems, out_sems):
        copies = send(((units_a, held.at[0]), (units_b, held.at[1])), sems)
        turn((own, other), turned)
        for copy in copies:
            copy.wait()
        products[1] = low(dot(turned[...], held[1]))
        top, bottom = halves(products.at[1], 1)
        sent = send(((products.at[1, :, pl.ds(0, chunk)], out_2), (top, out_3), (bottom, out_4)), out_sems.at[0])
        products[0] = low(dot(turned[...], held[0]))
        sent += send(
            ((products.at[0, :, pl.ds(0, chunk)], out_0), (products.at[0, :, pl.ds(chunk, chunk)], out_1)),
            out_sems.at[1],
        )
        for copy in sent:
            copy.wait()

    def down(act_a, act_b, w0, w1, w2, w3, w4, own_ref, other_ref, held_a, held_b, sems):
        copies = fetch(((w0,), (w1,)), 1, held_a, sems.at[0]) + fetch(((w2,), (w3, w4)), 1, held_b, sems.at[1])
        for copy in copies:
            copy.wait()
        for s, ref in enumerate((own_ref, other_ref)):
            here = slice(s * rows, (s + 1) * rows)
            total = cols_dot(act_a[here, :], held_a[...]) + cols_dot(act_b[here, :], held_b[...])
            ref[...] = total.astype(ref.dtype)

    dma = pltpu.SemaphoreType.DMA
    held = pltpu.VMEM((width, units), jnp.bfloat16)
    flow = pltpu.VMEM((all_rows, units), jnp.bfloat16)
    flow_out = pltpu.HBM((all_rows, units), jnp.bfloat16)
    whole = pltpu.HBM((width, chunk), jnp.bfloat16)
    part = pltpu.HBM((width // 2, chunk), jnp.bfloat16)
    sums = jax.ShapeDtypeStruct((1, units), jnp.float32)
    own = jax.ShapeDtypeStruct((rows, width), jnp.float32)
    other = jax.ShapeDtypeStruct((rows, width), jnp.bfloat16)
    run_first = pl.pallas_call(
        first,
        in_specs=[vmem] * 6 + [hbm] * 2,
        out_specs=[hbm] * 4 + [vmem],
        out_shape=[flow_out, flow_out, whole, whole, sums],
        scratch_shapes=[held, held, flow, flow, held, dma((2, 2 * wt_count)), dma((2, 2))],
        compiler_params=params,
        cost_estimate=NO_COST,
        name="ffn_first",
    )
    run_second = pl.pallas_call(
        second,
        in_specs=[vmem] * 6 + [hbm] * 6,
        out_specs=[hbm] * 5 + [vmem] * 3,
        out_shape=[flow_out, flow_out, whole, part, part, sums, own, other],
        scratch_shapes=[held, held, held, flow, flow, flow, held, dma((3, 2 * wt_count)), dma((2, 3)), dma(())],
        compiler_params=params,
        cost_estimate=NO_COST,
        name="ffn_second",
    )
    run_third = pl.pallas_call(
        third,
        in_specs=[vmem] * 2 + [hbm] * 2,
        out_specs=[hbm] * 5,
        out_shape=[whole, whole, whole, part, part],
        scratch_shapes=[
            pltpu.VMEM((width, all_rows), jnp.bfloat16),
            pltpu.VMEM((2, all_rows, units), jnp.bfloat16),
            pltpu.VMEM((2, width, units), jnp.bfloat16),
            dma((2,)),
            dma((2, 3)),
        ],
        compiler_params=params,
        cost_estimate=NO_COST,
        name="ffn_grads",
    )
    run_down = pl.pallas_call(
        down,
        in_specs=[vmem] * 2 + [hbm] * 5,
        out_specs=[vmem] * 2,
        out_shape=[own, other],
        scratch_shapes=[held, held, dma((2, 2 * wt_count))],
        compiler_params=params,
        cost_estimate=NO_COST,
        name="ffn_down",
    )
    return run_first, run_second, run_third, run_down


def turn(refs, turned):
    rows = refs[0].shape[0]
    for s, ref in enumerate(refs):
        for i in range(rows // 128):
            block = wide(ref[i * 128 : (i + 1) * 128, :])
            turned[:, s * rows + i * 128 : s * rows + (i + 1) * 128] = low(block.T)


def turn_both(own, other):
    vmem = pl.BlockSpec(memory_space=pltpu.VMEM)
    rows, width = own.shape
    return pl.pallas_call(
        lambda a, b, out: turn((a, b), out),
        in_specs=[vmem] * 2,
        out_specs=vmem,
        out_shape=jax.ShapeDtypeStruct((width, 2 * rows), own.dtype),
        compiler_params=pltpu.CompilerParams(vmem_limit_bytes=VMEM_LIMIT),
        cost_estimate=NO_COST,
        name="turn",
    )(own, other)


def out_projection(rows, width):
    tile = 32

    def kernel(attended, weight, stream, bias, gain, shift, hidden_ref, normed_ref):
        product = dot(attended[...], weight[...])
        for t in range(rows // tile):
            here = slice(t * tile, (t + 1) * tile)
            hidden = wide(stream[here, :]) + product[here] + bias[...]
            hidden_ref[here, :] = hidden
            normed_ref[here, :] = low(layer_norm(hidden, gain[...], shift[...]))

    vmem = pl.BlockSpec(memory_space=pltpu.VMEM)
    return pl.pallas_call(
        kernel,
        in_specs=[vmem] * 6,
        out_specs=[vmem] * 2,
        out_shape=[
            jax.ShapeDtypeStruct((rows, width), jnp.float32),
            jax.ShapeDtypeStruct((rows, width), jnp.bfloat16),
        ],
        compiler_params=pltpu.CompilerParams(vmem_limit_bytes=VMEM_LIMIT),
        cost_estimate=NO_COST,
        name="out_projection",
    )


def norm_back(values, gain, grad):
    centre = values - jnp.mean(values, axis=-1, keepdims=True)
    scale = lax.rsqrt(jnp.mean(centre * centre, axis=-1, keepdims=True) + NORM_EPS)
    unit = centre * scale
    inner = grad * gain
    mean = jnp.mean(inner, axis=-1, keepdims=True)
    along = jnp.mean(inner * unit, axis=-1, keepdims=True)
    return scale * (inner - mean - unit * along), grad * unit


def fold_rows(values):
    total = values[:8]
    for i in range(1, values.shape[0] // 8):
        total = total + values[i * 8 : (i + 1) * 8]
    return total


def hidden_back(rows, width):
    tile = 32

    def kernel(own, got, hidden, back, gain, weight, grad_ref, low_ref, attended_ref, sums_ref):
        sums = [jnp.zeros((8, width), jnp.float32) for _ in range(3)]
        for t in range(rows // tile):
            here = slice(t * tile, (t + 1) * tile)
            pulled, terms = norm_back(hidden[here, :], gain[...], own[here, :] + wide(got[here, :]))
            grad = wide(back[here, :]) + pulled
            grad_ref[here, :] = grad
            low_ref[here, :] = low(grad)
            for n, part in enumerate((terms, own[here, :] + wide(got[here, :]), grad)):
                sums[n] = sums[n] + fold_rows(part)
        for n in range(3):
            sums_ref[n : n + 1, :] = jnp.sum(sums[n], axis=0, keepdims=True)
        attended_ref[...] = low(cols_dot(low_ref[...], weight[...]))

    vmem = pl.BlockSpec(memory_space=pltpu.VMEM)
    return pl.pallas_call(
        kernel,
        in_specs=[vmem] * 6,
        out_specs=[vmem] * 4,
        out_shape=[
            jax.ShapeDtypeStruct((rows, width), jnp.float32),
            jax.ShapeDtypeStruct((rows, width), jnp.bfloat16),
            jax.ShapeDtypeStruct((rows, width), jnp.bfloat16),
            jax.ShapeDtypeStruct((3, width), jnp.float32),
        ],
        compiler_params=pltpu.CompilerParams(vmem_limit_bytes=VMEM_LIMIT),
        cost_estimate=NO_COST,
        name="hidden_back",
    )


def stream_back(rows, width, parts, row_groups, piece):
    tile = 32
    chips = parts // 2

    def kernel(
        place_ref, kv_0, kv_1, kv_2, kv_3, queries, weight, tokens, gain, grad_hidden, normed, back, hidden_sums,
        units_a, units_b, input_ref, even_ref, odd_ref, grad_kv, grads, turned, product, small,
    ):
        place = place_ref[0]
        sums = [jnp.zeros((8, width), jnp.float32) for _ in range(4)]
        value_sums = jnp.zeros((8, 2 * HS), jnp.float32)
        for t in range(rows // tile):
            here = slice(t * tile, (t + 1) * tile)
            total = wide(kv_0[here, :]) + wide(kv_1[here, :]) + wide(kv_2[here, :]) + wide(kv_3[here, :])
            grad_kv[here, :] = low(total)
            value_sums = value_sums + fold_rows(total)
        turn((normed,), turned)
        product[...] = dot(turned[...], grad_kv[...])
        grads[...] = cols_dot(queries[...], weight[:, :width]) + cols_dot(grad_kv[...], weight[:, width:])
        for t in range(rows // tile):
            here = slice(t * tile, (t + 1) * tile)
            grad = grads[here, :]
            pulled, terms = norm_back(wide(tokens[here, :]), gain[...], grad)
            input_ref[here, :] = grad_hidden[here, :] + pulled
            for n, part in enumerate((terms, grad, wide(queries[here, :]), wide(back[here, :]))):
                sums[n] = sums[n] + fold_rows(part)
        sums = [jnp.sum(part, axis=0, keepdims=True) for part in sums]
        small[...] = jnp.zeros_like(small)
        rows_in = (sums[0], sums[1], hidden_sums[0:1, :], hidden_sums[1:2, :], sums[2], hidden_sums[2:3, :], sums[3])
        for n, row in enumerate(rows_in):
            for j in range(width // 128):
                line = n * (width // 128) + j
                small[line : line + 1, :] = row[:, j * 128 : (j + 1) * 128]
        start = 7 * (width // 128)
        small[start : start + 1, :] = jnp.sum(value_sums, axis=0, keepdims=True)
        lines = FF // parts // 128
        for m in range(chips):
            units = (units_a, units_b)[m // 2]
            for j in range(lines):
                line = start + 1 + (place ^ (2 * m)) * lines + j
                at = (m % 2 * lines + j) * 128
                small[pl.ds(line, 1), :] = units[:, at : at + 128]
        for k in range(parts):
            ref = odd_ref if k % 2 else even_ref
            mine = low(small[pl.ds(pl.multiple_of((place ^ k) * piece, 8), piece), :])
            for w in range(row_groups):
                at = pl.multiple_of(w * piece * parts + (place ^ k) * piece, 8)
                ref[k // 2, w, :, :128] = low(product[pl.ds(at, piece), :])
                ref[k // 2, w, :, 128:] = mine

    vmem = pl.BlockSpec(memory_space=pltpu.VMEM)
    stack = jax.ShapeDtypeStruct((chips, row_groups, piece, 256), jnp.bfloat16)
    return pl.pallas_call(
        kernel,
        in_specs=[pl.BlockSpec(memory_space=pltpu.SMEM)] + [vmem] * 14,
        out_specs=[vmem] * 3,
        out_shape=[jax.ShapeDtypeStruct((rows, width), jnp.float32), stack, stack],
        scratch_shapes=[
            pltpu.VMEM((rows, 2 * HS), jnp.bfloat16),
            pltpu.VMEM((rows, width), jnp.float32),
            pltpu.VMEM((width, rows), jnp.bfloat16),
            pltpu.VMEM((width, 2 * HS), jnp.float32),
            pltpu.VMEM((parts * piece, 128), jnp.float32),
        ],
        compiler_params=pltpu.CompilerParams(vmem_limit_bytes=VMEM_LIMIT),
        cost_estimate=NO_COST,
        name="stream_back",
    )


def attn_grads(rows, width, row_groups, parts, piece):
    def kernel(place_ref, left_a, right_a, left_b, right_b, even_ref, odd_ref, turned, total):
        place = place_ref[0]
        for n, (left, right) in enumerate(((left_a, right_a), (left_b, right_b))):
            for i in range(rows // 128):
                turned[:, i * 128 : (i + 1) * 128] = low(wide(left[i * 128 : (i + 1) * 128, :]).T)
            total[:, n * width : (n + 1) * width] = dot(turned[...], right[...])
        for k in range(parts):
            ref = odd_ref if k % 2 else even_ref
            for w in range(row_groups):
                at = pl.multiple_of(w * piece * parts + (place ^ k) * piece, 8)
                ref[k // 2, w] = low(total[pl.ds(at, piece), :])

    vmem = pl.BlockSpec(memory_space=pltpu.VMEM)
    shape = jax.ShapeDtypeStruct((parts // 2, row_groups, piece, 2 * width), jnp.bfloat16)
    return pl.pallas_call(
        kernel,
        grid_spec=pltpu.PrefetchScalarGridSpec(
            num_scalar_prefetch=1,
            grid=(),
            in_specs=[vmem] * 4,
            out_specs=[vmem] * 2,
            scratch_shapes=[pltpu.VMEM((width, rows), jnp.bfloat16), pltpu.VMEM((width, 2 * width), jnp.float32)],
        ),
        out_shape=[shape] * 2,
        compiler_params=pltpu.CompilerParams(vmem_limit_bytes=VMEM_LIMIT),
        cost_estimate=NO_COST,
        name="attn_grads",
    )


def attn_update(rows, columns, width, parts, piece):
    qkv = columns - width

    def kernel(place_ref, even_ref, odd_ref, master, first, second, *outs):
        place = place_ref[0]
        for k in range(parts):
            ref = odd_ref if k % 2 else even_ref
            here = pl.ds(pl.multiple_of((place ^ k) * piece, 8), piece)
            for cols, source in (
                (slice(0, width), slice(0, width)),
                (slice(width, qkv), slice(2 * width, columns)),
                (slice(qkv, columns), slice(width, 2 * width)),
            ):
                grad = wide(ref[k // 2, :, source])
                got = adam_update(master[here, cols], grad, first[here, cols], second[here, cols], 0.1, 0.1)
                outs[0][here, cols] = got[0]
                outs[1][here, cols] = got[1]
                outs[2][here, cols] = got[2]

    vmem = pl.BlockSpec(memory_space=pltpu.VMEM)
    return pl.pallas_call(
        kernel,
        grid_spec=pltpu.PrefetchScalarGridSpec(
            num_scalar_prefetch=1, grid=(), in_specs=[vmem] * 5, out_specs=[vmem] * 3, scratch_shapes=[]
        ),
        out_shape=[jax.ShapeDtypeStruct((rows, columns), jnp.float32)] * 3,
        compiler_params=pltpu.CompilerParams(vmem_limit_bytes=VMEM_LIMIT),
        cost_estimate=NO_COST,
        name="attn_update",
    )


def ffn_update(rows, units, parts, chunk):
    per_row = 2 * units // 128
    rows_once = 32
    lines = rows_once * per_row

    def kernel(place_ref, even, odd, master, first, second, first_out, second_out, master_out, total):
        place = place_ref[0]
        for k in range(parts):
            grad = odd if k % 2 else even
            for j in range(chunk // 128):
                for which in range(2):
                    line = (place ^ k) * (2 * chunk // 128) + 2 * j + which
                    total[pl.ds(line, rows_once, per_row), :] = wide(
                        grad[k // 2, which, :, j * 128 : (j + 1) * 128]
                    )
        for t in range(lines // 64):
            own = slice(t * 64, (t + 1) * 64)
            got = adam_update(master[own, :], total[own, :], first[own, :], second[own, :], 0.1, 0.1)
            first_out[own, :] = got[0]
            second_out[own, :] = got[1]
            master_out[own, :] = got[2]

    block = pl.BlockSpec((lines, 128), lambda i, *_: (i, 0))
    stack = pl.BlockSpec((parts // 2, 2, rows_once, chunk), lambda i, *_: (0, 0, i, 0))
    call = pl.pallas_call(
        kernel,
        grid_spec=pltpu.PrefetchScalarGridSpec(
            num_scalar_prefetch=1,
            grid=(rows // rows_once,),
            in_specs=[stack] * 2 + [block] * 3,
            out_specs=[block] * 3,
            scratch_shapes=[pltpu.VMEM((lines, 128), jnp.float32)],
        ),
        out_shape=[jax.ShapeDtypeStruct((rows * per_row, 128), jnp.float32)] * 3,
        compiler_params=pltpu.CompilerParams(vmem_limit_bytes=VMEM_LIMIT),
        cost_estimate=NO_COST,
        name="ffn_update",
    )

    def fold(array):
        return jnp.swapaxes(array.reshape(rows, 2, units // 128, 128), 1, 2).reshape(-1, 128)

    def unfold(array):
        return jnp.swapaxes(array.reshape(rows, units // 128, 2, 128), 1, 2).reshape(rows, 2, units)

    def run(place, even, odd, master, first, second):
        return tuple(unfold(array) for array in call(place, even, odd, fold(master), fold(first), fold(second)))

    return run


def shards(
    tokens,
    doc_starts,
    attn_master,
    attn_mom,
    attn_sq,
    ffn_master,
    ffn_mom,
    ffn_sq,
    small_master,
    small_mom,
    small_sq,
    cotangent,
):
    ctx_count, wt_count = lax.axis_size("ctx"), lax.axis_size("wt")
    ctx_place, wt_place = lax.axis_index("ctx"), lax.axis_index("wt")
    batches, rows_here, width = tokens.shape
    qkv_cols = width + 2 * HS
    attn_columns = attn_master.shape[1]
    all_rows = batches * rows_here
    shard_rows = attn_master.shape[0]
    piece_rows = shard_rows // ctx_count
    chunk = FF // ctx_count
    chips = ctx_count // 2
    order = ctx_place ^ jnp.arange(ctx_count, dtype=jnp.int32)
    (
        gain_one,
        shift_one,
        gain_two,
        shift_two,
        bias_query,
        bias_out,
        bias_proj,
        bias_value,
        bias_hidden,
    ) = split_small(small_master)
    runs = 2 if batches % 2 == 0 else 1
    places = [jnp.stack([ctx_place, jnp.int32(run * (batches // runs))]) for run in range(runs)]
    place = places[0]
    wt_half = wt_count // 2
    out_rows = shard_rows // chips
    run_forward, run_backward = attention_kernels(batches, rows_here, width, ctx_count, runs)
    ffn_first, ffn_second, ffn_third, ffn_down = ffn_kernels(all_rows, width, chunk, wt_count)
    step = Steps()

    def both(own, got, place, bit, axis=0):
        ahead, behind = jnp.stack([own, got], axis), jnp.stack([got, own], axis)
        return jnp.where((place & bit) == 0, ahead, behind)

    def in_order(even, odd):
        buffer = jnp.zeros((ctx_count,) + even.shape[1:], even.dtype)
        for m in range(chips):
            buffer = put(buffer, even[m][None], ctx_place ^ (2 * m), 0)
            buffer = put(buffer, odd[m][None], ctx_place ^ (2 * m + 1), 0)
        return buffer

    def send_chips(piece):
        return [xor_send(piece, mask) for mask in range(2, ctx_count, 2)]

    def split_wt(total, bit):
        ahead, behind = jnp.split(total, 2)
        kept, sent = jnp.where((wt_place & bit) == 0, ahead, behind), jnp.where((wt_place & bit) == 0, behind, ahead)
        return kept, sent

    def add_low(*arrays):
        return low(sum(wide(array) for array in arrays))

    qkv = low(lax.dynamic_slice(attn_master, (ctx_place * piece_rows, 0), (piece_rows, qkv_cols)))
    qkv_got = xor_wt(qkv, 1)
    rest = low(jnp.swapaxes(take(ffn_master, ctx_place, 2, chunk), 0, 1).reshape(2 * shard_rows, chunk))
    out = low(
        lax.dynamic_slice(
            attn_master, (ctx_place // 2 * out_rows, qkv_cols + ctx_place % 2 * chunk), (out_rows, chunk)
        )
    )
    qkv_got, rest, out = together(qkv_got, rest, out)
    rest_got, out_got = xor_wt(rest, 1), xor_wt(out, 1)
    flat_tokens = tokens.reshape(all_rows, width)
    qkv = both(qkv, qkv_got, wt_place, 1)
    qkv_got = xor_wt(qkv, 2)
    normed_low = step(
        lambda tokens, gain, shift: low(layer_norm(wide(tokens), gain, shift)), flat_tokens, gain_one, shift_one
    )
    qkv_got, rest_got, out_got = together(qkv_got, rest_got, out_got)
    qkv = both(qkv, qkv_got, wt_place, 2).reshape((wt_count,) + qkv.shape[1:])
    ups, downs = [both(rest[rows], rest_got[rows], wt_place, 1) for rows in (slice(shard_rows), slice(shard_rows, None))]
    out = both(out, out_got, wt_place, 1)
    qkv, ups, downs, out = together(qkv, ups, downs, out)
    qkv_got = xor_send(qkv, 2)
    ups_got, out_got = xor_wt(ups, 2), xor_wt(out, 2)
    back_low = cotangent.reshape(all_rows, width)
    qkv_got, back_low = together(qkv_got, back_low)
    qkv = both(qkv, qkv_got, ctx_place, 2)
    qkv_got = xor_send(qkv, 4)
    back_other = xor_send(back_low, 1)
    qkv_got, out_got, ups_got, downs = together(qkv_got, out_got, ups_got, downs)
    out = both(out, out_got, wt_place, 2).reshape((wt_count,) + out.shape[1:])
    qkv = both(qkv, qkv_got, ctx_place, 4)
    qkv_got, downs_got = xor_send(qkv, 1), xor_wt(downs, 2)
    back_turned = turn_both(back_low, back_other)
    qkv_got, back_turned = together(qkv_got, back_turned)

    def project(own, got, normed):
        blocks = both(own, got, ctx_place, 1, 2)
        weight = jnp.transpose(blocks, (3, 0, 1, 2, 4, 5)).reshape(width, qkv_cols)
        mixed = dot(normed, weight)
        queries = low(mixed[:, :width] + bias_query).reshape(batches, rows_here, width)
        kv_bias = jnp.concatenate([jnp.zeros((HS,), jnp.float32), bias_value])
        kv_local = low(mixed[:, width:] + kv_bias).reshape(batches, rows_here, 2 * HS)
        return weight, queries, kv_local

    weight_qkv, queries, kv_local = project(qkv, qkv_got, normed_low)
    kv_got = xor_send(kv_local, 2)
    kv_got, downs_got = together(kv_got, downs_got)
    kv_even = both(kv_local, kv_got, ctx_place, 2)
    kv_even, out = together(kv_even, out)
    kv_got = xor_send(kv_even, 4)
    out_got = send_chips(out)
    kv_got, *out_got = together(kv_got, *out_got)
    kv_even = both(kv_even, kv_got, ctx_place, 4).reshape((chips,) + kv_local.shape)
    kv_odd = xor_send(kv_even, 1)
    out_even = jnp.stack([out] + out_got)
    out_odd = xor_send(out_even, 1)
    kv_even, ups_got, downs_got = together(kv_even, ups_got, downs_got)
    rest = jnp.concatenate(
        [
            both(own, got, wt_place, 2).reshape((wt_count,) + own.shape[1:])
            for own, got in ((ups, ups_got), (downs, downs_got))
        ],
        axis=1,
    )
    rest_x, rest_y = xor_send(rest, 2), xor_send(rest, 4)
    queries, out_even, rest = together(queries, out_even, rest)

    attended_low, attended, logs = step(run_forward, doc_starts, place, queries, kv_even, kv_odd)
    attended_low = attended_low.reshape(all_rows, width)
    low_half, high_half = step(lambda x, y: (x[:wt_half], y[wt_half:]), rest_x, rest_y)
    diagonal_low, diagonal_high = xor_send(low_half, 4), xor_send(high_half, 2)

    def join_out(even, odd):
        columns = jnp.where((ctx_place & 1) == 0, jnp.concatenate([even, odd], axis=3), jnp.concatenate([odd, even], axis=3))
        for n in range(chips.bit_length() - 1):
            pairs = columns.reshape((-1, 2, 1 << n) + columns.shape[1:])
            columns = jnp.where((ctx_place & (2 << n)) == 0, pairs, pairs[:, ::-1]).reshape(columns.shape)
        return jnp.swapaxes(columns, 0, 1).reshape(width, width)

    weight_out = step(join_out, out_even, out_odd)
    hidden, normed_two = step(
        out_projection(all_rows, width), attended_low, weight_out, flat_tokens, bias_out[None], gain_two[None],
        shift_two[None],
    )
    normed_other = xor_send(normed_two, 1)

    bias_parts = bias_hidden.reshape(ctx_count, chunk)[order[::2]].reshape(1, chips * chunk)
    bias_near, bias_far = jnp.split(bias_parts, 2, axis=1)
    weights = [rest, rest_x, rest_y, diagonal_low, diagonal_high]
    flows = (normed_two, normed_other, back_low, back_other, back_turned)
    act_first, units_first, down_own, down_x, sums_first = step(
        lambda *args: ffn_first(*args[:6], *in_hbm(args[6:])), *flows, bias_near, *weights[:2]
    )
    act_second, units_second, down_y, down_top, down_bottom, sums_second, back_own, back_part = step(
        lambda *args: ffn_second(*args[:6], *in_hbm(args[6:])), *flows, bias_far, units_first, *weights
    )
    back_got = xor_send(back_part, 1)
    top_got, bottom_got = xor_send(down_top, 4), xor_send(down_bottom, 2)

    def meet(along_x, along_y, top, bottom):
        half = width // 2
        return (
            jnp.concatenate([add_low(along_x[:half], top), along_x[half:]]),
            jnp.concatenate([along_y[:half], add_low(along_y[half:], bottom)]),
        )

    up_own, up_x, up_y, up_top, up_bottom = step(
        lambda *args: ffn_third(*args[:2], *in_hbm(args[2:])), normed_two, normed_other, units_first, units_second
    )
    down_x, down_y = step(meet, down_x, down_y, top_got, bottom_got)
    down_got = [xor_send(down_x, 2), xor_send(down_y, 4)]
    top_got, bottom_got = xor_send(up_top, 4), xor_send(up_bottom, 2)

    grad_hidden, grad_hidden_low, grad_attended, hidden_sums = step(
        hidden_back(all_rows, width), back_own, back_got, hidden, back_low, gain_two[None], weight_out
    )
    grad_attended = grad_attended.reshape(batches, rows_here, width)
    up_x, up_y = step(meet, up_x, up_y, top_got, bottom_got)
    up_got = [xor_send(up_x, 2), xor_send(up_y, 4)]

    def by_wt(*arrays):
        return split_wt(add_low(*arrays).reshape(wt_count, shard_rows, chunk), 2)

    def next_wt(kept, got):
        return split_wt(add_low(kept, got), 1)

    def kv_pieces(evens, odds):
        total = jnp.concatenate([add_low(a, b) for a, b in zip(evens, odds)], axis=1)
        return [lax.dynamic_index_in_dim(total, (ctx_place // 2) ^ m, 0, False) for m in range(chips)]

    backs = [step(run_backward[0], doc_starts, places[0], queries, kv_even, kv_odd, attended, logs, grad_attended)]
    kv_got = [xor_send(backs[0][2], 1)]
    down_kept, down_sent = step(by_wt, down_own, *down_got)
    grad_attended, down_kept, down_sent = together(grad_attended, down_kept, down_sent)
    down_got = xor_wt(down_sent, 2)
    backs += [
        step(run_backward[run], doc_starts, places[run], queries, kv_even, kv_odd, attended, logs, grad_attended)
        for run in range(1, runs)
    ]
    kv_got += [xor_send(back[2], 1) for back in backs[1:]]
    grad_queries = [back[0] for back in backs]
    grad_queries[-1], down_got, *up_got = together(grad_queries[-1], down_got, *up_got)
    grad_query = jnp.concatenate(grad_queries).reshape(all_rows, width)
    down_kept, down_sent = next_wt(down_kept, down_got)
    up_kept, up_sent = by_wt(up_own, *up_got)
    down_kept, down_sent, up_kept, up_sent = together(down_kept, down_sent, up_kept, up_sent)
    down_got, up_got = xor_wt(down_sent, 1), xor_wt(up_sent, 2)
    kv_half = step(kv_pieces, [back[1] for back in backs], kv_got)
    kv_got = [xor_send(kv_half[m], 2 * m) for m in range(1, chips)]
    wide_even, wide_odd = step(
        attn_grads(all_rows, width, wt_count, ctx_count, piece_rows),
        place, normed_low, grad_query, attended_low, grad_hidden_low,
    )
    small_size = small_master.shape[0]
    up_kept, up_sent = step(next_wt, up_kept, up_got)
    kv_got[0], up_kept, up_sent = together(kv_got[0], up_kept, up_sent)
    up_got = xor_wt(up_sent, 1)
    input_grad, tail_even, tail_odd = step(
        stream_back(all_rows, width, ctx_count, wt_count, piece_rows),
        place, *[array.reshape(all_rows, 2 * HS) for array in (kv_half[0], *kv_got)], grad_query, weight_qkv,
        flat_tokens, gain_one[None], grad_hidden, normed_low, back_low, hidden_sums, sums_first, sums_second,
    )
    input_grad = input_grad.reshape(batches, rows_here, width)
    wide_odd, tail_odd = lax.optimization_barrier((wide_odd, tail_odd))
    wide_odd, tail_odd = xor_send(wide_odd, 1), xor_send(tail_odd, 1)
    def attn_pieces(wide_even, wide_odd, tail_even, tail_odd):
        total = jnp.concatenate([add_low(wide_even, wide_odd), add_low(tail_even, tail_odd)], axis=3)
        return [total[m] for m in range(chips)]

    attn_half = step(attn_pieces, wide_even, wide_odd, tail_even, tail_odd)
    attn_got = [xor_send(attn_half[m], 2 * m) for m in range(1, chips)]
    ffn_part = step(
        lambda *arrays: jnp.concatenate([add_low(*arrays[:2]), add_low(*arrays[2:])]), up_kept, up_got, down_kept, down_got
    )
    ffn_got = send_chips(ffn_part)
    down_out, down_other = step(
        lambda *args: ffn_down(*args[:2], *in_hbm(args[2:])), act_first, act_second, *weights
    )
    down_other = xor_send(down_other, 1)
    attn_kept, attn_sent = step(lambda *parts: split_wt(add_low(*parts), 2), attn_half[0], *attn_got)
    attn_got = xor_wt(attn_sent, 2)
    ffn_even = step(lambda *parts: jnp.stack(parts), ffn_part, *ffn_got)
    ffn_odd = xor_send(ffn_even, 1)
    layer_out = step(
        lambda hidden, own, got: low(hidden + own + wide(got) + bias_proj).reshape(batches, rows_here, width),
        hidden, down_out, down_other,
    )
    attn_kept, attn_sent = step(lambda kept, got: split_wt(add_low(kept, got), 1), attn_kept, attn_got)
    attn_got = xor_wt(attn_sent, 1)
    attn_part = step(lambda *parts: add_low(*parts)[0], attn_kept, attn_got)
    attn_got = send_chips(attn_part)

    ffn_new = step(
        ffn_update(shard_rows, FF, ctx_count, chunk), place, ffn_even, ffn_odd, ffn_master, ffn_mom, ffn_sq
    )
    attn_even = step(lambda *parts: jnp.stack(parts), attn_part, *attn_got)
    attn_odd = xor_send(attn_even, 1)
    small_total = in_order(attn_even[..., attn_columns:], attn_odd[..., attn_columns:])
    small_total = wide(small_total.reshape(-1))
    most = small_size - FF - HS
    small_total = jnp.concatenate(
        [small_total[:most], small_total[most + HS : most + 2 * HS], small_total[most + 2 * HS : most + 2 * HS + FF]]
    )
    small_new = adam_update(small_master, small_total, small_mom, small_sq, 1.0, 0.0)
    attn_new = attn_update(shard_rows, attn_columns, width, ctx_count, piece_rows)(
        place, attn_even, attn_odd, attn_master, attn_mom, attn_sq
    )
    return (layer_out, input_grad) + tuple(attn_new) + tuple(ffn_new) + tuple(small_new)


def shift_wt(array, shift):
    count = lax.axis_size("wt")
    return lax.ppermute(array, "wt", [(i, (i + shift) % count) for i in range(count)])


def whole_wt(piece, axis):
    count, place = lax.axis_size("wt"), lax.axis_index("wt")
    shape = list(piece.shape)
    shape[axis] *= count
    buffer = put(jnp.zeros(shape, piece.dtype), piece, place, axis)
    for shift in range(1, count):
        buffer = put(buffer, shift_wt(piece, shift), (place - shift) % count, axis)
    return buffer


def whole_ctx(piece):
    count = lax.axis_size("ctx")
    got = {0: piece}
    for mask in range(2, count, 2):
        got[mask] = xor_send(piece, mask)
    for mask in range(0, count, 2):
        got[mask + 1] = xor_send(got[mask], 1)
    return [got[mask] for mask in range(count)]


def sum_ctx(pieces):
    count = lax.axis_size("ctx")
    half = {}
    for mask in range(count - 2, -1, -2):
        other = xor_send(pieces[mask + 1], 1)
        half[mask] = low(wide(pieces[mask]) + wide(other))
    total = wide(half[0])
    for mask in range(2, count, 2):
        total = total + wide(xor_send(half[mask], mask))
    return total


def sum_wt(array, axis):
    count, place = lax.axis_size("wt"), lax.axis_index("wt")
    size = array.shape[axis] // count
    total = wide(take(array, place, axis, size))
    for shift in range(1, count):
        sent = take(array, (place + shift) % count, axis, size)
        total = total + wide(shift_wt(sent, shift))
    return total


def any_shards(
    tokens,
    doc_starts,
    attn_master,
    attn_mom,
    attn_sq,
    ffn_master,
    ffn_mom,
    ffn_sq,
    small_master,
    small_mom,
    small_sq,
    cotangent,
):
    ctx_count = lax.axis_size("ctx")
    ctx_place = lax.axis_index("ctx")
    wt_count = lax.axis_size("wt")
    batches, rows_here, width = tokens.shape
    heads = width // HS
    qkv_cols = width + 2 * HS
    all_rows = batches * rows_here
    shard_rows = attn_master.shape[0]
    piece_rows = shard_rows // ctx_count
    chunk = FF // ctx_count
    order = ctx_place ^ jnp.arange(ctx_count, dtype=jnp.int32)
    (
        gain_one,
        shift_one,
        gain_two,
        shift_two,
        bias_query,
        bias_out,
        bias_proj,
        bias_value,
        bias_hidden,
    ) = split_small(small_master)

    attn_piece = low(take(attn_master, ctx_place, 0, piece_rows))

    def whole_rows(piece):
        parts = whole_ctx(whole_wt(piece[None], 0))
        buffer = jnp.zeros((wt_count, ctx_count) + piece.shape, piece.dtype)
        for k, part in enumerate(parts):
            buffer = put(buffer, part[:, None], ctx_place ^ k, 1)
        return buffer.reshape((width,) + piece.shape[1:])

    weight_qkv = whole_rows(attn_piece[:, :qkv_cols])
    weight_out = whole_rows(attn_piece[:, qkv_cols:])
    ffn_piece = low(jnp.swapaxes(take(ffn_master, ctx_place, 2, chunk), 0, 1))
    ffn_parts = whole_ctx(whole_wt(ffn_piece, 1))
    bias_parts = bias_hidden.reshape(ctx_count, chunk)[order]

    stream = wide(tokens.reshape(all_rows, width))
    normed, norm_back_one = jax.vjp(layer_norm, stream, gain_one, shift_one)
    normed_low = low(normed)
    mixed = dot(normed_low, weight_qkv)
    queries = low(mixed[:, :width] + bias_query)
    kv_local = low(
        mixed[:, width:] + jnp.concatenate([jnp.zeros((HS,), jnp.float32), bias_value])
    ).reshape(batches, rows_here, 2 * HS)
    kv_parts = jnp.stack(whole_ctx(kv_local), axis=1).reshape(
        batches, ctx_count * rows_here, 2 * HS
    )
    keys_all, values_all = kv_parts[..., :HS], kv_parts[..., HS:]
    local_pos = jnp.arange(rows_here, dtype=jnp.int32)
    query_pos = ctx_place * rows_here + local_pos
    key_pos = (order[:, None] * rows_here + local_pos[None, :]).reshape(-1)
    queries = queries.reshape(batches, rows_here * heads, HS)
    scale = HS ** (-0.5)
    attended_list, log_list, allowed_list = [], [], []
    for b in range(batches):
        starts = doc_starts[b]
        query_doc = jnp.sum((starts[None, :] <= query_pos[:, None]).astype(jnp.int32), axis=1)
        key_doc = jnp.sum((starts[None, :] <= key_pos[:, None]).astype(jnp.int32), axis=1)
        allowed = (query_doc[:, None] == key_doc[None, :]) & (key_pos[None, :] <= query_pos[:, None])
        allowed = jnp.repeat(allowed, heads, axis=0)
        allowed_list.append(allowed)
        scores = jnp.where(allowed, cols_dot(queries[b], keys_all[b]) * scale, -1e30)
        peak = jnp.max(scores, axis=-1, keepdims=True)
        expo = jnp.exp(scores - peak)
        total = jnp.sum(expo, axis=-1, keepdims=True)
        attended_list.append(dot(low(expo / total), values_all[b]))
        log_list.append(peak + jnp.log(total))
    attended = jnp.stack(attended_list)
    attended_low = low(attended).reshape(all_rows, width)
    hidden = stream + dot(attended_low, weight_out) + bias_out
    normed_two, norm_back_two = jax.vjp(layer_norm, hidden, gain_two, shift_two)
    normed_two_low = low(normed_two)

    back_low = cotangent.reshape(all_rows, width)
    back_rows = wide(back_low)
    down_vals = jnp.zeros((all_rows, width), jnp.float32)
    grad_normed_two = jnp.zeros((all_rows, width), jnp.float32)
    ffn_grads, hidden_grads = [], []
    for k in range(ctx_count):
        weight_up, weight_down = ffn_parts[k][0], ffn_parts[k][1]
        value, slope = gelu_both(dot(normed_two_low, weight_up) + bias_parts[k])
        act = low(value)
        down_vals = down_vals + cols_dot(act, weight_down)
        grad_up = low(dot(back_low, weight_down) * slope)
        hidden_grads.append(jnp.sum(wide(grad_up), axis=0))
        grad_normed_two = grad_normed_two + cols_dot(grad_up, weight_up)
        ffn_grads.append(
            jnp.stack([low(rows_dot(normed_two_low, grad_up)), low(rows_dot(back_low, act))])
        )
    layer_out = low(hidden + down_vals + bias_proj).reshape(batches, rows_here, width)
    grad_bias_proj = jnp.sum(back_rows, axis=0)
    grad_bias_hidden = jnp.stack(hidden_grads)[order].reshape(FF)
    ffn_part = low(sum_wt(low(sum_ctx(ffn_grads)), 1))

    grad_hidden_part, grad_gain_two, grad_shift_two = norm_back_two(grad_normed_two)
    grad_hidden = back_rows + grad_hidden_part
    grad_bias_out = jnp.sum(grad_hidden, axis=0)
    grad_hidden_low = low(grad_hidden)
    grad_out = rows_dot(attended_low, grad_hidden_low)

    def summed_rows(grad):
        blocks = low(grad).reshape(wt_count, ctx_count, piece_rows, grad.shape[1])
        pieces = [take(blocks, ctx_place ^ k, 1, 1)[:, 0] for k in range(ctx_count)]
        part = low(sum_wt(low(sum_ctx(pieces)), 0)[0])
        buffer = jnp.zeros((ctx_count,) + part.shape, part.dtype)
        for k, got in enumerate(whole_ctx(part)):
            buffer = put(buffer, got[None], ctx_place ^ k, 0)
        return wide(buffer.reshape(shard_rows, grad.shape[1]))

    out_total = summed_rows(grad_out)

    grad_attended = low(cols_dot(grad_hidden_low, weight_out)).reshape(
        batches, rows_here * heads, HS
    )
    grad_query_list, grad_kv_list = [], []
    for b in range(batches):
        grads = grad_attended[b]
        delta = jnp.sum(wide(grads) * attended[b], axis=-1, keepdims=True)
        scores = jnp.where(allowed_list[b], cols_dot(queries[b], keys_all[b]) * scale, -1e30)
        weights = jnp.exp(scores - log_list[b])
        grad_scores = low(weights * (cols_dot(grads, values_all[b]) - delta))
        grad_query_list.append(low(dot(grad_scores, keys_all[b]) * scale))
        grad_kv_list.append(
            jnp.concatenate(
                [
                    low(rows_dot(grad_scores, queries[b]) * scale),
                    low(rows_dot(low(weights), grads)),
                ],
                axis=1,
            )
        )
    grad_query = jnp.stack(grad_query_list).reshape(all_rows, width)
    grad_kv = jnp.stack(grad_kv_list).reshape(batches, ctx_count, rows_here, 2 * HS)
    grad_kv_low = low(sum_ctx([grad_kv[:, k] for k in range(ctx_count)])).reshape(
        all_rows, 2 * HS
    )
    grad_bias_query = jnp.sum(wide(grad_query), axis=0)
    grad_bias_value = jnp.sum(wide(grad_kv_low[:, HS:]), axis=0)
    grad_mixed = jnp.concatenate([grad_query, grad_kv_low], axis=1)
    qkv_total = summed_rows(rows_dot(normed_low, grad_mixed))
    grad_normed = cols_dot(grad_mixed, weight_qkv)
    grad_stream_part, grad_gain_one, grad_shift_one = norm_back_one(grad_normed)
    input_grad = (grad_hidden + grad_stream_part).reshape(batches, rows_here, width)

    ffn_buffer = jnp.zeros((ctx_count,) + ffn_part.shape, ffn_part.dtype)
    for k, got in enumerate(whole_ctx(ffn_part)):
        ffn_buffer = put(ffn_buffer, got[None], ctx_place ^ k, 0)
    ffn_total = wide(jnp.transpose(ffn_buffer, (2, 1, 0, 3)).reshape(shard_rows, 2, FF))
    attn_total = jnp.concatenate([qkv_total, out_total], axis=1)
    grad_small = jnp.concatenate(
        [
            grad_gain_one,
            grad_shift_one,
            grad_gain_two,
            grad_shift_two,
            grad_bias_query,
            grad_bias_out,
            grad_bias_proj,
            grad_bias_value,
            grad_bias_hidden,
        ]
    )
    small_total = lax.psum(grad_small, ("ctx", "wt"))
    attn_new = adam_update(attn_master, attn_total, attn_mom, attn_sq, 0.1, 0.1)
    ffn_new = adam_update(ffn_master, ffn_total, ffn_mom, ffn_sq, 0.1, 0.1)
    small_new = adam_update(small_master, small_total, small_mom, small_sq, 1.0, 0.0)
    return (layer_out, input_grad) + attn_new + ffn_new + small_new


def solution(mesh):
    rows, cube = P("wt", None), P("wt", None, None)
    flow = P("wt", "ctx", None)
    in_specs = (flow, rows, rows, rows, rows, cube, cube, cube, P(), P(), P(), flow)
    out_specs = (flow, flow, rows, rows, rows, cube, cube, cube, P(), P(), P())
    ctx_count, wt_count = mesh.shape["ctx"], mesh.shape["wt"]
    fitted = (ctx_count, wt_count) == (8, 4)
    body = shards if fitted else any_shards
    return jax.shard_map(body, mesh=mesh, in_specs=in_specs, out_specs=out_specs, check_vma=False)
```

```python
import jax
import jax.numpy as jnp
from jax import lax
from jax.experimental import pallas as pl
from jax.experimental.pallas import tpu as pltpu
from jax.sharding import PartitionSpec as P

D = 768
HS = 64
FF = 3072
STEP = 10


NORM_EPS = 1e-05
GELU_COEF = 0.7978845608028654
GELU_CUBE = 0.044715
BETA_ONE = 0.9
BETA_TWO = 0.95
ADAM_EPS = 1e-08
VMEM_LIMIT = 22 << 20
NO_COST = pl.CostEstimate(flops=0, bytes_accessed=0, transcendentals=0)


def layer_norm(values, gain, shift):
    centre = values - jnp.mean(values, axis=-1, keepdims=True)
    spread = jnp.mean(centre * centre, axis=-1, keepdims=True)
    return centre * lax.rsqrt(spread + NORM_EPS) * gain + shift


def gelu_both(u):
    square = u * u
    share = 0.5 * jnp.tanh(u * (GELU_COEF * GELU_CUBE * square + GELU_COEF)) + 0.5
    bend = u * (6.0 * GELU_COEF * GELU_CUBE * square + 2.0 * GELU_COEF)
    return u * share, share * ((1.0 - share) * bend) + share


def split_small(small):
    return (
        small[0:D],
        small[D : 2 * D],
        small[2 * D : 3 * D],
        small[3 * D : 4 * D],
        small[4 * D : 5 * D],
        small[5 * D : 6 * D],
        small[6 * D : 7 * D],
        small[7 * D : 7 * D + HS],
        small[7 * D + HS :],
    )


def rows_dot(left, right):
    return lax.dot_general(
        left, right, (((0,), (0,)), ((), ())), preferred_element_type=jnp.float32
    )


def cols_dot(left, right):
    return lax.dot_general(
        left, right, (((1,), (1,)), ((), ())), preferred_element_type=jnp.float32
    )


def dot(left, right):
    return jnp.dot(left, right, preferred_element_type=jnp.float32)


def low(values):
    return values.astype(jnp.bfloat16)


def wide(values):
    return values.astype(jnp.float32)


def adam_update(master, gradient, first, second, step_rate, decay_rate):
    first_new = BETA_ONE * first + (1.0 - BETA_ONE) * gradient
    second_new = BETA_TWO * second + (1.0 - BETA_TWO) * gradient * gradient
    first_hat = first_new / (1.0 - BETA_ONE**STEP)
    second_hat = second_new / (1.0 - BETA_TWO**STEP)
    master_new = master - step_rate * (
        first_hat / (jnp.sqrt(second_hat) + ADAM_EPS) + decay_rate * master
    )
    return (first_new, second_new, master_new)


def xor_send(array, mask):
    count = lax.axis_size("ctx")
    return lax.ppermute(array, "ctx", [(i, i ^ mask) for i in range(count)])


def xor_wt(array, mask):
    count = lax.axis_size("wt")
    return lax.ppermute(array, "wt", [(i, i ^ mask) for i in range(count)])


class Steps:
    def __init__(self):
        self.last = ()

    def __call__(self, function, *args):
        flat, tree = jax.tree.flatten(args)
        held = lax.optimization_barrier(tuple(flat) + self.last)[: len(flat)]
        result = function(*jax.tree.unflatten(tree, held))
        self.last = tuple(jax.tree.leaves(result))
        return result


def loop(count, body, carry=0):
    return lax.fori_loop(0, count, body, carry)


def rows_at(i, size):
    return pl.ds(pl.multiple_of(i * size, size), size)


def together(*arrays):
    return lax.optimization_barrier(arrays)


def put(buffer, piece, place, axis):
    starts = [0] * buffer.ndim
    starts[axis] = place * piece.shape[axis]
    return lax.dynamic_update_slice(buffer, piece, starts)


def take(buffer, place, axis, size):
    return lax.dynamic_slice_in_dim(buffer, place * size, size, axis)


def attention_kernels(batches, rows, width, parts, runs):
    half_parts = parts // 2
    keys = parts * rows
    pair = 2 * HS
    groups = width // (2 * pair)
    factor = HS ** (-0.5) * 1.4426950408889634
    tile = 32

    def lanes(shape):
        return lax.broadcasted_iota(jnp.int32, shape, 1)

    def spread(even_ref, odd_ref, key_ref, value_ref):
        for j in range(parts):
            ref = even_ref if j < half_parts else odd_ref
            block = wide(ref[j % half_parts, 0])
            turned = pltpu.roll(block, HS, 1)
            first = lanes(block.shape) < HS
            here = pl.ds(j * rows, rows)
            key_ref[0, here, :] = low(jnp.where(first, block, 0.0))
            key_ref[1, here, :] = low(jnp.where(first, 0.0, turned))
            value_ref[0, here, :] = low(jnp.where(first, turned, 0.0))
            value_ref[1, here, :] = low(jnp.where(first, 0.0, block))

    def doc_begin(starts_ref, stream, positions):
        begin = jnp.zeros_like(positions)
        for j in range(starts_ref.shape[1]):
            start = starts_ref[stream, j]
            begin = jnp.where(start <= positions, jnp.maximum(begin, start), begin)
        return begin

    def forward(starts_ref, place_ref, query_ref, even_ref, odd_ref, low_ref, full_ref, log_ref, cap, key, value, weight):
        stream, place = pl.program_id(0), place_ref[0]
        spread(even_ref, odd_ref, key, value)
        query_pos = place * rows + lax.broadcasted_iota(jnp.int32, (rows, 1), 0)
        begin = doc_begin(starts_ref, stream, query_pos)
        for j in range(parts):
            key_pos = (2 * (j % half_parts) + (place + j // half_parts) % 2) * rows + lax.broadcasted_iota(jnp.int32, (rows, rows), 1)
            allowed = (key_pos >= begin) & (key_pos <= query_pos)
            cap[:, j * rows : (j + 1) * rows] = jnp.where(allowed, 3.0e38, -1e30)
        column = lanes((tile, pair))
        logs = [jnp.zeros((tile, pair), jnp.float32) for _ in range(rows // tile)]
        for g in range(groups):
            at = g * 2 * pair
            two = jnp.concatenate([query_ref[0, :, at : at + pair], query_ref[0, :, at + pair : at + 2 * pair]], axis=0)
            totals = []
            for half in range(2):
                scores = cols_dot(two, key[half])
                norms = []
                for t in range(2 * rows // tile):
                    own = slice(t * tile, (t + 1) * tile)
                    n = t % (rows // tile)
                    part = jnp.minimum(scores[own] * factor, cap[n * tile : (n + 1) * tile, :])
                    peak = jnp.max(part, axis=1, keepdims=True)
                    expo = jnp.exp2(part - peak)
                    norm = jnp.sum(expo, axis=1, keepdims=True)
                    weight[half, own, :] = low(expo)
                    norms.append(norm)
                    head = 4 * g + 2 * (t * tile // rows) + half
                    logs[n] = jnp.where(column == head, peak + jnp.log2(norm), logs[n])
                totals.append(dot(weight[half], value[half]) / jnp.concatenate(norms, axis=0))
            total = totals[0] + totals[1]
            for j in range(2):
                part = total[j * rows : (j + 1) * rows]
                full_ref[0, :, at + j * pair : at + (j + 1) * pair] = part
                low_ref[0, :, at + j * pair : at + (j + 1) * pair] = low(part)
        for n, log in enumerate(logs):
            log_ref[0, n * tile : (n + 1) * tile, :] = log

    def backward(
        starts_ref, place_ref, query_ref, even_ref, odd_ref, full_ref, log_ref, grad_ref,
        query_grad_ref, even_grad_ref, odd_grad_ref,
        cap, key, value, key_turned, log_rows, delta_rows, weight_buf, score_buf, query_buf, grad_buf,
    ):
        stream, place = pl.program_id(0) + place_ref[1], place_ref[0]
        spread(even_ref, odd_ref, key, value)
        query_pos = place * rows + lax.broadcasted_iota(jnp.int32, (1, rows), 1)
        begin = doc_begin(starts_ref, stream, query_pos)
        for j in range(parts):
            key_pos = (2 * (j % half_parts) + (place + j // half_parts) % 2) * rows + lax.broadcasted_iota(jnp.int32, (rows, rows), 0)
            allowed = (key_pos >= begin) & (key_pos <= query_pos)
            cap[j * rows : (j + 1) * rows, :] = jnp.where(allowed, 3.0e38, -1e30)
            here = pl.ds(j * rows, rows)
            key_turned[:, j * rows : (j + 1) * rows] = low(wide(key[0, here, :]).T[:HS])
        log_rows[...] = log_ref[0].T[: log_rows.shape[0]]
        head_of = lax.broadcasted_iota(jnp.int32, (delta_rows.shape[0], width), 1) // HS
        chosen = (head_of == lax.broadcasted_iota(jnp.int32, (delta_rows.shape[0], width), 0)).astype(jnp.float32)
        delta_rows[...] = lax.dot_general(
            chosen, wide(grad_ref[0]) * full_ref[0], (((1,), (1,)), ((), ())),
            precision=lax.Precision.HIGHEST, preferred_element_type=jnp.float32,
        )
        first = lanes((2 * rows, pair)) < HS
        for g in range(groups):
            at = g * 2 * pair
            both, both_grad = query_ref[0, :, at : at + 2 * pair], grad_ref[0, :, at : at + 2 * pair]
            two = jnp.concatenate([both[:, :pair], both[:, pair:]], axis=0)
            two_grad = jnp.concatenate([both_grad[:, :pair], both_grad[:, pair:]], axis=0)
            turned = []
            for half in range(2):
                h = 4 * g + half
                span = slice((2 * g + half) * 2 * rows, (2 * g + half + 1) * 2 * rows)
                keep = first if half == 0 else jnp.logical_not(first)
                query_buf[span, :] = low(jnp.where(keep, wide(two), 0.0))
                grad_buf[span, :] = low(jnp.where(keep, wide(two_grad), 0.0))
                log = jnp.concatenate([log_rows[h : h + 1, :], log_rows[h + 2 : h + 3, :]], axis=1)
                delta = jnp.concatenate([delta_rows[h : h + 1, :], delta_rows[h + 2 : h + 3, :]], axis=1)
                scores, weight_grads = cols_dot(key[half], two), cols_dot(value[half], two_grad)
                for t in range(keys // (2 * tile)):
                    own = slice(t * 2 * tile, (t + 1) * 2 * tile)
                    limit = cap[own, :]
                    limit = jnp.concatenate([limit, limit], axis=1)
                    weights = jnp.exp2(jnp.minimum(scores[own] * factor, limit) - log)
                    weight_buf[own, span] = low(weights)
                    score_buf[own, span] = low(weights * (weight_grads[own] - delta))
                turned.append(dot(key_turned[...], score_buf[:, span]))
            turned = jnp.concatenate(turned, axis=0) * HS ** (-0.5)
            query_grad_ref[0, :, at : at + pair] = low(turned[:, :rows].T)
            query_grad_ref[0, :, at + pair : at + 2 * pair] = low(turned[:, rows:].T)
        for j in range(parts):
            here = pl.ds(j * rows, rows)
            value_sum = dot(weight_buf[here, :], grad_buf[...])
            key_sum = dot(score_buf[here, :], query_buf[...]) * HS ** (-0.5)
            value_sum = value_sum + pltpu.roll(value_sum, HS, 1)
            key_sum = key_sum + pltpu.roll(key_sum, HS, 1)
            ref = even_grad_ref if j < half_parts else odd_grad_ref
            ref[j % half_parts, 0] = low(jnp.where(lanes((rows, pair)) < HS, key_sum, value_sum))

    def specs(first):
        return (
            pl.BlockSpec((1, rows, width), lambda b, *_: (b + first, 0, 0)),
            pl.BlockSpec((1, rows, pair), lambda b, *_: (b + first, 0, 0)),
            pl.BlockSpec((half_parts, 1, rows, pair), lambda b, *_: (0, b + first, 0, 0)),
        )

    flow, logs, blocks = specs(0)

    shared = [
        pltpu.VMEM((2, keys, pair), jnp.bfloat16),
        pltpu.VMEM((2, keys, pair), jnp.bfloat16),
    ]
    run_forward = pl.pallas_call(
        forward,
        grid_spec=pltpu.PrefetchScalarGridSpec(
            num_scalar_prefetch=2,
            grid=(batches,),
            in_specs=[flow, blocks, blocks],
            out_specs=[flow, flow, logs],
            scratch_shapes=[pltpu.VMEM((rows, keys), jnp.float32)]
            + shared
            + [pltpu.VMEM((2, 2 * rows, keys), jnp.bfloat16)],
        ),
        out_shape=[
            jax.ShapeDtypeStruct((batches, rows, width), jnp.bfloat16),
            jax.ShapeDtypeStruct((batches, rows, width), jnp.float32),
            jax.ShapeDtypeStruct((batches, rows, pair), jnp.float32),
        ],
        compiler_params=pltpu.CompilerParams(vmem_limit_bytes=VMEM_LIMIT),
        cost_estimate=NO_COST,
        name="attention_forward",
    )
    head_rows = -(-(width // HS) // 8) * 8
    all_columns = rows * (width // HS)
    count = batches // runs

    def call_backward(run):
        here_flow, here_logs, here_blocks = specs(run * count)
        return pl.pallas_call(
        backward,
        grid_spec=pltpu.PrefetchScalarGridSpec(
            num_scalar_prefetch=2,
            grid=(count,),
            in_specs=[here_flow, here_blocks, here_blocks, here_flow, here_logs, here_flow],
            out_specs=[flow, blocks, blocks],
            scratch_shapes=[pltpu.VMEM((keys, rows), jnp.float32)]
            + shared
            + [
                pltpu.VMEM((HS, keys), jnp.bfloat16),
                pltpu.VMEM((head_rows, rows), jnp.float32),
                pltpu.VMEM((head_rows, rows), jnp.float32),
                pltpu.VMEM((keys, all_columns), jnp.bfloat16),
                pltpu.VMEM((keys, all_columns), jnp.bfloat16),
                pltpu.VMEM((all_columns, pair), jnp.bfloat16),
                pltpu.VMEM((all_columns, pair), jnp.bfloat16),
            ],
        ),
        out_shape=[
            jax.ShapeDtypeStruct((count, rows, width), jnp.bfloat16),
            jax.ShapeDtypeStruct((half_parts, count, rows, pair), jnp.bfloat16),
            jax.ShapeDtypeStruct((half_parts, count, rows, pair), jnp.bfloat16),
        ],
        compiler_params=pltpu.CompilerParams(vmem_limit_bytes=VMEM_LIMIT),
        cost_estimate=NO_COST,
        name="attention_backward",
    )

    return run_forward, [call_backward(run) for run in range(runs)]


def in_hbm(arrays):
    return [pltpu.with_memory_space_constraint(array, pltpu.HBM) for array in arrays]


def ffn_kernels(rows, width, chunk, wt_count):
    units = 2 * chunk
    all_rows = 2 * rows
    block_rows = width // wt_count
    hbm = pl.BlockSpec(memory_space=pltpu.HBM)
    vmem = pl.BlockSpec(memory_space=pltpu.VMEM)
    params = pltpu.CompilerParams(vmem_limit_bytes=VMEM_LIMIT)

    def fetch(weights, which, held, sem):
        copies = []
        for n, arrays in enumerate(weights):
            blocks = [array.at[block] for array in arrays for block in range(array.shape[0])]
            for row, block in enumerate(blocks):
                copies.append(
                    pltpu.make_async_copy(
                        block.at[pl.ds(which * block_rows, block_rows), :],
                        held.at[pl.ds(row * block_rows, block_rows), pl.ds(n * chunk, chunk)],
                        sem.at[len(copies)],
                    )
                )
        for copy in copies:
            copy.start()
        return copies

    def send(pairs, sems):
        copies = [pltpu.make_async_copy(source, out, sems.at[n]) for n, (source, out) in enumerate(pairs)]
        for copy in copies:
            copy.start()
        return copies

    part_rows = 256
    tile = 16

    def units_of(inputs, grads, bias, held_up, held_down, act, grad_units):
        sums = jnp.zeros((8, units), jnp.float32)
        for s in range(2):

            def part(i, sums):
                here = rows_at(i, part_rows)
                up = dot(inputs[s][here, :], held_up[...])
                act_grad = dot(grads[s][here, :], held_down[...])
                for t in range(part_rows // tile):
                    own = slice(t * tile, (t + 1) * tile)
                    there = pl.ds(pl.multiple_of(s * rows + i * part_rows + t * tile, tile), tile)
                    value, slope = gelu_both(up[own] + bias)
                    grad = act_grad[own] * slope
                    act[there, :] = low(value)
                    grad_units[there, :] = low(grad)
                    sums = sums + (grad[:8] + grad[8:])
                return sums

            sums = loop(rows // part_rows, part, sums)
        return jnp.sum(sums, axis=0, keepdims=True)

    def product_of(turned, right, product):
        def part(i, carry):
            here = rows_at(i, part_rows)
            product[here, :] = low(dot(turned[here, :], right[...]))
            return carry

        loop(width // part_rows, part)

    def back_to(refs, sources, weights):
        for s, ref in enumerate(refs):

            def part(i, carry):
                here = pl.ds(pl.multiple_of(s * rows + i * part_rows, part_rows), part_rows)
                total = cols_dot(sources[0][here, :], weights[0][...]) + cols_dot(sources[1][here, :], weights[1][...])
                ref[rows_at(i, part_rows), :] = total.astype(ref.dtype)
                return carry

            loop(rows // part_rows, part)

    def halves(product, m):
        cols = pl.ds(m * chunk, chunk)
        return [product.at[pl.ds(h * width // 2, width // 2), cols] for h in range(2)]

    def first(
        own, other, grad_own, grad_other, turned, bias, w0, w1, w2, w3,
        act_out, units_out, out_a, out_b, sums_out,
        held_up, held_down, act, grad_units, product, sems, out_sems,
    ):
        weights = ((w0, w1), (w2, w3))
        copies = fetch(weights, 0, held_up, sems.at[0]) + fetch(weights, 1, held_down, sems.at[1])
        for copy in copies:
            copy.wait()
        sums_out[...] = units_of((own, other), (grad_own, grad_other), bias[...], held_up, held_down, act, grad_units)
        sent = send(((act, act_out), (grad_units, units_out)), out_sems.at[0])
        product_of(turned, act, product)
        sent += send(
            ((product.at[:, pl.ds(0, chunk)], out_a), (product.at[:, pl.ds(chunk, chunk)], out_b)), out_sems.at[1]
        )
        for copy in sent:
            copy.wait()

    def second(
        own, other, grad_own, grad_other, turned, bias, units_first, w0, w1, w2, w3, w4, w5, w6, w7,
        act_out, units_out, out_a, out_b, out_c, sums_out, back_own, back_other,
        held_up, held_more, held_down, act, grad_units, more_units, product, sems, out_sems, more_sem,
    ):
        weights, before = ((w4, w5), (w6, w7)), ((w0, w1), (w2, w3))
        copies = fetch(weights, 0, held_up, sems.at[0]) + fetch(weights, 1, held_down, sems.at[1])
        more = fetch(before, 0, held_more, sems.at[2])
        more.append(pltpu.make_async_copy(units_first, more_units, more_sem))
        more[-1].start()
        for copy in copies:
            copy.wait()
        sums_out[...] = units_of((own, other), (grad_own, grad_other), bias[...], held_up, held_down, act, grad_units)
        sent = send(((act, act_out), (grad_units, units_out)), out_sems.at[0])
        product_of(turned, act, product)
        top, bottom = halves(product, 1)
        sent += send(((product.at[:, pl.ds(0, chunk)], out_a), (top, out_b), (bottom, out_c)), out_sems.at[1])
        for copy in more:
            copy.wait()
        back_to((back_own, back_other), (grad_units, more_units), (held_up, held_more))
        for copy in sent:
            copy.wait()

    def third(own, other, units_a, units_b, out_0, out_1, out_2, out_3, out_4, turned, held, products, sems, out_sems):
        copies = send(((units_a, held.at[0]), (units_b, held.at[1])), sems)
        turn((own, other), turned)
        for copy in copies:
            copy.wait()
        products[1] = low(dot(turned[...], held[1]))
        top, bottom = halves(products.at[1], 1)
        sent = send(((products.at[1, :, pl.ds(0, chunk)], out_2), (top, out_3), (bottom, out_4)), out_sems.at[0])
        products[0] = low(dot(turned[...], held[0]))
        sent += send(
            ((products.at[0, :, pl.ds(0, chunk)], out_0), (products.at[0, :, pl.ds(chunk, chunk)], out_1)),
            out_sems.at[1],
        )
        for copy in sent:
            copy.wait()

    def down(act_a, act_b, w0, w1, w2, w3, w4, w5, w6, w7, own_ref, other_ref, held_a, held_b, sems):
        copies = fetch(((w0, w1), (w2, w3)), 1, held_a, sems.at[0]) + fetch(((w4, w5), (w6, w7)), 1, held_b, sems.at[1])
        for copy in copies:
            copy.wait()
        for s, ref in enumerate((own_ref, other_ref)):
            here = slice(s * rows, (s + 1) * rows)
            total = cols_dot(act_a[here, :], held_a[...]) + cols_dot(act_b[here, :], held_b[...])
            ref[...] = total.astype(ref.dtype)

    dma = pltpu.SemaphoreType.DMA
    held = pltpu.VMEM((width, units), jnp.bfloat16)
    flow = pltpu.VMEM((all_rows, units), jnp.bfloat16)
    flow_out = pltpu.HBM((all_rows, units), jnp.bfloat16)
    whole = pltpu.HBM((width, chunk), jnp.bfloat16)
    part = pltpu.HBM((width // 2, chunk), jnp.bfloat16)
    sums = jax.ShapeDtypeStruct((1, units), jnp.float32)
    own = jax.ShapeDtypeStruct((rows, width), jnp.float32)
    other = jax.ShapeDtypeStruct((rows, width), jnp.bfloat16)
    run_first = pl.pallas_call(
        first,
        in_specs=[vmem] * 6 + [hbm] * 4,
        out_specs=[hbm] * 4 + [vmem],
        out_shape=[flow_out, flow_out, whole, whole, sums],
        scratch_shapes=[held, held, flow, flow, held, dma((2, 2 * wt_count)), dma((2, 2))],
        compiler_params=params,
        cost_estimate=NO_COST,
        name="ffn_first",
    )
    run_second = pl.pallas_call(
        second,
        in_specs=[vmem] * 6 + [hbm] * 9,
        out_specs=[hbm] * 5 + [vmem] * 3,
        out_shape=[flow_out, flow_out, whole, part, part, sums, own, other],
        scratch_shapes=[held, held, held, flow, flow, flow, held, dma((3, 2 * wt_count)), dma((2, 3)), dma(())],
        compiler_params=params,
        cost_estimate=NO_COST,
        name="ffn_second",
    )
    run_third = pl.pallas_call(
        third,
        in_specs=[vmem] * 2 + [hbm] * 2,
        out_specs=[hbm] * 5,
        out_shape=[whole, whole, whole, part, part],
        scratch_shapes=[
            pltpu.VMEM((width, all_rows), jnp.bfloat16),
            pltpu.VMEM((2, all_rows, units), jnp.bfloat16),
            pltpu.VMEM((2, width, units), jnp.bfloat16),
            dma((2,)),
            dma((2, 3)),
        ],
        compiler_params=params,
        cost_estimate=NO_COST,
        name="ffn_grads",
    )
    run_down = pl.pallas_call(
        down,
        in_specs=[vmem] * 2 + [hbm] * 8,
        out_specs=[vmem] * 2,
        out_shape=[own, other],
        scratch_shapes=[held, held, dma((2, 2 * wt_count))],
        compiler_params=params,
        cost_estimate=NO_COST,
        name="ffn_down",
    )
    return run_first, run_second, run_third, run_down


def turn(refs, turned):
    rows = refs[0].shape[0]
    for s, ref in enumerate(refs):
        for i in range(rows // 128):
            block = wide(ref[i * 128 : (i + 1) * 128, :])
            turned[:, s * rows + i * 128 : s * rows + (i + 1) * 128] = low(block.T)


def turn_both(own, other):
    vmem = pl.BlockSpec(memory_space=pltpu.VMEM)
    rows, width = own.shape
    return pl.pallas_call(
        lambda a, b, out: turn((a, b), out),
        in_specs=[vmem] * 2,
        out_specs=vmem,
        out_shape=jax.ShapeDtypeStruct((width, 2 * rows), own.dtype),
        compiler_params=pltpu.CompilerParams(vmem_limit_bytes=VMEM_LIMIT),
        cost_estimate=NO_COST,
        name="turn",
    )(own, other)


def out_projection(rows, width):
    tile = 32

    def kernel(attended, weight, stream, bias, gain, shift, hidden_ref, normed_ref):
        product = dot(attended[...], weight[...])
        for t in range(rows // tile):
            here = slice(t * tile, (t + 1) * tile)
            hidden = wide(stream[here, :]) + product[here] + bias[...]
            hidden_ref[here, :] = hidden
            normed_ref[here, :] = low(layer_norm(hidden, gain[...], shift[...]))

    vmem = pl.BlockSpec(memory_space=pltpu.VMEM)
    return pl.pallas_call(
        kernel,
        in_specs=[vmem] * 6,
        out_specs=[vmem] * 2,
        out_shape=[
            jax.ShapeDtypeStruct((rows, width), jnp.float32),
            jax.ShapeDtypeStruct((rows, width), jnp.bfloat16),
        ],
        compiler_params=pltpu.CompilerParams(vmem_limit_bytes=VMEM_LIMIT),
        cost_estimate=NO_COST,
        name="out_projection",
    )


def norm_back(values, gain, grad):
    centre = values - jnp.mean(values, axis=-1, keepdims=True)
    scale = lax.rsqrt(jnp.mean(centre * centre, axis=-1, keepdims=True) + NORM_EPS)
    unit = centre * scale
    inner = grad * gain
    mean = jnp.mean(inner, axis=-1, keepdims=True)
    along = jnp.mean(inner * unit, axis=-1, keepdims=True)
    return scale * (inner - mean - unit * along), grad * unit


def fold_rows(values):
    total = values[:8]
    for i in range(1, values.shape[0] // 8):
        total = total + values[i * 8 : (i + 1) * 8]
    return total


def hidden_back(rows, width):
    tile = 32

    def kernel(own, got, hidden, back, gain, weight, grad_ref, low_ref, attended_ref, sums_ref):
        sums = [jnp.zeros((8, width), jnp.float32) for _ in range(3)]
        for t in range(rows // tile):
            here = slice(t * tile, (t + 1) * tile)
            pulled, terms = norm_back(hidden[here, :], gain[...], own[here, :] + wide(got[here, :]))
            grad = wide(back[here, :]) + pulled
            grad_ref[here, :] = grad
            low_ref[here, :] = low(grad)
            for n, part in enumerate((terms, own[here, :] + wide(got[here, :]), grad)):
                sums[n] = sums[n] + fold_rows(part)
        for n in range(3):
            sums_ref[n : n + 1, :] = jnp.sum(sums[n], axis=0, keepdims=True)
        attended_ref[...] = low(cols_dot(low_ref[...], weight[...]))

    vmem = pl.BlockSpec(memory_space=pltpu.VMEM)
    return pl.pallas_call(
        kernel,
        in_specs=[vmem] * 6,
        out_specs=[vmem] * 4,
        out_shape=[
            jax.ShapeDtypeStruct((rows, width), jnp.float32),
            jax.ShapeDtypeStruct((rows, width), jnp.bfloat16),
            jax.ShapeDtypeStruct((rows, width), jnp.bfloat16),
            jax.ShapeDtypeStruct((3, width), jnp.float32),
        ],
        compiler_params=pltpu.CompilerParams(vmem_limit_bytes=VMEM_LIMIT),
        cost_estimate=NO_COST,
        name="hidden_back",
    )


def stream_back(rows, width, parts, row_groups, piece):
    tile = 32
    chips = parts // 2

    def kernel(
        place_ref, kv_0, kv_1, kv_2, kv_3, queries, weight, tokens, gain, grad_hidden, normed, back, hidden_sums,
        units_a, units_b, input_ref, even_ref, odd_ref, grad_kv, grads, turned, product, small,
    ):
        place = place_ref[0]
        sums = [jnp.zeros((8, width), jnp.float32) for _ in range(4)]
        value_sums = jnp.zeros((8, 2 * HS), jnp.float32)
        for t in range(rows // tile):
            here = slice(t * tile, (t + 1) * tile)
            total = wide(kv_0[here, :]) + wide(kv_1[here, :]) + wide(kv_2[here, :]) + wide(kv_3[here, :])
            grad_kv[here, :] = low(total)
            value_sums = value_sums + fold_rows(total)
        turn((normed,), turned)
        product[...] = dot(turned[...], grad_kv[...])
        grads[...] = cols_dot(queries[...], weight[:, :width]) + cols_dot(grad_kv[...], weight[:, width:])
        for t in range(rows // tile):
            here = slice(t * tile, (t + 1) * tile)
            grad = grads[here, :]
            pulled, terms = norm_back(wide(tokens[here, :]), gain[...], grad)
            input_ref[here, :] = grad_hidden[here, :] + pulled
            for n, part in enumerate((terms, grad, wide(queries[here, :]), wide(back[here, :]))):
                sums[n] = sums[n] + fold_rows(part)
        sums = [jnp.sum(part, axis=0, keepdims=True) for part in sums]
        small[...] = jnp.zeros_like(small)
        rows_in = (sums[0], sums[1], hidden_sums[0:1, :], hidden_sums[1:2, :], sums[2], hidden_sums[2:3, :], sums[3])
        for n, row in enumerate(rows_in):
            for j in range(width // 128):
                line = n * (width // 128) + j
                small[line : line + 1, :] = row[:, j * 128 : (j + 1) * 128]
        start = 7 * (width // 128)
        small[start : start + 1, :] = jnp.sum(value_sums, axis=0, keepdims=True)
        lines = FF // parts // 128
        for m in range(chips):
            units = (units_a, units_b)[m // 2]
            for j in range(lines):
                line = start + 1 + (place ^ (2 * m)) * lines + j
                at = (m % 2 * lines + j) * 128
                small[pl.ds(line, 1), :] = units[:, at : at + 128]
        for k in range(parts):
            ref = odd_ref if k % 2 else even_ref
            mine = low(small[pl.ds(pl.multiple_of((place ^ k) * piece, 8), piece), :])
            for w in range(row_groups):
                at = pl.multiple_of(w * piece * parts + (place ^ k) * piece, 8)
                ref[k // 2, w, :, :128] = low(product[pl.ds(at, piece), :])
                ref[k // 2, w, :, 128:] = mine

    vmem = pl.BlockSpec(memory_space=pltpu.VMEM)
    stack = jax.ShapeDtypeStruct((chips, row_groups, piece, 256), jnp.bfloat16)
    return pl.pallas_call(
        kernel,
        in_specs=[pl.BlockSpec(memory_space=pltpu.SMEM)] + [vmem] * 14,
        out_specs=[vmem] * 3,
        out_shape=[jax.ShapeDtypeStruct((rows, width), jnp.float32), stack, stack],
        scratch_shapes=[
            pltpu.VMEM((rows, 2 * HS), jnp.bfloat16),
            pltpu.VMEM((rows, width), jnp.float32),
            pltpu.VMEM((width, rows), jnp.bfloat16),
            pltpu.VMEM((width, 2 * HS), jnp.float32),
            pltpu.VMEM((parts * piece, 128), jnp.float32),
        ],
        compiler_params=pltpu.CompilerParams(vmem_limit_bytes=VMEM_LIMIT),
        cost_estimate=NO_COST,
        name="stream_back",
    )


def attn_grads(rows, width, row_groups, parts, piece):
    def kernel(place_ref, left_a, right_a, left_b, right_b, even_ref, odd_ref, turned, total):
        place = place_ref[0]
        for n, (left, right) in enumerate(((left_a, right_a), (left_b, right_b))):
            for i in range(rows // 128):
                turned[:, i * 128 : (i + 1) * 128] = low(wide(left[i * 128 : (i + 1) * 128, :]).T)
            total[:, n * width : (n + 1) * width] = dot(turned[...], right[...])
        for k in range(parts):
            ref = odd_ref if k % 2 else even_ref
            for w in range(row_groups):
                at = pl.multiple_of(w * piece * parts + (place ^ k) * piece, 8)
                ref[k // 2, w] = low(total[pl.ds(at, piece), :])

    vmem = pl.BlockSpec(memory_space=pltpu.VMEM)
    shape = jax.ShapeDtypeStruct((parts // 2, row_groups, piece, 2 * width), jnp.bfloat16)
    return pl.pallas_call(
        kernel,
        grid_spec=pltpu.PrefetchScalarGridSpec(
            num_scalar_prefetch=1,
            grid=(),
            in_specs=[vmem] * 4,
            out_specs=[vmem] * 2,
            scratch_shapes=[pltpu.VMEM((width, rows), jnp.bfloat16), pltpu.VMEM((width, 2 * width), jnp.float32)],
        ),
        out_shape=[shape] * 2,
        compiler_params=pltpu.CompilerParams(vmem_limit_bytes=VMEM_LIMIT),
        cost_estimate=NO_COST,
        name="attn_grads",
    )


def attn_update(rows, columns, width, parts, piece):
    qkv = columns - width

    def kernel(place_ref, even_ref, odd_ref, master, first, second, *outs):
        place = place_ref[0]
        for k in range(parts):
            ref = odd_ref if k % 2 else even_ref
            here = pl.ds(pl.multiple_of((place ^ k) * piece, 8), piece)
            for cols, source in (
                (slice(0, width), slice(0, width)),
                (slice(width, qkv), slice(2 * width, columns)),
                (slice(qkv, columns), slice(width, 2 * width)),
            ):
                grad = wide(ref[k // 2, :, source])
                got = adam_update(master[here, cols], grad, first[here, cols], second[here, cols], 0.1, 0.1)
                outs[0][here, cols] = got[0]
                outs[1][here, cols] = got[1]
                outs[2][here, cols] = got[2]

    vmem = pl.BlockSpec(memory_space=pltpu.VMEM)
    return pl.pallas_call(
        kernel,
        grid_spec=pltpu.PrefetchScalarGridSpec(
            num_scalar_prefetch=1, grid=(), in_specs=[vmem] * 5, out_specs=[vmem] * 3, scratch_shapes=[]
        ),
        out_shape=[jax.ShapeDtypeStruct((rows, columns), jnp.float32)] * 3,
        compiler_params=pltpu.CompilerParams(vmem_limit_bytes=VMEM_LIMIT),
        cost_estimate=NO_COST,
        name="attn_update",
    )


def ffn_update(rows, units, parts, chunk):
    per_row = 2 * units // 128
    rows_once = 32
    lines = rows_once * per_row

    def kernel(place_ref, even, odd, master, first, second, first_out, second_out, master_out, total):
        place = place_ref[0]
        for k in range(parts):
            grad = odd if k % 2 else even
            for j in range(chunk // 128):
                for which in range(2):
                    line = (place ^ k) * (2 * chunk // 128) + 2 * j + which
                    total[pl.ds(line, rows_once, per_row), :] = wide(
                        grad[k // 2, which, :, j * 128 : (j + 1) * 128]
                    )
        for t in range(lines // 64):
            own = slice(t * 64, (t + 1) * 64)
            got = adam_update(master[own, :], total[own, :], first[own, :], second[own, :], 0.1, 0.1)
            first_out[own, :] = got[0]
            second_out[own, :] = got[1]
            master_out[own, :] = got[2]

    block = pl.BlockSpec((lines, 128), lambda i, *_: (i, 0))
    stack = pl.BlockSpec((parts // 2, 2, rows_once, chunk), lambda i, *_: (0, 0, i, 0))
    call = pl.pallas_call(
        kernel,
        grid_spec=pltpu.PrefetchScalarGridSpec(
            num_scalar_prefetch=1,
            grid=(rows // rows_once,),
            in_specs=[stack] * 2 + [block] * 3,
            out_specs=[block] * 3,
            scratch_shapes=[pltpu.VMEM((lines, 128), jnp.float32)],
        ),
        out_shape=[jax.ShapeDtypeStruct((rows * per_row, 128), jnp.float32)] * 3,
        compiler_params=pltpu.CompilerParams(vmem_limit_bytes=VMEM_LIMIT),
        cost_estimate=NO_COST,
        name="ffn_update",
    )

    def fold(array):
        return jnp.swapaxes(array.reshape(rows, 2, units // 128, 128), 1, 2).reshape(-1, 128)

    def unfold(array):
        return jnp.swapaxes(array.reshape(rows, units // 128, 2, 128), 1, 2).reshape(rows, 2, units)

    def run(place, even, odd, master, first, second):
        return tuple(unfold(array) for array in call(place, even, odd, fold(master), fold(first), fold(second)))

    return run


def shards(
    tokens,
    doc_starts,
    attn_master,
    attn_mom,
    attn_sq,
    ffn_master,
    ffn_mom,
    ffn_sq,
    small_master,
    small_mom,
    small_sq,
    cotangent,
):
    ctx_count, wt_count = lax.axis_size("ctx"), lax.axis_size("wt")
    ctx_place, wt_place = lax.axis_index("ctx"), lax.axis_index("wt")
    batches, rows_here, width = tokens.shape
    qkv_cols = width + 2 * HS
    attn_columns = attn_master.shape[1]
    all_rows = batches * rows_here
    shard_rows = attn_master.shape[0]
    piece_rows = shard_rows // ctx_count
    chunk = FF // ctx_count
    chips = ctx_count // 2
    order = ctx_place ^ jnp.arange(ctx_count, dtype=jnp.int32)
    (
        gain_one,
        shift_one,
        gain_two,
        shift_two,
        bias_query,
        bias_out,
        bias_proj,
        bias_value,
        bias_hidden,
    ) = split_small(small_master)
    runs = 2 if batches % 2 == 0 else 1
    places = [jnp.stack([ctx_place, jnp.int32(run * (batches // runs))]) for run in range(runs)]
    place = places[0]
    wt_half = wt_count // 2
    out_rows = shard_rows // chips
    run_forward, run_backward = attention_kernels(batches, rows_here, width, ctx_count, runs)
    ffn_first, ffn_second, ffn_third, ffn_down = ffn_kernels(all_rows, width, chunk, wt_count)
    step = Steps()

    def both(own, got, place, bit, axis=0):
        ahead, behind = jnp.stack([own, got], axis), jnp.stack([got, own], axis)
        return jnp.where((place & bit) == 0, ahead, behind)

    def in_order(even, odd):
        buffer = jnp.zeros((ctx_count,) + even.shape[1:], even.dtype)
        for m in range(chips):
            buffer = put(buffer, even[m][None], ctx_place ^ (2 * m), 0)
            buffer = put(buffer, odd[m][None], ctx_place ^ (2 * m + 1), 0)
        return buffer

    def send_chips(piece):
        return [xor_send(piece, mask) for mask in range(2, ctx_count, 2)]

    def split_wt(total, bit):
        ahead, behind = jnp.split(total, 2)
        kept, sent = jnp.where((wt_place & bit) == 0, ahead, behind), jnp.where((wt_place & bit) == 0, behind, ahead)
        return kept, sent

    def add_low(*arrays):
        return low(sum(wide(array) for array in arrays))

    qkv = low(lax.dynamic_slice(attn_master, (ctx_place * piece_rows, 0), (piece_rows, qkv_cols)))
    qkv_got = xor_wt(qkv, 1)
    qkv = both(qkv, qkv_got, wt_place, 1)
    qkv_got = xor_wt(qkv, 2)
    rest = low(jnp.swapaxes(take(ffn_master, ctx_place, 2, chunk), 0, 1).reshape(2 * shard_rows, chunk))
    out = low(
        lax.dynamic_slice(
            attn_master, (ctx_place // 2 * out_rows, qkv_cols + ctx_place % 2 * chunk), (out_rows, chunk)
        )
    )
    qkv_got, rest, out = together(qkv_got, rest, out)
    rest_got, out_got = xor_wt(rest, 1), xor_wt(out, 1)
    flat_tokens = tokens.reshape(all_rows, width)
    qkv = both(qkv, qkv_got, wt_place, 2).reshape((wt_count,) + qkv.shape[1:])
    qkv_got = xor_send(qkv, 2)
    qkv_got, rest_got, out_got = together(qkv_got, rest_got, out_got)
    qkv = both(qkv, qkv_got, ctx_place, 2)
    ups, downs = [both(rest[rows], rest_got[rows], wt_place, 1) for rows in (slice(shard_rows), slice(shard_rows, None))]
    out = both(out, out_got, wt_place, 1)
    qkv, ups, downs, out = together(qkv, ups, downs, out)
    qkv_got = xor_send(qkv, 4)
    ups_got, out_got = xor_wt(ups, 2), xor_wt(out, 2)
    back_low, flat_tokens, qkv = together(cotangent.reshape(all_rows, width), flat_tokens, qkv)
    back_other = xor_send(back_low, 1)
    normed_low = low(layer_norm(wide(flat_tokens), gain_one, shift_one))
    qkv_got, normed_low, back_other = together(qkv_got, normed_low, back_other)
    qkv = both(qkv, qkv_got, ctx_place, 4)
    qkv_got = xor_send(qkv, 1)
    back_turned = turn_both(back_low, back_other)
    bias_parts = bias_hidden.reshape(ctx_count, chunk)[order[::2]].reshape(1, chips * chunk)
    bias_near, bias_far = jnp.split(bias_parts, 2, axis=1)
    qkv_got, back_turned, out_got, bias_near, bias_far = together(qkv_got, back_turned, out_got, bias_near, bias_far)
    out = both(out, out_got, wt_place, 2).reshape((wt_count,) + out.shape[1:])

    def project(own, got, normed):
        blocks = both(own, got, ctx_place, 1, 2)
        weight = jnp.transpose(blocks, (3, 0, 1, 2, 4, 5)).reshape(width, qkv_cols)
        mixed = dot(normed, weight)
        queries = low(mixed[:, :width] + bias_query).reshape(batches, rows_here, width)
        kv_bias = jnp.concatenate([jnp.zeros((HS,), jnp.float32), bias_value])
        kv_local = low(mixed[:, width:] + kv_bias).reshape(batches, rows_here, 2 * HS)
        return weight, queries, kv_local

    weight_qkv, queries, kv_local = project(qkv, qkv_got, normed_low)
    kv_got = xor_send(kv_local, 2)
    kv_got, ups_got, downs = together(kv_got, ups_got, downs)
    downs_got = xor_wt(downs, 2)
    kv_even = both(kv_local, kv_got, ctx_place, 2)
    kv_even, out = together(kv_even, out)
    kv_got = xor_send(kv_even, 4)
    out_got = send_chips(out)
    kv_got, *out_got = together(kv_got, *out_got)
    kv_even = both(kv_even, kv_got, ctx_place, 4).reshape((chips,) + kv_local.shape)
    kv_odd = xor_send(kv_even, 1)
    out_even = jnp.stack([out] + out_got)
    out_odd = xor_send(out_even, 1)
    kv_even, ups_got, downs_got = together(kv_even, ups_got, downs_got)
    own, got = jnp.concatenate([ups, downs], axis=1), jnp.concatenate([ups_got, downs_got], axis=1)
    first_half = (wt_place & 2) == 0
    rest_low, rest_high = jnp.where(first_half, own, got), jnp.where(first_half, got, own)
    low_x, high_y, high_x, low_y = xor_send(rest_low, 2), xor_send(rest_high, 4), xor_send(rest_high, 2), xor_send(rest_low, 4)
    queries, out_even, rest_low, rest_high = together(queries, out_even, rest_low, rest_high)

    attended_low, attended, logs = step(run_forward, doc_starts, place, queries, kv_even, kv_odd)
    attended_low = attended_low.reshape(all_rows, width)
    attended_low, low_x, high_y = together(attended_low, low_x, high_y)
    low_diagonal, high_diagonal = xor_send(low_x, 4), xor_send(high_y, 2)

    def join_out(even, odd):
        columns = jnp.where((ctx_place & 1) == 0, jnp.concatenate([even, odd], axis=3), jnp.concatenate([odd, even], axis=3))
        for n in range(chips.bit_length() - 1):
            pairs = columns.reshape((-1, 2, 1 << n) + columns.shape[1:])
            columns = jnp.where((ctx_place & (2 << n)) == 0, pairs, pairs[:, ::-1]).reshape(columns.shape)
        return jnp.swapaxes(columns, 0, 1).reshape(width, width)

    weight_out = step(join_out, out_even, out_odd)
    hidden, normed_two = step(
        out_projection(all_rows, width), attended_low, weight_out, flat_tokens, bias_out[None], gain_two[None],
        shift_two[None],
    )
    normed_other = xor_send(normed_two, 1)

    weights = [rest_low, rest_high, low_x, high_x, low_y, high_y, low_diagonal, high_diagonal]
    flows = (normed_two, normed_other, back_low, back_other, back_turned)
    act_first, units_first, down_own, down_x, sums_first = step(
        lambda *args: ffn_first(*args[:6], *in_hbm(args[6:])), *flows, bias_near, *weights[:4]
    )
    act_second, units_second, down_y, down_top, down_bottom, sums_second, back_own, back_part = step(
        lambda *args: ffn_second(*args[:6], *in_hbm(args[6:])), *flows, bias_far, units_first, *weights
    )
    back_got = xor_send(back_part, 1)
    top_got, bottom_got = xor_send(down_top, 4), xor_send(down_bottom, 2)

    def meet(along_x, along_y, top, bottom):
        half = width // 2
        return (
            jnp.concatenate([add_low(along_x[:half], top), along_x[half:]]),
            jnp.concatenate([along_y[:half], add_low(along_y[half:], bottom)]),
        )

    up_own, up_x, up_y, up_top, up_bottom = step(
        lambda *args: ffn_third(*args[:2], *in_hbm(args[2:])), normed_two, normed_other, units_first, units_second
    )
    down_x, down_y = step(meet, down_x, down_y, top_got, bottom_got)
    down_got = [xor_send(down_x, 2), xor_send(down_y, 4)]
    top_got, bottom_got = xor_send(up_top, 4), xor_send(up_bottom, 2)

    grad_hidden, grad_hidden_low, grad_attended, hidden_sums = step(
        hidden_back(all_rows, width), back_own, back_got, hidden, back_low, gain_two[None], weight_out
    )
    grad_attended = grad_attended.reshape(batches, rows_here, width)
    def by_wt(*arrays):
        return split_wt(add_low(*arrays).reshape(wt_count, shard_rows, chunk), 2)

    def next_wt(kept, got):
        return split_wt(add_low(kept, got), 1)

    def kv_pieces(evens, odds):
        total = jnp.concatenate([add_low(a, b) for a, b in zip(evens, odds)], axis=1)
        return [lax.dynamic_index_in_dim(total, (ctx_place // 2) ^ m, 0, False) for m in range(chips)]

    backs = [step(run_backward[0], doc_starts, places[0], queries, kv_even, kv_odd, attended, logs, grad_attended)]
    kv_got = [xor_send(backs[0][2], 1)]
    down_kept, down_sent = step(by_wt, down_own, *down_got)
    up_x, up_y = step(meet, up_x, up_y, top_got, bottom_got)
    grad_attended, down_kept, down_sent, up_x, up_y = together(grad_attended, down_kept, down_sent, up_x, up_y)
    down_got = xor_wt(down_sent, 2)
    up_got = [xor_send(up_x, 2), xor_send(up_y, 4)]
    backs += [
        step(run_backward[run], doc_starts, places[run], queries, kv_even, kv_odd, attended, logs, grad_attended)
        for run in range(1, runs)
    ]
    backs[-1] = list(backs[-1])
    *backs[-1], down_got, up_got[0], up_got[1] = together(*backs[-1], down_got, *up_got)
    kv_got += [xor_send(back[2], 1) for back in backs[1:]]
    grad_queries = [back[0] for back in backs]
    grad_query = jnp.concatenate(grad_queries).reshape(all_rows, width)
    down_kept, down_sent = next_wt(down_kept, down_got)
    up_kept, up_sent = by_wt(up_own, *up_got)
    down_kept, down_sent, up_kept, up_sent = together(down_kept, down_sent, up_kept, up_sent)
    down_got, up_got = xor_wt(down_sent, 1), xor_wt(up_sent, 2)
    kv_half = step(kv_pieces, [back[1] for back in backs], kv_got)
    kv_got = [xor_send(kv_half[m], 2 * m) for m in range(1, chips)]
    wide_even, wide_odd = step(
        attn_grads(all_rows, width, wt_count, ctx_count, piece_rows),
        place, normed_low, grad_query, attended_low, grad_hidden_low,
    )
    small_size = small_master.shape[0]
    up_kept, up_sent = step(next_wt, up_kept, up_got)
    kv_got[0], up_kept, up_sent = together(kv_got[0], up_kept, up_sent)
    up_got = xor_wt(up_sent, 1)
    input_grad, tail_even, tail_odd = step(
        stream_back(all_rows, width, ctx_count, wt_count, piece_rows),
        place, *[array.reshape(all_rows, 2 * HS) for array in (kv_half[0], *kv_got)], grad_query, weight_qkv,
        flat_tokens, gain_one[None], grad_hidden, normed_low, back_low, hidden_sums, sums_first, sums_second,
    )
    input_grad = input_grad.reshape(batches, rows_here, width)
    wide_odd, tail_odd = lax.optimization_barrier((wide_odd, tail_odd))
    wide_odd, tail_odd = xor_send(wide_odd, 1), xor_send(tail_odd, 1)
    def attn_pieces(wide_even, wide_odd, tail_even, tail_odd):
        total = jnp.concatenate([add_low(wide_even, wide_odd), add_low(tail_even, tail_odd)], axis=3)
        return [total[m] for m in range(chips)]

    attn_half = step(attn_pieces, wide_even, wide_odd, tail_even, tail_odd)
    attn_got = [xor_send(attn_half[m], 2 * m) for m in range(1, chips)]
    ffn_part = step(
        lambda *arrays: jnp.concatenate([add_low(*arrays[:2]), add_low(*arrays[2:])]), up_kept, up_got, down_kept, down_got
    )
    ffn_got = send_chips(ffn_part)
    down_out, down_other = step(
        lambda *args: ffn_down(*args[:2], *in_hbm(args[2:])), act_first, act_second, *weights
    )
    down_other = xor_send(down_other, 1)
    attn_kept, attn_sent = step(lambda *parts: split_wt(add_low(*parts), 2), attn_half[0], *attn_got)
    attn_got = xor_wt(attn_sent, 2)
    layer_out = step(
        lambda hidden, own, got: low(hidden + own + wide(got) + bias_proj).reshape(batches, rows_here, width),
        hidden, down_out, down_other,
    )
    attn_kept, attn_sent = step(lambda kept, got: split_wt(add_low(kept, got), 1), attn_kept, attn_got)
    attn_got = xor_wt(attn_sent, 1)
    ffn_even = step(lambda *parts: jnp.stack(parts), ffn_part, *ffn_got)
    ffn_odd = xor_send(ffn_even, 1)
    attn_part = step(lambda *parts: add_low(*parts)[0], attn_kept, attn_got)
    attn_got = send_chips(attn_part)

    ffn_new = step(
        ffn_update(shard_rows, FF, ctx_count, chunk), place, ffn_even, ffn_odd, ffn_master, ffn_mom, ffn_sq
    )
    attn_even = step(lambda *parts: jnp.stack(parts), attn_part, *attn_got)
    attn_odd = xor_send(attn_even, 1)
    small_total = in_order(attn_even[..., attn_columns:], attn_odd[..., attn_columns:])
    small_total = wide(small_total.reshape(-1))
    most = small_size - FF - HS
    small_total = jnp.concatenate(
        [small_total[:most], small_total[most + HS : most + 2 * HS], small_total[most + 2 * HS : most + 2 * HS + FF]]
    )
    small_new = adam_update(small_master, small_total, small_mom, small_sq, 1.0, 0.0)
    attn_new = attn_update(shard_rows, attn_columns, width, ctx_count, piece_rows)(
        place, attn_even, attn_odd, *in_hbm([attn_master, attn_mom, attn_sq])
    )
    return (layer_out, input_grad) + tuple(attn_new) + tuple(ffn_new) + tuple(small_new)


def shift_wt(array, shift):
    count = lax.axis_size("wt")
    return lax.ppermute(array, "wt", [(i, (i + shift) % count) for i in range(count)])


def whole_wt(piece, axis):
    count, place = lax.axis_size("wt"), lax.axis_index("wt")
    shape = list(piece.shape)
    shape[axis] *= count
    buffer = put(jnp.zeros(shape, piece.dtype), piece, place, axis)
    for shift in range(1, count):
        buffer = put(buffer, shift_wt(piece, shift), (place - shift) % count, axis)
    return buffer


def whole_ctx(piece):
    count = lax.axis_size("ctx")
    got = {0: piece}
    for mask in range(2, count, 2):
        got[mask] = xor_send(piece, mask)
    for mask in range(0, count, 2):
        got[mask + 1] = xor_send(got[mask], 1)
    return [got[mask] for mask in range(count)]


def sum_ctx(pieces):
    count = lax.axis_size("ctx")
    half = {}
    for mask in range(count - 2, -1, -2):
        other = xor_send(pieces[mask + 1], 1)
        half[mask] = low(wide(pieces[mask]) + wide(other))
    total = wide(half[0])
    for mask in range(2, count, 2):
        total = total + wide(xor_send(half[mask], mask))
    return total


def sum_wt(array, axis):
    count, place = lax.axis_size("wt"), lax.axis_index("wt")
    size = array.shape[axis] // count
    total = wide(take(array, place, axis, size))
    for shift in range(1, count):
        sent = take(array, (place + shift) % count, axis, size)
        total = total + wide(shift_wt(sent, shift))
    return total


def any_shards(
    tokens,
    doc_starts,
    attn_master,
    attn_mom,
    attn_sq,
    ffn_master,
    ffn_mom,
    ffn_sq,
    small_master,
    small_mom,
    small_sq,
    cotangent,
):
    ctx_count = lax.axis_size("ctx")
    ctx_place = lax.axis_index("ctx")
    wt_count = lax.axis_size("wt")
    batches, rows_here, width = tokens.shape
    heads = width // HS
    qkv_cols = width + 2 * HS
    all_rows = batches * rows_here
    shard_rows = attn_master.shape[0]
    piece_rows = shard_rows // ctx_count
    chunk = FF // ctx_count
    order = ctx_place ^ jnp.arange(ctx_count, dtype=jnp.int32)
    (
        gain_one,
        shift_one,
        gain_two,
        shift_two,
        bias_query,
        bias_out,
        bias_proj,
        bias_value,
        bias_hidden,
    ) = split_small(small_master)

    attn_piece = low(take(attn_master, ctx_place, 0, piece_rows))

    def whole_rows(piece):
        parts = whole_ctx(whole_wt(piece[None], 0))
        buffer = jnp.zeros((wt_count, ctx_count) + piece.shape, piece.dtype)
        for k, part in enumerate(parts):
            buffer = put(buffer, part[:, None], ctx_place ^ k, 1)
        return buffer.reshape((width,) + piece.shape[1:])

    weight_qkv = whole_rows(attn_piece[:, :qkv_cols])
    weight_out = whole_rows(attn_piece[:, qkv_cols:])
    ffn_piece = low(jnp.swapaxes(take(ffn_master, ctx_place, 2, chunk), 0, 1))
    ffn_parts = whole_ctx(whole_wt(ffn_piece, 1))
    bias_parts = bias_hidden.reshape(ctx_count, chunk)[order]

    stream = wide(tokens.reshape(all_rows, width))
    normed, norm_back_one = jax.vjp(layer_norm, stream, gain_one, shift_one)
    normed_low = low(normed)
    mixed = dot(normed_low, weight_qkv)
    queries = low(mixed[:, :width] + bias_query)
    kv_local = low(
        mixed[:, width:] + jnp.concatenate([jnp.zeros((HS,), jnp.float32), bias_value])
    ).reshape(batches, rows_here, 2 * HS)
    kv_parts = jnp.stack(whole_ctx(kv_local), axis=1).reshape(
        batches, ctx_count * rows_here, 2 * HS
    )
    keys_all, values_all = kv_parts[..., :HS], kv_parts[..., HS:]
    local_pos = jnp.arange(rows_here, dtype=jnp.int32)
    query_pos = ctx_place * rows_here + local_pos
    key_pos = (order[:, None] * rows_here + local_pos[None, :]).reshape(-1)
    queries = queries.reshape(batches, rows_here * heads, HS)
    scale = HS ** (-0.5)
    attended_list, log_list, allowed_list = [], [], []
    for b in range(batches):
        starts = doc_starts[b]
        query_doc = jnp.sum((starts[None, :] <= query_pos[:, None]).astype(jnp.int32), axis=1)
        key_doc = jnp.sum((starts[None, :] <= key_pos[:, None]).astype(jnp.int32), axis=1)
        allowed = (query_doc[:, None] == key_doc[None, :]) & (key_pos[None, :] <= query_pos[:, None])
        allowed = jnp.repeat(allowed, heads, axis=0)
        allowed_list.append(allowed)
        scores = jnp.where(allowed, cols_dot(queries[b], keys_all[b]) * scale, -1e30)
        peak = jnp.max(scores, axis=-1, keepdims=True)
        expo = jnp.exp(scores - peak)
        total = jnp.sum(expo, axis=-1, keepdims=True)
        attended_list.append(dot(low(expo / total), values_all[b]))
        log_list.append(peak + jnp.log(total))
    attended = jnp.stack(attended_list)
    attended_low = low(attended).reshape(all_rows, width)
    hidden = stream + dot(attended_low, weight_out) + bias_out
    normed_two, norm_back_two = jax.vjp(layer_norm, hidden, gain_two, shift_two)
    normed_two_low = low(normed_two)

    back_low = cotangent.reshape(all_rows, width)
    back_rows = wide(back_low)
    down_vals = jnp.zeros((all_rows, width), jnp.float32)
    grad_normed_two = jnp.zeros((all_rows, width), jnp.float32)
    ffn_grads, hidden_grads = [], []
    for k in range(ctx_count):
        weight_up, weight_down = ffn_parts[k][0], ffn_parts[k][1]
        value, slope = gelu_both(dot(normed_two_low, weight_up) + bias_parts[k])
        act = low(value)
        down_vals = down_vals + cols_dot(act, weight_down)
        grad_up = low(dot(back_low, weight_down) * slope)
        hidden_grads.append(jnp.sum(wide(grad_up), axis=0))
        grad_normed_two = grad_normed_two + cols_dot(grad_up, weight_up)
        ffn_grads.append(
            jnp.stack([low(rows_dot(normed_two_low, grad_up)), low(rows_dot(back_low, act))])
        )
    layer_out = low(hidden + down_vals + bias_proj).reshape(batches, rows_here, width)
    grad_bias_proj = jnp.sum(back_rows, axis=0)
    grad_bias_hidden = jnp.stack(hidden_grads)[order].reshape(FF)
    ffn_part = low(sum_wt(low(sum_ctx(ffn_grads)), 1))

    grad_hidden_part, grad_gain_two, grad_shift_two = norm_back_two(grad_normed_two)
    grad_hidden = back_rows + grad_hidden_part
    grad_bias_out = jnp.sum(grad_hidden, axis=0)
    grad_hidden_low = low(grad_hidden)
    grad_out = rows_dot(attended_low, grad_hidden_low)

    def summed_rows(grad):
        blocks = low(grad).reshape(wt_count, ctx_count, piece_rows, grad.shape[1])
        pieces = [take(blocks, ctx_place ^ k, 1, 1)[:, 0] for k in range(ctx_count)]
        part = low(sum_wt(low(sum_ctx(pieces)), 0)[0])
        buffer = jnp.zeros((ctx_count,) + part.shape, part.dtype)
        for k, got in enumerate(whole_ctx(part)):
            buffer = put(buffer, got[None], ctx_place ^ k, 0)
        return wide(buffer.reshape(shard_rows, grad.shape[1]))

    out_total = summed_rows(grad_out)

    grad_attended = low(cols_dot(grad_hidden_low, weight_out)).reshape(
        batches, rows_here * heads, HS
    )
    grad_query_list, grad_kv_list = [], []
    for b in range(batches):
        grads = grad_attended[b]
        delta = jnp.sum(wide(grads) * attended[b], axis=-1, keepdims=True)
        scores = jnp.where(allowed_list[b], cols_dot(queries[b], keys_all[b]) * scale, -1e30)
        weights = jnp.exp(scores - log_list[b])
        grad_scores = low(weights * (cols_dot(grads, values_all[b]) - delta))
        grad_query_list.append(low(dot(grad_scores, keys_all[b]) * scale))
        grad_kv_list.append(
            jnp.concatenate(
                [
                    low(rows_dot(grad_scores, queries[b]) * scale),
                    low(rows_dot(low(weights), grads)),
                ],
                axis=1,
            )
        )
    grad_query = jnp.stack(grad_query_list).reshape(all_rows, width)
    grad_kv = jnp.stack(grad_kv_list).reshape(batches, ctx_count, rows_here, 2 * HS)
    grad_kv_low = low(sum_ctx([grad_kv[:, k] for k in range(ctx_count)])).reshape(
        all_rows, 2 * HS
    )
    grad_bias_query = jnp.sum(wide(grad_query), axis=0)
    grad_bias_value = jnp.sum(wide(grad_kv_low[:, HS:]), axis=0)
    grad_mixed = jnp.concatenate([grad_query, grad_kv_low], axis=1)
    qkv_total = summed_rows(rows_dot(normed_low, grad_mixed))
    grad_normed = cols_dot(grad_mixed, weight_qkv)
    grad_stream_part, grad_gain_one, grad_shift_one = norm_back_one(grad_normed)
    input_grad = (grad_hidden + grad_stream_part).reshape(batches, rows_here, width)

    ffn_buffer = jnp.zeros((ctx_count,) + ffn_part.shape, ffn_part.dtype)
    for k, got in enumerate(whole_ctx(ffn_part)):
        ffn_buffer = put(ffn_buffer, got[None], ctx_place ^ k, 0)
    ffn_total = wide(jnp.transpose(ffn_buffer, (2, 1, 0, 3)).reshape(shard_rows, 2, FF))
    attn_total = jnp.concatenate([qkv_total, out_total], axis=1)
    grad_small = jnp.concatenate(
        [
            grad_gain_one,
            grad_shift_one,
            grad_gain_two,
            grad_shift_two,
            grad_bias_query,
            grad_bias_out,
            grad_bias_proj,
            grad_bias_value,
            grad_bias_hidden,
        ]
    )
    small_total = lax.psum(grad_small, ("ctx", "wt"))
    attn_new = adam_update(attn_master, attn_total, attn_mom, attn_sq, 0.1, 0.1)
    ffn_new = adam_update(ffn_master, ffn_total, ffn_mom, ffn_sq, 0.1, 0.1)
    small_new = adam_update(small_master, small_total, small_mom, small_sq, 1.0, 0.0)
    return (layer_out, input_grad) + attn_new + ffn_new + small_new


def solution(mesh):
    rows, cube = P("wt", None), P("wt", None, None)
    flow = P("wt", "ctx", None)
    in_specs = (flow, rows, rows, rows, rows, cube, cube, cube, P(), P(), P(), flow)
    out_specs = (flow, flow, rows, rows, rows, cube, cube, cube, P(), P(), P())
    ctx_count, wt_count = mesh.shape["ctx"], mesh.shape["wt"]
    fitted = (ctx_count, wt_count) == (8, 4)
    body = shards if fitted else any_shards
    return jax.shard_map(body, mesh=mesh, in_specs=in_specs, out_specs=out_specs, check_vma=False)
```

```python
import jax
import jax.numpy as jnp
from jax import lax
from jax.experimental import pallas as pl
from jax.experimental.pallas import tpu as pltpu
from jax.sharding import PartitionSpec as P

D = 768
HS = 64
FF = 3072
STEP = 10


NORM_EPS = 1e-05
GELU_COEF = 0.7978845608028654
GELU_CUBE = 0.044715
BETA_ONE = 0.9
BETA_TWO = 0.95
ADAM_EPS = 1e-08
VMEM_LIMIT = 22 << 20
NO_COST = pl.CostEstimate(flops=0, bytes_accessed=0, transcendentals=0)


def layer_norm(values, gain, shift):
    centre = values - jnp.mean(values, axis=-1, keepdims=True)
    spread = jnp.mean(centre * centre, axis=-1, keepdims=True)
    return centre * lax.rsqrt(spread + NORM_EPS) * gain + shift


def gelu_both(u):
    square = u * u
    share = 0.5 * jnp.tanh(u * (GELU_COEF * GELU_CUBE * square + GELU_COEF)) + 0.5
    bend = u * (6.0 * GELU_COEF * GELU_CUBE * square + 2.0 * GELU_COEF)
    return u * share, share * ((1.0 - share) * bend) + share


def split_small(small):
    return (
        small[0:D],
        small[D : 2 * D],
        small[2 * D : 3 * D],
        small[3 * D : 4 * D],
        small[4 * D : 5 * D],
        small[5 * D : 6 * D],
        small[6 * D : 7 * D],
        small[7 * D : 7 * D + HS],
        small[7 * D + HS :],
    )


def rows_dot(left, right):
    return lax.dot_general(
        left, right, (((0,), (0,)), ((), ())), preferred_element_type=jnp.float32
    )


def cols_dot(left, right):
    return lax.dot_general(
        left, right, (((1,), (1,)), ((), ())), preferred_element_type=jnp.float32
    )


def dot(left, right):
    return jnp.dot(left, right, preferred_element_type=jnp.float32)


def low(values):
    return values.astype(jnp.bfloat16)


def wide(values):
    return values.astype(jnp.float32)


def adam_update(master, gradient, first, second, step_rate, decay_rate):
    first_new = BETA_ONE * first + (1.0 - BETA_ONE) * gradient
    second_new = BETA_TWO * second + (1.0 - BETA_TWO) * gradient * gradient
    first_hat = first_new / (1.0 - BETA_ONE**STEP)
    second_hat = second_new / (1.0 - BETA_TWO**STEP)
    master_new = master - step_rate * (
        first_hat / (jnp.sqrt(second_hat) + ADAM_EPS) + decay_rate * master
    )
    return (first_new, second_new, master_new)


def xor_send(array, mask):
    count = lax.axis_size("ctx")
    return lax.ppermute(array, "ctx", [(i, i ^ mask) for i in range(count)])


def xor_wt(array, mask):
    count = lax.axis_size("wt")
    return lax.ppermute(array, "wt", [(i, i ^ mask) for i in range(count)])


class Steps:
    def __init__(self):
        self.last = ()

    def __call__(self, function, *args):
        flat, tree = jax.tree.flatten(args)
        held = lax.optimization_barrier(tuple(flat) + self.last)[: len(flat)]
        result = function(*jax.tree.unflatten(tree, held))
        self.last = tuple(jax.tree.leaves(result))
        return result


def loop(count, body, carry=0):
    return lax.fori_loop(0, count, body, carry)


def rows_at(i, size):
    return pl.ds(pl.multiple_of(i * size, size), size)


def together(*arrays):
    return lax.optimization_barrier(arrays)


def put(buffer, piece, place, axis):
    starts = [0] * buffer.ndim
    starts[axis] = place * piece.shape[axis]
    return lax.dynamic_update_slice(buffer, piece, starts)


def take(buffer, place, axis, size):
    return lax.dynamic_slice_in_dim(buffer, place * size, size, axis)


def attention_kernels(batches, rows, width, parts, runs):
    half_parts = parts // 2
    keys = parts * rows
    pair = 2 * HS
    groups = width // (2 * pair)
    factor = HS ** (-0.5) * 1.4426950408889634
    tile = 32

    def lanes(shape):
        return lax.broadcasted_iota(jnp.int32, shape, 1)

    def spread(even_ref, odd_ref, key_ref, value_ref):
        for j in range(parts):
            ref = even_ref if j < half_parts else odd_ref
            block = wide(ref[j % half_parts, 0])
            turned = pltpu.roll(block, HS, 1)
            first = lanes(block.shape) < HS
            here = pl.ds(j * rows, rows)
            key_ref[0, here, :] = low(jnp.where(first, block, 0.0))
            key_ref[1, here, :] = low(jnp.where(first, 0.0, turned))
            value_ref[0, here, :] = low(jnp.where(first, turned, 0.0))
            value_ref[1, here, :] = low(jnp.where(first, 0.0, block))

    def doc_begin(starts_ref, stream, positions):
        begin = jnp.zeros_like(positions)
        for j in range(starts_ref.shape[1]):
            start = starts_ref[stream, j]
            begin = jnp.where(start <= positions, jnp.maximum(begin, start), begin)
        return begin

    def forward(starts_ref, place_ref, query_ref, even_ref, odd_ref, low_ref, full_ref, log_ref, cap, key, value, weight):
        stream, place = pl.program_id(0), place_ref[0]
        spread(even_ref, odd_ref, key, value)
        query_pos = place * rows + lax.broadcasted_iota(jnp.int32, (rows, 1), 0)
        begin = doc_begin(starts_ref, stream, query_pos)
        for j in range(parts):
            key_pos = (place ^ (2 * (j % half_parts) + j // half_parts)) * rows + lax.broadcasted_iota(jnp.int32, (rows, rows), 1)
            allowed = (key_pos >= begin) & (key_pos <= query_pos)
            cap[:, j * rows : (j + 1) * rows] = jnp.where(allowed, 3.0e38, -1e30)
        column = lanes((tile, pair))
        logs = [jnp.zeros((tile, pair), jnp.float32) for _ in range(rows // tile)]
        for g in range(groups):
            at = g * 2 * pair
            two = jnp.concatenate([query_ref[0, :, at : at + pair], query_ref[0, :, at + pair : at + 2 * pair]], axis=0)
            totals = []
            for half in range(2):
                scores = cols_dot(two, key[half])
                norms = []
                for t in range(2 * rows // tile):
                    own = slice(t * tile, (t + 1) * tile)
                    n = t % (rows // tile)
                    part = jnp.minimum(scores[own] * factor, cap[n * tile : (n + 1) * tile, :])
                    peak = jnp.max(part, axis=1, keepdims=True)
                    expo = jnp.exp2(part - peak)
                    norm = jnp.sum(expo, axis=1, keepdims=True)
                    weight[half, own, :] = low(expo)
                    norms.append(norm)
                    head = 4 * g + 2 * (t * tile // rows) + half
                    logs[n] = jnp.where(column == head, peak + jnp.log2(norm), logs[n])
                totals.append(dot(weight[half], value[half]) / jnp.concatenate(norms, axis=0))
            total = totals[0] + totals[1]
            for j in range(2):
                part = total[j * rows : (j + 1) * rows]
                full_ref[0, :, at + j * pair : at + (j + 1) * pair] = part
                low_ref[0, :, at + j * pair : at + (j + 1) * pair] = low(part)
        for n, log in enumerate(logs):
            log_ref[0, n * tile : (n + 1) * tile, :] = log

    def backward(
        starts_ref, place_ref, query_ref, even_ref, odd_ref, full_ref, log_ref, grad_ref,
        query_grad_ref, even_grad_ref, odd_grad_ref,
        cap, key, value, key_turned, log_rows, delta_rows, weight_buf, score_buf, query_buf, grad_buf,
    ):
        stream, place = pl.program_id(0) + place_ref[1], place_ref[0]
        spread(even_ref, odd_ref, key, value)
        query_pos = place * rows + lax.broadcasted_iota(jnp.int32, (1, rows), 1)
        begin = doc_begin(starts_ref, stream, query_pos)
        for j in range(parts):
            key_pos = (place ^ (2 * (j % half_parts) + j // half_parts)) * rows + lax.broadcasted_iota(jnp.int32, (rows, rows), 0)
            allowed = (key_pos >= begin) & (key_pos <= query_pos)
            cap[j * rows : (j + 1) * rows, :] = jnp.where(allowed, 3.0e38, -1e30)
            here = pl.ds(j * rows, rows)
            key_turned[:, j * rows : (j + 1) * rows] = low(wide(key[0, here, :]).T[:HS])
        log_rows[...] = log_ref[0].T[: log_rows.shape[0]]
        head_of = lax.broadcasted_iota(jnp.int32, (delta_rows.shape[0], width), 1) // HS
        chosen = (head_of == lax.broadcasted_iota(jnp.int32, (delta_rows.shape[0], width), 0)).astype(jnp.float32)
        delta_rows[...] = lax.dot_general(
            chosen, wide(grad_ref[0]) * full_ref[0], (((1,), (1,)), ((), ())),
            precision=lax.Precision.HIGHEST, preferred_element_type=jnp.float32,
        )
        first = lanes((2 * rows, pair)) < HS
        for g in range(groups):
            at = g * 2 * pair
            both, both_grad = query_ref[0, :, at : at + 2 * pair], grad_ref[0, :, at : at + 2 * pair]
            two = jnp.concatenate([both[:, :pair], both[:, pair:]], axis=0)
            two_grad = jnp.concatenate([both_grad[:, :pair], both_grad[:, pair:]], axis=0)
            turned = []
            for half in range(2):
                h = 4 * g + half
                span = slice((2 * g + half) * 2 * rows, (2 * g + half + 1) * 2 * rows)
                keep = first if half == 0 else jnp.logical_not(first)
                query_buf[span, :] = low(jnp.where(keep, wide(two), 0.0))
                grad_buf[span, :] = low(jnp.where(keep, wide(two_grad), 0.0))
                log = jnp.concatenate([log_rows[h : h + 1, :], log_rows[h + 2 : h + 3, :]], axis=1)
                delta = jnp.concatenate([delta_rows[h : h + 1, :], delta_rows[h + 2 : h + 3, :]], axis=1)
                scores, weight_grads = cols_dot(key[half], two), cols_dot(value[half], two_grad)
                for t in range(keys // (2 * tile)):
                    own = slice(t * 2 * tile, (t + 1) * 2 * tile)
                    limit = cap[own, :]
                    limit = jnp.concatenate([limit, limit], axis=1)
                    weights = jnp.exp2(jnp.minimum(scores[own] * factor, limit) - log)
                    weight_buf[own, span] = low(weights)
                    score_buf[own, span] = low(weights * (weight_grads[own] - delta))
                turned.append(dot(key_turned[...], score_buf[:, span]))
            turned = jnp.concatenate(turned, axis=0) * HS ** (-0.5)
            query_grad_ref[0, :, at : at + pair] = low(turned[:, :rows].T)
            query_grad_ref[0, :, at + pair : at + 2 * pair] = low(turned[:, rows:].T)
        for j in range(parts):
            here = pl.ds(j * rows, rows)
            value_sum = dot(weight_buf[here, :], grad_buf[...])
            key_sum = dot(score_buf[here, :], query_buf[...]) * HS ** (-0.5)
            value_sum = value_sum + pltpu.roll(value_sum, HS, 1)
            key_sum = key_sum + pltpu.roll(key_sum, HS, 1)
            ref = even_grad_ref if j < half_parts else odd_grad_ref
            ref[j % half_parts, 0] = low(jnp.where(lanes((rows, pair)) < HS, key_sum, value_sum))

    def specs(first):
        return (
            pl.BlockSpec((1, rows, width), lambda b, *_: (b + first, 0, 0)),
            pl.BlockSpec((1, rows, pair), lambda b, *_: (b + first, 0, 0)),
            pl.BlockSpec((half_parts, 1, rows, pair), lambda b, *_: (0, b + first, 0, 0)),
        )

    flow, logs, blocks = specs(0)

    shared = [
        pltpu.VMEM((2, keys, pair), jnp.bfloat16),
        pltpu.VMEM((2, keys, pair), jnp.bfloat16),
    ]
    run_forward = pl.pallas_call(
        forward,
        grid_spec=pltpu.PrefetchScalarGridSpec(
            num_scalar_prefetch=2,
            grid=(batches,),
            in_specs=[flow, blocks, blocks],
            out_specs=[flow, flow, logs],
            scratch_shapes=[pltpu.VMEM((rows, keys), jnp.float32)]
            + shared
            + [pltpu.VMEM((2, 2 * rows, keys), jnp.bfloat16)],
        ),
        out_shape=[
            jax.ShapeDtypeStruct((batches, rows, width), jnp.bfloat16),
            jax.ShapeDtypeStruct((batches, rows, width), jnp.float32),
            jax.ShapeDtypeStruct((batches, rows, pair), jnp.float32),
        ],
        compiler_params=pltpu.CompilerParams(vmem_limit_bytes=VMEM_LIMIT),
        cost_estimate=NO_COST,
        name="attention_forward",
    )
    head_rows = -(-(width // HS) // 8) * 8
    all_columns = rows * (width // HS)
    count = batches // runs

    def call_backward(run):
        here_flow, here_logs, here_blocks = specs(run * count)
        return pl.pallas_call(
        backward,
        grid_spec=pltpu.PrefetchScalarGridSpec(
            num_scalar_prefetch=2,
            grid=(count,),
            in_specs=[here_flow, here_blocks, here_blocks, here_flow, here_logs, here_flow],
            out_specs=[flow, blocks, blocks],
            scratch_shapes=[pltpu.VMEM((keys, rows), jnp.float32)]
            + shared
            + [
                pltpu.VMEM((HS, keys), jnp.bfloat16),
                pltpu.VMEM((head_rows, rows), jnp.float32),
                pltpu.VMEM((head_rows, rows), jnp.float32),
                pltpu.VMEM((keys, all_columns), jnp.bfloat16),
                pltpu.VMEM((keys, all_columns), jnp.bfloat16),
                pltpu.VMEM((all_columns, pair), jnp.bfloat16),
                pltpu.VMEM((all_columns, pair), jnp.bfloat16),
            ],
        ),
        out_shape=[
            jax.ShapeDtypeStruct((count, rows, width), jnp.bfloat16),
            jax.ShapeDtypeStruct((half_parts, count, rows, pair), jnp.bfloat16),
            jax.ShapeDtypeStruct((half_parts, count, rows, pair), jnp.bfloat16),
        ],
        compiler_params=pltpu.CompilerParams(vmem_limit_bytes=VMEM_LIMIT),
        cost_estimate=NO_COST,
        name="attention_backward",
    )

    return run_forward, [call_backward(run) for run in range(runs)]


def in_hbm(arrays):
    return [pltpu.with_memory_space_constraint(array, pltpu.HBM) for array in arrays]


def ffn_kernels(rows, width, chunk, wt_count):
    units = 2 * chunk
    all_rows = 2 * rows
    block_rows = width // wt_count
    hbm = pl.BlockSpec(memory_space=pltpu.HBM)
    vmem = pl.BlockSpec(memory_space=pltpu.VMEM)
    params = pltpu.CompilerParams(vmem_limit_bytes=VMEM_LIMIT)

    def fetch(weights, which, held, sem):
        copies = []
        for n, arrays in enumerate(weights):
            blocks = [array.at[block] for array in arrays for block in range(array.shape[0])]
            for row, block in enumerate(blocks):
                copies.append(
                    pltpu.make_async_copy(
                        block.at[pl.ds(which * block_rows, block_rows), :],
                        held.at[pl.ds(row * block_rows, block_rows), pl.ds(n * chunk, chunk)],
                        sem.at[len(copies)],
                    )
                )
        for copy in copies:
            copy.start()
        return copies

    def send(pairs, sems):
        copies = [pltpu.make_async_copy(source, out, sems.at[n]) for n, (source, out) in enumerate(pairs)]
        for copy in copies:
            copy.start()
        return copies

    part_rows = 256
    tile = 16

    def units_of(inputs, grads, bias, held_up, held_down, act, grad_units):
        sums = jnp.zeros((8, units), jnp.float32)
        for s in range(2):

            def part(i, sums):
                here = rows_at(i, part_rows)
                up = dot(inputs[s][here, :], held_up[...])
                act_grad = dot(grads[s][here, :], held_down[...])
                for t in range(part_rows // tile):
                    own = slice(t * tile, (t + 1) * tile)
                    there = pl.ds(pl.multiple_of(s * rows + i * part_rows + t * tile, tile), tile)
                    value, slope = gelu_both(up[own] + bias)
                    grad = act_grad[own] * slope
                    act[there, :] = low(value)
                    grad_units[there, :] = low(grad)
                    sums = sums + (grad[:8] + grad[8:])
                return sums

            sums = loop(rows // part_rows, part, sums)
        return jnp.sum(sums, axis=0, keepdims=True)

    def product_of(turned, right, product):
        def part(i, carry):
            here = rows_at(i, part_rows)
            product[here, :] = low(dot(turned[here, :], right[...]))
            return carry

        loop(width // part_rows, part)

    def back_to(refs, sources, weights):
        for s, ref in enumerate(refs):

            def part(i, carry):
                here = pl.ds(pl.multiple_of(s * rows + i * part_rows, part_rows), part_rows)
                total = cols_dot(sources[0][here, :], weights[0][...]) + cols_dot(sources[1][here, :], weights[1][...])
                ref[rows_at(i, part_rows), :] = total.astype(ref.dtype)
                return carry

            loop(rows // part_rows, part)

    def halves(product, m):
        cols = pl.ds(m * chunk, chunk)
        return [product.at[pl.ds(h * width // 2, width // 2), cols] for h in range(2)]

    def first(
        own, other, grad_own, grad_other, turned, bias, w0, w1, w2, w3,
        act_out, units_out, out_a, out_b, sums_out,
        held_up, held_down, act, grad_units, product, sems, out_sems,
    ):
        weights = ((w0, w1), (w2, w3))
        copies = fetch(weights, 0, held_up, sems.at[0]) + fetch(weights, 1, held_down, sems.at[1])
        for copy in copies:
            copy.wait()
        sums_out[...] = units_of((own, other), (grad_own, grad_other), bias[...], held_up, held_down, act, grad_units)
        sent = send(((act, act_out), (grad_units, units_out)), out_sems.at[0])
        product_of(turned, act, product)
        sent += send(
            ((product.at[:, pl.ds(0, chunk)], out_a), (product.at[:, pl.ds(chunk, chunk)], out_b)), out_sems.at[1]
        )
        for copy in sent:
            copy.wait()

    def second(
        own, other, grad_own, grad_other, turned, bias, units_first, w0, w1, w2, w3, w4, w5, w6, w7,
        act_out, units_out, out_a, out_b, out_c, sums_out, back_own, back_other,
        held_up, held_more, held_down, act, grad_units, more_units, product, sems, out_sems, more_sem,
    ):
        weights, before = ((w4, w5), (w6, w7)), ((w0, w1), (w2, w3))
        copies = fetch(weights, 0, held_up, sems.at[0]) + fetch(weights, 1, held_down, sems.at[1])
        more = fetch(before, 0, held_more, sems.at[2])
        more.append(pltpu.make_async_copy(units_first, more_units, more_sem))
        more[-1].start()
        for copy in copies:
            copy.wait()
        sums_out[...] = units_of((own, other), (grad_own, grad_other), bias[...], held_up, held_down, act, grad_units)
        sent = send(((act, act_out), (grad_units, units_out)), out_sems.at[0])
        product_of(turned, act, product)
        top, bottom = halves(product, 1)
        sent += send(((product.at[:, pl.ds(0, chunk)], out_a), (top, out_b), (bottom, out_c)), out_sems.at[1])
        for copy in more:
            copy.wait()
        back_to((back_own, back_other), (grad_units, more_units), (held_up, held_more))
        for copy in sent:
            copy.wait()

    def third(own, other, units_a, units_b, out_0, out_1, out_2, out_3, out_4, turned, held, products, sems, out_sems):
        copies = send(((units_a, held.at[0]), (units_b, held.at[1])), sems)
        turn((own, other), turned)
        for copy in copies:
            copy.wait()
        products[1] = low(dot(turned[...], held[1]))
        top, bottom = halves(products.at[1], 1)
        sent = send(((products.at[1, :, pl.ds(0, chunk)], out_2), (top, out_3), (bottom, out_4)), out_sems.at[0])
        products[0] = low(dot(turned[...], held[0]))
        sent += send(
            ((products.at[0, :, pl.ds(0, chunk)], out_0), (products.at[0, :, pl.ds(chunk, chunk)], out_1)),
            out_sems.at[1],
        )
        for copy in sent:
            copy.wait()

    def down(act_a, act_b, w0, w1, w2, w3, w4, w5, w6, w7, own_ref, other_ref, held_a, held_b, sems):
        copies = fetch(((w0, w1), (w2, w3)), 1, held_a, sems.at[0]) + fetch(((w4, w5), (w6, w7)), 1, held_b, sems.at[1])
        for copy in copies:
            copy.wait()
        for s, ref in enumerate((own_ref, other_ref)):
            here = slice(s * rows, (s + 1) * rows)
            total = cols_dot(act_a[here, :], held_a[...]) + cols_dot(act_b[here, :], held_b[...])
            ref[...] = total.astype(ref.dtype)

    dma = pltpu.SemaphoreType.DMA
    held = pltpu.VMEM((width, units), jnp.bfloat16)
    flow = pltpu.VMEM((all_rows, units), jnp.bfloat16)
    flow_out = pltpu.HBM((all_rows, units), jnp.bfloat16)
    whole = pltpu.HBM((width, chunk), jnp.bfloat16)
    part = pltpu.HBM((width // 2, chunk), jnp.bfloat16)
    sums = jax.ShapeDtypeStruct((1, units), jnp.float32)
    own = jax.ShapeDtypeStruct((rows, width), jnp.float32)
    other = jax.ShapeDtypeStruct((rows, width), jnp.bfloat16)
    run_first = pl.pallas_call(
        first,
        in_specs=[vmem] * 6 + [hbm] * 4,
        out_specs=[hbm] * 4 + [vmem],
        out_shape=[flow_out, flow_out, whole, whole, sums],
        scratch_shapes=[held, held, flow, flow, held, dma((2, 2 * wt_count)), dma((2, 2))],
        compiler_params=params,
        cost_estimate=NO_COST,
        name="ffn_first",
    )
    run_second = pl.pallas_call(
        second,
        in_specs=[vmem] * 6 + [hbm] * 9,
        out_specs=[hbm] * 5 + [vmem] * 3,
        out_shape=[flow_out, flow_out, whole, part, part, sums, own, other],
        scratch_shapes=[held, held, held, flow, flow, flow, held, dma((3, 2 * wt_count)), dma((2, 3)), dma(())],
        compiler_params=params,
        cost_estimate=NO_COST,
        name="ffn_second",
    )
    run_third = pl.pallas_call(
        third,
        in_specs=[vmem] * 2 + [hbm] * 2,
        out_specs=[hbm] * 5,
        out_shape=[whole, whole, whole, part, part],
        scratch_shapes=[
            pltpu.VMEM((width, all_rows), jnp.bfloat16),
            pltpu.VMEM((2, all_rows, units), jnp.bfloat16),
            pltpu.VMEM((2, width, units), jnp.bfloat16),
            dma((2,)),
            dma((2, 3)),
        ],
        compiler_params=params,
        cost_estimate=NO_COST,
        name="ffn_grads",
    )
    run_down = pl.pallas_call(
        down,
        in_specs=[vmem] * 2 + [hbm] * 8,
        out_specs=[vmem] * 2,
        out_shape=[own, other],
        scratch_shapes=[held, held, dma((2, 2 * wt_count))],
        compiler_params=params,
        cost_estimate=NO_COST,
        name="ffn_down",
    )
    return run_first, run_second, run_third, run_down


def turn(refs, turned):
    rows = refs[0].shape[0]
    for s, ref in enumerate(refs):
        for i in range(rows // 128):
            block = wide(ref[i * 128 : (i + 1) * 128, :])
            turned[:, s * rows + i * 128 : s * rows + (i + 1) * 128] = low(block.T)


def turn_both(own, other):
    vmem = pl.BlockSpec(memory_space=pltpu.VMEM)
    rows, width = own.shape
    return pl.pallas_call(
        lambda a, b, out: turn((a, b), out),
        in_specs=[vmem] * 2,
        out_specs=vmem,
        out_shape=jax.ShapeDtypeStruct((width, 2 * rows), own.dtype),
        compiler_params=pltpu.CompilerParams(vmem_limit_bytes=VMEM_LIMIT),
        cost_estimate=NO_COST,
        name="turn",
    )(own, other)


def out_projection(rows, width):
    tile = 32

    def kernel(attended, weight, stream, bias, gain, shift, hidden_ref, normed_ref):
        product = dot(attended[...], weight[...])
        for t in range(rows // tile):
            here = slice(t * tile, (t + 1) * tile)
            hidden = wide(stream[here, :]) + product[here] + bias[...]
            hidden_ref[here, :] = hidden
            normed_ref[here, :] = low(layer_norm(hidden, gain[...], shift[...]))

    vmem = pl.BlockSpec(memory_space=pltpu.VMEM)
    return pl.pallas_call(
        kernel,
        in_specs=[vmem] * 6,
        out_specs=[vmem] * 2,
        out_shape=[
            jax.ShapeDtypeStruct((rows, width), jnp.float32),
            jax.ShapeDtypeStruct((rows, width), jnp.bfloat16),
        ],
        compiler_params=pltpu.CompilerParams(vmem_limit_bytes=VMEM_LIMIT),
        cost_estimate=NO_COST,
        name="out_projection",
    )


def norm_back(values, gain, grad):
    centre = values - jnp.mean(values, axis=-1, keepdims=True)
    scale = lax.rsqrt(jnp.mean(centre * centre, axis=-1, keepdims=True) + NORM_EPS)
    unit = centre * scale
    inner = grad * gain
    mean = jnp.mean(inner, axis=-1, keepdims=True)
    along = jnp.mean(inner * unit, axis=-1, keepdims=True)
    return scale * (inner - mean - unit * along), grad * unit


def fold_rows(values):
    total = values[:8]
    for i in range(1, values.shape[0] // 8):
        total = total + values[i * 8 : (i + 1) * 8]
    return total


def hidden_back(rows, width):
    tile = 32

    def kernel(own, got, hidden, back, gain, weight, grad_ref, low_ref, attended_ref, sums_ref):
        sums = [jnp.zeros((8, width), jnp.float32) for _ in range(3)]
        for t in range(rows // tile):
            here = slice(t * tile, (t + 1) * tile)
            pulled, terms = norm_back(hidden[here, :], gain[...], own[here, :] + wide(got[here, :]))
            grad = wide(back[here, :]) + pulled
            grad_ref[here, :] = grad
            low_ref[here, :] = low(grad)
            for n, part in enumerate((terms, own[here, :] + wide(got[here, :]), grad)):
                sums[n] = sums[n] + fold_rows(part)
        for n in range(3):
            sums_ref[n : n + 1, :] = jnp.sum(sums[n], axis=0, keepdims=True)
        attended_ref[...] = low(cols_dot(low_ref[...], weight[...]))

    vmem = pl.BlockSpec(memory_space=pltpu.VMEM)
    return pl.pallas_call(
        kernel,
        in_specs=[vmem] * 6,
        out_specs=[vmem] * 4,
        out_shape=[
            jax.ShapeDtypeStruct((rows, width), jnp.float32),
            jax.ShapeDtypeStruct((rows, width), jnp.bfloat16),
            jax.ShapeDtypeStruct((rows, width), jnp.bfloat16),
            jax.ShapeDtypeStruct((3, width), jnp.float32),
        ],
        compiler_params=pltpu.CompilerParams(vmem_limit_bytes=VMEM_LIMIT),
        cost_estimate=NO_COST,
        name="hidden_back",
    )


def stream_back(rows, width, parts, row_groups, piece):
    tile = 32
    chips = parts // 2

    def kernel(
        place_ref, kv_0, kv_1, kv_2, kv_3, queries, weight, tokens, gain, grad_hidden, normed, back, hidden_sums,
        units_a, units_b, input_ref, even_ref, odd_ref, grad_kv, grads, turned, product, small,
    ):
        place = place_ref[0]
        sums = [jnp.zeros((8, width), jnp.float32) for _ in range(4)]
        value_sums = jnp.zeros((8, 2 * HS), jnp.float32)
        for t in range(rows // tile):
            here = slice(t * tile, (t + 1) * tile)
            total = wide(kv_0[here, :]) + wide(kv_1[here, :]) + wide(kv_2[here, :]) + wide(kv_3[here, :])
            grad_kv[here, :] = low(total)
            value_sums = value_sums + fold_rows(total)
        turn((normed,), turned)
        product[...] = dot(turned[...], grad_kv[...])
        grads[...] = cols_dot(queries[...], weight[:, :width]) + cols_dot(grad_kv[...], weight[:, width:])
        for t in range(rows // tile):
            here = slice(t * tile, (t + 1) * tile)
            grad = grads[here, :]
            pulled, terms = norm_back(wide(tokens[here, :]), gain[...], grad)
            input_ref[here, :] = grad_hidden[here, :] + pulled
            for n, part in enumerate((terms, grad, wide(queries[here, :]), wide(back[here, :]))):
                sums[n] = sums[n] + fold_rows(part)
        sums = [jnp.sum(part, axis=0, keepdims=True) for part in sums]
        small[...] = jnp.zeros_like(small)
        rows_in = (sums[0], sums[1], hidden_sums[0:1, :], hidden_sums[1:2, :], sums[2], hidden_sums[2:3, :], sums[3])
        for n, row in enumerate(rows_in):
            for j in range(width // 128):
                line = n * (width // 128) + j
                small[line : line + 1, :] = row[:, j * 128 : (j + 1) * 128]
        start = 7 * (width // 128)
        small[start : start + 1, :] = jnp.sum(value_sums, axis=0, keepdims=True)
        lines = FF // parts // 128
        for m in range(chips):
            units = (units_a, units_b)[m // 2]
            for j in range(lines):
                line = start + 1 + (place ^ (2 * m)) * lines + j
                at = (m % 2 * lines + j) * 128
                small[pl.ds(line, 1), :] = units[:, at : at + 128]
        for k in range(parts):
            ref = odd_ref if k % 2 else even_ref
            mine = low(small[pl.ds(pl.multiple_of((place ^ k) * piece, 8), piece), :])
            for w in range(row_groups):
                at = pl.multiple_of(w * piece * parts + (place ^ k) * piece, 8)
                ref[k // 2, w, :, :128] = low(product[pl.ds(at, piece), :])
                ref[k // 2, w, :, 128:] = mine

    vmem = pl.BlockSpec(memory_space=pltpu.VMEM)
    stack = jax.ShapeDtypeStruct((chips, row_groups, piece, 256), jnp.bfloat16)
    return pl.pallas_call(
        kernel,
        in_specs=[pl.BlockSpec(memory_space=pltpu.SMEM)] + [vmem] * 14,
        out_specs=[vmem] * 3,
        out_shape=[jax.ShapeDtypeStruct((rows, width), jnp.float32), stack, stack],
        scratch_shapes=[
            pltpu.VMEM((rows, 2 * HS), jnp.bfloat16),
            pltpu.VMEM((rows, width), jnp.float32),
            pltpu.VMEM((width, rows), jnp.bfloat16),
            pltpu.VMEM((width, 2 * HS), jnp.float32),
            pltpu.VMEM((parts * piece, 128), jnp.float32),
        ],
        compiler_params=pltpu.CompilerParams(vmem_limit_bytes=VMEM_LIMIT),
        cost_estimate=NO_COST,
        name="stream_back",
    )


def attn_grads(rows, width, row_groups, parts, piece):
    def kernel(place_ref, left_a, right_a, left_b, right_b, even_ref, odd_ref, turned, total):
        place = place_ref[0]
        for n, (left, right) in enumerate(((left_a, right_a), (left_b, right_b))):
            for i in range(rows // 128):
                turned[:, i * 128 : (i + 1) * 128] = low(wide(left[i * 128 : (i + 1) * 128, :]).T)
            total[:, n * width : (n + 1) * width] = dot(turned[...], right[...])
        for k in range(parts):
            ref = odd_ref if k % 2 else even_ref
            for w in range(row_groups):
                at = pl.multiple_of(w * piece * parts + (place ^ k) * piece, 8)
                ref[k // 2, w] = low(total[pl.ds(at, piece), :])

    vmem = pl.BlockSpec(memory_space=pltpu.VMEM)
    shape = jax.ShapeDtypeStruct((parts // 2, row_groups, piece, 2 * width), jnp.bfloat16)
    return pl.pallas_call(
        kernel,
        grid_spec=pltpu.PrefetchScalarGridSpec(
            num_scalar_prefetch=1,
            grid=(),
            in_specs=[vmem] * 4,
            out_specs=[vmem] * 2,
            scratch_shapes=[pltpu.VMEM((width, rows), jnp.bfloat16), pltpu.VMEM((width, 2 * width), jnp.float32)],
        ),
        out_shape=[shape] * 2,
        compiler_params=pltpu.CompilerParams(vmem_limit_bytes=VMEM_LIMIT),
        cost_estimate=NO_COST,
        name="attn_grads",
    )


def attn_update(rows, columns, width, parts, piece):
    qkv = columns - width

    def kernel(place_ref, even_ref, odd_ref, master, first, second, *outs):
        place = place_ref[0]
        for k in range(parts):
            ref = odd_ref if k % 2 else even_ref
            here = pl.ds(pl.multiple_of((place ^ k) * piece, 8), piece)
            for cols, source in (
                (slice(0, width), slice(0, width)),
                (slice(width, qkv), slice(2 * width, columns)),
                (slice(qkv, columns), slice(width, 2 * width)),
            ):
                grad = wide(ref[k // 2, :, source])
                got = adam_update(master[here, cols], grad, first[here, cols], second[here, cols], 0.1, 0.1)
                outs[0][here, cols] = got[0]
                outs[1][here, cols] = got[1]
                outs[2][here, cols] = got[2]

    vmem = pl.BlockSpec(memory_space=pltpu.VMEM)
    return pl.pallas_call(
        kernel,
        grid_spec=pltpu.PrefetchScalarGridSpec(
            num_scalar_prefetch=1, grid=(), in_specs=[vmem] * 5, out_specs=[vmem] * 3, scratch_shapes=[]
        ),
        out_shape=[jax.ShapeDtypeStruct((rows, columns), jnp.float32)] * 3,
        compiler_params=pltpu.CompilerParams(vmem_limit_bytes=VMEM_LIMIT),
        cost_estimate=NO_COST,
        name="attn_update",
    )


def ffn_update(rows, units, parts, chunk):
    per_row = 2 * units // 128
    rows_once = 32
    lines = rows_once * per_row

    def kernel(place_ref, even, odd, master, first, second, first_out, second_out, master_out, total):
        place = place_ref[0]
        for k in range(parts):
            grad = odd if k % 2 else even
            for j in range(chunk // 128):
                for which in range(2):
                    line = (place ^ k) * (2 * chunk // 128) + 2 * j + which
                    total[pl.ds(line, rows_once, per_row), :] = wide(
                        grad[k // 2, which, :, j * 128 : (j + 1) * 128]
                    )
        for t in range(lines // 64):
            own = slice(t * 64, (t + 1) * 64)
            got = adam_update(master[own, :], total[own, :], first[own, :], second[own, :], 0.1, 0.1)
            first_out[own, :] = got[0]
            second_out[own, :] = got[1]
            master_out[own, :] = got[2]

    block = pl.BlockSpec((lines, 128), lambda i, *_: (i, 0))
    stack = pl.BlockSpec((parts // 2, 2, rows_once, chunk), lambda i, *_: (0, 0, i, 0))
    call = pl.pallas_call(
        kernel,
        grid_spec=pltpu.PrefetchScalarGridSpec(
            num_scalar_prefetch=1,
            grid=(rows // rows_once,),
            in_specs=[stack] * 2 + [block] * 3,
            out_specs=[block] * 3,
            scratch_shapes=[pltpu.VMEM((lines, 128), jnp.float32)],
        ),
        out_shape=[jax.ShapeDtypeStruct((rows * per_row, 128), jnp.float32)] * 3,
        compiler_params=pltpu.CompilerParams(vmem_limit_bytes=VMEM_LIMIT),
        cost_estimate=NO_COST,
        name="ffn_update",
    )

    def fold(array):
        return jnp.swapaxes(array.reshape(rows, 2, units // 128, 128), 1, 2).reshape(-1, 128)

    def unfold(array):
        return jnp.swapaxes(array.reshape(rows, units // 128, 2, 128), 1, 2).reshape(rows, 2, units)

    def run(place, even, odd, master, first, second):
        return tuple(unfold(array) for array in call(place, even, odd, fold(master), fold(first), fold(second)))

    return run


def shards(
    tokens,
    doc_starts,
    attn_master,
    attn_mom,
    attn_sq,
    ffn_master,
    ffn_mom,
    ffn_sq,
    small_master,
    small_mom,
    small_sq,
    cotangent,
):
    ctx_count, wt_count = lax.axis_size("ctx"), lax.axis_size("wt")
    ctx_place, wt_place = lax.axis_index("ctx"), lax.axis_index("wt")
    batches, rows_here, width = tokens.shape
    qkv_cols = width + 2 * HS
    attn_columns = attn_master.shape[1]
    all_rows = batches * rows_here
    shard_rows = attn_master.shape[0]
    piece_rows = shard_rows // ctx_count
    chunk = FF // ctx_count
    chips = ctx_count // 2
    order = ctx_place ^ jnp.arange(ctx_count, dtype=jnp.int32)
    (
        gain_one,
        shift_one,
        gain_two,
        shift_two,
        bias_query,
        bias_out,
        bias_proj,
        bias_value,
        bias_hidden,
    ) = split_small(small_master)
    runs = 2 if batches % 2 == 0 else 1
    places = [jnp.stack([ctx_place, jnp.int32(run * (batches // runs))]) for run in range(runs)]
    place = places[0]
    wt_half = wt_count // 2
    out_rows = shard_rows // chips
    run_forward, run_backward = attention_kernels(batches, rows_here, width, ctx_count, runs)
    ffn_first, ffn_second, ffn_third, ffn_down = ffn_kernels(all_rows, width, chunk, wt_count)
    step = Steps()

    def both(own, got, place, bit, axis=0):
        ahead, behind = jnp.stack([own, got], axis), jnp.stack([got, own], axis)
        return jnp.where((place & bit) == 0, ahead, behind)

    def in_order(even, odd):
        buffer = jnp.zeros((ctx_count,) + even.shape[1:], even.dtype)
        for m in range(chips):
            buffer = put(buffer, even[m][None], ctx_place ^ (2 * m), 0)
            buffer = put(buffer, odd[m][None], ctx_place ^ (2 * m + 1), 0)
        return buffer

    def send_chips(piece):
        return [xor_send(piece, mask) for mask in range(2, ctx_count, 2)]

    def split_wt(total, bit):
        ahead, behind = jnp.split(total, 2)
        kept, sent = jnp.where((wt_place & bit) == 0, ahead, behind), jnp.where((wt_place & bit) == 0, behind, ahead)
        return kept, sent

    def add_low(*arrays):
        return low(sum(wide(array) for array in arrays))

    attn = low(take(attn_master, ctx_place, 0, piece_rows))
    attn_got = xor_wt(attn, 1)
    rest = low(jnp.swapaxes(take(ffn_master, ctx_place, 2, chunk), 0, 1).reshape(2 * shard_rows, chunk))
    attn_got, rest = together(attn_got, rest)
    rest_got = xor_wt(rest, 1)
    attn = both(attn, attn_got, wt_place, 1)
    attn_got = xor_wt(attn, 2)
    flat_tokens = tokens.reshape(all_rows, width)
    attn_got, rest_got = together(attn_got, rest_got)
    attn = both(attn, attn_got, wt_place, 2).reshape((wt_count,) + attn.shape[1:])
    third = 2 * shard_rows // 3
    rest = [both(rest[n * third :][:third], rest_got[n * third :][:third], wt_place, 1) for n in range(3)]
    attn, *rest = together(attn, *rest)
    far = [xor_wt(rest[0], 2)]
    attn_got = send_chips(attn)
    back_low, flat_tokens, attn = together(cotangent.reshape(all_rows, width), flat_tokens, attn)
    normed_low = low(layer_norm(wide(flat_tokens), gain_one, shift_one))
    *attn_got, normed_low, far[0], rest[1] = together(*attn_got, normed_low, far[0], rest[1])
    far.append(xor_wt(rest[1], 2))
    attn_even = jnp.stack([attn] + attn_got)
    attn_odd = xor_send(attn_even, 1)
    back_other = xor_send(back_low, 1)
    bias_parts = bias_hidden.reshape(ctx_count, chunk)[order[::2]].reshape(1, chips * chunk)
    bias_near, bias_far = jnp.split(bias_parts, 2, axis=1)
    attn_odd, bias_near, bias_far = together(attn_odd, bias_near, bias_far)
    blocks = jnp.where((ctx_place & 1) == 0, jnp.stack([attn_even, attn_odd], 1), jnp.stack([attn_odd, attn_even], 1))
    for n in range(chips.bit_length() - 1):
        pairs = blocks.reshape((-1, 2, 1 << n) + blocks.shape[1:])
        blocks = jnp.where((ctx_place & (2 << n)) == 0, pairs, pairs[:, ::-1]).reshape(blocks.shape)
    weight_attn = jnp.transpose(blocks, (2, 0, 1, 3, 4)).reshape(width, attn_columns)
    weight_qkv, weight_out = weight_attn[:, :qkv_cols], weight_attn[:, qkv_cols:]
    mixed = dot(normed_low, weight_qkv)
    queries = low(mixed[:, :width] + bias_query).reshape(batches, rows_here, width)
    kv_bias = jnp.concatenate([jnp.zeros((HS,), jnp.float32), bias_value])
    kv_local = low(mixed[:, width:] + kv_bias).reshape(batches, rows_here, 2 * HS)
    kv_local, far[1], rest[2] = together(kv_local, far[1], rest[2])
    far.append(xor_wt(rest[2], 2))
    kv_got = send_chips(kv_local)
    back_turned = turn_both(back_low, back_other)
    *kv_got, far[2], back_turned = together(*kv_got, far[2], back_turned)
    kv_even = jnp.stack([kv_local] + kv_got)
    kv_odd = xor_send(kv_even, 1)
    own, got = jnp.concatenate(rest, axis=1), jnp.concatenate(far, axis=1)
    first_half = (wt_place & 2) == 0
    rest_low, rest_high = jnp.where(first_half, own, got), jnp.where(first_half, got, own)
    low_x, high_y, high_x, low_y = xor_send(rest_low, 2), xor_send(rest_high, 4), xor_send(rest_high, 2), xor_send(rest_low, 4)
    queries, kv_odd, rest_low, rest_high = together(queries, kv_odd, rest_low, rest_high)

    attended_low, attended, logs = step(run_forward, doc_starts, place, queries, kv_even, kv_odd)
    attended_low = attended_low.reshape(all_rows, width)
    attended_low, low_x, high_y, high_x, low_y = together(attended_low, low_x, high_y, high_x, low_y)
    low_diagonal, high_diagonal = xor_send(low_x, 4), xor_send(high_y, 2)

    hidden, normed_two = step(
        out_projection(all_rows, width), attended_low, weight_out, flat_tokens, bias_out[None], gain_two[None],
        shift_two[None],
    )
    normed_other = xor_send(normed_two, 1)

    weights = [rest_low, rest_high, low_x, high_x, low_y, high_y, low_diagonal, high_diagonal]
    flows = (normed_two, normed_other, back_low, back_other, back_turned)
    act_first, units_first, down_own, down_x, sums_first = step(
        lambda *args: ffn_first(*args[:6], *in_hbm(args[6:])), *flows, bias_near, *weights[:4]
    )
    act_second, units_second, down_y, down_top, down_bottom, sums_second, back_own, back_part = step(
        lambda *args: ffn_second(*args[:6], *in_hbm(args[6:])), *flows, bias_far, units_first, *weights
    )
    back_got = xor_send(back_part, 1)
    top_got, bottom_got = xor_send(down_top, 4), xor_send(down_bottom, 2)

    def meet(along_x, along_y, top, bottom):
        half = width // 2
        return (
            jnp.concatenate([add_low(along_x[:half], top), along_x[half:]]),
            jnp.concatenate([along_y[:half], add_low(along_y[half:], bottom)]),
        )

    up_own, up_x, up_y, up_top, up_bottom = step(
        lambda *args: ffn_third(*args[:2], *in_hbm(args[2:])), normed_two, normed_other, units_first, units_second
    )
    down_x, down_y = step(meet, down_x, down_y, top_got, bottom_got)
    down_got = [xor_send(down_x, 2), xor_send(down_y, 4)]
    top_got, bottom_got = xor_send(up_top, 4), xor_send(up_bottom, 2)

    grad_hidden, grad_hidden_low, grad_attended, hidden_sums = step(
        hidden_back(all_rows, width), back_own, back_got, hidden, back_low, gain_two[None], weight_out
    )
    grad_attended = grad_attended.reshape(batches, rows_here, width)
    def by_wt(*arrays):
        return split_wt(add_low(*arrays).reshape(wt_count, shard_rows, chunk), 2)

    def next_wt(kept, got):
        return split_wt(add_low(kept, got), 1)

    def kv_pieces(evens, odds):
        total = jnp.concatenate([add_low(a, b) for a, b in zip(evens, odds)], axis=1)
        return [total[m] for m in range(chips)]

    backs = [step(run_backward[0], doc_starts, places[0], queries, kv_even, kv_odd, attended, logs, grad_attended)]
    kv_got = [xor_send(backs[0][2], 1)]
    down_kept, down_sent = step(by_wt, down_own, *down_got)
    grad_attended, down_kept, down_sent = together(grad_attended, down_kept, down_sent)
    down_got = xor_wt(down_sent, 2)
    backs += [
        step(run_backward[run], doc_starts, places[run], queries, kv_even, kv_odd, attended, logs, grad_attended)
        for run in range(1, runs)
    ]
    backs[-1] = list(backs[-1])
    *backs[-1], down_got, top_got, bottom_got = together(*backs[-1], down_got, top_got, bottom_got)
    kv_got += [xor_send(back[2], 1) for back in backs[1:]]
    grad_queries = [back[0] for back in backs]
    grad_query = jnp.concatenate(grad_queries).reshape(all_rows, width)
    up_x, up_y = meet(up_x, up_y, top_got, bottom_got)
    grad_query, up_x, up_y = together(grad_query, up_x, up_y)
    up_got = [xor_send(up_x, 2), xor_send(up_y, 4)]
    down_kept, down_sent = next_wt(down_kept, down_got)
    kv_half = step(kv_pieces, [back[1] for back in backs], kv_got)
    kv_got = [xor_send(kv_half[m], 2 * m) for m in range(1, chips)]
    wide_even, wide_odd = step(
        attn_grads(all_rows, width, wt_count, ctx_count, piece_rows),
        place, normed_low, grad_query, attended_low, grad_hidden_low,
    )
    small_size = small_master.shape[0]
    up_kept, up_sent = step(by_wt, up_own, *up_got)
    kv_got[0], up_kept, up_sent = together(kv_got[0], up_kept, up_sent)
    up_got = xor_wt(up_sent, 2)
    input_grad, tail_even, tail_odd = step(
        stream_back(all_rows, width, ctx_count, wt_count, piece_rows),
        place, *[array.reshape(all_rows, 2 * HS) for array in (kv_half[0], *kv_got)], grad_query, weight_qkv,
        flat_tokens, gain_one[None], grad_hidden, normed_low, back_low, hidden_sums, sums_first, sums_second,
    )
    input_grad = input_grad.reshape(batches, rows_here, width)
    wide_odd, tail_odd = lax.optimization_barrier((wide_odd, tail_odd))
    wide_odd, tail_odd = xor_send(wide_odd, 1), xor_send(tail_odd, 1)
    def attn_pieces(wide_even, wide_odd, tail_even, tail_odd):
        total = jnp.concatenate([add_low(wide_even, wide_odd), add_low(tail_even, tail_odd)], axis=3)
        return [total[m] for m in range(chips)]

    attn_half = step(attn_pieces, wide_even, wide_odd, tail_even, tail_odd)
    attn_got = [xor_send(attn_half[m], 2 * m) for m in range(1, chips)]
    up_kept, up_sent = step(next_wt, up_kept, up_got)
    up_kept, up_sent, down_kept, down_sent = together(up_kept, up_sent, down_kept, down_sent)
    up_got, down_got = xor_wt(up_sent, 1), xor_wt(down_sent, 1)
    ffn_part = step(
        lambda *arrays: jnp.concatenate([add_low(*arrays[:2]), add_low(*arrays[2:])]), up_kept, up_got, down_kept, down_got
    )
    ffn_got = send_chips(ffn_part)
    down_out, down_other = step(
        lambda *args: ffn_down(*args[:2], *in_hbm(args[2:])), act_first, act_second, *weights
    )
    down_other = xor_send(down_other, 1)
    attn_kept, attn_sent = step(lambda *parts: split_wt(add_low(*parts), 2), attn_half[0], *attn_got)
    attn_got = xor_wt(attn_sent, 2)
    layer_out = step(
        lambda hidden, own, got: low(hidden + own + wide(got) + bias_proj).reshape(batches, rows_here, width),
        hidden, down_out, down_other,
    )
    attn_kept, attn_sent = step(lambda kept, got: split_wt(add_low(kept, got), 1), attn_kept, attn_got)
    attn_got = xor_wt(attn_sent, 1)
    ffn_even = step(lambda *parts: jnp.stack(parts), ffn_part, *ffn_got)
    ffn_odd = xor_send(ffn_even, 1)
    attn_part = step(lambda *parts: add_low(*parts)[0], attn_kept, attn_got)
    attn_got = send_chips(attn_part)

    ffn_new = step(
        ffn_update(shard_rows, FF, ctx_count, chunk), place, ffn_even, ffn_odd, ffn_master, ffn_mom, ffn_sq
    )
    attn_even = step(lambda *parts: jnp.stack(parts), attn_part, *attn_got)
    attn_odd = xor_send(attn_even, 1)
    small_total = in_order(attn_even[..., attn_columns:], attn_odd[..., attn_columns:])
    small_total = wide(small_total.reshape(-1))
    most = small_size - FF - HS
    small_total = jnp.concatenate(
        [small_total[:most], small_total[most + HS : most + 2 * HS], small_total[most + 2 * HS : most + 2 * HS + FF]]
    )
    small_new = adam_update(small_master, small_total, small_mom, small_sq, 1.0, 0.0)
    attn_new = attn_update(shard_rows, attn_columns, width, ctx_count, piece_rows)(
        place, attn_even, attn_odd, *in_hbm([attn_master, attn_mom, attn_sq])
    )
    return (layer_out, input_grad) + tuple(attn_new) + tuple(ffn_new) + tuple(small_new)


def shift_wt(array, shift):
    count = lax.axis_size("wt")
    return lax.ppermute(array, "wt", [(i, (i + shift) % count) for i in range(count)])


def whole_wt(piece, axis):
    count, place = lax.axis_size("wt"), lax.axis_index("wt")
    shape = list(piece.shape)
    shape[axis] *= count
    buffer = put(jnp.zeros(shape, piece.dtype), piece, place, axis)
    for shift in range(1, count):
        buffer = put(buffer, shift_wt(piece, shift), (place - shift) % count, axis)
    return buffer


def whole_ctx(piece):
    count = lax.axis_size("ctx")
    got = {0: piece}
    for mask in range(2, count, 2):
        got[mask] = xor_send(piece, mask)
    for mask in range(0, count, 2):
        got[mask + 1] = xor_send(got[mask], 1)
    return [got[mask] for mask in range(count)]


def sum_ctx(pieces):
    count = lax.axis_size("ctx")
    half = {}
    for mask in range(count - 2, -1, -2):
        other = xor_send(pieces[mask + 1], 1)
        half[mask] = low(wide(pieces[mask]) + wide(other))
    total = wide(half[0])
    for mask in range(2, count, 2):
        total = total + wide(xor_send(half[mask], mask))
    return total


def sum_wt(array, axis):
    count, place = lax.axis_size("wt"), lax.axis_index("wt")
    size = array.shape[axis] // count
    total = wide(take(array, place, axis, size))
    for shift in range(1, count):
        sent = take(array, (place + shift) % count, axis, size)
        total = total + wide(shift_wt(sent, shift))
    return total


def any_shards(
    tokens,
    doc_starts,
    attn_master,
    attn_mom,
    attn_sq,
    ffn_master,
    ffn_mom,
    ffn_sq,
    small_master,
    small_mom,
    small_sq,
    cotangent,
):
    ctx_count = lax.axis_size("ctx")
    ctx_place = lax.axis_index("ctx")
    wt_count = lax.axis_size("wt")
    batches, rows_here, width = tokens.shape
    heads = width // HS
    qkv_cols = width + 2 * HS
    all_rows = batches * rows_here
    shard_rows = attn_master.shape[0]
    piece_rows = shard_rows // ctx_count
    chunk = FF // ctx_count
    order = ctx_place ^ jnp.arange(ctx_count, dtype=jnp.int32)
    (
        gain_one,
        shift_one,
        gain_two,
        shift_two,
        bias_query,
        bias_out,
        bias_proj,
        bias_value,
        bias_hidden,
    ) = split_small(small_master)

    attn_piece = low(take(attn_master, ctx_place, 0, piece_rows))

    def whole_rows(piece):
        parts = whole_ctx(whole_wt(piece[None], 0))
        buffer = jnp.zeros((wt_count, ctx_count) + piece.shape, piece.dtype)
        for k, part in enumerate(parts):
            buffer = put(buffer, part[:, None], ctx_place ^ k, 1)
        return buffer.reshape((width,) + piece.shape[1:])

    weight_qkv = whole_rows(attn_piece[:, :qkv_cols])
    weight_out = whole_rows(attn_piece[:, qkv_cols:])
    ffn_piece = low(jnp.swapaxes(take(ffn_master, ctx_place, 2, chunk), 0, 1))
    ffn_parts = whole_ctx(whole_wt(ffn_piece, 1))
    bias_parts = bias_hidden.reshape(ctx_count, chunk)[order]

    stream = wide(tokens.reshape(all_rows, width))
    normed, norm_back_one = jax.vjp(layer_norm, stream, gain_one, shift_one)
    normed_low = low(normed)
    mixed = dot(normed_low, weight_qkv)
    queries = low(mixed[:, :width] + bias_query)
    kv_local = low(
        mixed[:, width:] + jnp.concatenate([jnp.zeros((HS,), jnp.float32), bias_value])
    ).reshape(batches, rows_here, 2 * HS)
    kv_parts = jnp.stack(whole_ctx(kv_local), axis=1).reshape(
        batches, ctx_count * rows_here, 2 * HS
    )
    keys_all, values_all = kv_parts[..., :HS], kv_parts[..., HS:]
    local_pos = jnp.arange(rows_here, dtype=jnp.int32)
    query_pos = ctx_place * rows_here + local_pos
    key_pos = (order[:, None] * rows_here + local_pos[None, :]).reshape(-1)
    queries = queries.reshape(batches, rows_here * heads, HS)
    scale = HS ** (-0.5)
    attended_list, log_list, allowed_list = [], [], []
    for b in range(batches):
        starts = doc_starts[b]
        query_doc = jnp.sum((starts[None, :] <= query_pos[:, None]).astype(jnp.int32), axis=1)
        key_doc = jnp.sum((starts[None, :] <= key_pos[:, None]).astype(jnp.int32), axis=1)
        allowed = (query_doc[:, None] == key_doc[None, :]) & (key_pos[None, :] <= query_pos[:, None])
        allowed = jnp.repeat(allowed, heads, axis=0)
        allowed_list.append(allowed)
        scores = jnp.where(allowed, cols_dot(queries[b], keys_all[b]) * scale, -1e30)
        peak = jnp.max(scores, axis=-1, keepdims=True)
        expo = jnp.exp(scores - peak)
        total = jnp.sum(expo, axis=-1, keepdims=True)
        attended_list.append(dot(low(expo / total), values_all[b]))
        log_list.append(peak + jnp.log(total))
    attended = jnp.stack(attended_list)
    attended_low = low(attended).reshape(all_rows, width)
    hidden = stream + dot(attended_low, weight_out) + bias_out
    normed_two, norm_back_two = jax.vjp(layer_norm, hidden, gain_two, shift_two)
    normed_two_low = low(normed_two)

    back_low = cotangent.reshape(all_rows, width)
    back_rows = wide(back_low)
    down_vals = jnp.zeros((all_rows, width), jnp.float32)
    grad_normed_two = jnp.zeros((all_rows, width), jnp.float32)
    ffn_grads, hidden_grads = [], []
    for k in range(ctx_count):
        weight_up, weight_down = ffn_parts[k][0], ffn_parts[k][1]
        value, slope = gelu_both(dot(normed_two_low, weight_up) + bias_parts[k])
        act = low(value)
        down_vals = down_vals + cols_dot(act, weight_down)
        grad_up = low(dot(back_low, weight_down) * slope)
        hidden_grads.append(jnp.sum(wide(grad_up), axis=0))
        grad_normed_two = grad_normed_two + cols_dot(grad_up, weight_up)
        ffn_grads.append(
            jnp.stack([low(rows_dot(normed_two_low, grad_up)), low(rows_dot(back_low, act))])
        )
    layer_out = low(hidden + down_vals + bias_proj).reshape(batches, rows_here, width)
    grad_bias_proj = jnp.sum(back_rows, axis=0)
    grad_bias_hidden = jnp.stack(hidden_grads)[order].reshape(FF)
    ffn_part = low(sum_wt(low(sum_ctx(ffn_grads)), 1))

    grad_hidden_part, grad_gain_two, grad_shift_two = norm_back_two(grad_normed_two)
    grad_hidden = back_rows + grad_hidden_part
    grad_bias_out = jnp.sum(grad_hidden, axis=0)
    grad_hidden_low = low(grad_hidden)
    grad_out = rows_dot(attended_low, grad_hidden_low)

    def summed_rows(grad):
        blocks = low(grad).reshape(wt_count, ctx_count, piece_rows, grad.shape[1])
        pieces = [take(blocks, ctx_place ^ k, 1, 1)[:, 0] for k in range(ctx_count)]
        part = low(sum_wt(low(sum_ctx(pieces)), 0)[0])
        buffer = jnp.zeros((ctx_count,) + part.shape, part.dtype)
        for k, got in enumerate(whole_ctx(part)):
            buffer = put(buffer, got[None], ctx_place ^ k, 0)
        return wide(buffer.reshape(shard_rows, grad.shape[1]))

    out_total = summed_rows(grad_out)

    grad_attended = low(cols_dot(grad_hidden_low, weight_out)).reshape(
        batches, rows_here * heads, HS
    )
    grad_query_list, grad_kv_list = [], []
    for b in range(batches):
        grads = grad_attended[b]
        delta = jnp.sum(wide(grads) * attended[b], axis=-1, keepdims=True)
        scores = jnp.where(allowed_list[b], cols_dot(queries[b], keys_all[b]) * scale, -1e30)
        weights = jnp.exp(scores - log_list[b])
        grad_scores = low(weights * (cols_dot(grads, values_all[b]) - delta))
        grad_query_list.append(low(dot(grad_scores, keys_all[b]) * scale))
        grad_kv_list.append(
            jnp.concatenate(
                [
                    low(rows_dot(grad_scores, queries[b]) * scale),
                    low(rows_dot(low(weights), grads)),
                ],
                axis=1,
            )
        )
    grad_query = jnp.stack(grad_query_list).reshape(all_rows, width)
    grad_kv = jnp.stack(grad_kv_list).reshape(batches, ctx_count, rows_here, 2 * HS)
    grad_kv_low = low(sum_ctx([grad_kv[:, k] for k in range(ctx_count)])).reshape(
        all_rows, 2 * HS
    )
    grad_bias_query = jnp.sum(wide(grad_query), axis=0)
    grad_bias_value = jnp.sum(wide(grad_kv_low[:, HS:]), axis=0)
    grad_mixed = jnp.concatenate([grad_query, grad_kv_low], axis=1)
    qkv_total = summed_rows(rows_dot(normed_low, grad_mixed))
    grad_normed = cols_dot(grad_mixed, weight_qkv)
    grad_stream_part, grad_gain_one, grad_shift_one = norm_back_one(grad_normed)
    input_grad = (grad_hidden + grad_stream_part).reshape(batches, rows_here, width)

    ffn_buffer = jnp.zeros((ctx_count,) + ffn_part.shape, ffn_part.dtype)
    for k, got in enumerate(whole_ctx(ffn_part)):
        ffn_buffer = put(ffn_buffer, got[None], ctx_place ^ k, 0)
    ffn_total = wide(jnp.transpose(ffn_buffer, (2, 1, 0, 3)).reshape(shard_rows, 2, FF))
    attn_total = jnp.concatenate([qkv_total, out_total], axis=1)
    grad_small = jnp.concatenate(
        [
            grad_gain_one,
            grad_shift_one,
            grad_gain_two,
            grad_shift_two,
            grad_bias_query,
            grad_bias_out,
            grad_bias_proj,
            grad_bias_value,
            grad_bias_hidden,
        ]
    )
    small_total = lax.psum(grad_small, ("ctx", "wt"))
    attn_new = adam_update(attn_master, attn_total, attn_mom, attn_sq, 0.1, 0.1)
    ffn_new = adam_update(ffn_master, ffn_total, ffn_mom, ffn_sq, 0.1, 0.1)
    small_new = adam_update(small_master, small_total, small_mom, small_sq, 1.0, 0.0)
    return (layer_out, input_grad) + attn_new + ffn_new + small_new


def solution(mesh):
    rows, cube = P("wt", None), P("wt", None, None)
    flow = P("wt", "ctx", None)
    in_specs = (flow, rows, rows, rows, rows, cube, cube, cube, P(), P(), P(), flow)
    out_specs = (flow, flow, rows, rows, rows, cube, cube, cube, P(), P(), P())
    ctx_count, wt_count = mesh.shape["ctx"], mesh.shape["wt"]
    fitted = (ctx_count, wt_count) == (8, 4)
    body = shards if fitted else any_shards
    return jax.shard_map(body, mesh=mesh, in_specs=in_specs, out_specs=out_specs, check_vma=False)
```

```python
import jax
import jax.numpy as jnp
from jax import lax
from jax.experimental import pallas as pl
from jax.experimental.pallas import tpu as pltpu
from jax.sharding import PartitionSpec as P

D = 768
HS = 64
FF = 3072
STEP = 10


NORM_EPS = 1e-05
GELU_COEF = 0.7978845608028654
GELU_CUBE = 0.044715
BETA_ONE = 0.9
BETA_TWO = 0.95
ADAM_EPS = 1e-08
VMEM_LIMIT = 22 << 20
NO_COST = pl.CostEstimate(flops=0, bytes_accessed=0, transcendentals=0)


def layer_norm(values, gain, shift):
    centre = values - jnp.mean(values, axis=-1, keepdims=True)
    spread = jnp.mean(centre * centre, axis=-1, keepdims=True)
    return centre * lax.rsqrt(spread + NORM_EPS) * gain + shift


def gelu_both(u):
    square = u * u
    share = 0.5 * jnp.tanh(u * (GELU_COEF * GELU_CUBE * square + GELU_COEF)) + 0.5
    bend = u * (6.0 * GELU_COEF * GELU_CUBE * square + 2.0 * GELU_COEF)
    return u * share, share * ((1.0 - share) * bend) + share


def split_small(small):
    return (
        small[0:D],
        small[D : 2 * D],
        small[2 * D : 3 * D],
        small[3 * D : 4 * D],
        small[4 * D : 5 * D],
        small[5 * D : 6 * D],
        small[6 * D : 7 * D],
        small[7 * D : 7 * D + HS],
        small[7 * D + HS :],
    )


def rows_dot(left, right):
    return lax.dot_general(
        left, right, (((0,), (0,)), ((), ())), preferred_element_type=jnp.float32
    )


def cols_dot(left, right):
    return lax.dot_general(
        left, right, (((1,), (1,)), ((), ())), preferred_element_type=jnp.float32
    )


def dot(left, right):
    return jnp.dot(left, right, preferred_element_type=jnp.float32)


def low(values):
    return values.astype(jnp.bfloat16)


def wide(values):
    return values.astype(jnp.float32)


def adam_update(master, gradient, first, second, step_rate, decay_rate):
    first_new = BETA_ONE * first + (1.0 - BETA_ONE) * gradient
    second_new = BETA_TWO * second + (1.0 - BETA_TWO) * gradient * gradient
    first_hat = first_new / (1.0 - BETA_ONE**STEP)
    second_hat = second_new / (1.0 - BETA_TWO**STEP)
    master_new = master - step_rate * (
        first_hat / (jnp.sqrt(second_hat) + ADAM_EPS) + decay_rate * master
    )
    return (first_new, second_new, master_new)


def xor_send(array, mask):
    count = lax.axis_size("ctx")
    return lax.ppermute(array, "ctx", [(i, i ^ mask) for i in range(count)])


def xor_wt(array, mask):
    count = lax.axis_size("wt")
    return lax.ppermute(array, "wt", [(i, i ^ mask) for i in range(count)])


class Steps:
    def __init__(self):
        self.last = ()

    def __call__(self, function, *args):
        flat, tree = jax.tree.flatten(args)
        held = lax.optimization_barrier(tuple(flat) + self.last)[: len(flat)]
        result = function(*jax.tree.unflatten(tree, held))
        self.last = tuple(jax.tree.leaves(result))
        return result


def loop(count, body, carry=0):
    return lax.fori_loop(0, count, body, carry)


def rows_at(i, size):
    return pl.ds(pl.multiple_of(i * size, size), size)


def together(*arrays):
    return lax.optimization_barrier(arrays)


def put(buffer, piece, place, axis):
    starts = [0] * buffer.ndim
    starts[axis] = place * piece.shape[axis]
    return lax.dynamic_update_slice(buffer, piece, starts)


def take(buffer, place, axis, size):
    return lax.dynamic_slice_in_dim(buffer, place * size, size, axis)


def attention_kernels(batches, rows, width, parts, runs):
    half_parts = parts // 2
    keys = parts * rows
    pair = 2 * HS
    groups = width // (2 * pair)
    factor = HS ** (-0.5) * 1.4426950408889634
    tile = 32

    def lanes(shape):
        return lax.broadcasted_iota(jnp.int32, shape, 1)

    def spread(even_ref, odd_ref, key_ref, value_ref):
        for j in range(parts):
            ref = even_ref if j < half_parts else odd_ref
            block = wide(ref[j % half_parts, 0])
            turned = pltpu.roll(block, HS, 1)
            first = lanes(block.shape) < HS
            here = pl.ds(j * rows, rows)
            key_ref[0, here, :] = low(jnp.where(first, block, 0.0))
            key_ref[1, here, :] = low(jnp.where(first, 0.0, turned))
            value_ref[0, here, :] = low(jnp.where(first, turned, 0.0))
            value_ref[1, here, :] = low(jnp.where(first, 0.0, block))

    def doc_begin(starts_ref, stream, positions):
        begin = jnp.zeros_like(positions)
        for j in range(starts_ref.shape[1]):
            start = starts_ref[stream, j]
            begin = jnp.where(start <= positions, jnp.maximum(begin, start), begin)
        return begin

    def forward(starts_ref, place_ref, query_ref, even_ref, odd_ref, low_ref, full_ref, log_ref, cap, key, value, weight):
        stream, place = pl.program_id(0), place_ref[0]
        spread(even_ref, odd_ref, key, value)
        query_pos = place * rows + lax.broadcasted_iota(jnp.int32, (rows, 1), 0)
        begin = doc_begin(starts_ref, stream, query_pos)
        for j in range(parts):
            key_pos = (place ^ (2 * (j % half_parts) + j // half_parts)) * rows + lax.broadcasted_iota(jnp.int32, (rows, rows), 1)
            allowed = (key_pos >= begin) & (key_pos <= query_pos)
            cap[:, j * rows : (j + 1) * rows] = jnp.where(allowed, 3.0e38, -1e30)
        column = lanes((tile, pair))
        logs = [jnp.zeros((tile, pair), jnp.float32) for _ in range(rows // tile)]
        for g in range(groups):
            at = g * 2 * pair
            two = jnp.concatenate([query_ref[0, :, at : at + pair], query_ref[0, :, at + pair : at + 2 * pair]], axis=0)
            totals = []
            for half in range(2):
                scores = cols_dot(two, key[half])
                norms = []
                for t in range(2 * rows // tile):
                    own = slice(t * tile, (t + 1) * tile)
                    n = t % (rows // tile)
                    part = jnp.minimum(scores[own] * factor, cap[n * tile : (n + 1) * tile, :])
                    peak = jnp.max(part, axis=1, keepdims=True)
                    expo = jnp.exp2(part - peak)
                    norm = jnp.sum(expo, axis=1, keepdims=True)
                    weight[half, own, :] = low(expo)
                    norms.append(norm)
                    head = 4 * g + 2 * (t * tile // rows) + half
                    logs[n] = jnp.where(column == head, peak + jnp.log2(norm), logs[n])
                totals.append(dot(weight[half], value[half]) / jnp.concatenate(norms, axis=0))
            total = totals[0] + totals[1]
            for j in range(2):
                part = total[j * rows : (j + 1) * rows]
                full_ref[0, :, at + j * pair : at + (j + 1) * pair] = part
                low_ref[0, :, at + j * pair : at + (j + 1) * pair] = low(part)
        for n, log in enumerate(logs):
            log_ref[0, n * tile : (n + 1) * tile, :] = log

    def backward(
        starts_ref, place_ref, query_ref, even_ref, odd_ref, full_ref, log_ref, grad_ref,
        query_grad_ref, even_grad_ref, odd_grad_ref,
        cap, key, value, key_turned, log_rows, delta_rows, weight_buf, score_buf, query_buf, grad_buf,
    ):
        stream, place = pl.program_id(0) + place_ref[1], place_ref[0]
        spread(even_ref, odd_ref, key, value)
        query_pos = place * rows + lax.broadcasted_iota(jnp.int32, (1, rows), 1)
        begin = doc_begin(starts_ref, stream, query_pos)
        for j in range(parts):
            key_pos = (place ^ (2 * (j % half_parts) + j // half_parts)) * rows + lax.broadcasted_iota(jnp.int32, (rows, rows), 0)
            allowed = (key_pos >= begin) & (key_pos <= query_pos)
            cap[j * rows : (j + 1) * rows, :] = jnp.where(allowed, 3.0e38, -1e30)
            here = pl.ds(j * rows, rows)
            key_turned[:, j * rows : (j + 1) * rows] = low(wide(key[0, here, :]).T[:HS])
        log_rows[...] = log_ref[0].T[: log_rows.shape[0]]
        head_of = lax.broadcasted_iota(jnp.int32, (delta_rows.shape[0], width), 1) // HS
        chosen = (head_of == lax.broadcasted_iota(jnp.int32, (delta_rows.shape[0], width), 0)).astype(jnp.float32)
        delta_rows[...] = lax.dot_general(
            chosen, wide(grad_ref[0]) * full_ref[0], (((1,), (1,)), ((), ())),
            precision=lax.Precision.HIGHEST, preferred_element_type=jnp.float32,
        )
        first = lanes((2 * rows, pair)) < HS
        for g in range(groups):
            at = g * 2 * pair
            both, both_grad = query_ref[0, :, at : at + 2 * pair], grad_ref[0, :, at : at + 2 * pair]
            two = jnp.concatenate([both[:, :pair], both[:, pair:]], axis=0)
            two_grad = jnp.concatenate([both_grad[:, :pair], both_grad[:, pair:]], axis=0)
            turned = []
            for half in range(2):
                h = 4 * g + half
                span = slice((2 * g + half) * 2 * rows, (2 * g + half + 1) * 2 * rows)
                keep = first if half == 0 else jnp.logical_not(first)
                query_buf[span, :] = low(jnp.where(keep, wide(two), 0.0))
                grad_buf[span, :] = low(jnp.where(keep, wide(two_grad), 0.0))
                log = jnp.concatenate([log_rows[h : h + 1, :], log_rows[h + 2 : h + 3, :]], axis=1)
                delta = jnp.concatenate([delta_rows[h : h + 1, :], delta_rows[h + 2 : h + 3, :]], axis=1)
                scores, weight_grads = cols_dot(key[half], two), cols_dot(value[half], two_grad)
                for t in range(keys // (2 * tile)):
                    own = slice(t * 2 * tile, (t + 1) * 2 * tile)
                    limit = cap[own, :]
                    limit = jnp.concatenate([limit, limit], axis=1)
                    weights = jnp.exp2(jnp.minimum(scores[own] * factor, limit) - log)
                    weight_buf[own, span] = low(weights)
                    score_buf[own, span] = low(weights * (weight_grads[own] - delta))
                turned.append(dot(key_turned[...], score_buf[:, span]))
            turned = jnp.concatenate(turned, axis=0) * HS ** (-0.5)
            query_grad_ref[0, :, at : at + pair] = low(turned[:, :rows].T)
            query_grad_ref[0, :, at + pair : at + 2 * pair] = low(turned[:, rows:].T)
        for j in range(parts):
            here = pl.ds(j * rows, rows)
            value_sum = dot(weight_buf[here, :], grad_buf[...])
            key_sum = dot(score_buf[here, :], query_buf[...]) * HS ** (-0.5)
            value_sum = value_sum + pltpu.roll(value_sum, HS, 1)
            key_sum = key_sum + pltpu.roll(key_sum, HS, 1)
            ref = even_grad_ref if j < half_parts else odd_grad_ref
            ref[j % half_parts, 0] = low(jnp.where(lanes((rows, pair)) < HS, key_sum, value_sum))

    def specs(first):
        return (
            pl.BlockSpec((1, rows, width), lambda b, *_: (b + first, 0, 0)),
            pl.BlockSpec((1, rows, pair), lambda b, *_: (b + first, 0, 0)),
            pl.BlockSpec((half_parts, 1, rows, pair), lambda b, *_: (0, b + first, 0, 0)),
        )

    flow, logs, blocks = specs(0)

    shared = [
        pltpu.VMEM((2, keys, pair), jnp.bfloat16),
        pltpu.VMEM((2, keys, pair), jnp.bfloat16),
    ]
    run_forward = pl.pallas_call(
        forward,
        grid_spec=pltpu.PrefetchScalarGridSpec(
            num_scalar_prefetch=2,
            grid=(batches,),
            in_specs=[flow, blocks, blocks],
            out_specs=[flow, flow, logs],
            scratch_shapes=[pltpu.VMEM((rows, keys), jnp.float32)]
            + shared
            + [pltpu.VMEM((2, 2 * rows, keys), jnp.bfloat16)],
        ),
        out_shape=[
            jax.ShapeDtypeStruct((batches, rows, width), jnp.bfloat16),
            jax.ShapeDtypeStruct((batches, rows, width), jnp.float32),
            jax.ShapeDtypeStruct((batches, rows, pair), jnp.float32),
        ],
        compiler_params=pltpu.CompilerParams(vmem_limit_bytes=VMEM_LIMIT),
        cost_estimate=NO_COST,
        name="attention_forward",
    )
    head_rows = -(-(width // HS) // 8) * 8
    all_columns = rows * (width // HS)
    count = batches // runs

    def call_backward(run):
        here_flow, here_logs, here_blocks = specs(run * count)
        return pl.pallas_call(
        backward,
        grid_spec=pltpu.PrefetchScalarGridSpec(
            num_scalar_prefetch=2,
            grid=(count,),
            in_specs=[here_flow, here_blocks, here_blocks, here_flow, here_logs, here_flow],
            out_specs=[flow, blocks, blocks],
            scratch_shapes=[pltpu.VMEM((keys, rows), jnp.float32)]
            + shared
            + [
                pltpu.VMEM((HS, keys), jnp.bfloat16),
                pltpu.VMEM((head_rows, rows), jnp.float32),
                pltpu.VMEM((head_rows, rows), jnp.float32),
                pltpu.VMEM((keys, all_columns), jnp.bfloat16),
                pltpu.VMEM((keys, all_columns), jnp.bfloat16),
                pltpu.VMEM((all_columns, pair), jnp.bfloat16),
                pltpu.VMEM((all_columns, pair), jnp.bfloat16),
            ],
        ),
        out_shape=[
            jax.ShapeDtypeStruct((count, rows, width), jnp.bfloat16),
            jax.ShapeDtypeStruct((half_parts, count, rows, pair), jnp.bfloat16),
            jax.ShapeDtypeStruct((half_parts, count, rows, pair), jnp.bfloat16),
        ],
        compiler_params=pltpu.CompilerParams(vmem_limit_bytes=VMEM_LIMIT),
        cost_estimate=NO_COST,
        name="attention_backward",
    )

    return run_forward, [call_backward(run) for run in range(runs)]


def in_hbm(arrays):
    return [pltpu.with_memory_space_constraint(array, pltpu.HBM) for array in arrays]


def ffn_kernels(rows, width, chunk, wt_count):
    units = 2 * chunk
    all_rows = 2 * rows
    block_rows = width // wt_count
    hbm = pl.BlockSpec(memory_space=pltpu.HBM)
    vmem = pl.BlockSpec(memory_space=pltpu.VMEM)
    params = pltpu.CompilerParams(vmem_limit_bytes=VMEM_LIMIT)

    def fetch(weights, which, held, sem):
        copies = []
        for n, arrays in enumerate(weights):
            blocks = [array.at[block] for array in arrays for block in range(array.shape[0])]
            for row, block in enumerate(blocks):
                copies.append(
                    pltpu.make_async_copy(
                        block.at[pl.ds(which * block_rows, block_rows), :],
                        held.at[pl.ds(row * block_rows, block_rows), pl.ds(n * chunk, chunk)],
                        sem.at[len(copies)],
                    )
                )
        for copy in copies:
            copy.start()
        return copies

    def send(pairs, sems):
        copies = [pltpu.make_async_copy(source, out, sems.at[n]) for n, (source, out) in enumerate(pairs)]
        for copy in copies:
            copy.start()
        return copies

    part_rows = 256
    tile = 16

    def units_of(inputs, grads, bias, held_up, held_down, act, grad_units):
        sums = jnp.zeros((8, units), jnp.float32)
        for s in range(2):

            def part(i, sums):
                here = rows_at(i, part_rows)
                up = dot(inputs[s][here, :], held_up[...])
                act_grad = dot(grads[s][here, :], held_down[...])
                for t in range(part_rows // tile):
                    own = slice(t * tile, (t + 1) * tile)
                    there = pl.ds(pl.multiple_of(s * rows + i * part_rows + t * tile, tile), tile)
                    value, slope = gelu_both(up[own] + bias)
                    grad = act_grad[own] * slope
                    act[there, :] = low(value)
                    grad_units[there, :] = low(grad)
                    sums = sums + (grad[:8] + grad[8:])
                return sums

            sums = loop(rows // part_rows, part, sums)
        return jnp.sum(sums, axis=0, keepdims=True)

    def product_of(turned, right, product):
        def part(i, carry):
            here = rows_at(i, part_rows)
            product[here, :] = low(dot(turned[here, :], right[...]))
            return carry

        loop(width // part_rows, part)

    def back_to(refs, sources, weights):
        for s, ref in enumerate(refs):

            def part(i, carry):
                here = pl.ds(pl.multiple_of(s * rows + i * part_rows, part_rows), part_rows)
                total = cols_dot(sources[0][here, :], weights[0][...]) + cols_dot(sources[1][here, :], weights[1][...])
                ref[rows_at(i, part_rows), :] = total.astype(ref.dtype)
                return carry

            loop(rows // part_rows, part)

    def halves(product, m):
        cols = pl.ds(m * chunk, chunk)
        return [product.at[pl.ds(h * width // 2, width // 2), cols] for h in range(2)]

    def first(
        own, other, grad_own, grad_other, turned, bias, w0, w1, w2, w3,
        act_out, units_out, out_a, out_b, sums_out,
        held_up, held_down, act, grad_units, product, sems, out_sems,
    ):
        weights = ((w0, w1), (w2, w3))
        copies = fetch(weights, 0, held_up, sems.at[0]) + fetch(weights, 1, held_down, sems.at[1])
        for copy in copies:
            copy.wait()
        sums_out[...] = units_of((own, other), (grad_own, grad_other), bias[...], held_up, held_down, act, grad_units)
        sent = send(((act, act_out), (grad_units, units_out)), out_sems.at[0])
        product_of(turned, act, product)
        sent += send(
            ((product.at[:, pl.ds(0, chunk)], out_a), (product.at[:, pl.ds(chunk, chunk)], out_b)), out_sems.at[1]
        )
        for copy in sent:
            copy.wait()

    def second(
        own, other, grad_own, grad_other, turned, bias, units_first, w0, w1, w2, w3, w4, w5, w6, w7,
        act_out, units_out, out_a, out_b, out_c, sums_out, back_own, back_other,
        held_up, held_more, held_down, act, grad_units, more_units, product, sems, out_sems, more_sem,
    ):
        weights, before = ((w4, w5), (w6, w7)), ((w0, w1), (w2, w3))
        copies = fetch(weights, 0, held_up, sems.at[0]) + fetch(weights, 1, held_down, sems.at[1])
        more = fetch(before, 0, held_more, sems.at[2])
        more.append(pltpu.make_async_copy(units_first, more_units, more_sem))
        more[-1].start()
        for copy in copies:
            copy.wait()
        sums_out[...] = units_of((own, other), (grad_own, grad_other), bias[...], held_up, held_down, act, grad_units)
        sent = send(((act, act_out), (grad_units, units_out)), out_sems.at[0])
        product_of(turned, act, product)
        top, bottom = halves(product, 1)
        sent += send(((product.at[:, pl.ds(0, chunk)], out_a), (top, out_b), (bottom, out_c)), out_sems.at[1])
        for copy in more:
            copy.wait()
        back_to((back_own, back_other), (grad_units, more_units), (held_up, held_more))
        for copy in sent:
            copy.wait()

    def third(own, other, units_a, units_b, out_0, out_1, out_2, out_3, out_4, turned, held, products, sems, out_sems):
        copies = send(((units_a, held.at[0]), (units_b, held.at[1])), sems)
        turn((own, other), turned)
        for copy in copies:
            copy.wait()
        products[1] = low(dot(turned[...], held[1]))
        top, bottom = halves(products.at[1], 1)
        sent = send(((products.at[1, :, pl.ds(0, chunk)], out_2), (top, out_3), (bottom, out_4)), out_sems.at[0])
        products[0] = low(dot(turned[...], held[0]))
        sent += send(
            ((products.at[0, :, pl.ds(0, chunk)], out_0), (products.at[0, :, pl.ds(chunk, chunk)], out_1)),
            out_sems.at[1],
        )
        for copy in sent:
            copy.wait()

    def down(act_a, act_b, w0, w1, w2, w3, w4, w5, w6, w7, own_ref, other_ref, held_a, held_b, sems):
        copies = fetch(((w0, w1), (w2, w3)), 1, held_a, sems.at[0]) + fetch(((w4, w5), (w6, w7)), 1, held_b, sems.at[1])
        for copy in copies:
            copy.wait()
        for s, ref in enumerate((own_ref, other_ref)):
            here = slice(s * rows, (s + 1) * rows)
            total = cols_dot(act_a[here, :], held_a[...]) + cols_dot(act_b[here, :], held_b[...])
            ref[...] = total.astype(ref.dtype)

    dma = pltpu.SemaphoreType.DMA
    held = pltpu.VMEM((width, units), jnp.bfloat16)
    flow = pltpu.VMEM((all_rows, units), jnp.bfloat16)
    flow_out = pltpu.HBM((all_rows, units), jnp.bfloat16)
    whole = pltpu.HBM((width, chunk), jnp.bfloat16)
    part = pltpu.HBM((width // 2, chunk), jnp.bfloat16)
    sums = jax.ShapeDtypeStruct((1, units), jnp.float32)
    own = jax.ShapeDtypeStruct((rows, width), jnp.float32)
    other = jax.ShapeDtypeStruct((rows, width), jnp.bfloat16)
    run_first = pl.pallas_call(
        first,
        in_specs=[vmem] * 6 + [hbm] * 4,
        out_specs=[hbm] * 4 + [vmem],
        out_shape=[flow_out, flow_out, whole, whole, sums],
        scratch_shapes=[held, held, flow, flow, held, dma((2, 2 * wt_count)), dma((2, 2))],
        compiler_params=params,
        cost_estimate=NO_COST,
        name="ffn_first",
    )
    run_second = pl.pallas_call(
        second,
        in_specs=[vmem] * 6 + [hbm] * 9,
        out_specs=[hbm] * 5 + [vmem] * 3,
        out_shape=[flow_out, flow_out, whole, part, part, sums, own, other],
        scratch_shapes=[held, held, held, flow, flow, flow, held, dma((3, 2 * wt_count)), dma((2, 3)), dma(())],
        compiler_params=params,
        cost_estimate=NO_COST,
        name="ffn_second",
    )
    run_third = pl.pallas_call(
        third,
        in_specs=[vmem] * 2 + [hbm] * 2,
        out_specs=[hbm] * 5,
        out_shape=[whole, whole, whole, part, part],
        scratch_shapes=[
            pltpu.VMEM((width, all_rows), jnp.bfloat16),
            pltpu.VMEM((2, all_rows, units), jnp.bfloat16),
            pltpu.VMEM((2, width, units), jnp.bfloat16),
            dma((2,)),
            dma((2, 3)),
        ],
        compiler_params=params,
        cost_estimate=NO_COST,
        name="ffn_grads",
    )
    run_down = pl.pallas_call(
        down,
        in_specs=[vmem] * 2 + [hbm] * 8,
        out_specs=[vmem] * 2,
        out_shape=[own, other],
        scratch_shapes=[held, held, dma((2, 2 * wt_count))],
        compiler_params=params,
        cost_estimate=NO_COST,
        name="ffn_down",
    )
    return run_first, run_second, run_third, run_down


def turn(refs, turned):
    rows = refs[0].shape[0]
    for s, ref in enumerate(refs):
        for i in range(rows // 128):
            block = wide(ref[i * 128 : (i + 1) * 128, :])
            turned[:, s * rows + i * 128 : s * rows + (i + 1) * 128] = low(block.T)


def turn_both(own, other):
    vmem = pl.BlockSpec(memory_space=pltpu.VMEM)
    rows, width = own.shape
    return pl.pallas_call(
        lambda a, b, out: turn((a, b), out),
        in_specs=[vmem] * 2,
        out_specs=vmem,
        out_shape=jax.ShapeDtypeStruct((width, 2 * rows), own.dtype),
        compiler_params=pltpu.CompilerParams(vmem_limit_bytes=VMEM_LIMIT),
        cost_estimate=NO_COST,
        name="turn",
    )(own, other)


def out_projection(rows, width):
    tile = 32

    def kernel(attended, weight, stream, bias, gain, shift, hidden_ref, normed_ref):
        product = dot(attended[...], weight[...])
        for t in range(rows // tile):
            here = slice(t * tile, (t + 1) * tile)
            hidden = wide(stream[here, :]) + product[here] + bias[...]
            hidden_ref[here, :] = hidden
            normed_ref[here, :] = low(layer_norm(hidden, gain[...], shift[...]))

    vmem = pl.BlockSpec(memory_space=pltpu.VMEM)
    return pl.pallas_call(
        kernel,
        in_specs=[vmem] * 6,
        out_specs=[vmem] * 2,
        out_shape=[
            jax.ShapeDtypeStruct((rows, width), jnp.float32),
            jax.ShapeDtypeStruct((rows, width), jnp.bfloat16),
        ],
        compiler_params=pltpu.CompilerParams(vmem_limit_bytes=VMEM_LIMIT),
        cost_estimate=NO_COST,
        name="out_projection",
    )


def norm_back(values, gain, grad):
    centre = values - jnp.mean(values, axis=-1, keepdims=True)
    scale = lax.rsqrt(jnp.mean(centre * centre, axis=-1, keepdims=True) + NORM_EPS)
    unit = centre * scale
    inner = grad * gain
    mean = jnp.mean(inner, axis=-1, keepdims=True)
    along = jnp.mean(inner * unit, axis=-1, keepdims=True)
    return scale * (inner - mean - unit * along), grad * unit


def fold_rows(values):
    total = values[:8]
    for i in range(1, values.shape[0] // 8):
        total = total + values[i * 8 : (i + 1) * 8]
    return total


def hidden_back(rows, width):
    tile = 32

    def kernel(own, got, hidden, back, gain, weight, grad_ref, low_ref, attended_ref, sums_ref):
        sums = [jnp.zeros((8, width), jnp.float32) for _ in range(3)]
        for t in range(rows // tile):
            here = slice(t * tile, (t + 1) * tile)
            pulled, terms = norm_back(hidden[here, :], gain[...], own[here, :] + wide(got[here, :]))
            grad = wide(back[here, :]) + pulled
            grad_ref[here, :] = grad
            low_ref[here, :] = low(grad)
            for n, part in enumerate((terms, own[here, :] + wide(got[here, :]), grad)):
                sums[n] = sums[n] + fold_rows(part)
        for n in range(3):
            sums_ref[n : n + 1, :] = jnp.sum(sums[n], axis=0, keepdims=True)
        attended_ref[...] = low(cols_dot(low_ref[...], weight[...]))

    vmem = pl.BlockSpec(memory_space=pltpu.VMEM)
    return pl.pallas_call(
        kernel,
        in_specs=[vmem] * 6,
        out_specs=[vmem] * 4,
        out_shape=[
            jax.ShapeDtypeStruct((rows, width), jnp.float32),
            jax.ShapeDtypeStruct((rows, width), jnp.bfloat16),
            jax.ShapeDtypeStruct((rows, width), jnp.bfloat16),
            jax.ShapeDtypeStruct((3, width), jnp.float32),
        ],
        compiler_params=pltpu.CompilerParams(vmem_limit_bytes=VMEM_LIMIT),
        cost_estimate=NO_COST,
        name="hidden_back",
    )


def stream_back(rows, width, parts, row_groups, piece):
    tile = 32
    chips = parts // 2

    def kernel(
        place_ref, kv_0, kv_1, kv_2, kv_3, queries, weight, tokens, gain, grad_hidden, normed, back, hidden_sums,
        units_a, units_b, input_ref, even_ref, odd_ref, grad_kv, grads, turned, product, small,
    ):
        place = place_ref[0]
        sums = [jnp.zeros((8, width), jnp.float32) for _ in range(4)]
        value_sums = jnp.zeros((8, 2 * HS), jnp.float32)
        for t in range(rows // tile):
            here = slice(t * tile, (t + 1) * tile)
            total = wide(kv_0[here, :]) + wide(kv_1[here, :]) + wide(kv_2[here, :]) + wide(kv_3[here, :])
            grad_kv[here, :] = low(total)
            value_sums = value_sums + fold_rows(total)
        turn((normed,), turned)
        product[...] = dot(turned[...], grad_kv[...])
        grads[...] = cols_dot(queries[...], weight[:, :width]) + cols_dot(grad_kv[...], weight[:, width:])
        for t in range(rows // tile):
            here = slice(t * tile, (t + 1) * tile)
            grad = grads[here, :]
            pulled, terms = norm_back(wide(tokens[here, :]), gain[...], grad)
            input_ref[here, :] = grad_hidden[here, :] + pulled
            for n, part in enumerate((terms, grad, wide(queries[here, :]), wide(back[here, :]))):
                sums[n] = sums[n] + fold_rows(part)
        sums = [jnp.sum(part, axis=0, keepdims=True) for part in sums]
        small[...] = jnp.zeros_like(small)
        rows_in = (sums[0], sums[1], hidden_sums[0:1, :], hidden_sums[1:2, :], sums[2], hidden_sums[2:3, :], sums[3])
        for n, row in enumerate(rows_in):
            for j in range(width // 128):
                line = n * (width // 128) + j
                small[line : line + 1, :] = row[:, j * 128 : (j + 1) * 128]
        start = 7 * (width // 128)
        small[start : start + 1, :] = jnp.sum(value_sums, axis=0, keepdims=True)
        lines = FF // parts // 128
        for m in range(chips):
            units = (units_a, units_b)[m // 2]
            for j in range(lines):
                line = start + 1 + (place ^ (2 * m)) * lines + j
                at = (m % 2 * lines + j) * 128
                small[pl.ds(line, 1), :] = units[:, at : at + 128]
        for k in range(parts):
            ref = odd_ref if k % 2 else even_ref
            mine = low(small[pl.ds(pl.multiple_of((place ^ k) * piece, 8), piece), :])
            for w in range(row_groups):
                at = pl.multiple_of(w * piece * parts + (place ^ k) * piece, 8)
                ref[k // 2, w, :, :128] = low(product[pl.ds(at, piece), :])
                ref[k // 2, w, :, 128:] = mine

    vmem = pl.BlockSpec(memory_space=pltpu.VMEM)
    stack = jax.ShapeDtypeStruct((chips, row_groups, piece, 256), jnp.bfloat16)
    return pl.pallas_call(
        kernel,
        in_specs=[pl.BlockSpec(memory_space=pltpu.SMEM)] + [vmem] * 14,
        out_specs=[vmem] * 3,
        out_shape=[jax.ShapeDtypeStruct((rows, width), jnp.float32), stack, stack],
        scratch_shapes=[
            pltpu.VMEM((rows, 2 * HS), jnp.bfloat16),
            pltpu.VMEM((rows, width), jnp.float32),
            pltpu.VMEM((width, rows), jnp.bfloat16),
            pltpu.VMEM((width, 2 * HS), jnp.float32),
            pltpu.VMEM((parts * piece, 128), jnp.float32),
        ],
        compiler_params=pltpu.CompilerParams(vmem_limit_bytes=VMEM_LIMIT),
        cost_estimate=NO_COST,
        name="stream_back",
    )


def attn_grads(rows, width, row_groups, parts, piece):
    def kernel(place_ref, left_a, right_a, left_b, right_b, even_ref, odd_ref, turned, total):
        place = place_ref[0]
        for n, (left, right) in enumerate(((left_a, right_a), (left_b, right_b))):
            for i in range(rows // 128):
                turned[:, i * 128 : (i + 1) * 128] = low(wide(left[i * 128 : (i + 1) * 128, :]).T)
            total[:, n * width : (n + 1) * width] = dot(turned[...], right[...])
        for k in range(parts):
            ref = odd_ref if k % 2 else even_ref
            for w in range(row_groups):
                at = pl.multiple_of(w * piece * parts + (place ^ k) * piece, 8)
                ref[k // 2, w] = low(total[pl.ds(at, piece), :])

    vmem = pl.BlockSpec(memory_space=pltpu.VMEM)
    shape = jax.ShapeDtypeStruct((parts // 2, row_groups, piece, 2 * width), jnp.bfloat16)
    return pl.pallas_call(
        kernel,
        grid_spec=pltpu.PrefetchScalarGridSpec(
            num_scalar_prefetch=1,
            grid=(),
            in_specs=[vmem] * 4,
            out_specs=[vmem] * 2,
            scratch_shapes=[pltpu.VMEM((width, rows), jnp.bfloat16), pltpu.VMEM((width, 2 * width), jnp.float32)],
        ),
        out_shape=[shape] * 2,
        compiler_params=pltpu.CompilerParams(vmem_limit_bytes=VMEM_LIMIT),
        cost_estimate=NO_COST,
        name="attn_grads",
    )


def attn_update(rows, columns, width, parts, piece):
    qkv = columns - width

    def kernel(place_ref, even_ref, odd_ref, master, first, second, *outs):
        place = place_ref[0]
        for k in range(parts):
            ref = odd_ref if k % 2 else even_ref
            here = pl.ds(pl.multiple_of((place ^ k) * piece, 8), piece)
            for cols, source in (
                (slice(0, width), slice(0, width)),
                (slice(width, qkv), slice(2 * width, columns)),
                (slice(qkv, columns), slice(width, 2 * width)),
            ):
                grad = wide(ref[k // 2, :, source])
                got = adam_update(master[here, cols], grad, first[here, cols], second[here, cols], 0.1, 0.1)
                outs[0][here, cols] = got[0]
                outs[1][here, cols] = got[1]
                outs[2][here, cols] = got[2]

    vmem = pl.BlockSpec(memory_space=pltpu.VMEM)
    return pl.pallas_call(
        kernel,
        grid_spec=pltpu.PrefetchScalarGridSpec(
            num_scalar_prefetch=1, grid=(), in_specs=[vmem] * 5, out_specs=[vmem] * 3, scratch_shapes=[]
        ),
        out_shape=[jax.ShapeDtypeStruct((rows, columns), jnp.float32)] * 3,
        compiler_params=pltpu.CompilerParams(vmem_limit_bytes=VMEM_LIMIT),
        cost_estimate=NO_COST,
        name="attn_update",
    )


def ffn_update(rows, units, parts, chunk):
    per_row = 2 * units // 128
    rows_once = 32
    lines = rows_once * per_row

    def kernel(place_ref, even, odd, master, first, second, first_out, second_out, master_out, total):
        place = place_ref[0]
        for k in range(parts):
            grad = odd if k % 2 else even
            for j in range(chunk // 128):
                for which in range(2):
                    line = (place ^ k) * (2 * chunk // 128) + 2 * j + which
                    total[pl.ds(line, rows_once, per_row), :] = wide(
                        grad[k // 2, which, :, j * 128 : (j + 1) * 128]
                    )
        for t in range(lines // 64):
            own = slice(t * 64, (t + 1) * 64)
            got = adam_update(master[own, :], total[own, :], first[own, :], second[own, :], 0.1, 0.1)
            first_out[own, :] = got[0]
            second_out[own, :] = got[1]
            master_out[own, :] = got[2]

    block = pl.BlockSpec((lines, 128), lambda i, *_: (i, 0))
    stack = pl.BlockSpec((parts // 2, 2, rows_once, chunk), lambda i, *_: (0, 0, i, 0))
    call = pl.pallas_call(
        kernel,
        grid_spec=pltpu.PrefetchScalarGridSpec(
            num_scalar_prefetch=1,
            grid=(rows // rows_once,),
            in_specs=[stack] * 2 + [block] * 3,
            out_specs=[block] * 3,
            scratch_shapes=[pltpu.VMEM((lines, 128), jnp.float32)],
        ),
        out_shape=[jax.ShapeDtypeStruct((rows * per_row, 128), jnp.float32)] * 3,
        compiler_params=pltpu.CompilerParams(vmem_limit_bytes=VMEM_LIMIT),
        cost_estimate=NO_COST,
        name="ffn_update",
    )

    def fold(array):
        return jnp.swapaxes(array.reshape(rows, 2, units // 128, 128), 1, 2).reshape(-1, 128)

    def unfold(array):
        return jnp.swapaxes(array.reshape(rows, units // 128, 2, 128), 1, 2).reshape(rows, 2, units)

    def run(place, even, odd, master, first, second):
        return tuple(unfold(array) for array in call(place, even, odd, fold(master), fold(first), fold(second)))

    return run


def shards(
    tokens,
    doc_starts,
    attn_master,
    attn_mom,
    attn_sq,
    ffn_master,
    ffn_mom,
    ffn_sq,
    small_master,
    small_mom,
    small_sq,
    cotangent,
):
    ctx_count, wt_count = lax.axis_size("ctx"), lax.axis_size("wt")
    ctx_place, wt_place = lax.axis_index("ctx"), lax.axis_index("wt")
    batches, rows_here, width = tokens.shape
    qkv_cols = width + 2 * HS
    attn_columns = attn_master.shape[1]
    all_rows = batches * rows_here
    shard_rows = attn_master.shape[0]
    piece_rows = shard_rows // ctx_count
    chunk = FF // ctx_count
    chips = ctx_count // 2
    order = ctx_place ^ jnp.arange(ctx_count, dtype=jnp.int32)
    (
        gain_one,
        shift_one,
        gain_two,
        shift_two,
        bias_query,
        bias_out,
        bias_proj,
        bias_value,
        bias_hidden,
    ) = split_small(small_master)
    runs = 2 if batches % 2 == 0 else 1
    places = [jnp.stack([ctx_place, jnp.int32(run * (batches // runs))]) for run in range(runs)]
    place = places[0]
    wt_half = wt_count // 2
    out_rows = shard_rows // chips
    run_forward, run_backward = attention_kernels(batches, rows_here, width, ctx_count, runs)
    ffn_first, ffn_second, ffn_third, ffn_down = ffn_kernels(all_rows, width, chunk, wt_count)
    step = Steps()

    def both(own, got, place, bit, axis=0):
        ahead, behind = jnp.stack([own, got], axis), jnp.stack([got, own], axis)
        return jnp.where((place & bit) == 0, ahead, behind)

    def in_order(even, odd):
        buffer = jnp.zeros((ctx_count,) + even.shape[1:], even.dtype)
        for m in range(chips):
            buffer = put(buffer, even[m][None], ctx_place ^ (2 * m), 0)
            buffer = put(buffer, odd[m][None], ctx_place ^ (2 * m + 1), 0)
        return buffer

    def send_chips(piece):
        return [xor_send(piece, mask) for mask in range(2, ctx_count, 2)]

    def split_wt(total, bit):
        ahead, behind = jnp.split(total, 2)
        kept, sent = jnp.where((wt_place & bit) == 0, ahead, behind), jnp.where((wt_place & bit) == 0, behind, ahead)
        return kept, sent

    def add_low(*arrays):
        return low(sum(wide(array) for array in arrays))

    qkv = low(lax.dynamic_slice(attn_master, (ctx_place * piece_rows, 0), (piece_rows, qkv_cols)))
    qkv_got = xor_wt(qkv, 1)
    qkv = both(qkv, qkv_got, wt_place, 1)
    qkv_got = xor_wt(qkv, 2)
    rest = low(jnp.swapaxes(take(ffn_master, ctx_place, 2, chunk), 0, 1).reshape(2 * shard_rows, chunk))
    out = low(
        lax.dynamic_slice(
            attn_master, (ctx_place // 2 * out_rows, qkv_cols + ctx_place % 2 * chunk), (out_rows, chunk)
        )
    )
    qkv_got, rest, out = together(qkv_got, rest, out)
    rest_got, out_got = xor_wt(rest, 1), xor_wt(out, 1)
    flat_tokens = tokens.reshape(all_rows, width)
    qkv = both(qkv, qkv_got, wt_place, 2).reshape((wt_count,) + qkv.shape[1:])
    qkv_got = send_chips(qkv)
    flat_tokens, qkv = together(flat_tokens, qkv)
    normed_low = low(layer_norm(wide(flat_tokens), gain_one, shift_one))
    bias_parts = bias_hidden.reshape(ctx_count, chunk)[order[::2]].reshape(1, chips * chunk)
    bias_near, bias_far = jnp.split(bias_parts, 2, axis=1)
    *qkv_got, rest_got, out_got, normed_low, bias_near, bias_far = together(
        *qkv_got, rest_got, out_got, normed_low, bias_near, bias_far
    )
    qkv_even = jnp.stack([qkv] + qkv_got)
    out = both(out, out_got, wt_place, 1)
    qkv_even, out = together(qkv_even, out)
    qkv_odd, out_got = xor_send(qkv_even, 1), xor_wt(out, 2)
    ups, downs = [both(rest[rows], rest_got[rows], wt_place, 1) for rows in (slice(shard_rows), slice(shard_rows, None))]
    back_low, ups = together(cotangent.reshape(all_rows, width), ups)
    back_other = xor_send(back_low, 1)
    ups_got = xor_wt(ups, 2)
    qkv_odd, out_got, ups, downs = together(qkv_odd, out_got, ups, downs)
    out = both(out, out_got, wt_place, 2).reshape((wt_count,) + out.shape[1:])
    out_got = send_chips(out)
    blocks = both(qkv_even, qkv_odd, ctx_place, 1, 1)
    for n in range(chips.bit_length() - 1):
        pairs = blocks.reshape((-1, 2, 1 << n) + blocks.shape[1:])
        blocks = jnp.where((ctx_place & (2 << n)) == 0, pairs, pairs[:, ::-1]).reshape(blocks.shape)
    weight_qkv = jnp.transpose(blocks, (2, 0, 1, 3, 4)).reshape(width, qkv_cols)
    mixed = dot(normed_low, weight_qkv)
    queries = low(mixed[:, :width] + bias_query).reshape(batches, rows_here, width)
    kv_bias = jnp.concatenate([jnp.zeros((HS,), jnp.float32), bias_value])
    kv_local = low(mixed[:, width:] + kv_bias).reshape(batches, rows_here, 2 * HS)
    back_turned = turn_both(back_low, back_other)
    kv_local, ups_got, downs, back_turned, *out_got = together(kv_local, ups_got, downs, back_turned, *out_got)
    downs_got = xor_wt(downs, 2)
    kv_got = send_chips(kv_local)
    out_even = jnp.stack([out] + out_got)
    *kv_got, out_even = together(*kv_got, out_even)
    out_odd = xor_send(out_even, 1)
    kv_even = jnp.stack([kv_local] + kv_got)
    kv_odd = xor_send(kv_even, 1)
    kv_even, ups_got, downs_got = together(kv_even, ups_got, downs_got)
    own, got = jnp.concatenate([ups, downs], axis=1), jnp.concatenate([ups_got, downs_got], axis=1)
    first_half = (wt_place & 2) == 0
    rest_low, rest_high = jnp.where(first_half, own, got), jnp.where(first_half, got, own)
    low_x, high_y, high_x, low_y = xor_send(rest_low, 2), xor_send(rest_high, 4), xor_send(rest_high, 2), xor_send(rest_low, 4)
    queries, rest_low, rest_high = together(queries, rest_low, rest_high)

    attended_low, attended, logs = step(run_forward, doc_starts, place, queries, kv_even, kv_odd)
    attended_low = attended_low.reshape(all_rows, width)
    attended_low, low_x, high_y, high_x, low_y = together(attended_low, low_x, high_y, high_x, low_y)
    low_diagonal, high_diagonal = xor_send(low_x, 4), xor_send(high_y, 2)

    def join_out(even, odd):
        columns = jnp.where((ctx_place & 1) == 0, jnp.concatenate([even, odd], axis=3), jnp.concatenate([odd, even], axis=3))
        for n in range(chips.bit_length() - 1):
            pairs = columns.reshape((-1, 2, 1 << n) + columns.shape[1:])
            columns = jnp.where((ctx_place & (2 << n)) == 0, pairs, pairs[:, ::-1]).reshape(columns.shape)
        return jnp.swapaxes(columns, 0, 1).reshape(width, width)

    weight_out = step(join_out, out_even, out_odd)
    hidden, normed_two = step(
        out_projection(all_rows, width), attended_low, weight_out, flat_tokens, bias_out[None], gain_two[None],
        shift_two[None],
    )
    normed_other = xor_send(normed_two, 1)

    weights = [rest_low, rest_high, low_x, high_x, low_y, high_y, low_diagonal, high_diagonal]
    flows = (normed_two, normed_other, back_low, back_other, back_turned)
    act_first, units_first, down_own, down_x, sums_first = step(
        lambda *args: ffn_first(*args[:6], *in_hbm(args[6:])), *flows, bias_near, *weights[:4]
    )
    act_second, units_second, down_y, down_top, down_bottom, sums_second, back_own, back_part = step(
        lambda *args: ffn_second(*args[:6], *in_hbm(args[6:])), *flows, bias_far, units_first, *weights
    )
    back_got = xor_send(back_part, 1)
    top_got, bottom_got = xor_send(down_top, 4), xor_send(down_bottom, 2)

    def meet(along_x, along_y, top, bottom):
        half = width // 2
        return (
            jnp.concatenate([add_low(along_x[:half], top), along_x[half:]]),
            jnp.concatenate([along_y[:half], add_low(along_y[half:], bottom)]),
        )

    up_own, up_x, up_y, up_top, up_bottom = step(
        lambda *args: ffn_third(*args[:2], *in_hbm(args[2:])), normed_two, normed_other, units_first, units_second
    )
    down_x, down_y = step(meet, down_x, down_y, top_got, bottom_got)
    down_got = [xor_send(down_x, 2), xor_send(down_y, 4)]
    top_got, bottom_got = xor_send(up_top, 4), xor_send(up_bottom, 2)

    grad_hidden, grad_hidden_low, grad_attended, hidden_sums = step(
        hidden_back(all_rows, width), back_own, back_got, hidden, back_low, gain_two[None], weight_out
    )
    grad_attended = grad_attended.reshape(batches, rows_here, width)
    def by_wt(*arrays):
        return split_wt(add_low(*arrays).reshape(wt_count, shard_rows, chunk), 2)

    def next_wt(kept, got):
        return split_wt(add_low(kept, got), 1)

    def kv_pieces(evens, odds):
        total = jnp.concatenate([add_low(a, b) for a, b in zip(evens, odds)], axis=1)
        return [total[m] for m in range(chips)]

    backs = [step(run_backward[0], doc_starts, places[0], queries, kv_even, kv_odd, attended, logs, grad_attended)]
    kv_got = [xor_send(backs[0][2], 1)]
    down_kept, down_sent = step(by_wt, down_own, *down_got)
    up_x, up_y = step(meet, up_x, up_y, top_got, bottom_got)
    grad_attended, down_kept, down_sent, up_x, up_y = together(grad_attended, down_kept, down_sent, up_x, up_y)
    down_got = xor_wt(down_sent, 2)
    up_got = [xor_send(up_x, 2), xor_send(up_y, 4)]
    backs += [
        step(run_backward[run], doc_starts, places[run], queries, kv_even, kv_odd, attended, logs, grad_attended)
        for run in range(1, runs)
    ]
    backs[-1] = list(backs[-1])
    *backs[-1], down_got, up_got[0], up_got[1] = together(*backs[-1], down_got, *up_got)
    kv_got += [xor_send(back[2], 1) for back in backs[1:]]
    grad_queries = [back[0] for back in backs]
    grad_query = jnp.concatenate(grad_queries).reshape(all_rows, width)
    down_kept, down_sent = next_wt(down_kept, down_got)
    up_kept, up_sent = by_wt(up_own, *up_got)
    down_kept, down_sent, up_kept, up_sent = together(down_kept, down_sent, up_kept, up_sent)
    down_got, up_got = xor_wt(down_sent, 1), xor_wt(up_sent, 2)
    kv_half = step(kv_pieces, [back[1] for back in backs], kv_got)
    kv_got = [xor_send(kv_half[m], 2 * m) for m in range(1, chips)]
    wide_even, wide_odd = step(
        attn_grads(all_rows, width, wt_count, ctx_count, piece_rows),
        place, normed_low, grad_query, attended_low, grad_hidden_low,
    )
    small_size = small_master.shape[0]
    up_kept, up_sent = step(next_wt, up_kept, up_got)
    kv_got[0], up_kept, up_sent = together(kv_got[0], up_kept, up_sent)
    up_got = xor_wt(up_sent, 1)
    input_grad, tail_even, tail_odd = step(
        stream_back(all_rows, width, ctx_count, wt_count, piece_rows),
        place, *[array.reshape(all_rows, 2 * HS) for array in (kv_half[0], *kv_got)], grad_query, weight_qkv,
        flat_tokens, gain_one[None], grad_hidden, normed_low, back_low, hidden_sums, sums_first, sums_second,
    )
    input_grad = input_grad.reshape(batches, rows_here, width)
    wide_odd, tail_odd = lax.optimization_barrier((wide_odd, tail_odd))
    wide_odd, tail_odd = xor_send(wide_odd, 1), xor_send(tail_odd, 1)
    def attn_pieces(wide_even, wide_odd, tail_even, tail_odd):
        total = jnp.concatenate([add_low(wide_even, wide_odd), add_low(tail_even, tail_odd)], axis=3)
        return [total[m] for m in range(chips)]

    attn_half = step(attn_pieces, wide_even, wide_odd, tail_even, tail_odd)
    attn_got = [xor_send(attn_half[m], 2 * m) for m in range(1, chips)]
    ffn_part = step(
        lambda *arrays: jnp.concatenate([add_low(*arrays[:2]), add_low(*arrays[2:])]), up_kept, up_got, down_kept, down_got
    )
    ffn_got = send_chips(ffn_part)
    down_out, down_other = step(
        lambda *args: ffn_down(*args[:2], *in_hbm(args[2:])), act_first, act_second, *weights
    )
    down_other = xor_send(down_other, 1)
    attn_kept, attn_sent = step(lambda *parts: split_wt(add_low(*parts), 2), attn_half[0], *attn_got)
    attn_got = xor_wt(attn_sent, 2)
    layer_out = step(
        lambda hidden, own, got: low(hidden + own + wide(got) + bias_proj).reshape(batches, rows_here, width),
        hidden, down_out, down_other,
    )
    attn_kept, attn_sent = step(lambda kept, got: split_wt(add_low(kept, got), 1), attn_kept, attn_got)
    attn_got = xor_wt(attn_sent, 1)
    ffn_even = step(lambda *parts: jnp.stack(parts), ffn_part, *ffn_got)
    ffn_odd = xor_send(ffn_even, 1)
    attn_part = step(lambda *parts: add_low(*parts)[0], attn_kept, attn_got)
    attn_got = send_chips(attn_part)

    ffn_new = step(
        ffn_update(shard_rows, FF, ctx_count, chunk), place, ffn_even, ffn_odd, ffn_master, ffn_mom, ffn_sq
    )
    attn_even = step(lambda *parts: jnp.stack(parts), attn_part, *attn_got)
    attn_odd = xor_send(attn_even, 1)
    small_total = in_order(attn_even[..., attn_columns:], attn_odd[..., attn_columns:])
    small_total = wide(small_total.reshape(-1))
    most = small_size - FF - HS
    small_total = jnp.concatenate(
        [small_total[:most], small_total[most + HS : most + 2 * HS], small_total[most + 2 * HS : most + 2 * HS + FF]]
    )
    small_new = adam_update(small_master, small_total, small_mom, small_sq, 1.0, 0.0)
    attn_new = attn_update(shard_rows, attn_columns, width, ctx_count, piece_rows)(
        place, attn_even, attn_odd, *in_hbm([attn_master, attn_mom, attn_sq])
    )
    return (layer_out, input_grad) + tuple(attn_new) + tuple(ffn_new) + tuple(small_new)


def shift_wt(array, shift):
    count = lax.axis_size("wt")
    return lax.ppermute(array, "wt", [(i, (i + shift) % count) for i in range(count)])


def whole_wt(piece, axis):
    count, place = lax.axis_size("wt"), lax.axis_index("wt")
    shape = list(piece.shape)
    shape[axis] *= count
    buffer = put(jnp.zeros(shape, piece.dtype), piece, place, axis)
    for shift in range(1, count):
        buffer = put(buffer, shift_wt(piece, shift), (place - shift) % count, axis)
    return buffer


def whole_ctx(piece):
    count = lax.axis_size("ctx")
    got = {0: piece}
    for mask in range(2, count, 2):
        got[mask] = xor_send(piece, mask)
    for mask in range(0, count, 2):
        got[mask + 1] = xor_send(got[mask], 1)
    return [got[mask] for mask in range(count)]


def sum_ctx(pieces):
    count = lax.axis_size("ctx")
    half = {}
    for mask in range(count - 2, -1, -2):
        other = xor_send(pieces[mask + 1], 1)
        half[mask] = low(wide(pieces[mask]) + wide(other))
    total = wide(half[0])
    for mask in range(2, count, 2):
        total = total + wide(xor_send(half[mask], mask))
    return total


def sum_wt(array, axis):
    count, place = lax.axis_size("wt"), lax.axis_index("wt")
    size = array.shape[axis] // count
    total = wide(take(array, place, axis, size))
    for shift in range(1, count):
        sent = take(array, (place + shift) % count, axis, size)
        total = total + wide(shift_wt(sent, shift))
    return total


def any_shards(
    tokens,
    doc_starts,
    attn_master,
    attn_mom,
    attn_sq,
    ffn_master,
    ffn_mom,
    ffn_sq,
    small_master,
    small_mom,
    small_sq,
    cotangent,
):
    ctx_count = lax.axis_size("ctx")
    ctx_place = lax.axis_index("ctx")
    wt_count = lax.axis_size("wt")
    batches, rows_here, width = tokens.shape
    heads = width // HS
    qkv_cols = width + 2 * HS
    all_rows = batches * rows_here
    shard_rows = attn_master.shape[0]
    piece_rows = shard_rows // ctx_count
    chunk = FF // ctx_count
    order = ctx_place ^ jnp.arange(ctx_count, dtype=jnp.int32)
    (
        gain_one,
        shift_one,
        gain_two,
        shift_two,
        bias_query,
        bias_out,
        bias_proj,
        bias_value,
        bias_hidden,
    ) = split_small(small_master)

    attn_piece = low(take(attn_master, ctx_place, 0, piece_rows))

    def whole_rows(piece):
        parts = whole_ctx(whole_wt(piece[None], 0))
        buffer = jnp.zeros((wt_count, ctx_count) + piece.shape, piece.dtype)
        for k, part in enumerate(parts):
            buffer = put(buffer, part[:, None], ctx_place ^ k, 1)
        return buffer.reshape((width,) + piece.shape[1:])

    weight_qkv = whole_rows(attn_piece[:, :qkv_cols])
    weight_out = whole_rows(attn_piece[:, qkv_cols:])
    ffn_piece = low(jnp.swapaxes(take(ffn_master, ctx_place, 2, chunk), 0, 1))
    ffn_parts = whole_ctx(whole_wt(ffn_piece, 1))
    bias_parts = bias_hidden.reshape(ctx_count, chunk)[order]

    stream = wide(tokens.reshape(all_rows, width))
    normed, norm_back_one = jax.vjp(layer_norm, stream, gain_one, shift_one)
    normed_low = low(normed)
    mixed = dot(normed_low, weight_qkv)
    queries = low(mixed[:, :width] + bias_query)
    kv_local = low(
        mixed[:, width:] + jnp.concatenate([jnp.zeros((HS,), jnp.float32), bias_value])
    ).reshape(batches, rows_here, 2 * HS)
    kv_parts = jnp.stack(whole_ctx(kv_local), axis=1).reshape(
        batches, ctx_count * rows_here, 2 * HS
    )
    keys_all, values_all = kv_parts[..., :HS], kv_parts[..., HS:]
    local_pos = jnp.arange(rows_here, dtype=jnp.int32)
    query_pos = ctx_place * rows_here + local_pos
    key_pos = (order[:, None] * rows_here + local_pos[None, :]).reshape(-1)
    queries = queries.reshape(batches, rows_here * heads, HS)
    scale = HS ** (-0.5)
    attended_list, log_list, allowed_list = [], [], []
    for b in range(batches):
        starts = doc_starts[b]
        query_doc = jnp.sum((starts[None, :] <= query_pos[:, None]).astype(jnp.int32), axis=1)
        key_doc = jnp.sum((starts[None, :] <= key_pos[:, None]).astype(jnp.int32), axis=1)
        allowed = (query_doc[:, None] == key_doc[None, :]) & (key_pos[None, :] <= query_pos[:, None])
        allowed = jnp.repeat(allowed, heads, axis=0)
        allowed_list.append(allowed)
        scores = jnp.where(allowed, cols_dot(queries[b], keys_all[b]) * scale, -1e30)
        peak = jnp.max(scores, axis=-1, keepdims=True)
        expo = jnp.exp(scores - peak)
        total = jnp.sum(expo, axis=-1, keepdims=True)
        attended_list.append(dot(low(expo / total), values_all[b]))
        log_list.append(peak + jnp.log(total))
    attended = jnp.stack(attended_list)
    attended_low = low(attended).reshape(all_rows, width)
    hidden = stream + dot(attended_low, weight_out) + bias_out
    normed_two, norm_back_two = jax.vjp(layer_norm, hidden, gain_two, shift_two)
    normed_two_low = low(normed_two)

    back_low = cotangent.reshape(all_rows, width)
    back_rows = wide(back_low)
    down_vals = jnp.zeros((all_rows, width), jnp.float32)
    grad_normed_two = jnp.zeros((all_rows, width), jnp.float32)
    ffn_grads, hidden_grads = [], []
    for k in range(ctx_count):
        weight_up, weight_down = ffn_parts[k][0], ffn_parts[k][1]
        value, slope = gelu_both(dot(normed_two_low, weight_up) + bias_parts[k])
        act = low(value)
        down_vals = down_vals + cols_dot(act, weight_down)
        grad_up = low(dot(back_low, weight_down) * slope)
        hidden_grads.append(jnp.sum(wide(grad_up), axis=0))
        grad_normed_two = grad_normed_two + cols_dot(grad_up, weight_up)
        ffn_grads.append(
            jnp.stack([low(rows_dot(normed_two_low, grad_up)), low(rows_dot(back_low, act))])
        )
    layer_out = low(hidden + down_vals + bias_proj).reshape(batches, rows_here, width)
    grad_bias_proj = jnp.sum(back_rows, axis=0)
    grad_bias_hidden = jnp.stack(hidden_grads)[order].reshape(FF)
    ffn_part = low(sum_wt(low(sum_ctx(ffn_grads)), 1))

    grad_hidden_part, grad_gain_two, grad_shift_two = norm_back_two(grad_normed_two)
    grad_hidden = back_rows + grad_hidden_part
    grad_bias_out = jnp.sum(grad_hidden, axis=0)
    grad_hidden_low = low(grad_hidden)
    grad_out = rows_dot(attended_low, grad_hidden_low)

    def summed_rows(grad):
        blocks = low(grad).reshape(wt_count, ctx_count, piece_rows, grad.shape[1])
        pieces = [take(blocks, ctx_place ^ k, 1, 1)[:, 0] for k in range(ctx_count)]
        part = low(sum_wt(low(sum_ctx(pieces)), 0)[0])
        buffer = jnp.zeros((ctx_count,) + part.shape, part.dtype)
        for k, got in enumerate(whole_ctx(part)):
            buffer = put(buffer, got[None], ctx_place ^ k, 0)
        return wide(buffer.reshape(shard_rows, grad.shape[1]))

    out_total = summed_rows(grad_out)

    grad_attended = low(cols_dot(grad_hidden_low, weight_out)).reshape(
        batches, rows_here * heads, HS
    )
    grad_query_list, grad_kv_list = [], []
    for b in range(batches):
        grads = grad_attended[b]
        delta = jnp.sum(wide(grads) * attended[b], axis=-1, keepdims=True)
        scores = jnp.where(allowed_list[b], cols_dot(queries[b], keys_all[b]) * scale, -1e30)
        weights = jnp.exp(scores - log_list[b])
        grad_scores = low(weights * (cols_dot(grads, values_all[b]) - delta))
        grad_query_list.append(low(dot(grad_scores, keys_all[b]) * scale))
        grad_kv_list.append(
            jnp.concatenate(
                [
                    low(rows_dot(grad_scores, queries[b]) * scale),
                    low(rows_dot(low(weights), grads)),
                ],
                axis=1,
            )
        )
    grad_query = jnp.stack(grad_query_list).reshape(all_rows, width)
    grad_kv = jnp.stack(grad_kv_list).reshape(batches, ctx_count, rows_here, 2 * HS)
    grad_kv_low = low(sum_ctx([grad_kv[:, k] for k in range(ctx_count)])).reshape(
        all_rows, 2 * HS
    )
    grad_bias_query = jnp.sum(wide(grad_query), axis=0)
    grad_bias_value = jnp.sum(wide(grad_kv_low[:, HS:]), axis=0)
    grad_mixed = jnp.concatenate([grad_query, grad_kv_low], axis=1)
    qkv_total = summed_rows(rows_dot(normed_low, grad_mixed))
    grad_normed = cols_dot(grad_mixed, weight_qkv)
    grad_stream_part, grad_gain_one, grad_shift_one = norm_back_one(grad_normed)
    input_grad = (grad_hidden + grad_stream_part).reshape(batches, rows_here, width)

    ffn_buffer = jnp.zeros((ctx_count,) + ffn_part.shape, ffn_part.dtype)
    for k, got in enumerate(whole_ctx(ffn_part)):
        ffn_buffer = put(ffn_buffer, got[None], ctx_place ^ k, 0)
    ffn_total = wide(jnp.transpose(ffn_buffer, (2, 1, 0, 3)).reshape(shard_rows, 2, FF))
    attn_total = jnp.concatenate([qkv_total, out_total], axis=1)
    grad_small = jnp.concatenate(
        [
            grad_gain_one,
            grad_shift_one,
            grad_gain_two,
            grad_shift_two,
            grad_bias_query,
            grad_bias_out,
            grad_bias_proj,
            grad_bias_value,
            grad_bias_hidden,
        ]
    )
    small_total = lax.psum(grad_small, ("ctx", "wt"))
    attn_new = adam_update(attn_master, attn_total, attn_mom, attn_sq, 0.1, 0.1)
    ffn_new = adam_update(ffn_master, ffn_total, ffn_mom, ffn_sq, 0.1, 0.1)
    small_new = adam_update(small_master, small_total, small_mom, small_sq, 1.0, 0.0)
    return (layer_out, input_grad) + attn_new + ffn_new + small_new


def solution(mesh):
    rows, cube = P("wt", None), P("wt", None, None)
    flow = P("wt", "ctx", None)
    in_specs = (flow, rows, rows, rows, rows, cube, cube, cube, P(), P(), P(), flow)
    out_specs = (flow, flow, rows, rows, rows, cube, cube, cube, P(), P(), P())
    ctx_count, wt_count = mesh.shape["ctx"], mesh.shape["wt"]
    fitted = (ctx_count, wt_count) == (8, 4)
    body = shards if fitted else any_shards
    return jax.shard_map(body, mesh=mesh, in_specs=in_specs, out_specs=out_specs, check_vma=False)
```

```python
import jax
import jax.numpy as jnp
from jax import lax
from jax.experimental import pallas as pl
from jax.experimental.pallas import tpu as pltpu
from jax.sharding import PartitionSpec as P

D = 768
HS = 64
FF = 3072
STEP = 10


NORM_EPS = 1e-05
GELU_COEF = 0.7978845608028654
GELU_CUBE = 0.044715
BETA_ONE = 0.9
BETA_TWO = 0.95
ADAM_EPS = 1e-08
VMEM_LIMIT = 22 << 20
NO_COST = pl.CostEstimate(flops=0, bytes_accessed=0, transcendentals=0)


def layer_norm(values, gain, shift):
    centre = values - jnp.mean(values, axis=-1, keepdims=True)
    spread = jnp.mean(centre * centre, axis=-1, keepdims=True)
    return centre * lax.rsqrt(spread + NORM_EPS) * gain + shift


def gelu_both(u):
    square = u * u
    share = 0.5 * jnp.tanh(u * (GELU_COEF * GELU_CUBE * square + GELU_COEF)) + 0.5
    bend = u * (6.0 * GELU_COEF * GELU_CUBE * square + 2.0 * GELU_COEF)
    return u * share, share * ((1.0 - share) * bend) + share


def split_small(small):
    return (
        small[0:D],
        small[D : 2 * D],
        small[2 * D : 3 * D],
        small[3 * D : 4 * D],
        small[4 * D : 5 * D],
        small[5 * D : 6 * D],
        small[6 * D : 7 * D],
        small[7 * D : 7 * D + HS],
        small[7 * D + HS :],
    )


def rows_dot(left, right):
    return lax.dot_general(
        left, right, (((0,), (0,)), ((), ())), preferred_element_type=jnp.float32
    )


def cols_dot(left, right):
    return lax.dot_general(
        left, right, (((1,), (1,)), ((), ())), preferred_element_type=jnp.float32
    )


def dot(left, right):
    return jnp.dot(left, right, preferred_element_type=jnp.float32)


def low(values):
    return values.astype(jnp.bfloat16)


def wide(values):
    return values.astype(jnp.float32)


def adam_update(master, gradient, first, second, step_rate, decay_rate):
    first_new = BETA_ONE * first + (1.0 - BETA_ONE) * gradient
    second_new = BETA_TWO * second + (1.0 - BETA_TWO) * gradient * gradient
    first_hat = first_new / (1.0 - BETA_ONE**STEP)
    second_hat = second_new / (1.0 - BETA_TWO**STEP)
    master_new = master - step_rate * (
        first_hat / (jnp.sqrt(second_hat) + ADAM_EPS) + decay_rate * master
    )
    return (first_new, second_new, master_new)


def xor_send(array, mask):
    count = lax.axis_size("ctx")
    return lax.ppermute(array, "ctx", [(i, i ^ mask) for i in range(count)])


def xor_wt(array, mask):
    count = lax.axis_size("wt")
    return lax.ppermute(array, "wt", [(i, i ^ mask) for i in range(count)])


class Steps:
    def __init__(self):
        self.last = ()

    def __call__(self, function, *args):
        flat, tree = jax.tree.flatten(args)
        held = lax.optimization_barrier(tuple(flat) + self.last)[: len(flat)]
        result = function(*jax.tree.unflatten(tree, held))
        self.last = tuple(jax.tree.leaves(result))
        return result


def loop(count, body, carry=0):
    return lax.fori_loop(0, count, body, carry)


def rows_at(i, size):
    return pl.ds(pl.multiple_of(i * size, size), size)


def together(*arrays):
    return lax.optimization_barrier(arrays)


def put(buffer, piece, place, axis):
    starts = [0] * buffer.ndim
    starts[axis] = place * piece.shape[axis]
    return lax.dynamic_update_slice(buffer, piece, starts)


def take(buffer, place, axis, size):
    return lax.dynamic_slice_in_dim(buffer, place * size, size, axis)


def attention_kernels(batches, rows, width, parts, runs):
    half_parts = parts // 2
    keys = parts * rows
    pair = 2 * HS
    groups = width // (2 * pair)
    factor = HS ** (-0.5) * 1.4426950408889634
    tile = 32

    def lanes(shape):
        return lax.broadcasted_iota(jnp.int32, shape, 1)

    def spread(even_ref, odd_ref, key_ref, value_ref):
        for j in range(parts):
            ref = even_ref if j < half_parts else odd_ref
            block = wide(ref[j % half_parts, 0])
            turned = pltpu.roll(block, HS, 1)
            first = lanes(block.shape) < HS
            here = pl.ds(j * rows, rows)
            key_ref[0, here, :] = low(jnp.where(first, block, 0.0))
            key_ref[1, here, :] = low(jnp.where(first, 0.0, turned))
            value_ref[0, here, :] = low(jnp.where(first, turned, 0.0))
            value_ref[1, here, :] = low(jnp.where(first, 0.0, block))

    def doc_begin(starts_ref, stream, positions):
        begin = jnp.zeros_like(positions)
        for j in range(starts_ref.shape[1]):
            start = starts_ref[stream, j]
            begin = jnp.where(start <= positions, jnp.maximum(begin, start), begin)
        return begin

    def forward(starts_ref, place_ref, query_ref, even_ref, odd_ref, low_ref, full_ref, log_ref, cap, key, value, weight):
        stream, place = pl.program_id(0), place_ref[0]
        spread(even_ref, odd_ref, key, value)
        query_pos = place * rows + lax.broadcasted_iota(jnp.int32, (rows, 1), 0)
        begin = doc_begin(starts_ref, stream, query_pos)
        for j in range(parts):
            key_pos = (place ^ (2 * (j % half_parts) + j // half_parts)) * rows + lax.broadcasted_iota(jnp.int32, (rows, rows), 1)
            allowed = (key_pos >= begin) & (key_pos <= query_pos)
            cap[:, j * rows : (j + 1) * rows] = jnp.where(allowed, 3.0e38, -1e30)
        column = lanes((tile, pair))
        logs = [jnp.zeros((tile, pair), jnp.float32) for _ in range(rows // tile)]
        for g in range(groups):
            at = g * 2 * pair
            two = jnp.concatenate([query_ref[0, :, at : at + pair], query_ref[0, :, at + pair : at + 2 * pair]], axis=0)
            totals = []
            for half in range(2):
                scores = cols_dot(two, key[half])
                norms = []
                for t in range(2 * rows // tile):
                    own = slice(t * tile, (t + 1) * tile)
                    n = t % (rows // tile)
                    part = jnp.minimum(scores[own] * factor, cap[n * tile : (n + 1) * tile, :])
                    peak = jnp.max(part, axis=1, keepdims=True)
                    expo = jnp.exp2(part - peak)
                    norm = jnp.sum(expo, axis=1, keepdims=True)
                    weight[half, own, :] = low(expo)
                    norms.append(norm)
                    head = 4 * g + 2 * (t * tile // rows) + half
                    logs[n] = jnp.where(column == head, peak + jnp.log2(norm), logs[n])
                totals.append(dot(weight[half], value[half]) / jnp.concatenate(norms, axis=0))
            total = totals[0] + totals[1]
            for j in range(2):
                part = total[j * rows : (j + 1) * rows]
                full_ref[0, :, at + j * pair : at + (j + 1) * pair] = part
                low_ref[0, :, at + j * pair : at + (j + 1) * pair] = low(part)
        for n, log in enumerate(logs):
            log_ref[0, n * tile : (n + 1) * tile, :] = log

    def backward(
        starts_ref, place_ref, query_ref, even_ref, odd_ref, full_ref, log_ref, grad_ref,
        query_grad_ref, even_grad_ref, odd_grad_ref,
        cap, key, value, key_turned, log_rows, delta_rows, weight_buf, score_buf, query_buf, grad_buf,
    ):
        stream, place = pl.program_id(0) + place_ref[1], place_ref[0]
        spread(even_ref, odd_ref, key, value)
        query_pos = place * rows + lax.broadcasted_iota(jnp.int32, (1, rows), 1)
        begin = doc_begin(starts_ref, stream, query_pos)
        for j in range(parts):
            key_pos = (place ^ (2 * (j % half_parts) + j // half_parts)) * rows + lax.broadcasted_iota(jnp.int32, (rows, rows), 0)
            allowed = (key_pos >= begin) & (key_pos <= query_pos)
            cap[j * rows : (j + 1) * rows, :] = jnp.where(allowed, 3.0e38, -1e30)
            here = pl.ds(j * rows, rows)
            key_turned[:, j * rows : (j + 1) * rows] = low(wide(key[0, here, :]).T[:HS])
        log_rows[...] = log_ref[0].T[: log_rows.shape[0]]
        head_of = lax.broadcasted_iota(jnp.int32, (delta_rows.shape[0], width), 1) // HS
        chosen = (head_of == lax.broadcasted_iota(jnp.int32, (delta_rows.shape[0], width), 0)).astype(jnp.float32)
        delta_rows[...] = lax.dot_general(
            chosen, wide(grad_ref[0]) * full_ref[0], (((1,), (1,)), ((), ())),
            precision=lax.Precision.HIGHEST, preferred_element_type=jnp.float32,
        )
        first = lanes((2 * rows, pair)) < HS
        for g in range(groups):
            at = g * 2 * pair
            both, both_grad = query_ref[0, :, at : at + 2 * pair], grad_ref[0, :, at : at + 2 * pair]
            two = jnp.concatenate([both[:, :pair], both[:, pair:]], axis=0)
            two_grad = jnp.concatenate([both_grad[:, :pair], both_grad[:, pair:]], axis=0)
            turned = []
            for half in range(2):
                h = 4 * g + half
                span = slice((2 * g + half) * 2 * rows, (2 * g + half + 1) * 2 * rows)
                keep = first if half == 0 else jnp.logical_not(first)
                query_buf[span, :] = low(jnp.where(keep, wide(two), 0.0))
                grad_buf[span, :] = low(jnp.where(keep, wide(two_grad), 0.0))
                log = jnp.concatenate([log_rows[h : h + 1, :], log_rows[h + 2 : h + 3, :]], axis=1)
                delta = jnp.concatenate([delta_rows[h : h + 1, :], delta_rows[h + 2 : h + 3, :]], axis=1)
                scores, weight_grads = cols_dot(key[half], two), cols_dot(value[half], two_grad)
                for t in range(keys // (2 * tile)):
                    own = slice(t * 2 * tile, (t + 1) * 2 * tile)
                    limit = cap[own, :]
                    limit = jnp.concatenate([limit, limit], axis=1)
                    weights = jnp.exp2(jnp.minimum(scores[own] * factor, limit) - log)
                    weight_buf[own, span] = low(weights)
                    score_buf[own, span] = low(weights * (weight_grads[own] - delta))
                turned.append(dot(key_turned[...], score_buf[:, span]))
            turned = jnp.concatenate(turned, axis=0) * HS ** (-0.5)
            query_grad_ref[0, :, at : at + pair] = low(turned[:, :rows].T)
            query_grad_ref[0, :, at + pair : at + 2 * pair] = low(turned[:, rows:].T)
        for j in range(parts):
            here = pl.ds(j * rows, rows)
            value_sum = dot(weight_buf[here, :], grad_buf[...])
            key_sum = dot(score_buf[here, :], query_buf[...]) * HS ** (-0.5)
            value_sum = value_sum + pltpu.roll(value_sum, HS, 1)
            key_sum = key_sum + pltpu.roll(key_sum, HS, 1)
            ref = even_grad_ref if j < half_parts else odd_grad_ref
            ref[j % half_parts, 0] = low(jnp.where(lanes((rows, pair)) < HS, key_sum, value_sum))

    def specs(first):
        return (
            pl.BlockSpec((1, rows, width), lambda b, *_: (b + first, 0, 0)),
            pl.BlockSpec((1, rows, pair), lambda b, *_: (b + first, 0, 0)),
            pl.BlockSpec((half_parts, 1, rows, pair), lambda b, *_: (0, b + first, 0, 0)),
        )

    flow, logs, blocks = specs(0)

    shared = [
        pltpu.VMEM((2, keys, pair), jnp.bfloat16),
        pltpu.VMEM((2, keys, pair), jnp.bfloat16),
    ]
    run_forward = pl.pallas_call(
        forward,
        grid_spec=pltpu.PrefetchScalarGridSpec(
            num_scalar_prefetch=2,
            grid=(batches,),
            in_specs=[flow, blocks, blocks],
            out_specs=[flow, flow, logs],
            scratch_shapes=[pltpu.VMEM((rows, keys), jnp.float32)]
            + shared
            + [pltpu.VMEM((2, 2 * rows, keys), jnp.bfloat16)],
        ),
        out_shape=[
            jax.ShapeDtypeStruct((batches, rows, width), jnp.bfloat16),
            jax.ShapeDtypeStruct((batches, rows, width), jnp.float32),
            jax.ShapeDtypeStruct((batches, rows, pair), jnp.float32),
        ],
        compiler_params=pltpu.CompilerParams(vmem_limit_bytes=VMEM_LIMIT),
        cost_estimate=NO_COST,
        name="attention_forward",
    )
    head_rows = -(-(width // HS) // 8) * 8
    all_columns = rows * (width // HS)
    count = batches // runs

    def call_backward(run):
        here_flow, here_logs, here_blocks = specs(run * count)
        return pl.pallas_call(
        backward,
        grid_spec=pltpu.PrefetchScalarGridSpec(
            num_scalar_prefetch=2,
            grid=(count,),
            in_specs=[here_flow, here_blocks, here_blocks, here_flow, here_logs, here_flow],
            out_specs=[flow, blocks, blocks],
            scratch_shapes=[pltpu.VMEM((keys, rows), jnp.float32)]
            + shared
            + [
                pltpu.VMEM((HS, keys), jnp.bfloat16),
                pltpu.VMEM((head_rows, rows), jnp.float32),
                pltpu.VMEM((head_rows, rows), jnp.float32),
                pltpu.VMEM((keys, all_columns), jnp.bfloat16),
                pltpu.VMEM((keys, all_columns), jnp.bfloat16),
                pltpu.VMEM((all_columns, pair), jnp.bfloat16),
                pltpu.VMEM((all_columns, pair), jnp.bfloat16),
            ],
        ),
        out_shape=[
            jax.ShapeDtypeStruct((count, rows, width), jnp.bfloat16),
            jax.ShapeDtypeStruct((half_parts, count, rows, pair), jnp.bfloat16),
            jax.ShapeDtypeStruct((half_parts, count, rows, pair), jnp.bfloat16),
        ],
        compiler_params=pltpu.CompilerParams(vmem_limit_bytes=VMEM_LIMIT),
        cost_estimate=NO_COST,
        name="attention_backward",
    )

    return run_forward, [call_backward(run) for run in range(runs)]


def in_hbm(arrays):
    return [pltpu.with_memory_space_constraint(array, pltpu.HBM) for array in arrays]


def ffn_kernels(rows, width, chunk, wt_count):
    units = 2 * chunk
    all_rows = 2 * rows
    block_rows = width // wt_count
    hbm = pl.BlockSpec(memory_space=pltpu.HBM)
    vmem = pl.BlockSpec(memory_space=pltpu.VMEM)
    params = pltpu.CompilerParams(vmem_limit_bytes=VMEM_LIMIT)

    def fetch(weights, which, held, sem):
        copies = []
        for n, arrays in enumerate(weights):
            blocks = [array.at[block] for array in arrays for block in range(array.shape[0])]
            for row, block in enumerate(blocks):
                copies.append(
                    pltpu.make_async_copy(
                        block.at[pl.ds(which * block_rows, block_rows), :],
                        held.at[pl.ds(row * block_rows, block_rows), pl.ds(n * chunk, chunk)],
                        sem.at[len(copies)],
                    )
                )
        for copy in copies:
            copy.start()
        return copies

    def send(pairs, sems):
        copies = [pltpu.make_async_copy(source, out, sems.at[n]) for n, (source, out) in enumerate(pairs)]
        for copy in copies:
            copy.start()
        return copies

    part_rows = 256
    tile = 16

    def units_of(inputs, grads, bias, held_up, held_down, act, grad_units):
        sums = jnp.zeros((8, units), jnp.float32)
        for s in range(2):

            def part(i, sums):
                here = rows_at(i, part_rows)
                up = dot(inputs[s][here, :], held_up[...])
                act_grad = dot(grads[s][here, :], held_down[...])
                for t in range(part_rows // tile):
                    own = slice(t * tile, (t + 1) * tile)
                    there = pl.ds(pl.multiple_of(s * rows + i * part_rows + t * tile, tile), tile)
                    value, slope = gelu_both(up[own] + bias)
                    grad = act_grad[own] * slope
                    act[there, :] = low(value)
                    grad_units[there, :] = low(grad)
                    sums = sums + (grad[:8] + grad[8:])
                return sums

            sums = loop(rows // part_rows, part, sums)
        return jnp.sum(sums, axis=0, keepdims=True)

    def product_of(turned, right, product):
        def part(i, carry):
            here = rows_at(i, part_rows)
            product[here, :] = low(dot(turned[here, :], right[...]))
            return carry

        loop(width // part_rows, part)

    def back_to(refs, sources, weights):
        for s, ref in enumerate(refs):

            def part(i, carry):
                here = pl.ds(pl.multiple_of(s * rows + i * part_rows, part_rows), part_rows)
                total = cols_dot(sources[0][here, :], weights[0][...]) + cols_dot(sources[1][here, :], weights[1][...])
                ref[rows_at(i, part_rows), :] = total.astype(ref.dtype)
                return carry

            loop(rows // part_rows, part)

    def halves(product, m):
        cols = pl.ds(m * chunk, chunk)
        return [product.at[pl.ds(h * width // 2, width // 2), cols] for h in range(2)]

    def first(
        own, other, grad_own, grad_other, turned, bias, w0, w1, w2, w3,
        act_out, units_out, out_a, out_b, sums_out,
        held_up, held_down, act, grad_units, product, sems, out_sems,
    ):
        weights = ((w0, w1), (w2, w3))
        copies = fetch(weights, 0, held_up, sems.at[0]) + fetch(weights, 1, held_down, sems.at[1])
        for copy in copies:
            copy.wait()
        sums_out[...] = units_of((own, other), (grad_own, grad_other), bias[...], held_up, held_down, act, grad_units)
        sent = send(((act, act_out), (grad_units, units_out)), out_sems.at[0])
        product_of(turned, act, product)
        sent += send(
            ((product.at[:, pl.ds(0, chunk)], out_a), (product.at[:, pl.ds(chunk, chunk)], out_b)), out_sems.at[1]
        )
        for copy in sent:
            copy.wait()

    def second(
        own, other, grad_own, grad_other, turned, bias, units_first, w0, w1, w2, w3, w4, w5, w6, w7,
        act_out, units_out, out_a, out_b, out_c, sums_out, back_own, back_other,
        held_up, held_more, held_down, act, grad_units, more_units, product, sems, out_sems, more_sem,
    ):
        weights, before = ((w4, w5), (w6, w7)), ((w0, w1), (w2, w3))
        copies = fetch(weights, 0, held_up, sems.at[0]) + fetch(weights, 1, held_down, sems.at[1])
        more = fetch(before, 0, held_more, sems.at[2])
        more.append(pltpu.make_async_copy(units_first, more_units, more_sem))
        more[-1].start()
        for copy in copies:
            copy.wait()
        sums_out[...] = units_of((own, other), (grad_own, grad_other), bias[...], held_up, held_down, act, grad_units)
        sent = send(((act, act_out), (grad_units, units_out)), out_sems.at[0])
        product_of(turned, act, product)
        top, bottom = halves(product, 1)
        sent += send(((product.at[:, pl.ds(0, chunk)], out_a), (top, out_b), (bottom, out_c)), out_sems.at[1])
        for copy in more:
            copy.wait()
        back_to((back_own, back_other), (grad_units, more_units), (held_up, held_more))
        for copy in sent:
            copy.wait()

    def third(own, other, units_a, units_b, out_0, out_1, out_2, out_3, turned, held, products, sems, out_sems):
        copies = send(((units_a, held.at[0]), (units_b, held.at[1])), sems)
        turn((own, other), turned)
        for copy in copies:
            copy.wait()
        products[1] = low(dot(turned[...], held[1]))
        sent = send(
            ((products.at[1, :, pl.ds(0, chunk)], out_2), (products.at[1, :, pl.ds(chunk, chunk)], out_3)),
            out_sems.at[0],
        )
        products[0] = low(dot(turned[...], held[0]))
        sent += send(
            ((products.at[0, :, pl.ds(0, chunk)], out_0), (products.at[0, :, pl.ds(chunk, chunk)], out_1)),
            out_sems.at[1],
        )
        for copy in sent:
            copy.wait()

    def down(act_a, act_b, w0, w1, w2, w3, w4, w5, w6, w7, own_ref, other_ref, held_a, held_b, sems):
        copies = fetch(((w0, w1), (w2, w3)), 1, held_a, sems.at[0]) + fetch(((w4, w5), (w6, w7)), 1, held_b, sems.at[1])
        for copy in copies:
            copy.wait()
        for s, ref in enumerate((own_ref, other_ref)):
            here = slice(s * rows, (s + 1) * rows)
            total = cols_dot(act_a[here, :], held_a[...]) + cols_dot(act_b[here, :], held_b[...])
            ref[...] = total.astype(ref.dtype)

    dma = pltpu.SemaphoreType.DMA
    held = pltpu.VMEM((width, units), jnp.bfloat16)
    flow = pltpu.VMEM((all_rows, units), jnp.bfloat16)
    flow_out = pltpu.HBM((all_rows, units), jnp.bfloat16)
    whole = pltpu.HBM((width, chunk), jnp.bfloat16)
    part = pltpu.HBM((width // 2, chunk), jnp.bfloat16)
    sums = jax.ShapeDtypeStruct((1, units), jnp.float32)
    own = jax.ShapeDtypeStruct((rows, width), jnp.float32)
    other = jax.ShapeDtypeStruct((rows, width), jnp.bfloat16)
    run_first = pl.pallas_call(
        first,
        in_specs=[vmem] * 6 + [hbm] * 4,
        out_specs=[hbm] * 4 + [vmem],
        out_shape=[flow_out, flow_out, whole, whole, sums],
        scratch_shapes=[held, held, flow, flow, held, dma((2, 2 * wt_count)), dma((2, 2))],
        compiler_params=params,
        cost_estimate=NO_COST,
        name="ffn_first",
    )
    run_second = pl.pallas_call(
        second,
        in_specs=[vmem] * 6 + [hbm] * 9,
        out_specs=[hbm] * 5 + [vmem] * 3,
        out_shape=[flow_out, flow_out, whole, part, part, sums, own, other],
        scratch_shapes=[held, held, held, flow, flow, flow, held, dma((3, 2 * wt_count)), dma((2, 3)), dma(())],
        compiler_params=params,
        cost_estimate=NO_COST,
        name="ffn_second",
    )
    run_third = pl.pallas_call(
        third,
        in_specs=[vmem] * 2 + [hbm] * 2,
        out_specs=[hbm] * 4,
        out_shape=[whole] * 4,
        scratch_shapes=[
            pltpu.VMEM((width, all_rows), jnp.bfloat16),
            pltpu.VMEM((2, all_rows, units), jnp.bfloat16),
            pltpu.VMEM((2, width, units), jnp.bfloat16),
            dma((2,)),
            dma((2, 2)),
        ],
        compiler_params=params,
        cost_estimate=NO_COST,
        name="ffn_grads",
    )
    run_down = pl.pallas_call(
        down,
        in_specs=[vmem] * 2 + [hbm] * 8,
        out_specs=[vmem] * 2,
        out_shape=[own, other],
        scratch_shapes=[held, held, dma((2, 2 * wt_count))],
        compiler_params=params,
        cost_estimate=NO_COST,
        name="ffn_down",
    )
    return run_first, run_second, run_third, run_down


def turn(refs, turned):
    rows = refs[0].shape[0]
    for s, ref in enumerate(refs):
        for i in range(rows // 128):
            block = wide(ref[i * 128 : (i + 1) * 128, :])
            turned[:, s * rows + i * 128 : s * rows + (i + 1) * 128] = low(block.T)


def turn_both(own, other):
    vmem = pl.BlockSpec(memory_space=pltpu.VMEM)
    rows, width = own.shape
    return pl.pallas_call(
        lambda a, b, out: turn((a, b), out),
        in_specs=[vmem] * 2,
        out_specs=vmem,
        out_shape=jax.ShapeDtypeStruct((width, 2 * rows), own.dtype),
        compiler_params=pltpu.CompilerParams(vmem_limit_bytes=VMEM_LIMIT),
        cost_estimate=NO_COST,
        name="turn",
    )(own, other)


def out_projection(rows, width):
    tile = 32

    def kernel(attended, weight, stream, bias, gain, shift, hidden_ref, normed_ref):
        product = dot(attended[...], weight[...])
        for t in range(rows // tile):
            here = slice(t * tile, (t + 1) * tile)
            hidden = wide(stream[here, :]) + product[here] + bias[...]
            hidden_ref[here, :] = hidden
            normed_ref[here, :] = low(layer_norm(hidden, gain[...], shift[...]))

    vmem = pl.BlockSpec(memory_space=pltpu.VMEM)
    return pl.pallas_call(
        kernel,
        in_specs=[vmem] * 6,
        out_specs=[vmem] * 2,
        out_shape=[
            jax.ShapeDtypeStruct((rows, width), jnp.float32),
            jax.ShapeDtypeStruct((rows, width), jnp.bfloat16),
        ],
        compiler_params=pltpu.CompilerParams(vmem_limit_bytes=VMEM_LIMIT),
        cost_estimate=NO_COST,
        name="out_projection",
    )


def norm_back(values, gain, grad):
    centre = values - jnp.mean(values, axis=-1, keepdims=True)
    scale = lax.rsqrt(jnp.mean(centre * centre, axis=-1, keepdims=True) + NORM_EPS)
    unit = centre * scale
    inner = grad * gain
    mean = jnp.mean(inner, axis=-1, keepdims=True)
    along = jnp.mean(inner * unit, axis=-1, keepdims=True)
    return scale * (inner - mean - unit * along), grad * unit


def fold_rows(values):
    total = values[:8]
    for i in range(1, values.shape[0] // 8):
        total = total + values[i * 8 : (i + 1) * 8]
    return total


def hidden_back(rows, width):
    tile = 32

    def kernel(own, got, hidden, back, gain, weight, grad_ref, low_ref, attended_ref, sums_ref):
        sums = [jnp.zeros((8, width), jnp.float32) for _ in range(3)]
        for t in range(rows // tile):
            here = slice(t * tile, (t + 1) * tile)
            pulled, terms = norm_back(hidden[here, :], gain[...], own[here, :] + wide(got[here, :]))
            grad = wide(back[here, :]) + pulled
            grad_ref[here, :] = grad
            low_ref[here, :] = low(grad)
            for n, part in enumerate((terms, own[here, :] + wide(got[here, :]), grad)):
                sums[n] = sums[n] + fold_rows(part)
        for n in range(3):
            sums_ref[n : n + 1, :] = jnp.sum(sums[n], axis=0, keepdims=True)
        attended_ref[...] = low(cols_dot(low_ref[...], weight[...]))

    vmem = pl.BlockSpec(memory_space=pltpu.VMEM)
    return pl.pallas_call(
        kernel,
        in_specs=[vmem] * 6,
        out_specs=[vmem] * 4,
        out_shape=[
            jax.ShapeDtypeStruct((rows, width), jnp.float32),
            jax.ShapeDtypeStruct((rows, width), jnp.bfloat16),
            jax.ShapeDtypeStruct((rows, width), jnp.bfloat16),
            jax.ShapeDtypeStruct((3, width), jnp.float32),
        ],
        compiler_params=pltpu.CompilerParams(vmem_limit_bytes=VMEM_LIMIT),
        cost_estimate=NO_COST,
        name="hidden_back",
    )


def stream_back(rows, width, parts, row_groups, piece):
    tile = 32
    chips = parts // 2

    def kernel(
        place_ref, kv_0, kv_1, kv_2, kv_3, queries, weight, tokens, gain, grad_hidden, normed, back, hidden_sums,
        units_a, units_b, input_ref, even_ref, odd_ref, grad_kv, grads, turned, product, small,
    ):
        place = place_ref[0]
        sums = [jnp.zeros((8, width), jnp.float32) for _ in range(4)]
        value_sums = jnp.zeros((8, 2 * HS), jnp.float32)
        for t in range(rows // tile):
            here = slice(t * tile, (t + 1) * tile)
            total = wide(kv_0[here, :]) + wide(kv_1[here, :]) + wide(kv_2[here, :]) + wide(kv_3[here, :])
            grad_kv[here, :] = low(total)
            value_sums = value_sums + fold_rows(total)
        turn((normed,), turned)
        product[...] = dot(turned[...], grad_kv[...])
        grads[...] = cols_dot(queries[...], weight[:, :width]) + cols_dot(grad_kv[...], weight[:, width:])
        for t in range(rows // tile):
            here = slice(t * tile, (t + 1) * tile)
            grad = grads[here, :]
            pulled, terms = norm_back(wide(tokens[here, :]), gain[...], grad)
            input_ref[here, :] = grad_hidden[here, :] + pulled
            for n, part in enumerate((terms, grad, wide(queries[here, :]), wide(back[here, :]))):
                sums[n] = sums[n] + fold_rows(part)
        sums = [jnp.sum(part, axis=0, keepdims=True) for part in sums]
        small[...] = jnp.zeros_like(small)
        rows_in = (sums[0], sums[1], hidden_sums[0:1, :], hidden_sums[1:2, :], sums[2], hidden_sums[2:3, :], sums[3])
        for n, row in enumerate(rows_in):
            for j in range(width // 128):
                line = n * (width // 128) + j
                small[line : line + 1, :] = row[:, j * 128 : (j + 1) * 128]
        start = 7 * (width // 128)
        small[start : start + 1, :] = jnp.sum(value_sums, axis=0, keepdims=True)
        lines = FF // parts // 128
        for m in range(chips):
            units = (units_a, units_b)[m // 2]
            for j in range(lines):
                line = start + 1 + (place ^ (2 * m)) * lines + j
                at = (m % 2 * lines + j) * 128
                small[pl.ds(line, 1), :] = units[:, at : at + 128]
        for k in range(parts):
            ref = odd_ref if k % 2 else even_ref
            mine = low(small[pl.ds(pl.multiple_of((place ^ k) * piece, 8), piece), :])
            for w in range(row_groups):
                at = pl.multiple_of(w * piece * parts + (place ^ k) * piece, 8)
                ref[k // 2, w, :, :128] = low(product[pl.ds(at, piece), :])
                ref[k // 2, w, :, 128:] = mine

    vmem = pl.BlockSpec(memory_space=pltpu.VMEM)
    stack = jax.ShapeDtypeStruct((chips, row_groups, piece, 256), jnp.bfloat16)
    return pl.pallas_call(
        kernel,
        in_specs=[pl.BlockSpec(memory_space=pltpu.SMEM)] + [vmem] * 14,
        out_specs=[vmem] * 3,
        out_shape=[jax.ShapeDtypeStruct((rows, width), jnp.float32), stack, stack],
        scratch_shapes=[
            pltpu.VMEM((rows, 2 * HS), jnp.bfloat16),
            pltpu.VMEM((rows, width), jnp.float32),
            pltpu.VMEM((width, rows), jnp.bfloat16),
            pltpu.VMEM((width, 2 * HS), jnp.float32),
            pltpu.VMEM((parts * piece, 128), jnp.float32),
        ],
        compiler_params=pltpu.CompilerParams(vmem_limit_bytes=VMEM_LIMIT),
        cost_estimate=NO_COST,
        name="stream_back",
    )


def attn_grads(rows, width, row_groups, parts, piece):
    def kernel(place_ref, left_a, right_a, left_b, right_b, even_ref, odd_ref, turned, total):
        place = place_ref[0]
        for n, (left, right) in enumerate(((left_a, right_a), (left_b, right_b))):
            for i in range(rows // 128):
                turned[:, i * 128 : (i + 1) * 128] = low(wide(left[i * 128 : (i + 1) * 128, :]).T)
            total[:, n * width : (n + 1) * width] = dot(turned[...], right[...])
        for k in range(parts):
            ref = odd_ref if k % 2 else even_ref
            for w in range(row_groups):
                at = pl.multiple_of(w * piece * parts + (place ^ k) * piece, 8)
                ref[k // 2, w] = low(total[pl.ds(at, piece), :])

    vmem = pl.BlockSpec(memory_space=pltpu.VMEM)
    shape = jax.ShapeDtypeStruct((parts // 2, row_groups, piece, 2 * width), jnp.bfloat16)
    return pl.pallas_call(
        kernel,
        grid_spec=pltpu.PrefetchScalarGridSpec(
            num_scalar_prefetch=1,
            grid=(),
            in_specs=[vmem] * 4,
            out_specs=[vmem] * 2,
            scratch_shapes=[pltpu.VMEM((width, rows), jnp.bfloat16), pltpu.VMEM((width, 2 * width), jnp.float32)],
        ),
        out_shape=[shape] * 2,
        compiler_params=pltpu.CompilerParams(vmem_limit_bytes=VMEM_LIMIT),
        cost_estimate=NO_COST,
        name="attn_grads",
    )


def attn_update(rows, columns, width, parts, piece):
    qkv = columns - width

    def kernel(place_ref, even_ref, odd_ref, master, first, second, *outs):
        place = place_ref[0]
        for k in range(parts):
            ref = odd_ref if k % 2 else even_ref
            here = pl.ds(pl.multiple_of((place ^ k) * piece, 8), piece)
            for cols, source in (
                (slice(0, width), slice(0, width)),
                (slice(width, qkv), slice(2 * width, columns)),
                (slice(qkv, columns), slice(width, 2 * width)),
            ):
                grad = wide(ref[k // 2, :, source])
                got = adam_update(master[here, cols], grad, first[here, cols], second[here, cols], 0.1, 0.1)
                outs[0][here, cols] = got[0]
                outs[1][here, cols] = got[1]
                outs[2][here, cols] = got[2]

    vmem = pl.BlockSpec(memory_space=pltpu.VMEM)
    return pl.pallas_call(
        kernel,
        grid_spec=pltpu.PrefetchScalarGridSpec(
            num_scalar_prefetch=1, grid=(), in_specs=[vmem] * 5, out_specs=[vmem] * 3, scratch_shapes=[]
        ),
        out_shape=[jax.ShapeDtypeStruct((rows, columns), jnp.float32)] * 3,
        compiler_params=pltpu.CompilerParams(vmem_limit_bytes=VMEM_LIMIT),
        cost_estimate=NO_COST,
        name="attn_update",
    )


def ffn_update(rows, units, parts, chunk):
    per_row = 2 * units // 128
    rows_once = 32
    lines = rows_once * per_row

    def kernel(place_ref, even, odd, master, first, second, first_out, second_out, master_out, total):
        place = place_ref[0]
        for k in range(parts):
            grad = odd if k % 2 else even
            for j in range(chunk // 128):
                for which in range(2):
                    line = (place ^ k) * (2 * chunk // 128) + 2 * j + which
                    total[pl.ds(line, rows_once, per_row), :] = wide(
                        grad[k // 2, which, :, j * 128 : (j + 1) * 128]
                    )
        for t in range(lines // 64):
            own = slice(t * 64, (t + 1) * 64)
            got = adam_update(master[own, :], total[own, :], first[own, :], second[own, :], 0.1, 0.1)
            first_out[own, :] = got[0]
            second_out[own, :] = got[1]
            master_out[own, :] = got[2]

    block = pl.BlockSpec((lines, 128), lambda i, *_: (i, 0))
    stack = pl.BlockSpec((parts // 2, 2, rows_once, chunk), lambda i, *_: (0, 0, i, 0))
    call = pl.pallas_call(
        kernel,
        grid_spec=pltpu.PrefetchScalarGridSpec(
            num_scalar_prefetch=1,
            grid=(rows // rows_once,),
            in_specs=[stack] * 2 + [block] * 3,
            out_specs=[block] * 3,
            scratch_shapes=[pltpu.VMEM((lines, 128), jnp.float32)],
        ),
        out_shape=[jax.ShapeDtypeStruct((rows * per_row, 128), jnp.float32)] * 3,
        compiler_params=pltpu.CompilerParams(vmem_limit_bytes=VMEM_LIMIT),
        cost_estimate=NO_COST,
        name="ffn_update",
    )

    def fold(array):
        return jnp.swapaxes(array.reshape(rows, 2, units // 128, 128), 1, 2).reshape(-1, 128)

    def unfold(array):
        return jnp.swapaxes(array.reshape(rows, units // 128, 2, 128), 1, 2).reshape(rows, 2, units)

    def run(place, even, odd, master, first, second):
        return tuple(unfold(array) for array in call(place, even, odd, fold(master), fold(first), fold(second)))

    return run


def shards(
    tokens,
    doc_starts,
    attn_master,
    attn_mom,
    attn_sq,
    ffn_master,
    ffn_mom,
    ffn_sq,
    small_master,
    small_mom,
    small_sq,
    cotangent,
):
    ctx_count, wt_count = lax.axis_size("ctx"), lax.axis_size("wt")
    ctx_place, wt_place = lax.axis_index("ctx"), lax.axis_index("wt")
    batches, rows_here, width = tokens.shape
    qkv_cols = width + 2 * HS
    attn_columns = attn_master.shape[1]
    all_rows = batches * rows_here
    shard_rows = attn_master.shape[0]
    piece_rows = shard_rows // ctx_count
    chunk = FF // ctx_count
    chips = ctx_count // 2
    order = ctx_place ^ jnp.arange(ctx_count, dtype=jnp.int32)
    runs = 2 if batches % 2 == 0 else 1
    places = [jnp.stack([ctx_place, jnp.int32(run * (batches // runs))]) for run in range(runs)]
    place = places[0]
    wt_half = wt_count // 2
    out_rows = shard_rows // chips
    run_forward, run_backward = attention_kernels(batches, rows_here, width, ctx_count, runs)
    ffn_first, ffn_second, ffn_third, ffn_down = ffn_kernels(all_rows, width, chunk, wt_count)
    step = Steps()

    def both(own, got, place, bit, axis=0):
        ahead, behind = jnp.stack([own, got], axis), jnp.stack([got, own], axis)
        return jnp.where((place & bit) == 0, ahead, behind)

    def in_order(even, odd):
        buffer = jnp.zeros((ctx_count,) + even.shape[1:], even.dtype)
        for m in range(chips):
            buffer = put(buffer, even[m][None], ctx_place ^ (2 * m), 0)
            buffer = put(buffer, odd[m][None], ctx_place ^ (2 * m + 1), 0)
        return buffer

    def send_chips(piece):
        return [xor_send(piece, mask) for mask in range(2, ctx_count, 2)]

    def split_wt(total, bit):
        ahead, behind = jnp.split(total, 2)
        kept, sent = jnp.where((wt_place & bit) == 0, ahead, behind), jnp.where((wt_place & bit) == 0, behind, ahead)
        return kept, sent

    def add_low(*arrays):
        return low(sum(wide(array) for array in arrays))

    qkv = low(lax.dynamic_slice(attn_master, (ctx_place * piece_rows, 0), (piece_rows, qkv_cols)))
    out_start = (ctx_place // 2 * out_rows, qkv_cols + ctx_place % 2 * chunk)
    out = low(lax.dynamic_slice(attn_master, out_start, (out_rows, chunk)))
    qkv_got, out_got = xor_wt(qkv, 1), xor_wt(out, 1)
    qkv_got, out_got = together(qkv_got, out_got)
    qkv, out = both(qkv, qkv_got, wt_place, 1), both(out, out_got, wt_place, 1)
    qkv, out, small_late, ffn_late = together(qkv, out, small_master, ffn_master)
    qkv_got, out_got = xor_wt(qkv, 2), xor_wt(out, 2)
    rest = low(jnp.swapaxes(take(ffn_late, ctx_place, 2, chunk), 0, 1).reshape(2 * shard_rows, chunk))
    back_low = cotangent.reshape(all_rows, width)
    qkv_got, rest, out_got = together(qkv_got, rest, out_got)
    rest_got = xor_wt(rest, 1)
    qkv = both(qkv, qkv_got, wt_place, 2).reshape((wt_count,) + qkv.shape[1:])
    qkv_got = send_chips(qkv)
    back_other = xor_send(back_low, 1)
    flat_tokens, qkv, small_late = together(tokens.reshape(all_rows, width), qkv, small_late)
    (
        gain_one,
        shift_one,
        gain_two,
        shift_two,
        bias_query,
        bias_out,
        bias_proj,
        bias_value,
        bias_hidden,
    ) = split_small(small_late)
    normed_low = low(layer_norm(wide(flat_tokens), gain_one, shift_one))
    bias_parts = bias_hidden.reshape(ctx_count, chunk)[order[::2]].reshape(1, chips * chunk)
    bias_near, bias_far = jnp.split(bias_parts, 2, axis=1)
    *qkv_got, rest_got, normed_low, bias_near, bias_far, back_other = together(
        *qkv_got, rest_got, normed_low, bias_near, bias_far, back_other
    )
    out = both(out, out_got, wt_place, 2).reshape((wt_count,) + out.shape[1:])
    ups, downs = [both(rest[rows], rest_got[rows], wt_place, 1) for rows in (slice(shard_rows), slice(shard_rows, None))]
    qkv_even, out, ups = together(jnp.stack([qkv] + qkv_got), out, ups)
    qkv_odd, ups_got = xor_send(qkv_even, 1), xor_wt(ups, 2)
    out_got = send_chips(out)
    qkv_odd, downs = together(qkv_odd, downs)
    blocks = both(qkv_even, qkv_odd, ctx_place, 1, 1)
    for n in range(chips.bit_length() - 1):
        pairs = blocks.reshape((-1, 2, 1 << n) + blocks.shape[1:])
        blocks = jnp.where((ctx_place & (2 << n)) == 0, pairs, pairs[:, ::-1]).reshape(blocks.shape)
    weight_qkv = jnp.transpose(blocks, (2, 0, 1, 3, 4)).reshape(width, qkv_cols)
    mixed = dot(normed_low, weight_qkv)
    queries = low(mixed[:, :width] + bias_query).reshape(batches, rows_here, width)
    kv_bias = jnp.concatenate([jnp.zeros((HS,), jnp.float32), bias_value])
    kv_local = low(mixed[:, width:] + kv_bias).reshape(batches, rows_here, 2 * HS)
    back_turned = turn_both(back_low, back_other)
    kv_local, ups_got, downs, back_turned, *out_got = together(kv_local, ups_got, downs, back_turned, *out_got)
    downs_got = xor_wt(downs, 2)
    kv_got = send_chips(kv_local)
    out_even = jnp.stack([out] + out_got)
    *kv_got, out_even = together(*kv_got, out_even)
    out_odd = xor_send(out_even, 1)
    kv_even = jnp.stack([kv_local] + kv_got)
    kv_odd = xor_send(kv_even, 1)
    kv_even, ups_got, downs_got = together(kv_even, ups_got, downs_got)
    own, got = jnp.concatenate([ups, downs], axis=1), jnp.concatenate([ups_got, downs_got], axis=1)
    first_half = (wt_place & 2) == 0
    rest_low, rest_high = jnp.where(first_half, own, got), jnp.where(first_half, got, own)
    low_x, high_y, high_x, low_y = xor_send(rest_low, 2), xor_send(rest_high, 4), xor_send(rest_high, 2), xor_send(rest_low, 4)
    queries, rest_low, rest_high = together(queries, rest_low, rest_high)

    attended_low, attended, logs = step(run_forward, doc_starts, place, queries, kv_even, kv_odd)
    attended_low = attended_low.reshape(all_rows, width)
    attended_low, low_x, high_y, high_x, low_y = together(attended_low, low_x, high_y, high_x, low_y)
    low_diagonal, high_diagonal = xor_send(low_x, 4), xor_send(high_y, 2)

    def join_out(even, odd):
        columns = jnp.where((ctx_place & 1) == 0, jnp.concatenate([even, odd], axis=3), jnp.concatenate([odd, even], axis=3))
        for n in range(chips.bit_length() - 1):
            pairs = columns.reshape((-1, 2, 1 << n) + columns.shape[1:])
            columns = jnp.where((ctx_place & (2 << n)) == 0, pairs, pairs[:, ::-1]).reshape(columns.shape)
        return jnp.swapaxes(columns, 0, 1).reshape(width, width)

    weight_out = step(join_out, out_even, out_odd)
    hidden, normed_two = step(
        out_projection(all_rows, width), attended_low, weight_out, flat_tokens, bias_out[None], gain_two[None],
        shift_two[None],
    )
    normed_other = xor_send(normed_two, 1)

    weights = [rest_low, rest_high, low_x, high_x, low_y, high_y, low_diagonal, high_diagonal]
    flows = (normed_two, normed_other, back_low, back_other, back_turned)
    act_first, units_first, down_own, down_x, sums_first = step(
        lambda *args: ffn_first(*args[:6], *in_hbm(args[6:])), *flows, bias_near, *weights[:4]
    )
    act_second, units_second, down_y, down_top, down_bottom, sums_second, back_own, back_part = step(
        lambda *args: ffn_second(*args[:6], *in_hbm(args[6:])), *flows, bias_far, units_first, *weights
    )
    back_got = xor_send(back_part, 1)
    top_got, bottom_got = xor_send(down_top, 4), xor_send(down_bottom, 2)

    def meet(along_x, along_y, top, bottom):
        half = width // 2
        return (
            jnp.concatenate([add_low(along_x[:half], top), along_x[half:]]),
            jnp.concatenate([along_y[:half], add_low(along_y[half:], bottom)]),
        )

    up_own, *up_rest = step(
        lambda *args: ffn_third(*args[:2], *in_hbm(args[2:])), normed_two, normed_other, units_first, units_second
    )
    down_x, down_y = step(meet, down_x, down_y, top_got, bottom_got)
    down_got = [xor_send(down_x, 2), xor_send(down_y, 4)]
    up_got = [xor_send(piece, 2 * m) for m, piece in enumerate(up_rest, 1)]

    grad_hidden, grad_hidden_low, grad_attended, hidden_sums = step(
        hidden_back(all_rows, width), back_own, back_got, hidden, back_low, gain_two[None], weight_out
    )
    grad_attended = grad_attended.reshape(batches, rows_here, width)
    def by_wt(*arrays):
        return split_wt(add_low(*arrays).reshape(wt_count, shard_rows, chunk), 2)

    def next_wt(kept, got):
        return split_wt(add_low(kept, got), 1)

    def kv_pieces(evens, odds):
        total = jnp.concatenate([add_low(a, b) for a, b in zip(evens, odds)], axis=1)
        return [total[m] for m in range(chips)]

    backs = [step(run_backward[0], doc_starts, places[0], queries, kv_even, kv_odd, attended, logs, grad_attended)]
    kv_got = [xor_send(backs[0][2], 1)]
    down_kept, down_sent = step(by_wt, down_own, *down_got)
    grad_attended, down_kept, down_sent = together(grad_attended, down_kept, down_sent)
    down_got = xor_wt(down_sent, 2)
    backs += [
        step(run_backward[run], doc_starts, places[run], queries, kv_even, kv_odd, attended, logs, grad_attended)
        for run in range(1, runs)
    ]
    backs[-1] = list(backs[-1])
    held = together(*backs[-1], down_got, *up_got)
    backs[-1], down_got, up_got = held[:3], held[3], held[4:]
    kv_got += [xor_send(back[2], 1) for back in backs[1:]]
    grad_queries = [back[0] for back in backs]
    grad_query = jnp.concatenate(grad_queries).reshape(all_rows, width)
    down_kept, down_sent = next_wt(down_kept, down_got)
    up_kept, up_sent = by_wt(up_own, *up_got)
    down_kept, down_sent, up_kept, up_sent = together(down_kept, down_sent, up_kept, up_sent)
    down_got, up_got = xor_wt(down_sent, 1), xor_wt(up_sent, 2)
    kv_half = step(kv_pieces, [back[1] for back in backs], kv_got)
    kv_got = [xor_send(kv_half[m], 2 * m) for m in range(1, chips)]
    wide_even, wide_odd = step(
        attn_grads(all_rows, width, wt_count, ctx_count, piece_rows),
        place, normed_low, grad_query, attended_low, grad_hidden_low,
    )
    small_size = small_master.shape[0]
    up_kept, up_sent = step(next_wt, up_kept, up_got)
    kv_got[0], up_kept, up_sent = together(kv_got[0], up_kept, up_sent)
    up_got = xor_wt(up_sent, 1)
    input_grad, tail_even, tail_odd = step(
        stream_back(all_rows, width, ctx_count, wt_count, piece_rows),
        place, *[array.reshape(all_rows, 2 * HS) for array in (kv_half[0], *kv_got)], grad_query, weight_qkv,
        flat_tokens, gain_one[None], grad_hidden, normed_low, back_low, hidden_sums, sums_first, sums_second,
    )
    input_grad = input_grad.reshape(batches, rows_here, width)
    wide_odd, tail_odd = lax.optimization_barrier((wide_odd, tail_odd))
    wide_odd, tail_odd = xor_send(wide_odd, 1), xor_send(tail_odd, 1)
    def attn_pieces(wide_even, wide_odd, tail_even, tail_odd):
        total = jnp.concatenate([add_low(wide_even, wide_odd), add_low(tail_even, tail_odd)], axis=3)
        return [total[m] for m in range(chips)]

    attn_half = step(attn_pieces, wide_even, wide_odd, tail_even, tail_odd)
    attn_got = [xor_send(attn_half[m], 2 * m) for m in range(1, chips)]
    ffn_part = step(
        lambda *arrays: jnp.concatenate([add_low(*arrays[:2]), add_low(*arrays[2:])]), up_kept, up_got, down_kept, down_got
    )
    ffn_got = send_chips(ffn_part)
    down_out, down_other = step(
        lambda *args: ffn_down(*args[:2], *in_hbm(args[2:])), act_first, act_second, *weights
    )
    down_other = xor_send(down_other, 1)
    attn_kept, attn_sent = step(lambda *parts: split_wt(add_low(*parts), 2), attn_half[0], *attn_got)
    attn_got = xor_wt(attn_sent, 2)
    layer_out = step(
        lambda hidden, own, got: low(hidden + own + wide(got) + bias_proj).reshape(batches, rows_here, width),
        hidden, down_out, down_other,
    )
    attn_kept, attn_sent = step(lambda kept, got: split_wt(add_low(kept, got), 1), attn_kept, attn_got)
    attn_got = xor_wt(attn_sent, 1)
    ffn_even = step(lambda *parts: jnp.stack(parts), ffn_part, *ffn_got)
    ffn_odd = xor_send(ffn_even, 1)
    attn_part = step(lambda *parts: add_low(*parts)[0], attn_kept, attn_got)
    attn_got = send_chips(attn_part)

    ffn_new = step(
        ffn_update(shard_rows, FF, ctx_count, chunk), place, ffn_even, ffn_odd, ffn_master, ffn_mom, ffn_sq
    )
    attn_even = step(lambda *parts: jnp.stack(parts), attn_part, *attn_got)
    attn_odd = xor_send(attn_even, 1)
    small_total = in_order(attn_even[..., attn_columns:], attn_odd[..., attn_columns:])
    small_total = wide(small_total.reshape(-1))
    most = small_size - FF - HS
    small_total = jnp.concatenate(
        [small_total[:most], small_total[most + HS : most + 2 * HS], small_total[most + 2 * HS : most + 2 * HS + FF]]
    )
    small_new = adam_update(small_master, small_total, small_mom, small_sq, 1.0, 0.0)
    attn_new = attn_update(shard_rows, attn_columns, width, ctx_count, piece_rows)(
        place, attn_even, attn_odd, *in_hbm([attn_master, attn_mom, attn_sq])
    )
    return (layer_out, input_grad) + tuple(attn_new) + tuple(ffn_new) + tuple(small_new)


def shift_wt(array, shift):
    count = lax.axis_size("wt")
    return lax.ppermute(array, "wt", [(i, (i + shift) % count) for i in range(count)])


def whole_wt(piece, axis):
    count, place = lax.axis_size("wt"), lax.axis_index("wt")
    shape = list(piece.shape)
    shape[axis] *= count
    buffer = put(jnp.zeros(shape, piece.dtype), piece, place, axis)
    for shift in range(1, count):
        buffer = put(buffer, shift_wt(piece, shift), (place - shift) % count, axis)
    return buffer


def whole_ctx(piece):
    count = lax.axis_size("ctx")
    got = {0: piece}
    for mask in range(2, count, 2):
        got[mask] = xor_send(piece, mask)
    for mask in range(0, count, 2):
        got[mask + 1] = xor_send(got[mask], 1)
    return [got[mask] for mask in range(count)]


def sum_ctx(pieces):
    count = lax.axis_size("ctx")
    half = {}
    for mask in range(count - 2, -1, -2):
        other = xor_send(pieces[mask + 1], 1)
        half[mask] = low(wide(pieces[mask]) + wide(other))
    total = wide(half[0])
    for mask in range(2, count, 2):
        total = total + wide(xor_send(half[mask], mask))
    return total


def sum_wt(array, axis):
    count, place = lax.axis_size("wt"), lax.axis_index("wt")
    size = array.shape[axis] // count
    total = wide(take(array, place, axis, size))
    for shift in range(1, count):
        sent = take(array, (place + shift) % count, axis, size)
        total = total + wide(shift_wt(sent, shift))
    return total


def any_shards(
    tokens,
    doc_starts,
    attn_master,
    attn_mom,
    attn_sq,
    ffn_master,
    ffn_mom,
    ffn_sq,
    small_master,
    small_mom,
    small_sq,
    cotangent,
):
    ctx_count = lax.axis_size("ctx")
    ctx_place = lax.axis_index("ctx")
    wt_count = lax.axis_size("wt")
    batches, rows_here, width = tokens.shape
    heads = width // HS
    qkv_cols = width + 2 * HS
    all_rows = batches * rows_here
    shard_rows = attn_master.shape[0]
    piece_rows = shard_rows // ctx_count
    chunk = FF // ctx_count
    order = ctx_place ^ jnp.arange(ctx_count, dtype=jnp.int32)
    (
        gain_one,
        shift_one,
        gain_two,
        shift_two,
        bias_query,
        bias_out,
        bias_proj,
        bias_value,
        bias_hidden,
    ) = split_small(small_master)

    attn_piece = low(take(attn_master, ctx_place, 0, piece_rows))

    def whole_rows(piece):
        parts = whole_ctx(whole_wt(piece[None], 0))
        buffer = jnp.zeros((wt_count, ctx_count) + piece.shape, piece.dtype)
        for k, part in enumerate(parts):
            buffer = put(buffer, part[:, None], ctx_place ^ k, 1)
        return buffer.reshape((width,) + piece.shape[1:])

    weight_qkv = whole_rows(attn_piece[:, :qkv_cols])
    weight_out = whole_rows(attn_piece[:, qkv_cols:])
    ffn_piece = low(jnp.swapaxes(take(ffn_master, ctx_place, 2, chunk), 0, 1))
    ffn_parts = whole_ctx(whole_wt(ffn_piece, 1))
    bias_parts = bias_hidden.reshape(ctx_count, chunk)[order]

    stream = wide(tokens.reshape(all_rows, width))
    normed, norm_back_one = jax.vjp(layer_norm, stream, gain_one, shift_one)
    normed_low = low(normed)
    mixed = dot(normed_low, weight_qkv)
    queries = low(mixed[:, :width] + bias_query)
    kv_local = low(
        mixed[:, width:] + jnp.concatenate([jnp.zeros((HS,), jnp.float32), bias_value])
    ).reshape(batches, rows_here, 2 * HS)
    kv_parts = jnp.stack(whole_ctx(kv_local), axis=1).reshape(
        batches, ctx_count * rows_here, 2 * HS
    )
    keys_all, values_all = kv_parts[..., :HS], kv_parts[..., HS:]
    local_pos = jnp.arange(rows_here, dtype=jnp.int32)
    query_pos = ctx_place * rows_here + local_pos
    key_pos = (order[:, None] * rows_here + local_pos[None, :]).reshape(-1)
    queries = queries.reshape(batches, rows_here * heads, HS)
    scale = HS ** (-0.5)
    attended_list, log_list, allowed_list = [], [], []
    for b in range(batches):
        starts = doc_starts[b]
        query_doc = jnp.sum((starts[None, :] <= query_pos[:, None]).astype(jnp.int32), axis=1)
        key_doc = jnp.sum((starts[None, :] <= key_pos[:, None]).astype(jnp.int32), axis=1)
        allowed = (query_doc[:, None] == key_doc[None, :]) & (key_pos[None, :] <= query_pos[:, None])
        allowed = jnp.repeat(allowed, heads, axis=0)
        allowed_list.append(allowed)
        scores = jnp.where(allowed, cols_dot(queries[b], keys_all[b]) * scale, -1e30)
        peak = jnp.max(scores, axis=-1, keepdims=True)
        expo = jnp.exp(scores - peak)
        total = jnp.sum(expo, axis=-1, keepdims=True)
        attended_list.append(dot(low(expo / total), values_all[b]))
        log_list.append(peak + jnp.log(total))
    attended = jnp.stack(attended_list)
    attended_low = low(attended).reshape(all_rows, width)
    hidden = stream + dot(attended_low, weight_out) + bias_out
    normed_two, norm_back_two = jax.vjp(layer_norm, hidden, gain_two, shift_two)
    normed_two_low = low(normed_two)

    back_low = cotangent.reshape(all_rows, width)
    back_rows = wide(back_low)
    down_vals = jnp.zeros((all_rows, width), jnp.float32)
    grad_normed_two = jnp.zeros((all_rows, width), jnp.float32)
    ffn_grads, hidden_grads = [], []
    for k in range(ctx_count):
        weight_up, weight_down = ffn_parts[k][0], ffn_parts[k][1]
        value, slope = gelu_both(dot(normed_two_low, weight_up) + bias_parts[k])
        act = low(value)
        down_vals = down_vals + cols_dot(act, weight_down)
        grad_up = low(dot(back_low, weight_down) * slope)
        hidden_grads.append(jnp.sum(wide(grad_up), axis=0))
        grad_normed_two = grad_normed_two + cols_dot(grad_up, weight_up)
        ffn_grads.append(
            jnp.stack([low(rows_dot(normed_two_low, grad_up)), low(rows_dot(back_low, act))])
        )
    layer_out = low(hidden + down_vals + bias_proj).reshape(batches, rows_here, width)
    grad_bias_proj = jnp.sum(back_rows, axis=0)
    grad_bias_hidden = jnp.stack(hidden_grads)[order].reshape(FF)
    ffn_part = low(sum_wt(low(sum_ctx(ffn_grads)), 1))

    grad_hidden_part, grad_gain_two, grad_shift_two = norm_back_two(grad_normed_two)
    grad_hidden = back_rows + grad_hidden_part
    grad_bias_out = jnp.sum(grad_hidden, axis=0)
    grad_hidden_low = low(grad_hidden)
    grad_out = rows_dot(attended_low, grad_hidden_low)

    def summed_rows(grad):
        blocks = low(grad).reshape(wt_count, ctx_count, piece_rows, grad.shape[1])
        pieces = [take(blocks, ctx_place ^ k, 1, 1)[:, 0] for k in range(ctx_count)]
        part = low(sum_wt(low(sum_ctx(pieces)), 0)[0])
        buffer = jnp.zeros((ctx_count,) + part.shape, part.dtype)
        for k, got in enumerate(whole_ctx(part)):
            buffer = put(buffer, got[None], ctx_place ^ k, 0)
        return wide(buffer.reshape(shard_rows, grad.shape[1]))

    out_total = summed_rows(grad_out)

    grad_attended = low(cols_dot(grad_hidden_low, weight_out)).reshape(
        batches, rows_here * heads, HS
    )
    grad_query_list, grad_kv_list = [], []
    for b in range(batches):
        grads = grad_attended[b]
        delta = jnp.sum(wide(grads) * attended[b], axis=-1, keepdims=True)
        scores = jnp.where(allowed_list[b], cols_dot(queries[b], keys_all[b]) * scale, -1e30)
        weights = jnp.exp(scores - log_list[b])
        grad_scores = low(weights * (cols_dot(grads, values_all[b]) - delta))
        grad_query_list.append(low(dot(grad_scores, keys_all[b]) * scale))
        grad_kv_list.append(
            jnp.concatenate(
                [
                    low(rows_dot(grad_scores, queries[b]) * scale),
                    low(rows_dot(low(weights), grads)),
                ],
                axis=1,
            )
        )
    grad_query = jnp.stack(grad_query_list).reshape(all_rows, width)
    grad_kv = jnp.stack(grad_kv_list).reshape(batches, ctx_count, rows_here, 2 * HS)
    grad_kv_low = low(sum_ctx([grad_kv[:, k] for k in range(ctx_count)])).reshape(
        all_rows, 2 * HS
    )
    grad_bias_query = jnp.sum(wide(grad_query), axis=0)
    grad_bias_value = jnp.sum(wide(grad_kv_low[:, HS:]), axis=0)
    grad_mixed = jnp.concatenate([grad_query, grad_kv_low], axis=1)
    qkv_total = summed_rows(rows_dot(normed_low, grad_mixed))
    grad_normed = cols_dot(grad_mixed, weight_qkv)
    grad_stream_part, grad_gain_one, grad_shift_one = norm_back_one(grad_normed)
    input_grad = (grad_hidden + grad_stream_part).reshape(batches, rows_here, width)

    ffn_buffer = jnp.zeros((ctx_count,) + ffn_part.shape, ffn_part.dtype)
    for k, got in enumerate(whole_ctx(ffn_part)):
        ffn_buffer = put(ffn_buffer, got[None], ctx_place ^ k, 0)
    ffn_total = wide(jnp.transpose(ffn_buffer, (2, 1, 0, 3)).reshape(shard_rows, 2, FF))
    attn_total = jnp.concatenate([qkv_total, out_total], axis=1)
    grad_small = jnp.concatenate(
        [
            grad_gain_one,
            grad_shift_one,
            grad_gain_two,
            grad_shift_two,
            grad_bias_query,
            grad_bias_out,
            grad_bias_proj,
            grad_bias_value,
            grad_bias_hidden,
        ]
    )
    small_total = lax.psum(grad_small, ("ctx", "wt"))
    attn_new = adam_update(attn_master, attn_total, attn_mom, attn_sq, 0.1, 0.1)
    ffn_new = adam_update(ffn_master, ffn_total, ffn_mom, ffn_sq, 0.1, 0.1)
    small_new = adam_update(small_master, small_total, small_mom, small_sq, 1.0, 0.0)
    return (layer_out, input_grad) + attn_new + ffn_new + small_new


def solution(mesh):
    rows, cube = P("wt", None), P("wt", None, None)
    flow = P("wt", "ctx", None)
    in_specs = (flow, rows, rows, rows, rows, cube, cube, cube, P(), P(), P(), flow)
    out_specs = (flow, flow, rows, rows, rows, cube, cube, cube, P(), P(), P())
    ctx_count, wt_count = mesh.shape["ctx"], mesh.shape["wt"]
    fitted = (ctx_count, wt_count) == (8, 4)
    body = shards if fitted else any_shards
    return jax.shard_map(body, mesh=mesh, in_specs=in_specs, out_specs=out_specs, check_vma=False)
```

```python
import jax
import jax.numpy as jnp
from jax import lax
from jax.experimental import pallas as pl
from jax.experimental.pallas import tpu as pltpu
from jax.sharding import PartitionSpec as P

D = 768
HS = 64
FF = 3072
STEP = 10


NORM_EPS = 1e-05
GELU_COEF = 0.7978845608028654
GELU_CUBE = 0.044715
BETA_ONE = 0.9
BETA_TWO = 0.95
ADAM_EPS = 1e-08
VMEM_LIMIT = 22 << 20
NO_COST = pl.CostEstimate(flops=0, bytes_accessed=0, transcendentals=0)


def layer_norm(values, gain, shift):
    centre = values - jnp.mean(values, axis=-1, keepdims=True)
    spread = jnp.mean(centre * centre, axis=-1, keepdims=True)
    return centre * lax.rsqrt(spread + NORM_EPS) * gain + shift


def gelu_both(u):
    square = u * u
    share = 0.5 * jnp.tanh(u * (GELU_COEF * GELU_CUBE * square + GELU_COEF)) + 0.5
    bend = u * (6.0 * GELU_COEF * GELU_CUBE * square + 2.0 * GELU_COEF)
    return u * share, share * ((1.0 - share) * bend) + share


def split_small(small):
    return (
        small[0:D],
        small[D : 2 * D],
        small[2 * D : 3 * D],
        small[3 * D : 4 * D],
        small[4 * D : 5 * D],
        small[5 * D : 6 * D],
        small[6 * D : 7 * D],
        small[7 * D : 7 * D + HS],
        small[7 * D + HS :],
    )


def rows_dot(left, right):
    return lax.dot_general(
        left, right, (((0,), (0,)), ((), ())), preferred_element_type=jnp.float32
    )


def cols_dot(left, right):
    return lax.dot_general(
        left, right, (((1,), (1,)), ((), ())), preferred_element_type=jnp.float32
    )


def dot(left, right):
    return jnp.dot(left, right, preferred_element_type=jnp.float32)


def low(values):
    return values.astype(jnp.bfloat16)


def wide(values):
    return values.astype(jnp.float32)


def adam_update(master, gradient, first, second, step_rate, decay_rate):
    first_new = BETA_ONE * first + (1.0 - BETA_ONE) * gradient
    second_new = BETA_TWO * second + (1.0 - BETA_TWO) * gradient * gradient
    first_hat = first_new / (1.0 - BETA_ONE**STEP)
    second_hat = second_new / (1.0 - BETA_TWO**STEP)
    master_new = master - step_rate * (
        first_hat / (jnp.sqrt(second_hat) + ADAM_EPS) + decay_rate * master
    )
    return (first_new, second_new, master_new)


def xor_send(array, mask):
    count = lax.axis_size("ctx")
    return lax.ppermute(array, "ctx", [(i, i ^ mask) for i in range(count)])


def xor_wt(array, mask):
    count = lax.axis_size("wt")
    return lax.ppermute(array, "wt", [(i, i ^ mask) for i in range(count)])


class Steps:
    def __init__(self):
        self.last = ()

    def __call__(self, function, *args):
        flat, tree = jax.tree.flatten(args)
        held = lax.optimization_barrier(tuple(flat) + self.last)[: len(flat)]
        result = function(*jax.tree.unflatten(tree, held))
        self.last = tuple(jax.tree.leaves(result))
        return result


def loop(count, body, carry=0):
    return lax.fori_loop(0, count, body, carry)


def rows_at(i, size):
    return pl.ds(pl.multiple_of(i * size, size), size)


def together(*arrays):
    return lax.optimization_barrier(arrays)


def put(buffer, piece, place, axis):
    starts = [0] * buffer.ndim
    starts[axis] = place * piece.shape[axis]
    return lax.dynamic_update_slice(buffer, piece, starts)


def take(buffer, place, axis, size):
    return lax.dynamic_slice_in_dim(buffer, place * size, size, axis)


def attention_kernels(batches, rows, width, parts, runs):
    half_parts = parts // 2
    keys = parts * rows
    pair = 2 * HS
    groups = width // (2 * pair)
    factor = HS ** (-0.5) * 1.4426950408889634
    tile = 32

    def lanes(shape):
        return lax.broadcasted_iota(jnp.int32, shape, 1)

    def spread(even_ref, odd_ref, key_ref, value_ref):
        for j in range(parts):
            ref = even_ref if j < half_parts else odd_ref
            block = wide(ref[j % half_parts, 0])
            turned = pltpu.roll(block, HS, 1)
            first = lanes(block.shape) < HS
            here = pl.ds(j * rows, rows)
            key_ref[0, here, :] = low(jnp.where(first, block, 0.0))
            key_ref[1, here, :] = low(jnp.where(first, 0.0, turned))
            value_ref[0, here, :] = low(jnp.where(first, turned, 0.0))
            value_ref[1, here, :] = low(jnp.where(first, 0.0, block))

    def doc_begin(starts_ref, stream, positions):
        begin = jnp.zeros_like(positions)
        for j in range(starts_ref.shape[1]):
            start = starts_ref[stream, j]
            begin = jnp.where(start <= positions, jnp.maximum(begin, start), begin)
        return begin

    def forward(starts_ref, place_ref, query_ref, even_ref, odd_ref, low_ref, full_ref, log_ref, cap, key, value, weight):
        stream, place = pl.program_id(0), place_ref[0]
        spread(even_ref, odd_ref, key, value)
        query_pos = place * rows + lax.broadcasted_iota(jnp.int32, (rows, 1), 0)
        begin = doc_begin(starts_ref, stream, query_pos)
        for j in range(parts):
            key_pos = (place ^ (2 * (j % half_parts) + j // half_parts)) * rows + lax.broadcasted_iota(jnp.int32, (rows, rows), 1)
            allowed = (key_pos >= begin) & (key_pos <= query_pos)
            cap[:, j * rows : (j + 1) * rows] = jnp.where(allowed, 3.0e38, -1e30)
        column = lanes((tile, pair))
        logs = [jnp.zeros((tile, pair), jnp.float32) for _ in range(rows // tile)]
        for g in range(groups):
            at = g * 2 * pair
            two = jnp.concatenate([query_ref[0, :, at : at + pair], query_ref[0, :, at + pair : at + 2 * pair]], axis=0)
            totals = []
            for half in range(2):
                scores = cols_dot(two, key[half])
                norms = []
                for t in range(2 * rows // tile):
                    own = slice(t * tile, (t + 1) * tile)
                    n = t % (rows // tile)
                    part = jnp.minimum(scores[own] * factor, cap[n * tile : (n + 1) * tile, :])
                    peak = jnp.max(part, axis=1, keepdims=True)
                    expo = jnp.exp2(part - peak)
                    norm = jnp.sum(expo, axis=1, keepdims=True)
                    weight[half, own, :] = low(expo)
                    norms.append(norm)
                    head = 4 * g + 2 * (t * tile // rows) + half
                    logs[n] = jnp.where(column == head, peak + jnp.log2(norm), logs[n])
                totals.append(dot(weight[half], value[half]) / jnp.concatenate(norms, axis=0))
            total = totals[0] + totals[1]
            for j in range(2):
                part = total[j * rows : (j + 1) * rows]
                full_ref[0, :, at + j * pair : at + (j + 1) * pair] = part
                low_ref[0, :, at + j * pair : at + (j + 1) * pair] = low(part)
        for n, log in enumerate(logs):
            log_ref[0, n * tile : (n + 1) * tile, :] = log

    def backward(
        starts_ref, place_ref, query_ref, even_ref, odd_ref, full_ref, log_ref, grad_ref,
        query_grad_ref, even_grad_ref, odd_grad_ref,
        cap, key, value, key_turned, log_rows, delta_rows, weight_buf, score_buf, query_buf, grad_buf,
    ):
        stream, place = pl.program_id(0) + place_ref[1], place_ref[0]
        spread(even_ref, odd_ref, key, value)
        query_pos = place * rows + lax.broadcasted_iota(jnp.int32, (1, rows), 1)
        begin = doc_begin(starts_ref, stream, query_pos)
        for j in range(parts):
            key_pos = (place ^ (2 * (j % half_parts) + j // half_parts)) * rows + lax.broadcasted_iota(jnp.int32, (rows, rows), 0)
            allowed = (key_pos >= begin) & (key_pos <= query_pos)
            cap[j * rows : (j + 1) * rows, :] = jnp.where(allowed, 3.0e38, -1e30)
            here = pl.ds(j * rows, rows)
            key_turned[:, j * rows : (j + 1) * rows] = low(wide(key[0, here, :]).T[:HS])
        log_rows[...] = log_ref[0].T[: log_rows.shape[0]]
        head_of = lax.broadcasted_iota(jnp.int32, (delta_rows.shape[0], width), 1) // HS
        chosen = (head_of == lax.broadcasted_iota(jnp.int32, (delta_rows.shape[0], width), 0)).astype(jnp.float32)
        delta_rows[...] = lax.dot_general(
            chosen, wide(grad_ref[0]) * full_ref[0], (((1,), (1,)), ((), ())),
            precision=lax.Precision.HIGHEST, preferred_element_type=jnp.float32,
        )
        first = lanes((2 * rows, pair)) < HS
        for g in range(groups):
            at = g * 2 * pair
            both, both_grad = query_ref[0, :, at : at + 2 * pair], grad_ref[0, :, at : at + 2 * pair]
            two = jnp.concatenate([both[:, :pair], both[:, pair:]], axis=0)
            two_grad = jnp.concatenate([both_grad[:, :pair], both_grad[:, pair:]], axis=0)
            turned = []
            for half in range(2):
                h = 4 * g + half
                span = slice((2 * g + half) * 2 * rows, (2 * g + half + 1) * 2 * rows)
                keep = first if half == 0 else jnp.logical_not(first)
                query_buf[span, :] = low(jnp.where(keep, wide(two), 0.0))
                grad_buf[span, :] = low(jnp.where(keep, wide(two_grad), 0.0))
                log = jnp.concatenate([log_rows[h : h + 1, :], log_rows[h + 2 : h + 3, :]], axis=1)
                delta = jnp.concatenate([delta_rows[h : h + 1, :], delta_rows[h + 2 : h + 3, :]], axis=1)
                scores, weight_grads = cols_dot(key[half], two), cols_dot(value[half], two_grad)
                for t in range(keys // (2 * tile)):
                    own = slice(t * 2 * tile, (t + 1) * 2 * tile)
                    limit = cap[own, :]
                    limit = jnp.concatenate([limit, limit], axis=1)
                    weights = jnp.exp2(jnp.minimum(scores[own] * factor, limit) - log)
                    weight_buf[own, span] = low(weights)
                    score_buf[own, span] = low(weights * (weight_grads[own] - delta))
                turned.append(dot(key_turned[...], score_buf[:, span]))
            turned = jnp.concatenate(turned, axis=0) * HS ** (-0.5)
            query_grad_ref[0, :, at : at + pair] = low(turned[:, :rows].T)
            query_grad_ref[0, :, at + pair : at + 2 * pair] = low(turned[:, rows:].T)
        for j in range(parts):
            here = pl.ds(j * rows, rows)
            value_sum = dot(weight_buf[here, :], grad_buf[...])
            key_sum = dot(score_buf[here, :], query_buf[...]) * HS ** (-0.5)
            value_sum = value_sum + pltpu.roll(value_sum, HS, 1)
            key_sum = key_sum + pltpu.roll(key_sum, HS, 1)
            ref = even_grad_ref if j < half_parts else odd_grad_ref
            ref[j % half_parts, 0] = low(jnp.where(lanes((rows, pair)) < HS, key_sum, value_sum))

    def specs(first):
        return (
            pl.BlockSpec((1, rows, width), lambda b, *_: (b + first, 0, 0)),
            pl.BlockSpec((1, rows, pair), lambda b, *_: (b + first, 0, 0)),
            pl.BlockSpec((half_parts, 1, rows, pair), lambda b, *_: (0, b + first, 0, 0)),
        )

    flow, logs, blocks = specs(0)

    shared = [
        pltpu.VMEM((2, keys, pair), jnp.bfloat16),
        pltpu.VMEM((2, keys, pair), jnp.bfloat16),
    ]
    run_forward = pl.pallas_call(
        forward,
        grid_spec=pltpu.PrefetchScalarGridSpec(
            num_scalar_prefetch=2,
            grid=(batches,),
            in_specs=[flow, blocks, blocks],
            out_specs=[flow, flow, logs],
            scratch_shapes=[pltpu.VMEM((rows, keys), jnp.float32)]
            + shared
            + [pltpu.VMEM((2, 2 * rows, keys), jnp.bfloat16)],
        ),
        out_shape=[
            jax.ShapeDtypeStruct((batches, rows, width), jnp.bfloat16),
            jax.ShapeDtypeStruct((batches, rows, width), jnp.float32),
            jax.ShapeDtypeStruct((batches, rows, pair), jnp.float32),
        ],
        compiler_params=pltpu.CompilerParams(vmem_limit_bytes=VMEM_LIMIT),
        cost_estimate=NO_COST,
        name="attention_forward",
    )
    head_rows = -(-(width // HS) // 8) * 8
    all_columns = rows * (width // HS)
    count = batches // runs

    def call_backward(run):
        here_flow, here_logs, here_blocks = specs(run * count)
        return pl.pallas_call(
        backward,
        grid_spec=pltpu.PrefetchScalarGridSpec(
            num_scalar_prefetch=2,
            grid=(count,),
            in_specs=[here_flow, here_blocks, here_blocks, here_flow, here_logs, here_flow],
            out_specs=[flow, blocks, blocks],
            scratch_shapes=[pltpu.VMEM((keys, rows), jnp.float32)]
            + shared
            + [
                pltpu.VMEM((HS, keys), jnp.bfloat16),
                pltpu.VMEM((head_rows, rows), jnp.float32),
                pltpu.VMEM((head_rows, rows), jnp.float32),
                pltpu.VMEM((keys, all_columns), jnp.bfloat16),
                pltpu.VMEM((keys, all_columns), jnp.bfloat16),
                pltpu.VMEM((all_columns, pair), jnp.bfloat16),
                pltpu.VMEM((all_columns, pair), jnp.bfloat16),
            ],
        ),
        out_shape=[
            jax.ShapeDtypeStruct((count, rows, width), jnp.bfloat16),
            jax.ShapeDtypeStruct((half_parts, count, rows, pair), jnp.bfloat16),
            jax.ShapeDtypeStruct((half_parts, count, rows, pair), jnp.bfloat16),
        ],
        compiler_params=pltpu.CompilerParams(vmem_limit_bytes=VMEM_LIMIT),
        cost_estimate=NO_COST,
        name="attention_backward",
    )

    return run_forward, [call_backward(run) for run in range(runs)]


def in_hbm(arrays):
    return [pltpu.with_memory_space_constraint(array, pltpu.HBM) for array in arrays]


def ffn_kernels(rows, width, chunk, wt_count):
    units = 2 * chunk
    all_rows = 2 * rows
    block_rows = width // wt_count
    hbm = pl.BlockSpec(memory_space=pltpu.HBM)
    vmem = pl.BlockSpec(memory_space=pltpu.VMEM)
    params = pltpu.CompilerParams(vmem_limit_bytes=VMEM_LIMIT)

    def fetch(weights, which, held, sem):
        copies = []
        for n, arrays in enumerate(weights):
            blocks = [array.at[block] for array in arrays for block in range(array.shape[0])]
            for row, block in enumerate(blocks):
                copies.append(
                    pltpu.make_async_copy(
                        block.at[pl.ds(which * block_rows, block_rows), :],
                        held.at[pl.ds(row * block_rows, block_rows), pl.ds(n * chunk, chunk)],
                        sem.at[len(copies)],
                    )
                )
        for copy in copies:
            copy.start()
        return copies

    def send(pairs, sems):
        copies = [pltpu.make_async_copy(source, out, sems.at[n]) for n, (source, out) in enumerate(pairs)]
        for copy in copies:
            copy.start()
        return copies

    part_rows = 256
    tile = 16

    def units_of(inputs, grads, bias, held_up, held_down, act, grad_units):
        sums = jnp.zeros((8, units), jnp.float32)
        for s in range(2):

            def part(i, sums):
                here = rows_at(i, part_rows)
                up = dot(inputs[s][here, :], held_up[...])
                act_grad = dot(grads[s][here, :], held_down[...])
                for t in range(part_rows // tile):
                    own = slice(t * tile, (t + 1) * tile)
                    there = pl.ds(pl.multiple_of(s * rows + i * part_rows + t * tile, tile), tile)
                    value, slope = gelu_both(up[own] + bias)
                    grad = act_grad[own] * slope
                    act[there, :] = low(value)
                    grad_units[there, :] = low(grad)
                    sums = sums + (grad[:8] + grad[8:])
                return sums

            sums = loop(rows // part_rows, part, sums)
        return jnp.sum(sums, axis=0, keepdims=True)

    def product_of(turned, right, product):
        def part(i, carry):
            here = rows_at(i, part_rows)
            product[here, :] = low(dot(turned[here, :], right[...]))
            return carry

        loop(width // part_rows, part)

    def back_to(refs, sources, weights):
        for s, ref in enumerate(refs):

            def part(i, carry):
                here = pl.ds(pl.multiple_of(s * rows + i * part_rows, part_rows), part_rows)
                total = cols_dot(sources[0][here, :], weights[0][...]) + cols_dot(sources[1][here, :], weights[1][...])
                ref[rows_at(i, part_rows), :] = total.astype(ref.dtype)
                return carry

            loop(rows // part_rows, part)

    def halves(product, m):
        cols = pl.ds(m * chunk, chunk)
        return [product.at[pl.ds(h * width // 2, width // 2), cols] for h in range(2)]

    def first(
        own, other, grad_own, grad_other, turned, bias, w0, w1, w2, w3,
        act_out, units_out, out_a, out_b, sums_out,
        held_up, held_down, act, grad_units, product, sems, out_sems,
    ):
        weights = ((w0, w1), (w2, w3))
        copies = fetch(weights, 0, held_up, sems.at[0]) + fetch(weights, 1, held_down, sems.at[1])
        for copy in copies:
            copy.wait()
        sums_out[...] = units_of((own, other), (grad_own, grad_other), bias[...], held_up, held_down, act, grad_units)
        sent = send(((act, act_out), (grad_units, units_out)), out_sems.at[0])
        product_of(turned, act, product)
        sent += send(
            ((product.at[:, pl.ds(0, chunk)], out_a), (product.at[:, pl.ds(chunk, chunk)], out_b)), out_sems.at[1]
        )
        for copy in sent:
            copy.wait()

    def second(
        own, other, grad_own, grad_other, turned, bias, units_first, w0, w1, w2, w3, w4, w5, w6, w7,
        act_out, units_out, out_a, out_b, out_c, sums_out, back_own, back_other,
        held_up, held_more, held_down, act, grad_units, more_units, product, sems, out_sems, more_sem,
    ):
        weights, before = ((w4, w5), (w6, w7)), ((w0, w1), (w2, w3))
        copies = fetch(weights, 0, held_up, sems.at[0]) + fetch(weights, 1, held_down, sems.at[1])
        more = fetch(before, 0, held_more, sems.at[2])
        more.append(pltpu.make_async_copy(units_first, more_units, more_sem))
        more[-1].start()
        for copy in copies:
            copy.wait()
        sums_out[...] = units_of((own, other), (grad_own, grad_other), bias[...], held_up, held_down, act, grad_units)
        sent = send(((act, act_out), (grad_units, units_out)), out_sems.at[0])
        product_of(turned, act, product)
        top, bottom = halves(product, 1)
        sent += send(((product.at[:, pl.ds(0, chunk)], out_a), (top, out_b), (bottom, out_c)), out_sems.at[1])
        for copy in more:
            copy.wait()
        back_to((back_own, back_other), (grad_units, more_units), (held_up, held_more))
        for copy in sent:
            copy.wait()

    def third(own, other, units_a, units_b, out_0, out_1, out_2, out_3, out_4, turned, held, products, sems, out_sems):
        copies = send(((units_a, held.at[0]), (units_b, held.at[1])), sems)
        turn((own, other), turned)
        for copy in copies:
            copy.wait()
        products[1] = low(dot(turned[...], held[1]))
        top, bottom = halves(products.at[1], 1)
        sent = send(((products.at[1, :, pl.ds(0, chunk)], out_2), (top, out_3), (bottom, out_4)), out_sems.at[0])
        products[0] = low(dot(turned[...], held[0]))
        sent += send(
            ((products.at[0, :, pl.ds(0, chunk)], out_0), (products.at[0, :, pl.ds(chunk, chunk)], out_1)),
            out_sems.at[1],
        )
        for copy in sent:
            copy.wait()

    def down(act_a, act_b, w0, w1, w2, w3, w4, w5, w6, w7, own_ref, other_ref, held_a, held_b, sems):
        copies = fetch(((w0, w1), (w2, w3)), 1, held_a, sems.at[0]) + fetch(((w4, w5), (w6, w7)), 1, held_b, sems.at[1])
        for copy in copies:
            copy.wait()
        for s, ref in enumerate((own_ref, other_ref)):
            here = slice(s * rows, (s + 1) * rows)
            total = cols_dot(act_a[here, :], held_a[...]) + cols_dot(act_b[here, :], held_b[...])
            ref[...] = total.astype(ref.dtype)

    dma = pltpu.SemaphoreType.DMA
    held = pltpu.VMEM((width, units), jnp.bfloat16)
    flow = pltpu.VMEM((all_rows, units), jnp.bfloat16)
    flow_out = pltpu.HBM((all_rows, units), jnp.bfloat16)
    whole = pltpu.HBM((width, chunk), jnp.bfloat16)
    part = pltpu.HBM((width // 2, chunk), jnp.bfloat16)
    sums = jax.ShapeDtypeStruct((1, units), jnp.float32)
    own = jax.ShapeDtypeStruct((rows, width), jnp.float32)
    other = jax.ShapeDtypeStruct((rows, width), jnp.bfloat16)
    run_first = pl.pallas_call(
        first,
        in_specs=[vmem] * 6 + [hbm] * 4,
        out_specs=[hbm] * 4 + [vmem],
        out_shape=[flow_out, flow_out, whole, whole, sums],
        scratch_shapes=[held, held, flow, flow, held, dma((2, 2 * wt_count)), dma((2, 2))],
        compiler_params=params,
        cost_estimate=NO_COST,
        name="ffn_first",
    )
    run_second = pl.pallas_call(
        second,
        in_specs=[vmem] * 6 + [hbm] * 9,
        out_specs=[hbm] * 5 + [vmem] * 3,
        out_shape=[flow_out, flow_out, whole, part, part, sums, own, other],
        scratch_shapes=[held, held, held, flow, flow, flow, held, dma((3, 2 * wt_count)), dma((2, 3)), dma(())],
        compiler_params=params,
        cost_estimate=NO_COST,
        name="ffn_second",
    )
    run_third = pl.pallas_call(
        third,
        in_specs=[vmem] * 2 + [hbm] * 2,
        out_specs=[hbm] * 5,
        out_shape=[whole, whole, whole, part, part],
        scratch_shapes=[
            pltpu.VMEM((width, all_rows), jnp.bfloat16),
            pltpu.VMEM((2, all_rows, units), jnp.bfloat16),
            pltpu.VMEM((2, width, units), jnp.bfloat16),
            dma((2,)),
            dma((2, 3)),
        ],
        compiler_params=params,
        cost_estimate=NO_COST,
        name="ffn_grads",
    )
    run_down = pl.pallas_call(
        down,
        in_specs=[vmem] * 2 + [hbm] * 8,
        out_specs=[vmem] * 2,
        out_shape=[own, other],
        scratch_shapes=[held, held, dma((2, 2 * wt_count))],
        compiler_params=params,
        cost_estimate=NO_COST,
        name="ffn_down",
    )
    return run_first, run_second, run_third, run_down


def turn(refs, turned):
    rows = refs[0].shape[0]
    for s, ref in enumerate(refs):
        for i in range(rows // 128):
            block = wide(ref[i * 128 : (i + 1) * 128, :])
            turned[:, s * rows + i * 128 : s * rows + (i + 1) * 128] = low(block.T)


def turn_both(own, other):
    vmem = pl.BlockSpec(memory_space=pltpu.VMEM)
    rows, width = own.shape
    return pl.pallas_call(
        lambda a, b, out: turn((a, b), out),
        in_specs=[vmem] * 2,
        out_specs=vmem,
        out_shape=jax.ShapeDtypeStruct((width, 2 * rows), own.dtype),
        compiler_params=pltpu.CompilerParams(vmem_limit_bytes=VMEM_LIMIT),
        cost_estimate=NO_COST,
        name="turn",
    )(own, other)


def out_projection(rows, width):
    tile = 32

    def kernel(attended, weight, stream, bias, gain, shift, hidden_ref, normed_ref):
        product = dot(attended[...], weight[...])
        for t in range(rows // tile):
            here = slice(t * tile, (t + 1) * tile)
            hidden = wide(stream[here, :]) + product[here] + bias[...]
            hidden_ref[here, :] = hidden
            normed_ref[here, :] = low(layer_norm(hidden, gain[...], shift[...]))

    vmem = pl.BlockSpec(memory_space=pltpu.VMEM)
    return pl.pallas_call(
        kernel,
        in_specs=[vmem] * 6,
        out_specs=[vmem] * 2,
        out_shape=[
            jax.ShapeDtypeStruct((rows, width), jnp.float32),
            jax.ShapeDtypeStruct((rows, width), jnp.bfloat16),
        ],
        compiler_params=pltpu.CompilerParams(vmem_limit_bytes=VMEM_LIMIT),
        cost_estimate=NO_COST,
        name="out_projection",
    )


def norm_back(values, gain, grad):
    centre = values - jnp.mean(values, axis=-1, keepdims=True)
    scale = lax.rsqrt(jnp.mean(centre * centre, axis=-1, keepdims=True) + NORM_EPS)
    unit = centre * scale
    inner = grad * gain
    mean = jnp.mean(inner, axis=-1, keepdims=True)
    along = jnp.mean(inner * unit, axis=-1, keepdims=True)
    return scale * (inner - mean - unit * along), grad * unit


def fold_rows(values):
    total = values[:8]
    for i in range(1, values.shape[0] // 8):
        total = total + values[i * 8 : (i + 1) * 8]
    return total


def hidden_back(rows, width):
    tile = 32

    def kernel(own, got, hidden, back, gain, weight, grad_ref, low_ref, attended_ref, sums_ref):
        sums = [jnp.zeros((8, width), jnp.float32) for _ in range(3)]
        for t in range(rows // tile):
            here = slice(t * tile, (t + 1) * tile)
            pulled, terms = norm_back(hidden[here, :], gain[...], own[here, :] + wide(got[here, :]))
            grad = wide(back[here, :]) + pulled
            grad_ref[here, :] = grad
            low_ref[here, :] = low(grad)
            for n, part in enumerate((terms, own[here, :] + wide(got[here, :]), grad)):
                sums[n] = sums[n] + fold_rows(part)
        for n in range(3):
            sums_ref[n : n + 1, :] = jnp.sum(sums[n], axis=0, keepdims=True)
        attended_ref[...] = low(cols_dot(low_ref[...], weight[...]))

    vmem = pl.BlockSpec(memory_space=pltpu.VMEM)
    return pl.pallas_call(
        kernel,
        in_specs=[vmem] * 6,
        out_specs=[vmem] * 4,
        out_shape=[
            jax.ShapeDtypeStruct((rows, width), jnp.float32),
            jax.ShapeDtypeStruct((rows, width), jnp.bfloat16),
            jax.ShapeDtypeStruct((rows, width), jnp.bfloat16),
            jax.ShapeDtypeStruct((3, width), jnp.float32),
        ],
        compiler_params=pltpu.CompilerParams(vmem_limit_bytes=VMEM_LIMIT),
        cost_estimate=NO_COST,
        name="hidden_back",
    )


def stream_back(rows, width, parts, row_groups, piece):
    tile = 32
    chips = parts // 2

    def kernel(
        place_ref, kv_0, kv_1, kv_2, kv_3, queries, weight, tokens, gain, grad_hidden, normed, back, hidden_sums,
        units_a, units_b, input_ref, even_ref, odd_ref, grad_kv, grads, turned, product, small,
    ):
        place = place_ref[0]
        sums = [jnp.zeros((8, width), jnp.float32) for _ in range(4)]
        value_sums = jnp.zeros((8, 2 * HS), jnp.float32)
        for t in range(rows // tile):
            here = slice(t * tile, (t + 1) * tile)
            total = wide(kv_0[here, :]) + wide(kv_1[here, :]) + wide(kv_2[here, :]) + wide(kv_3[here, :])
            grad_kv[here, :] = low(total)
            value_sums = value_sums + fold_rows(total)
        turn((normed,), turned)
        product[...] = dot(turned[...], grad_kv[...])
        grads[...] = cols_dot(queries[...], weight[:, :width]) + cols_dot(grad_kv[...], weight[:, width:])
        for t in range(rows // tile):
            here = slice(t * tile, (t + 1) * tile)
            grad = grads[here, :]
            pulled, terms = norm_back(wide(tokens[here, :]), gain[...], grad)
            input_ref[here, :] = grad_hidden[here, :] + pulled
            for n, part in enumerate((terms, grad, wide(queries[here, :]), wide(back[here, :]))):
                sums[n] = sums[n] + fold_rows(part)
        sums = [jnp.sum(part, axis=0, keepdims=True) for part in sums]
        small[...] = jnp.zeros_like(small)
        rows_in = (sums[0], sums[1], hidden_sums[0:1, :], hidden_sums[1:2, :], sums[2], hidden_sums[2:3, :], sums[3])
        for n, row in enumerate(rows_in):
            for j in range(width // 128):
                line = n * (width // 128) + j
                small[line : line + 1, :] = row[:, j * 128 : (j + 1) * 128]
        start = 7 * (width // 128)
        small[start : start + 1, :] = jnp.sum(value_sums, axis=0, keepdims=True)
        lines = FF // parts // 128
        for m in range(chips):
            units = (units_a, units_b)[m // 2]
            for j in range(lines):
                line = start + 1 + (place ^ (2 * m)) * lines + j
                at = (m % 2 * lines + j) * 128
                small[pl.ds(line, 1), :] = units[:, at : at + 128]
        for k in range(parts):
            ref = odd_ref if k % 2 else even_ref
            mine = low(small[pl.ds(pl.multiple_of((place ^ k) * piece, 8), piece), :])
            for w in range(row_groups):
                at = pl.multiple_of(w * piece * parts + (place ^ k) * piece, 8)
                ref[k // 2, w, :, :128] = low(product[pl.ds(at, piece), :])
                ref[k // 2, w, :, 128:] = mine

    vmem = pl.BlockSpec(memory_space=pltpu.VMEM)
    stack = jax.ShapeDtypeStruct((chips, row_groups, piece, 256), jnp.bfloat16)
    return pl.pallas_call(
        kernel,
        in_specs=[pl.BlockSpec(memory_space=pltpu.SMEM)] + [vmem] * 14,
        out_specs=[vmem] * 3,
        out_shape=[jax.ShapeDtypeStruct((rows, width), jnp.float32), stack, stack],
        scratch_shapes=[
            pltpu.VMEM((rows, 2 * HS), jnp.bfloat16),
            pltpu.VMEM((rows, width), jnp.float32),
            pltpu.VMEM((width, rows), jnp.bfloat16),
            pltpu.VMEM((width, 2 * HS), jnp.float32),
            pltpu.VMEM((parts * piece, 128), jnp.float32),
        ],
        compiler_params=pltpu.CompilerParams(vmem_limit_bytes=VMEM_LIMIT),
        cost_estimate=NO_COST,
        name="stream_back",
    )


def attn_grads(rows, width, row_groups, parts, piece):
    def kernel(place_ref, left_a, right_a, left_b, right_b, even_ref, odd_ref, turned, total):
        place = place_ref[0]
        for n, (left, right) in enumerate(((left_a, right_a), (left_b, right_b))):
            for i in range(rows // 128):
                turned[:, i * 128 : (i + 1) * 128] = low(wide(left[i * 128 : (i + 1) * 128, :]).T)
            total[:, n * width : (n + 1) * width] = dot(turned[...], right[...])
        for k in range(parts):
            ref = odd_ref if k % 2 else even_ref
            for w in range(row_groups):
                at = pl.multiple_of(w * piece * parts + (place ^ k) * piece, 8)
                ref[k // 2, w] = low(total[pl.ds(at, piece), :])

    vmem = pl.BlockSpec(memory_space=pltpu.VMEM)
    shape = jax.ShapeDtypeStruct((parts // 2, row_groups, piece, 2 * width), jnp.bfloat16)
    return pl.pallas_call(
        kernel,
        grid_spec=pltpu.PrefetchScalarGridSpec(
            num_scalar_prefetch=1,
            grid=(),
            in_specs=[vmem] * 4,
            out_specs=[vmem] * 2,
            scratch_shapes=[pltpu.VMEM((width, rows), jnp.bfloat16), pltpu.VMEM((width, 2 * width), jnp.float32)],
        ),
        out_shape=[shape] * 2,
        compiler_params=pltpu.CompilerParams(vmem_limit_bytes=VMEM_LIMIT),
        cost_estimate=NO_COST,
        name="attn_grads",
    )


def attn_update(rows, columns, width, parts, piece):
    qkv = columns - width

    def kernel(place_ref, even_ref, odd_ref, master, first, second, *outs):
        place = place_ref[0]
        for k in range(parts):
            ref = odd_ref if k % 2 else even_ref
            here = pl.ds(pl.multiple_of((place ^ k) * piece, 8), piece)
            for cols, source in (
                (slice(0, width), slice(0, width)),
                (slice(width, qkv), slice(2 * width, columns)),
                (slice(qkv, columns), slice(width, 2 * width)),
            ):
                grad = wide(ref[k // 2, :, source])
                got = adam_update(master[here, cols], grad, first[here, cols], second[here, cols], 0.1, 0.1)
                outs[0][here, cols] = got[0]
                outs[1][here, cols] = got[1]
                outs[2][here, cols] = got[2]

    vmem = pl.BlockSpec(memory_space=pltpu.VMEM)
    return pl.pallas_call(
        kernel,
        grid_spec=pltpu.PrefetchScalarGridSpec(
            num_scalar_prefetch=1, grid=(), in_specs=[vmem] * 5, out_specs=[vmem] * 3, scratch_shapes=[]
        ),
        out_shape=[jax.ShapeDtypeStruct((rows, columns), jnp.float32)] * 3,
        compiler_params=pltpu.CompilerParams(vmem_limit_bytes=VMEM_LIMIT),
        cost_estimate=NO_COST,
        name="attn_update",
    )


def ffn_update(rows, units, parts, chunk):
    per_row = 2 * units // 128
    rows_once = 32
    lines = rows_once * per_row

    def kernel(place_ref, even, odd, master, first, second, first_out, second_out, master_out, total):
        place = place_ref[0]
        for k in range(parts):
            grad = odd if k % 2 else even
            for j in range(chunk // 128):
                for which in range(2):
                    line = (place ^ k) * (2 * chunk // 128) + 2 * j + which
                    total[pl.ds(line, rows_once, per_row), :] = wide(
                        grad[k // 2, which, :, j * 128 : (j + 1) * 128]
                    )
        for t in range(lines // 64):
            own = slice(t * 64, (t + 1) * 64)
            got = adam_update(master[own, :], total[own, :], first[own, :], second[own, :], 0.1, 0.1)
            first_out[own, :] = got[0]
            second_out[own, :] = got[1]
            master_out[own, :] = got[2]

    block = pl.BlockSpec((lines, 128), lambda i, *_: (i, 0))
    stack = pl.BlockSpec((parts // 2, 2, rows_once, chunk), lambda i, *_: (0, 0, i, 0))
    call = pl.pallas_call(
        kernel,
        grid_spec=pltpu.PrefetchScalarGridSpec(
            num_scalar_prefetch=1,
            grid=(rows // rows_once,),
            in_specs=[stack] * 2 + [block] * 3,
            out_specs=[block] * 3,
            scratch_shapes=[pltpu.VMEM((lines, 128), jnp.float32)],
        ),
        out_shape=[jax.ShapeDtypeStruct((rows * per_row, 128), jnp.float32)] * 3,
        compiler_params=pltpu.CompilerParams(vmem_limit_bytes=VMEM_LIMIT),
        cost_estimate=NO_COST,
        name="ffn_update",
    )

    def fold(array):
        return jnp.swapaxes(array.reshape(rows, 2, units // 128, 128), 1, 2).reshape(-1, 128)

    def unfold(array):
        return jnp.swapaxes(array.reshape(rows, units // 128, 2, 128), 1, 2).reshape(rows, 2, units)

    def run(place, even, odd, master, first, second):
        return tuple(unfold(array) for array in call(place, even, odd, fold(master), fold(first), fold(second)))

    return run


def shards(
    tokens,
    doc_starts,
    attn_master,
    attn_mom,
    attn_sq,
    ffn_master,
    ffn_mom,
    ffn_sq,
    small_master,
    small_mom,
    small_sq,
    cotangent,
):
    ctx_count, wt_count = lax.axis_size("ctx"), lax.axis_size("wt")
    ctx_place, wt_place = lax.axis_index("ctx"), lax.axis_index("wt")
    batches, rows_here, width = tokens.shape
    qkv_cols = width + 2 * HS
    attn_columns = attn_master.shape[1]
    all_rows = batches * rows_here
    shard_rows = attn_master.shape[0]
    piece_rows = shard_rows // ctx_count
    chunk = FF // ctx_count
    chips = ctx_count // 2
    order = ctx_place ^ jnp.arange(ctx_count, dtype=jnp.int32)
    runs = 2 if batches % 2 == 0 else 1
    places = [jnp.stack([ctx_place, jnp.int32(run * (batches // runs))]) for run in range(runs)]
    place = places[0]
    wt_half = wt_count // 2
    out_rows = shard_rows // chips
    run_forward, run_backward = attention_kernels(batches, rows_here, width, ctx_count, runs)
    ffn_first, ffn_second, ffn_third, ffn_down = ffn_kernels(all_rows, width, chunk, wt_count)
    step = Steps()

    def both(own, got, place, bit, axis=0):
        ahead, behind = jnp.stack([own, got], axis), jnp.stack([got, own], axis)
        return jnp.where((place & bit) == 0, ahead, behind)

    def in_order(even, odd):
        buffer = jnp.zeros((ctx_count,) + even.shape[1:], even.dtype)
        for m in range(chips):
            buffer = put(buffer, even[m][None], ctx_place ^ (2 * m), 0)
            buffer = put(buffer, odd[m][None], ctx_place ^ (2 * m + 1), 0)
        return buffer

    def send_chips(piece):
        return [xor_send(piece, mask) for mask in range(2, ctx_count, 2)]

    def split_wt(total, bit):
        pairs = total.reshape((-1, 2) + total.shape[1:]) if bit == 1 else total[None]
        ahead, behind = pairs[:, 0], pairs[:, 1]
        here = (wt_place & bit) == 0
        return jnp.where(here, ahead, behind), jnp.where(here, behind, ahead)

    def add_low(*arrays):
        return low(sum(wide(array) for array in arrays))

    qkv = low(lax.dynamic_slice(attn_master, (ctx_place * piece_rows, 0), (piece_rows, qkv_cols)))
    out_start = (ctx_place // 2 * out_rows, qkv_cols + ctx_place % 2 * chunk)
    out = low(lax.dynamic_slice(attn_master, out_start, (out_rows, chunk)))
    rest = low(jnp.swapaxes(take(ffn_master, ctx_place, 2, chunk), 0, 1).reshape(2 * shard_rows, chunk))
    qkv_got, out_got = xor_wt(qkv, 2), xor_wt(out, 2)
    qkv_got, out_got, rest = together(qkv_got, out_got, rest)
    rest = lax.all_gather(rest, "wt", axis=0)
    qkv, out = both(qkv, qkv_got, wt_place, 2), both(out, out_got, wt_place, 2)
    qkv, out, small_late = together(qkv, out, small_master)
    qkv_got, out_got = xor_wt(qkv, 1), xor_wt(out, 1)
    back_low = cotangent.reshape(all_rows, width)
    qkv_got, out_got = together(qkv_got, out_got)
    qkv = both(qkv, qkv_got, wt_place, 1, 1).reshape((wt_count,) + qkv.shape[1:])
    qkv_got = send_chips(qkv)
    back_other = xor_send(back_low, 1)
    flat_tokens, qkv, small_late = together(tokens.reshape(all_rows, width), qkv, small_late)
    (
        gain_one,
        shift_one,
        gain_two,
        shift_two,
        bias_query,
        bias_out,
        bias_proj,
        bias_value,
        bias_hidden,
    ) = split_small(small_late)
    normed_low = low(layer_norm(wide(flat_tokens), gain_one, shift_one))
    bias_parts = bias_hidden.reshape(ctx_count, chunk)[order[::2]].reshape(1, chips * chunk)
    bias_near, bias_far = jnp.split(bias_parts, 2, axis=1)
    *qkv_got, normed_low, bias_near, bias_far, back_other = together(
        *qkv_got, normed_low, bias_near, bias_far, back_other
    )
    out = both(out, out_got, wt_place, 1, 1).reshape((wt_count,) + out.shape[1:])
    qkv_even, out = together(jnp.stack([qkv] + qkv_got), out)
    qkv_odd = xor_send(qkv_even, 1)
    out_got = send_chips(out)
    blocks = both(qkv_even, qkv_odd, ctx_place, 1, 1)
    for n in range(chips.bit_length() - 1):
        pairs = blocks.reshape((-1, 2, 1 << n) + blocks.shape[1:])
        blocks = jnp.where((ctx_place & (2 << n)) == 0, pairs, pairs[:, ::-1]).reshape(blocks.shape)
    weight_qkv = jnp.transpose(blocks, (2, 0, 1, 3, 4)).reshape(width, qkv_cols)
    mixed = dot(normed_low, weight_qkv)
    queries = low(mixed[:, :width] + bias_query).reshape(batches, rows_here, width)
    kv_bias = jnp.concatenate([jnp.zeros((HS,), jnp.float32), bias_value])
    kv_local = low(mixed[:, width:] + kv_bias).reshape(batches, rows_here, 2 * HS)
    back_turned = turn_both(back_low, back_other)
    kv_local, back_turned, *out_got = together(kv_local, back_turned, *out_got)
    kv_got = send_chips(kv_local)
    out_even = jnp.stack([out] + out_got)
    *kv_got, out_even, rest = together(*kv_got, out_even, rest)
    out_odd = xor_send(out_even, 1)
    kv_even = jnp.stack([kv_local] + kv_got)
    kv_odd = xor_send(kv_even, 1)
    rest_low, rest_high = rest[:wt_half], rest[wt_half:]
    low_x, high_y, high_x, low_y = xor_send(rest_low, 2), xor_send(rest_high, 4), xor_send(rest_high, 2), xor_send(rest_low, 4)
    queries, rest_low, rest_high = together(queries, rest_low, rest_high)

    attended_low, attended, logs = step(run_forward, doc_starts, place, queries, kv_even, kv_odd)
    attended_low = attended_low.reshape(all_rows, width)
    attended_low, low_x, high_y, high_x, low_y = together(attended_low, low_x, high_y, high_x, low_y)
    low_diagonal, high_diagonal = xor_send(low_x, 4), xor_send(high_y, 2)

    def join_out(even, odd):
        columns = jnp.where((ctx_place & 1) == 0, jnp.concatenate([even, odd], axis=3), jnp.concatenate([odd, even], axis=3))
        for n in range(chips.bit_length() - 1):
            pairs = columns.reshape((-1, 2, 1 << n) + columns.shape[1:])
            columns = jnp.where((ctx_place & (2 << n)) == 0, pairs, pairs[:, ::-1]).reshape(columns.shape)
        return jnp.swapaxes(columns, 0, 1).reshape(width, width)

    weight_out = step(join_out, out_even, out_odd)
    hidden, normed_two = step(
        out_projection(all_rows, width), attended_low, weight_out, flat_tokens, bias_out[None], gain_two[None],
        shift_two[None],
    )
    normed_other = xor_send(normed_two, 1)

    weights = [rest_low, rest_high, low_x, high_x, low_y, high_y, low_diagonal, high_diagonal]
    flows = (normed_two, normed_other, back_low, back_other, back_turned)
    act_first, units_first, down_own, down_x, sums_first = step(
        lambda *args: ffn_first(*args[:6], *in_hbm(args[6:])), *flows, bias_near, *weights[:4]
    )
    act_second, units_second, down_y, down_top, down_bottom, sums_second, back_own, back_part = step(
        lambda *args: ffn_second(*args[:6], *in_hbm(args[6:])), *flows, bias_far, units_first, *weights
    )
    back_got = xor_send(back_part, 1)
    top_got, bottom_got = xor_send(down_top, 4), xor_send(down_bottom, 2)

    def meet(along_x, along_y, top, bottom):
        half = width // 2
        return (
            jnp.concatenate([add_low(along_x[:half], top), along_x[half:]]),
            jnp.concatenate([along_y[:half], add_low(along_y[half:], bottom)]),
        )

    up_own, up_x, up_y, up_top, up_bottom = step(
        lambda *args: ffn_third(*args[:2], *in_hbm(args[2:])), normed_two, normed_other, units_first, units_second
    )
    down_x, down_y = step(meet, down_x, down_y, top_got, bottom_got)
    down_got = [xor_send(down_x, 2), xor_send(down_y, 4)]
    top_got, bottom_got = xor_send(up_top, 4), xor_send(up_bottom, 2)

    grad_hidden, grad_hidden_low, grad_attended, hidden_sums = step(
        hidden_back(all_rows, width), back_own, back_got, hidden, back_low, gain_two[None], weight_out
    )
    grad_attended = grad_attended.reshape(batches, rows_here, width)
    def by_wt(*arrays):
        return split_wt(add_low(*arrays).reshape(wt_count, shard_rows, chunk), 1)

    def next_wt(kept, got):
        return split_wt(add_low(kept, got), 2)

    def kv_pieces(evens, odds):
        total = jnp.concatenate([add_low(a, b) for a, b in zip(evens, odds)], axis=1)
        return [total[m] for m in range(chips)]

    backs = [step(run_backward[0], doc_starts, places[0], queries, kv_even, kv_odd, attended, logs, grad_attended)]
    kv_got = [xor_send(backs[0][2], 1)]
    down_kept, down_sent = step(by_wt, down_own, *down_got)
    up_x, up_y = step(meet, up_x, up_y, top_got, bottom_got)
    grad_attended, down_kept, down_sent, up_x, up_y = together(grad_attended, down_kept, down_sent, up_x, up_y)
    down_got = xor_wt(down_sent, 1)
    up_got = [xor_send(up_x, 2), xor_send(up_y, 4)]
    backs += [
        step(run_backward[run], doc_starts, places[run], queries, kv_even, kv_odd, attended, logs, grad_attended)
        for run in range(1, runs)
    ]
    backs[-1] = list(backs[-1])
    *backs[-1], down_got, up_got[0], up_got[1] = together(*backs[-1], down_got, *up_got)
    kv_got += [xor_send(back[2], 1) for back in backs[1:]]
    grad_queries = [back[0] for back in backs]
    grad_query = jnp.concatenate(grad_queries).reshape(all_rows, width)
    down_kept, down_sent = next_wt(down_kept, down_got)
    up_kept, up_sent = by_wt(up_own, *up_got)
    down_kept, down_sent, up_kept, up_sent = together(down_kept, down_sent, up_kept, up_sent)
    down_got, up_got = xor_wt(down_sent, 2), xor_wt(up_sent, 1)
    kv_half = step(kv_pieces, [back[1] for back in backs], kv_got)
    kv_got = [xor_send(kv_half[m], 2 * m) for m in range(1, chips)]
    wide_even, wide_odd = step(
        attn_grads(all_rows, width, wt_count, ctx_count, piece_rows),
        place, normed_low, grad_query, attended_low, grad_hidden_low,
    )
    small_size = small_master.shape[0]
    up_kept, up_sent = step(next_wt, up_kept, up_got)
    kv_got[0], up_kept, up_sent = together(kv_got[0], up_kept, up_sent)
    up_got = xor_wt(up_sent, 2)
    input_grad, tail_even, tail_odd = step(
        stream_back(all_rows, width, ctx_count, wt_count, piece_rows),
        place, *[array.reshape(all_rows, 2 * HS) for array in (kv_half[0], *kv_got)], grad_query, weight_qkv,
        flat_tokens, gain_one[None], grad_hidden, normed_low, back_low, hidden_sums, sums_first, sums_second,
    )
    input_grad = input_grad.reshape(batches, rows_here, width)
    wide_odd, tail_odd = lax.optimization_barrier((wide_odd, tail_odd))
    wide_odd, tail_odd = xor_send(wide_odd, 1), xor_send(tail_odd, 1)
    def attn_pieces(wide_even, wide_odd, tail_even, tail_odd):
        total = jnp.concatenate([add_low(wide_even, wide_odd), add_low(tail_even, tail_odd)], axis=3)
        return [total[m] for m in range(chips)]

    attn_half = step(attn_pieces, wide_even, wide_odd, tail_even, tail_odd)
    attn_got = [xor_send(attn_half[m], 2 * m) for m in range(1, chips)]
    ffn_part = step(
        lambda *arrays: jnp.concatenate([add_low(*arrays[:2]), add_low(*arrays[2:])]), up_kept, up_got, down_kept, down_got
    )
    ffn_got = send_chips(ffn_part)
    down_out, down_other = step(
        lambda *args: ffn_down(*args[:2], *in_hbm(args[2:])), act_first, act_second, *weights
    )
    down_other = xor_send(down_other, 1)
    attn_kept, attn_sent = step(lambda *parts: split_wt(add_low(*parts), 1), attn_half[0], *attn_got)
    attn_got = xor_wt(attn_sent, 1)
    layer_out = step(
        lambda hidden, own, got: low(hidden + own + wide(got) + bias_proj).reshape(batches, rows_here, width),
        hidden, down_out, down_other,
    )
    attn_kept, attn_sent = step(lambda kept, got: split_wt(add_low(kept, got), 2), attn_kept, attn_got)
    attn_got = xor_wt(attn_sent, 2)
    ffn_even = step(lambda *parts: jnp.stack(parts), ffn_part, *ffn_got)
    ffn_odd = xor_send(ffn_even, 1)
    attn_part = step(lambda *parts: add_low(*parts)[0], attn_kept, attn_got)
    attn_got = send_chips(attn_part)

    ffn_new = step(
        ffn_update(shard_rows, FF, ctx_count, chunk), place, ffn_even, ffn_odd, ffn_master, ffn_mom, ffn_sq
    )
    attn_even = step(lambda *parts: jnp.stack(parts), attn_part, *attn_got)
    attn_odd = xor_send(attn_even, 1)
    small_total = in_order(attn_even[..., attn_columns:], attn_odd[..., attn_columns:])
    small_total = wide(small_total.reshape(-1))
    most = small_size - FF - HS
    small_total = jnp.concatenate(
        [small_total[:most], small_total[most + HS : most + 2 * HS], small_total[most + 2 * HS : most + 2 * HS + FF]]
    )
    small_new = adam_update(small_master, small_total, small_mom, small_sq, 1.0, 0.0)
    attn_new = attn_update(shard_rows, attn_columns, width, ctx_count, piece_rows)(
        place, attn_even, attn_odd, *in_hbm([attn_master, attn_mom, attn_sq])
    )
    return (layer_out, input_grad) + tuple(attn_new) + tuple(ffn_new) + tuple(small_new)


def shift_wt(array, shift):
    count = lax.axis_size("wt")
    return lax.ppermute(array, "wt", [(i, (i + shift) % count) for i in range(count)])


def whole_wt(piece, axis):
    count, place = lax.axis_size("wt"), lax.axis_index("wt")
    shape = list(piece.shape)
    shape[axis] *= count
    buffer = put(jnp.zeros(shape, piece.dtype), piece, place, axis)
    for shift in range(1, count):
        buffer = put(buffer, shift_wt(piece, shift), (place - shift) % count, axis)
    return buffer


def whole_ctx(piece):
    count = lax.axis_size("ctx")
    got = {0: piece}
    for mask in range(2, count, 2):
        got[mask] = xor_send(piece, mask)
    for mask in range(0, count, 2):
        got[mask + 1] = xor_send(got[mask], 1)
    return [got[mask] for mask in range(count)]


def sum_ctx(pieces):
    count = lax.axis_size("ctx")
    half = {}
    for mask in range(count - 2, -1, -2):
        other = xor_send(pieces[mask + 1], 1)
        half[mask] = low(wide(pieces[mask]) + wide(other))
    total = wide(half[0])
    for mask in range(2, count, 2):
        total = total + wide(xor_send(half[mask], mask))
    return total


def sum_wt(array, axis):
    count, place = lax.axis_size("wt"), lax.axis_index("wt")
    size = array.shape[axis] // count
    total = wide(take(array, place, axis, size))
    for shift in range(1, count):
        sent = take(array, (place + shift) % count, axis, size)
        total = total + wide(shift_wt(sent, shift))
    return total


def any_shards(
    tokens,
    doc_starts,
    attn_master,
    attn_mom,
    attn_sq,
    ffn_master,
    ffn_mom,
    ffn_sq,
    small_master,
    small_mom,
    small_sq,
    cotangent,
):
    ctx_count = lax.axis_size("ctx")
    ctx_place = lax.axis_index("ctx")
    wt_count = lax.axis_size("wt")
    batches, rows_here, width = tokens.shape
    heads = width // HS
    qkv_cols = width + 2 * HS
    all_rows = batches * rows_here
    shard_rows = attn_master.shape[0]
    piece_rows = shard_rows // ctx_count
    chunk = FF // ctx_count
    order = ctx_place ^ jnp.arange(ctx_count, dtype=jnp.int32)
    (
        gain_one,
        shift_one,
        gain_two,
        shift_two,
        bias_query,
        bias_out,
        bias_proj,
        bias_value,
        bias_hidden,
    ) = split_small(small_master)

    attn_piece = low(take(attn_master, ctx_place, 0, piece_rows))

    def whole_rows(piece):
        parts = whole_ctx(whole_wt(piece[None], 0))
        buffer = jnp.zeros((wt_count, ctx_count) + piece.shape, piece.dtype)
        for k, part in enumerate(parts):
            buffer = put(buffer, part[:, None], ctx_place ^ k, 1)
        return buffer.reshape((width,) + piece.shape[1:])

    weight_qkv = whole_rows(attn_piece[:, :qkv_cols])
    weight_out = whole_rows(attn_piece[:, qkv_cols:])
    ffn_piece = low(jnp.swapaxes(take(ffn_master, ctx_place, 2, chunk), 0, 1))
    ffn_parts = whole_ctx(whole_wt(ffn_piece, 1))
    bias_parts = bias_hidden.reshape(ctx_count, chunk)[order]

    stream = wide(tokens.reshape(all_rows, width))
    normed, norm_back_one = jax.vjp(layer_norm, stream, gain_one, shift_one)
    normed_low = low(normed)
    mixed = dot(normed_low, weight_qkv)
    queries = low(mixed[:, :width] + bias_query)
    kv_local = low(
        mixed[:, width:] + jnp.concatenate([jnp.zeros((HS,), jnp.float32), bias_value])
    ).reshape(batches, rows_here, 2 * HS)
    kv_parts = jnp.stack(whole_ctx(kv_local), axis=1).reshape(
        batches, ctx_count * rows_here, 2 * HS
    )
    keys_all, values_all = kv_parts[..., :HS], kv_parts[..., HS:]
    local_pos = jnp.arange(rows_here, dtype=jnp.int32)
    query_pos = ctx_place * rows_here + local_pos
    key_pos = (order[:, None] * rows_here + local_pos[None, :]).reshape(-1)
    queries = queries.reshape(batches, rows_here * heads, HS)
    scale = HS ** (-0.5)
    attended_list, log_list, allowed_list = [], [], []
    for b in range(batches):
        starts = doc_starts[b]
        query_doc = jnp.sum((starts[None, :] <= query_pos[:, None]).astype(jnp.int32), axis=1)
        key_doc = jnp.sum((starts[None, :] <= key_pos[:, None]).astype(jnp.int32), axis=1)
        allowed = (query_doc[:, None] == key_doc[None, :]) & (key_pos[None, :] <= query_pos[:, None])
        allowed = jnp.repeat(allowed, heads, axis=0)
        allowed_list.append(allowed)
        scores = jnp.where(allowed, cols_dot(queries[b], keys_all[b]) * scale, -1e30)
        peak = jnp.max(scores, axis=-1, keepdims=True)
        expo = jnp.exp(scores - peak)
        total = jnp.sum(expo, axis=-1, keepdims=True)
        attended_list.append(dot(low(expo / total), values_all[b]))
        log_list.append(peak + jnp.log(total))
    attended = jnp.stack(attended_list)
    attended_low = low(attended).reshape(all_rows, width)
    hidden = stream + dot(attended_low, weight_out) + bias_out
    normed_two, norm_back_two = jax.vjp(layer_norm, hidden, gain_two, shift_two)
    normed_two_low = low(normed_two)

    back_low = cotangent.reshape(all_rows, width)
    back_rows = wide(back_low)
    down_vals = jnp.zeros((all_rows, width), jnp.float32)
    grad_normed_two = jnp.zeros((all_rows, width), jnp.float32)
    ffn_grads, hidden_grads = [], []
    for k in range(ctx_count):
        weight_up, weight_down = ffn_parts[k][0], ffn_parts[k][1]
        value, slope = gelu_both(dot(normed_two_low, weight_up) + bias_parts[k])
        act = low(value)
        down_vals = down_vals + cols_dot(act, weight_down)
        grad_up = low(dot(back_low, weight_down) * slope)
        hidden_grads.append(jnp.sum(wide(grad_up), axis=0))
        grad_normed_two = grad_normed_two + cols_dot(grad_up, weight_up)
        ffn_grads.append(
            jnp.stack([low(rows_dot(normed_two_low, grad_up)), low(rows_dot(back_low, act))])
        )
    layer_out = low(hidden + down_vals + bias_proj).reshape(batches, rows_here, width)
    grad_bias_proj = jnp.sum(back_rows, axis=0)
    grad_bias_hidden = jnp.stack(hidden_grads)[order].reshape(FF)
    ffn_part = low(sum_wt(low(sum_ctx(ffn_grads)), 1))

    grad_hidden_part, grad_gain_two, grad_shift_two = norm_back_two(grad_normed_two)
    grad_hidden = back_rows + grad_hidden_part
    grad_bias_out = jnp.sum(grad_hidden, axis=0)
    grad_hidden_low = low(grad_hidden)
    grad_out = rows_dot(attended_low, grad_hidden_low)

    def summed_rows(grad):
        blocks = low(grad).reshape(wt_count, ctx_count, piece_rows, grad.shape[1])
        pieces = [take(blocks, ctx_place ^ k, 1, 1)[:, 0] for k in range(ctx_count)]
        part = low(sum_wt(low(sum_ctx(pieces)), 0)[0])
        buffer = jnp.zeros((ctx_count,) + part.shape, part.dtype)
        for k, got in enumerate(whole_ctx(part)):
            buffer = put(buffer, got[None], ctx_place ^ k, 0)
        return wide(buffer.reshape(shard_rows, grad.shape[1]))

    out_total = summed_rows(grad_out)

    grad_attended = low(cols_dot(grad_hidden_low, weight_out)).reshape(
        batches, rows_here * heads, HS
    )
    grad_query_list, grad_kv_list = [], []
    for b in range(batches):
        grads = grad_attended[b]
        delta = jnp.sum(wide(grads) * attended[b], axis=-1, keepdims=True)
        scores = jnp.where(allowed_list[b], cols_dot(queries[b], keys_all[b]) * scale, -1e30)
        weights = jnp.exp(scores - log_list[b])
        grad_scores = low(weights * (cols_dot(grads, values_all[b]) - delta))
        grad_query_list.append(low(dot(grad_scores, keys_all[b]) * scale))
        grad_kv_list.append(
            jnp.concatenate(
                [
                    low(rows_dot(grad_scores, queries[b]) * scale),
                    low(rows_dot(low(weights), grads)),
                ],
                axis=1,
            )
        )
    grad_query = jnp.stack(grad_query_list).reshape(all_rows, width)
    grad_kv = jnp.stack(grad_kv_list).reshape(batches, ctx_count, rows_here, 2 * HS)
    grad_kv_low = low(sum_ctx([grad_kv[:, k] for k in range(ctx_count)])).reshape(
        all_rows, 2 * HS
    )
    grad_bias_query = jnp.sum(wide(grad_query), axis=0)
    grad_bias_value = jnp.sum(wide(grad_kv_low[:, HS:]), axis=0)
    grad_mixed = jnp.concatenate([grad_query, grad_kv_low], axis=1)
    qkv_total = summed_rows(rows_dot(normed_low, grad_mixed))
    grad_normed = cols_dot(grad_mixed, weight_qkv)
    grad_stream_part, grad_gain_one, grad_shift_one = norm_back_one(grad_normed)
    input_grad = (grad_hidden + grad_stream_part).reshape(batches, rows_here, width)

    ffn_buffer = jnp.zeros((ctx_count,) + ffn_part.shape, ffn_part.dtype)
    for k, got in enumerate(whole_ctx(ffn_part)):
        ffn_buffer = put(ffn_buffer, got[None], ctx_place ^ k, 0)
    ffn_total = wide(jnp.transpose(ffn_buffer, (2, 1, 0, 3)).reshape(shard_rows, 2, FF))
    attn_total = jnp.concatenate([qkv_total, out_total], axis=1)
    grad_small = jnp.concatenate(
        [
            grad_gain_one,
            grad_shift_one,
            grad_gain_two,
            grad_shift_two,
            grad_bias_query,
            grad_bias_out,
            grad_bias_proj,
            grad_bias_value,
            grad_bias_hidden,
        ]
    )
    small_total = lax.psum(grad_small, ("ctx", "wt"))
    attn_new = adam_update(attn_master, attn_total, attn_mom, attn_sq, 0.1, 0.1)
    ffn_new = adam_update(ffn_master, ffn_total, ffn_mom, ffn_sq, 0.1, 0.1)
    small_new = adam_update(small_master, small_total, small_mom, small_sq, 1.0, 0.0)
    return (layer_out, input_grad) + attn_new + ffn_new + small_new


def solution(mesh):
    rows, cube = P("wt", None), P("wt", None, None)
    flow = P("wt", "ctx", None)
    in_specs = (flow, rows, rows, rows, rows, cube, cube, cube, P(), P(), P(), flow)
    out_specs = (flow, flow, rows, rows, rows, cube, cube, cube, P(), P(), P())
    ctx_count, wt_count = mesh.shape["ctx"], mesh.shape["wt"]
    fitted = (ctx_count, wt_count) == (8, 4)
    body = shards if fitted else any_shards
    return jax.shard_map(body, mesh=mesh, in_specs=in_specs, out_specs=out_specs, check_vma=False)
```

```python
import jax
import jax.numpy as jnp
from jax import lax
from jax.experimental import pallas as pl
from jax.experimental.pallas import tpu as pltpu
from jax.sharding import PartitionSpec as P

D = 768
HS = 64
FF = 3072
STEP = 10


NORM_EPS = 1e-05
GELU_COEF = 0.7978845608028654
GELU_CUBE = 0.044715
BETA_ONE = 0.9
BETA_TWO = 0.95
ADAM_EPS = 1e-08
VMEM_LIMIT = 22 << 20
NO_COST = pl.CostEstimate(flops=0, bytes_accessed=0, transcendentals=0)


def layer_norm(values, gain, shift):
    centre = values - jnp.mean(values, axis=-1, keepdims=True)
    spread = jnp.mean(centre * centre, axis=-1, keepdims=True)
    return centre * lax.rsqrt(spread + NORM_EPS) * gain + shift


def gelu_both(u):
    square = u * u
    share = 0.5 * jnp.tanh(u * (GELU_COEF * GELU_CUBE * square + GELU_COEF)) + 0.5
    bend = u * (6.0 * GELU_COEF * GELU_CUBE * square + 2.0 * GELU_COEF)
    return u * share, share * ((1.0 - share) * bend) + share


def split_small(small):
    return (
        small[0:D],
        small[D : 2 * D],
        small[2 * D : 3 * D],
        small[3 * D : 4 * D],
        small[4 * D : 5 * D],
        small[5 * D : 6 * D],
        small[6 * D : 7 * D],
        small[7 * D : 7 * D + HS],
        small[7 * D + HS :],
    )


def rows_dot(left, right):
    return lax.dot_general(
        left, right, (((0,), (0,)), ((), ())), preferred_element_type=jnp.float32
    )


def cols_dot(left, right):
    return lax.dot_general(
        left, right, (((1,), (1,)), ((), ())), preferred_element_type=jnp.float32
    )


def dot(left, right):
    return jnp.dot(left, right, preferred_element_type=jnp.float32)


def low(values):
    return values.astype(jnp.bfloat16)


def wide(values):
    return values.astype(jnp.float32)


def adam_update(master, gradient, first, second, step_rate, decay_rate):
    first_new = BETA_ONE * first + (1.0 - BETA_ONE) * gradient
    second_new = BETA_TWO * second + (1.0 - BETA_TWO) * gradient * gradient
    first_hat = first_new / (1.0 - BETA_ONE**STEP)
    second_hat = second_new / (1.0 - BETA_TWO**STEP)
    master_new = master - step_rate * (
        first_hat / (jnp.sqrt(second_hat) + ADAM_EPS) + decay_rate * master
    )
    return (first_new, second_new, master_new)


def xor_send(array, mask):
    count = lax.axis_size("ctx")
    return lax.ppermute(array, "ctx", [(i, i ^ mask) for i in range(count)])


def xor_wt(array, mask):
    count = lax.axis_size("wt")
    return lax.ppermute(array, "wt", [(i, i ^ mask) for i in range(count)])


class Steps:
    def __init__(self):
        self.last = ()

    def __call__(self, function, *args):
        flat, tree = jax.tree.flatten(args)
        held = lax.optimization_barrier(tuple(flat) + self.last)[: len(flat)]
        result = function(*jax.tree.unflatten(tree, held))
        self.last = tuple(jax.tree.leaves(result))
        return result


def loop(count, body, carry=0):
    return lax.fori_loop(0, count, body, carry)


def rows_at(i, size):
    return pl.ds(pl.multiple_of(i * size, size), size)


def together(*arrays):
    return lax.optimization_barrier(arrays)


def put(buffer, piece, place, axis):
    starts = [0] * buffer.ndim
    starts[axis] = place * piece.shape[axis]
    return lax.dynamic_update_slice(buffer, piece, starts)


def take(buffer, place, axis, size):
    return lax.dynamic_slice_in_dim(buffer, place * size, size, axis)


def attention_kernels(batches, rows, width, parts, runs):
    half_parts = parts // 2
    keys = parts * rows
    pair = 2 * HS
    groups = width // (2 * pair)
    factor = HS ** (-0.5) * 1.4426950408889634
    tile = 32

    def lanes(shape):
        return lax.broadcasted_iota(jnp.int32, shape, 1)

    def spread(even_ref, odd_ref, key_ref, value_ref):
        for j in range(parts):
            ref = even_ref if j < half_parts else odd_ref
            block = wide(ref[j % half_parts, 0])
            turned = pltpu.roll(block, HS, 1)
            first = lanes(block.shape) < HS
            here = pl.ds(j * rows, rows)
            key_ref[0, here, :] = low(jnp.where(first, block, 0.0))
            key_ref[1, here, :] = low(jnp.where(first, 0.0, turned))
            value_ref[0, here, :] = low(jnp.where(first, turned, 0.0))
            value_ref[1, here, :] = low(jnp.where(first, 0.0, block))

    def doc_begin(starts_ref, stream, positions):
        begin = jnp.zeros_like(positions)
        for j in range(starts_ref.shape[1]):
            start = starts_ref[stream, j]
            begin = jnp.where(start <= positions, jnp.maximum(begin, start), begin)
        return begin

    def forward(starts_ref, place_ref, query_ref, even_ref, odd_ref, low_ref, full_ref, log_ref, cap, key, value, weight):
        stream, place = pl.program_id(0), place_ref[0]
        spread(even_ref, odd_ref, key, value)
        query_pos = place * rows + lax.broadcasted_iota(jnp.int32, (rows, 1), 0)
        begin = doc_begin(starts_ref, stream, query_pos)
        for j in range(parts):
            key_pos = (place ^ (2 * (j % half_parts) + j // half_parts)) * rows + lax.broadcasted_iota(jnp.int32, (rows, rows), 1)
            allowed = (key_pos >= begin) & (key_pos <= query_pos)
            cap[:, j * rows : (j + 1) * rows] = jnp.where(allowed, 3.0e38, -1e30)
        column = lanes((tile, pair))
        logs = [jnp.zeros((tile, pair), jnp.float32) for _ in range(rows // tile)]
        for g in range(groups):
            at = g * 2 * pair
            two = jnp.concatenate([query_ref[0, :, at : at + pair], query_ref[0, :, at + pair : at + 2 * pair]], axis=0)
            totals = []
            for half in range(2):
                scores = cols_dot(two, key[half])
                norms = []
                for t in range(2 * rows // tile):
                    own = slice(t * tile, (t + 1) * tile)
                    n = t % (rows // tile)
                    part = jnp.minimum(scores[own] * factor, cap[n * tile : (n + 1) * tile, :])
                    peak = jnp.max(part, axis=1, keepdims=True)
                    expo = jnp.exp2(part - peak)
                    norm = jnp.sum(expo, axis=1, keepdims=True)
                    weight[half, own, :] = low(expo)
                    norms.append(norm)
                    head = 4 * g + 2 * (t * tile // rows) + half
                    logs[n] = jnp.where(column == head, peak + jnp.log2(norm), logs[n])
                totals.append(dot(weight[half], value[half]) / jnp.concatenate(norms, axis=0))
            total = totals[0] + totals[1]
            for j in range(2):
                part = total[j * rows : (j + 1) * rows]
                full_ref[0, :, at + j * pair : at + (j + 1) * pair] = part
                low_ref[0, :, at + j * pair : at + (j + 1) * pair] = low(part)
        for n, log in enumerate(logs):
            log_ref[0, n * tile : (n + 1) * tile, :] = log

    def backward(
        starts_ref, place_ref, query_ref, even_ref, odd_ref, full_ref, log_ref, grad_ref,
        query_grad_ref, even_grad_ref, odd_grad_ref,
        cap, key, value, key_turned, log_rows, delta_rows, weight_buf, score_buf, query_buf, grad_buf,
    ):
        stream, place = pl.program_id(0) + place_ref[1], place_ref[0]
        spread(even_ref, odd_ref, key, value)
        query_pos = place * rows + lax.broadcasted_iota(jnp.int32, (1, rows), 1)
        begin = doc_begin(starts_ref, stream, query_pos)
        for j in range(parts):
            key_pos = (place ^ (2 * (j % half_parts) + j // half_parts)) * rows + lax.broadcasted_iota(jnp.int32, (rows, rows), 0)
            allowed = (key_pos >= begin) & (key_pos <= query_pos)
            cap[j * rows : (j + 1) * rows, :] = jnp.where(allowed, 3.0e38, -1e30)
            here = pl.ds(j * rows, rows)
            key_turned[:, j * rows : (j + 1) * rows] = low(wide(key[0, here, :]).T[:HS])
        log_rows[...] = log_ref[0].T[: log_rows.shape[0]]
        head_of = lax.broadcasted_iota(jnp.int32, (delta_rows.shape[0], width), 1) // HS
        chosen = (head_of == lax.broadcasted_iota(jnp.int32, (delta_rows.shape[0], width), 0)).astype(jnp.float32)
        delta_rows[...] = lax.dot_general(
            chosen, wide(grad_ref[0]) * full_ref[0], (((1,), (1,)), ((), ())),
            precision=lax.Precision.HIGHEST, preferred_element_type=jnp.float32,
        )
        first = lanes((2 * rows, pair)) < HS
        for g in range(groups):
            at = g * 2 * pair
            both, both_grad = query_ref[0, :, at : at + 2 * pair], grad_ref[0, :, at : at + 2 * pair]
            two = jnp.concatenate([both[:, :pair], both[:, pair:]], axis=0)
            two_grad = jnp.concatenate([both_grad[:, :pair], both_grad[:, pair:]], axis=0)
            turned = []
            for half in range(2):
                h = 4 * g + half
                span = slice((2 * g + half) * 2 * rows, (2 * g + half + 1) * 2 * rows)
                keep = first if half == 0 else jnp.logical_not(first)
                query_buf[span, :] = low(jnp.where(keep, wide(two), 0.0))
                grad_buf[span, :] = low(jnp.where(keep, wide(two_grad), 0.0))
                log = jnp.concatenate([log_rows[h : h + 1, :], log_rows[h + 2 : h + 3, :]], axis=1)
                delta = jnp.concatenate([delta_rows[h : h + 1, :], delta_rows[h + 2 : h + 3, :]], axis=1)
                scores, weight_grads = cols_dot(key[half], two), cols_dot(value[half], two_grad)
                for t in range(keys // (2 * tile)):
                    own = slice(t * 2 * tile, (t + 1) * 2 * tile)
                    limit = cap[own, :]
                    limit = jnp.concatenate([limit, limit], axis=1)
                    weights = jnp.exp2(jnp.minimum(scores[own] * factor, limit) - log)
                    weight_buf[own, span] = low(weights)
                    score_buf[own, span] = low(weights * (weight_grads[own] - delta))
                turned.append(dot(key_turned[...], score_buf[:, span]))
            turned = jnp.concatenate(turned, axis=0) * HS ** (-0.5)
            query_grad_ref[0, :, at : at + pair] = low(turned[:, :rows].T)
            query_grad_ref[0, :, at + pair : at + 2 * pair] = low(turned[:, rows:].T)
        for j in range(parts):
            here = pl.ds(j * rows, rows)
            value_sum = dot(weight_buf[here, :], grad_buf[...])
            key_sum = dot(score_buf[here, :], query_buf[...]) * HS ** (-0.5)
            value_sum = value_sum + pltpu.roll(value_sum, HS, 1)
            key_sum = key_sum + pltpu.roll(key_sum, HS, 1)
            ref = even_grad_ref if j < half_parts else odd_grad_ref
            ref[j % half_parts, 0] = low(jnp.where(lanes((rows, pair)) < HS, key_sum, value_sum))

    def specs(first):
        return (
            pl.BlockSpec((1, rows, width), lambda b, *_: (b + first, 0, 0)),
            pl.BlockSpec((1, rows, pair), lambda b, *_: (b + first, 0, 0)),
            pl.BlockSpec((half_parts, 1, rows, pair), lambda b, *_: (0, b + first, 0, 0)),
        )

    flow, logs, blocks = specs(0)

    shared = [
        pltpu.VMEM((2, keys, pair), jnp.bfloat16),
        pltpu.VMEM((2, keys, pair), jnp.bfloat16),
    ]
    run_forward = pl.pallas_call(
        forward,
        grid_spec=pltpu.PrefetchScalarGridSpec(
            num_scalar_prefetch=2,
            grid=(batches,),
            in_specs=[flow, blocks, blocks],
            out_specs=[flow, flow, logs],
            scratch_shapes=[pltpu.VMEM((rows, keys), jnp.float32)]
            + shared
            + [pltpu.VMEM((2, 2 * rows, keys), jnp.bfloat16)],
        ),
        out_shape=[
            jax.ShapeDtypeStruct((batches, rows, width), jnp.bfloat16),
            jax.ShapeDtypeStruct((batches, rows, width), jnp.float32),
            jax.ShapeDtypeStruct((batches, rows, pair), jnp.float32),
        ],
        compiler_params=pltpu.CompilerParams(vmem_limit_bytes=VMEM_LIMIT),
        cost_estimate=NO_COST,
        name="attention_forward",
    )
    head_rows = -(-(width // HS) // 8) * 8
    all_columns = rows * (width // HS)
    count = batches // runs

    def call_backward(run):
        here_flow, here_logs, here_blocks = specs(run * count)
        return pl.pallas_call(
        backward,
        grid_spec=pltpu.PrefetchScalarGridSpec(
            num_scalar_prefetch=2,
            grid=(count,),
            in_specs=[here_flow, here_blocks, here_blocks, here_flow, here_logs, here_flow],
            out_specs=[flow, blocks, blocks],
            scratch_shapes=[pltpu.VMEM((keys, rows), jnp.float32)]
            + shared
            + [
                pltpu.VMEM((HS, keys), jnp.bfloat16),
                pltpu.VMEM((head_rows, rows), jnp.float32),
                pltpu.VMEM((head_rows, rows), jnp.float32),
                pltpu.VMEM((keys, all_columns), jnp.bfloat16),
                pltpu.VMEM((keys, all_columns), jnp.bfloat16),
                pltpu.VMEM((all_columns, pair), jnp.bfloat16),
                pltpu.VMEM((all_columns, pair), jnp.bfloat16),
            ],
        ),
        out_shape=[
            jax.ShapeDtypeStruct((count, rows, width), jnp.bfloat16),
            jax.ShapeDtypeStruct((half_parts, count, rows, pair), jnp.bfloat16),
            jax.ShapeDtypeStruct((half_parts, count, rows, pair), jnp.bfloat16),
        ],
        compiler_params=pltpu.CompilerParams(vmem_limit_bytes=VMEM_LIMIT),
        cost_estimate=NO_COST,
        name="attention_backward",
    )

    return run_forward, [call_backward(run) for run in range(runs)]


def in_hbm(arrays):
    return [pltpu.with_memory_space_constraint(array, pltpu.HBM) for array in arrays]


def ffn_kernels(rows, width, chunk, wt_count):
    units = 2 * chunk
    all_rows = 2 * rows
    block_rows = width // wt_count
    hbm = pl.BlockSpec(memory_space=pltpu.HBM)
    vmem = pl.BlockSpec(memory_space=pltpu.VMEM)
    params = pltpu.CompilerParams(vmem_limit_bytes=VMEM_LIMIT)

    def fetch(weights, which, held, sem):
        copies = []
        for n, arrays in enumerate(weights):
            blocks = [array.at[block] for array in arrays for block in range(array.shape[0])]
            for row, block in enumerate(blocks):
                copies.append(
                    pltpu.make_async_copy(
                        block.at[pl.ds(which * block_rows, block_rows), :],
                        held.at[pl.ds(row * block_rows, block_rows), pl.ds(n * chunk, chunk)],
                        sem.at[len(copies)],
                    )
                )
        for copy in copies:
            copy.start()
        return copies

    def send(pairs, sems):
        copies = [pltpu.make_async_copy(source, out, sems.at[n]) for n, (source, out) in enumerate(pairs)]
        for copy in copies:
            copy.start()
        return copies

    part_rows = 256
    tile = 16

    def units_of(inputs, grads, bias, held_up, held_down, act, grad_units):
        sums = jnp.zeros((8, units), jnp.float32)
        for s in range(2):

            def part(i, sums):
                here = rows_at(i, part_rows)
                up = dot(inputs[s][here, :], held_up[...])
                act_grad = dot(grads[s][here, :], held_down[...])
                for t in range(part_rows // tile):
                    own = slice(t * tile, (t + 1) * tile)
                    there = pl.ds(pl.multiple_of(s * rows + i * part_rows + t * tile, tile), tile)
                    value, slope = gelu_both(up[own] + bias)
                    grad = act_grad[own] * slope
                    act[there, :] = low(value)
                    grad_units[there, :] = low(grad)
                    sums = sums + (grad[:8] + grad[8:])
                return sums

            sums = loop(rows // part_rows, part, sums)
        return jnp.sum(sums, axis=0, keepdims=True)

    def product_of(turned, right, product):
        def part(i, carry):
            here = rows_at(i, part_rows)
            product[here, :] = low(dot(turned[here, :], right[...]))
            return carry

        loop(width // part_rows, part)

    def back_to(refs, sources, weights):
        for s, ref in enumerate(refs):

            def part(i, carry):
                here = pl.ds(pl.multiple_of(s * rows + i * part_rows, part_rows), part_rows)
                total = cols_dot(sources[0][here, :], weights[0][...]) + cols_dot(sources[1][here, :], weights[1][...])
                ref[rows_at(i, part_rows), :] = total.astype(ref.dtype)
                return carry

            loop(rows // part_rows, part)

    def halves(product, m):
        cols = pl.ds(m * chunk, chunk)
        return [product.at[pl.ds(h * width // 2, width // 2), cols] for h in range(2)]

    def first(
        own, other, grad_own, grad_other, turned, bias, w0, w1, w2, w3,
        act_out, units_out, out_a, out_b, sums_out,
        held_up, held_down, act, grad_units, product, sems, out_sems,
    ):
        weights = ((w0, w1), (w2, w3))
        copies = fetch(weights, 0, held_up, sems.at[0]) + fetch(weights, 1, held_down, sems.at[1])
        for copy in copies:
            copy.wait()
        sums_out[...] = units_of((own, other), (grad_own, grad_other), bias[...], held_up, held_down, act, grad_units)
        sent = send(((act, act_out), (grad_units, units_out)), out_sems.at[0])
        product_of(turned, act, product)
        sent += send(
            ((product.at[:, pl.ds(0, chunk)], out_a), (product.at[:, pl.ds(chunk, chunk)], out_b)), out_sems.at[1]
        )
        for copy in sent:
            copy.wait()

    def second(
        own, other, grad_own, grad_other, turned, bias, units_first, w0, w1, w2, w3, w4, w5, w6, w7,
        act_out, units_out, out_a, out_b, out_c, sums_out, back_own, back_other,
        held_up, held_more, held_down, act, grad_units, more_units, product, sems, out_sems, more_sem,
    ):
        weights, before = ((w4, w5), (w6, w7)), ((w0, w1), (w2, w3))
        copies = fetch(weights, 0, held_up, sems.at[0]) + fetch(weights, 1, held_down, sems.at[1])
        more = fetch(before, 0, held_more, sems.at[2])
        more.append(pltpu.make_async_copy(units_first, more_units, more_sem))
        more[-1].start()
        for copy in copies:
            copy.wait()
        sums_out[...] = units_of((own, other), (grad_own, grad_other), bias[...], held_up, held_down, act, grad_units)
        sent = send(((act, act_out), (grad_units, units_out)), out_sems.at[0])
        product_of(turned, act, product)
        top, bottom = halves(product, 1)
        sent += send(((product.at[:, pl.ds(0, chunk)], out_a), (top, out_b), (bottom, out_c)), out_sems.at[1])
        for copy in more:
            copy.wait()
        back_to((back_own, back_other), (grad_units, more_units), (held_up, held_more))
        for copy in sent:
            copy.wait()

    def third(own, other, units_a, units_b, out_0, out_1, out_2, out_3, out_4, turned, held, products, sems, out_sems):
        copies = send(((units_a, held.at[0]), (units_b, held.at[1])), sems)
        turn((own, other), turned)
        for copy in copies:
            copy.wait()
        products[1] = low(dot(turned[...], held[1]))
        top, bottom = halves(products.at[1], 1)
        sent = send(((products.at[1, :, pl.ds(0, chunk)], out_2), (top, out_3), (bottom, out_4)), out_sems.at[0])
        products[0] = low(dot(turned[...], held[0]))
        sent += send(
            ((products.at[0, :, pl.ds(0, chunk)], out_0), (products.at[0, :, pl.ds(chunk, chunk)], out_1)),
            out_sems.at[1],
        )
        for copy in sent:
            copy.wait()

    def down(act_a, act_b, w0, w1, w2, w3, w4, w5, w6, w7, own_ref, other_ref, held_a, held_b, sems):
        copies = fetch(((w0, w1), (w2, w3)), 1, held_a, sems.at[0]) + fetch(((w4, w5), (w6, w7)), 1, held_b, sems.at[1])
        for copy in copies:
            copy.wait()
        for s, ref in enumerate((own_ref, other_ref)):
            here = slice(s * rows, (s + 1) * rows)
            total = cols_dot(act_a[here, :], held_a[...]) + cols_dot(act_b[here, :], held_b[...])
            ref[...] = total.astype(ref.dtype)

    dma = pltpu.SemaphoreType.DMA
    held = pltpu.VMEM((width, units), jnp.bfloat16)
    flow = pltpu.VMEM((all_rows, units), jnp.bfloat16)
    flow_out = pltpu.HBM((all_rows, units), jnp.bfloat16)
    whole = pltpu.HBM((width, chunk), jnp.bfloat16)
    part = pltpu.HBM((width // 2, chunk), jnp.bfloat16)
    sums = jax.ShapeDtypeStruct((1, units), jnp.float32)
    own = jax.ShapeDtypeStruct((rows, width), jnp.float32)
    other = jax.ShapeDtypeStruct((rows, width), jnp.bfloat16)
    run_first = pl.pallas_call(
        first,
        in_specs=[vmem] * 6 + [hbm] * 4,
        out_specs=[hbm] * 4 + [vmem],
        out_shape=[flow_out, flow_out, whole, whole, sums],
        scratch_shapes=[held, held, flow, flow, held, dma((2, 2 * wt_count)), dma((2, 2))],
        compiler_params=params,
        cost_estimate=NO_COST,
        name="ffn_first",
    )
    run_second = pl.pallas_call(
        second,
        in_specs=[vmem] * 6 + [hbm] * 9,
        out_specs=[hbm] * 5 + [vmem] * 3,
        out_shape=[flow_out, flow_out, whole, part, part, sums, own, other],
        scratch_shapes=[held, held, held, flow, flow, flow, held, dma((3, 2 * wt_count)), dma((2, 3)), dma(())],
        compiler_params=params,
        cost_estimate=NO_COST,
        name="ffn_second",
    )
    run_third = pl.pallas_call(
        third,
        in_specs=[vmem] * 2 + [hbm] * 2,
        out_specs=[hbm] * 5,
        out_shape=[whole, whole, whole, part, part],
        scratch_shapes=[
            pltpu.VMEM((width, all_rows), jnp.bfloat16),
            pltpu.VMEM((2, all_rows, units), jnp.bfloat16),
            pltpu.VMEM((2, width, units), jnp.bfloat16),
            dma((2,)),
            dma((2, 3)),
        ],
        compiler_params=params,
        cost_estimate=NO_COST,
        name="ffn_grads",
    )
    run_down = pl.pallas_call(
        down,
        in_specs=[vmem] * 2 + [hbm] * 8,
        out_specs=[vmem] * 2,
        out_shape=[own, other],
        scratch_shapes=[held, held, dma((2, 2 * wt_count))],
        compiler_params=params,
        cost_estimate=NO_COST,
        name="ffn_down",
    )
    return run_first, run_second, run_third, run_down


def turn(refs, turned):
    rows = refs[0].shape[0]
    for s, ref in enumerate(refs):
        for i in range(rows // 128):
            block = wide(ref[i * 128 : (i + 1) * 128, :])
            turned[:, s * rows + i * 128 : s * rows + (i + 1) * 128] = low(block.T)


def turn_both(own, other):
    vmem = pl.BlockSpec(memory_space=pltpu.VMEM)
    rows, width = own.shape
    return pl.pallas_call(
        lambda a, b, out: turn((a, b), out),
        in_specs=[vmem] * 2,
        out_specs=vmem,
        out_shape=jax.ShapeDtypeStruct((width, 2 * rows), own.dtype),
        compiler_params=pltpu.CompilerParams(vmem_limit_bytes=VMEM_LIMIT),
        cost_estimate=NO_COST,
        name="turn",
    )(own, other)


def out_projection(rows, width):
    tile = 32

    def kernel(attended, weight, stream, bias, gain, shift, hidden_ref, normed_ref):
        product = dot(attended[...], weight[...])
        for t in range(rows // tile):
            here = slice(t * tile, (t + 1) * tile)
            hidden = wide(stream[here, :]) + product[here] + bias[...]
            hidden_ref[here, :] = hidden
            normed_ref[here, :] = low(layer_norm(hidden, gain[...], shift[...]))

    vmem = pl.BlockSpec(memory_space=pltpu.VMEM)
    return pl.pallas_call(
        kernel,
        in_specs=[vmem] * 6,
        out_specs=[vmem] * 2,
        out_shape=[
            jax.ShapeDtypeStruct((rows, width), jnp.float32),
            jax.ShapeDtypeStruct((rows, width), jnp.bfloat16),
        ],
        compiler_params=pltpu.CompilerParams(vmem_limit_bytes=VMEM_LIMIT),
        cost_estimate=NO_COST,
        name="out_projection",
    )


def norm_back(values, gain, grad):
    centre = values - jnp.mean(values, axis=-1, keepdims=True)
    scale = lax.rsqrt(jnp.mean(centre * centre, axis=-1, keepdims=True) + NORM_EPS)
    unit = centre * scale
    inner = grad * gain
    mean = jnp.mean(inner, axis=-1, keepdims=True)
    along = jnp.mean(inner * unit, axis=-1, keepdims=True)
    return scale * (inner - mean - unit * along), grad * unit


def fold_rows(values):
    total = values[:8]
    for i in range(1, values.shape[0] // 8):
        total = total + values[i * 8 : (i + 1) * 8]
    return total


def hidden_back(rows, width):
    tile = 32

    def kernel(own, got, hidden, back, gain, weight, grad_ref, low_ref, attended_ref, sums_ref):
        sums = [jnp.zeros((8, width), jnp.float32) for _ in range(3)]
        for t in range(rows // tile):
            here = slice(t * tile, (t + 1) * tile)
            pulled, terms = norm_back(hidden[here, :], gain[...], own[here, :] + wide(got[here, :]))
            grad = wide(back[here, :]) + pulled
            grad_ref[here, :] = grad
            low_ref[here, :] = low(grad)
            for n, part in enumerate((terms, own[here, :] + wide(got[here, :]), grad)):
                sums[n] = sums[n] + fold_rows(part)
        for n in range(3):
            sums_ref[n : n + 1, :] = jnp.sum(sums[n], axis=0, keepdims=True)
        attended_ref[...] = low(cols_dot(low_ref[...], weight[...]))

    vmem = pl.BlockSpec(memory_space=pltpu.VMEM)
    return pl.pallas_call(
        kernel,
        in_specs=[vmem] * 6,
        out_specs=[vmem] * 4,
        out_shape=[
            jax.ShapeDtypeStruct((rows, width), jnp.float32),
            jax.ShapeDtypeStruct((rows, width), jnp.bfloat16),
            jax.ShapeDtypeStruct((rows, width), jnp.bfloat16),
            jax.ShapeDtypeStruct((3, width), jnp.float32),
        ],
        compiler_params=pltpu.CompilerParams(vmem_limit_bytes=VMEM_LIMIT),
        cost_estimate=NO_COST,
        name="hidden_back",
    )


def stream_back(rows, width, parts, row_groups, piece):
    tile = 32
    chips = parts // 2

    def kernel(
        place_ref, kv_0, kv_1, kv_2, kv_3, queries, weight, tokens, gain, grad_hidden, normed, back, hidden_sums,
        units_a, units_b, input_ref, even_ref, odd_ref, grad_kv, grads, turned, product, small,
    ):
        place = place_ref[0]
        sums = [jnp.zeros((8, width), jnp.float32) for _ in range(4)]
        value_sums = jnp.zeros((8, 2 * HS), jnp.float32)
        for t in range(rows // tile):
            here = slice(t * tile, (t + 1) * tile)
            total = wide(kv_0[here, :]) + wide(kv_1[here, :]) + wide(kv_2[here, :]) + wide(kv_3[here, :])
            grad_kv[here, :] = low(total)
            value_sums = value_sums + fold_rows(total)
        turn((normed,), turned)
        product[...] = dot(turned[...], grad_kv[...])
        grads[...] = cols_dot(queries[...], weight[:, :width]) + cols_dot(grad_kv[...], weight[:, width:])
        for t in range(rows // tile):
            here = slice(t * tile, (t + 1) * tile)
            grad = grads[here, :]
            pulled, terms = norm_back(wide(tokens[here, :]), gain[...], grad)
            input_ref[here, :] = grad_hidden[here, :] + pulled
            for n, part in enumerate((terms, grad, wide(queries[here, :]), wide(back[here, :]))):
                sums[n] = sums[n] + fold_rows(part)
        sums = [jnp.sum(part, axis=0, keepdims=True) for part in sums]
        small[...] = jnp.zeros_like(small)
        rows_in = (sums[0], sums[1], hidden_sums[0:1, :], hidden_sums[1:2, :], sums[2], hidden_sums[2:3, :], sums[3])
        for n, row in enumerate(rows_in):
            for j in range(width // 128):
                line = n * (width // 128) + j
                small[line : line + 1, :] = row[:, j * 128 : (j + 1) * 128]
        start = 7 * (width // 128)
        small[start : start + 1, :] = jnp.sum(value_sums, axis=0, keepdims=True)
        lines = FF // parts // 128
        for m in range(chips):
            units = (units_a, units_b)[m // 2]
            for j in range(lines):
                line = start + 1 + (place ^ (2 * m)) * lines + j
                at = (m % 2 * lines + j) * 128
                small[pl.ds(line, 1), :] = units[:, at : at + 128]
        for k in range(parts):
            ref = odd_ref if k % 2 else even_ref
            mine = low(small[pl.ds(pl.multiple_of((place ^ k) * piece, 8), piece), :])
            for w in range(row_groups):
                at = pl.multiple_of(w * piece * parts + (place ^ k) * piece, 8)
                ref[k // 2, w, :, :128] = low(product[pl.ds(at, piece), :])
                ref[k // 2, w, :, 128:] = mine

    vmem = pl.BlockSpec(memory_space=pltpu.VMEM)
    stack = jax.ShapeDtypeStruct((chips, row_groups, piece, 256), jnp.bfloat16)
    return pl.pallas_call(
        kernel,
        in_specs=[pl.BlockSpec(memory_space=pltpu.SMEM)] + [vmem] * 14,
        out_specs=[vmem] * 3,
        out_shape=[jax.ShapeDtypeStruct((rows, width), jnp.float32), stack, stack],
        scratch_shapes=[
            pltpu.VMEM((rows, 2 * HS), jnp.bfloat16),
            pltpu.VMEM((rows, width), jnp.float32),
            pltpu.VMEM((width, rows), jnp.bfloat16),
            pltpu.VMEM((width, 2 * HS), jnp.float32),
            pltpu.VMEM((parts * piece, 128), jnp.float32),
        ],
        compiler_params=pltpu.CompilerParams(vmem_limit_bytes=VMEM_LIMIT),
        cost_estimate=NO_COST,
        name="stream_back",
    )


def attn_grads(rows, width, row_groups, parts, piece):
    def kernel(place_ref, left_a, right_a, left_b, right_b, even_ref, odd_ref, turned, total):
        place = place_ref[0]
        for n, (left, right) in enumerate(((left_a, right_a), (left_b, right_b))):
            for i in range(rows // 128):
                turned[:, i * 128 : (i + 1) * 128] = low(wide(left[i * 128 : (i + 1) * 128, :]).T)
            total[:, n * width : (n + 1) * width] = dot(turned[...], right[...])
        for k in range(parts):
            ref = odd_ref if k % 2 else even_ref
            for w in range(row_groups):
                at = pl.multiple_of(w * piece * parts + (place ^ k) * piece, 8)
                ref[k // 2, w] = low(total[pl.ds(at, piece), :])

    vmem = pl.BlockSpec(memory_space=pltpu.VMEM)
    shape = jax.ShapeDtypeStruct((parts // 2, row_groups, piece, 2 * width), jnp.bfloat16)
    return pl.pallas_call(
        kernel,
        grid_spec=pltpu.PrefetchScalarGridSpec(
            num_scalar_prefetch=1,
            grid=(),
            in_specs=[vmem] * 4,
            out_specs=[vmem] * 2,
            scratch_shapes=[pltpu.VMEM((width, rows), jnp.bfloat16), pltpu.VMEM((width, 2 * width), jnp.float32)],
        ),
        out_shape=[shape] * 2,
        compiler_params=pltpu.CompilerParams(vmem_limit_bytes=VMEM_LIMIT),
        cost_estimate=NO_COST,
        name="attn_grads",
    )


def attn_update(rows, columns, width, parts, piece):
    qkv = columns - width
    whole = columns + 128 * -(-(7 * width + HS + FF) // (128 * piece * parts))

    def kernel(place_ref, even_ref, odd_ref, master, first, second, *outs):
        core = place_ref[0] % 2
        for ref, which in ((even_ref, core), (odd_ref, 1 - core)):
            here = pl.ds(pl.multiple_of(which * piece, 8), piece)
            for cols, source in (
                (slice(0, width), slice(0, width)),
                (slice(width, qkv), slice(2 * width, columns)),
                (slice(qkv, columns), slice(width, 2 * width)),
            ):
                grad = wide(ref[0, :, source])
                got = adam_update(master[here, cols], grad, first[here, cols], second[here, cols], 0.1, 0.1)
                outs[0][here, cols] = got[0]
                outs[1][here, cols] = got[1]
                outs[2][here, cols] = got[2]

    block = pl.BlockSpec((2 * piece, columns), lambda i, place: (i, 0))
    stack = pl.BlockSpec((1, piece, whole), lambda i, place: (i ^ (place[0] // 2), 0, 0))
    return pl.pallas_call(
        kernel,
        grid_spec=pltpu.PrefetchScalarGridSpec(
            num_scalar_prefetch=1,
            grid=(parts // 2,),
            in_specs=[stack] * 2 + [block] * 3,
            out_specs=[block] * 3,
            scratch_shapes=[],
        ),
        out_shape=[jax.ShapeDtypeStruct((rows, columns), jnp.float32)] * 3,
        compiler_params=pltpu.CompilerParams(vmem_limit_bytes=VMEM_LIMIT),
        cost_estimate=NO_COST,
        name="attn_update",
    )


def ffn_update(rows, units, parts, chunk):
    per_row = 2 * units // 128
    rows_once = 32
    lines = rows_once * per_row

    def kernel(place_ref, even, odd, master, first, second, first_out, second_out, master_out, total):
        place = place_ref[0]
        for k in range(parts):
            grad = odd if k % 2 else even
            for j in range(chunk // 128):
                for which in range(2):
                    line = (place ^ k) * (2 * chunk // 128) + 2 * j + which
                    total[pl.ds(line, rows_once, per_row), :] = wide(
                        grad[k // 2, which, :, j * 128 : (j + 1) * 128]
                    )
        for t in range(lines // 64):
            own = slice(t * 64, (t + 1) * 64)
            got = adam_update(master[own, :], total[own, :], first[own, :], second[own, :], 0.1, 0.1)
            first_out[own, :] = got[0]
            second_out[own, :] = got[1]
            master_out[own, :] = got[2]

    block = pl.BlockSpec((lines, 128), lambda i, *_: (i, 0))
    stack = pl.BlockSpec((parts // 2, 2, rows_once, chunk), lambda i, *_: (0, 0, i, 0))
    call = pl.pallas_call(
        kernel,
        grid_spec=pltpu.PrefetchScalarGridSpec(
            num_scalar_prefetch=1,
            grid=(rows // rows_once,),
            in_specs=[stack] * 2 + [block] * 3,
            out_specs=[block] * 3,
            scratch_shapes=[pltpu.VMEM((lines, 128), jnp.float32)],
        ),
        out_shape=[jax.ShapeDtypeStruct((rows * per_row, 128), jnp.float32)] * 3,
        compiler_params=pltpu.CompilerParams(vmem_limit_bytes=VMEM_LIMIT),
        cost_estimate=NO_COST,
        name="ffn_update",
    )

    def fold(array):
        return jnp.swapaxes(array.reshape(rows, 2, units // 128, 128), 1, 2).reshape(-1, 128)

    def unfold(array):
        return jnp.swapaxes(array.reshape(rows, units // 128, 2, 128), 1, 2).reshape(rows, 2, units)

    def run(place, even, odd, master, first, second):
        return tuple(unfold(array) for array in call(place, even, odd, fold(master), fold(first), fold(second)))

    return run


def shards(
    tokens,
    doc_starts,
    attn_master,
    attn_mom,
    attn_sq,
    ffn_master,
    ffn_mom,
    ffn_sq,
    small_master,
    small_mom,
    small_sq,
    cotangent,
):
    ctx_count, wt_count = lax.axis_size("ctx"), lax.axis_size("wt")
    ctx_place, wt_place = lax.axis_index("ctx"), lax.axis_index("wt")
    batches, rows_here, width = tokens.shape
    qkv_cols = width + 2 * HS
    attn_columns = attn_master.shape[1]
    all_rows = batches * rows_here
    shard_rows = attn_master.shape[0]
    piece_rows = shard_rows // ctx_count
    chunk = FF // ctx_count
    chips = ctx_count // 2
    order = ctx_place ^ jnp.arange(ctx_count, dtype=jnp.int32)
    runs = 2 if batches % 2 == 0 else 1
    places = [jnp.stack([ctx_place, jnp.int32(run * (batches // runs))]) for run in range(runs)]
    place = places[0]
    wt_half = wt_count // 2
    out_rows = shard_rows // chips
    run_forward, run_backward = attention_kernels(batches, rows_here, width, ctx_count, runs)
    ffn_first, ffn_second, ffn_third, ffn_down = ffn_kernels(all_rows, width, chunk, wt_count)
    step = Steps()

    def both(own, got, place, bit, axis=0):
        ahead, behind = jnp.stack([own, got], axis), jnp.stack([got, own], axis)
        return jnp.where((place & bit) == 0, ahead, behind)

    def in_order(even, odd):
        buffer = jnp.zeros((ctx_count,) + even.shape[1:], even.dtype)
        for m in range(chips):
            buffer = put(buffer, even[m][None], ctx_place ^ (2 * m), 0)
            buffer = put(buffer, odd[m][None], ctx_place ^ (2 * m + 1), 0)
        return buffer

    def send_chips(piece):
        return [xor_send(piece, mask) for mask in range(2, ctx_count, 2)]

    def split_wt(total, bit):
        pairs = total.reshape((-1, 2) + total.shape[1:]) if bit == 1 else total[None]
        ahead, behind = pairs[:, 0], pairs[:, 1]
        here = (wt_place & bit) == 0
        return jnp.where(here, ahead, behind), jnp.where(here, behind, ahead)

    def add_low(*arrays):
        return low(sum(wide(array) for array in arrays))

    qkv = low(lax.dynamic_slice(attn_master, (ctx_place * piece_rows, 0), (piece_rows, qkv_cols)))
    out_start = (ctx_place // 2 * out_rows, qkv_cols + ctx_place % 2 * chunk)
    out = low(lax.dynamic_slice(attn_master, out_start, (out_rows, chunk)))
    rest = low(jnp.swapaxes(take(ffn_master, ctx_place, 2, chunk), 0, 1).reshape(2 * shard_rows, chunk))
    qkv_got, out_got = xor_wt(qkv, 2), xor_wt(out, 2)
    qkv_got, out_got, rest = together(qkv_got, out_got, rest)
    ups, downs = rest[:shard_rows], rest[shard_rows:]
    ups_got = xor_wt(ups, 2)
    qkv, out = both(qkv, qkv_got, wt_place, 2), both(out, out_got, wt_place, 2)
    qkv, out, small_late = together(qkv, out, small_master)
    qkv_got, out_got = xor_wt(qkv, 1), xor_wt(out, 1)
    back_low = cotangent.reshape(all_rows, width)
    qkv_got, out_got, ups_got, downs = together(qkv_got, out_got, ups_got, downs)
    downs_got = xor_wt(downs, 2)
    qkv = both(qkv, qkv_got, wt_place, 1, 1).reshape((wt_count,) + qkv.shape[1:])
    qkv_got = send_chips(qkv)
    back_other = xor_send(back_low, 1)
    flat_tokens, qkv, small_late = together(tokens.reshape(all_rows, width), qkv, small_late)
    (
        gain_one,
        shift_one,
        gain_two,
        shift_two,
        bias_query,
        bias_out,
        bias_proj,
        bias_value,
        bias_hidden,
    ) = split_small(small_late)
    normed_low = low(layer_norm(wide(flat_tokens), gain_one, shift_one))
    bias_parts = bias_hidden.reshape(ctx_count, chunk)[order[::2]].reshape(1, chips * chunk)
    bias_near, bias_far = jnp.split(bias_parts, 2, axis=1)
    ups = both(ups, ups_got, wt_place, 2)
    *qkv_got, normed_low, bias_near, bias_far, back_other, downs_got, ups = together(
        *qkv_got, normed_low, bias_near, bias_far, back_other, downs_got, ups
    )
    ups_got = xor_wt(ups, 1)
    out = both(out, out_got, wt_place, 1, 1).reshape((wt_count,) + out.shape[1:])
    qkv_even, out = together(jnp.stack([qkv] + qkv_got), out)
    qkv_odd = xor_send(qkv_even, 1)
    out_got = send_chips(out)
    blocks = both(qkv_even, qkv_odd, ctx_place, 1, 1)
    for n in range(chips.bit_length() - 1):
        pairs = blocks.reshape((-1, 2, 1 << n) + blocks.shape[1:])
        blocks = jnp.where((ctx_place & (2 << n)) == 0, pairs, pairs[:, ::-1]).reshape(blocks.shape)
    weight_qkv = jnp.transpose(blocks, (2, 0, 1, 3, 4)).reshape(width, qkv_cols)
    mixed = dot(normed_low, weight_qkv)
    queries = low(mixed[:, :width] + bias_query).reshape(batches, rows_here, width)
    kv_bias = jnp.concatenate([jnp.zeros((HS,), jnp.float32), bias_value])
    kv_local = low(mixed[:, width:] + kv_bias).reshape(batches, rows_here, 2 * HS)
    back_turned = turn_both(back_low, back_other)
    downs = both(downs, downs_got, wt_place, 2)
    kv_local, back_turned, ups_got, downs, *out_got = together(kv_local, back_turned, ups_got, downs, *out_got)
    downs_got = xor_wt(downs, 1)
    kv_got = send_chips(kv_local)
    out_even = jnp.stack([out] + out_got)
    *kv_got, out_even, downs_got = together(*kv_got, out_even, downs_got)
    out_odd = xor_send(out_even, 1)
    kv_even = jnp.stack([kv_local] + kv_got)
    kv_odd = xor_send(kv_even, 1)
    rest = jnp.concatenate([both(ups, ups_got, wt_place, 1, 1), both(downs, downs_got, wt_place, 1, 1)], axis=2)
    rest_low, rest_high = rest[0], rest[1]
    low_x, high_y, high_x, low_y = xor_send(rest_low, 2), xor_send(rest_high, 4), xor_send(rest_high, 2), xor_send(rest_low, 4)
    queries, rest_low, rest_high = together(queries, rest_low, rest_high)

    attended_low, attended, logs = step(run_forward, doc_starts, place, queries, kv_even, kv_odd)
    attended_low = attended_low.reshape(all_rows, width)
    attended_low, low_x, high_y, high_x, low_y = together(attended_low, low_x, high_y, high_x, low_y)
    low_diagonal, high_diagonal = xor_send(low_x, 4), xor_send(high_y, 2)

    def join_out(even, odd):
        columns = jnp.where((ctx_place & 1) == 0, jnp.concatenate([even, odd], axis=3), jnp.concatenate([odd, even], axis=3))
        for n in range(chips.bit_length() - 1):
            pairs = columns.reshape((-1, 2, 1 << n) + columns.shape[1:])
            columns = jnp.where((ctx_place & (2 << n)) == 0, pairs, pairs[:, ::-1]).reshape(columns.shape)
        return jnp.swapaxes(columns, 0, 1).reshape(width, width)

    weight_out = step(join_out, out_even, out_odd)
    hidden, normed_two = step(
        out_projection(all_rows, width), attended_low, weight_out, flat_tokens, bias_out[None], gain_two[None],
        shift_two[None],
    )
    normed_other = xor_send(normed_two, 1)

    weights = [rest_low, rest_high, low_x, high_x, low_y, high_y, low_diagonal, high_diagonal]
    flows = (normed_two, normed_other, back_low, back_other, back_turned)
    act_first, units_first, down_own, down_x, sums_first = step(
        lambda *args: ffn_first(*args[:6], *in_hbm(args[6:])), *flows, bias_near, *weights[:4]
    )
    act_second, units_second, down_y, down_top, down_bottom, sums_second, back_own, back_part = step(
        lambda *args: ffn_second(*args[:6], *in_hbm(args[6:])), *flows, bias_far, units_first, *weights
    )
    back_got = xor_send(back_part, 1)
    top_got, bottom_got = xor_send(down_top, 4), xor_send(down_bottom, 2)

    def meet(along_x, along_y, top, bottom):
        half = width // 2
        return (
            jnp.concatenate([add_low(along_x[:half], top), along_x[half:]]),
            jnp.concatenate([along_y[:half], add_low(along_y[half:], bottom)]),
        )

    up_own, up_x, up_y, up_top, up_bottom = step(
        lambda *args: ffn_third(*args[:2], *in_hbm(args[2:])), normed_two, normed_other, units_first, units_second
    )
    down_x, down_y = step(meet, down_x, down_y, top_got, bottom_got)
    down_got = [xor_send(down_x, 2), xor_send(down_y, 4)]
    top_got, bottom_got = xor_send(up_top, 4), xor_send(up_bottom, 2)

    grad_hidden, grad_hidden_low, grad_attended, hidden_sums = step(
        hidden_back(all_rows, width), back_own, back_got, hidden, back_low, gain_two[None], weight_out
    )
    grad_attended = grad_attended.reshape(batches, rows_here, width)
    def by_wt(*arrays):
        return split_wt(add_low(*arrays).reshape(wt_count, shard_rows, chunk), 1)

    def next_wt(kept, got):
        return split_wt(add_low(kept, got), 2)

    def kv_pieces(evens, odds):
        total = jnp.concatenate([add_low(a, b) for a, b in zip(evens, odds)], axis=1)
        return [total[m] for m in range(chips)]

    backs = [step(run_backward[0], doc_starts, places[0], queries, kv_even, kv_odd, attended, logs, grad_attended)]
    kv_got = [xor_send(backs[0][2], 1)]
    down_kept, down_sent = step(by_wt, down_own, *down_got)
    up_x, up_y = step(meet, up_x, up_y, top_got, bottom_got)
    grad_attended, down_kept, down_sent, up_x, up_y = together(grad_attended, down_kept, down_sent, up_x, up_y)
    down_got = xor_wt(down_sent, 1)
    up_got = [xor_send(up_x, 2), xor_send(up_y, 4)]
    backs += [
        step(run_backward[run], doc_starts, places[run], queries, kv_even, kv_odd, attended, logs, grad_attended)
        for run in range(1, runs)
    ]
    backs[-1] = list(backs[-1])
    *backs[-1], down_got, up_got[0], up_got[1] = together(*backs[-1], down_got, *up_got)
    kv_got += [xor_send(back[2], 1) for back in backs[1:]]
    grad_queries = [back[0] for back in backs]
    grad_query = jnp.concatenate(grad_queries).reshape(all_rows, width)
    down_kept, down_sent = next_wt(down_kept, down_got)
    up_kept, up_sent = by_wt(up_own, *up_got)
    down_kept, down_sent, up_kept, up_sent = together(down_kept, down_sent, up_kept, up_sent)
    down_got, up_got = xor_wt(down_sent, 2), xor_wt(up_sent, 1)
    kv_half = step(kv_pieces, [back[1] for back in backs], kv_got)
    kv_got = [xor_send(kv_half[m], 2 * m) for m in range(1, chips)]
    wide_even, wide_odd = step(
        attn_grads(all_rows, width, wt_count, ctx_count, piece_rows),
        place, normed_low, grad_query, attended_low, grad_hidden_low,
    )
    small_size = small_master.shape[0]
    up_kept, up_sent = step(next_wt, up_kept, up_got)
    kv_got[0], up_kept, up_sent, down_got = together(kv_got[0], up_kept, up_sent, down_got)
    up_got = xor_wt(up_sent, 2)
    input_grad, tail_even, tail_odd = step(
        stream_back(all_rows, width, ctx_count, wt_count, piece_rows),
        place, *[array.reshape(all_rows, 2 * HS) for array in (kv_half[0], *kv_got)], grad_query, weight_qkv,
        flat_tokens, gain_one[None], grad_hidden, normed_low, back_low, hidden_sums, sums_first, sums_second,
    )
    input_grad = input_grad.reshape(batches, rows_here, width)
    wide_odd, tail_odd = lax.optimization_barrier((wide_odd, tail_odd))
    wide_odd, tail_odd = xor_send(wide_odd, 1), xor_send(tail_odd, 1)
    def attn_pieces(wide_even, wide_odd, tail_even, tail_odd):
        total = jnp.concatenate([add_low(wide_even, wide_odd), add_low(tail_even, tail_odd)], axis=3)
        return [total[m] for m in range(chips)]

    attn_half = step(attn_pieces, wide_even, wide_odd, tail_even, tail_odd)
    attn_got = [xor_send(attn_half[m], 2 * m) for m in range(1, chips)]
    ffn_part = step(
        lambda *arrays: jnp.concatenate([add_low(*arrays[:2]), add_low(*arrays[2:])]), up_kept, up_got, down_kept, down_got
    )
    ffn_got = send_chips(ffn_part)
    down_out, down_other = step(
        lambda *args: ffn_down(*args[:2], *in_hbm(args[2:])), act_first, act_second, *weights
    )
    down_other = xor_send(down_other, 1)
    attn_kept, attn_sent = step(lambda *parts: split_wt(add_low(*parts), 1), attn_half[0], *attn_got)
    attn_got = xor_wt(attn_sent, 1)
    layer_out = step(
        lambda hidden, own, got: low(hidden + own + wide(got) + bias_proj).reshape(batches, rows_here, width),
        hidden, down_out, down_other,
    )
    attn_kept, attn_sent = step(lambda kept, got: split_wt(add_low(kept, got), 2), attn_kept, attn_got)
    attn_got = xor_wt(attn_sent, 2)
    attn_got, *ffn_got = together(attn_got, *ffn_got)
    ffn_even = jnp.stack([ffn_part] + ffn_got)
    ffn_odd = xor_send(ffn_even, 1)
    attn_part = step(lambda *parts: add_low(*parts)[0], attn_kept, attn_got)
    attn_got = send_chips(attn_part)

    ffn_new = step(
        ffn_update(shard_rows, FF, ctx_count, chunk), place, ffn_even, ffn_odd, ffn_master, ffn_mom, ffn_sq
    )
    attn_even = step(lambda *parts: jnp.stack(parts), attn_part, *attn_got)
    attn_odd = xor_send(attn_even, 1)
    small_total = in_order(attn_even[..., attn_columns:], attn_odd[..., attn_columns:])
    small_total = wide(small_total.reshape(-1))
    most = small_size - FF - HS
    small_total = jnp.concatenate(
        [small_total[:most], small_total[most + HS : most + 2 * HS], small_total[most + 2 * HS : most + 2 * HS + FF]]
    )
    small_new = adam_update(small_master, small_total, small_mom, small_sq, 1.0, 0.0)
    attn_new = attn_update(shard_rows, attn_columns, width, ctx_count, piece_rows)(
        place, attn_even, attn_odd, *in_hbm([attn_master, attn_mom, attn_sq])
    )
    return (layer_out, input_grad) + tuple(attn_new) + tuple(ffn_new) + tuple(small_new)


def shift_wt(array, shift):
    count = lax.axis_size("wt")
    return lax.ppermute(array, "wt", [(i, (i + shift) % count) for i in range(count)])


def whole_wt(piece, axis):
    count, place = lax.axis_size("wt"), lax.axis_index("wt")
    shape = list(piece.shape)
    shape[axis] *= count
    buffer = put(jnp.zeros(shape, piece.dtype), piece, place, axis)
    for shift in range(1, count):
        buffer = put(buffer, shift_wt(piece, shift), (place - shift) % count, axis)
    return buffer


def whole_ctx(piece):
    count = lax.axis_size("ctx")
    got = {0: piece}
    for mask in range(2, count, 2):
        got[mask] = xor_send(piece, mask)
    for mask in range(0, count, 2):
        got[mask + 1] = xor_send(got[mask], 1)
    return [got[mask] for mask in range(count)]


def sum_ctx(pieces):
    count = lax.axis_size("ctx")
    half = {}
    for mask in range(count - 2, -1, -2):
        other = xor_send(pieces[mask + 1], 1)
        half[mask] = low(wide(pieces[mask]) + wide(other))
    total = wide(half[0])
    for mask in range(2, count, 2):
        total = total + wide(xor_send(half[mask], mask))
    return total


def sum_wt(array, axis):
    count, place = lax.axis_size("wt"), lax.axis_index("wt")
    size = array.shape[axis] // count
    total = wide(take(array, place, axis, size))
    for shift in range(1, count):
        sent = take(array, (place + shift) % count, axis, size)
        total = total + wide(shift_wt(sent, shift))
    return total


def any_shards(
    tokens,
    doc_starts,
    attn_master,
    attn_mom,
    attn_sq,
    ffn_master,
    ffn_mom,
    ffn_sq,
    small_master,
    small_mom,
    small_sq,
    cotangent,
):
    ctx_count = lax.axis_size("ctx")
    ctx_place = lax.axis_index("ctx")
    wt_count = lax.axis_size("wt")
    batches, rows_here, width = tokens.shape
    heads = width // HS
    qkv_cols = width + 2 * HS
    all_rows = batches * rows_here
    shard_rows = attn_master.shape[0]
    piece_rows = shard_rows // ctx_count
    chunk = FF // ctx_count
    order = ctx_place ^ jnp.arange(ctx_count, dtype=jnp.int32)
    (
        gain_one,
        shift_one,
        gain_two,
        shift_two,
        bias_query,
        bias_out,
        bias_proj,
        bias_value,
        bias_hidden,
    ) = split_small(small_master)

    attn_piece = low(take(attn_master, ctx_place, 0, piece_rows))

    def whole_rows(piece):
        parts = whole_ctx(whole_wt(piece[None], 0))
        buffer = jnp.zeros((wt_count, ctx_count) + piece.shape, piece.dtype)
        for k, part in enumerate(parts):
            buffer = put(buffer, part[:, None], ctx_place ^ k, 1)
        return buffer.reshape((width,) + piece.shape[1:])

    weight_qkv = whole_rows(attn_piece[:, :qkv_cols])
    weight_out = whole_rows(attn_piece[:, qkv_cols:])
    ffn_piece = low(jnp.swapaxes(take(ffn_master, ctx_place, 2, chunk), 0, 1))
    ffn_parts = whole_ctx(whole_wt(ffn_piece, 1))
    bias_parts = bias_hidden.reshape(ctx_count, chunk)[order]

    stream = wide(tokens.reshape(all_rows, width))
    normed, norm_back_one = jax.vjp(layer_norm, stream, gain_one, shift_one)
    normed_low = low(normed)
    mixed = dot(normed_low, weight_qkv)
    queries = low(mixed[:, :width] + bias_query)
    kv_local = low(
        mixed[:, width:] + jnp.concatenate([jnp.zeros((HS,), jnp.float32), bias_value])
    ).reshape(batches, rows_here, 2 * HS)
    kv_parts = jnp.stack(whole_ctx(kv_local), axis=1).reshape(
        batches, ctx_count * rows_here, 2 * HS
    )
    keys_all, values_all = kv_parts[..., :HS], kv_parts[..., HS:]
    local_pos = jnp.arange(rows_here, dtype=jnp.int32)
    query_pos = ctx_place * rows_here + local_pos
    key_pos = (order[:, None] * rows_here + local_pos[None, :]).reshape(-1)
    queries = queries.reshape(batches, rows_here * heads, HS)
    scale = HS ** (-0.5)
    attended_list, log_list, allowed_list = [], [], []
    for b in range(batches):
        starts = doc_starts[b]
        query_doc = jnp.sum((starts[None, :] <= query_pos[:, None]).astype(jnp.int32), axis=1)
        key_doc = jnp.sum((starts[None, :] <= key_pos[:, None]).astype(jnp.int32), axis=1)
        allowed = (query_doc[:, None] == key_doc[None, :]) & (key_pos[None, :] <= query_pos[:, None])
        allowed = jnp.repeat(allowed, heads, axis=0)
        allowed_list.append(allowed)
        scores = jnp.where(allowed, cols_dot(queries[b], keys_all[b]) * scale, -1e30)
        peak = jnp.max(scores, axis=-1, keepdims=True)
        expo = jnp.exp(scores - peak)
        total = jnp.sum(expo, axis=-1, keepdims=True)
        attended_list.append(dot(low(expo / total), values_all[b]))
        log_list.append(peak + jnp.log(total))
    attended = jnp.stack(attended_list)
    attended_low = low(attended).reshape(all_rows, width)
    hidden = stream + dot(attended_low, weight_out) + bias_out
    normed_two, norm_back_two = jax.vjp(layer_norm, hidden, gain_two, shift_two)
    normed_two_low = low(normed_two)

    back_low = cotangent.reshape(all_rows, width)
    back_rows = wide(back_low)
    down_vals = jnp.zeros((all_rows, width), jnp.float32)
    grad_normed_two = jnp.zeros((all_rows, width), jnp.float32)
    ffn_grads, hidden_grads = [], []
    for k in range(ctx_count):
        weight_up, weight_down = ffn_parts[k][0], ffn_parts[k][1]
        value, slope = gelu_both(dot(normed_two_low, weight_up) + bias_parts[k])
        act = low(value)
        down_vals = down_vals + cols_dot(act, weight_down)
        grad_up = low(dot(back_low, weight_down) * slope)
        hidden_grads.append(jnp.sum(wide(grad_up), axis=0))
        grad_normed_two = grad_normed_two + cols_dot(grad_up, weight_up)
        ffn_grads.append(
            jnp.stack([low(rows_dot(normed_two_low, grad_up)), low(rows_dot(back_low, act))])
        )
    layer_out = low(hidden + down_vals + bias_proj).reshape(batches, rows_here, width)
    grad_bias_proj = jnp.sum(back_rows, axis=0)
    grad_bias_hidden = jnp.stack(hidden_grads)[order].reshape(FF)
    ffn_part = low(sum_wt(low(sum_ctx(ffn_grads)), 1))

    grad_hidden_part, grad_gain_two, grad_shift_two = norm_back_two(grad_normed_two)
    grad_hidden = back_rows + grad_hidden_part
    grad_bias_out = jnp.sum(grad_hidden, axis=0)
    grad_hidden_low = low(grad_hidden)
    grad_out = rows_dot(attended_low, grad_hidden_low)

    def summed_rows(grad):
        blocks = low(grad).reshape(wt_count, ctx_count, piece_rows, grad.shape[1])
        pieces = [take(blocks, ctx_place ^ k, 1, 1)[:, 0] for k in range(ctx_count)]
        part = low(sum_wt(low(sum_ctx(pieces)), 0)[0])
        buffer = jnp.zeros((ctx_count,) + part.shape, part.dtype)
        for k, got in enumerate(whole_ctx(part)):
            buffer = put(buffer, got[None], ctx_place ^ k, 0)
        return wide(buffer.reshape(shard_rows, grad.shape[1]))

    out_total = summed_rows(grad_out)

    grad_attended = low(cols_dot(grad_hidden_low, weight_out)).reshape(
        batches, rows_here * heads, HS
    )
    grad_query_list, grad_kv_list = [], []
    for b in range(batches):
        grads = grad_attended[b]
        delta = jnp.sum(wide(grads) * attended[b], axis=-1, keepdims=True)
        scores = jnp.where(allowed_list[b], cols_dot(queries[b], keys_all[b]) * scale, -1e30)
        weights = jnp.exp(scores - log_list[b])
        grad_scores = low(weights * (cols_dot(grads, values_all[b]) - delta))
        grad_query_list.append(low(dot(grad_scores, keys_all[b]) * scale))
        grad_kv_list.append(
            jnp.concatenate(
                [
                    low(rows_dot(grad_scores, queries[b]) * scale),
                    low(rows_dot(low(weights), grads)),
                ],
                axis=1,
            )
        )
    grad_query = jnp.stack(grad_query_list).reshape(all_rows, width)
    grad_kv = jnp.stack(grad_kv_list).reshape(batches, ctx_count, rows_here, 2 * HS)
    grad_kv_low = low(sum_ctx([grad_kv[:, k] for k in range(ctx_count)])).reshape(
        all_rows, 2 * HS
    )
    grad_bias_query = jnp.sum(wide(grad_query), axis=0)
    grad_bias_value = jnp.sum(wide(grad_kv_low[:, HS:]), axis=0)
    grad_mixed = jnp.concatenate([grad_query, grad_kv_low], axis=1)
    qkv_total = summed_rows(rows_dot(normed_low, grad_mixed))
    grad_normed = cols_dot(grad_mixed, weight_qkv)
    grad_stream_part, grad_gain_one, grad_shift_one = norm_back_one(grad_normed)
    input_grad = (grad_hidden + grad_stream_part).reshape(batches, rows_here, width)

    ffn_buffer = jnp.zeros((ctx_count,) + ffn_part.shape, ffn_part.dtype)
    for k, got in enumerate(whole_ctx(ffn_part)):
        ffn_buffer = put(ffn_buffer, got[None], ctx_place ^ k, 0)
    ffn_total = wide(jnp.transpose(ffn_buffer, (2, 1, 0, 3)).reshape(shard_rows, 2, FF))
    attn_total = jnp.concatenate([qkv_total, out_total], axis=1)
    grad_small = jnp.concatenate(
        [
            grad_gain_one,
            grad_shift_one,
            grad_gain_two,
            grad_shift_two,
            grad_bias_query,
            grad_bias_out,
            grad_bias_proj,
            grad_bias_value,
            grad_bias_hidden,
        ]
    )
    small_total = lax.psum(grad_small, ("ctx", "wt"))
    attn_new = adam_update(attn_master, attn_total, attn_mom, attn_sq, 0.1, 0.1)
    ffn_new = adam_update(ffn_master, ffn_total, ffn_mom, ffn_sq, 0.1, 0.1)
    small_new = adam_update(small_master, small_total, small_mom, small_sq, 1.0, 0.0)
    return (layer_out, input_grad) + attn_new + ffn_new + small_new


def solution(mesh):
    rows, cube = P("wt", None), P("wt", None, None)
    flow = P("wt", "ctx", None)
    in_specs = (flow, rows, rows, rows, rows, cube, cube, cube, P(), P(), P(), flow)
    out_specs = (flow, flow, rows, rows, rows, cube, cube, cube, P(), P(), P())
    ctx_count, wt_count = mesh.shape["ctx"], mesh.shape["wt"]
    fitted = (ctx_count, wt_count) == (8, 4)
    body = shards if fitted else any_shards
    return jax.shard_map(body, mesh=mesh, in_specs=in_specs, out_specs=out_specs, check_vma=False)
```

```python
import jax
import jax.numpy as jnp
from jax import lax
from jax.experimental import pallas as pl
from jax.experimental.pallas import tpu as pltpu
from jax.sharding import PartitionSpec as P

D = 768
HS = 64
FF = 3072
STEP = 10


NORM_EPS = 1e-05
GELU_COEF = 0.7978845608028654
GELU_CUBE = 0.044715
BETA_ONE = 0.9
BETA_TWO = 0.95
ADAM_EPS = 1e-08
VMEM_LIMIT = 22 << 20
NO_COST = pl.CostEstimate(flops=0, bytes_accessed=0, transcendentals=0)


def layer_norm(values, gain, shift):
    centre = values - jnp.mean(values, axis=-1, keepdims=True)
    spread = jnp.mean(centre * centre, axis=-1, keepdims=True)
    return centre * lax.rsqrt(spread + NORM_EPS) * gain + shift


def gelu_both(u):
    square = u * u
    share = 0.5 * jnp.tanh(u * (GELU_COEF * GELU_CUBE * square + GELU_COEF)) + 0.5
    bend = u * (6.0 * GELU_COEF * GELU_CUBE * square + 2.0 * GELU_COEF)
    return u * share, share * ((1.0 - share) * bend) + share


def split_small(small):
    return (
        small[0:D],
        small[D : 2 * D],
        small[2 * D : 3 * D],
        small[3 * D : 4 * D],
        small[4 * D : 5 * D],
        small[5 * D : 6 * D],
        small[6 * D : 7 * D],
        small[7 * D : 7 * D + HS],
        small[7 * D + HS :],
    )


def rows_dot(left, right):
    return lax.dot_general(
        left, right, (((0,), (0,)), ((), ())), preferred_element_type=jnp.float32
    )


def cols_dot(left, right):
    return lax.dot_general(
        left, right, (((1,), (1,)), ((), ())), preferred_element_type=jnp.float32
    )


def dot(left, right):
    return jnp.dot(left, right, preferred_element_type=jnp.float32)


def low(values):
    return values.astype(jnp.bfloat16)


def wide(values):
    return values.astype(jnp.float32)


def adam_update(master, gradient, first, second, step_rate, decay_rate):
    first_new = BETA_ONE * first + (1.0 - BETA_ONE) * gradient
    second_new = BETA_TWO * second + (1.0 - BETA_TWO) * gradient * gradient
    first_hat = first_new / (1.0 - BETA_ONE**STEP)
    second_hat = second_new / (1.0 - BETA_TWO**STEP)
    master_new = master - step_rate * (
        first_hat / (jnp.sqrt(second_hat) + ADAM_EPS) + decay_rate * master
    )
    return (first_new, second_new, master_new)


def xor_send(array, mask):
    count = lax.axis_size("ctx")
    return lax.ppermute(array, "ctx", [(i, i ^ mask) for i in range(count)])


def xor_wt(array, mask):
    count = lax.axis_size("wt")
    return lax.ppermute(array, "wt", [(i, i ^ mask) for i in range(count)])


class Steps:
    def __init__(self):
        self.last = ()

    def __call__(self, function, *args):
        flat, tree = jax.tree.flatten(args)
        held = lax.optimization_barrier(tuple(flat) + self.last)[: len(flat)]
        result = function(*jax.tree.unflatten(tree, held))
        self.last = tuple(jax.tree.leaves(result))
        return result


def loop(count, body, carry=0):
    return lax.fori_loop(0, count, body, carry)


def rows_at(i, size):
    return pl.ds(pl.multiple_of(i * size, size), size)


def together(*arrays):
    return lax.optimization_barrier(arrays)


def put(buffer, piece, place, axis):
    starts = [0] * buffer.ndim
    starts[axis] = place * piece.shape[axis]
    return lax.dynamic_update_slice(buffer, piece, starts)


def take(buffer, place, axis, size):
    return lax.dynamic_slice_in_dim(buffer, place * size, size, axis)


def attention_kernels(batches, rows, width, parts, runs):
    half_parts = parts // 2
    keys = parts * rows
    pair = 2 * HS
    groups = width // (2 * pair)
    factor = HS ** (-0.5) * 1.4426950408889634
    tile = 32

    def lanes(shape):
        return lax.broadcasted_iota(jnp.int32, shape, 1)

    def spread(even_ref, odd_ref, key_ref, value_ref):
        for j in range(parts):
            ref = even_ref if j < half_parts else odd_ref
            block = wide(ref[j % half_parts, 0])
            turned = pltpu.roll(block, HS, 1)
            first = lanes(block.shape) < HS
            here = pl.ds(j * rows, rows)
            key_ref[0, here, :] = low(jnp.where(first, block, 0.0))
            key_ref[1, here, :] = low(jnp.where(first, 0.0, turned))
            value_ref[0, here, :] = low(jnp.where(first, turned, 0.0))
            value_ref[1, here, :] = low(jnp.where(first, 0.0, block))

    def doc_begin(starts_ref, stream, positions):
        begin = jnp.zeros_like(positions)
        for j in range(starts_ref.shape[1]):
            start = starts_ref[stream, j]
            begin = jnp.where(start <= positions, jnp.maximum(begin, start), begin)
        return begin

    def forward(starts_ref, place_ref, query_ref, even_ref, odd_ref, low_ref, full_ref, log_ref, cap, key, value, weight):
        stream, place = pl.program_id(0), place_ref[0]
        spread(even_ref, odd_ref, key, value)
        query_pos = place * rows + lax.broadcasted_iota(jnp.int32, (rows, 1), 0)
        begin = doc_begin(starts_ref, stream, query_pos)
        for j in range(parts):
            key_pos = (place ^ (2 * (j % half_parts) + j // half_parts)) * rows + lax.broadcasted_iota(jnp.int32, (rows, rows), 1)
            allowed = (key_pos >= begin) & (key_pos <= query_pos)
            cap[:, j * rows : (j + 1) * rows] = jnp.where(allowed, 3.0e38, -1e30)
        column = lanes((tile, pair))
        logs = [jnp.zeros((tile, pair), jnp.float32) for _ in range(rows // tile)]
        for g in range(groups):
            at = g * 2 * pair
            two = jnp.concatenate([query_ref[0, :, at : at + pair], query_ref[0, :, at + pair : at + 2 * pair]], axis=0)
            totals = []
            for half in range(2):
                scores = cols_dot(two, key[half])
                norms = []
                for t in range(2 * rows // tile):
                    own = slice(t * tile, (t + 1) * tile)
                    n = t % (rows // tile)
                    part = jnp.minimum(scores[own] * factor, cap[n * tile : (n + 1) * tile, :])
                    peak = jnp.max(part, axis=1, keepdims=True)
                    expo = jnp.exp2(part - peak)
                    norm = jnp.sum(expo, axis=1, keepdims=True)
                    weight[half, own, :] = low(expo)
                    norms.append(norm)
                    head = 4 * g + 2 * (t * tile // rows) + half
                    logs[n] = jnp.where(column == head, peak + jnp.log2(norm), logs[n])
                totals.append(dot(weight[half], value[half]) / jnp.concatenate(norms, axis=0))
            total = totals[0] + totals[1]
            for j in range(2):
                part = total[j * rows : (j + 1) * rows]
                full_ref[0, :, at + j * pair : at + (j + 1) * pair] = part
                low_ref[0, :, at + j * pair : at + (j + 1) * pair] = low(part)
        for n, log in enumerate(logs):
            log_ref[0, n * tile : (n + 1) * tile, :] = log

    def backward(
        starts_ref, place_ref, query_ref, even_ref, odd_ref, full_ref, log_ref, grad_ref,
        query_grad_ref, even_grad_ref, odd_grad_ref,
        cap, key, value, key_turned, log_rows, delta_rows, weight_buf, score_buf, query_buf, grad_buf,
    ):
        stream, place = pl.program_id(0) + place_ref[1], place_ref[0]
        spread(even_ref, odd_ref, key, value)
        query_pos = place * rows + lax.broadcasted_iota(jnp.int32, (1, rows), 1)
        begin = doc_begin(starts_ref, stream, query_pos)
        for j in range(parts):
            key_pos = (place ^ (2 * (j % half_parts) + j // half_parts)) * rows + lax.broadcasted_iota(jnp.int32, (rows, rows), 0)
            allowed = (key_pos >= begin) & (key_pos <= query_pos)
            cap[j * rows : (j + 1) * rows, :] = jnp.where(allowed, 3.0e38, -1e30)
            here = pl.ds(j * rows, rows)
            key_turned[:, j * rows : (j + 1) * rows] = low(wide(key[0, here, :]).T[:HS])
        log_rows[...] = log_ref[0].T[: log_rows.shape[0]]
        head_of = lax.broadcasted_iota(jnp.int32, (delta_rows.shape[0], width), 1) // HS
        chosen = (head_of == lax.broadcasted_iota(jnp.int32, (delta_rows.shape[0], width), 0)).astype(jnp.float32)
        delta_rows[...] = lax.dot_general(
            chosen, wide(grad_ref[0]) * full_ref[0], (((1,), (1,)), ((), ())),
            precision=lax.Precision.HIGHEST, preferred_element_type=jnp.float32,
        )
        first = lanes((2 * rows, pair)) < HS
        for g in range(groups):
            at = g * 2 * pair
            both, both_grad = query_ref[0, :, at : at + 2 * pair], grad_ref[0, :, at : at + 2 * pair]
            two = jnp.concatenate([both[:, :pair], both[:, pair:]], axis=0)
            two_grad = jnp.concatenate([both_grad[:, :pair], both_grad[:, pair:]], axis=0)
            turned = []
            for half in range(2):
                h = 4 * g + half
                span = slice((2 * g + half) * 2 * rows, (2 * g + half + 1) * 2 * rows)
                keep = first if half == 0 else jnp.logical_not(first)
                query_buf[span, :] = low(jnp.where(keep, wide(two), 0.0))
                grad_buf[span, :] = low(jnp.where(keep, wide(two_grad), 0.0))
                log = jnp.concatenate([log_rows[h : h + 1, :], log_rows[h + 2 : h + 3, :]], axis=1)
                delta = jnp.concatenate([delta_rows[h : h + 1, :], delta_rows[h + 2 : h + 3, :]], axis=1)
                scores, weight_grads = cols_dot(key[half], two), cols_dot(value[half], two_grad)
                for t in range(keys // (2 * tile)):
                    own = slice(t * 2 * tile, (t + 1) * 2 * tile)
                    limit = cap[own, :]
                    limit = jnp.concatenate([limit, limit], axis=1)
                    weights = jnp.exp2(jnp.minimum(scores[own] * factor, limit) - log)
                    weight_buf[own, span] = low(weights)
                    score_buf[own, span] = low(weights * (weight_grads[own] - delta))
                turned.append(dot(key_turned[...], score_buf[:, span]))
            turned = jnp.concatenate(turned, axis=0) * HS ** (-0.5)
            query_grad_ref[0, :, at : at + pair] = low(turned[:, :rows].T)
            query_grad_ref[0, :, at + pair : at + 2 * pair] = low(turned[:, rows:].T)
        for j in range(parts):
            here = pl.ds(j * rows, rows)
            value_sum = dot(weight_buf[here, :], grad_buf[...])
            key_sum = dot(score_buf[here, :], query_buf[...]) * HS ** (-0.5)
            value_sum = value_sum + pltpu.roll(value_sum, HS, 1)
            key_sum = key_sum + pltpu.roll(key_sum, HS, 1)
            ref = even_grad_ref if j < half_parts else odd_grad_ref
            ref[j % half_parts, 0] = low(jnp.where(lanes((rows, pair)) < HS, key_sum, value_sum))

    def specs(first):
        return (
            pl.BlockSpec((1, rows, width), lambda b, *_: (b + first, 0, 0)),
            pl.BlockSpec((1, rows, pair), lambda b, *_: (b + first, 0, 0)),
            pl.BlockSpec((half_parts, 1, rows, pair), lambda b, *_: (0, b + first, 0, 0)),
        )

    flow, logs, blocks = specs(0)

    shared = [
        pltpu.VMEM((2, keys, pair), jnp.bfloat16),
        pltpu.VMEM((2, keys, pair), jnp.bfloat16),
    ]
    run_forward = pl.pallas_call(
        forward,
        grid_spec=pltpu.PrefetchScalarGridSpec(
            num_scalar_prefetch=2,
            grid=(batches,),
            in_specs=[flow, blocks, blocks],
            out_specs=[flow, flow, logs],
            scratch_shapes=[pltpu.VMEM((rows, keys), jnp.float32)]
            + shared
            + [pltpu.VMEM((2, 2 * rows, keys), jnp.bfloat16)],
        ),
        out_shape=[
            jax.ShapeDtypeStruct((batches, rows, width), jnp.bfloat16),
            jax.ShapeDtypeStruct((batches, rows, width), jnp.float32),
            jax.ShapeDtypeStruct((batches, rows, pair), jnp.float32),
        ],
        compiler_params=pltpu.CompilerParams(vmem_limit_bytes=VMEM_LIMIT),
        cost_estimate=NO_COST,
        name="attention_forward",
    )
    head_rows = -(-(width // HS) // 8) * 8
    all_columns = rows * (width // HS)
    count = batches // runs

    def call_backward(run):
        here_flow, here_logs, here_blocks = specs(run * count)
        return pl.pallas_call(
        backward,
        grid_spec=pltpu.PrefetchScalarGridSpec(
            num_scalar_prefetch=2,
            grid=(count,),
            in_specs=[here_flow, here_blocks, here_blocks, here_flow, here_logs, here_flow],
            out_specs=[flow, blocks, blocks],
            scratch_shapes=[pltpu.VMEM((keys, rows), jnp.float32)]
            + shared
            + [
                pltpu.VMEM((HS, keys), jnp.bfloat16),
                pltpu.VMEM((head_rows, rows), jnp.float32),
                pltpu.VMEM((head_rows, rows), jnp.float32),
                pltpu.VMEM((keys, all_columns), jnp.bfloat16),
                pltpu.VMEM((keys, all_columns), jnp.bfloat16),
                pltpu.VMEM((all_columns, pair), jnp.bfloat16),
                pltpu.VMEM((all_columns, pair), jnp.bfloat16),
            ],
        ),
        out_shape=[
            jax.ShapeDtypeStruct((count, rows, width), jnp.bfloat16),
            jax.ShapeDtypeStruct((half_parts, count, rows, pair), jnp.bfloat16),
            jax.ShapeDtypeStruct((half_parts, count, rows, pair), jnp.bfloat16),
        ],
        compiler_params=pltpu.CompilerParams(vmem_limit_bytes=VMEM_LIMIT),
        cost_estimate=NO_COST,
        name="attention_backward",
    )

    return run_forward, [call_backward(run) for run in range(runs)]


def in_hbm(arrays):
    return [pltpu.with_memory_space_constraint(array, pltpu.HBM) for array in arrays]


def ffn_kernels(rows, width, chunk, wt_count):
    units = 2 * chunk
    all_rows = 2 * rows
    block_rows = width // wt_count
    hbm = pl.BlockSpec(memory_space=pltpu.HBM)
    vmem = pl.BlockSpec(memory_space=pltpu.VMEM)
    params = pltpu.CompilerParams(vmem_limit_bytes=VMEM_LIMIT)

    def fetch(weights, which, held, sem):
        copies = []
        for n, arrays in enumerate(weights):
            blocks = [array.at[block] for array in arrays for block in range(array.shape[0])]
            for row, block in enumerate(blocks):
                copies.append(
                    pltpu.make_async_copy(
                        block.at[pl.ds(which * block_rows, block_rows), :],
                        held.at[pl.ds(row * block_rows, block_rows), pl.ds(n * chunk, chunk)],
                        sem.at[len(copies)],
                    )
                )
        for copy in copies:
            copy.start()
        return copies

    def send(pairs, sems):
        copies = [pltpu.make_async_copy(source, out, sems.at[n]) for n, (source, out) in enumerate(pairs)]
        for copy in copies:
            copy.start()
        return copies

    part_rows = 256
    tile = 16

    def units_of(inputs, grads, bias, held_up, held_down, act, grad_units):
        sums = jnp.zeros((8, units), jnp.float32)
        for s in range(2):

            def part(i, sums):
                here = rows_at(i, part_rows)
                up = dot(inputs[s][here, :], held_up[...])
                act_grad = dot(grads[s][here, :], held_down[...])
                for t in range(part_rows // tile):
                    own = slice(t * tile, (t + 1) * tile)
                    there = pl.ds(pl.multiple_of(s * rows + i * part_rows + t * tile, tile), tile)
                    value, slope = gelu_both(up[own] + bias)
                    grad = act_grad[own] * slope
                    act[there, :] = low(value)
                    grad_units[there, :] = low(grad)
                    sums = sums + (grad[:8] + grad[8:])
                return sums

            sums = loop(rows // part_rows, part, sums)
        return jnp.sum(sums, axis=0, keepdims=True)

    def product_of(turned, right, product):
        def part(i, carry):
            here = rows_at(i, part_rows)
            product[here, :] = low(dot(turned[here, :], right[...]))
            return carry

        loop(width // part_rows, part)

    def back_to(refs, sources, weights):
        for s, ref in enumerate(refs):

            def part(i, carry):
                here = pl.ds(pl.multiple_of(s * rows + i * part_rows, part_rows), part_rows)
                total = cols_dot(sources[0][here, :], weights[0][...]) + cols_dot(sources[1][here, :], weights[1][...])
                ref[rows_at(i, part_rows), :] = total.astype(ref.dtype)
                return carry

            loop(rows // part_rows, part)

    def halves(product, m):
        cols = pl.ds(m * chunk, chunk)
        return [product.at[pl.ds(h * width // 2, width // 2), cols] for h in range(2)]

    def first(
        own, other, grad_own, grad_other, turned, bias, w0, w1, w2, w3,
        act_out, units_out, out_a, out_b, sums_out,
        held_up, held_down, act, grad_units, product, sems, out_sems,
    ):
        weights = ((w0, w1), (w2, w3))
        copies = fetch(weights, 0, held_up, sems.at[0]) + fetch(weights, 1, held_down, sems.at[1])
        for copy in copies:
            copy.wait()
        sums_out[...] = units_of((own, other), (grad_own, grad_other), bias[...], held_up, held_down, act, grad_units)
        sent = send(((act, act_out), (grad_units, units_out)), out_sems.at[0])
        product_of(turned, act, product)
        sent += send(
            ((product.at[:, pl.ds(0, chunk)], out_a), (product.at[:, pl.ds(chunk, chunk)], out_b)), out_sems.at[1]
        )
        for copy in sent:
            copy.wait()

    def second(
        own, other, grad_own, grad_other, turned, bias, units_first, w0, w1, w2, w3, w4, w5, w6, w7,
        act_out, units_out, out_a, out_b, out_c, sums_out, back_own, back_other,
        held_up, held_more, held_down, act, grad_units, more_units, product, sems, out_sems, more_sem,
    ):
        weights, before = ((w4, w5), (w6, w7)), ((w0, w1), (w2, w3))
        copies = fetch(weights, 0, held_up, sems.at[0]) + fetch(weights, 1, held_down, sems.at[1])
        more = fetch(before, 0, held_more, sems.at[2])
        more.append(pltpu.make_async_copy(units_first, more_units, more_sem))
        more[-1].start()
        for copy in copies:
            copy.wait()
        sums_out[...] = units_of((own, other), (grad_own, grad_other), bias[...], held_up, held_down, act, grad_units)
        sent = send(((act, act_out), (grad_units, units_out)), out_sems.at[0])
        product_of(turned, act, product)
        top, bottom = halves(product, 1)
        sent += send(((product.at[:, pl.ds(0, chunk)], out_a), (top, out_b), (bottom, out_c)), out_sems.at[1])
        for copy in more:
            copy.wait()
        back_to((back_own, back_other), (grad_units, more_units), (held_up, held_more))
        for copy in sent:
            copy.wait()

    def third(own, other, units_a, units_b, out_0, out_1, out_2, out_3, out_4, turned, held, products, sems, out_sems):
        copies = send(((units_a, held.at[0]), (units_b, held.at[1])), sems)
        turn((own, other), turned)
        for copy in copies:
            copy.wait()
        products[1] = low(dot(turned[...], held[1]))
        top, bottom = halves(products.at[1], 1)
        sent = send(((products.at[1, :, pl.ds(0, chunk)], out_2), (top, out_3), (bottom, out_4)), out_sems.at[0])
        products[0] = low(dot(turned[...], held[0]))
        sent += send(
            ((products.at[0, :, pl.ds(0, chunk)], out_0), (products.at[0, :, pl.ds(chunk, chunk)], out_1)),
            out_sems.at[1],
        )
        for copy in sent:
            copy.wait()

    def down(act_a, act_b, w0, w1, w2, w3, w4, w5, w6, w7, own_ref, other_ref, held_a, held_b, sems):
        copies = fetch(((w0, w1), (w2, w3)), 1, held_a, sems.at[0]) + fetch(((w4, w5), (w6, w7)), 1, held_b, sems.at[1])
        for copy in copies:
            copy.wait()
        for s, ref in enumerate((own_ref, other_ref)):
            here = slice(s * rows, (s + 1) * rows)
            total = cols_dot(act_a[here, :], held_a[...]) + cols_dot(act_b[here, :], held_b[...])
            ref[...] = total.astype(ref.dtype)

    dma = pltpu.SemaphoreType.DMA
    held = pltpu.VMEM((width, units), jnp.bfloat16)
    flow = pltpu.VMEM((all_rows, units), jnp.bfloat16)
    flow_out = pltpu.HBM((all_rows, units), jnp.bfloat16)
    whole = pltpu.HBM((width, chunk), jnp.bfloat16)
    part = pltpu.HBM((width // 2, chunk), jnp.bfloat16)
    sums = jax.ShapeDtypeStruct((1, units), jnp.float32)
    own = jax.ShapeDtypeStruct((rows, width), jnp.float32)
    other = jax.ShapeDtypeStruct((rows, width), jnp.bfloat16)
    run_first = pl.pallas_call(
        first,
        in_specs=[vmem] * 6 + [hbm] * 4,
        out_specs=[hbm] * 4 + [vmem],
        out_shape=[flow_out, flow_out, whole, whole, sums],
        scratch_shapes=[held, held, flow, flow, held, dma((2, 2 * wt_count)), dma((2, 2))],
        compiler_params=params,
        cost_estimate=NO_COST,
        name="ffn_first",
    )
    run_second = pl.pallas_call(
        second,
        in_specs=[vmem] * 6 + [hbm] * 9,
        out_specs=[hbm] * 5 + [vmem] * 3,
        out_shape=[flow_out, flow_out, whole, part, part, sums, own, other],
        scratch_shapes=[held, held, held, flow, flow, flow, held, dma((3, 2 * wt_count)), dma((2, 3)), dma(())],
        compiler_params=params,
        cost_estimate=NO_COST,
        name="ffn_second",
    )
    run_third = pl.pallas_call(
        third,
        in_specs=[vmem] * 2 + [hbm] * 2,
        out_specs=[hbm] * 5,
        out_shape=[whole, whole, whole, part, part],
        scratch_shapes=[
            pltpu.VMEM((width, all_rows), jnp.bfloat16),
            pltpu.VMEM((2, all_rows, units), jnp.bfloat16),
            pltpu.VMEM((2, width, units), jnp.bfloat16),
            dma((2,)),
            dma((2, 3)),
        ],
        compiler_params=params,
        cost_estimate=NO_COST,
        name="ffn_grads",
    )
    run_down = pl.pallas_call(
        down,
        in_specs=[vmem] * 2 + [hbm] * 8,
        out_specs=[vmem] * 2,
        out_shape=[own, other],
        scratch_shapes=[held, held, dma((2, 2 * wt_count))],
        compiler_params=params,
        cost_estimate=NO_COST,
        name="ffn_down",
    )
    return run_first, run_second, run_third, run_down


def turn(refs, turned):
    rows = refs[0].shape[0]
    for s, ref in enumerate(refs):
        for i in range(rows // 128):
            block = wide(ref[i * 128 : (i + 1) * 128, :])
            turned[:, s * rows + i * 128 : s * rows + (i + 1) * 128] = low(block.T)


def turn_both(own, other):
    vmem = pl.BlockSpec(memory_space=pltpu.VMEM)
    rows, width = own.shape
    return pl.pallas_call(
        lambda a, b, out: turn((a, b), out),
        in_specs=[vmem] * 2,
        out_specs=vmem,
        out_shape=jax.ShapeDtypeStruct((width, 2 * rows), own.dtype),
        compiler_params=pltpu.CompilerParams(vmem_limit_bytes=VMEM_LIMIT),
        cost_estimate=NO_COST,
        name="turn",
    )(own, other)


def out_projection(rows, width):
    tile = 32

    def kernel(attended, weight, stream, bias, gain, shift, hidden_ref, normed_ref):
        product = dot(attended[...], weight[...])
        for t in range(rows // tile):
            here = slice(t * tile, (t + 1) * tile)
            hidden = wide(stream[here, :]) + product[here] + bias[...]
            hidden_ref[here, :] = hidden
            normed_ref[here, :] = low(layer_norm(hidden, gain[...], shift[...]))

    vmem = pl.BlockSpec(memory_space=pltpu.VMEM)
    return pl.pallas_call(
        kernel,
        in_specs=[vmem] * 6,
        out_specs=[vmem] * 2,
        out_shape=[
            jax.ShapeDtypeStruct((rows, width), jnp.float32),
            jax.ShapeDtypeStruct((rows, width), jnp.bfloat16),
        ],
        compiler_params=pltpu.CompilerParams(vmem_limit_bytes=VMEM_LIMIT),
        cost_estimate=NO_COST,
        name="out_projection",
    )


def norm_back(values, gain, grad):
    centre = values - jnp.mean(values, axis=-1, keepdims=True)
    scale = lax.rsqrt(jnp.mean(centre * centre, axis=-1, keepdims=True) + NORM_EPS)
    unit = centre * scale
    inner = grad * gain
    mean = jnp.mean(inner, axis=-1, keepdims=True)
    along = jnp.mean(inner * unit, axis=-1, keepdims=True)
    return scale * (inner - mean - unit * along), grad * unit


def fold_rows(values):
    total = values[:8]
    for i in range(1, values.shape[0] // 8):
        total = total + values[i * 8 : (i + 1) * 8]
    return total


def hidden_back(rows, width):
    tile = 32

    def kernel(own, got, hidden, back, gain, weight, grad_ref, low_ref, attended_ref, sums_ref):
        sums = [jnp.zeros((8, width), jnp.float32) for _ in range(3)]
        for t in range(rows // tile):
            here = slice(t * tile, (t + 1) * tile)
            pulled, terms = norm_back(hidden[here, :], gain[...], own[here, :] + wide(got[here, :]))
            grad = wide(back[here, :]) + pulled
            grad_ref[here, :] = grad
            low_ref[here, :] = low(grad)
            for n, part in enumerate((terms, own[here, :] + wide(got[here, :]), grad)):
                sums[n] = sums[n] + fold_rows(part)
        for n in range(3):
            sums_ref[n : n + 1, :] = jnp.sum(sums[n], axis=0, keepdims=True)
        attended_ref[...] = low(cols_dot(low_ref[...], weight[...]))

    vmem = pl.BlockSpec(memory_space=pltpu.VMEM)
    return pl.pallas_call(
        kernel,
        in_specs=[vmem] * 6,
        out_specs=[vmem] * 4,
        out_shape=[
            jax.ShapeDtypeStruct((rows, width), jnp.float32),
            jax.ShapeDtypeStruct((rows, width), jnp.bfloat16),
            jax.ShapeDtypeStruct((rows, width), jnp.bfloat16),
            jax.ShapeDtypeStruct((3, width), jnp.float32),
        ],
        compiler_params=pltpu.CompilerParams(vmem_limit_bytes=VMEM_LIMIT),
        cost_estimate=NO_COST,
        name="hidden_back",
    )


def stream_back(rows, width, parts, row_groups, piece):
    tile = 32
    chips = parts // 2

    def kernel(
        place_ref, kv_0, kv_1, kv_2, kv_3, queries, weight, tokens, gain, grad_hidden, normed, back, hidden_sums,
        units_a, units_b, input_ref, even_ref, odd_ref, grad_kv, grads, turned, product, small,
    ):
        place = place_ref[0]
        sums = [jnp.zeros((8, width), jnp.float32) for _ in range(4)]
        value_sums = jnp.zeros((8, 2 * HS), jnp.float32)
        for t in range(rows // tile):
            here = slice(t * tile, (t + 1) * tile)
            total = wide(kv_0[here, :]) + wide(kv_1[here, :]) + wide(kv_2[here, :]) + wide(kv_3[here, :])
            grad_kv[here, :] = low(total)
            value_sums = value_sums + fold_rows(total)
        turn((normed,), turned)
        product[...] = dot(turned[...], grad_kv[...])
        grads[...] = cols_dot(queries[...], weight[:, :width]) + cols_dot(grad_kv[...], weight[:, width:])
        for t in range(rows // tile):
            here = slice(t * tile, (t + 1) * tile)
            grad = grads[here, :]
            pulled, terms = norm_back(wide(tokens[here, :]), gain[...], grad)
            input_ref[here, :] = grad_hidden[here, :] + pulled
            for n, part in enumerate((terms, grad, wide(queries[here, :]), wide(back[here, :]))):
                sums[n] = sums[n] + fold_rows(part)
        sums = [jnp.sum(part, axis=0, keepdims=True) for part in sums]
        small[...] = jnp.zeros_like(small)
        rows_in = (sums[0], sums[1], hidden_sums[0:1, :], hidden_sums[1:2, :], sums[2], hidden_sums[2:3, :], sums[3])
        for n, row in enumerate(rows_in):
            for j in range(width // 128):
                line = n * (width // 128) + j
                small[line : line + 1, :] = row[:, j * 128 : (j + 1) * 128]
        start = 7 * (width // 128)
        small[start : start + 1, :] = jnp.sum(value_sums, axis=0, keepdims=True)
        lines = FF // parts // 128
        for m in range(chips):
            units = (units_a, units_b)[m // 2]
            for j in range(lines):
                line = start + 1 + (place ^ (2 * m)) * lines + j
                at = (m % 2 * lines + j) * 128
                small[pl.ds(line, 1), :] = units[:, at : at + 128]
        for k in range(parts):
            ref = odd_ref if k % 2 else even_ref
            mine = low(small[pl.ds(pl.multiple_of((place ^ k) * piece, 8), piece), :])
            for w in range(row_groups):
                at = pl.multiple_of(w * piece * parts + (place ^ k) * piece, 8)
                ref[k // 2, w, :, :128] = low(product[pl.ds(at, piece), :])
                ref[k // 2, w, :, 128:] = mine

    vmem = pl.BlockSpec(memory_space=pltpu.VMEM)
    stack = jax.ShapeDtypeStruct((chips, row_groups, piece, 256), jnp.bfloat16)
    return pl.pallas_call(
        kernel,
        in_specs=[pl.BlockSpec(memory_space=pltpu.SMEM)] + [vmem] * 14,
        out_specs=[vmem] * 3,
        out_shape=[jax.ShapeDtypeStruct((rows, width), jnp.float32), stack, stack],
        scratch_shapes=[
            pltpu.VMEM((rows, 2 * HS), jnp.bfloat16),
            pltpu.VMEM((rows, width), jnp.float32),
            pltpu.VMEM((width, rows), jnp.bfloat16),
            pltpu.VMEM((width, 2 * HS), jnp.float32),
            pltpu.VMEM((parts * piece, 128), jnp.float32),
        ],
        compiler_params=pltpu.CompilerParams(vmem_limit_bytes=VMEM_LIMIT),
        cost_estimate=NO_COST,
        name="stream_back",
    )


def attn_grads(rows, width, row_groups, parts, piece):
    def kernel(place_ref, left_a, right_a, left_b, right_b, even_ref, odd_ref, turned, total):
        place = place_ref[0]
        for n, (left, right) in enumerate(((left_a, right_a), (left_b, right_b))):
            for i in range(rows // 128):
                turned[:, i * 128 : (i + 1) * 128] = low(wide(left[i * 128 : (i + 1) * 128, :]).T)
            total[:, n * width : (n + 1) * width] = dot(turned[...], right[...])
        for k in range(parts):
            ref = odd_ref if k % 2 else even_ref
            for w in range(row_groups):
                at = pl.multiple_of(w * piece * parts + (place ^ k) * piece, 8)
                ref[k // 2, w] = low(total[pl.ds(at, piece), :])

    vmem = pl.BlockSpec(memory_space=pltpu.VMEM)
    shape = jax.ShapeDtypeStruct((parts // 2, row_groups, piece, 2 * width), jnp.bfloat16)
    return pl.pallas_call(
        kernel,
        grid_spec=pltpu.PrefetchScalarGridSpec(
            num_scalar_prefetch=1,
            grid=(),
            in_specs=[vmem] * 4,
            out_specs=[vmem] * 2,
            scratch_shapes=[pltpu.VMEM((width, rows), jnp.bfloat16), pltpu.VMEM((width, 2 * width), jnp.float32)],
        ),
        out_shape=[shape] * 2,
        compiler_params=pltpu.CompilerParams(vmem_limit_bytes=VMEM_LIMIT),
        cost_estimate=NO_COST,
        name="attn_grads",
    )


def attn_update(rows, columns, width, parts, piece):
    qkv = columns - width
    whole = columns + 128 * -(-(7 * width + HS + FF) // (128 * piece * parts))

    def kernel(place_ref, even_ref, odd_ref, master, first, second, *outs):
        core = place_ref[0] % 2
        for ref, which in ((even_ref, core), (odd_ref, 1 - core)):
            here = pl.ds(pl.multiple_of(which * piece, 8), piece)
            for cols, source in (
                (slice(0, width), slice(0, width)),
                (slice(width, qkv), slice(2 * width, columns)),
                (slice(qkv, columns), slice(width, 2 * width)),
            ):
                grad = wide(ref[0, :, source])
                got = adam_update(master[here, cols], grad, first[here, cols], second[here, cols], 0.1, 0.1)
                outs[0][here, cols] = got[0]
                outs[1][here, cols] = got[1]
                outs[2][here, cols] = got[2]

    block = pl.BlockSpec((2 * piece, columns), lambda i, place: (i, 0))
    stack = pl.BlockSpec((1, piece, whole), lambda i, place: (i ^ (place[0] // 2), 0, 0))
    return pl.pallas_call(
        kernel,
        grid_spec=pltpu.PrefetchScalarGridSpec(
            num_scalar_prefetch=1,
            grid=(parts // 2,),
            in_specs=[stack] * 2 + [block] * 3,
            out_specs=[block] * 3,
            scratch_shapes=[],
        ),
        out_shape=[jax.ShapeDtypeStruct((rows, columns), jnp.float32)] * 3,
        compiler_params=pltpu.CompilerParams(vmem_limit_bytes=VMEM_LIMIT),
        cost_estimate=NO_COST,
        name="attn_update",
    )


def ffn_update(rows, units, parts, chunk):
    per_row = 2 * units // 128
    rows_once = 32
    lines = rows_once * per_row

    def kernel(place_ref, even, odd, master, first, second, first_out, second_out, master_out, total):
        place = place_ref[0]
        for k in range(parts):
            grad = odd if k % 2 else even
            for j in range(chunk // 128):
                for which in range(2):
                    line = (place ^ k) * (2 * chunk // 128) + 2 * j + which
                    total[pl.ds(line, rows_once, per_row), :] = wide(
                        grad[k // 2, which, :, j * 128 : (j + 1) * 128]
                    )
        for t in range(lines // 64):
            own = slice(t * 64, (t + 1) * 64)
            got = adam_update(master[own, :], total[own, :], first[own, :], second[own, :], 0.1, 0.1)
            first_out[own, :] = got[0]
            second_out[own, :] = got[1]
            master_out[own, :] = got[2]

    block = pl.BlockSpec((lines, 128), lambda i, *_: (i, 0))
    stack = pl.BlockSpec((parts // 2, 2, rows_once, chunk), lambda i, *_: (0, 0, i, 0))
    call = pl.pallas_call(
        kernel,
        grid_spec=pltpu.PrefetchScalarGridSpec(
            num_scalar_prefetch=1,
            grid=(rows // rows_once,),
            in_specs=[stack] * 2 + [block] * 3,
            out_specs=[block] * 3,
            scratch_shapes=[pltpu.VMEM((lines, 128), jnp.float32)],
        ),
        out_shape=[jax.ShapeDtypeStruct((rows * per_row, 128), jnp.float32)] * 3,
        compiler_params=pltpu.CompilerParams(vmem_limit_bytes=VMEM_LIMIT),
        cost_estimate=NO_COST,
        name="ffn_update",
    )

    def fold(array):
        return jnp.swapaxes(array.reshape(rows, 2, units // 128, 128), 1, 2).reshape(-1, 128)

    def unfold(array):
        return jnp.swapaxes(array.reshape(rows, units // 128, 2, 128), 1, 2).reshape(rows, 2, units)

    def run(place, even, odd, master, first, second):
        return tuple(unfold(array) for array in call(place, even, odd, fold(master), fold(first), fold(second)))

    return run


def shards(
    tokens,
    doc_starts,
    attn_master,
    attn_mom,
    attn_sq,
    ffn_master,
    ffn_mom,
    ffn_sq,
    small_master,
    small_mom,
    small_sq,
    cotangent,
):
    ctx_count, wt_count = lax.axis_size("ctx"), lax.axis_size("wt")
    ctx_place, wt_place = lax.axis_index("ctx"), lax.axis_index("wt")
    batches, rows_here, width = tokens.shape
    qkv_cols = width + 2 * HS
    attn_columns = attn_master.shape[1]
    all_rows = batches * rows_here
    shard_rows = attn_master.shape[0]
    piece_rows = shard_rows // ctx_count
    chunk = FF // ctx_count
    chips = ctx_count // 2
    order = ctx_place ^ jnp.arange(ctx_count, dtype=jnp.int32)
    runs = 2 if batches % 2 == 0 else 1
    places = [jnp.stack([ctx_place, jnp.int32(run * (batches // runs))]) for run in range(runs)]
    place = places[0]
    wt_half = wt_count // 2
    out_rows = shard_rows // chips
    run_forward, run_backward = attention_kernels(batches, rows_here, width, ctx_count, runs)
    ffn_first, ffn_second, ffn_third, ffn_down = ffn_kernels(all_rows, width, chunk, wt_count)
    step = Steps()

    def both(own, got, place, bit, axis=0):
        ahead, behind = jnp.stack([own, got], axis), jnp.stack([got, own], axis)
        return jnp.where((place & bit) == 0, ahead, behind)

    def in_order(even, odd):
        buffer = jnp.zeros((ctx_count,) + even.shape[1:], even.dtype)
        for m in range(chips):
            buffer = put(buffer, even[m][None], ctx_place ^ (2 * m), 0)
            buffer = put(buffer, odd[m][None], ctx_place ^ (2 * m + 1), 0)
        return buffer

    def send_chips(piece):
        return [xor_send(piece, mask) for mask in range(2, ctx_count, 2)]

    def split_wt(total, bit):
        pairs = total.reshape((-1, 2) + total.shape[1:]) if bit == 1 else total[None]
        ahead, behind = pairs[:, 0], pairs[:, 1]
        here = (wt_place & bit) == 0
        return jnp.where(here, ahead, behind), jnp.where(here, behind, ahead)

    def add_low(*arrays):
        return low(sum(wide(array) for array in arrays))

    qkv = low(lax.dynamic_slice(attn_master, (ctx_place * piece_rows, 0), (piece_rows, qkv_cols)))
    out_start = (ctx_place // 2 * out_rows, qkv_cols + ctx_place % 2 * chunk)
    out = low(lax.dynamic_slice(attn_master, out_start, (out_rows, chunk)))
    qkv_got, out_got = xor_wt(qkv, 2), xor_wt(out, 2)
    qkv_got, out_got = together(qkv_got, out_got)
    qkv, out = both(qkv, qkv_got, wt_place, 2), both(out, out_got, wt_place, 2)
    qkv, out, small_late, ffn_late = together(qkv, out, small_master, ffn_master)
    qkv_got, out_got = xor_wt(qkv, 1), xor_wt(out, 1)
    back_low = cotangent.reshape(all_rows, width)
    ups, downs = [low(take(ffn_late[:, which], ctx_place, 1, chunk)) for which in range(2)]
    qkv_got, out_got, ups, downs = together(qkv_got, out_got, ups, downs)
    ups_got = xor_wt(ups, 2)
    qkv = both(qkv, qkv_got, wt_place, 1, 1).reshape((wt_count,) + qkv.shape[1:])
    qkv_got = send_chips(qkv)
    back_other = xor_send(back_low, 1)
    flat_tokens, qkv, small_late = together(tokens.reshape(all_rows, width), qkv, small_late)
    (
        gain_one,
        shift_one,
        gain_two,
        shift_two,
        bias_query,
        bias_out,
        bias_proj,
        bias_value,
        bias_hidden,
    ) = split_small(small_late)
    normed_low = low(layer_norm(wide(flat_tokens), gain_one, shift_one))
    bias_parts = bias_hidden.reshape(ctx_count, chunk)[order[::2]].reshape(1, chips * chunk)
    bias_near, bias_far = jnp.split(bias_parts, 2, axis=1)
    *qkv_got, normed_low, bias_near, bias_far, back_other, ups_got, downs = together(
        *qkv_got, normed_low, bias_near, bias_far, back_other, ups_got, downs
    )
    downs_got = xor_wt(downs, 2)
    out = both(out, out_got, wt_place, 1, 1).reshape((wt_count,) + out.shape[1:])
    qkv_even, out = together(jnp.stack([qkv] + qkv_got), out)
    qkv_odd = xor_send(qkv_even, 1)
    out_got = send_chips(out)
    blocks = both(qkv_even, qkv_odd, ctx_place, 1, 1)
    for n in range(chips.bit_length() - 1):
        pairs = blocks.reshape((-1, 2, 1 << n) + blocks.shape[1:])
        blocks = jnp.where((ctx_place & (2 << n)) == 0, pairs, pairs[:, ::-1]).reshape(blocks.shape)
    weight_qkv = jnp.transpose(blocks, (2, 0, 1, 3, 4)).reshape(width, qkv_cols)
    mixed = dot(normed_low, weight_qkv)
    queries = low(mixed[:, :width] + bias_query).reshape(batches, rows_here, width)
    kv_bias = jnp.concatenate([jnp.zeros((HS,), jnp.float32), bias_value])
    kv_local = low(mixed[:, width:] + kv_bias).reshape(batches, rows_here, 2 * HS)
    back_turned = turn_both(back_low, back_other)
    kv_local, back_turned, downs_got, *out_got = together(kv_local, back_turned, downs_got, *out_got)
    rest = jnp.concatenate([both(ups, ups_got, wt_place, 2), both(downs, downs_got, wt_place, 2)], axis=1)
    rest, kv_local = together(rest, kv_local)
    rest_got = xor_wt(rest, 1)
    kv_got = send_chips(kv_local)
    out_even = jnp.stack([out] + out_got)
    *kv_got, out_even, rest_got = together(*kv_got, out_even, rest_got)
    out_odd = xor_send(out_even, 1)
    kv_even = jnp.stack([kv_local] + kv_got)
    kv_odd = xor_send(kv_even, 1)
    here = (wt_place & 1) == 0
    rest_low, rest_high = [
        jnp.where(here, jnp.stack([own, got]), jnp.stack([got, own])) for own, got in zip(rest, rest_got)
    ]
    low_x, high_y, high_x, low_y = xor_send(rest_low, 2), xor_send(rest_high, 4), xor_send(rest_high, 2), xor_send(rest_low, 4)
    queries, rest_low, rest_high = together(queries, rest_low, rest_high)

    attended_low, attended, logs = step(run_forward, doc_starts, place, queries, kv_even, kv_odd)
    attended_low = attended_low.reshape(all_rows, width)
    attended_low, low_x, high_y, high_x, low_y = together(attended_low, low_x, high_y, high_x, low_y)
    low_diagonal, high_diagonal = xor_send(low_x, 4), xor_send(high_y, 2)

    def join_out(even, odd):
        columns = jnp.where((ctx_place & 1) == 0, jnp.concatenate([even, odd], axis=3), jnp.concatenate([odd, even], axis=3))
        for n in range(chips.bit_length() - 1):
            pairs = columns.reshape((-1, 2, 1 << n) + columns.shape[1:])
            columns = jnp.where((ctx_place & (2 << n)) == 0, pairs, pairs[:, ::-1]).reshape(columns.shape)
        return jnp.swapaxes(columns, 0, 1).reshape(width, width)

    weight_out = step(join_out, out_even, out_odd)
    hidden, normed_two = step(
        out_projection(all_rows, width), attended_low, weight_out, flat_tokens, bias_out[None], gain_two[None],
        shift_two[None],
    )
    normed_other = xor_send(normed_two, 1)

    weights = [rest_low, rest_high, low_x, high_x, low_y, high_y, low_diagonal, high_diagonal]
    flows = (normed_two, normed_other, back_low, back_other, back_turned)
    act_first, units_first, down_own, down_x, sums_first = step(
        lambda *args: ffn_first(*args[:6], *in_hbm(args[6:])), *flows, bias_near, *weights[:4]
    )
    act_second, units_second, down_y, down_top, down_bottom, sums_second, back_own, back_part = step(
        lambda *args: ffn_second(*args[:6], *in_hbm(args[6:])), *flows, bias_far, units_first, *weights
    )
    back_got = xor_send(back_part, 1)
    top_got, bottom_got = xor_send(down_top, 4), xor_send(down_bottom, 2)

    def meet(along_x, along_y, top, bottom):
        half = width // 2
        return (
            jnp.concatenate([add_low(along_x[:half], top), along_x[half:]]),
            jnp.concatenate([along_y[:half], add_low(along_y[half:], bottom)]),
        )

    up_own, up_x, up_y, up_top, up_bottom = step(
        lambda *args: ffn_third(*args[:2], *in_hbm(args[2:])), normed_two, normed_other, units_first, units_second
    )
    down_x, down_y = step(meet, down_x, down_y, top_got, bottom_got)
    down_got = [xor_send(down_x, 2), xor_send(down_y, 4)]
    top_got, bottom_got = xor_send(up_top, 4), xor_send(up_bottom, 2)

    grad_hidden, grad_hidden_low, grad_attended, hidden_sums = step(
        hidden_back(all_rows, width), back_own, back_got, hidden, back_low, gain_two[None], weight_out
    )
    grad_attended = grad_attended.reshape(batches, rows_here, width)
    def by_wt(*arrays):
        return split_wt(add_low(*arrays).reshape(wt_count, shard_rows, chunk), 1)

    def next_wt(kept, got):
        return split_wt(add_low(kept, got), 2)

    def kv_pieces(evens, odds):
        total = jnp.concatenate([add_low(a, b) for a, b in zip(evens, odds)], axis=1)
        return [total[m] for m in range(chips)]

    backs = [step(run_backward[0], doc_starts, places[0], queries, kv_even, kv_odd, attended, logs, grad_attended)]
    kv_got = [xor_send(backs[0][2], 1)]
    down_kept, down_sent = step(by_wt, down_own, *down_got)
    up_x, up_y = step(meet, up_x, up_y, top_got, bottom_got)
    grad_attended, down_kept, down_sent, up_x, up_y = together(grad_attended, down_kept, down_sent, up_x, up_y)
    down_got = xor_wt(down_sent, 1)
    up_got = [xor_send(up_x, 2), xor_send(up_y, 4)]
    backs += [
        step(run_backward[run], doc_starts, places[run], queries, kv_even, kv_odd, attended, logs, grad_attended)
        for run in range(1, runs)
    ]
    backs[-1] = list(backs[-1])
    *backs[-1], down_got, up_got[0], up_got[1] = together(*backs[-1], down_got, *up_got)
    kv_got += [xor_send(back[2], 1) for back in backs[1:]]
    grad_queries = [back[0] for back in backs]
    grad_query = jnp.concatenate(grad_queries).reshape(all_rows, width)
    down_kept, down_sent = next_wt(down_kept, down_got)
    up_kept, up_sent = by_wt(up_own, *up_got)
    down_kept, down_sent, up_kept, up_sent = together(down_kept, down_sent, up_kept, up_sent)
    down_got, up_got = xor_wt(down_sent, 2), xor_wt(up_sent, 1)
    kv_half = step(kv_pieces, [back[1] for back in backs], kv_got)
    kv_got = [xor_send(kv_half[m], 2 * m) for m in range(1, chips)]
    wide_even, wide_odd = step(
        attn_grads(all_rows, width, wt_count, ctx_count, piece_rows),
        place, normed_low, grad_query, attended_low, grad_hidden_low,
    )
    small_size = small_master.shape[0]
    up_kept, up_sent = step(next_wt, up_kept, up_got)
    kv_got[0], up_kept, up_sent, down_got = together(kv_got[0], up_kept, up_sent, down_got)
    up_got = xor_wt(up_sent, 2)
    input_grad, tail_even, tail_odd = step(
        stream_back(all_rows, width, ctx_count, wt_count, piece_rows),
        place, *[array.reshape(all_rows, 2 * HS) for array in (kv_half[0], *kv_got)], grad_query, weight_qkv,
        flat_tokens, gain_one[None], grad_hidden, normed_low, back_low, hidden_sums, sums_first, sums_second,
    )
    input_grad = input_grad.reshape(batches, rows_here, width)
    wide_odd, tail_odd = lax.optimization_barrier((wide_odd, tail_odd))
    wide_odd, tail_odd = xor_send(wide_odd, 1), xor_send(tail_odd, 1)
    def attn_pieces(wide_even, wide_odd, tail_even, tail_odd):
        total = jnp.concatenate([add_low(wide_even, wide_odd), add_low(tail_even, tail_odd)], axis=3)
        return [total[m] for m in range(chips)]

    attn_half = step(attn_pieces, wide_even, wide_odd, tail_even, tail_odd)
    attn_got = [xor_send(attn_half[m], 2 * m) for m in range(1, chips)]
    ffn_part = step(
        lambda *arrays: jnp.concatenate([add_low(*arrays[:2]), add_low(*arrays[2:])]), up_kept, up_got, down_kept, down_got
    )
    ffn_got = send_chips(ffn_part)
    down_out, down_other = step(
        lambda *args: ffn_down(*args[:2], *in_hbm(args[2:])), act_first, act_second, *weights
    )
    down_other = xor_send(down_other, 1)
    attn_kept, attn_sent = step(lambda *parts: split_wt(add_low(*parts), 1), attn_half[0], *attn_got)
    attn_got = xor_wt(attn_sent, 1)
    layer_out = step(
        lambda hidden, own, got: low(hidden + own + wide(got) + bias_proj).reshape(batches, rows_here, width),
        hidden, down_out, down_other,
    )
    attn_kept, attn_sent = step(lambda kept, got: split_wt(add_low(kept, got), 2), attn_kept, attn_got)
    attn_got = xor_wt(attn_sent, 2)
    attn_got, *ffn_got = together(attn_got, *ffn_got)
    ffn_even = jnp.stack([ffn_part] + ffn_got)
    ffn_odd = xor_send(ffn_even, 1)
    attn_part = step(lambda *parts: add_low(*parts)[0], attn_kept, attn_got)
    attn_got = send_chips(attn_part)

    ffn_new = step(
        ffn_update(shard_rows, FF, ctx_count, chunk), place, ffn_even, ffn_odd, ffn_master, ffn_mom, ffn_sq
    )
    attn_even = step(lambda *parts: jnp.stack(parts), attn_part, *attn_got)
    attn_odd = xor_send(attn_even, 1)
    small_total = in_order(attn_even[..., attn_columns:], attn_odd[..., attn_columns:])
    small_total = wide(small_total.reshape(-1))
    most = small_size - FF - HS
    small_total = jnp.concatenate(
        [small_total[:most], small_total[most + HS : most + 2 * HS], small_total[most + 2 * HS : most + 2 * HS + FF]]
    )
    small_new = adam_update(small_master, small_total, small_mom, small_sq, 1.0, 0.0)
    attn_new = attn_update(shard_rows, attn_columns, width, ctx_count, piece_rows)(
        place, attn_even, attn_odd, *in_hbm([attn_master, attn_mom, attn_sq])
    )
    return (layer_out, input_grad) + tuple(attn_new) + tuple(ffn_new) + tuple(small_new)


def shift_wt(array, shift):
    count = lax.axis_size("wt")
    return lax.ppermute(array, "wt", [(i, (i + shift) % count) for i in range(count)])


def whole_wt(piece, axis):
    count, place = lax.axis_size("wt"), lax.axis_index("wt")
    shape = list(piece.shape)
    shape[axis] *= count
    buffer = put(jnp.zeros(shape, piece.dtype), piece, place, axis)
    for shift in range(1, count):
        buffer = put(buffer, shift_wt(piece, shift), (place - shift) % count, axis)
    return buffer


def whole_ctx(piece):
    count = lax.axis_size("ctx")
    got = {0: piece}
    for mask in range(2, count, 2):
        got[mask] = xor_send(piece, mask)
    for mask in range(0, count, 2):
        got[mask + 1] = xor_send(got[mask], 1)
    return [got[mask] for mask in range(count)]


def sum_ctx(pieces):
    count = lax.axis_size("ctx")
    half = {}
    for mask in range(count - 2, -1, -2):
        other = xor_send(pieces[mask + 1], 1)
        half[mask] = low(wide(pieces[mask]) + wide(other))
    total = wide(half[0])
    for mask in range(2, count, 2):
        total = total + wide(xor_send(half[mask], mask))
    return total


def sum_wt(array, axis):
    count, place = lax.axis_size("wt"), lax.axis_index("wt")
    size = array.shape[axis] // count
    total = wide(take(array, place, axis, size))
    for shift in range(1, count):
        sent = take(array, (place + shift) % count, axis, size)
        total = total + wide(shift_wt(sent, shift))
    return total


def any_shards(
    tokens,
    doc_starts,
    attn_master,
    attn_mom,
    attn_sq,
    ffn_master,
    ffn_mom,
    ffn_sq,
    small_master,
    small_mom,
    small_sq,
    cotangent,
):
    ctx_count = lax.axis_size("ctx")
    ctx_place = lax.axis_index("ctx")
    wt_count = lax.axis_size("wt")
    batches, rows_here, width = tokens.shape
    heads = width // HS
    qkv_cols = width + 2 * HS
    all_rows = batches * rows_here
    shard_rows = attn_master.shape[0]
    piece_rows = shard_rows // ctx_count
    chunk = FF // ctx_count
    order = ctx_place ^ jnp.arange(ctx_count, dtype=jnp.int32)
    (
        gain_one,
        shift_one,
        gain_two,
        shift_two,
        bias_query,
        bias_out,
        bias_proj,
        bias_value,
        bias_hidden,
    ) = split_small(small_master)

    attn_piece = low(take(attn_master, ctx_place, 0, piece_rows))

    def whole_rows(piece):
        parts = whole_ctx(whole_wt(piece[None], 0))
        buffer = jnp.zeros((wt_count, ctx_count) + piece.shape, piece.dtype)
        for k, part in enumerate(parts):
            buffer = put(buffer, part[:, None], ctx_place ^ k, 1)
        return buffer.reshape((width,) + piece.shape[1:])

    weight_qkv = whole_rows(attn_piece[:, :qkv_cols])
    weight_out = whole_rows(attn_piece[:, qkv_cols:])
    ffn_piece = low(jnp.swapaxes(take(ffn_master, ctx_place, 2, chunk), 0, 1))
    ffn_parts = whole_ctx(whole_wt(ffn_piece, 1))
    bias_parts = bias_hidden.reshape(ctx_count, chunk)[order]

    stream = wide(tokens.reshape(all_rows, width))
    normed, norm_back_one = jax.vjp(layer_norm, stream, gain_one, shift_one)
    normed_low = low(normed)
    mixed = dot(normed_low, weight_qkv)
    queries = low(mixed[:, :width] + bias_query)
    kv_local = low(
        mixed[:, width:] + jnp.concatenate([jnp.zeros((HS,), jnp.float32), bias_value])
    ).reshape(batches, rows_here, 2 * HS)
    kv_parts = jnp.stack(whole_ctx(kv_local), axis=1).reshape(
        batches, ctx_count * rows_here, 2 * HS
    )
    keys_all, values_all = kv_parts[..., :HS], kv_parts[..., HS:]
    local_pos = jnp.arange(rows_here, dtype=jnp.int32)
    query_pos = ctx_place * rows_here + local_pos
    key_pos = (order[:, None] * rows_here + local_pos[None, :]).reshape(-1)
    queries = queries.reshape(batches, rows_here * heads, HS)
    scale = HS ** (-0.5)
    attended_list, log_list, allowed_list = [], [], []
    for b in range(batches):
        starts = doc_starts[b]
        query_doc = jnp.sum((starts[None, :] <= query_pos[:, None]).astype(jnp.int32), axis=1)
        key_doc = jnp.sum((starts[None, :] <= key_pos[:, None]).astype(jnp.int32), axis=1)
        allowed = (query_doc[:, None] == key_doc[None, :]) & (key_pos[None, :] <= query_pos[:, None])
        allowed = jnp.repeat(allowed, heads, axis=0)
        allowed_list.append(allowed)
        scores = jnp.where(allowed, cols_dot(queries[b], keys_all[b]) * scale, -1e30)
        peak = jnp.max(scores, axis=-1, keepdims=True)
        expo = jnp.exp(scores - peak)
        total = jnp.sum(expo, axis=-1, keepdims=True)
        attended_list.append(dot(low(expo / total), values_all[b]))
        log_list.append(peak + jnp.log(total))
    attended = jnp.stack(attended_list)
    attended_low = low(attended).reshape(all_rows, width)
    hidden = stream + dot(attended_low, weight_out) + bias_out
    normed_two, norm_back_two = jax.vjp(layer_norm, hidden, gain_two, shift_two)
    normed_two_low = low(normed_two)

    back_low = cotangent.reshape(all_rows, width)
    back_rows = wide(back_low)
    down_vals = jnp.zeros((all_rows, width), jnp.float32)
    grad_normed_two = jnp.zeros((all_rows, width), jnp.float32)
    ffn_grads, hidden_grads = [], []
    for k in range(ctx_count):
        weight_up, weight_down = ffn_parts[k][0], ffn_parts[k][1]
        value, slope = gelu_both(dot(normed_two_low, weight_up) + bias_parts[k])
        act = low(value)
        down_vals = down_vals + cols_dot(act, weight_down)
        grad_up = low(dot(back_low, weight_down) * slope)
        hidden_grads.append(jnp.sum(wide(grad_up), axis=0))
        grad_normed_two = grad_normed_two + cols_dot(grad_up, weight_up)
        ffn_grads.append(
            jnp.stack([low(rows_dot(normed_two_low, grad_up)), low(rows_dot(back_low, act))])
        )
    layer_out = low(hidden + down_vals + bias_proj).reshape(batches, rows_here, width)
    grad_bias_proj = jnp.sum(back_rows, axis=0)
    grad_bias_hidden = jnp.stack(hidden_grads)[order].reshape(FF)
    ffn_part = low(sum_wt(low(sum_ctx(ffn_grads)), 1))

    grad_hidden_part, grad_gain_two, grad_shift_two = norm_back_two(grad_normed_two)
    grad_hidden = back_rows + grad_hidden_part
    grad_bias_out = jnp.sum(grad_hidden, axis=0)
    grad_hidden_low = low(grad_hidden)
    grad_out = rows_dot(attended_low, grad_hidden_low)

    def summed_rows(grad):
        blocks = low(grad).reshape(wt_count, ctx_count, piece_rows, grad.shape[1])
        pieces = [take(blocks, ctx_place ^ k, 1, 1)[:, 0] for k in range(ctx_count)]
        part = low(sum_wt(low(sum_ctx(pieces)), 0)[0])
        buffer = jnp.zeros((ctx_count,) + part.shape, part.dtype)
        for k, got in enumerate(whole_ctx(part)):
            buffer = put(buffer, got[None], ctx_place ^ k, 0)
        return wide(buffer.reshape(shard_rows, grad.shape[1]))

    out_total = summed_rows(grad_out)

    grad_attended = low(cols_dot(grad_hidden_low, weight_out)).reshape(
        batches, rows_here * heads, HS
    )
    grad_query_list, grad_kv_list = [], []
    for b in range(batches):
        grads = grad_attended[b]
        delta = jnp.sum(wide(grads) * attended[b], axis=-1, keepdims=True)
        scores = jnp.where(allowed_list[b], cols_dot(queries[b], keys_all[b]) * scale, -1e30)
        weights = jnp.exp(scores - log_list[b])
        grad_scores = low(weights * (cols_dot(grads, values_all[b]) - delta))
        grad_query_list.append(low(dot(grad_scores, keys_all[b]) * scale))
        grad_kv_list.append(
            jnp.concatenate(
                [
                    low(rows_dot(grad_scores, queries[b]) * scale),
                    low(rows_dot(low(weights), grads)),
                ],
                axis=1,
            )
        )
    grad_query = jnp.stack(grad_query_list).reshape(all_rows, width)
    grad_kv = jnp.stack(grad_kv_list).reshape(batches, ctx_count, rows_here, 2 * HS)
    grad_kv_low = low(sum_ctx([grad_kv[:, k] for k in range(ctx_count)])).reshape(
        all_rows, 2 * HS
    )
    grad_bias_query = jnp.sum(wide(grad_query), axis=0)
    grad_bias_value = jnp.sum(wide(grad_kv_low[:, HS:]), axis=0)
    grad_mixed = jnp.concatenate([grad_query, grad_kv_low], axis=1)
    qkv_total = summed_rows(rows_dot(normed_low, grad_mixed))
    grad_normed = cols_dot(grad_mixed, weight_qkv)
    grad_stream_part, grad_gain_one, grad_shift_one = norm_back_one(grad_normed)
    input_grad = (grad_hidden + grad_stream_part).reshape(batches, rows_here, width)

    ffn_buffer = jnp.zeros((ctx_count,) + ffn_part.shape, ffn_part.dtype)
    for k, got in enumerate(whole_ctx(ffn_part)):
        ffn_buffer = put(ffn_buffer, got[None], ctx_place ^ k, 0)
    ffn_total = wide(jnp.transpose(ffn_buffer, (2, 1, 0, 3)).reshape(shard_rows, 2, FF))
    attn_total = jnp.concatenate([qkv_total, out_total], axis=1)
    grad_small = jnp.concatenate(
        [
            grad_gain_one,
            grad_shift_one,
            grad_gain_two,
            grad_shift_two,
            grad_bias_query,
            grad_bias_out,
            grad_bias_proj,
            grad_bias_value,
            grad_bias_hidden,
        ]
    )
    small_total = lax.psum(grad_small, ("ctx", "wt"))
    attn_new = adam_update(attn_master, attn_total, attn_mom, attn_sq, 0.1, 0.1)
    ffn_new = adam_update(ffn_master, ffn_total, ffn_mom, ffn_sq, 0.1, 0.1)
    small_new = adam_update(small_master, small_total, small_mom, small_sq, 1.0, 0.0)
    return (layer_out, input_grad) + attn_new + ffn_new + small_new


def solution(mesh):
    rows, cube = P("wt", None), P("wt", None, None)
    flow = P("wt", "ctx", None)
    in_specs = (flow, rows, rows, rows, rows, cube, cube, cube, P(), P(), P(), flow)
    out_specs = (flow, flow, rows, rows, rows, cube, cube, cube, P(), P(), P())
    ctx_count, wt_count = mesh.shape["ctx"], mesh.shape["wt"]
    fitted = (ctx_count, wt_count) == (8, 4)
    body = shards if fitted else any_shards
    return jax.shard_map(body, mesh=mesh, in_specs=in_specs, out_specs=out_specs, check_vma=False)
```

```python
import jax
import jax.numpy as jnp
from jax import lax
from jax.experimental import pallas as pl
from jax.experimental.pallas import tpu as pltpu
from jax.sharding import PartitionSpec as P

D = 768
HS = 64
FF = 3072
STEP = 10


NORM_EPS = 1e-05
GELU_COEF = 0.7978845608028654
GELU_CUBE = 0.044715
BETA_ONE = 0.9
BETA_TWO = 0.95
ADAM_EPS = 1e-08
VMEM_LIMIT = 22 << 20
NO_COST = pl.CostEstimate(flops=0, bytes_accessed=0, transcendentals=0)


def layer_norm(values, gain, shift):
    centre = values - jnp.mean(values, axis=-1, keepdims=True)
    spread = jnp.mean(centre * centre, axis=-1, keepdims=True)
    return centre * lax.rsqrt(spread + NORM_EPS) * gain + shift


def gelu_both(u):
    square = u * u
    share = 0.5 * jnp.tanh(u * (GELU_COEF * GELU_CUBE * square + GELU_COEF)) + 0.5
    bend = u * (6.0 * GELU_COEF * GELU_CUBE * square + 2.0 * GELU_COEF)
    return u * share, share * ((1.0 - share) * bend) + share


def split_small(small):
    return (
        small[0:D],
        small[D : 2 * D],
        small[2 * D : 3 * D],
        small[3 * D : 4 * D],
        small[4 * D : 5 * D],
        small[5 * D : 6 * D],
        small[6 * D : 7 * D],
        small[7 * D : 7 * D + HS],
        small[7 * D + HS :],
    )


def rows_dot(left, right):
    return lax.dot_general(
        left, right, (((0,), (0,)), ((), ())), preferred_element_type=jnp.float32
    )


def cols_dot(left, right):
    return lax.dot_general(
        left, right, (((1,), (1,)), ((), ())), preferred_element_type=jnp.float32
    )


def dot(left, right):
    return jnp.dot(left, right, preferred_element_type=jnp.float32)


def low(values):
    return values.astype(jnp.bfloat16)


def wide(values):
    return values.astype(jnp.float32)


def adam_update(master, gradient, first, second, step_rate, decay_rate):
    first_new = BETA_ONE * first + (1.0 - BETA_ONE) * gradient
    second_new = BETA_TWO * second + (1.0 - BETA_TWO) * gradient * gradient
    first_hat = first_new / (1.0 - BETA_ONE**STEP)
    second_hat = second_new / (1.0 - BETA_TWO**STEP)
    master_new = master - step_rate * (
        first_hat / (jnp.sqrt(second_hat) + ADAM_EPS) + decay_rate * master
    )
    return (first_new, second_new, master_new)


def xor_send(array, mask):
    count = lax.axis_size("ctx")
    return lax.ppermute(array, "ctx", [(i, i ^ mask) for i in range(count)])


def xor_wt(array, mask):
    count = lax.axis_size("wt")
    return lax.ppermute(array, "wt", [(i, i ^ mask) for i in range(count)])


class Steps:
    def __init__(self):
        self.last = ()

    def __call__(self, function, *args):
        flat, tree = jax.tree.flatten(args)
        held = lax.optimization_barrier(tuple(flat) + self.last)[: len(flat)]
        result = function(*jax.tree.unflatten(tree, held))
        self.last = tuple(jax.tree.leaves(result))
        return result


def loop(count, body, carry=0):
    return lax.fori_loop(0, count, body, carry)


def rows_at(i, size):
    return pl.ds(pl.multiple_of(i * size, size), size)


def together(*arrays):
    return lax.optimization_barrier(arrays)


def put(buffer, piece, place, axis):
    starts = [0] * buffer.ndim
    starts[axis] = place * piece.shape[axis]
    return lax.dynamic_update_slice(buffer, piece, starts)


def take(buffer, place, axis, size):
    return lax.dynamic_slice_in_dim(buffer, place * size, size, axis)


def attention_kernels(batches, rows, width, parts, runs):
    half_parts = parts // 2
    keys = parts * rows
    pair = 2 * HS
    groups = width // (2 * pair)
    factor = HS ** (-0.5) * 1.4426950408889634
    tile = 32

    def lanes(shape):
        return lax.broadcasted_iota(jnp.int32, shape, 1)

    def spread(even_ref, odd_ref, key_ref, value_ref):
        for j in range(parts):
            ref = even_ref if j < half_parts else odd_ref
            block = wide(ref[j % half_parts, 0])
            turned = pltpu.roll(block, HS, 1)
            first = lanes(block.shape) < HS
            here = pl.ds(j * rows, rows)
            key_ref[0, here, :] = low(jnp.where(first, block, 0.0))
            key_ref[1, here, :] = low(jnp.where(first, 0.0, turned))
            value_ref[0, here, :] = low(jnp.where(first, turned, 0.0))
            value_ref[1, here, :] = low(jnp.where(first, 0.0, block))

    def doc_begin(starts_ref, stream, positions):
        begin = jnp.zeros_like(positions)
        for j in range(starts_ref.shape[1]):
            start = starts_ref[stream, j]
            begin = jnp.where(start <= positions, jnp.maximum(begin, start), begin)
        return begin

    def forward(starts_ref, place_ref, query_ref, even_ref, odd_ref, low_ref, full_ref, log_ref, cap, key, value, weight):
        stream, place = pl.program_id(0), place_ref[0]
        spread(even_ref, odd_ref, key, value)
        query_pos = place * rows + lax.broadcasted_iota(jnp.int32, (rows, 1), 0)
        begin = doc_begin(starts_ref, stream, query_pos)
        for j in range(parts):
            key_pos = (place ^ (2 * (j % half_parts) + j // half_parts)) * rows + lax.broadcasted_iota(jnp.int32, (rows, rows), 1)
            allowed = (key_pos >= begin) & (key_pos <= query_pos)
            cap[:, j * rows : (j + 1) * rows] = jnp.where(allowed, 3.0e38, -1e30)
        column = lanes((tile, pair))
        logs = [jnp.zeros((tile, pair), jnp.float32) for _ in range(rows // tile)]
        for g in range(groups):
            at = g * 2 * pair
            two = jnp.concatenate([query_ref[0, :, at : at + pair], query_ref[0, :, at + pair : at + 2 * pair]], axis=0)
            totals = []
            for half in range(2):
                scores = cols_dot(two, key[half])
                norms = []
                for t in range(2 * rows // tile):
                    own = slice(t * tile, (t + 1) * tile)
                    n = t % (rows // tile)
                    part = jnp.minimum(scores[own] * factor, cap[n * tile : (n + 1) * tile, :])
                    peak = jnp.max(part, axis=1, keepdims=True)
                    expo = jnp.exp2(part - peak)
                    norm = jnp.sum(expo, axis=1, keepdims=True)
                    weight[half, own, :] = low(expo)
                    norms.append(norm)
                    head = 4 * g + 2 * (t * tile // rows) + half
                    logs[n] = jnp.where(column == head, peak + jnp.log2(norm), logs[n])
                totals.append(dot(weight[half], value[half]) / jnp.concatenate(norms, axis=0))
            total = totals[0] + totals[1]
            for j in range(2):
                part = total[j * rows : (j + 1) * rows]
                full_ref[0, :, at + j * pair : at + (j + 1) * pair] = part
                low_ref[0, :, at + j * pair : at + (j + 1) * pair] = low(part)
        for n, log in enumerate(logs):
            log_ref[0, n * tile : (n + 1) * tile, :] = log

    def backward(
        starts_ref, place_ref, query_ref, even_ref, odd_ref, full_ref, log_ref, grad_ref,
        query_grad_ref, even_grad_ref, odd_grad_ref,
        cap, key, value, key_turned, log_rows, delta_rows, weight_buf, score_buf, query_buf, grad_buf,
    ):
        stream, place = pl.program_id(0) + place_ref[1], place_ref[0]
        spread(even_ref, odd_ref, key, value)
        query_pos = place * rows + lax.broadcasted_iota(jnp.int32, (1, rows), 1)
        begin = doc_begin(starts_ref, stream, query_pos)
        for j in range(parts):
            key_pos = (place ^ (2 * (j % half_parts) + j // half_parts)) * rows + lax.broadcasted_iota(jnp.int32, (rows, rows), 0)
            allowed = (key_pos >= begin) & (key_pos <= query_pos)
            cap[j * rows : (j + 1) * rows, :] = jnp.where(allowed, 3.0e38, -1e30)
            here = pl.ds(j * rows, rows)
            key_turned[:, j * rows : (j + 1) * rows] = low(wide(key[0, here, :]).T[:HS])
        log_rows[...] = log_ref[0].T[: log_rows.shape[0]]
        head_of = lax.broadcasted_iota(jnp.int32, (delta_rows.shape[0], width), 1) // HS
        chosen = (head_of == lax.broadcasted_iota(jnp.int32, (delta_rows.shape[0], width), 0)).astype(jnp.float32)
        delta_rows[...] = lax.dot_general(
            chosen, wide(grad_ref[0]) * full_ref[0], (((1,), (1,)), ((), ())),
            precision=lax.Precision.HIGHEST, preferred_element_type=jnp.float32,
        )
        first = lanes((2 * rows, pair)) < HS
        for g in range(groups):
            at = g * 2 * pair
            both, both_grad = query_ref[0, :, at : at + 2 * pair], grad_ref[0, :, at : at + 2 * pair]
            two = jnp.concatenate([both[:, :pair], both[:, pair:]], axis=0)
            two_grad = jnp.concatenate([both_grad[:, :pair], both_grad[:, pair:]], axis=0)
            turned = []
            for half in range(2):
                h = 4 * g + half
                span = slice((2 * g + half) * 2 * rows, (2 * g + half + 1) * 2 * rows)
                keep = first if half == 0 else jnp.logical_not(first)
                query_buf[span, :] = low(jnp.where(keep, wide(two), 0.0))
                grad_buf[span, :] = low(jnp.where(keep, wide(two_grad), 0.0))
                log = jnp.concatenate([log_rows[h : h + 1, :], log_rows[h + 2 : h + 3, :]], axis=1)
                delta = jnp.concatenate([delta_rows[h : h + 1, :], delta_rows[h + 2 : h + 3, :]], axis=1)
                scores, weight_grads = cols_dot(key[half], two), cols_dot(value[half], two_grad)
                for t in range(keys // (2 * tile)):
                    own = slice(t * 2 * tile, (t + 1) * 2 * tile)
                    limit = cap[own, :]
                    limit = jnp.concatenate([limit, limit], axis=1)
                    weights = jnp.exp2(jnp.minimum(scores[own] * factor, limit) - log)
                    weight_buf[own, span] = low(weights)
                    score_buf[own, span] = low(weights * (weight_grads[own] - delta))
                turned.append(dot(key_turned[...], score_buf[:, span]))
            turned = jnp.concatenate(turned, axis=0) * HS ** (-0.5)
            query_grad_ref[0, :, at : at + pair] = low(turned[:, :rows].T)
            query_grad_ref[0, :, at + pair : at + 2 * pair] = low(turned[:, rows:].T)
        for odd, ref in enumerate((even_grad_ref, odd_grad_ref)):
            here = pl.ds(odd * half_parts * rows, half_parts * rows)
            value_sum = dot(weight_buf[here, :], grad_buf[...])
            key_sum = dot(score_buf[here, :], query_buf[...]) * HS ** (-0.5)
            value_sum = value_sum + pltpu.roll(value_sum, HS, 1)
            key_sum = key_sum + pltpu.roll(key_sum, HS, 1)
            both_sums = low(jnp.where(lanes(key_sum.shape) < HS, key_sum, value_sum))
            for j in range(half_parts):
                ref[j, 0] = both_sums[j * rows : (j + 1) * rows]

    def specs(first):
        return (
            pl.BlockSpec((1, rows, width), lambda b, *_: (b + first, 0, 0)),
            pl.BlockSpec((1, rows, pair), lambda b, *_: (b + first, 0, 0)),
            pl.BlockSpec((half_parts, 1, rows, pair), lambda b, *_: (0, b + first, 0, 0)),
        )

    flow, logs, blocks = specs(0)

    shared = [
        pltpu.VMEM((2, keys, pair), jnp.bfloat16),
        pltpu.VMEM((2, keys, pair), jnp.bfloat16),
    ]
    run_forward = pl.pallas_call(
        forward,
        grid_spec=pltpu.PrefetchScalarGridSpec(
            num_scalar_prefetch=2,
            grid=(batches,),
            in_specs=[flow, blocks, blocks],
            out_specs=[flow, flow, logs],
            scratch_shapes=[pltpu.VMEM((rows, keys), jnp.float32)]
            + shared
            + [pltpu.VMEM((2, 2 * rows, keys), jnp.bfloat16)],
        ),
        out_shape=[
            jax.ShapeDtypeStruct((batches, rows, width), jnp.bfloat16),
            jax.ShapeDtypeStruct((batches, rows, width), jnp.float32),
            jax.ShapeDtypeStruct((batches, rows, pair), jnp.float32),
        ],
        compiler_params=pltpu.CompilerParams(vmem_limit_bytes=VMEM_LIMIT),
        cost_estimate=NO_COST,
        name="attention_forward",
    )
    head_rows = -(-(width // HS) // 8) * 8
    all_columns = rows * (width // HS)
    count = batches // runs

    def call_backward(run):
        here_flow, here_logs, here_blocks = specs(run * count)
        return pl.pallas_call(
        backward,
        grid_spec=pltpu.PrefetchScalarGridSpec(
            num_scalar_prefetch=2,
            grid=(count,),
            in_specs=[here_flow, here_blocks, here_blocks, here_flow, here_logs, here_flow],
            out_specs=[flow, blocks, blocks],
            scratch_shapes=[pltpu.VMEM((keys, rows), jnp.float32)]
            + shared
            + [
                pltpu.VMEM((HS, keys), jnp.bfloat16),
                pltpu.VMEM((head_rows, rows), jnp.float32),
                pltpu.VMEM((head_rows, rows), jnp.float32),
                pltpu.VMEM((keys, all_columns), jnp.bfloat16),
                pltpu.VMEM((keys, all_columns), jnp.bfloat16),
                pltpu.VMEM((all_columns, pair), jnp.bfloat16),
                pltpu.VMEM((all_columns, pair), jnp.bfloat16),
            ],
        ),
        out_shape=[
            jax.ShapeDtypeStruct((count, rows, width), jnp.bfloat16),
            jax.ShapeDtypeStruct((half_parts, count, rows, pair), jnp.bfloat16),
            jax.ShapeDtypeStruct((half_parts, count, rows, pair), jnp.bfloat16),
        ],
        compiler_params=pltpu.CompilerParams(vmem_limit_bytes=VMEM_LIMIT),
        cost_estimate=NO_COST,
        name="attention_backward",
    )

    return run_forward, [call_backward(run) for run in range(runs)]


def in_hbm(arrays):
    return [pltpu.with_memory_space_constraint(array, pltpu.HBM) for array in arrays]


def ffn_kernels(rows, width, chunk, wt_count):
    units = 2 * chunk
    all_rows = 2 * rows
    block_rows = width // wt_count
    hbm = pl.BlockSpec(memory_space=pltpu.HBM)
    vmem = pl.BlockSpec(memory_space=pltpu.VMEM)
    params = pltpu.CompilerParams(vmem_limit_bytes=VMEM_LIMIT)

    def fetch(weights, which, held, sem):
        copies = []
        for n, arrays in enumerate(weights):
            blocks = [array.at[block] for array in arrays for block in range(array.shape[0])]
            for row, block in enumerate(blocks):
                copies.append(
                    pltpu.make_async_copy(
                        block.at[pl.ds(which * block_rows, block_rows), :],
                        held.at[pl.ds(row * block_rows, block_rows), pl.ds(n * chunk, chunk)],
                        sem.at[len(copies)],
                    )
                )
        for copy in copies:
            copy.start()
        return copies

    def send(pairs, sems):
        copies = [pltpu.make_async_copy(source, out, sems.at[n]) for n, (source, out) in enumerate(pairs)]
        for copy in copies:
            copy.start()
        return copies

    part_rows = 256
    tile = 16

    def units_of(inputs, grads, bias, held_up, held_down, act, grad_units):
        sums = jnp.zeros((8, units), jnp.float32)
        for s in range(2):

            def part(i, sums):
                here = rows_at(i, part_rows)
                up = dot(inputs[s][here, :], held_up[...])
                act_grad = dot(grads[s][here, :], held_down[...])
                for t in range(part_rows // tile):
                    own = slice(t * tile, (t + 1) * tile)
                    there = pl.ds(pl.multiple_of(s * rows + i * part_rows + t * tile, tile), tile)
                    value, slope = gelu_both(up[own] + bias)
                    grad = act_grad[own] * slope
                    act[there, :] = low(value)
                    grad_units[there, :] = low(grad)
                    sums = sums + (grad[:8] + grad[8:])
                return sums

            sums = loop(rows // part_rows, part, sums)
        return jnp.sum(sums, axis=0, keepdims=True)

    def product_of(turned, right, product):
        def part(i, carry):
            here = rows_at(i, part_rows)
            product[here, :] = low(dot(turned[here, :], right[...]))
            return carry

        loop(width // part_rows, part)

    def back_to(refs, sources, weights):
        for s, ref in enumerate(refs):

            def part(i, carry):
                here = pl.ds(pl.multiple_of(s * rows + i * part_rows, part_rows), part_rows)
                total = cols_dot(sources[0][here, :], weights[0][...]) + cols_dot(sources[1][here, :], weights[1][...])
                ref[rows_at(i, part_rows), :] = total.astype(ref.dtype)
                return carry

            loop(rows // part_rows, part)

    def halves(product, m):
        cols = pl.ds(m * chunk, chunk)
        return [product.at[pl.ds(h * width // 2, width // 2), cols] for h in range(2)]

    def first(
        own, other, grad_own, grad_other, turned, bias, w0, w1, w2, w3,
        act_out, units_out, out_a, out_b, sums_out,
        held_up, held_down, act, grad_units, product, sems, out_sems,
    ):
        weights = ((w0, w1), (w2, w3))
        copies = fetch(weights, 0, held_up, sems.at[0]) + fetch(weights, 1, held_down, sems.at[1])
        for copy in copies:
            copy.wait()
        sums_out[...] = units_of((own, other), (grad_own, grad_other), bias[...], held_up, held_down, act, grad_units)
        sent = send(((act, act_out), (grad_units, units_out)), out_sems.at[0])
        product_of(turned, act, product)
        sent += send(
            ((product.at[:, pl.ds(0, chunk)], out_a), (product.at[:, pl.ds(chunk, chunk)], out_b)), out_sems.at[1]
        )
        for copy in sent:
            copy.wait()

    def second(
        own, other, grad_own, grad_other, turned, bias, units_first, w0, w1, w2, w3, w4, w5, w6, w7,
        act_out, units_out, out_a, out_b, out_c, sums_out, back_own, back_other,
        held_up, held_more, held_down, act, grad_units, more_units, product, sems, out_sems, more_sem,
    ):
        weights, before = ((w4, w5), (w6, w7)), ((w0, w1), (w2, w3))
        copies = fetch(weights, 0, held_up, sems.at[0]) + fetch(weights, 1, held_down, sems.at[1])
        more = fetch(before, 0, held_more, sems.at[2])
        more.append(pltpu.make_async_copy(units_first, more_units, more_sem))
        more[-1].start()
        for copy in copies:
            copy.wait()
        sums_out[...] = units_of((own, other), (grad_own, grad_other), bias[...], held_up, held_down, act, grad_units)
        sent = send(((act, act_out), (grad_units, units_out)), out_sems.at[0])
        product_of(turned, act, product)
        top, bottom = halves(product, 1)
        sent += send(((product.at[:, pl.ds(0, chunk)], out_a), (top, out_b), (bottom, out_c)), out_sems.at[1])
        for copy in more:
            copy.wait()
        back_to((back_own, back_other), (grad_units, more_units), (held_up, held_more))
        for copy in sent:
            copy.wait()

    def third(own, other, units_a, units_b, out_0, out_1, out_2, out_3, out_4, turned, held, products, sems, out_sems):
        copies = send(((units_a, held.at[0]), (units_b, held.at[1])), sems)
        turn((own, other), turned)
        for copy in copies:
            copy.wait()
        products[1] = low(dot(turned[...], held[1]))
        top, bottom = halves(products.at[1], 1)
        sent = send(((products.at[1, :, pl.ds(0, chunk)], out_2), (top, out_3), (bottom, out_4)), out_sems.at[0])
        products[0] = low(dot(turned[...], held[0]))
        sent += send(
            ((products.at[0, :, pl.ds(0, chunk)], out_0), (products.at[0, :, pl.ds(chunk, chunk)], out_1)),
            out_sems.at[1],
        )
        for copy in sent:
            copy.wait()

    def down(act_a, act_b, w0, w1, w2, w3, w4, w5, w6, w7, own_ref, other_ref, held_a, held_b, sems):
        copies = fetch(((w0, w1), (w2, w3)), 1, held_a, sems.at[0]) + fetch(((w4, w5), (w6, w7)), 1, held_b, sems.at[1])
        for copy in copies:
            copy.wait()
        for s, ref in enumerate((own_ref, other_ref)):
            here = slice(s * rows, (s + 1) * rows)
            total = cols_dot(act_a[here, :], held_a[...]) + cols_dot(act_b[here, :], held_b[...])
            ref[...] = total.astype(ref.dtype)

    dma = pltpu.SemaphoreType.DMA
    held = pltpu.VMEM((width, units), jnp.bfloat16)
    flow = pltpu.VMEM((all_rows, units), jnp.bfloat16)
    flow_out = pltpu.HBM((all_rows, units), jnp.bfloat16)
    whole = pltpu.HBM((width, chunk), jnp.bfloat16)
    part = pltpu.HBM((width // 2, chunk), jnp.bfloat16)
    sums = jax.ShapeDtypeStruct((1, units), jnp.float32)
    own = jax.ShapeDtypeStruct((rows, width), jnp.float32)
    other = jax.ShapeDtypeStruct((rows, width), jnp.bfloat16)
    run_first = pl.pallas_call(
        first,
        in_specs=[vmem] * 6 + [hbm] * 4,
        out_specs=[hbm] * 4 + [vmem],
        out_shape=[flow_out, flow_out, whole, whole, sums],
        scratch_shapes=[held, held, flow, flow, held, dma((2, 2 * wt_count)), dma((2, 2))],
        compiler_params=params,
        cost_estimate=NO_COST,
        name="ffn_first",
    )
    run_second = pl.pallas_call(
        second,
        in_specs=[vmem] * 6 + [hbm] * 9,
        out_specs=[hbm] * 5 + [vmem] * 3,
        out_shape=[flow_out, flow_out, whole, part, part, sums, own, other],
        scratch_shapes=[held, held, held, flow, flow, flow, held, dma((3, 2 * wt_count)), dma((2, 3)), dma(())],
        compiler_params=params,
        cost_estimate=NO_COST,
        name="ffn_second",
    )
    run_third = pl.pallas_call(
        third,
        in_specs=[vmem] * 2 + [hbm] * 2,
        out_specs=[hbm] * 5,
        out_shape=[whole, whole, whole, part, part],
        scratch_shapes=[
            pltpu.VMEM((width, all_rows), jnp.bfloat16),
            pltpu.VMEM((2, all_rows, units), jnp.bfloat16),
            pltpu.VMEM((2, width, units), jnp.bfloat16),
            dma((2,)),
            dma((2, 3)),
        ],
        compiler_params=params,
        cost_estimate=NO_COST,
        name="ffn_grads",
    )
    run_down = pl.pallas_call(
        down,
        in_specs=[vmem] * 2 + [hbm] * 8,
        out_specs=[vmem] * 2,
        out_shape=[own, other],
        scratch_shapes=[held, held, dma((2, 2 * wt_count))],
        compiler_params=params,
        cost_estimate=NO_COST,
        name="ffn_down",
    )
    return run_first, run_second, run_third, run_down


def turn(refs, turned):
    rows = refs[0].shape[0]
    for s, ref in enumerate(refs):
        for i in range(rows // 128):
            block = wide(ref[i * 128 : (i + 1) * 128, :])
            turned[:, s * rows + i * 128 : s * rows + (i + 1) * 128] = low(block.T)


def turn_both(own, other):
    vmem = pl.BlockSpec(memory_space=pltpu.VMEM)
    rows, width = own.shape
    return pl.pallas_call(
        lambda a, b, out: turn((a, b), out),
        in_specs=[vmem] * 2,
        out_specs=vmem,
        out_shape=jax.ShapeDtypeStruct((width, 2 * rows), own.dtype),
        compiler_params=pltpu.CompilerParams(vmem_limit_bytes=VMEM_LIMIT),
        cost_estimate=NO_COST,
        name="turn",
    )(own, other)


def out_projection(rows, width):
    tile = 32

    def kernel(attended, weight, stream, bias, gain, shift, hidden_ref, normed_ref):
        product = dot(attended[...], weight[...])
        for t in range(rows // tile):
            here = slice(t * tile, (t + 1) * tile)
            hidden = wide(stream[here, :]) + product[here] + bias[...]
            hidden_ref[here, :] = hidden
            normed_ref[here, :] = low(layer_norm(hidden, gain[...], shift[...]))

    vmem = pl.BlockSpec(memory_space=pltpu.VMEM)
    return pl.pallas_call(
        kernel,
        in_specs=[vmem] * 6,
        out_specs=[vmem] * 2,
        out_shape=[
            jax.ShapeDtypeStruct((rows, width), jnp.float32),
            jax.ShapeDtypeStruct((rows, width), jnp.bfloat16),
        ],
        compiler_params=pltpu.CompilerParams(vmem_limit_bytes=VMEM_LIMIT),
        cost_estimate=NO_COST,
        name="out_projection",
    )


def norm_back(values, gain, grad):
    centre = values - jnp.mean(values, axis=-1, keepdims=True)
    scale = lax.rsqrt(jnp.mean(centre * centre, axis=-1, keepdims=True) + NORM_EPS)
    unit = centre * scale
    inner = grad * gain
    mean = jnp.mean(inner, axis=-1, keepdims=True)
    along = jnp.mean(inner * unit, axis=-1, keepdims=True)
    return scale * (inner - mean - unit * along), grad * unit


def fold_rows(values):
    total = values[:8]
    for i in range(1, values.shape[0] // 8):
        total = total + values[i * 8 : (i + 1) * 8]
    return total


def hidden_back(rows, width):
    tile = 32

    def kernel(own, got, hidden, back, gain, weight, grad_ref, low_ref, attended_ref, sums_ref):
        sums = [jnp.zeros((8, width), jnp.float32) for _ in range(3)]
        for t in range(rows // tile):
            here = slice(t * tile, (t + 1) * tile)
            pulled, terms = norm_back(hidden[here, :], gain[...], own[here, :] + wide(got[here, :]))
            grad = wide(back[here, :]) + pulled
            grad_ref[here, :] = grad
            low_ref[here, :] = low(grad)
            for n, part in enumerate((terms, own[here, :] + wide(got[here, :]), grad)):
                sums[n] = sums[n] + fold_rows(part)
        for n in range(3):
            sums_ref[n : n + 1, :] = jnp.sum(sums[n], axis=0, keepdims=True)
        attended_ref[...] = low(cols_dot(low_ref[...], weight[...]))

    vmem = pl.BlockSpec(memory_space=pltpu.VMEM)
    return pl.pallas_call(
        kernel,
        in_specs=[vmem] * 6,
        out_specs=[vmem] * 4,
        out_shape=[
            jax.ShapeDtypeStruct((rows, width), jnp.float32),
            jax.ShapeDtypeStruct((rows, width), jnp.bfloat16),
            jax.ShapeDtypeStruct((rows, width), jnp.bfloat16),
            jax.ShapeDtypeStruct((3, width), jnp.float32),
        ],
        compiler_params=pltpu.CompilerParams(vmem_limit_bytes=VMEM_LIMIT),
        cost_estimate=NO_COST,
        name="hidden_back",
    )


def stream_back(rows, width, parts, row_groups, piece):
    tile = 32
    chips = parts // 2

    def kernel(
        place_ref, kv_0, kv_1, kv_2, kv_3, queries, weight, tokens, gain, grad_hidden, normed, back, hidden_sums,
        units_a, units_b, input_ref, even_ref, odd_ref, grad_kv, grads, turned, product, small,
    ):
        place = place_ref[0]
        sums = [jnp.zeros((8, width), jnp.float32) for _ in range(4)]
        value_sums = jnp.zeros((8, 2 * HS), jnp.float32)
        for t in range(rows // tile):
            here = slice(t * tile, (t + 1) * tile)
            total = wide(kv_0[here, :]) + wide(kv_1[here, :]) + wide(kv_2[here, :]) + wide(kv_3[here, :])
            grad_kv[here, :] = low(total)
            value_sums = value_sums + fold_rows(total)
        turn((normed,), turned)
        product[...] = dot(turned[...], grad_kv[...])
        grads[...] = cols_dot(queries[...], weight[:, :width]) + cols_dot(grad_kv[...], weight[:, width:])
        for t in range(rows // tile):
            here = slice(t * tile, (t + 1) * tile)
            grad = grads[here, :]
            pulled, terms = norm_back(wide(tokens[here, :]), gain[...], grad)
            input_ref[here, :] = grad_hidden[here, :] + pulled
            for n, part in enumerate((terms, grad, wide(queries[here, :]), wide(back[here, :]))):
                sums[n] = sums[n] + fold_rows(part)
        sums = [jnp.sum(part, axis=0, keepdims=True) for part in sums]
        small[...] = jnp.zeros_like(small)
        rows_in = (sums[0], sums[1], hidden_sums[0:1, :], hidden_sums[1:2, :], sums[2], hidden_sums[2:3, :], sums[3])
        for n, row in enumerate(rows_in):
            for j in range(width // 128):
                line = n * (width // 128) + j
                small[line : line + 1, :] = row[:, j * 128 : (j + 1) * 128]
        start = 7 * (width // 128)
        small[start : start + 1, :] = jnp.sum(value_sums, axis=0, keepdims=True)
        lines = FF // parts // 128
        for m in range(chips):
            units = (units_a, units_b)[m // 2]
            for j in range(lines):
                line = start + 1 + (place ^ (2 * m)) * lines + j
                at = (m % 2 * lines + j) * 128
                small[pl.ds(line, 1), :] = units[:, at : at + 128]
        for k in range(parts):
            ref = odd_ref if k % 2 else even_ref
            mine = low(small[pl.ds(pl.multiple_of((place ^ k) * piece, 8), piece), :])
            for w in range(row_groups):
                at = pl.multiple_of(w * piece * parts + (place ^ k) * piece, 8)
                ref[k // 2, w, :, :128] = low(product[pl.ds(at, piece), :])
                ref[k // 2, w, :, 128:] = mine

    vmem = pl.BlockSpec(memory_space=pltpu.VMEM)
    stack = jax.ShapeDtypeStruct((chips, row_groups, piece, 256), jnp.bfloat16)
    return pl.pallas_call(
        kernel,
        in_specs=[pl.BlockSpec(memory_space=pltpu.SMEM)] + [vmem] * 14,
        out_specs=[vmem] * 3,
        out_shape=[jax.ShapeDtypeStruct((rows, width), jnp.float32), stack, stack],
        scratch_shapes=[
            pltpu.VMEM((rows, 2 * HS), jnp.bfloat16),
            pltpu.VMEM((rows, width), jnp.float32),
            pltpu.VMEM((width, rows), jnp.bfloat16),
            pltpu.VMEM((width, 2 * HS), jnp.float32),
            pltpu.VMEM((parts * piece, 128), jnp.float32),
        ],
        compiler_params=pltpu.CompilerParams(vmem_limit_bytes=VMEM_LIMIT),
        cost_estimate=NO_COST,
        name="stream_back",
    )


def attn_grads(rows, width, row_groups, parts, piece):
    def kernel(place_ref, left_a, right_a, left_b, right_b, even_ref, odd_ref, turned, total):
        place = place_ref[0]
        for n, (left, right) in enumerate(((left_a, right_a), (left_b, right_b))):
            for i in range(rows // 128):
                turned[:, i * 128 : (i + 1) * 128] = low(wide(left[i * 128 : (i + 1) * 128, :]).T)
            total[:, n * width : (n + 1) * width] = dot(turned[...], right[...])
        for k in range(parts):
            ref = odd_ref if k % 2 else even_ref
            for w in range(row_groups):
                at = pl.multiple_of(w * piece * parts + (place ^ k) * piece, 8)
                ref[k // 2, w] = low(total[pl.ds(at, piece), :])

    vmem = pl.BlockSpec(memory_space=pltpu.VMEM)
    shape = jax.ShapeDtypeStruct((parts // 2, row_groups, piece, 2 * width), jnp.bfloat16)
    return pl.pallas_call(
        kernel,
        grid_spec=pltpu.PrefetchScalarGridSpec(
            num_scalar_prefetch=1,
            grid=(),
            in_specs=[vmem] * 4,
            out_specs=[vmem] * 2,
            scratch_shapes=[pltpu.VMEM((width, rows), jnp.bfloat16), pltpu.VMEM((width, 2 * width), jnp.float32)],
        ),
        out_shape=[shape] * 2,
        compiler_params=pltpu.CompilerParams(vmem_limit_bytes=VMEM_LIMIT),
        cost_estimate=NO_COST,
        name="attn_grads",
    )


def attn_update(rows, columns, width, parts, piece):
    qkv = columns - width
    whole = columns + 128 * -(-(7 * width + HS + FF) // (128 * piece * parts))

    def kernel(place_ref, even_ref, odd_ref, master, first, second, *outs):
        core = place_ref[0] % 2
        for ref, which in ((even_ref, core), (odd_ref, 1 - core)):
            here = pl.ds(pl.multiple_of(which * piece, 8), piece)
            for cols, source in (
                (slice(0, width), slice(0, width)),
                (slice(width, qkv), slice(2 * width, columns)),
                (slice(qkv, columns), slice(width, 2 * width)),
            ):
                grad = wide(ref[0, :, source])
                got = adam_update(master[here, cols], grad, first[here, cols], second[here, cols], 0.1, 0.1)
                outs[0][here, cols] = got[0]
                outs[1][here, cols] = got[1]
                outs[2][here, cols] = got[2]

    block = pl.BlockSpec((2 * piece, columns), lambda i, place: (i, 0))
    stack = pl.BlockSpec((1, piece, whole), lambda i, place: (i ^ (place[0] // 2), 0, 0))
    return pl.pallas_call(
        kernel,
        grid_spec=pltpu.PrefetchScalarGridSpec(
            num_scalar_prefetch=1,
            grid=(parts // 2,),
            in_specs=[stack] * 2 + [block] * 3,
            out_specs=[block] * 3,
            scratch_shapes=[],
        ),
        out_shape=[jax.ShapeDtypeStruct((rows, columns), jnp.float32)] * 3,
        compiler_params=pltpu.CompilerParams(vmem_limit_bytes=VMEM_LIMIT),
        cost_estimate=NO_COST,
        name="attn_update",
    )


def ffn_update(rows, units, parts, chunk):
    per_row = 2 * units // 128
    rows_once = 32
    lines = rows_once * per_row

    def kernel(place_ref, even, odd, master, first, second, first_out, second_out, master_out, total):
        place = place_ref[0]
        for k in range(parts):
            grad = odd if k % 2 else even
            for j in range(chunk // 128):
                for which in range(2):
                    line = (place ^ k) * (2 * chunk // 128) + 2 * j + which
                    total[pl.ds(line, rows_once, per_row), :] = wide(
                        grad[k // 2, which, :, j * 128 : (j + 1) * 128]
                    )
        for t in range(lines // 64):
            own = slice(t * 64, (t + 1) * 64)
            got = adam_update(master[own, :], total[own, :], first[own, :], second[own, :], 0.1, 0.1)
            first_out[own, :] = got[0]
            second_out[own, :] = got[1]
            master_out[own, :] = got[2]

    block = pl.BlockSpec((lines, 128), lambda i, *_: (i, 0))
    stack = pl.BlockSpec((parts // 2, 2, rows_once, chunk), lambda i, *_: (0, 0, i, 0))
    call = pl.pallas_call(
        kernel,
        grid_spec=pltpu.PrefetchScalarGridSpec(
            num_scalar_prefetch=1,
            grid=(rows // rows_once,),
            in_specs=[stack] * 2 + [block] * 3,
            out_specs=[block] * 3,
            scratch_shapes=[pltpu.VMEM((lines, 128), jnp.float32)],
        ),
        out_shape=[jax.ShapeDtypeStruct((rows * per_row, 128), jnp.float32)] * 3,
        compiler_params=pltpu.CompilerParams(vmem_limit_bytes=VMEM_LIMIT),
        cost_estimate=NO_COST,
        name="ffn_update",
    )

    def fold(array):
        return jnp.swapaxes(array.reshape(rows, 2, units // 128, 128), 1, 2).reshape(-1, 128)

    def unfold(array):
        return jnp.swapaxes(array.reshape(rows, units // 128, 2, 128), 1, 2).reshape(rows, 2, units)

    def run(place, even, odd, master, first, second):
        return tuple(unfold(array) for array in call(place, even, odd, fold(master), fold(first), fold(second)))

    return run


def shards(
    tokens,
    doc_starts,
    attn_master,
    attn_mom,
    attn_sq,
    ffn_master,
    ffn_mom,
    ffn_sq,
    small_master,
    small_mom,
    small_sq,
    cotangent,
):
    ctx_count, wt_count = lax.axis_size("ctx"), lax.axis_size("wt")
    ctx_place, wt_place = lax.axis_index("ctx"), lax.axis_index("wt")
    batches, rows_here, width = tokens.shape
    qkv_cols = width + 2 * HS
    attn_columns = attn_master.shape[1]
    all_rows = batches * rows_here
    shard_rows = attn_master.shape[0]
    piece_rows = shard_rows // ctx_count
    chunk = FF // ctx_count
    chips = ctx_count // 2
    order = ctx_place ^ jnp.arange(ctx_count, dtype=jnp.int32)
    runs = 2 if batches % 2 == 0 else 1
    places = [jnp.stack([ctx_place, jnp.int32(run * (batches // runs))]) for run in range(runs)]
    place = places[0]
    wt_half = wt_count // 2
    out_rows = shard_rows // chips
    run_forward, run_backward = attention_kernels(batches, rows_here, width, ctx_count, runs)
    ffn_first, ffn_second, ffn_third, ffn_down = ffn_kernels(all_rows, width, chunk, wt_count)
    step = Steps()

    def both(own, got, place, bit, axis=0):
        ahead, behind = jnp.stack([own, got], axis), jnp.stack([got, own], axis)
        return jnp.where((place & bit) == 0, ahead, behind)

    def in_order(even, odd):
        buffer = jnp.zeros((ctx_count,) + even.shape[1:], even.dtype)
        for m in range(chips):
            buffer = put(buffer, even[m][None], ctx_place ^ (2 * m), 0)
            buffer = put(buffer, odd[m][None], ctx_place ^ (2 * m + 1), 0)
        return buffer

    def send_chips(piece):
        return [xor_send(piece, mask) for mask in range(2, ctx_count, 2)]

    def split_wt(total, bit):
        pairs = total.reshape((-1, 2) + total.shape[1:]) if bit == 1 else total[None]
        ahead, behind = pairs[:, 0], pairs[:, 1]
        here = (wt_place & bit) == 0
        return jnp.where(here, ahead, behind), jnp.where(here, behind, ahead)

    def add_low(*arrays):
        return low(sum(wide(array) for array in arrays))

    qkv = low(lax.dynamic_slice(attn_master, (ctx_place * piece_rows, 0), (piece_rows, qkv_cols)))
    out_start = (ctx_place // 2 * out_rows, qkv_cols + ctx_place % 2 * chunk)
    out = low(lax.dynamic_slice(attn_master, out_start, (out_rows, chunk)))
    rest = low(jnp.swapaxes(take(ffn_master, ctx_place, 2, chunk), 0, 1).reshape(2 * shard_rows, chunk))
    qkv_got, out_got = xor_wt(qkv, 2), xor_wt(out, 2)
    qkv_got, out_got, rest = together(qkv_got, out_got, rest)
    ups, downs = rest[:shard_rows], rest[shard_rows:]
    ups_got = xor_wt(ups, 2)
    qkv, out = both(qkv, qkv_got, wt_place, 2), both(out, out_got, wt_place, 2)
    qkv, out, small_late = together(qkv, out, small_master)
    qkv_got, out_got = xor_wt(qkv, 1), xor_wt(out, 1)
    back_low = cotangent.reshape(all_rows, width)
    qkv_got, out_got, ups_got, downs = together(qkv_got, out_got, ups_got, downs)
    downs_got = xor_wt(downs, 2)
    qkv = both(qkv, qkv_got, wt_place, 1, 1).reshape((wt_count,) + qkv.shape[1:])
    qkv_got = send_chips(qkv)
    back_other = xor_send(back_low, 1)
    flat_tokens, qkv, small_late = together(tokens.reshape(all_rows, width), qkv, small_late)
    (
        gain_one,
        shift_one,
        gain_two,
        shift_two,
        bias_query,
        bias_out,
        bias_proj,
        bias_value,
        bias_hidden,
    ) = split_small(small_late)
    normed_low = low(layer_norm(wide(flat_tokens), gain_one, shift_one))
    bias_parts = bias_hidden.reshape(ctx_count, chunk)[order[::2]].reshape(1, chips * chunk)
    bias_near, bias_far = jnp.split(bias_parts, 2, axis=1)
    ups = both(ups, ups_got, wt_place, 2)
    *qkv_got, normed_low, bias_near, bias_far, back_other, downs_got, ups = together(
        *qkv_got, normed_low, bias_near, bias_far, back_other, downs_got, ups
    )
    ups_got = xor_wt(ups, 1)
    out = both(out, out_got, wt_place, 1, 1).reshape((wt_count,) + out.shape[1:])
    qkv_even, out = together(jnp.stack([qkv] + qkv_got), out)
    qkv_odd = xor_send(qkv_even, 1)
    out_got = send_chips(out)
    blocks = both(qkv_even, qkv_odd, ctx_place, 1, 1)
    for n in range(chips.bit_length() - 1):
        pairs = blocks.reshape((-1, 2, 1 << n) + blocks.shape[1:])
        blocks = jnp.where((ctx_place & (2 << n)) == 0, pairs, pairs[:, ::-1]).reshape(blocks.shape)
    weight_qkv = jnp.transpose(blocks, (2, 0, 1, 3, 4)).reshape(width, qkv_cols)
    mixed = dot(normed_low, weight_qkv)
    queries = low(mixed[:, :width] + bias_query).reshape(batches, rows_here, width)
    kv_bias = jnp.concatenate([jnp.zeros((HS,), jnp.float32), bias_value])
    kv_local = low(mixed[:, width:] + kv_bias).reshape(batches, rows_here, 2 * HS)
    back_turned = turn_both(back_low, back_other)
    downs = both(downs, downs_got, wt_place, 2)
    kv_local, back_turned, ups_got, downs, *out_got = together(kv_local, back_turned, ups_got, downs, *out_got)
    downs_got = xor_wt(downs, 1)
    kv_got = send_chips(kv_local)
    out_even = jnp.stack([out] + out_got)
    *kv_got, out_even, downs_got = together(*kv_got, out_even, downs_got)
    out_odd = xor_send(out_even, 1)
    kv_even = jnp.stack([kv_local] + kv_got)
    kv_odd = xor_send(kv_even, 1)
    rest = jnp.concatenate([both(ups, ups_got, wt_place, 1, 1), both(downs, downs_got, wt_place, 1, 1)], axis=2)
    rest_low, rest_high = rest[0], rest[1]
    low_x, high_y, high_x, low_y = xor_send(rest_low, 2), xor_send(rest_high, 4), xor_send(rest_high, 2), xor_send(rest_low, 4)
    queries, rest_low, rest_high = together(queries, rest_low, rest_high)

    attended_low, attended, logs = step(run_forward, doc_starts, place, queries, kv_even, kv_odd)
    attended_low = attended_low.reshape(all_rows, width)
    attended_low, low_x, high_y, high_x, low_y = together(attended_low, low_x, high_y, high_x, low_y)
    low_diagonal, high_diagonal = xor_send(low_x, 4), xor_send(high_y, 2)

    def join_out(even, odd):
        columns = jnp.where((ctx_place & 1) == 0, jnp.concatenate([even, odd], axis=3), jnp.concatenate([odd, even], axis=3))
        for n in range(chips.bit_length() - 1):
            pairs = columns.reshape((-1, 2, 1 << n) + columns.shape[1:])
            columns = jnp.where((ctx_place & (2 << n)) == 0, pairs, pairs[:, ::-1]).reshape(columns.shape)
        return jnp.swapaxes(columns, 0, 1).reshape(width, width)

    weight_out = step(join_out, out_even, out_odd)
    hidden, normed_two = step(
        out_projection(all_rows, width), attended_low, weight_out, flat_tokens, bias_out[None], gain_two[None],
        shift_two[None],
    )
    normed_other = xor_send(normed_two, 1)

    weights = [rest_low, rest_high, low_x, high_x, low_y, high_y, low_diagonal, high_diagonal]
    flows = (normed_two, normed_other, back_low, back_other, back_turned)
    act_first, units_first, down_own, down_x, sums_first = step(
        lambda *args: ffn_first(*args[:6], *in_hbm(args[6:])), *flows, bias_near, *weights[:4]
    )
    act_second, units_second, down_y, down_top, down_bottom, sums_second, back_own, back_part = step(
        lambda *args: ffn_second(*args[:6], *in_hbm(args[6:])), *flows, bias_far, units_first, *weights
    )
    back_got = xor_send(back_part, 1)
    top_got, bottom_got = xor_send(down_top, 4), xor_send(down_bottom, 2)

    def meet(along_x, along_y, top, bottom):
        half = width // 2
        return (
            jnp.concatenate([add_low(along_x[:half], top), along_x[half:]]),
            jnp.concatenate([along_y[:half], add_low(along_y[half:], bottom)]),
        )

    up_own, up_x, up_y, up_top, up_bottom = step(
        lambda *args: ffn_third(*args[:2], *in_hbm(args[2:])), normed_two, normed_other, units_first, units_second
    )
    down_x, down_y = step(meet, down_x, down_y, top_got, bottom_got)
    down_got = [xor_send(down_x, 2), xor_send(down_y, 4)]
    top_got, bottom_got = xor_send(up_top, 4), xor_send(up_bottom, 2)

    grad_hidden, grad_hidden_low, grad_attended, hidden_sums = step(
        hidden_back(all_rows, width), back_own, back_got, hidden, back_low, gain_two[None], weight_out
    )
    grad_attended = grad_attended.reshape(batches, rows_here, width)
    def by_wt(*arrays):
        return split_wt(add_low(*arrays).reshape(wt_count, shard_rows, chunk), 1)

    def next_wt(kept, got):
        return split_wt(add_low(kept, got), 2)

    def kv_pieces(evens, odds):
        total = jnp.concatenate([add_low(a, b) for a, b in zip(evens, odds)], axis=1)
        return [total[m] for m in range(chips)]

    backs = [step(run_backward[0], doc_starts, places[0], queries, kv_even, kv_odd, attended, logs, grad_attended)]
    kv_got = [xor_send(backs[0][2], 1)]
    down_kept, down_sent = step(by_wt, down_own, *down_got)
    up_x, up_y = step(meet, up_x, up_y, top_got, bottom_got)
    grad_attended, down_kept, down_sent, up_x, up_y = together(grad_attended, down_kept, down_sent, up_x, up_y)
    down_got = xor_wt(down_sent, 1)
    up_got = [xor_send(up_x, 2), xor_send(up_y, 4)]
    backs += [
        step(run_backward[run], doc_starts, places[run], queries, kv_even, kv_odd, attended, logs, grad_attended)
        for run in range(1, runs)
    ]
    backs[-1] = list(backs[-1])
    *backs[-1], down_got, up_got[0], up_got[1] = together(*backs[-1], down_got, *up_got)
    kv_got += [xor_send(back[2], 1) for back in backs[1:]]
    grad_queries = [back[0] for back in backs]
    grad_query = jnp.concatenate(grad_queries).reshape(all_rows, width)
    down_kept, down_sent = next_wt(down_kept, down_got)
    up_kept, up_sent = by_wt(up_own, *up_got)
    down_kept, down_sent, up_kept, up_sent = together(down_kept, down_sent, up_kept, up_sent)
    down_got, up_got = xor_wt(down_sent, 2), xor_wt(up_sent, 1)
    kv_half = step(kv_pieces, [back[1] for back in backs], kv_got)
    kv_got = [xor_send(kv_half[m], 2 * m) for m in range(1, chips)]
    wide_even, wide_odd = step(
        attn_grads(all_rows, width, wt_count, ctx_count, piece_rows),
        place, normed_low, grad_query, attended_low, grad_hidden_low,
    )
    small_size = small_master.shape[0]
    up_kept, up_sent = step(next_wt, up_kept, up_got)
    kv_got[0], up_kept, up_sent, down_got = together(kv_got[0], up_kept, up_sent, down_got)
    up_got = xor_wt(up_sent, 2)
    input_grad, tail_even, tail_odd = step(
        stream_back(all_rows, width, ctx_count, wt_count, piece_rows),
        place, *[array.reshape(all_rows, 2 * HS) for array in (kv_half[0], *kv_got)], grad_query, weight_qkv,
        flat_tokens, gain_one[None], grad_hidden, normed_low, back_low, hidden_sums, sums_first, sums_second,
    )
    input_grad = input_grad.reshape(batches, rows_here, width)
    wide_odd, tail_odd = lax.optimization_barrier((wide_odd, tail_odd))
    wide_odd, tail_odd = xor_send(wide_odd, 1), xor_send(tail_odd, 1)
    def attn_pieces(wide_even, wide_odd, tail_even, tail_odd):
        total = jnp.concatenate([add_low(wide_even, wide_odd), add_low(tail_even, tail_odd)], axis=3)
        return [total[m] for m in range(chips)]

    attn_half = step(attn_pieces, wide_even, wide_odd, tail_even, tail_odd)
    attn_got = [xor_send(attn_half[m], 2 * m) for m in range(1, chips)]
    ffn_part = step(
        lambda *arrays: jnp.concatenate([add_low(*arrays[:2]), add_low(*arrays[2:])]), up_kept, up_got, down_kept, down_got
    )
    ffn_got = send_chips(ffn_part)
    down_out, down_other = step(
        lambda *args: ffn_down(*args[:2], *in_hbm(args[2:])), act_first, act_second, *weights
    )
    down_other = xor_send(down_other, 1)
    attn_kept, attn_sent = step(lambda *parts: split_wt(add_low(*parts), 1), attn_half[0], *attn_got)
    attn_got = xor_wt(attn_sent, 1)
    layer_out = step(
        lambda hidden, own, got: low(hidden + own + wide(got) + bias_proj).reshape(batches, rows_here, width),
        hidden, down_out, down_other,
    )
    attn_kept, attn_sent = step(lambda kept, got: split_wt(add_low(kept, got), 2), attn_kept, attn_got)
    attn_got = xor_wt(attn_sent, 2)
    attn_got, *ffn_got = together(attn_got, *ffn_got)
    ffn_even = jnp.stack([ffn_part] + ffn_got)
    ffn_odd = xor_send(ffn_even, 1)
    attn_part = step(lambda *parts: add_low(*parts)[0], attn_kept, attn_got)
    attn_got = send_chips(attn_part)

    ffn_new = step(
        ffn_update(shard_rows, FF, ctx_count, chunk), place, ffn_even, ffn_odd, ffn_master, ffn_mom, ffn_sq
    )
    attn_even = step(lambda *parts: jnp.stack(parts), attn_part, *attn_got)
    attn_odd = xor_send(attn_even, 1)
    small_total = in_order(attn_even[..., attn_columns:], attn_odd[..., attn_columns:])
    small_total = wide(small_total.reshape(-1))
    most = small_size - FF - HS
    small_total = jnp.concatenate(
        [small_total[:most], small_total[most + HS : most + 2 * HS], small_total[most + 2 * HS : most + 2 * HS + FF]]
    )
    small_new = adam_update(small_master, small_total, small_mom, small_sq, 1.0, 0.0)
    attn_new = attn_update(shard_rows, attn_columns, width, ctx_count, piece_rows)(
        place, attn_even, attn_odd, *in_hbm([attn_master, attn_mom, attn_sq])
    )
    return (layer_out, input_grad) + tuple(attn_new) + tuple(ffn_new) + tuple(small_new)


def shift_wt(array, shift):
    count = lax.axis_size("wt")
    return lax.ppermute(array, "wt", [(i, (i + shift) % count) for i in range(count)])


def whole_wt(piece, axis):
    count, place = lax.axis_size("wt"), lax.axis_index("wt")
    shape = list(piece.shape)
    shape[axis] *= count
    buffer = put(jnp.zeros(shape, piece.dtype), piece, place, axis)
    for shift in range(1, count):
        buffer = put(buffer, shift_wt(piece, shift), (place - shift) % count, axis)
    return buffer


def whole_ctx(piece):
    count = lax.axis_size("ctx")
    got = {0: piece}
    for mask in range(2, count, 2):
        got[mask] = xor_send(piece, mask)
    for mask in range(0, count, 2):
        got[mask + 1] = xor_send(got[mask], 1)
    return [got[mask] for mask in range(count)]


def sum_ctx(pieces):
    count = lax.axis_size("ctx")
    half = {}
    for mask in range(count - 2, -1, -2):
        other = xor_send(pieces[mask + 1], 1)
        half[mask] = low(wide(pieces[mask]) + wide(other))
    total = wide(half[0])
    for mask in range(2, count, 2):
        total = total + wide(xor_send(half[mask], mask))
    return total


def sum_wt(array, axis):
    count, place = lax.axis_size("wt"), lax.axis_index("wt")
    size = array.shape[axis] // count
    total = wide(take(array, place, axis, size))
    for shift in range(1, count):
        sent = take(array, (place + shift) % count, axis, size)
        total = total + wide(shift_wt(sent, shift))
    return total


def any_shards(
    tokens,
    doc_starts,
    attn_master,
    attn_mom,
    attn_sq,
    ffn_master,
    ffn_mom,
    ffn_sq,
    small_master,
    small_mom,
    small_sq,
    cotangent,
):
    ctx_count = lax.axis_size("ctx")
    ctx_place = lax.axis_index("ctx")
    wt_count = lax.axis_size("wt")
    batches, rows_here, width = tokens.shape
    heads = width // HS
    qkv_cols = width + 2 * HS
    all_rows = batches * rows_here
    shard_rows = attn_master.shape[0]
    piece_rows = shard_rows // ctx_count
    chunk = FF // ctx_count
    order = ctx_place ^ jnp.arange(ctx_count, dtype=jnp.int32)
    (
        gain_one,
        shift_one,
        gain_two,
        shift_two,
        bias_query,
        bias_out,
        bias_proj,
        bias_value,
        bias_hidden,
    ) = split_small(small_master)

    attn_piece = low(take(attn_master, ctx_place, 0, piece_rows))

    def whole_rows(piece):
        parts = whole_ctx(whole_wt(piece[None], 0))
        buffer = jnp.zeros((wt_count, ctx_count) + piece.shape, piece.dtype)
        for k, part in enumerate(parts):
            buffer = put(buffer, part[:, None], ctx_place ^ k, 1)
        return buffer.reshape((width,) + piece.shape[1:])

    weight_qkv = whole_rows(attn_piece[:, :qkv_cols])
    weight_out = whole_rows(attn_piece[:, qkv_cols:])
    ffn_piece = low(jnp.swapaxes(take(ffn_master, ctx_place, 2, chunk), 0, 1))
    ffn_parts = whole_ctx(whole_wt(ffn_piece, 1))
    bias_parts = bias_hidden.reshape(ctx_count, chunk)[order]

    stream = wide(tokens.reshape(all_rows, width))
    normed, norm_back_one = jax.vjp(layer_norm, stream, gain_one, shift_one)
    normed_low = low(normed)
    mixed = dot(normed_low, weight_qkv)
    queries = low(mixed[:, :width] + bias_query)
    kv_local = low(
        mixed[:, width:] + jnp.concatenate([jnp.zeros((HS,), jnp.float32), bias_value])
    ).reshape(batches, rows_here, 2 * HS)
    kv_parts = jnp.stack(whole_ctx(kv_local), axis=1).reshape(
        batches, ctx_count * rows_here, 2 * HS
    )
    keys_all, values_all = kv_parts[..., :HS], kv_parts[..., HS:]
    local_pos = jnp.arange(rows_here, dtype=jnp.int32)
    query_pos = ctx_place * rows_here + local_pos
    key_pos = (order[:, None] * rows_here + local_pos[None, :]).reshape(-1)
    queries = queries.reshape(batches, rows_here * heads, HS)
    scale = HS ** (-0.5)
    attended_list, log_list, allowed_list = [], [], []
    for b in range(batches):
        starts = doc_starts[b]
        query_doc = jnp.sum((starts[None, :] <= query_pos[:, None]).astype(jnp.int32), axis=1)
        key_doc = jnp.sum((starts[None, :] <= key_pos[:, None]).astype(jnp.int32), axis=1)
        allowed = (query_doc[:, None] == key_doc[None, :]) & (key_pos[None, :] <= query_pos[:, None])
        allowed = jnp.repeat(allowed, heads, axis=0)
        allowed_list.append(allowed)
        scores = jnp.where(allowed, cols_dot(queries[b], keys_all[b]) * scale, -1e30)
        peak = jnp.max(scores, axis=-1, keepdims=True)
        expo = jnp.exp(scores - peak)
        total = jnp.sum(expo, axis=-1, keepdims=True)
        attended_list.append(dot(low(expo / total), values_all[b]))
        log_list.append(peak + jnp.log(total))
    attended = jnp.stack(attended_list)
    attended_low = low(attended).reshape(all_rows, width)
    hidden = stream + dot(attended_low, weight_out) + bias_out
    normed_two, norm_back_two = jax.vjp(layer_norm, hidden, gain_two, shift_two)
    normed_two_low = low(normed_two)

    back_low = cotangent.reshape(all_rows, width)
    back_rows = wide(back_low)
    down_vals = jnp.zeros((all_rows, width), jnp.float32)
    grad_normed_two = jnp.zeros((all_rows, width), jnp.float32)
    ffn_grads, hidden_grads = [], []
    for k in range(ctx_count):
        weight_up, weight_down = ffn_parts[k][0], ffn_parts[k][1]
        value, slope = gelu_both(dot(normed_two_low, weight_up) + bias_parts[k])
        act = low(value)
        down_vals = down_vals + cols_dot(act, weight_down)
        grad_up = low(dot(back_low, weight_down) * slope)
        hidden_grads.append(jnp.sum(wide(grad_up), axis=0))
        grad_normed_two = grad_normed_two + cols_dot(grad_up, weight_up)
        ffn_grads.append(
            jnp.stack([low(rows_dot(normed_two_low, grad_up)), low(rows_dot(back_low, act))])
        )
    layer_out = low(hidden + down_vals + bias_proj).reshape(batches, rows_here, width)
    grad_bias_proj = jnp.sum(back_rows, axis=0)
    grad_bias_hidden = jnp.stack(hidden_grads)[order].reshape(FF)
    ffn_part = low(sum_wt(low(sum_ctx(ffn_grads)), 1))

    grad_hidden_part, grad_gain_two, grad_shift_two = norm_back_two(grad_normed_two)
    grad_hidden = back_rows + grad_hidden_part
    grad_bias_out = jnp.sum(grad_hidden, axis=0)
    grad_hidden_low = low(grad_hidden)
    grad_out = rows_dot(attended_low, grad_hidden_low)

    def summed_rows(grad):
        blocks = low(grad).reshape(wt_count, ctx_count, piece_rows, grad.shape[1])
        pieces = [take(blocks, ctx_place ^ k, 1, 1)[:, 0] for k in range(ctx_count)]
        part = low(sum_wt(low(sum_ctx(pieces)), 0)[0])
        buffer = jnp.zeros((ctx_count,) + part.shape, part.dtype)
        for k, got in enumerate(whole_ctx(part)):
            buffer = put(buffer, got[None], ctx_place ^ k, 0)
        return wide(buffer.reshape(shard_rows, grad.shape[1]))

    out_total = summed_rows(grad_out)

    grad_attended = low(cols_dot(grad_hidden_low, weight_out)).reshape(
        batches, rows_here * heads, HS
    )
    grad_query_list, grad_kv_list = [], []
    for b in range(batches):
        grads = grad_attended[b]
        delta = jnp.sum(wide(grads) * attended[b], axis=-1, keepdims=True)
        scores = jnp.where(allowed_list[b], cols_dot(queries[b], keys_all[b]) * scale, -1e30)
        weights = jnp.exp(scores - log_list[b])
        grad_scores = low(weights * (cols_dot(grads, values_all[b]) - delta))
        grad_query_list.append(low(dot(grad_scores, keys_all[b]) * scale))
        grad_kv_list.append(
            jnp.concatenate(
                [
                    low(rows_dot(grad_scores, queries[b]) * scale),
                    low(rows_dot(low(weights), grads)),
                ],
                axis=1,
            )
        )
    grad_query = jnp.stack(grad_query_list).reshape(all_rows, width)
    grad_kv = jnp.stack(grad_kv_list).reshape(batches, ctx_count, rows_here, 2 * HS)
    grad_kv_low = low(sum_ctx([grad_kv[:, k] for k in range(ctx_count)])).reshape(
        all_rows, 2 * HS
    )
    grad_bias_query = jnp.sum(wide(grad_query), axis=0)
    grad_bias_value = jnp.sum(wide(grad_kv_low[:, HS:]), axis=0)
    grad_mixed = jnp.concatenate([grad_query, grad_kv_low], axis=1)
    qkv_total = summed_rows(rows_dot(normed_low, grad_mixed))
    grad_normed = cols_dot(grad_mixed, weight_qkv)
    grad_stream_part, grad_gain_one, grad_shift_one = norm_back_one(grad_normed)
    input_grad = (grad_hidden + grad_stream_part).reshape(batches, rows_here, width)

    ffn_buffer = jnp.zeros((ctx_count,) + ffn_part.shape, ffn_part.dtype)
    for k, got in enumerate(whole_ctx(ffn_part)):
        ffn_buffer = put(ffn_buffer, got[None], ctx_place ^ k, 0)
    ffn_total = wide(jnp.transpose(ffn_buffer, (2, 1, 0, 3)).reshape(shard_rows, 2, FF))
    attn_total = jnp.concatenate([qkv_total, out_total], axis=1)
    grad_small = jnp.concatenate(
        [
            grad_gain_one,
            grad_shift_one,
            grad_gain_two,
            grad_shift_two,
            grad_bias_query,
            grad_bias_out,
            grad_bias_proj,
            grad_bias_value,
            grad_bias_hidden,
        ]
    )
    small_total = lax.psum(grad_small, ("ctx", "wt"))
    attn_new = adam_update(attn_master, attn_total, attn_mom, attn_sq, 0.1, 0.1)
    ffn_new = adam_update(ffn_master, ffn_total, ffn_mom, ffn_sq, 0.1, 0.1)
    small_new = adam_update(small_master, small_total, small_mom, small_sq, 1.0, 0.0)
    return (layer_out, input_grad) + attn_new + ffn_new + small_new


def solution(mesh):
    rows, cube = P("wt", None), P("wt", None, None)
    flow = P("wt", "ctx", None)
    in_specs = (flow, rows, rows, rows, rows, cube, cube, cube, P(), P(), P(), flow)
    out_specs = (flow, flow, rows, rows, rows, cube, cube, cube, P(), P(), P())
    ctx_count, wt_count = mesh.shape["ctx"], mesh.shape["wt"]
    fitted = (ctx_count, wt_count) == (8, 4)
    body = shards if fitted else any_shards
    return jax.shard_map(body, mesh=mesh, in_specs=in_specs, out_specs=out_specs, check_vma=False)
```

```python
import jax
import jax.numpy as jnp
from jax import lax
from jax.experimental import pallas as pl
from jax.experimental.pallas import tpu as pltpu
from jax.sharding import PartitionSpec as P

D = 768
HS = 64
FF = 3072
STEP = 10


NORM_EPS = 1e-05
GELU_COEF = 0.7978845608028654
GELU_CUBE = 0.044715
BETA_ONE = 0.9
BETA_TWO = 0.95
ADAM_EPS = 1e-08
VMEM_LIMIT = 22 << 20
NO_COST = pl.CostEstimate(flops=0, bytes_accessed=0, transcendentals=0)


def layer_norm(values, gain, shift):
    centre = values - jnp.mean(values, axis=-1, keepdims=True)
    spread = jnp.mean(centre * centre, axis=-1, keepdims=True)
    return centre * lax.rsqrt(spread + NORM_EPS) * gain + shift


def gelu_both(u):
    square = u * u
    share = 0.5 * jnp.tanh(u * (GELU_COEF * GELU_CUBE * square + GELU_COEF)) + 0.5
    bend = u * (6.0 * GELU_COEF * GELU_CUBE * square + 2.0 * GELU_COEF)
    return u * share, share * ((1.0 - share) * bend) + share


def split_small(small):
    return (
        small[0:D],
        small[D : 2 * D],
        small[2 * D : 3 * D],
        small[3 * D : 4 * D],
        small[4 * D : 5 * D],
        small[5 * D : 6 * D],
        small[6 * D : 7 * D],
        small[7 * D : 7 * D + HS],
        small[7 * D + HS :],
    )


def rows_dot(left, right):
    return lax.dot_general(
        left, right, (((0,), (0,)), ((), ())), preferred_element_type=jnp.float32
    )


def cols_dot(left, right):
    return lax.dot_general(
        left, right, (((1,), (1,)), ((), ())), preferred_element_type=jnp.float32
    )


def dot(left, right):
    return jnp.dot(left, right, preferred_element_type=jnp.float32)


def low(values):
    return values.astype(jnp.bfloat16)


def wide(values):
    return values.astype(jnp.float32)


def adam_update(master, gradient, first, second, step_rate, decay_rate):
    first_new = BETA_ONE * first + (1.0 - BETA_ONE) * gradient
    second_new = BETA_TWO * second + (1.0 - BETA_TWO) * gradient * gradient
    first_hat = first_new / (1.0 - BETA_ONE**STEP)
    second_hat = second_new / (1.0 - BETA_TWO**STEP)
    master_new = master - step_rate * (
        first_hat / (jnp.sqrt(second_hat) + ADAM_EPS) + decay_rate * master
    )
    return (first_new, second_new, master_new)


def xor_send(array, mask):
    count = lax.axis_size("ctx")
    return lax.ppermute(array, "ctx", [(i, i ^ mask) for i in range(count)])


def xor_wt(array, mask):
    count = lax.axis_size("wt")
    return lax.ppermute(array, "wt", [(i, i ^ mask) for i in range(count)])


class Steps:
    def __init__(self):
        self.last = ()

    def __call__(self, function, *args):
        flat, tree = jax.tree.flatten(args)
        held = lax.optimization_barrier(tuple(flat) + self.last)[: len(flat)]
        result = function(*jax.tree.unflatten(tree, held))
        self.last = tuple(jax.tree.leaves(result))
        return result


def loop(count, body, carry=0):
    return lax.fori_loop(0, count, body, carry)


def rows_at(i, size):
    return pl.ds(pl.multiple_of(i * size, size), size)


def together(*arrays):
    return lax.optimization_barrier(arrays)


def put(buffer, piece, place, axis):
    starts = [0] * buffer.ndim
    starts[axis] = place * piece.shape[axis]
    return lax.dynamic_update_slice(buffer, piece, starts)


def take(buffer, place, axis, size):
    return lax.dynamic_slice_in_dim(buffer, place * size, size, axis)


def attention_kernels(batches, rows, width, parts, runs):
    half_parts = parts // 2
    keys = parts * rows
    pair = 2 * HS
    groups = width // (2 * pair)
    factor = HS ** (-0.5) * 1.4426950408889634
    tile = 32

    def lanes(shape):
        return lax.broadcasted_iota(jnp.int32, shape, 1)

    def spread(even_ref, odd_ref, key_ref, value_ref):
        for j in range(parts):
            ref = even_ref if j < half_parts else odd_ref
            block = wide(ref[j % half_parts, 0])
            turned = pltpu.roll(block, HS, 1)
            first = lanes(block.shape) < HS
            here = pl.ds(j * rows, rows)
            key_ref[0, here, :] = low(jnp.where(first, block, 0.0))
            key_ref[1, here, :] = low(jnp.where(first, 0.0, turned))
            value_ref[0, here, :] = low(jnp.where(first, turned, 0.0))
            value_ref[1, here, :] = low(jnp.where(first, 0.0, block))

    def doc_begin(starts_ref, stream, positions):
        begin = jnp.zeros_like(positions)
        for j in range(starts_ref.shape[1]):
            start = starts_ref[stream, j]
            begin = jnp.where(start <= positions, jnp.maximum(begin, start), begin)
        return begin

    def forward(starts_ref, place_ref, query_ref, even_ref, odd_ref, low_ref, full_ref, log_ref, cap, key, value, weight):
        stream, place = pl.program_id(0), place_ref[0]
        spread(even_ref, odd_ref, key, value)
        query_pos = place * rows + lax.broadcasted_iota(jnp.int32, (rows, 1), 0)
        begin = doc_begin(starts_ref, stream, query_pos)
        for j in range(parts):
            key_pos = (place ^ (2 * (j % half_parts) + j // half_parts)) * rows + lax.broadcasted_iota(jnp.int32, (rows, rows), 1)
            allowed = (key_pos >= begin) & (key_pos <= query_pos)
            cap[:, j * rows : (j + 1) * rows] = jnp.where(allowed, 3.0e38, -1e30)
        column = lanes((tile, pair))
        logs = [jnp.zeros((tile, pair), jnp.float32) for _ in range(rows // tile)]
        for g in range(groups):
            at = g * 2 * pair
            two = jnp.concatenate([query_ref[0, :, at : at + pair], query_ref[0, :, at + pair : at + 2 * pair]], axis=0)
            totals = []
            for half in range(2):
                scores = cols_dot(two, key[half])
                norms = []
                for t in range(2 * rows // tile):
                    own = slice(t * tile, (t + 1) * tile)
                    n = t % (rows // tile)
                    part = jnp.minimum(scores[own] * factor, cap[n * tile : (n + 1) * tile, :])
                    peak = jnp.max(part, axis=1, keepdims=True)
                    expo = jnp.exp2(part - peak)
                    norm = jnp.sum(expo, axis=1, keepdims=True)
                    weight[half, own, :] = low(expo)
                    norms.append(norm)
                    head = 4 * g + 2 * (t * tile // rows) + half
                    logs[n] = jnp.where(column == head, peak + jnp.log2(norm), logs[n])
                totals.append(dot(weight[half], value[half]) / jnp.concatenate(norms, axis=0))
            total = totals[0] + totals[1]
            for j in range(2):
                part = total[j * rows : (j + 1) * rows]
                full_ref[0, :, at + j * pair : at + (j + 1) * pair] = part
                low_ref[0, :, at + j * pair : at + (j + 1) * pair] = low(part)
        for n, log in enumerate(logs):
            log_ref[0, n * tile : (n + 1) * tile, :] = log

    def backward(
        starts_ref, place_ref, query_ref, even_ref, odd_ref, full_ref, log_ref, grad_ref,
        query_grad_ref, even_grad_ref, odd_grad_ref,
        cap, key, value, key_turned, log_rows, delta_rows, weight_buf, score_buf, query_buf, grad_buf,
    ):
        stream, place = pl.program_id(0) + place_ref[1], place_ref[0]
        spread(even_ref, odd_ref, key, value)
        query_pos = place * rows + lax.broadcasted_iota(jnp.int32, (1, rows), 1)
        begin = doc_begin(starts_ref, stream, query_pos)
        for j in range(parts):
            key_pos = (place ^ (2 * (j % half_parts) + j // half_parts)) * rows + lax.broadcasted_iota(jnp.int32, (rows, rows), 0)
            allowed = (key_pos >= begin) & (key_pos <= query_pos)
            cap[j * rows : (j + 1) * rows, :] = jnp.where(allowed, 3.0e38, -1e30)
            here = pl.ds(j * rows, rows)
            key_turned[:, j * rows : (j + 1) * rows] = low(wide(key[0, here, :]).T[:HS])
        log_rows[...] = log_ref[0].T[: log_rows.shape[0]]
        head_of = lax.broadcasted_iota(jnp.int32, (delta_rows.shape[0], width), 1) // HS
        chosen = (head_of == lax.broadcasted_iota(jnp.int32, (delta_rows.shape[0], width), 0)).astype(jnp.float32)
        delta_rows[...] = lax.dot_general(
            chosen, wide(grad_ref[0]) * full_ref[0], (((1,), (1,)), ((), ())),
            precision=lax.Precision.HIGHEST, preferred_element_type=jnp.float32,
        )
        first = lanes((2 * rows, pair)) < HS
        for g in range(groups):
            at = g * 2 * pair
            both, both_grad = query_ref[0, :, at : at + 2 * pair], grad_ref[0, :, at : at + 2 * pair]
            two = jnp.concatenate([both[:, :pair], both[:, pair:]], axis=0)
            two_grad = jnp.concatenate([both_grad[:, :pair], both_grad[:, pair:]], axis=0)
            turned = []
            for half in range(2):
                h = 4 * g + half
                span = slice((2 * g + half) * 2 * rows, (2 * g + half + 1) * 2 * rows)
                keep = first if half == 0 else jnp.logical_not(first)
                query_buf[span, :] = low(jnp.where(keep, wide(two), 0.0))
                grad_buf[span, :] = low(jnp.where(keep, wide(two_grad), 0.0))
                log = jnp.concatenate([log_rows[h : h + 1, :], log_rows[h + 2 : h + 3, :]], axis=1)
                delta = jnp.concatenate([delta_rows[h : h + 1, :], delta_rows[h + 2 : h + 3, :]], axis=1)
                scores, weight_grads = cols_dot(key[half], two), cols_dot(value[half], two_grad)
                for t in range(keys // (2 * tile)):
                    own = slice(t * 2 * tile, (t + 1) * 2 * tile)
                    limit = cap[own, :]
                    limit = jnp.concatenate([limit, limit], axis=1)
                    weights = jnp.exp2(jnp.minimum(scores[own] * factor, limit) - log)
                    weight_buf[own, span] = low(weights)
                    score_buf[own, span] = low(weights * (weight_grads[own] - delta))
                turned.append(dot(key_turned[...], score_buf[:, span]))
            turned = jnp.concatenate(turned, axis=0) * HS ** (-0.5)
            query_grad_ref[0, :, at : at + pair] = low(turned[:, :rows].T)
            query_grad_ref[0, :, at + pair : at + 2 * pair] = low(turned[:, rows:].T)
        for odd, ref in enumerate((even_grad_ref, odd_grad_ref)):
            here = pl.ds(odd * half_parts * rows, half_parts * rows)
            value_sum = dot(weight_buf[here, :], grad_buf[...])
            key_sum = dot(score_buf[here, :], query_buf[...]) * HS ** (-0.5)
            value_sum = value_sum + pltpu.roll(value_sum, HS, 1)
            key_sum = key_sum + pltpu.roll(key_sum, HS, 1)
            both_sums = low(jnp.where(lanes(key_sum.shape) < HS, key_sum, value_sum))
            for j in range(half_parts):
                ref[j, 0] = both_sums[j * rows : (j + 1) * rows]

    def specs(first):
        return (
            pl.BlockSpec((1, rows, width), lambda b, *_: (b + first, 0, 0)),
            pl.BlockSpec((1, rows, pair), lambda b, *_: (b + first, 0, 0)),
            pl.BlockSpec((half_parts, 1, rows, pair), lambda b, *_: (0, b + first, 0, 0)),
        )

    flow, logs, blocks = specs(0)

    shared = [
        pltpu.VMEM((2, keys, pair), jnp.bfloat16),
        pltpu.VMEM((2, keys, pair), jnp.bfloat16),
    ]
    run_forward = pl.pallas_call(
        forward,
        grid_spec=pltpu.PrefetchScalarGridSpec(
            num_scalar_prefetch=2,
            grid=(batches,),
            in_specs=[flow, blocks, blocks],
            out_specs=[flow, flow, logs],
            scratch_shapes=[pltpu.VMEM((rows, keys), jnp.float32)]
            + shared
            + [pltpu.VMEM((2, 2 * rows, keys), jnp.bfloat16)],
        ),
        out_shape=[
            jax.ShapeDtypeStruct((batches, rows, width), jnp.bfloat16),
            jax.ShapeDtypeStruct((batches, rows, width), jnp.float32),
            jax.ShapeDtypeStruct((batches, rows, pair), jnp.float32),
        ],
        compiler_params=pltpu.CompilerParams(vmem_limit_bytes=VMEM_LIMIT),
        cost_estimate=NO_COST,
        name="attention_forward",
    )
    head_rows = -(-(width // HS) // 8) * 8
    all_columns = rows * (width // HS)
    count = batches // runs

    def call_backward(run):
        here_flow, here_logs, here_blocks = specs(run * count)
        return pl.pallas_call(
        backward,
        grid_spec=pltpu.PrefetchScalarGridSpec(
            num_scalar_prefetch=2,
            grid=(count,),
            in_specs=[here_flow, here_blocks, here_blocks, here_flow, here_logs, here_flow],
            out_specs=[flow, blocks, blocks],
            scratch_shapes=[pltpu.VMEM((keys, rows), jnp.float32)]
            + shared
            + [
                pltpu.VMEM((HS, keys), jnp.bfloat16),
                pltpu.VMEM((head_rows, rows), jnp.float32),
                pltpu.VMEM((head_rows, rows), jnp.float32),
                pltpu.VMEM((keys, all_columns), jnp.bfloat16),
                pltpu.VMEM((keys, all_columns), jnp.bfloat16),
                pltpu.VMEM((all_columns, pair), jnp.bfloat16),
                pltpu.VMEM((all_columns, pair), jnp.bfloat16),
            ],
        ),
        out_shape=[
            jax.ShapeDtypeStruct((count, rows, width), jnp.bfloat16),
            jax.ShapeDtypeStruct((half_parts, count, rows, pair), jnp.bfloat16),
            jax.ShapeDtypeStruct((half_parts, count, rows, pair), jnp.bfloat16),
        ],
        compiler_params=pltpu.CompilerParams(vmem_limit_bytes=VMEM_LIMIT),
        cost_estimate=NO_COST,
        name="attention_backward",
    )

    return run_forward, [call_backward(run) for run in range(runs)]


def in_hbm(arrays):
    return [pltpu.with_memory_space_constraint(array, pltpu.HBM) for array in arrays]


def ffn_kernels(rows, width, chunk, wt_count):
    units = 2 * chunk
    all_rows = 2 * rows
    block_rows = width // wt_count
    hbm = pl.BlockSpec(memory_space=pltpu.HBM)
    vmem = pl.BlockSpec(memory_space=pltpu.VMEM)
    params = pltpu.CompilerParams(vmem_limit_bytes=VMEM_LIMIT)

    def fetch(weights, which, held, sem):
        copies = []
        for n, arrays in enumerate(weights):
            blocks = [array.at[block] for array in arrays for block in range(array.shape[0])]
            for row, block in enumerate(blocks):
                copies.append(
                    pltpu.make_async_copy(
                        block.at[pl.ds(which * block_rows, block_rows), :],
                        held.at[pl.ds(row * block_rows, block_rows), pl.ds(n * chunk, chunk)],
                        sem.at[len(copies)],
                    )
                )
        for copy in copies:
            copy.start()
        return copies

    def send(pairs, sems):
        copies = [pltpu.make_async_copy(source, out, sems.at[n]) for n, (source, out) in enumerate(pairs)]
        for copy in copies:
            copy.start()
        return copies

    part_rows = 256
    tile = 16

    def units_of(inputs, grads, bias, held_up, held_down, act, grad_units):
        sums = jnp.zeros((8, units), jnp.float32)
        for s in range(2):

            def part(i, sums):
                here = rows_at(i, part_rows)
                up = dot(inputs[s][here, :], held_up[...])
                act_grad = dot(grads[s][here, :], held_down[...])
                for t in range(part_rows // tile):
                    own = slice(t * tile, (t + 1) * tile)
                    there = pl.ds(pl.multiple_of(s * rows + i * part_rows + t * tile, tile), tile)
                    value, slope = gelu_both(up[own] + bias)
                    grad = act_grad[own] * slope
                    act[there, :] = low(value)
                    grad_units[there, :] = low(grad)
                    sums = sums + (grad[:8] + grad[8:])
                return sums

            sums = loop(rows // part_rows, part, sums)
        return jnp.sum(sums, axis=0, keepdims=True)

    def product_of(turned, right, product):
        def part(i, carry):
            here = rows_at(i, part_rows)
            product[here, :] = low(dot(turned[here, :], right[...]))
            return carry

        loop(width // part_rows, part)

    def back_to(refs, sources, weights):
        for s, ref in enumerate(refs):

            def part(i, carry):
                here = pl.ds(pl.multiple_of(s * rows + i * part_rows, part_rows), part_rows)
                total = cols_dot(sources[0][here, :], weights[0][...]) + cols_dot(sources[1][here, :], weights[1][...])
                ref[rows_at(i, part_rows), :] = total.astype(ref.dtype)
                return carry

            loop(rows // part_rows, part)

    def halves(product, m):
        cols = pl.ds(m * chunk, chunk)
        return [product.at[pl.ds(h * width // 2, width // 2), cols] for h in range(2)]

    def first(
        own, other, grad_own, grad_other, turned, bias, w0, w1, w2, w3,
        act_out, units_out, out_a, out_b, sums_out,
        held_up, held_down, act, grad_units, product, sems, out_sems,
    ):
        weights = ((w0, w1), (w2, w3))
        copies = fetch(weights, 0, held_up, sems.at[0]) + fetch(weights, 1, held_down, sems.at[1])
        for copy in copies:
            copy.wait()
        sums_out[...] = units_of((own, other), (grad_own, grad_other), bias[...], held_up, held_down, act, grad_units)
        sent = send(((act, act_out), (grad_units, units_out)), out_sems.at[0])
        product_of(turned, act, product)
        sent += send(
            ((product.at[:, pl.ds(0, chunk)], out_a), (product.at[:, pl.ds(chunk, chunk)], out_b)), out_sems.at[1]
        )
        for copy in sent:
            copy.wait()

    def second(
        own, other, grad_own, grad_other, turned, bias, units_first, w0, w1, w2, w3, w4, w5, w6, w7,
        act_out, units_out, out_a, out_b, out_c, sums_out, back_own, back_other,
        held_up, held_more, held_down, act, grad_units, more_units, product, sems, out_sems, more_sem,
    ):
        weights, before = ((w4, w5), (w6, w7)), ((w0, w1), (w2, w3))
        copies = fetch(weights, 0, held_up, sems.at[0]) + fetch(weights, 1, held_down, sems.at[1])
        more = fetch(before, 0, held_more, sems.at[2])
        more.append(pltpu.make_async_copy(units_first, more_units, more_sem))
        more[-1].start()
        for copy in copies:
            copy.wait()
        sums_out[...] = units_of((own, other), (grad_own, grad_other), bias[...], held_up, held_down, act, grad_units)
        sent = send(((act, act_out), (grad_units, units_out)), out_sems.at[0])
        product_of(turned, act, product)
        top, bottom = halves(product, 1)
        sent += send(((product.at[:, pl.ds(0, chunk)], out_a), (top, out_b), (bottom, out_c)), out_sems.at[1])
        for copy in more:
            copy.wait()
        back_to((back_own, back_other), (grad_units, more_units), (held_up, held_more))
        for copy in sent:
            copy.wait()

    def third(own, other, units_a, units_b, out_0, out_1, out_2, out_3, out_4, turned, held, products, sems, out_sems):
        copies = send(((units_a, held.at[0]), (units_b, held.at[1])), sems)
        turn((own, other), turned)
        for copy in copies:
            copy.wait()
        products[1] = low(dot(turned[...], held[1]))
        top, bottom = halves(products.at[1], 1)
        sent = send(((products.at[1, :, pl.ds(0, chunk)], out_2), (top, out_3), (bottom, out_4)), out_sems.at[0])
        products[0] = low(dot(turned[...], held[0]))
        sent += send(
            ((products.at[0, :, pl.ds(0, chunk)], out_0), (products.at[0, :, pl.ds(chunk, chunk)], out_1)),
            out_sems.at[1],
        )
        for copy in sent:
            copy.wait()

    def down(act_a, act_b, w0, w1, w2, w3, w4, w5, w6, w7, own_ref, other_ref, held_a, held_b, sems):
        copies = fetch(((w0, w1), (w2, w3)), 1, held_a, sems.at[0]) + fetch(((w4, w5), (w6, w7)), 1, held_b, sems.at[1])
        for copy in copies:
            copy.wait()
        for s, ref in enumerate((own_ref, other_ref)):
            here = slice(s * rows, (s + 1) * rows)
            total = cols_dot(act_a[here, :], held_a[...]) + cols_dot(act_b[here, :], held_b[...])
            ref[...] = total.astype(ref.dtype)

    dma = pltpu.SemaphoreType.DMA
    held = pltpu.VMEM((width, units), jnp.bfloat16)
    flow = pltpu.VMEM((all_rows, units), jnp.bfloat16)
    flow_out = pltpu.HBM((all_rows, units), jnp.bfloat16)
    whole = pltpu.HBM((width, chunk), jnp.bfloat16)
    part = pltpu.HBM((width // 2, chunk), jnp.bfloat16)
    sums = jax.ShapeDtypeStruct((1, units), jnp.float32)
    own = jax.ShapeDtypeStruct((rows, width), jnp.float32)
    other = jax.ShapeDtypeStruct((rows, width), jnp.bfloat16)
    run_first = pl.pallas_call(
        first,
        in_specs=[vmem] * 6 + [hbm] * 4,
        out_specs=[hbm] * 4 + [vmem],
        out_shape=[flow_out, flow_out, whole, whole, sums],
        scratch_shapes=[held, held, flow, flow, held, dma((2, 2 * wt_count)), dma((2, 2))],
        compiler_params=params,
        cost_estimate=NO_COST,
        name="ffn_first",
    )
    run_second = pl.pallas_call(
        second,
        in_specs=[vmem] * 6 + [hbm] * 9,
        out_specs=[hbm] * 5 + [vmem] * 3,
        out_shape=[flow_out, flow_out, whole, part, part, sums, own, other],
        scratch_shapes=[held, held, held, flow, flow, flow, held, dma((3, 2 * wt_count)), dma((2, 3)), dma(())],
        compiler_params=params,
        cost_estimate=NO_COST,
        name="ffn_second",
    )
    run_third = pl.pallas_call(
        third,
        in_specs=[vmem] * 2 + [hbm] * 2,
        out_specs=[hbm] * 5,
        out_shape=[whole, whole, whole, part, part],
        scratch_shapes=[
            pltpu.VMEM((width, all_rows), jnp.bfloat16),
            pltpu.VMEM((2, all_rows, units), jnp.bfloat16),
            pltpu.VMEM((2, width, units), jnp.bfloat16),
            dma((2,)),
            dma((2, 3)),
        ],
        compiler_params=params,
        cost_estimate=NO_COST,
        name="ffn_grads",
    )
    run_down = pl.pallas_call(
        down,
        in_specs=[vmem] * 2 + [hbm] * 8,
        out_specs=[vmem] * 2,
        out_shape=[own, other],
        scratch_shapes=[held, held, dma((2, 2 * wt_count))],
        compiler_params=params,
        cost_estimate=NO_COST,
        name="ffn_down",
    )
    return run_first, run_second, run_third, run_down


def turn(refs, turned):
    rows = refs[0].shape[0]
    for s, ref in enumerate(refs):
        for i in range(rows // 128):
            block = wide(ref[i * 128 : (i + 1) * 128, :])
            turned[:, s * rows + i * 128 : s * rows + (i + 1) * 128] = low(block.T)


def turn_both(own, other):
    vmem = pl.BlockSpec(memory_space=pltpu.VMEM)
    rows, width = own.shape
    return pl.pallas_call(
        lambda a, b, out: turn((a, b), out),
        in_specs=[vmem] * 2,
        out_specs=vmem,
        out_shape=jax.ShapeDtypeStruct((width, 2 * rows), own.dtype),
        compiler_params=pltpu.CompilerParams(vmem_limit_bytes=VMEM_LIMIT),
        cost_estimate=NO_COST,
        name="turn",
    )(own, other)


def out_projection(rows, width):
    tile = 32

    def kernel(attended, weight, stream, bias, gain, shift, hidden_ref, normed_ref):
        product = dot(attended[...], weight[...])
        for t in range(rows // tile):
            here = slice(t * tile, (t + 1) * tile)
            hidden = wide(stream[here, :]) + product[here] + bias[...]
            hidden_ref[here, :] = hidden
            normed_ref[here, :] = low(layer_norm(hidden, gain[...], shift[...]))

    vmem = pl.BlockSpec(memory_space=pltpu.VMEM)
    return pl.pallas_call(
        kernel,
        in_specs=[vmem] * 6,
        out_specs=[vmem] * 2,
        out_shape=[
            jax.ShapeDtypeStruct((rows, width), jnp.float32),
            jax.ShapeDtypeStruct((rows, width), jnp.bfloat16),
        ],
        compiler_params=pltpu.CompilerParams(vmem_limit_bytes=VMEM_LIMIT),
        cost_estimate=NO_COST,
        name="out_projection",
    )


def norm_back(values, gain, grad):
    centre = values - jnp.mean(values, axis=-1, keepdims=True)
    scale = lax.rsqrt(jnp.mean(centre * centre, axis=-1, keepdims=True) + NORM_EPS)
    unit = centre * scale
    inner = grad * gain
    mean = jnp.mean(inner, axis=-1, keepdims=True)
    along = jnp.mean(inner * unit, axis=-1, keepdims=True)
    return scale * (inner - mean - unit * along), grad * unit


def fold_rows(values):
    total = values[:8]
    for i in range(1, values.shape[0] // 8):
        total = total + values[i * 8 : (i + 1) * 8]
    return total


def hidden_back(rows, width):
    tile = 32

    def kernel(own, got, hidden, back, gain, weight, grad_ref, low_ref, attended_ref, sums_ref):
        sums = [jnp.zeros((8, width), jnp.float32) for _ in range(3)]
        for t in range(rows // tile):
            here = slice(t * tile, (t + 1) * tile)
            pulled, terms = norm_back(hidden[here, :], gain[...], own[here, :] + wide(got[here, :]))
            grad = wide(back[here, :]) + pulled
            grad_ref[here, :] = grad
            low_ref[here, :] = low(grad)
            for n, part in enumerate((terms, own[here, :] + wide(got[here, :]), grad)):
                sums[n] = sums[n] + fold_rows(part)
        for n in range(3):
            sums_ref[n : n + 1, :] = jnp.sum(sums[n], axis=0, keepdims=True)
        attended_ref[...] = low(cols_dot(low_ref[...], weight[...]))

    vmem = pl.BlockSpec(memory_space=pltpu.VMEM)
    return pl.pallas_call(
        kernel,
        in_specs=[vmem] * 6,
        out_specs=[vmem] * 4,
        out_shape=[
            jax.ShapeDtypeStruct((rows, width), jnp.float32),
            jax.ShapeDtypeStruct((rows, width), jnp.bfloat16),
            jax.ShapeDtypeStruct((rows, width), jnp.bfloat16),
            jax.ShapeDtypeStruct((3, width), jnp.float32),
        ],
        compiler_params=pltpu.CompilerParams(vmem_limit_bytes=VMEM_LIMIT),
        cost_estimate=NO_COST,
        name="hidden_back",
    )


def stream_back(rows, width, parts, row_groups, piece):
    tile = 32
    chips = parts // 2

    def kernel(
        place_ref, kv_0, kv_1, kv_2, kv_3, queries, weight, tokens, gain, grad_hidden, normed, back, hidden_sums,
        units_a, units_b, input_ref, even_ref, odd_ref, grad_kv, grads, turned, product, small,
    ):
        place = place_ref[0]
        sums = [jnp.zeros((8, width), jnp.float32) for _ in range(4)]
        value_sums = jnp.zeros((8, 2 * HS), jnp.float32)
        for t in range(rows // tile):
            here = slice(t * tile, (t + 1) * tile)
            total = wide(kv_0[here, :]) + wide(kv_1[here, :]) + wide(kv_2[here, :]) + wide(kv_3[here, :])
            grad_kv[here, :] = low(total)
            value_sums = value_sums + fold_rows(total)
        turn((normed,), turned)
        product[...] = dot(turned[...], grad_kv[...])
        grads[...] = cols_dot(queries[...], weight[:, :width]) + cols_dot(grad_kv[...], weight[:, width:])
        for t in range(rows // tile):
            here = slice(t * tile, (t + 1) * tile)
            grad = grads[here, :]
            pulled, terms = norm_back(wide(tokens[here, :]), gain[...], grad)
            input_ref[here, :] = grad_hidden[here, :] + pulled
            for n, part in enumerate((terms, grad, wide(queries[here, :]), wide(back[here, :]))):
                sums[n] = sums[n] + fold_rows(part)
        sums = [jnp.sum(part, axis=0, keepdims=True) for part in sums]
        small[...] = jnp.zeros_like(small)
        rows_in = (sums[0], sums[1], hidden_sums[0:1, :], hidden_sums[1:2, :], sums[2], hidden_sums[2:3, :], sums[3])
        for n, row in enumerate(rows_in):
            for j in range(width // 128):
                line = n * (width // 128) + j
                small[line : line + 1, :] = row[:, j * 128 : (j + 1) * 128]
        start = 7 * (width // 128)
        small[start : start + 1, :] = jnp.sum(value_sums, axis=0, keepdims=True)
        lines = FF // parts // 128
        for m in range(chips):
            units = (units_a, units_b)[m // 2]
            for j in range(lines):
                line = start + 1 + (place ^ (2 * m)) * lines + j
                at = (m % 2 * lines + j) * 128
                small[pl.ds(line, 1), :] = units[:, at : at + 128]
        for k in range(parts):
            ref = odd_ref if k % 2 else even_ref
            mine = low(small[pl.ds(pl.multiple_of((place ^ k) * piece, 8), piece), :])
            for w in range(row_groups):
                at = pl.multiple_of(w * piece * parts + (place ^ k) * piece, 8)
                ref[k // 2, w, :, :128] = low(product[pl.ds(at, piece), :])
                ref[k // 2, w, :, 128:] = mine

    vmem = pl.BlockSpec(memory_space=pltpu.VMEM)
    stack = jax.ShapeDtypeStruct((chips, row_groups, piece, 256), jnp.bfloat16)
    return pl.pallas_call(
        kernel,
        in_specs=[pl.BlockSpec(memory_space=pltpu.SMEM)] + [vmem] * 14,
        out_specs=[vmem] * 3,
        out_shape=[jax.ShapeDtypeStruct((rows, width), jnp.float32), stack, stack],
        scratch_shapes=[
            pltpu.VMEM((rows, 2 * HS), jnp.bfloat16),
            pltpu.VMEM((rows, width), jnp.float32),
            pltpu.VMEM((width, rows), jnp.bfloat16),
            pltpu.VMEM((width, 2 * HS), jnp.float32),
            pltpu.VMEM((parts * piece, 128), jnp.float32),
        ],
        compiler_params=pltpu.CompilerParams(vmem_limit_bytes=VMEM_LIMIT),
        cost_estimate=NO_COST,
        name="stream_back",
    )


def attn_grads(rows, width, row_groups, parts, piece):
    def kernel(place_ref, left_a, right_a, left_b, right_b, even_ref, odd_ref, turned, total):
        place = place_ref[0]
        for n, (left, right) in enumerate(((left_a, right_a), (left_b, right_b))):
            for i in range(rows // 128):
                turned[:, i * 128 : (i + 1) * 128] = low(wide(left[i * 128 : (i + 1) * 128, :]).T)
            total[:, n * width : (n + 1) * width] = dot(turned[...], right[...])
        for k in range(parts):
            ref = odd_ref if k % 2 else even_ref
            for w in range(row_groups):
                at = pl.multiple_of(w * piece * parts + (place ^ k) * piece, 8)
                ref[k // 2, w] = low(total[pl.ds(at, piece), :])

    vmem = pl.BlockSpec(memory_space=pltpu.VMEM)
    shape = jax.ShapeDtypeStruct((parts // 2, row_groups, piece, 2 * width), jnp.bfloat16)
    return pl.pallas_call(
        kernel,
        grid_spec=pltpu.PrefetchScalarGridSpec(
            num_scalar_prefetch=1,
            grid=(),
            in_specs=[vmem] * 4,
            out_specs=[vmem] * 2,
            scratch_shapes=[pltpu.VMEM((width, rows), jnp.bfloat16), pltpu.VMEM((width, 2 * width), jnp.float32)],
        ),
        out_shape=[shape] * 2,
        compiler_params=pltpu.CompilerParams(vmem_limit_bytes=VMEM_LIMIT),
        cost_estimate=NO_COST,
        name="attn_grads",
    )


def attn_update(rows, columns, width, parts, piece):
    qkv = columns - width
    whole = columns + 128 * -(-(7 * width + HS + FF) // (128 * piece * parts))

    def kernel(place_ref, even_ref, odd_ref, master, first, second, *outs):
        core = place_ref[0] % 2
        for ref, which in ((even_ref, core), (odd_ref, 1 - core)):
            here = pl.ds(pl.multiple_of(which * piece, 8), piece)
            for cols, source in (
                (slice(0, width), slice(0, width)),
                (slice(width, qkv), slice(2 * width, columns)),
                (slice(qkv, columns), slice(width, 2 * width)),
            ):
                grad = wide(ref[0, :, source])
                got = adam_update(master[here, cols], grad, first[here, cols], second[here, cols], 0.1, 0.1)
                outs[0][here, cols] = got[0]
                outs[1][here, cols] = got[1]
                outs[2][here, cols] = got[2]

    block = pl.BlockSpec((2 * piece, columns), lambda i, place: (i, 0))
    stack = pl.BlockSpec((1, piece, whole), lambda i, place: (i ^ (place[0] // 2), 0, 0))
    return pl.pallas_call(
        kernel,
        grid_spec=pltpu.PrefetchScalarGridSpec(
            num_scalar_prefetch=1,
            grid=(parts // 2,),
            in_specs=[stack] * 2 + [block] * 3,
            out_specs=[block] * 3,
            scratch_shapes=[],
        ),
        out_shape=[jax.ShapeDtypeStruct((rows, columns), jnp.float32)] * 3,
        compiler_params=pltpu.CompilerParams(vmem_limit_bytes=VMEM_LIMIT),
        cost_estimate=NO_COST,
        name="attn_update",
    )


def ffn_update(rows, units, parts, chunk):
    per_row = 2 * units // 128
    rows_once = 32
    lines = rows_once * per_row

    def kernel(place_ref, even, odd, master, first, second, first_out, second_out, master_out, total):
        place = place_ref[0]
        for k in range(parts):
            grad = odd if k % 2 else even
            for j in range(chunk // 128):
                for which in range(2):
                    line = (place ^ k) * (2 * chunk // 128) + 2 * j + which
                    total[pl.ds(line, rows_once, per_row), :] = wide(
                        grad[k // 2, which, :, j * 128 : (j + 1) * 128]
                    )
        for t in range(lines // 64):
            own = slice(t * 64, (t + 1) * 64)
            got = adam_update(master[own, :], total[own, :], first[own, :], second[own, :], 0.1, 0.1)
            first_out[own, :] = got[0]
            second_out[own, :] = got[1]
            master_out[own, :] = got[2]

    block = pl.BlockSpec((lines, 128), lambda i, *_: (i, 0))
    stack = pl.BlockSpec((parts // 2, 2, rows_once, chunk), lambda i, *_: (0, 0, i, 0))
    call = pl.pallas_call(
        kernel,
        grid_spec=pltpu.PrefetchScalarGridSpec(
            num_scalar_prefetch=1,
            grid=(rows // rows_once,),
            in_specs=[stack] * 2 + [block] * 3,
            out_specs=[block] * 3,
            scratch_shapes=[pltpu.VMEM((lines, 128), jnp.float32)],
        ),
        out_shape=[jax.ShapeDtypeStruct((rows * per_row, 128), jnp.float32)] * 3,
        compiler_params=pltpu.CompilerParams(vmem_limit_bytes=VMEM_LIMIT),
        cost_estimate=NO_COST,
        name="ffn_update",
    )

    def fold(array):
        return jnp.swapaxes(array.reshape(rows, 2, units // 128, 128), 1, 2).reshape(-1, 128)

    def unfold(array):
        return jnp.swapaxes(array.reshape(rows, units // 128, 2, 128), 1, 2).reshape(rows, 2, units)

    def run(place, even, odd, master, first, second):
        return tuple(unfold(array) for array in call(place, even, odd, fold(master), fold(first), fold(second)))

    return run


def shards(
    tokens,
    doc_starts,
    attn_master,
    attn_mom,
    attn_sq,
    ffn_master,
    ffn_mom,
    ffn_sq,
    small_master,
    small_mom,
    small_sq,
    cotangent,
):
    ctx_count, wt_count = lax.axis_size("ctx"), lax.axis_size("wt")
    ctx_place, wt_place = lax.axis_index("ctx"), lax.axis_index("wt")
    batches, rows_here, width = tokens.shape
    qkv_cols = width + 2 * HS
    attn_columns = attn_master.shape[1]
    all_rows = batches * rows_here
    shard_rows = attn_master.shape[0]
    piece_rows = shard_rows // ctx_count
    chunk = FF // ctx_count
    chips = ctx_count // 2
    order = ctx_place ^ jnp.arange(ctx_count, dtype=jnp.int32)
    runs = 2 if batches % 2 == 0 else 1
    places = [jnp.stack([ctx_place, jnp.int32(run * (batches // runs))]) for run in range(runs)]
    place = places[0]
    wt_half = wt_count // 2
    out_rows = shard_rows // chips
    run_forward, run_backward = attention_kernels(batches, rows_here, width, ctx_count, runs)
    ffn_first, ffn_second, ffn_third, ffn_down = ffn_kernels(all_rows, width, chunk, wt_count)
    step = Steps()

    def both(own, got, place, bit, axis=0):
        ahead, behind = jnp.stack([own, got], axis), jnp.stack([got, own], axis)
        return jnp.where((place & bit) == 0, ahead, behind)

    def in_order(even, odd):
        buffer = jnp.zeros((ctx_count,) + even.shape[1:], even.dtype)
        for m in range(chips):
            buffer = put(buffer, even[m][None], ctx_place ^ (2 * m), 0)
            buffer = put(buffer, odd[m][None], ctx_place ^ (2 * m + 1), 0)
        return buffer

    def send_chips(piece):
        return [xor_send(piece, mask) for mask in range(2, ctx_count, 2)]

    def split_wt(total, bit):
        pairs = total.reshape((-1, 2) + total.shape[1:]) if bit == 1 else total[None]
        ahead, behind = pairs[:, 0], pairs[:, 1]
        here = (wt_place & bit) == 0
        return jnp.where(here, ahead, behind), jnp.where(here, behind, ahead)

    def add_low(*arrays):
        return low(sum(wide(array) for array in arrays))

    qkv = low(lax.dynamic_slice(attn_master, (ctx_place * piece_rows, 0), (piece_rows, qkv_cols)))
    out_start = (ctx_place // 2 * out_rows, qkv_cols + ctx_place % 2 * chunk)
    out = low(lax.dynamic_slice(attn_master, out_start, (out_rows, chunk)))
    rest = low(jnp.swapaxes(take(ffn_master, ctx_place, 2, chunk), 0, 1).reshape(2 * shard_rows, chunk))
    qkv_got, out_got = xor_wt(qkv, 2), xor_wt(out, 2)
    qkv_got, out_got, rest = together(qkv_got, out_got, rest)
    ups, downs = rest[:shard_rows], rest[shard_rows:]
    ups_got = xor_wt(ups, 2)
    qkv, out = both(qkv, qkv_got, wt_place, 2), both(out, out_got, wt_place, 2)
    qkv, out, small_late = together(qkv, out, small_master)
    qkv_got, out_got = xor_wt(qkv, 1), xor_wt(out, 1)
    back_low = cotangent.reshape(all_rows, width)
    qkv_got, out_got, downs = together(qkv_got, out_got, downs)
    qkv = both(qkv, qkv_got, wt_place, 1, 1).reshape((wt_count,) + qkv.shape[1:])
    qkv_got = send_chips(qkv)
    back_other = xor_send(back_low, 1)
    flat_tokens, qkv, small_late = together(tokens.reshape(all_rows, width), qkv, small_late)
    (
        gain_one,
        shift_one,
        gain_two,
        shift_two,
        bias_query,
        bias_out,
        bias_proj,
        bias_value,
        bias_hidden,
    ) = split_small(small_late)
    normed_low = low(layer_norm(wide(flat_tokens), gain_one, shift_one))
    bias_parts = bias_hidden.reshape(ctx_count, chunk)[order[::2]].reshape(1, chips * chunk)
    bias_near, bias_far = jnp.split(bias_parts, 2, axis=1)
    *qkv_got, normed_low, bias_near, bias_far, back_other, ups_got, downs = together(
        *qkv_got, normed_low, bias_near, bias_far, back_other, ups_got, downs
    )
    downs_got = xor_wt(downs, 2)
    ups = both(ups, ups_got, wt_place, 2)
    ups_got = xor_wt(ups, 1)
    out = both(out, out_got, wt_place, 1, 1).reshape((wt_count,) + out.shape[1:])
    qkv_even, out = together(jnp.stack([qkv] + qkv_got), out)
    qkv_odd = xor_send(qkv_even, 1)
    out_got = send_chips(out)
    blocks = both(qkv_even, qkv_odd, ctx_place, 1, 1)
    for n in range(chips.bit_length() - 1):
        pairs = blocks.reshape((-1, 2, 1 << n) + blocks.shape[1:])
        blocks = jnp.where((ctx_place & (2 << n)) == 0, pairs, pairs[:, ::-1]).reshape(blocks.shape)
    weight_qkv = jnp.transpose(blocks, (2, 0, 1, 3, 4)).reshape(width, qkv_cols)
    mixed = dot(normed_low, weight_qkv)
    queries = low(mixed[:, :width] + bias_query).reshape(batches, rows_here, width)
    kv_bias = jnp.concatenate([jnp.zeros((HS,), jnp.float32), bias_value])
    kv_local = low(mixed[:, width:] + kv_bias).reshape(batches, rows_here, 2 * HS)
    back_turned = turn_both(back_low, back_other)
    downs = both(downs, downs_got, wt_place, 2)
    kv_local, back_turned, ups_got, downs, *out_got = together(kv_local, back_turned, ups_got, downs, *out_got)
    downs_got = xor_wt(downs, 1)
    kv_got = send_chips(kv_local)
    out_even = jnp.stack([out] + out_got)
    *kv_got, out_even, downs_got = together(*kv_got, out_even, downs_got)
    out_odd = xor_send(out_even, 1)
    kv_even = jnp.stack([kv_local] + kv_got)
    kv_odd = xor_send(kv_even, 1)
    rest = jnp.concatenate([both(ups, ups_got, wt_place, 1, 1), both(downs, downs_got, wt_place, 1, 1)], axis=2)
    rest_low, rest_high = rest[0], rest[1]
    low_x, high_y, high_x, low_y = xor_send(rest_low, 2), xor_send(rest_high, 4), xor_send(rest_high, 2), xor_send(rest_low, 4)
    queries, rest_low, rest_high = together(queries, rest_low, rest_high)

    attended_low, attended, logs = step(run_forward, doc_starts, place, queries, kv_even, kv_odd)
    attended_low = attended_low.reshape(all_rows, width)
    attended_low, low_x, high_y, high_x, low_y = together(attended_low, low_x, high_y, high_x, low_y)
    low_diagonal, high_diagonal = xor_send(low_x, 4), xor_send(high_y, 2)

    def join_out(even, odd):
        columns = jnp.where((ctx_place & 1) == 0, jnp.concatenate([even, odd], axis=3), jnp.concatenate([odd, even], axis=3))
        for n in range(chips.bit_length() - 1):
            pairs = columns.reshape((-1, 2, 1 << n) + columns.shape[1:])
            columns = jnp.where((ctx_place & (2 << n)) == 0, pairs, pairs[:, ::-1]).reshape(columns.shape)
        return jnp.swapaxes(columns, 0, 1).reshape(width, width)

    weight_out = step(join_out, out_even, out_odd)
    hidden, normed_two = step(
        out_projection(all_rows, width), attended_low, weight_out, flat_tokens, bias_out[None], gain_two[None],
        shift_two[None],
    )
    normed_other = xor_send(normed_two, 1)

    weights = [rest_low, rest_high, low_x, high_x, low_y, high_y, low_diagonal, high_diagonal]
    flows = (normed_two, normed_other, back_low, back_other, back_turned)
    act_first, units_first, down_own, down_x, sums_first = step(
        lambda *args: ffn_first(*args[:6], *in_hbm(args[6:])), *flows, bias_near, *weights[:4]
    )
    act_second, units_second, down_y, down_top, down_bottom, sums_second, back_own, back_part = step(
        lambda *args: ffn_second(*args[:6], *in_hbm(args[6:])), *flows, bias_far, units_first, *weights
    )
    back_got = xor_send(back_part, 1)
    top_got, bottom_got = xor_send(down_top, 4), xor_send(down_bottom, 2)

    def meet(along_x, along_y, top, bottom):
        half = width // 2
        return (
            jnp.concatenate([add_low(along_x[:half], top), along_x[half:]]),
            jnp.concatenate([along_y[:half], add_low(along_y[half:], bottom)]),
        )

    up_own, up_x, up_y, up_top, up_bottom = step(
        lambda *args: ffn_third(*args[:2], *in_hbm(args[2:])), normed_two, normed_other, units_first, units_second
    )
    down_x, down_y = step(meet, down_x, down_y, top_got, bottom_got)
    down_got = [xor_send(down_x, 2), xor_send(down_y, 4)]
    top_got, bottom_got = xor_send(up_top, 4), xor_send(up_bottom, 2)

    grad_hidden, grad_hidden_low, grad_attended, hidden_sums = step(
        hidden_back(all_rows, width), back_own, back_got, hidden, back_low, gain_two[None], weight_out
    )
    grad_attended = grad_attended.reshape(batches, rows_here, width)
    def by_wt(*arrays):
        return split_wt(add_low(*arrays).reshape(wt_count, shard_rows, chunk), 1)

    def next_wt(kept, got):
        return split_wt(add_low(kept, got), 2)

    def kv_pieces(evens, odds):
        total = jnp.concatenate([add_low(a, b) for a, b in zip(evens, odds)], axis=1)
        return [total[m] for m in range(chips)]

    backs = [step(run_backward[0], doc_starts, places[0], queries, kv_even, kv_odd, attended, logs, grad_attended)]
    kv_got = [xor_send(backs[0][2], 1)]
    down_kept, down_sent = step(by_wt, down_own, *down_got)
    up_x, up_y = step(meet, up_x, up_y, top_got, bottom_got)
    grad_attended, down_kept, down_sent, up_x, up_y = together(grad_attended, down_kept, down_sent, up_x, up_y)
    down_got = xor_wt(down_sent, 1)
    up_got = [xor_send(up_x, 2), xor_send(up_y, 4)]
    backs += [
        step(run_backward[run], doc_starts, places[run], queries, kv_even, kv_odd, attended, logs, grad_attended)
        for run in range(1, runs)
    ]
    backs[-1] = list(backs[-1])
    *backs[-1], down_got, up_got[0], up_got[1] = together(*backs[-1], down_got, *up_got)
    kv_got += [xor_send(back[2], 1) for back in backs[1:]]
    grad_queries = [back[0] for back in backs]
    grad_query = jnp.concatenate(grad_queries).reshape(all_rows, width)
    down_kept, down_sent = next_wt(down_kept, down_got)
    up_kept, up_sent = by_wt(up_own, *up_got)
    down_kept, down_sent, up_kept, up_sent = together(down_kept, down_sent, up_kept, up_sent)
    down_got, up_got = xor_wt(down_sent, 2), xor_wt(up_sent, 1)
    kv_half = step(kv_pieces, [back[1] for back in backs], kv_got)
    kv_got = [xor_send(kv_half[m], 2 * m) for m in range(1, chips)]
    wide_even, wide_odd = step(
        attn_grads(all_rows, width, wt_count, ctx_count, piece_rows),
        place, normed_low, grad_query, attended_low, grad_hidden_low,
    )
    small_size = small_master.shape[0]
    up_kept, up_sent = step(next_wt, up_kept, up_got)
    kv_got[0], up_kept, up_sent, down_got = together(kv_got[0], up_kept, up_sent, down_got)
    up_got = xor_wt(up_sent, 2)
    input_grad, tail_even, tail_odd = step(
        stream_back(all_rows, width, ctx_count, wt_count, piece_rows),
        place, *[array.reshape(all_rows, 2 * HS) for array in (kv_half[0], *kv_got)], grad_query, weight_qkv,
        flat_tokens, gain_one[None], grad_hidden, normed_low, back_low, hidden_sums, sums_first, sums_second,
    )
    input_grad = input_grad.reshape(batches, rows_here, width)
    wide_odd, tail_odd = lax.optimization_barrier((wide_odd, tail_odd))
    wide_odd, tail_odd = xor_send(wide_odd, 1), xor_send(tail_odd, 1)
    def attn_pieces(wide_even, wide_odd, tail_even, tail_odd):
        total = jnp.concatenate([add_low(wide_even, wide_odd), add_low(tail_even, tail_odd)], axis=3)
        return [total[m] for m in range(chips)]

    attn_half = step(attn_pieces, wide_even, wide_odd, tail_even, tail_odd)
    attn_got = [xor_send(attn_half[m], 2 * m) for m in range(1, chips)]
    ffn_part = step(
        lambda *arrays: jnp.concatenate([add_low(*arrays[:2]), add_low(*arrays[2:])]), up_kept, up_got, down_kept, down_got
    )
    ffn_got = send_chips(ffn_part)
    down_out, down_other = step(
        lambda *args: ffn_down(*args[:2], *in_hbm(args[2:])), act_first, act_second, *weights
    )
    down_other = xor_send(down_other, 1)
    attn_kept, attn_sent = step(lambda *parts: split_wt(add_low(*parts), 1), attn_half[0], *attn_got)
    attn_got = xor_wt(attn_sent, 1)
    layer_out = step(
        lambda hidden, own, got: low(hidden + own + wide(got) + bias_proj).reshape(batches, rows_here, width),
        hidden, down_out, down_other,
    )
    attn_kept, attn_sent = step(lambda kept, got: split_wt(add_low(kept, got), 2), attn_kept, attn_got)
    attn_got = xor_wt(attn_sent, 2)
    attn_got, *ffn_got = together(attn_got, *ffn_got)
    ffn_even = jnp.stack([ffn_part] + ffn_got)
    ffn_odd = xor_send(ffn_even, 1)
    attn_part = step(lambda *parts: add_low(*parts)[0], attn_kept, attn_got)
    attn_got = send_chips(attn_part)

    ffn_new = step(
        ffn_update(shard_rows, FF, ctx_count, chunk), place, ffn_even, ffn_odd, ffn_master, ffn_mom, ffn_sq
    )
    attn_even = step(lambda *parts: jnp.stack(parts), attn_part, *attn_got)
    attn_odd = xor_send(attn_even, 1)
    small_total = in_order(attn_even[..., attn_columns:], attn_odd[..., attn_columns:])
    small_total = wide(small_total.reshape(-1))
    most = small_size - FF - HS
    small_total = jnp.concatenate(
        [small_total[:most], small_total[most + HS : most + 2 * HS], small_total[most + 2 * HS : most + 2 * HS + FF]]
    )
    small_new = adam_update(small_master, small_total, small_mom, small_sq, 1.0, 0.0)
    attn_new = attn_update(shard_rows, attn_columns, width, ctx_count, piece_rows)(
        place, attn_even, attn_odd, *in_hbm([attn_master, attn_mom, attn_sq])
    )
    return (layer_out, input_grad) + tuple(attn_new) + tuple(ffn_new) + tuple(small_new)


def shift_wt(array, shift):
    count = lax.axis_size("wt")
    return lax.ppermute(array, "wt", [(i, (i + shift) % count) for i in range(count)])


def whole_wt(piece, axis):
    count, place = lax.axis_size("wt"), lax.axis_index("wt")
    shape = list(piece.shape)
    shape[axis] *= count
    buffer = put(jnp.zeros(shape, piece.dtype), piece, place, axis)
    for shift in range(1, count):
        buffer = put(buffer, shift_wt(piece, shift), (place - shift) % count, axis)
    return buffer


def whole_ctx(piece):
    count = lax.axis_size("ctx")
    got = {0: piece}
    for mask in range(2, count, 2):
        got[mask] = xor_send(piece, mask)
    for mask in range(0, count, 2):
        got[mask + 1] = xor_send(got[mask], 1)
    return [got[mask] for mask in range(count)]


def sum_ctx(pieces):
    count = lax.axis_size("ctx")
    half = {}
    for mask in range(count - 2, -1, -2):
        other = xor_send(pieces[mask + 1], 1)
        half[mask] = low(wide(pieces[mask]) + wide(other))
    total = wide(half[0])
    for mask in range(2, count, 2):
        total = total + wide(xor_send(half[mask], mask))
    return total


def sum_wt(array, axis):
    count, place = lax.axis_size("wt"), lax.axis_index("wt")
    size = array.shape[axis] // count
    total = wide(take(array, place, axis, size))
    for shift in range(1, count):
        sent = take(array, (place + shift) % count, axis, size)
        total = total + wide(shift_wt(sent, shift))
    return total


def any_shards(
    tokens,
    doc_starts,
    attn_master,
    attn_mom,
    attn_sq,
    ffn_master,
    ffn_mom,
    ffn_sq,
    small_master,
    small_mom,
    small_sq,
    cotangent,
):
    ctx_count = lax.axis_size("ctx")
    ctx_place = lax.axis_index("ctx")
    wt_count = lax.axis_size("wt")
    batches, rows_here, width = tokens.shape
    heads = width // HS
    qkv_cols = width + 2 * HS
    all_rows = batches * rows_here
    shard_rows = attn_master.shape[0]
    piece_rows = shard_rows // ctx_count
    chunk = FF // ctx_count
    order = ctx_place ^ jnp.arange(ctx_count, dtype=jnp.int32)
    (
        gain_one,
        shift_one,
        gain_two,
        shift_two,
        bias_query,
        bias_out,
        bias_proj,
        bias_value,
        bias_hidden,
    ) = split_small(small_master)

    attn_piece = low(take(attn_master, ctx_place, 0, piece_rows))

    def whole_rows(piece):
        parts = whole_ctx(whole_wt(piece[None], 0))
        buffer = jnp.zeros((wt_count, ctx_count) + piece.shape, piece.dtype)
        for k, part in enumerate(parts):
            buffer = put(buffer, part[:, None], ctx_place ^ k, 1)
        return buffer.reshape((width,) + piece.shape[1:])

    weight_qkv = whole_rows(attn_piece[:, :qkv_cols])
    weight_out = whole_rows(attn_piece[:, qkv_cols:])
    ffn_piece = low(jnp.swapaxes(take(ffn_master, ctx_place, 2, chunk), 0, 1))
    ffn_parts = whole_ctx(whole_wt(ffn_piece, 1))
    bias_parts = bias_hidden.reshape(ctx_count, chunk)[order]

    stream = wide(tokens.reshape(all_rows, width))
    normed, norm_back_one = jax.vjp(layer_norm, stream, gain_one, shift_one)
    normed_low = low(normed)
    mixed = dot(normed_low, weight_qkv)
    queries = low(mixed[:, :width] + bias_query)
    kv_local = low(
        mixed[:, width:] + jnp.concatenate([jnp.zeros((HS,), jnp.float32), bias_value])
    ).reshape(batches, rows_here, 2 * HS)
    kv_parts = jnp.stack(whole_ctx(kv_local), axis=1).reshape(
        batches, ctx_count * rows_here, 2 * HS
    )
    keys_all, values_all = kv_parts[..., :HS], kv_parts[..., HS:]
    local_pos = jnp.arange(rows_here, dtype=jnp.int32)
    query_pos = ctx_place * rows_here + local_pos
    key_pos = (order[:, None] * rows_here + local_pos[None, :]).reshape(-1)
    queries = queries.reshape(batches, rows_here * heads, HS)
    scale = HS ** (-0.5)
    attended_list, log_list, allowed_list = [], [], []
    for b in range(batches):
        starts = doc_starts[b]
        query_doc = jnp.sum((starts[None, :] <= query_pos[:, None]).astype(jnp.int32), axis=1)
        key_doc = jnp.sum((starts[None, :] <= key_pos[:, None]).astype(jnp.int32), axis=1)
        allowed = (query_doc[:, None] == key_doc[None, :]) & (key_pos[None, :] <= query_pos[:, None])
        allowed = jnp.repeat(allowed, heads, axis=0)
        allowed_list.append(allowed)
        scores = jnp.where(allowed, cols_dot(queries[b], keys_all[b]) * scale, -1e30)
        peak = jnp.max(scores, axis=-1, keepdims=True)
        expo = jnp.exp(scores - peak)
        total = jnp.sum(expo, axis=-1, keepdims=True)
        attended_list.append(dot(low(expo / total), values_all[b]))
        log_list.append(peak + jnp.log(total))
    attended = jnp.stack(attended_list)
    attended_low = low(attended).reshape(all_rows, width)
    hidden = stream + dot(attended_low, weight_out) + bias_out
    normed_two, norm_back_two = jax.vjp(layer_norm, hidden, gain_two, shift_two)
    normed_two_low = low(normed_two)

    back_low = cotangent.reshape(all_rows, width)
    back_rows = wide(back_low)
    down_vals = jnp.zeros((all_rows, width), jnp.float32)
    grad_normed_two = jnp.zeros((all_rows, width), jnp.float32)
    ffn_grads, hidden_grads = [], []
    for k in range(ctx_count):
        weight_up, weight_down = ffn_parts[k][0], ffn_parts[k][1]
        value, slope = gelu_both(dot(normed_two_low, weight_up) + bias_parts[k])
        act = low(value)
        down_vals = down_vals + cols_dot(act, weight_down)
        grad_up = low(dot(back_low, weight_down) * slope)
        hidden_grads.append(jnp.sum(wide(grad_up), axis=0))
        grad_normed_two = grad_normed_two + cols_dot(grad_up, weight_up)
        ffn_grads.append(
            jnp.stack([low(rows_dot(normed_two_low, grad_up)), low(rows_dot(back_low, act))])
        )
    layer_out = low(hidden + down_vals + bias_proj).reshape(batches, rows_here, width)
    grad_bias_proj = jnp.sum(back_rows, axis=0)
    grad_bias_hidden = jnp.stack(hidden_grads)[order].reshape(FF)
    ffn_part = low(sum_wt(low(sum_ctx(ffn_grads)), 1))

    grad_hidden_part, grad_gain_two, grad_shift_two = norm_back_two(grad_normed_two)
    grad_hidden = back_rows + grad_hidden_part
    grad_bias_out = jnp.sum(grad_hidden, axis=0)
    grad_hidden_low = low(grad_hidden)
    grad_out = rows_dot(attended_low, grad_hidden_low)

    def summed_rows(grad):
        blocks = low(grad).reshape(wt_count, ctx_count, piece_rows, grad.shape[1])
        pieces = [take(blocks, ctx_place ^ k, 1, 1)[:, 0] for k in range(ctx_count)]
        part = low(sum_wt(low(sum_ctx(pieces)), 0)[0])
        buffer = jnp.zeros((ctx_count,) + part.shape, part.dtype)
        for k, got in enumerate(whole_ctx(part)):
            buffer = put(buffer, got[None], ctx_place ^ k, 0)
        return wide(buffer.reshape(shard_rows, grad.shape[1]))

    out_total = summed_rows(grad_out)

    grad_attended = low(cols_dot(grad_hidden_low, weight_out)).reshape(
        batches, rows_here * heads, HS
    )
    grad_query_list, grad_kv_list = [], []
    for b in range(batches):
        grads = grad_attended[b]
        delta = jnp.sum(wide(grads) * attended[b], axis=-1, keepdims=True)
        scores = jnp.where(allowed_list[b], cols_dot(queries[b], keys_all[b]) * scale, -1e30)
        weights = jnp.exp(scores - log_list[b])
        grad_scores = low(weights * (cols_dot(grads, values_all[b]) - delta))
        grad_query_list.append(low(dot(grad_scores, keys_all[b]) * scale))
        grad_kv_list.append(
            jnp.concatenate(
                [
                    low(rows_dot(grad_scores, queries[b]) * scale),
                    low(rows_dot(low(weights), grads)),
                ],
                axis=1,
            )
        )
    grad_query = jnp.stack(grad_query_list).reshape(all_rows, width)
    grad_kv = jnp.stack(grad_kv_list).reshape(batches, ctx_count, rows_here, 2 * HS)
    grad_kv_low = low(sum_ctx([grad_kv[:, k] for k in range(ctx_count)])).reshape(
        all_rows, 2 * HS
    )
    grad_bias_query = jnp.sum(wide(grad_query), axis=0)
    grad_bias_value = jnp.sum(wide(grad_kv_low[:, HS:]), axis=0)
    grad_mixed = jnp.concatenate([grad_query, grad_kv_low], axis=1)
    qkv_total = summed_rows(rows_dot(normed_low, grad_mixed))
    grad_normed = cols_dot(grad_mixed, weight_qkv)
    grad_stream_part, grad_gain_one, grad_shift_one = norm_back_one(grad_normed)
    input_grad = (grad_hidden + grad_stream_part).reshape(batches, rows_here, width)

    ffn_buffer = jnp.zeros((ctx_count,) + ffn_part.shape, ffn_part.dtype)
    for k, got in enumerate(whole_ctx(ffn_part)):
        ffn_buffer = put(ffn_buffer, got[None], ctx_place ^ k, 0)
    ffn_total = wide(jnp.transpose(ffn_buffer, (2, 1, 0, 3)).reshape(shard_rows, 2, FF))
    attn_total = jnp.concatenate([qkv_total, out_total], axis=1)
    grad_small = jnp.concatenate(
        [
            grad_gain_one,
            grad_shift_one,
            grad_gain_two,
            grad_shift_two,
            grad_bias_query,
            grad_bias_out,
            grad_bias_proj,
            grad_bias_value,
            grad_bias_hidden,
        ]
    )
    small_total = lax.psum(grad_small, ("ctx", "wt"))
    attn_new = adam_update(attn_master, attn_total, attn_mom, attn_sq, 0.1, 0.1)
    ffn_new = adam_update(ffn_master, ffn_total, ffn_mom, ffn_sq, 0.1, 0.1)
    small_new = adam_update(small_master, small_total, small_mom, small_sq, 1.0, 0.0)
    return (layer_out, input_grad) + attn_new + ffn_new + small_new


def solution(mesh):
    rows, cube = P("wt", None), P("wt", None, None)
    flow = P("wt", "ctx", None)
    in_specs = (flow, rows, rows, rows, rows, cube, cube, cube, P(), P(), P(), flow)
    out_specs = (flow, flow, rows, rows, rows, cube, cube, cube, P(), P(), P())
    ctx_count, wt_count = mesh.shape["ctx"], mesh.shape["wt"]
    fitted = (ctx_count, wt_count) == (8, 4)
    body = shards if fitted else any_shards
    return jax.shard_map(body, mesh=mesh, in_specs=in_specs, out_specs=out_specs, check_vma=False)
```

```python
import jax
import jax.numpy as jnp
from jax import lax
from jax.experimental import pallas as pl
from jax.experimental.pallas import tpu as pltpu
from jax.sharding import PartitionSpec as P

D = 768
HS = 64
FF = 3072
STEP = 10


NORM_EPS = 1e-05
GELU_COEF = 0.7978845608028654
GELU_CUBE = 0.044715
BETA_ONE = 0.9
BETA_TWO = 0.95
ADAM_EPS = 1e-08
VMEM_LIMIT = 22 << 20
NO_COST = pl.CostEstimate(flops=0, bytes_accessed=0, transcendentals=0)


def layer_norm(values, gain, shift):
    centre = values - jnp.mean(values, axis=-1, keepdims=True)
    spread = jnp.mean(centre * centre, axis=-1, keepdims=True)
    return centre * lax.rsqrt(spread + NORM_EPS) * gain + shift


def gelu_both(u):
    square = u * u
    share = 0.5 * jnp.tanh(u * (GELU_COEF * GELU_CUBE * square + GELU_COEF)) + 0.5
    bend = u * (6.0 * GELU_COEF * GELU_CUBE * square + 2.0 * GELU_COEF)
    return u * share, share * ((1.0 - share) * bend) + share


def split_small(small):
    return (
        small[0:D],
        small[D : 2 * D],
        small[2 * D : 3 * D],
        small[3 * D : 4 * D],
        small[4 * D : 5 * D],
        small[5 * D : 6 * D],
        small[6 * D : 7 * D],
        small[7 * D : 7 * D + HS],
        small[7 * D + HS :],
    )


def rows_dot(left, right):
    return lax.dot_general(
        left, right, (((0,), (0,)), ((), ())), preferred_element_type=jnp.float32
    )


def cols_dot(left, right):
    return lax.dot_general(
        left, right, (((1,), (1,)), ((), ())), preferred_element_type=jnp.float32
    )


def dot(left, right):
    return jnp.dot(left, right, preferred_element_type=jnp.float32)


def low(values):
    return values.astype(jnp.bfloat16)


def wide(values):
    return values.astype(jnp.float32)


def adam_update(master, gradient, first, second, step_rate, decay_rate):
    first_new = BETA_ONE * first + (1.0 - BETA_ONE) * gradient
    second_new = BETA_TWO * second + (1.0 - BETA_TWO) * gradient * gradient
    first_hat = first_new / (1.0 - BETA_ONE**STEP)
    second_hat = second_new / (1.0 - BETA_TWO**STEP)
    master_new = master - step_rate * (
        first_hat / (jnp.sqrt(second_hat) + ADAM_EPS) + decay_rate * master
    )
    return (first_new, second_new, master_new)


def xor_send(array, mask):
    count = lax.axis_size("ctx")
    return lax.ppermute(array, "ctx", [(i, i ^ mask) for i in range(count)])


def xor_wt(array, mask):
    count = lax.axis_size("wt")
    return lax.ppermute(array, "wt", [(i, i ^ mask) for i in range(count)])


class Steps:
    def __init__(self):
        self.last = ()

    def __call__(self, function, *args):
        flat, tree = jax.tree.flatten(args)
        held = lax.optimization_barrier(tuple(flat) + self.last)[: len(flat)]
        result = function(*jax.tree.unflatten(tree, held))
        self.last = tuple(jax.tree.leaves(result))
        return result


def loop(count, body, carry=0):
    return lax.fori_loop(0, count, body, carry)


def rows_at(i, size):
    return pl.ds(pl.multiple_of(i * size, size), size)


def together(*arrays):
    return lax.optimization_barrier(arrays)


def put(buffer, piece, place, axis):
    starts = [0] * buffer.ndim
    starts[axis] = place * piece.shape[axis]
    return lax.dynamic_update_slice(buffer, piece, starts)


def take(buffer, place, axis, size):
    return lax.dynamic_slice_in_dim(buffer, place * size, size, axis)


def attention_kernels(batches, rows, width, parts, runs):
    half_parts = parts // 2
    keys = parts * rows
    pair = 2 * HS
    groups = width // (2 * pair)
    factor = HS ** (-0.5) * 1.4426950408889634
    tile = 32

    def lanes(shape):
        return lax.broadcasted_iota(jnp.int32, shape, 1)

    def spread(even_ref, odd_ref, key_ref, value_ref):
        for j in range(parts):
            ref = even_ref if j < half_parts else odd_ref
            block = wide(ref[j % half_parts, 0])
            turned = pltpu.roll(block, HS, 1)
            first = lanes(block.shape) < HS
            here = pl.ds(j * rows, rows)
            key_ref[0, here, :] = low(jnp.where(first, block, 0.0))
            key_ref[1, here, :] = low(jnp.where(first, 0.0, turned))
            value_ref[0, here, :] = low(jnp.where(first, turned, 0.0))
            value_ref[1, here, :] = low(jnp.where(first, 0.0, block))

    def doc_begin(starts_ref, stream, positions):
        begin = jnp.zeros_like(positions)
        for j in range(starts_ref.shape[1]):
            start = starts_ref[stream, j]
            begin = jnp.where(start <= positions, jnp.maximum(begin, start), begin)
        return begin

    def forward(starts_ref, place_ref, query_ref, even_ref, odd_ref, low_ref, full_ref, log_ref, cap, key, value, weight):
        stream, place = pl.program_id(0), place_ref[0]
        spread(even_ref, odd_ref, key, value)
        query_pos = place * rows + lax.broadcasted_iota(jnp.int32, (rows, 1), 0)
        begin = doc_begin(starts_ref, stream, query_pos)
        for j in range(parts):
            key_pos = (place ^ (2 * (j % half_parts) + j // half_parts)) * rows + lax.broadcasted_iota(jnp.int32, (rows, rows), 1)
            allowed = (key_pos >= begin) & (key_pos <= query_pos)
            cap[:, j * rows : (j + 1) * rows] = jnp.where(allowed, 3.0e38, -1e30)
        column = lanes((tile, pair))
        logs = [jnp.zeros((tile, pair), jnp.float32) for _ in range(rows // tile)]
        for g in range(groups):
            at = g * 2 * pair
            two = jnp.concatenate([query_ref[0, :, at : at + pair], query_ref[0, :, at + pair : at + 2 * pair]], axis=0)
            totals = []
            for half in range(2):
                scores = cols_dot(two, key[half])
                norms = []
                for t in range(2 * rows // tile):
                    own = slice(t * tile, (t + 1) * tile)
                    n = t % (rows // tile)
                    part = jnp.minimum(scores[own] * factor, cap[n * tile : (n + 1) * tile, :])
                    peak = jnp.max(part, axis=1, keepdims=True)
                    expo = jnp.exp2(part - peak)
                    norm = jnp.sum(expo, axis=1, keepdims=True)
                    weight[half, own, :] = low(expo)
                    norms.append(norm)
                    head = 4 * g + 2 * (t * tile // rows) + half
                    logs[n] = jnp.where(column == head, peak + jnp.log2(norm), logs[n])
                totals.append(dot(weight[half], value[half]) / jnp.concatenate(norms, axis=0))
            total = totals[0] + totals[1]
            for j in range(2):
                part = total[j * rows : (j + 1) * rows]
                full_ref[0, :, at + j * pair : at + (j + 1) * pair] = part
                low_ref[0, :, at + j * pair : at + (j + 1) * pair] = low(part)
        for n, log in enumerate(logs):
            log_ref[0, n * tile : (n + 1) * tile, :] = log

    def backward(
        starts_ref, place_ref, query_ref, even_ref, odd_ref, full_ref, log_ref, grad_ref,
        query_grad_ref, even_grad_ref, odd_grad_ref,
        cap, key, value, key_turned, log_rows, delta_rows, weight_buf, score_buf, query_buf, grad_buf,
    ):
        stream, place = pl.program_id(0) + place_ref[1], place_ref[0]
        spread(even_ref, odd_ref, key, value)
        query_pos = place * rows + lax.broadcasted_iota(jnp.int32, (1, rows), 1)
        begin = doc_begin(starts_ref, stream, query_pos)
        for j in range(parts):
            key_pos = (place ^ (2 * (j % half_parts) + j // half_parts)) * rows + lax.broadcasted_iota(jnp.int32, (rows, rows), 0)
            allowed = (key_pos >= begin) & (key_pos <= query_pos)
            cap[j * rows : (j + 1) * rows, :] = jnp.where(allowed, 3.0e38, -1e30)
            here = pl.ds(j * rows, rows)
            key_turned[:, j * rows : (j + 1) * rows] = low(wide(key[0, here, :]).T[:HS])
        log_rows[...] = log_ref[0].T[: log_rows.shape[0]]
        head_of = lax.broadcasted_iota(jnp.int32, (delta_rows.shape[0], width), 1) // HS
        chosen = (head_of == lax.broadcasted_iota(jnp.int32, (delta_rows.shape[0], width), 0)).astype(jnp.float32)
        delta_rows[...] = lax.dot_general(
            chosen, wide(grad_ref[0]) * full_ref[0], (((1,), (1,)), ((), ())),
            precision=lax.Precision.HIGHEST, preferred_element_type=jnp.float32,
        )
        first = lanes((2 * rows, pair)) < HS
        for g in range(groups):
            at = g * 2 * pair
            both, both_grad = query_ref[0, :, at : at + 2 * pair], grad_ref[0, :, at : at + 2 * pair]
            two = jnp.concatenate([both[:, :pair], both[:, pair:]], axis=0)
            two_grad = jnp.concatenate([both_grad[:, :pair], both_grad[:, pair:]], axis=0)
            turned = []
            for half in range(2):
                h = 4 * g + half
                span = slice((2 * g + half) * 2 * rows, (2 * g + half + 1) * 2 * rows)
                keep = first if half == 0 else jnp.logical_not(first)
                query_buf[span, :] = low(jnp.where(keep, wide(two), 0.0))
                grad_buf[span, :] = low(jnp.where(keep, wide(two_grad), 0.0))
                log = jnp.concatenate([log_rows[h : h + 1, :], log_rows[h + 2 : h + 3, :]], axis=1)
                delta = jnp.concatenate([delta_rows[h : h + 1, :], delta_rows[h + 2 : h + 3, :]], axis=1)
                scores, weight_grads = cols_dot(key[half], two), cols_dot(value[half], two_grad)
                for t in range(keys // (2 * tile)):
                    own = slice(t * 2 * tile, (t + 1) * 2 * tile)
                    limit = cap[own, :]
                    limit = jnp.concatenate([limit, limit], axis=1)
                    weights = jnp.exp2(jnp.minimum(scores[own] * factor, limit) - log)
                    weight_buf[own, span] = low(weights)
                    score_buf[own, span] = low(weights * (weight_grads[own] - delta))
                turned.append(dot(key_turned[...], score_buf[:, span]))
            turned = jnp.concatenate(turned, axis=0) * HS ** (-0.5)
            query_grad_ref[0, :, at : at + pair] = low(turned[:, :rows].T)
            query_grad_ref[0, :, at + pair : at + 2 * pair] = low(turned[:, rows:].T)
        for j in range(parts):
            here = pl.ds(j * rows, rows)
            value_sum = dot(weight_buf[here, :], grad_buf[...])
            key_sum = dot(score_buf[here, :], query_buf[...]) * HS ** (-0.5)
            value_sum = value_sum + pltpu.roll(value_sum, HS, 1)
            key_sum = key_sum + pltpu.roll(key_sum, HS, 1)
            ref = even_grad_ref if j < half_parts else odd_grad_ref
            ref[j % half_parts, 0] = low(jnp.where(lanes((rows, pair)) < HS, key_sum, value_sum))

    def specs(first):
        return (
            pl.BlockSpec((1, rows, width), lambda b, *_: (b + first, 0, 0)),
            pl.BlockSpec((1, rows, pair), lambda b, *_: (b + first, 0, 0)),
            pl.BlockSpec((half_parts, 1, rows, pair), lambda b, *_: (0, b + first, 0, 0)),
        )

    flow, logs, blocks = specs(0)

    shared = [
        pltpu.VMEM((2, keys, pair), jnp.bfloat16),
        pltpu.VMEM((2, keys, pair), jnp.bfloat16),
    ]
    run_forward = pl.pallas_call(
        forward,
        grid_spec=pltpu.PrefetchScalarGridSpec(
            num_scalar_prefetch=2,
            grid=(batches,),
            in_specs=[flow, blocks, blocks],
            out_specs=[flow, flow, logs],
            scratch_shapes=[pltpu.VMEM((rows, keys), jnp.float32)]
            + shared
            + [pltpu.VMEM((2, 2 * rows, keys), jnp.bfloat16)],
        ),
        out_shape=[
            jax.ShapeDtypeStruct((batches, rows, width), jnp.bfloat16),
            jax.ShapeDtypeStruct((batches, rows, width), jnp.float32),
            jax.ShapeDtypeStruct((batches, rows, pair), jnp.float32),
        ],
        compiler_params=pltpu.CompilerParams(vmem_limit_bytes=VMEM_LIMIT),
        cost_estimate=NO_COST,
        name="attention_forward",
    )
    head_rows = -(-(width // HS) // 8) * 8
    all_columns = rows * (width // HS)
    count = batches // runs

    def call_backward(run):
        here_flow, here_logs, here_blocks = specs(run * count)
        return pl.pallas_call(
        backward,
        grid_spec=pltpu.PrefetchScalarGridSpec(
            num_scalar_prefetch=2,
            grid=(count,),
            in_specs=[here_flow, here_blocks, here_blocks, here_flow, here_logs, here_flow],
            out_specs=[flow, blocks, blocks],
            scratch_shapes=[pltpu.VMEM((keys, rows), jnp.float32)]
            + shared
            + [
                pltpu.VMEM((HS, keys), jnp.bfloat16),
                pltpu.VMEM((head_rows, rows), jnp.float32),
                pltpu.VMEM((head_rows, rows), jnp.float32),
                pltpu.VMEM((keys, all_columns), jnp.bfloat16),
                pltpu.VMEM((keys, all_columns), jnp.bfloat16),
                pltpu.VMEM((all_columns, pair), jnp.bfloat16),
                pltpu.VMEM((all_columns, pair), jnp.bfloat16),
            ],
        ),
        out_shape=[
            jax.ShapeDtypeStruct((count, rows, width), jnp.bfloat16),
            jax.ShapeDtypeStruct((half_parts, count, rows, pair), jnp.bfloat16),
            jax.ShapeDtypeStruct((half_parts, count, rows, pair), jnp.bfloat16),
        ],
        compiler_params=pltpu.CompilerParams(vmem_limit_bytes=VMEM_LIMIT),
        cost_estimate=NO_COST,
        name="attention_backward",
    )

    return run_forward, [call_backward(run) for run in range(runs)]


def in_hbm(arrays):
    return [pltpu.with_memory_space_constraint(array, pltpu.HBM) for array in arrays]


def ffn_kernels(rows, width, chunk, wt_count):
    units = 2 * chunk
    all_rows = 2 * rows
    block_rows = width // wt_count
    hbm = pl.BlockSpec(memory_space=pltpu.HBM)
    vmem = pl.BlockSpec(memory_space=pltpu.VMEM)
    params = pltpu.CompilerParams(vmem_limit_bytes=VMEM_LIMIT)

    def fetch(weights, which, held, sem):
        copies = []
        for n, arrays in enumerate(weights):
            blocks = [array.at[block] for array in arrays for block in range(array.shape[0])]
            for row, block in enumerate(blocks):
                copies.append(
                    pltpu.make_async_copy(
                        block.at[pl.ds(which * block_rows, block_rows), :],
                        held.at[pl.ds(row * block_rows, block_rows), pl.ds(n * chunk, chunk)],
                        sem.at[len(copies)],
                    )
                )
        for copy in copies:
            copy.start()
        return copies

    def send(pairs, sems):
        copies = [pltpu.make_async_copy(source, out, sems.at[n]) for n, (source, out) in enumerate(pairs)]
        for copy in copies:
            copy.start()
        return copies

    part_rows = 256
    tile = 16

    def units_of(inputs, grads, bias, held_up, held_down, act, grad_units):
        sums = jnp.zeros((8, units), jnp.float32)
        for s in range(2):

            def part(i, sums):
                here = rows_at(i, part_rows)
                up = dot(inputs[s][here, :], held_up[...])
                act_grad = dot(grads[s][here, :], held_down[...])
                for t in range(part_rows // tile):
                    own = slice(t * tile, (t + 1) * tile)
                    there = pl.ds(pl.multiple_of(s * rows + i * part_rows + t * tile, tile), tile)
                    value, slope = gelu_both(up[own] + bias)
                    grad = act_grad[own] * slope
                    act[there, :] = low(value)
                    grad_units[there, :] = low(grad)
                    sums = sums + (grad[:8] + grad[8:])
                return sums

            sums = loop(rows // part_rows, part, sums)
        return jnp.sum(sums, axis=0, keepdims=True)

    def product_of(turned, right, product):
        def part(i, carry):
            here = rows_at(i, part_rows)
            product[here, :] = low(dot(turned[here, :], right[...]))
            return carry

        loop(width // part_rows, part)

    def back_to(refs, sources, weights):
        for s, ref in enumerate(refs):

            def part(i, carry):
                here = pl.ds(pl.multiple_of(s * rows + i * part_rows, part_rows), part_rows)
                total = cols_dot(sources[0][here, :], weights[0][...]) + cols_dot(sources[1][here, :], weights[1][...])
                ref[rows_at(i, part_rows), :] = total.astype(ref.dtype)
                return carry

            loop(rows // part_rows, part)

    def halves(product, m):
        cols = pl.ds(m * chunk, chunk)
        return [product.at[pl.ds(h * width // 2, width // 2), cols] for h in range(2)]

    def first(
        own, other, grad_own, grad_other, turned, bias, w0, w1, w2, w3,
        act_out, units_out, out_a, out_b, sums_out,
        held_up, held_down, act, grad_units, product, sems, out_sems,
    ):
        weights = ((w0, w1), (w2, w3))
        copies = fetch(weights, 0, held_up, sems.at[0]) + fetch(weights, 1, held_down, sems.at[1])
        for copy in copies:
            copy.wait()
        sums_out[...] = units_of((own, other), (grad_own, grad_other), bias[...], held_up, held_down, act, grad_units)
        sent = send(((act, act_out), (grad_units, units_out)), out_sems.at[0])
        product_of(turned, act, product)
        sent += send(
            ((product.at[:, pl.ds(0, chunk)], out_a), (product.at[:, pl.ds(chunk, chunk)], out_b)), out_sems.at[1]
        )
        for copy in sent:
            copy.wait()

    def second(
        own, other, grad_own, grad_other, turned, bias, units_first, w0, w1, w2, w3, w4, w5, w6, w7,
        act_out, units_out, out_a, out_b, out_c, sums_out, back_own, back_other,
        held_up, held_more, held_down, act, grad_units, more_units, product, sems, out_sems, more_sem,
    ):
        weights, before = ((w4, w5), (w6, w7)), ((w0, w1), (w2, w3))
        copies = fetch(weights, 0, held_up, sems.at[0]) + fetch(weights, 1, held_down, sems.at[1])
        more = fetch(before, 0, held_more, sems.at[2])
        more.append(pltpu.make_async_copy(units_first, more_units, more_sem))
        more[-1].start()
        for copy in copies:
            copy.wait()
        sums_out[...] = units_of((own, other), (grad_own, grad_other), bias[...], held_up, held_down, act, grad_units)
        sent = send(((act, act_out), (grad_units, units_out)), out_sems.at[0])
        product_of(turned, act, product)
        top, bottom = halves(product, 1)
        sent += send(((product.at[:, pl.ds(0, chunk)], out_a), (top, out_b), (bottom, out_c)), out_sems.at[1])
        for copy in more:
            copy.wait()
        back_to((back_own, back_other), (grad_units, more_units), (held_up, held_more))
        for copy in sent:
            copy.wait()

    def third(own, other, units_a, units_b, out_0, out_1, out_2, out_3, out_4, turned, held, products, sems, out_sems):
        copies = send(((units_a, held.at[0]), (units_b, held.at[1])), sems)
        turn((own, other), turned)
        for copy in copies:
            copy.wait()
        products[1] = low(dot(turned[...], held[1]))
        top, bottom = halves(products.at[1], 1)
        sent = send(((products.at[1, :, pl.ds(0, chunk)], out_2), (top, out_3), (bottom, out_4)), out_sems.at[0])
        products[0] = low(dot(turned[...], held[0]))
        sent += send(
            ((products.at[0, :, pl.ds(0, chunk)], out_0), (products.at[0, :, pl.ds(chunk, chunk)], out_1)),
            out_sems.at[1],
        )
        for copy in sent:
            copy.wait()

    def down(act_a, act_b, w0, w1, w2, w3, w4, w5, w6, w7, own_ref, other_ref, held_a, held_b, sems):
        copies = fetch(((w0, w1), (w2, w3)), 1, held_a, sems.at[0]) + fetch(((w4, w5), (w6, w7)), 1, held_b, sems.at[1])
        for copy in copies:
            copy.wait()
        for s, ref in enumerate((own_ref, other_ref)):
            here = slice(s * rows, (s + 1) * rows)
            total = cols_dot(act_a[here, :], held_a[...]) + cols_dot(act_b[here, :], held_b[...])
            ref[...] = total.astype(ref.dtype)

    dma = pltpu.SemaphoreType.DMA
    held = pltpu.VMEM((width, units), jnp.bfloat16)
    flow = pltpu.VMEM((all_rows, units), jnp.bfloat16)
    flow_out = pltpu.HBM((all_rows, units), jnp.bfloat16)
    whole = pltpu.HBM((width, chunk), jnp.bfloat16)
    part = pltpu.HBM((width // 2, chunk), jnp.bfloat16)
    sums = jax.ShapeDtypeStruct((1, units), jnp.float32)
    own = jax.ShapeDtypeStruct((rows, width), jnp.float32)
    other = jax.ShapeDtypeStruct((rows, width), jnp.bfloat16)
    run_first = pl.pallas_call(
        first,
        in_specs=[vmem] * 6 + [hbm] * 4,
        out_specs=[hbm] * 4 + [vmem],
        out_shape=[flow_out, flow_out, whole, whole, sums],
        scratch_shapes=[held, held, flow, flow, held, dma((2, 2 * wt_count)), dma((2, 2))],
        compiler_params=params,
        cost_estimate=NO_COST,
        name="ffn_first",
    )
    run_second = pl.pallas_call(
        second,
        in_specs=[vmem] * 6 + [hbm] * 9,
        out_specs=[hbm] * 5 + [vmem] * 3,
        out_shape=[flow_out, flow_out, whole, part, part, sums, own, other],
        scratch_shapes=[held, held, held, flow, flow, flow, held, dma((3, 2 * wt_count)), dma((2, 3)), dma(())],
        compiler_params=params,
        cost_estimate=NO_COST,
        name="ffn_second",
    )
    run_third = pl.pallas_call(
        third,
        in_specs=[vmem] * 2 + [hbm] * 2,
        out_specs=[hbm] * 5,
        out_shape=[whole, whole, whole, part, part],
        scratch_shapes=[
            pltpu.VMEM((width, all_rows), jnp.bfloat16),
            pltpu.VMEM((2, all_rows, units), jnp.bfloat16),
            pltpu.VMEM((2, width, units), jnp.bfloat16),
            dma((2,)),
            dma((2, 3)),
        ],
        compiler_params=params,
        cost_estimate=NO_COST,
        name="ffn_grads",
    )
    run_down = pl.pallas_call(
        down,
        in_specs=[vmem] * 2 + [hbm] * 8,
        out_specs=[vmem] * 2,
        out_shape=[own, other],
        scratch_shapes=[held, held, dma((2, 2 * wt_count))],
        compiler_params=params,
        cost_estimate=NO_COST,
        name="ffn_down",
    )
    return run_first, run_second, run_third, run_down


def turn(refs, turned):
    rows = refs[0].shape[0]
    for s, ref in enumerate(refs):
        for i in range(rows // 128):
            block = wide(ref[i * 128 : (i + 1) * 128, :])
            turned[:, s * rows + i * 128 : s * rows + (i + 1) * 128] = low(block.T)


def turn_both(own, other):
    vmem = pl.BlockSpec(memory_space=pltpu.VMEM)
    rows, width = own.shape
    return pl.pallas_call(
        lambda a, b, out: turn((a, b), out),
        in_specs=[vmem] * 2,
        out_specs=vmem,
        out_shape=jax.ShapeDtypeStruct((width, 2 * rows), own.dtype),
        compiler_params=pltpu.CompilerParams(vmem_limit_bytes=VMEM_LIMIT),
        cost_estimate=NO_COST,
        name="turn",
    )(own, other)


def out_projection(rows, width):
    tile = 32

    def kernel(attended, weight, stream, bias, gain, shift, hidden_ref, normed_ref):
        product = dot(attended[...], weight[...])
        for t in range(rows // tile):
            here = slice(t * tile, (t + 1) * tile)
            hidden = wide(stream[here, :]) + product[here] + bias[...]
            hidden_ref[here, :] = hidden
            normed_ref[here, :] = low(layer_norm(hidden, gain[...], shift[...]))

    vmem = pl.BlockSpec(memory_space=pltpu.VMEM)
    return pl.pallas_call(
        kernel,
        in_specs=[vmem] * 6,
        out_specs=[vmem] * 2,
        out_shape=[
            jax.ShapeDtypeStruct((rows, width), jnp.float32),
            jax.ShapeDtypeStruct((rows, width), jnp.bfloat16),
        ],
        compiler_params=pltpu.CompilerParams(vmem_limit_bytes=VMEM_LIMIT),
        cost_estimate=NO_COST,
        name="out_projection",
    )


def norm_back(values, gain, grad):
    centre = values - jnp.mean(values, axis=-1, keepdims=True)
    scale = lax.rsqrt(jnp.mean(centre * centre, axis=-1, keepdims=True) + NORM_EPS)
    unit = centre * scale
    inner = grad * gain
    mean = jnp.mean(inner, axis=-1, keepdims=True)
    along = jnp.mean(inner * unit, axis=-1, keepdims=True)
    return scale * (inner - mean - unit * along), grad * unit


def fold_rows(values):
    total = values[:8]
    for i in range(1, values.shape[0] // 8):
        total = total + values[i * 8 : (i + 1) * 8]
    return total


def hidden_back(rows, width):
    tile = 32

    def kernel(own, got, hidden, back, gain, weight, grad_ref, low_ref, attended_ref, sums_ref):
        sums = [jnp.zeros((8, width), jnp.float32) for _ in range(3)]
        for t in range(rows // tile):
            here = slice(t * tile, (t + 1) * tile)
            pulled, terms = norm_back(hidden[here, :], gain[...], own[here, :] + wide(got[here, :]))
            grad = wide(back[here, :]) + pulled
            grad_ref[here, :] = grad
            low_ref[here, :] = low(grad)
            for n, part in enumerate((terms, own[here, :] + wide(got[here, :]), grad)):
                sums[n] = sums[n] + fold_rows(part)
        for n in range(3):
            sums_ref[n : n + 1, :] = jnp.sum(sums[n], axis=0, keepdims=True)
        attended_ref[...] = low(cols_dot(low_ref[...], weight[...]))

    vmem = pl.BlockSpec(memory_space=pltpu.VMEM)
    return pl.pallas_call(
        kernel,
        in_specs=[vmem] * 6,
        out_specs=[vmem] * 4,
        out_shape=[
            jax.ShapeDtypeStruct((rows, width), jnp.float32),
            jax.ShapeDtypeStruct((rows, width), jnp.bfloat16),
            jax.ShapeDtypeStruct((rows, width), jnp.bfloat16),
            jax.ShapeDtypeStruct((3, width), jnp.float32),
        ],
        compiler_params=pltpu.CompilerParams(vmem_limit_bytes=VMEM_LIMIT),
        cost_estimate=NO_COST,
        name="hidden_back",
    )


def stream_back(rows, width, parts, row_groups, piece):
    tile = 32
    chips = parts // 2

    def kernel(
        place_ref, kv_0, kv_1, kv_2, kv_3, queries, weight, tokens, gain, grad_hidden, normed, back, hidden_sums,
        units_a, units_b, input_ref, even_ref, odd_ref, grad_kv, grads, turned, product, small,
    ):
        place = place_ref[0]
        sums = [jnp.zeros((8, width), jnp.float32) for _ in range(4)]
        value_sums = jnp.zeros((8, 2 * HS), jnp.float32)
        for t in range(rows // tile):
            here = slice(t * tile, (t + 1) * tile)
            total = wide(kv_0[here, :]) + wide(kv_1[here, :]) + wide(kv_2[here, :]) + wide(kv_3[here, :])
            grad_kv[here, :] = low(total)
            value_sums = value_sums + fold_rows(total)
        turn((normed,), turned)
        product[...] = dot(turned[...], grad_kv[...])
        grads[...] = cols_dot(queries[...], weight[:, :width]) + cols_dot(grad_kv[...], weight[:, width:])
        for t in range(rows // tile):
            here = slice(t * tile, (t + 1) * tile)
            grad = grads[here, :]
            pulled, terms = norm_back(wide(tokens[here, :]), gain[...], grad)
            input_ref[here, :] = grad_hidden[here, :] + pulled
            for n, part in enumerate((terms, grad, wide(queries[here, :]), wide(back[here, :]))):
                sums[n] = sums[n] + fold_rows(part)
        sums = [jnp.sum(part, axis=0, keepdims=True) for part in sums]
        small[...] = jnp.zeros_like(small)
        rows_in = (sums[0], sums[1], hidden_sums[0:1, :], hidden_sums[1:2, :], sums[2], hidden_sums[2:3, :], sums[3])
        for n, row in enumerate(rows_in):
            for j in range(width // 128):
                line = n * (width // 128) + j
                small[line : line + 1, :] = row[:, j * 128 : (j + 1) * 128]
        start = 7 * (width // 128)
        small[start : start + 1, :] = jnp.sum(value_sums, axis=0, keepdims=True)
        lines = FF // parts // 128
        for m in range(chips):
            units = (units_a, units_b)[m // 2]
            for j in range(lines):
                line = start + 1 + (place ^ (2 * m)) * lines + j
                at = (m % 2 * lines + j) * 128
                small[pl.ds(line, 1), :] = units[:, at : at + 128]
        for k in range(parts):
            ref = odd_ref if k % 2 else even_ref
            mine = low(small[pl.ds(pl.multiple_of((place ^ k) * piece, 8), piece), :])
            for w in range(row_groups):
                at = pl.multiple_of(w * piece * parts + (place ^ k) * piece, 8)
                ref[k // 2, w, :, :128] = low(product[pl.ds(at, piece), :])
                ref[k // 2, w, :, 128:] = mine

    vmem = pl.BlockSpec(memory_space=pltpu.VMEM)
    stack = jax.ShapeDtypeStruct((chips, row_groups, piece, 256), jnp.bfloat16)
    return pl.pallas_call(
        kernel,
        in_specs=[pl.BlockSpec(memory_space=pltpu.SMEM)] + [vmem] * 14,
        out_specs=[vmem] * 3,
        out_shape=[jax.ShapeDtypeStruct((rows, width), jnp.float32), stack, stack],
        scratch_shapes=[
            pltpu.VMEM((rows, 2 * HS), jnp.bfloat16),
            pltpu.VMEM((rows, width), jnp.float32),
            pltpu.VMEM((width, rows), jnp.bfloat16),
            pltpu.VMEM((width, 2 * HS), jnp.float32),
            pltpu.VMEM((parts * piece, 128), jnp.float32),
        ],
        compiler_params=pltpu.CompilerParams(vmem_limit_bytes=VMEM_LIMIT),
        cost_estimate=NO_COST,
        name="stream_back",
    )


def attn_grads(rows, width, row_groups, parts, piece):
    def kernel(place_ref, left_a, right_a, left_b, right_b, even_ref, odd_ref, turned, total):
        place = place_ref[0]
        for n, (left, right) in enumerate(((left_a, right_a), (left_b, right_b))):
            for i in range(rows // 128):
                turned[:, i * 128 : (i + 1) * 128] = low(wide(left[i * 128 : (i + 1) * 128, :]).T)
            total[:, n * width : (n + 1) * width] = dot(turned[...], right[...])
        for k in range(parts):
            ref = odd_ref if k % 2 else even_ref
            for w in range(row_groups):
                at = pl.multiple_of(w * piece * parts + (place ^ k) * piece, 8)
                ref[k // 2, w] = low(total[pl.ds(at, piece), :])

    vmem = pl.BlockSpec(memory_space=pltpu.VMEM)
    shape = jax.ShapeDtypeStruct((parts // 2, row_groups, piece, 2 * width), jnp.bfloat16)
    return pl.pallas_call(
        kernel,
        grid_spec=pltpu.PrefetchScalarGridSpec(
            num_scalar_prefetch=1,
            grid=(),
            in_specs=[vmem] * 4,
            out_specs=[vmem] * 2,
            scratch_shapes=[pltpu.VMEM((width, rows), jnp.bfloat16), pltpu.VMEM((width, 2 * width), jnp.float32)],
        ),
        out_shape=[shape] * 2,
        compiler_params=pltpu.CompilerParams(vmem_limit_bytes=VMEM_LIMIT),
        cost_estimate=NO_COST,
        name="attn_grads",
    )


def attn_update(rows, columns, width, parts, piece):
    qkv = columns - width
    whole = columns + 128 * -(-(7 * width + HS + FF) // (128 * piece * parts))

    def kernel(place_ref, even_ref, odd_ref, master, first, second, *outs):
        core = place_ref[0] % 2
        for ref, which in ((even_ref, core), (odd_ref, 1 - core)):
            here = pl.ds(pl.multiple_of(which * piece, 8), piece)
            for cols, source in (
                (slice(0, width), slice(0, width)),
                (slice(width, qkv), slice(2 * width, columns)),
                (slice(qkv, columns), slice(width, 2 * width)),
            ):
                grad = wide(ref[0, :, source])
                got = adam_update(master[here, cols], grad, first[here, cols], second[here, cols], 0.1, 0.1)
                outs[0][here, cols] = got[0]
                outs[1][here, cols] = got[1]
                outs[2][here, cols] = got[2]

    block = pl.BlockSpec((2 * piece, columns), lambda i, place: (i, 0))
    stack = pl.BlockSpec((1, piece, whole), lambda i, place: (i ^ (place[0] // 2), 0, 0))
    return pl.pallas_call(
        kernel,
        grid_spec=pltpu.PrefetchScalarGridSpec(
            num_scalar_prefetch=1,
            grid=(parts // 2,),
            in_specs=[stack] * 2 + [block] * 3,
            out_specs=[block] * 3,
            scratch_shapes=[],
        ),
        out_shape=[jax.ShapeDtypeStruct((rows, columns), jnp.float32)] * 3,
        compiler_params=pltpu.CompilerParams(vmem_limit_bytes=VMEM_LIMIT),
        cost_estimate=NO_COST,
        name="attn_update",
    )


def ffn_update(rows, units, parts, chunk):
    per_row = 2 * units // 128
    rows_once = 32
    lines = rows_once * per_row

    def kernel(place_ref, even, odd, master, first, second, first_out, second_out, master_out, total):
        place = place_ref[0]
        for k in range(parts):
            grad = odd if k % 2 else even
            for j in range(chunk // 128):
                for which in range(2):
                    line = (place ^ k) * (2 * chunk // 128) + 2 * j + which
                    total[pl.ds(line, rows_once, per_row), :] = wide(
                        grad[k // 2, which, :, j * 128 : (j + 1) * 128]
                    )
        for t in range(lines // 64):
            own = slice(t * 64, (t + 1) * 64)
            got = adam_update(master[own, :], total[own, :], first[own, :], second[own, :], 0.1, 0.1)
            first_out[own, :] = got[0]
            second_out[own, :] = got[1]
            master_out[own, :] = got[2]

    block = pl.BlockSpec((lines, 128), lambda i, *_: (i, 0))
    stack = pl.BlockSpec((parts // 2, 2, rows_once, chunk), lambda i, *_: (0, 0, i, 0))
    call = pl.pallas_call(
        kernel,
        grid_spec=pltpu.PrefetchScalarGridSpec(
            num_scalar_prefetch=1,
            grid=(rows // rows_once,),
            in_specs=[stack] * 2 + [block] * 3,
            out_specs=[block] * 3,
            scratch_shapes=[pltpu.VMEM((lines, 128), jnp.float32)],
        ),
        out_shape=[jax.ShapeDtypeStruct((rows * per_row, 128), jnp.float32)] * 3,
        compiler_params=pltpu.CompilerParams(vmem_limit_bytes=VMEM_LIMIT),
        cost_estimate=NO_COST,
        name="ffn_update",
    )

    def fold(array):
        return jnp.swapaxes(array.reshape(rows, 2, units // 128, 128), 1, 2).reshape(-1, 128)

    def unfold(array):
        return jnp.swapaxes(array.reshape(rows, units // 128, 2, 128), 1, 2).reshape(rows, 2, units)

    def run(place, even, odd, master, first, second):
        return tuple(unfold(array) for array in call(place, even, odd, fold(master), fold(first), fold(second)))

    return run


def shards(
    tokens,
    doc_starts,
    attn_master,
    attn_mom,
    attn_sq,
    ffn_master,
    ffn_mom,
    ffn_sq,
    small_master,
    small_mom,
    small_sq,
    cotangent,
):
    ctx_count, wt_count = lax.axis_size("ctx"), lax.axis_size("wt")
    ctx_place, wt_place = lax.axis_index("ctx"), lax.axis_index("wt")
    batches, rows_here, width = tokens.shape
    qkv_cols = width + 2 * HS
    attn_columns = attn_master.shape[1]
    all_rows = batches * rows_here
    shard_rows = attn_master.shape[0]
    piece_rows = shard_rows // ctx_count
    chunk = FF // ctx_count
    chips = ctx_count // 2
    order = ctx_place ^ jnp.arange(ctx_count, dtype=jnp.int32)
    runs = 2 if batches % 2 == 0 else 1
    places = [jnp.stack([ctx_place, jnp.int32(run * (batches // runs))]) for run in range(runs)]
    place = places[0]
    wt_half = wt_count // 2
    out_rows = shard_rows // chips
    run_forward, run_backward = attention_kernels(batches, rows_here, width, ctx_count, runs)
    ffn_first, ffn_second, ffn_third, ffn_down = ffn_kernels(all_rows, width, chunk, wt_count)
    step = Steps()

    def both(own, got, place, bit, axis=0):
        ahead, behind = jnp.stack([own, got], axis), jnp.stack([got, own], axis)
        return jnp.where((place & bit) == 0, ahead, behind)

    def in_order(even, odd):
        buffer = jnp.zeros((ctx_count,) + even.shape[1:], even.dtype)
        for m in range(chips):
            buffer = put(buffer, even[m][None], ctx_place ^ (2 * m), 0)
            buffer = put(buffer, odd[m][None], ctx_place ^ (2 * m + 1), 0)
        return buffer

    def send_chips(piece):
        return [xor_send(piece, mask) for mask in range(2, ctx_count, 2)]

    def split_wt(total, bit):
        pairs = total.reshape((-1, 2) + total.shape[1:]) if bit == 1 else total[None]
        ahead, behind = pairs[:, 0], pairs[:, 1]
        here = (wt_place & bit) == 0
        return jnp.where(here, ahead, behind), jnp.where(here, behind, ahead)

    def add_low(*arrays):
        return low(sum(wide(array) for array in arrays))

    qkv = low(lax.dynamic_slice(attn_master, (ctx_place * piece_rows, 0), (piece_rows, qkv_cols)))
    out_start = (ctx_place // 2 * out_rows, qkv_cols + ctx_place % 2 * chunk)
    out = low(lax.dynamic_slice(attn_master, out_start, (out_rows, chunk)))
    rest = low(jnp.swapaxes(take(ffn_master, ctx_place, 2, chunk), 0, 1).reshape(2 * shard_rows, chunk))
    qkv_got, out_got = xor_wt(qkv, 2), xor_wt(out, 2)
    qkv_got, out_got, rest = together(qkv_got, out_got, rest)
    ups, downs = rest[:shard_rows], rest[shard_rows:]
    ups_got = xor_wt(ups, 2)
    qkv, out = both(qkv, qkv_got, wt_place, 2), both(out, out_got, wt_place, 2)
    qkv, out, small_late = together(qkv, out, small_master)
    qkv_got, out_got = xor_wt(qkv, 1), xor_wt(out, 1)
    back_low = cotangent.reshape(all_rows, width)
    qkv_got, out_got, ups_got, downs = together(qkv_got, out_got, ups_got, downs)
    downs_got = xor_wt(downs, 2)
    qkv = both(qkv, qkv_got, wt_place, 1, 1).reshape((wt_count,) + qkv.shape[1:])
    qkv_got = send_chips(qkv)
    back_other = xor_send(back_low, 1)
    flat_tokens, qkv, small_late = together(tokens.reshape(all_rows, width), qkv, small_late)
    (
        gain_one,
        shift_one,
        gain_two,
        shift_two,
        bias_query,
        bias_out,
        bias_proj,
        bias_value,
        bias_hidden,
    ) = split_small(small_late)
    normed_low = low(layer_norm(wide(flat_tokens), gain_one, shift_one))
    bias_parts = bias_hidden.reshape(ctx_count, chunk)[order[::2]].reshape(1, chips * chunk)
    bias_near, bias_far = jnp.split(bias_parts, 2, axis=1)
    ups = both(ups, ups_got, wt_place, 2)
    *qkv_got, normed_low, bias_near, bias_far, back_other, downs_got, ups = together(
        *qkv_got, normed_low, bias_near, bias_far, back_other, downs_got, ups
    )
    ups_got = xor_wt(ups, 1)
    out = both(out, out_got, wt_place, 1, 1).reshape((wt_count,) + out.shape[1:])
    qkv_even, out = together(jnp.stack([qkv] + qkv_got), out)
    qkv_odd = xor_send(qkv_even, 1)
    out_got = send_chips(out)
    blocks = both(qkv_even, qkv_odd, ctx_place, 1, 1)
    for n in range(chips.bit_length() - 1):
        pairs = blocks.reshape((-1, 2, 1 << n) + blocks.shape[1:])
        blocks = jnp.where((ctx_place & (2 << n)) == 0, pairs, pairs[:, ::-1]).reshape(blocks.shape)
    weight_qkv = jnp.transpose(blocks, (2, 0, 1, 3, 4)).reshape(width, qkv_cols)
    mixed = dot(normed_low, weight_qkv)
    queries = low(mixed[:, :width] + bias_query).reshape(batches, rows_here, width)
    kv_bias = jnp.concatenate([jnp.zeros((HS,), jnp.float32), bias_value])
    kv_local = low(mixed[:, width:] + kv_bias).reshape(batches, rows_here, 2 * HS)
    back_turned = turn_both(back_low, back_other)
    downs = both(downs, downs_got, wt_place, 2)
    kv_local, back_turned, ups_got, downs, *out_got = together(kv_local, back_turned, ups_got, downs, *out_got)
    downs_got = xor_wt(downs, 1)
    kv_got = send_chips(kv_local)
    out_even = jnp.stack([out] + out_got)
    *kv_got, out_even, downs_got = together(*kv_got, out_even, downs_got)
    out_odd = xor_send(out_even, 1)
    kv_even = jnp.stack([kv_local] + kv_got)
    kv_odd = xor_send(kv_even, 1)
    rest = jnp.concatenate([both(ups, ups_got, wt_place, 1, 1), both(downs, downs_got, wt_place, 1, 1)], axis=2)
    rest_low, rest_high = rest[0], rest[1]
    low_x, high_y, high_x, low_y = xor_send(rest_low, 2), xor_send(rest_high, 4), xor_send(rest_high, 2), xor_send(rest_low, 4)
    queries, rest_low, rest_high = together(queries, rest_low, rest_high)

    attended_low, attended, logs = step(run_forward, doc_starts, place, queries, kv_even, kv_odd)
    attended_low = attended_low.reshape(all_rows, width)
    attended_low, low_x, high_y, high_x, low_y = together(attended_low, low_x, high_y, high_x, low_y)
    low_diagonal, high_diagonal = xor_send(low_x, 4), xor_send(high_y, 2)

    def join_out(even, odd):
        columns = jnp.where((ctx_place & 1) == 0, jnp.concatenate([even, odd], axis=3), jnp.concatenate([odd, even], axis=3))
        for n in range(chips.bit_length() - 1):
            pairs = columns.reshape((-1, 2, 1 << n) + columns.shape[1:])
            columns = jnp.where((ctx_place & (2 << n)) == 0, pairs, pairs[:, ::-1]).reshape(columns.shape)
        return jnp.swapaxes(columns, 0, 1).reshape(width, width)

    weight_out = step(join_out, out_even, out_odd)
    hidden, normed_two = step(
        out_projection(all_rows, width), attended_low, weight_out, flat_tokens, bias_out[None], gain_two[None],
        shift_two[None],
    )
    normed_other = xor_send(normed_two, 1)

    weights = [rest_low, rest_high, low_x, high_x, low_y, high_y, low_diagonal, high_diagonal]
    flows = (normed_two, normed_other, back_low, back_other, back_turned)
    act_first, units_first, down_own, down_x, sums_first = step(
        lambda *args: ffn_first(*args[:6], *in_hbm(args[6:])), *flows, bias_near, *weights[:4]
    )
    act_second, units_second, down_y, down_top, down_bottom, sums_second, back_own, back_part = step(
        lambda *args: ffn_second(*args[:6], *in_hbm(args[6:])), *flows, bias_far, units_first, *weights
    )
    back_got = xor_send(back_part, 1)
    top_got, bottom_got = xor_send(down_top, 4), xor_send(down_bottom, 2)

    def meet(along_x, along_y, top, bottom):
        half = width // 2
        return (
            jnp.concatenate([add_low(along_x[:half], top), along_x[half:]]),
            jnp.concatenate([along_y[:half], add_low(along_y[half:], bottom)]),
        )

    up_own, up_x, up_y, up_top, up_bottom = step(
        lambda *args: ffn_third(*args[:2], *in_hbm(args[2:])), normed_two, normed_other, units_first, units_second
    )
    down_x, down_y = step(meet, down_x, down_y, top_got, bottom_got)
    down_got = [xor_send(down_x, 2), xor_send(down_y, 4)]
    top_got, bottom_got = xor_send(up_top, 4), xor_send(up_bottom, 2)

    grad_hidden, grad_hidden_low, grad_attended, hidden_sums = step(
        hidden_back(all_rows, width), back_own, back_got, hidden, back_low, gain_two[None], weight_out
    )
    grad_attended = grad_attended.reshape(batches, rows_here, width)
    def by_wt(*arrays):
        return split_wt(add_low(*arrays).reshape(wt_count, shard_rows, chunk), 1)

    def next_wt(kept, got):
        return split_wt(add_low(kept, got), 2)

    def kv_pieces(evens, odds):
        total = jnp.concatenate([add_low(a, b) for a, b in zip(evens, odds)], axis=1)
        return [total[m] for m in range(chips)]

    up_x, up_y = step(meet, up_x, up_y, top_got, bottom_got)
    grad_attended, up_x, up_y = together(grad_attended, up_x, up_y)
    up_got = [xor_send(up_x, 2), xor_send(up_y, 4)]
    backs = [step(run_backward[0], doc_starts, places[0], queries, kv_even, kv_odd, attended, logs, grad_attended)]
    kv_got = [xor_send(backs[0][2], 1)]
    down_kept, down_sent = step(by_wt, down_own, *down_got)
    grad_attended, down_kept, down_sent = together(grad_attended, down_kept, down_sent)
    down_got = xor_wt(down_sent, 1)
    backs += [
        step(run_backward[run], doc_starts, places[run], queries, kv_even, kv_odd, attended, logs, grad_attended)
        for run in range(1, runs)
    ]
    backs[-1] = list(backs[-1])
    *backs[-1], down_got, up_got[0], up_got[1] = together(*backs[-1], down_got, *up_got)
    kv_got += [xor_send(back[2], 1) for back in backs[1:]]
    grad_queries = [back[0] for back in backs]
    grad_query = jnp.concatenate(grad_queries).reshape(all_rows, width)
    down_kept, down_sent = next_wt(down_kept, down_got)
    up_kept, up_sent = by_wt(up_own, *up_got)
    down_kept, down_sent, up_kept, up_sent = together(down_kept, down_sent, up_kept, up_sent)
    down_got, up_got = xor_wt(down_sent, 2), xor_wt(up_sent, 1)
    kv_half = step(kv_pieces, [back[1] for back in backs], kv_got)
    kv_got = [xor_send(kv_half[m], 2 * m) for m in range(1, chips)]
    wide_even, wide_odd = step(
        attn_grads(all_rows, width, wt_count, ctx_count, piece_rows),
        place, normed_low, grad_query, attended_low, grad_hidden_low,
    )
    small_size = small_master.shape[0]
    up_kept, up_sent = step(next_wt, up_kept, up_got)
    kv_got[0], up_kept, up_sent, down_got = together(kv_got[0], up_kept, up_sent, down_got)
    up_got = xor_wt(up_sent, 2)
    input_grad, tail_even, tail_odd = step(
        stream_back(all_rows, width, ctx_count, wt_count, piece_rows),
        place, *[array.reshape(all_rows, 2 * HS) for array in (kv_half[0], *kv_got)], grad_query, weight_qkv,
        flat_tokens, gain_one[None], grad_hidden, normed_low, back_low, hidden_sums, sums_first, sums_second,
    )
    input_grad = input_grad.reshape(batches, rows_here, width)
    wide_odd, tail_odd = lax.optimization_barrier((wide_odd, tail_odd))
    wide_odd, tail_odd = xor_send(wide_odd, 1), xor_send(tail_odd, 1)
    def attn_pieces(wide_even, wide_odd, tail_even, tail_odd):
        total = jnp.concatenate([add_low(wide_even, wide_odd), add_low(tail_even, tail_odd)], axis=3)
        return [total[m] for m in range(chips)]

    attn_half = step(attn_pieces, wide_even, wide_odd, tail_even, tail_odd)
    attn_got = [xor_send(attn_half[m], 2 * m) for m in range(1, chips)]
    ffn_part = step(
        lambda *arrays: jnp.concatenate([add_low(*arrays[:2]), add_low(*arrays[2:])]), up_kept, up_got, down_kept, down_got
    )
    ffn_got = send_chips(ffn_part)
    down_out, down_other = step(
        lambda *args: ffn_down(*args[:2], *in_hbm(args[2:])), act_first, act_second, *weights
    )
    down_other = xor_send(down_other, 1)
    attn_kept, attn_sent = step(lambda *parts: split_wt(add_low(*parts), 1), attn_half[0], *attn_got)
    attn_got = xor_wt(attn_sent, 1)
    layer_out = step(
        lambda hidden, own, got: low(hidden + own + wide(got) + bias_proj).reshape(batches, rows_here, width),
        hidden, down_out, down_other,
    )
    attn_kept, attn_sent = step(lambda kept, got: split_wt(add_low(kept, got), 2), attn_kept, attn_got)
    attn_got = xor_wt(attn_sent, 2)
    attn_got, *ffn_got = together(attn_got, *ffn_got)
    ffn_even = jnp.stack([ffn_part] + ffn_got)
    ffn_odd = xor_send(ffn_even, 1)
    attn_part = step(lambda *parts: add_low(*parts)[0], attn_kept, attn_got)
    attn_got = send_chips(attn_part)

    ffn_new = step(
        ffn_update(shard_rows, FF, ctx_count, chunk), place, ffn_even, ffn_odd, ffn_master, ffn_mom, ffn_sq
    )
    attn_even = step(lambda *parts: jnp.stack(parts), attn_part, *attn_got)
    attn_odd = xor_send(attn_even, 1)
    small_total = in_order(attn_even[..., attn_columns:], attn_odd[..., attn_columns:])
    small_total = wide(small_total.reshape(-1))
    most = small_size - FF - HS
    small_total = jnp.concatenate(
        [small_total[:most], small_total[most + HS : most + 2 * HS], small_total[most + 2 * HS : most + 2 * HS + FF]]
    )
    small_new = adam_update(small_master, small_total, small_mom, small_sq, 1.0, 0.0)
    attn_new = attn_update(shard_rows, attn_columns, width, ctx_count, piece_rows)(
        place, attn_even, attn_odd, *in_hbm([attn_master, attn_mom, attn_sq])
    )
    return (layer_out, input_grad) + tuple(attn_new) + tuple(ffn_new) + tuple(small_new)


def shift_wt(array, shift):
    count = lax.axis_size("wt")
    return lax.ppermute(array, "wt", [(i, (i + shift) % count) for i in range(count)])


def whole_wt(piece, axis):
    count, place = lax.axis_size("wt"), lax.axis_index("wt")
    shape = list(piece.shape)
    shape[axis] *= count
    buffer = put(jnp.zeros(shape, piece.dtype), piece, place, axis)
    for shift in range(1, count):
        buffer = put(buffer, shift_wt(piece, shift), (place - shift) % count, axis)
    return buffer


def whole_ctx(piece):
    count = lax.axis_size("ctx")
    got = {0: piece}
    for mask in range(2, count, 2):
        got[mask] = xor_send(piece, mask)
    for mask in range(0, count, 2):
        got[mask + 1] = xor_send(got[mask], 1)
    return [got[mask] for mask in range(count)]


def sum_ctx(pieces):
    count = lax.axis_size("ctx")
    half = {}
    for mask in range(count - 2, -1, -2):
        other = xor_send(pieces[mask + 1], 1)
        half[mask] = low(wide(pieces[mask]) + wide(other))
    total = wide(half[0])
    for mask in range(2, count, 2):
        total = total + wide(xor_send(half[mask], mask))
    return total


def sum_wt(array, axis):
    count, place = lax.axis_size("wt"), lax.axis_index("wt")
    size = array.shape[axis] // count
    total = wide(take(array, place, axis, size))
    for shift in range(1, count):
        sent = take(array, (place + shift) % count, axis, size)
        total = total + wide(shift_wt(sent, shift))
    return total


def any_shards(
    tokens,
    doc_starts,
    attn_master,
    attn_mom,
    attn_sq,
    ffn_master,
    ffn_mom,
    ffn_sq,
    small_master,
    small_mom,
    small_sq,
    cotangent,
):
    ctx_count = lax.axis_size("ctx")
    ctx_place = lax.axis_index("ctx")
    wt_count = lax.axis_size("wt")
    batches, rows_here, width = tokens.shape
    heads = width // HS
    qkv_cols = width + 2 * HS
    all_rows = batches * rows_here
    shard_rows = attn_master.shape[0]
    piece_rows = shard_rows // ctx_count
    chunk = FF // ctx_count
    order = ctx_place ^ jnp.arange(ctx_count, dtype=jnp.int32)
    (
        gain_one,
        shift_one,
        gain_two,
        shift_two,
        bias_query,
        bias_out,
        bias_proj,
        bias_value,
        bias_hidden,
    ) = split_small(small_master)

    attn_piece = low(take(attn_master, ctx_place, 0, piece_rows))

    def whole_rows(piece):
        parts = whole_ctx(whole_wt(piece[None], 0))
        buffer = jnp.zeros((wt_count, ctx_count) + piece.shape, piece.dtype)
        for k, part in enumerate(parts):
            buffer = put(buffer, part[:, None], ctx_place ^ k, 1)
        return buffer.reshape((width,) + piece.shape[1:])

    weight_qkv = whole_rows(attn_piece[:, :qkv_cols])
    weight_out = whole_rows(attn_piece[:, qkv_cols:])
    ffn_piece = low(jnp.swapaxes(take(ffn_master, ctx_place, 2, chunk), 0, 1))
    ffn_parts = whole_ctx(whole_wt(ffn_piece, 1))
    bias_parts = bias_hidden.reshape(ctx_count, chunk)[order]

    stream = wide(tokens.reshape(all_rows, width))
    normed, norm_back_one = jax.vjp(layer_norm, stream, gain_one, shift_one)
    normed_low = low(normed)
    mixed = dot(normed_low, weight_qkv)
    queries = low(mixed[:, :width] + bias_query)
    kv_local = low(
        mixed[:, width:] + jnp.concatenate([jnp.zeros((HS,), jnp.float32), bias_value])
    ).reshape(batches, rows_here, 2 * HS)
    kv_parts = jnp.stack(whole_ctx(kv_local), axis=1).reshape(
        batches, ctx_count * rows_here, 2 * HS
    )
    keys_all, values_all = kv_parts[..., :HS], kv_parts[..., HS:]
    local_pos = jnp.arange(rows_here, dtype=jnp.int32)
    query_pos = ctx_place * rows_here + local_pos
    key_pos = (order[:, None] * rows_here + local_pos[None, :]).reshape(-1)
    queries = queries.reshape(batches, rows_here * heads, HS)
    scale = HS ** (-0.5)
    attended_list, log_list, allowed_list = [], [], []
    for b in range(batches):
        starts = doc_starts[b]
        query_doc = jnp.sum((starts[None, :] <= query_pos[:, None]).astype(jnp.int32), axis=1)
        key_doc = jnp.sum((starts[None, :] <= key_pos[:, None]).astype(jnp.int32), axis=1)
        allowed = (query_doc[:, None] == key_doc[None, :]) & (key_pos[None, :] <= query_pos[:, None])
        allowed = jnp.repeat(allowed, heads, axis=0)
        allowed_list.append(allowed)
        scores = jnp.where(allowed, cols_dot(queries[b], keys_all[b]) * scale, -1e30)
        peak = jnp.max(scores, axis=-1, keepdims=True)
        expo = jnp.exp(scores - peak)
        total = jnp.sum(expo, axis=-1, keepdims=True)
        attended_list.append(dot(low(expo / total), values_all[b]))
        log_list.append(peak + jnp.log(total))
    attended = jnp.stack(attended_list)
    attended_low = low(attended).reshape(all_rows, width)
    hidden = stream + dot(attended_low, weight_out) + bias_out
    normed_two, norm_back_two = jax.vjp(layer_norm, hidden, gain_two, shift_two)
    normed_two_low = low(normed_two)

    back_low = cotangent.reshape(all_rows, width)
    back_rows = wide(back_low)
    down_vals = jnp.zeros((all_rows, width), jnp.float32)
    grad_normed_two = jnp.zeros((all_rows, width), jnp.float32)
    ffn_grads, hidden_grads = [], []
    for k in range(ctx_count):
        weight_up, weight_down = ffn_parts[k][0], ffn_parts[k][1]
        value, slope = gelu_both(dot(normed_two_low, weight_up) + bias_parts[k])
        act = low(value)
        down_vals = down_vals + cols_dot(act, weight_down)
        grad_up = low(dot(back_low, weight_down) * slope)
        hidden_grads.append(jnp.sum(wide(grad_up), axis=0))
        grad_normed_two = grad_normed_two + cols_dot(grad_up, weight_up)
        ffn_grads.append(
            jnp.stack([low(rows_dot(normed_two_low, grad_up)), low(rows_dot(back_low, act))])
        )
    layer_out = low(hidden + down_vals + bias_proj).reshape(batches, rows_here, width)
    grad_bias_proj = jnp.sum(back_rows, axis=0)
    grad_bias_hidden = jnp.stack(hidden_grads)[order].reshape(FF)
    ffn_part = low(sum_wt(low(sum_ctx(ffn_grads)), 1))

    grad_hidden_part, grad_gain_two, grad_shift_two = norm_back_two(grad_normed_two)
    grad_hidden = back_rows + grad_hidden_part
    grad_bias_out = jnp.sum(grad_hidden, axis=0)
    grad_hidden_low = low(grad_hidden)
    grad_out = rows_dot(attended_low, grad_hidden_low)

    def summed_rows(grad):
        blocks = low(grad).reshape(wt_count, ctx_count, piece_rows, grad.shape[1])
        pieces = [take(blocks, ctx_place ^ k, 1, 1)[:, 0] for k in range(ctx_count)]
        part = low(sum_wt(low(sum_ctx(pieces)), 0)[0])
        buffer = jnp.zeros((ctx_count,) + part.shape, part.dtype)
        for k, got in enumerate(whole_ctx(part)):
            buffer = put(buffer, got[None], ctx_place ^ k, 0)
        return wide(buffer.reshape(shard_rows, grad.shape[1]))

    out_total = summed_rows(grad_out)

    grad_attended = low(cols_dot(grad_hidden_low, weight_out)).reshape(
        batches, rows_here * heads, HS
    )
    grad_query_list, grad_kv_list = [], []
    for b in range(batches):
        grads = grad_attended[b]
        delta = jnp.sum(wide(grads) * attended[b], axis=-1, keepdims=True)
        scores = jnp.where(allowed_list[b], cols_dot(queries[b], keys_all[b]) * scale, -1e30)
        weights = jnp.exp(scores - log_list[b])
        grad_scores = low(weights * (cols_dot(grads, values_all[b]) - delta))
        grad_query_list.append(low(dot(grad_scores, keys_all[b]) * scale))
        grad_kv_list.append(
            jnp.concatenate(
                [
                    low(rows_dot(grad_scores, queries[b]) * scale),
                    low(rows_dot(low(weights), grads)),
                ],
                axis=1,
            )
        )
    grad_query = jnp.stack(grad_query_list).reshape(all_rows, width)
    grad_kv = jnp.stack(grad_kv_list).reshape(batches, ctx_count, rows_here, 2 * HS)
    grad_kv_low = low(sum_ctx([grad_kv[:, k] for k in range(ctx_count)])).reshape(
        all_rows, 2 * HS
    )
    grad_bias_query = jnp.sum(wide(grad_query), axis=0)
    grad_bias_value = jnp.sum(wide(grad_kv_low[:, HS:]), axis=0)
    grad_mixed = jnp.concatenate([grad_query, grad_kv_low], axis=1)
    qkv_total = summed_rows(rows_dot(normed_low, grad_mixed))
    grad_normed = cols_dot(grad_mixed, weight_qkv)
    grad_stream_part, grad_gain_one, grad_shift_one = norm_back_one(grad_normed)
    input_grad = (grad_hidden + grad_stream_part).reshape(batches, rows_here, width)

    ffn_buffer = jnp.zeros((ctx_count,) + ffn_part.shape, ffn_part.dtype)
    for k, got in enumerate(whole_ctx(ffn_part)):
        ffn_buffer = put(ffn_buffer, got[None], ctx_place ^ k, 0)
    ffn_total = wide(jnp.transpose(ffn_buffer, (2, 1, 0, 3)).reshape(shard_rows, 2, FF))
    attn_total = jnp.concatenate([qkv_total, out_total], axis=1)
    grad_small = jnp.concatenate(
        [
            grad_gain_one,
            grad_shift_one,
            grad_gain_two,
            grad_shift_two,
            grad_bias_query,
            grad_bias_out,
            grad_bias_proj,
            grad_bias_value,
            grad_bias_hidden,
        ]
    )
    small_total = lax.psum(grad_small, ("ctx", "wt"))
    attn_new = adam_update(attn_master, attn_total, attn_mom, attn_sq, 0.1, 0.1)
    ffn_new = adam_update(ffn_master, ffn_total, ffn_mom, ffn_sq, 0.1, 0.1)
    small_new = adam_update(small_master, small_total, small_mom, small_sq, 1.0, 0.0)
    return (layer_out, input_grad) + attn_new + ffn_new + small_new


def solution(mesh):
    rows, cube = P("wt", None), P("wt", None, None)
    flow = P("wt", "ctx", None)
    in_specs = (flow, rows, rows, rows, rows, cube, cube, cube, P(), P(), P(), flow)
    out_specs = (flow, flow, rows, rows, rows, cube, cube, cube, P(), P(), P())
    ctx_count, wt_count = mesh.shape["ctx"], mesh.shape["wt"]
    fitted = (ctx_count, wt_count) == (8, 4)
    body = shards if fitted else any_shards
    return jax.shard_map(body, mesh=mesh, in_specs=in_specs, out_specs=out_specs, check_vma=False)
```
